32 devices in a mesh: dp: 8 (over z, x), group: 4 (over y, core).
Axes of the slice: x: 2, y: 2, z: 4, core: 2. Of those that a mesh axis runs over, the one named last changes fastest.
Arguments:
- tokens: bfloat16 [4096, 640], P(('dp', 'group')), may hold values from -6 to 6
- doc_ids: int32 [8, 512], P('dp'), may hold values from 0 to 2, as said below
- cotangent: bfloat16 [4096, 640], P(('dp', 'group')), may hold values from -6 to 6
- master: float32 [43520, 128], P(('dp', 'group'))
- first_moment: float32 [43520, 128], P(('dp', 'group')), may hold values from -38.4 to 38.4
- second_moment: float32 [43520, 128], P(('dp', 'group')), may hold values from 2.048 to 32.768
- gains: float32 [3072], replicated, may hold values from -0.5 to 0.5
- gain_first: float32 [3072], replicated, may hold values from -38.4 to 38.4
- gain_second: float32 [3072], replicated, may hold values from 2.048 to 32.768
Outputs:
- block_out: bfloat16 [4096, 640], P(('dp', 'group'))
- input_grad: bfloat16 [4096, 640], P(('dp', 'group'))
- moment_first: float32 [43520, 128], P(('dp', 'group'))
- moment_second: float32 [43520, 128], P(('dp', 'group'))
- master_new: float32 [43520, 128], P(('dp', 'group'))
- gain_moment_first: float32 [3072], replicated
- gain_moment_second: float32 [3072], replicated
- gains_new: float32 [3072], replicated
The draws below stay inside these ranges and needn't reach their ends.
Inputs may be any that keep to these rules, and one draw needn't show every extreme that they name: `doc_ids`: each sequence holds three documents numbered 0, 1, 2 in order; document 1 begins within the first 128 tokens and ends within the last 128 tokens.
All inputs are finite; a program needn't handle non-finite values.
Results may differ from the reference program's by a relative error of at most 0.015.
Values may be sent and summed in bfloat16 or wider, within the bound.
No kernel may reach another device: no remote copies, remote signals or barrier semaphores. Data moves between devices by JAX's collectives and lax.ppermute only.
A program may use at most 128 MiB of HBM per device.

```python
import math
import jax
import jax.numpy as jnp
from jax import lax

D = 640
HQ = 4
HD = 256
FF = 2048
WINDOW = 512
TOK_DEV = 128
STEP = 10
SEQ_LEN = 512
TOKENS = 4096
SHARD_ROWS = 1360
GAINS = 3072
N_DP = 8
DEVICES = 32


def draw_doc_ids(key, part):
    key = jax.random.fold_in(key, 11)
    first_key, second_key = jax.random.split(key)
    first_cut = jax.random.randint(first_key, (N_DP, 1), 1, TOK_DEV)
    second_cut = jax.random.randint(second_key, (N_DP, 1), SEQ_LEN - TOK_DEV + 1, SEQ_LEN)
    counter = jnp.arange(SEQ_LEN, dtype=jnp.int32)[None, :]
    return (counter >= first_cut).astype(jnp.int32) + (counter >= second_cut).astype(jnp.int32)


def draw_master(key, part):
    key = jax.random.fold_in(key, 5)
    entry_list = [D * HQ * HD, D * HD, D * HD, HQ * HD * D, D * FF, D * FF, FF * D]
    fan_list = [D, D, D, HQ * HD, D, D, FF]
    scale_rows = jnp.concatenate([jnp.full((entries // (128 * DEVICES),), fan_in ** (-0.5), jnp.float32) for entries, fan_in in zip(entry_list, fan_list)])
    base = jax.random.normal(key, (DEVICES, SHARD_ROWS, 128), jnp.float32)
    return (base * scale_rows[None, :, None]).reshape(DEVICES * SHARD_ROWS, 128)


def level_of(rng, shape, pieces, least, top_value):
    level = 1.0
    for position, blocks in pieces:
        draws = jax.random.uniform(jax.random.fold_in(jax.random.fold_in(rng, 6), position), (blocks,), jnp.float32, least / len(pieces), top_value / len(pieces))
        level = level * jnp.repeat(jnp.exp(draws), shape[position] // blocks).reshape((-1,) + (1,) * (len(shape) - 1 - position))
    return level


def centred(key, extent, spread, limit, cuts=(), kind=jnp.bfloat16):
    values = jax.random.normal(key, extent, jnp.float32) * spread
    if len(cuts) > 0:
        values = level_of(key, extent, cuts, -0.22, 0.18) * values
    return jnp.clip(values, min=-limit, max=limit).astype(kind)


def setup_inputs(seed: int = 0) -> dict:
    streams_of = jax.random.split(jax.random.key(seed), 10)
    tokens = centred(streams_of[0], (TOKENS, D), 1.0, 6.0, ((0, 32),))
    doc_ids = draw_doc_ids(jax.random.fold_in(streams_of[9], 71), 0)
    cotangent = centred(streams_of[2], (TOKENS, D), 1.0, 6.0, ((0, 32),))
    master = draw_master(jax.random.fold_in(streams_of[9], 71), 0)
    first_moment = centred(streams_of[4], (DEVICES * SHARD_ROWS, 128), (0.111 * TOKENS ** 0.5), 38.4, ((0, 32),), jnp.float32)
    second_moment = jnp.clip(jnp.exp(math.log(32.768) - 2.7725887 * jax.random.uniform(streams_of[5], (DEVICES * SHARD_ROWS, 128), jnp.float32) ** level_of(streams_of[5], (DEVICES * SHARD_ROWS, 128), ((0, 32),), -0.2, 0.2)), 2.048, 32.768)
    gains = jnp.clip(jax.random.uniform(streams_of[6], (GAINS,), jnp.float32, -0.5, 0.5), -0.5, 0.5)
    gain_first = centred(streams_of[7], (GAINS,), (0.111 * TOKENS ** 0.5), 38.4, (), jnp.float32)
    gain_second = jnp.clip(jnp.exp(jax.random.uniform(streams_of[8], (GAINS,), jnp.float32, math.log(2.048), math.log(32.768))), 2.048, 32.768)
    return {"tokens": tokens, "doc_ids": doc_ids, "cotangent": cotangent, "master": master, "first_moment": first_moment, "second_moment": second_moment, "gains": gains, "gain_first": gain_first, "gain_second": gain_second}


norm_eps = 1e-06
rope_base = 10000.0
beta_first = 0.9
beta_second = 0.999
learn_rate = 0.05
gain_rate = 0.25
adam_floor = 1e-08
weight_decay = 0.1
highest = lax.Precision.HIGHEST

@jax.custom_vjp
def low(v):
    return lax.optimization_barrier(v.astype(jnp.bfloat16)).astype(jnp.float32)

@jax.custom_vjp
def low_back(v):
    return v

def low_keep(v):
    return (low(v), None)

def low_pass(kept, grad):
    return (grad,)

def back_keep(v):
    return (v, None)

def back_low(kept, grad):
    return (low(grad),)
low.defvjp(low_keep, low_pass)
low_back.defvjp(back_keep, back_low)

def rms_norm(values, weight_vec):
    return values * lax.rsqrt(lax.optimization_barrier(jnp.mean(values * values, axis=-1, keepdims=True)) + norm_eps) * (1.0 + weight_vec)

def positions(doc_row):
    length = doc_row.shape[0]
    counter = jnp.arange(length, dtype=jnp.int32)
    starts_here = jnp.concatenate([jnp.ones((1,), jnp.bool_), doc_row[1:] != doc_row[:-1]])
    begins = lax.cummax(jnp.where(starts_here, counter, jnp.zeros_like(counter)), axis=0)
    return counter - begins

def angles_of(places):
    half_dim = HD // 2
    frequency = rope_base ** (-(jnp.arange(half_dim, dtype=jnp.float32) * 2.0 / HD))
    return places.astype(jnp.float32)[:, None] * frequency[None, :]

def rotate(values, angles):
    half_dim = values.shape[-1] // 2
    first_half = values[..., :half_dim]
    second_half = values[..., half_dim:]
    cosine = jnp.cos(angles)
    sine_part = jnp.sin(angles)
    return jnp.concatenate([first_half * cosine - second_half * sine_part, second_half * cosine + first_half * sine_part], axis=-1)

def matmul(left_side, right_side):
    return jnp.dot(left_side, right_side, precision=highest, preferred_element_type=jnp.float32)

def piece_rows(device_count):
    return [entries // (128 * device_count) for entries in (D * HQ * HD, D * HD, D * HD, HQ * HD * D, D * FF, D * FF, FF * D)]

def piece_shapes():
    return [(D, HQ * HD), (D, HD), (D, HD), (HQ * HD, D), (D, FF), (D, FF), (FF, D)]

def split_weights(flat_rows):
    blocks = flat_rows.reshape(DEVICES, SHARD_ROWS, 128)
    result = []
    row_start = 0
    for row_count, shape_pair in zip(piece_rows(DEVICES), piece_shapes()):
        result.append(blocks[:, row_start:row_start + row_count, :].reshape(shape_pair))
        row_start = row_start + row_count
    return tuple(result)

def join_grads(grad_list):
    blocks = [grad_piece.reshape(DEVICES, row_count, 128) for grad_piece, row_count in zip(grad_list, piece_rows(DEVICES))]
    return jnp.concatenate(blocks, axis=1).reshape(DEVICES * SHARD_ROWS, 128)

def attend(query_rot, key_rot, value_rows, doc_row):
    length = query_rot.shape[0]
    block_rows = min(512, length)
    key_pad = jnp.concatenate([jnp.zeros((WINDOW, HD), jnp.float32), key_rot])
    value_pad = jnp.concatenate([jnp.zeros((WINDOW, HD), jnp.float32), value_rows])
    doc_pad = jnp.concatenate([jnp.full((WINDOW,), -1, jnp.int32), doc_row.astype(jnp.int32)])

    def one_block(block_index):
        row_start = (block_index * block_rows).astype(jnp.int32)
        query_block = lax.dynamic_slice_in_dim(query_rot, row_start, block_rows, 0)
        key_block = lax.dynamic_slice_in_dim(key_pad, row_start, WINDOW + block_rows, 0)
        value_block = lax.dynamic_slice_in_dim(value_pad, row_start, WINDOW + block_rows, 0)
        key_docs = lax.dynamic_slice_in_dim(doc_pad, row_start, WINDOW + block_rows, 0)
        query_docs = lax.dynamic_slice_in_dim(doc_row.astype(jnp.int32), row_start, block_rows, 0)
        query_index = row_start + jnp.arange(block_rows, dtype=jnp.int32)
        key_index = row_start - WINDOW + jnp.arange(WINDOW + block_rows, dtype=jnp.int32)
        distance = query_index[:, None] - key_index[None, :]
        allowed = (distance >= 0) & (distance < WINDOW) & (key_docs[None, :] == query_docs[:, None])
        raw_scores = low_back(jnp.einsum('qhd,kd->hqk', query_block, key_block, precision=highest)) * HD ** (-0.5)
        probs = jax.nn.softmax(jnp.where(allowed[None], raw_scores, -1e+30), axis=-1)
        mixed = jnp.einsum('hqk,kd->qhd', low(probs), value_block, precision=highest)
        return mixed.reshape(block_rows, HQ * HD)
    blocks_out = lax.map(jax.checkpoint(one_block), jnp.arange(length // block_rows, dtype=jnp.int32))
    return blocks_out.reshape(length, HQ * HD)

def forward(inputs, weights, gain_all, doc_row):
    query_weight, key_weight, value_weight, out_weight, gate_weight, up_weight, down_weight = weights
    length = inputs.shape[0]
    norm_input = gain_all[0:D]
    norm_attn = gain_all[D:2 * D]
    norm_ffin = gain_all[2 * D:3 * D]
    norm_ffout = gain_all[3 * D:4 * D]
    norm_query = gain_all[4 * D:4 * D + HD]
    norm_key = gain_all[4 * D + HD:4 * D + 2 * HD]
    angles = angles_of(positions(doc_row))
    normed = low(rms_norm(inputs, norm_input))
    query_proj = low_back(matmul(normed, query_weight)).reshape(length, HQ, HD)
    key_proj = low_back(matmul(normed, key_weight))
    value_rows = low(low_back(matmul(normed, value_weight)))
    query_rot = low(rotate(rms_norm(query_proj, norm_query), angles[:, None, :]))
    key_rot = low(rotate(rms_norm(key_proj, norm_key), angles))
    attended = low(low_back(attend(query_rot, key_rot, value_rows, doc_row)))
    attn_out = low_back(matmul(attended, out_weight))
    middle = inputs + rms_norm(attn_out, norm_attn)
    normed_two = low(rms_norm(middle, norm_ffin))
    gate_proj = low_back(matmul(normed_two, gate_weight))
    up_proj = low_back(matmul(normed_two, up_weight))
    hidden = low(jax.nn.gelu(gate_proj, approximate=True) * up_proj)
    ffn_out = low_back(matmul(hidden, down_weight))
    return middle + rms_norm(ffn_out, norm_ffout)

def adam_update(gradient, first_old, second_old, params_old, rate, decay_rate):
    first_new = beta_first * first_old + (1.0 - beta_first) * gradient
    second_new = beta_second * second_old + (1.0 - beta_second) * gradient * gradient
    first_hat = first_new / (1.0 - beta_first ** STEP)
    second_hat = second_new / (1.0 - beta_second ** STEP)
    params_new = params_old - rate * (first_hat / (jnp.sqrt(second_hat) + adam_floor) + decay_rate * params_old)
    return (first_new, second_new, params_new)

def reference(tokens, doc_ids, cotangent, master, first_moment, second_moment, gains, gain_first, gain_second):
    weights = split_weights(low(master))
    inputs_all = tokens.astype(jnp.float32).reshape(N_DP, SEQ_LEN, D)
    upstream = cotangent.astype(jnp.float32).reshape(N_DP, SEQ_LEN, D)

    def one_sequence(carry, item):
        inputs, grad_out, doc_row = item

        def run(inputs_value, weights_value, gains_value):
            return forward(inputs_value, weights_value, gains_value, doc_row)
        outputs, backward = jax.vjp(run, inputs, weights, gains)
        grad_in, grad_weights, grad_gains = backward(grad_out)
        summed = tuple((running + adding for running, adding in zip(carry[0], grad_weights)))
        return ((summed, carry[1] + grad_gains), (outputs.astype(jnp.bfloat16), grad_in.astype(jnp.bfloat16)))
    start_carry = (tuple((jnp.zeros_like(weight_piece) for weight_piece in weights)), jnp.zeros_like(gains))
    (grad_weights, grad_gains), (outputs, grad_in) = lax.scan(one_sequence, start_carry, (inputs_all, upstream, doc_ids))
    grad_flat = join_grads(grad_weights)
    moment_first, moment_second, master_new = adam_update(grad_flat, first_moment, second_moment, master, learn_rate, weight_decay)
    gain_moment_first, gain_moment_second, gains_new = adam_update(grad_gains, gain_first, gain_second, gains, gain_rate, 0.0)
    return (outputs.reshape(TOKENS, D), grad_in.reshape(TOKENS, D), moment_first, moment_second, master_new, gain_moment_first, gain_moment_second, gains_new)
```

```python
import jax
import jax.numpy as jnp
from jax import lax
from jax.sharding import PartitionSpec as P

D = 640
HQ = 4
HD = 256
FF = 2048
WINDOW = 512
STEP = 10
ALL_AXES = ("dp", "group")


norm_eps = 1e-06
rope_base = 10000.0
beta_first = 0.9
beta_second = 0.999
learn_rate = 0.05
gain_rate = 0.25
adam_floor = 1e-08
weight_decay = 0.1


def shifted(value, axis, steps):
    count = lax.axis_size(axis)
    initial, last = (max(0, -steps), min(count, count - steps))
    return lax.ppermute(value, axis, [(source, source + steps) for source in range(initial, last)])


def rms_norm(values, weight_vec):
    return (
        values
        * lax.rsqrt(jnp.mean(values * values, axis=-1, keepdims=True) + norm_eps)
        * (1.0 + weight_vec)
    )


def positions(doc_row):
    length = doc_row.shape[0]
    counter = jnp.arange(length, dtype=jnp.int32)
    starts_here = jnp.concatenate([jnp.ones((1,), jnp.bool_), doc_row[1:] != doc_row[:-1]])
    begins = lax.cummax(jnp.where(starts_here, counter, jnp.zeros_like(counter)), axis=0)
    return counter - begins


def angles_of(places):
    half_dim = HD // 2
    frequency = rope_base ** (-(jnp.arange(half_dim, dtype=jnp.float32) * 2.0 / HD))
    return places.astype(jnp.float32)[:, None] * frequency[None, :]


def rotate(values, angles):
    half_dim = values.shape[-1] // 2
    first_half = values[..., :half_dim]
    second_half = values[..., half_dim:]
    cosine = jnp.cos(angles)
    sine_part = jnp.sin(angles)
    return jnp.concatenate(
        [
            first_half * cosine - second_half * sine_part,
            second_half * cosine + first_half * sine_part,
        ],
        axis=-1,
    )


def geglu(gate_in, up_in):
    return jax.nn.gelu(gate_in, approximate=True) * up_in


def adam_update(gradient, first_old, second_old, params_old, rate, decay_rate):
    first_new = beta_first * first_old + (1.0 - beta_first) * gradient
    second_new = beta_second * second_old + (1.0 - beta_second) * gradient * gradient
    first_hat = first_new / (1.0 - beta_first**STEP)
    second_hat = second_new / (1.0 - beta_second**STEP)
    params_new = params_old - rate * (
        first_hat / (jnp.sqrt(second_hat) + adam_floor) + decay_rate * params_old
    )
    return (first_new, second_new, params_new)


def piece_rows(device_count):
    return [
        entries // (128 * device_count)
        for entries in (D * HQ * HD, D * HD, D * HD, HQ * HD * D, D * FF, D * FF, FF * D)
    ]


def piece_shapes():
    return [(D, HQ * HD), (D, HD), (D, HD), (HQ * HD, D), (D, FF), (D, FF), (FF, D)]


def split_rows(stacked, row_list):
    result = []
    row_start = 0
    for row_count in row_list:
        result.append(stacked[row_start : row_start + row_count])
        row_start = row_start + row_count
    return result


def matmul(left_side, right_side):
    return jnp.dot(left_side, right_side, preferred_element_type=jnp.float32)


LOW_COUNT = 8


def aligned(device_count):
    return device_count % LOW_COUNT == 0 and D % device_count == 0


def swap(value, mask):
    count = lax.axis_size(ALL_AXES)
    return lax.ppermute(value, ALL_AXES, [(source, source ^ mask) for source in range(count)])


def gather_high(rows):
    high_count = lax.axis_size(ALL_AXES) // LOW_COUNT
    high = lax.axis_index(ALL_AXES) // LOW_COUNT
    parts = [rows] + [swap(rows, step * LOW_COUNT) for step in range(1, high_count)]
    return jnp.stack([lax.select_n(high ^ place, *parts) for place in range(high_count)])


def scatter_high(blocks):
    high_count = blocks.shape[0]
    high = lax.axis_index(ALL_AXES) // LOW_COUNT
    total = lax.dynamic_index_in_dim(blocks, high, 0, keepdims=False).astype(jnp.float32)
    sends = [
        lax.dynamic_index_in_dim(blocks, high ^ step, 0, keepdims=False)
        for step in range(1, high_count)
    ]
    for step, send in enumerate(sends, start=1):
        total = total + swap(send, step * LOW_COUNT).astype(jnp.float32)
    return total


def gather_relative(block, masks):
    for mask in masks:
        block = jnp.concatenate([block, swap(block, mask)], axis=0)
    return block


def scatter_relative(total, masks):
    for mask in masks:
        half = total.shape[0] // 2
        total = total[:half] + swap(total[half:].astype(jnp.bfloat16), mask).astype(jnp.float32)
    return total


def gather_placed(block, masks):
    low = lax.axis_index(ALL_AXES) % LOW_COUNT
    high_count, rows, columns = block.shape
    block = block.reshape(high_count, 1, 1, 1, rows, columns)
    for mask in masks:
        axis = {4: 1, 2: 2, 1: 3}[mask]
        other = swap(block, mask)
        block = jnp.where(
            (low & mask) == 0,
            jnp.concatenate([block, other], axis=axis),
            jnp.concatenate([other, block], axis=axis),
        )
    return block.reshape(high_count * LOW_COUNT * rows, columns)


def scatter_placed(total, high_count, masks):
    low = lax.axis_index(ALL_AXES) % LOW_COUNT
    columns = total.shape[1]
    rows = total.shape[0] // (high_count * LOW_COUNT)
    total = total.reshape(high_count, 2, 2, 2, rows, columns)
    for mask in masks:
        axis = {4: 1, 2: 2, 1: 3}[mask]
        bit = jnp.where((low & mask) == 0, 0, 1)
        send = lax.dynamic_index_in_dim(total, 1 - bit, axis).astype(jnp.bfloat16)
        total = lax.dynamic_index_in_dim(total, bit, axis) + swap(send, mask).astype(jnp.float32)
    return total.reshape(high_count, rows, columns)


RELATIVE_MASKS = (4, 2, 1)
PLACED_MASKS = (2, 4, 1)


def width_order(device_count):
    low = lax.axis_index(ALL_AXES) % LOW_COUNT
    rows = D // device_count
    high_count = device_count // LOW_COUNT
    column = jnp.arange(D, dtype=jnp.int32)
    place = column // (rows * high_count)
    mask = (place & 1) * RELATIVE_MASKS[0]
    mask = mask + ((place >> 1) & 1) * RELATIVE_MASKS[1] + (place >> 2) * RELATIVE_MASKS[2]
    high = (column // rows) % high_count
    picked = (high * LOW_COUNT + (low ^ mask)) * rows + column % rows
    return (jnp.arange(D, dtype=jnp.int32)[:, None] == picked[None, :]).astype(jnp.float32)


def gather_weights(master, device_count):
    shard_parts = [
        part_rows.astype(jnp.bfloat16) for part_rows in split_rows(master, piece_rows(device_count))
    ]
    if not aligned(device_count):
        full = [
            lax.all_gather(part, ALL_AXES, axis=0, tiled=True).reshape(shape_pair)
            for part, shape_pair in zip(shard_parts, piece_shapes())
        ]
        return (
            jnp.concatenate(full[0:3], axis=1),
            full[3],
            jnp.concatenate(full[4:6], axis=1),
            full[6],
            None,
        )
    block_width = D // LOW_COUNT
    high_count = device_count // LOW_COUNT
    rows = piece_rows(device_count)

    def high_pieces(first, last):
        stacked = gather_high(jnp.concatenate(shard_parts[first:last], axis=0))
        result = []
        row_start = 0
        for row_count in rows[first:last]:
            result.append(stacked[:, row_start : row_start + row_count])
            row_start = row_start + row_count
        return result

    query, key, value, out = high_pieces(0, 4)
    gate, up, down = high_pieces(4, 7)
    qkv = jnp.concatenate([piece.reshape(block_width, -1) for piece in (query, key, value)], axis=1)
    gate_up = jnp.concatenate([piece.reshape(block_width, -1) for piece in (gate, up)], axis=1)
    return (
        gather_relative(qkv, RELATIVE_MASKS),
        gather_placed(out.reshape(high_count, -1, D), PLACED_MASKS),
        gather_relative(gate_up, RELATIVE_MASKS),
        gather_placed(down.reshape(high_count, -1, D), PLACED_MASKS),
        width_order(device_count),
    )


def scatter_weights(wide, tall, wide_columns, device_count):
    splits = [sum(wide_columns[:count]) for count in range(1, len(wide_columns))]
    if not aligned(device_count):
        pieces = jnp.split(wide, splits, axis=1) + [tall]
        return jnp.concatenate(
            [
                lax.psum_scatter(
                    piece.reshape(-1, 128), ALL_AXES, scatter_dimension=0, tiled=True
                )
                for piece in pieces
            ],
            axis=0,
        )
    high_count = device_count // LOW_COUNT
    wide = scatter_relative(wide, RELATIVE_MASKS[::-1]).astype(jnp.bfloat16)
    tall = scatter_placed(tall, high_count, PLACED_MASKS[::-1]).astype(jnp.bfloat16)
    flat = [
        piece.reshape(high_count, -1, 128) for piece in jnp.split(wide, splits, axis=1) + [tall]
    ]
    return scatter_high(jnp.concatenate(flat, axis=1))


def sum_gains(values, device_count):
    if not aligned(device_count):
        return lax.psum(values, ALL_AXES)
    values = values.reshape(-1, 128)
    mask = 1
    while mask < device_count:
        values = values + swap(values, mask)
        mask = mask * 2
    return values.reshape(-1)


def shards(
    tokens, doc_ids, cotangent, master, first_moment, second_moment, gains, gain_first, gain_second
):
    group_size = lax.axis_size("group")
    devices_all = lax.axis_size("dp") * group_size
    group_index = lax.axis_index("group")
    local_rows = tokens.shape[0]
    qkv_weight, out_weight, gate_up_weight, down_weight, order = gather_weights(
        master, devices_all
    )
    norm_input = gains[0:D]
    norm_attn = gains[D : 2 * D]
    norm_ffin = gains[2 * D : 3 * D]
    norm_ffout = gains[3 * D : 4 * D]
    norm_query = gains[4 * D : 4 * D + HD]
    norm_key = gains[4 * D + HD : 4 * D + 2 * HD]
    doc_row = doc_ids[0]
    first_row = group_index * local_rows
    angles = lax.dynamic_slice_in_dim(angles_of(positions(doc_row)), first_row, local_rows, 0)
    query_docs = lax.dynamic_slice_in_dim(doc_row, first_row, local_rows, 0)

    def ordered(rows_low):
        if order is None:
            return rows_low
        return matmul(rows_low, order.astype(jnp.bfloat16)).astype(jnp.bfloat16)

    def restored(rows_in):
        if order is None:
            return rows_in
        return jnp.einsum("te,de->td", rows_in, order, precision=lax.Precision.HIGHEST)

    inputs = tokens.astype(jnp.float32)
    normed, back_input = jax.vjp(rms_norm, inputs, norm_input)
    normed_low = normed.astype(jnp.bfloat16)
    normed_low = ordered(normed_low)
    projections = matmul(normed_low, qkv_weight)
    query_proj = projections[:, : HQ * HD]
    key_proj = projections[:, HQ * HD : HQ * HD + HD]
    value_proj = projections[:, HQ * HD + HD :]

    def query_prep(flat_rows, gain_vec):
        return rotate(rms_norm(flat_rows.reshape(local_rows, HQ, HD), gain_vec), angles[:, None, :])

    def key_prep(rows_in, gain_vec):
        return rotate(rms_norm(rows_in, gain_vec), angles)

    query_rot, back_query = jax.vjp(query_prep, query_proj, norm_query)
    key_rot, back_key = jax.vjp(key_prep, key_proj, norm_key)
    query_low = query_rot.astype(jnp.bfloat16)
    key_low = key_rot.astype(jnp.bfloat16)
    value_low = value_proj.astype(jnp.bfloat16)
    reach = min(-(-(WINDOW - 1) // local_rows), group_size - 1)
    key_value = jnp.concatenate([key_low, value_low], axis=1)
    key_value_list = [key_value]
    for offset in range(1, reach + 1):
        key_value_list.insert(0, shifted(key_value, "group", offset))
    key_value_all = jnp.concatenate(key_value_list, axis=0)
    key_all = key_value_all[:, :HD]
    value_all = key_value_all[:, HD:]
    key_count = (reach + 1) * local_rows
    doc_pad = jnp.concatenate([jnp.full((reach * local_rows,), -1, jnp.int32), doc_row])
    key_docs = lax.dynamic_slice_in_dim(doc_pad, first_row, key_count, 0)
    key_index = (group_index - reach) * local_rows + jnp.arange(key_count, dtype=jnp.int32)
    query_index = first_row + jnp.arange(local_rows, dtype=jnp.int32)
    distance = query_index[:, None] - key_index[None, :]
    allowed = (distance >= 0) & (distance < WINDOW) & (key_docs[None, :] == query_docs[:, None])

    def scores_of(key_rows_low):
        raw_scores = jnp.einsum(
            "qhd,kd->hqk", query_low, key_rows_low, preferred_element_type=jnp.float32
        ) * HD ** (-0.5)
        return jnp.where(allowed[None], raw_scores, -1e30)

    masked = scores_of(key_all)
    top_score = jnp.max(masked, axis=-1, keepdims=True)
    log_total = top_score + jnp.log(jnp.sum(jnp.exp(masked - top_score), axis=-1, keepdims=True))
    probs = jnp.exp(masked - log_total)
    attended = jnp.einsum(
        "hqk,kd->qhd", probs.astype(jnp.bfloat16), value_all, preferred_element_type=jnp.float32
    )
    attended_low = attended.reshape(local_rows, HQ * HD).astype(jnp.bfloat16)
    attn_out = matmul(attended_low, out_weight)
    branch_one, back_attn = jax.vjp(rms_norm, attn_out, norm_attn)
    middle = inputs + branch_one
    normed_two, back_ffin = jax.vjp(rms_norm, middle, norm_ffin)
    normed_two_low = normed_two.astype(jnp.bfloat16)
    normed_two_low = ordered(normed_two_low)
    gate_up_proj = matmul(normed_two_low, gate_up_weight)
    gate_proj = gate_up_proj[:, :FF]
    up_proj = gate_up_proj[:, FF:]
    hidden, back_hidden = jax.vjp(geglu, gate_proj, up_proj)
    hidden_low = hidden.astype(jnp.bfloat16)
    ffn_out = matmul(hidden_low, down_weight)
    branch_two, back_ffout = jax.vjp(rms_norm, ffn_out, norm_ffout)
    outputs = middle + branch_two
    grad_out = cotangent.astype(jnp.float32)
    grad_ffn, grad_gain_ffout = back_ffout(grad_out)
    grad_ffn_low = grad_ffn.astype(jnp.bfloat16)
    grad_down_w = jnp.einsum(
        "tf,td->fd", hidden_low, grad_ffn_low, preferred_element_type=jnp.float32
    )
    grad_hidden = jnp.einsum(
        "td,fd->tf", grad_ffn_low, down_weight, preferred_element_type=jnp.float32
    )
    grad_gate, grad_up = back_hidden(grad_hidden)
    grad_gate_up_low = jnp.concatenate([grad_gate, grad_up], axis=1).astype(jnp.bfloat16)
    grad_gate_up_w = jnp.einsum(
        "td,tf->df", normed_two_low, grad_gate_up_low, preferred_element_type=jnp.float32
    )
    grads_ffn = scatter_weights(grad_gate_up_w, grad_down_w, (FF, FF), devices_all)
    grad_normed_two = restored(
        jnp.einsum(
            "tf,df->td", grad_gate_up_low, gate_up_weight, preferred_element_type=jnp.float32
        )
    )
    grad_middle_norm, grad_gain_ffin = back_ffin(grad_normed_two)
    grad_middle = grad_out + grad_middle_norm
    grad_attn, grad_gain_attn = back_attn(grad_middle)
    grad_attn_low = grad_attn.astype(jnp.bfloat16)
    grad_out_w = jnp.einsum(
        "to,td->od", attended_low, grad_attn_low, preferred_element_type=jnp.float32
    )
    grad_attended = jnp.einsum(
        "td,od->to", grad_attn_low, out_weight, preferred_element_type=jnp.float32
    )
    grad_attended_low = grad_attended.astype(jnp.bfloat16).reshape(local_rows, HQ, HD)
    probs_again = jnp.exp(scores_of(key_all) - log_total)
    grad_probs = jnp.einsum(
        "qhd,kd->hqk", grad_attended_low, value_all, preferred_element_type=jnp.float32
    )
    grad_value_all = jnp.einsum(
        "hqk,qhd->kd",
        probs_again.astype(jnp.bfloat16),
        grad_attended_low,
        preferred_element_type=jnp.float32,
    )
    grad_scores = probs_again * (
        grad_probs - jnp.sum(probs_again * grad_probs, axis=-1, keepdims=True)
    )
    grad_scores_low = (grad_scores * HD ** (-0.5)).astype(jnp.bfloat16)
    grad_query = jnp.einsum(
        "hqk,kd->qhd", grad_scores_low, key_all, preferred_element_type=jnp.float32
    )
    grad_key_all = jnp.einsum(
        "hqk,qhd->kd", grad_scores_low, query_low, preferred_element_type=jnp.float32
    )
    grad_both_all = jnp.concatenate([grad_key_all, grad_value_all], axis=1)
    both_total = grad_both_all[reach * local_rows :]
    for offset in range(1, reach + 1):
        row_start = (reach - offset) * local_rows
        both_total = both_total + shifted(
            grad_both_all[row_start : row_start + local_rows].astype(jnp.bfloat16),
            "group",
            -offset,
        ).astype(jnp.float32)
    key_total = both_total[:, :HD]
    value_total = both_total[:, HD:]
    grad_query_proj, grad_gain_query = back_query(grad_query)
    grad_key_proj, grad_gain_key = back_key(key_total)
    grad_qkv_low = jnp.concatenate([grad_query_proj, grad_key_proj, value_total], axis=1).astype(
        jnp.bfloat16
    )
    grad_qkv_w = jnp.einsum(
        "td,te->de", normed_low, grad_qkv_low, preferred_element_type=jnp.float32
    )
    grads_attn = scatter_weights(grad_qkv_w, grad_out_w, (HQ * HD, HD, HD), devices_all)
    grad_normed = restored(
        jnp.einsum("te,de->td", grad_qkv_low, qkv_weight, preferred_element_type=jnp.float32)
    )
    grad_input_norm, grad_gain_input = back_input(grad_normed)
    grad_inputs = grad_middle + grad_input_norm
    grads_local = jnp.concatenate([grads_attn, grads_ffn], axis=0)
    gain_grads = sum_gains(
        jnp.concatenate(
            [
                grad_gain_input,
                grad_gain_attn,
                grad_gain_ffin,
                grad_gain_ffout,
                grad_gain_query,
                grad_gain_key,
            ]
        ),
        devices_all,
    )
    moment_first, moment_second, master_new = adam_update(
        grads_local, first_moment, second_moment, master, learn_rate, weight_decay
    )
    gain_moment_first, gain_moment_second, gains_new = adam_update(
        gain_grads, gain_first, gain_second, gains, gain_rate, 0.0
    )
    return (
        outputs.astype(jnp.bfloat16),
        grad_inputs.astype(jnp.bfloat16),
        moment_first,
        moment_second,
        master_new,
        gain_moment_first,
        gain_moment_second,
        gains_new,
    )


def solution(mesh):
    placed = (
        P(("dp", "group"), None),
        P("dp", None),
        P(("dp", "group"), None),
        P(("dp", "group"), None),
        P(("dp", "group"), None),
        P(("dp", "group"), None),
        P(),
        P(),
        P(),
    )
    return jax.shard_map(
        shards,
        mesh=mesh,
        in_specs=placed,
        out_specs=(
            P(("dp", "group"), None),
            P(("dp", "group"), None),
            P(("dp", "group"), None),
            P(("dp", "group"), None),
            P(("dp", "group"), None),
            P(),
            P(),
            P(),
        ),
        check_vma=False,
    )
```

```python
import functools
import math

import jax
import jax.numpy as jnp
from jax import lax
from jax.experimental import pallas as pl
from jax.experimental.pallas import tpu as pltpu
from jax.sharding import PartitionSpec as P

D = 640
HQ = 4
HD = 256
FF = 2048
WINDOW = 512
STEP = 10
ALL_AXES = ("dp", "group")


norm_eps = 1e-06
rope_base = 10000.0
beta_first = 0.9
beta_second = 0.999
learn_rate = 0.05
gain_rate = 0.25
adam_floor = 1e-08
weight_decay = 0.1


def shifted(value, axis, steps):
    count = lax.axis_size(axis)
    initial, last = (max(0, -steps), min(count, count - steps))
    return lax.ppermute(value, axis, [(source, source + steps) for source in range(initial, last)])


def rms_norm(values, weight_vec):
    return (
        values
        * lax.rsqrt(jnp.mean(values * values, axis=-1, keepdims=True) + norm_eps)
        * (1.0 + weight_vec)
    )


def positions(doc_row):
    length = doc_row.shape[0]
    counter = jnp.arange(length, dtype=jnp.int32)
    starts_here = jnp.concatenate([jnp.ones((1,), jnp.bool_), doc_row[1:] != doc_row[:-1]])
    begins = lax.cummax(jnp.where(starts_here, counter, jnp.zeros_like(counter)), axis=0)
    return counter - begins


def angles_of(places):
    half_dim = HD // 2
    frequency = rope_base ** (-(jnp.arange(half_dim, dtype=jnp.float32) * 2.0 / HD))
    return places.astype(jnp.float32)[:, None] * frequency[None, :]


def rotate(values, angles):
    half_dim = values.shape[-1] // 2
    first_half = values[..., :half_dim]
    second_half = values[..., half_dim:]
    cosine = jnp.cos(angles)
    sine_part = jnp.sin(angles)
    return jnp.concatenate(
        [
            first_half * cosine - second_half * sine_part,
            second_half * cosine + first_half * sine_part,
        ],
        axis=-1,
    )


def geglu(gate_in, up_in):
    return jax.nn.gelu(gate_in, approximate=True) * up_in


def adam_update(gradient, first_old, second_old, params_old, rate, decay_rate):
    first_new = beta_first * first_old + (1.0 - beta_first) * gradient
    second_new = beta_second * second_old + (1.0 - beta_second) * gradient * gradient
    first_hat = first_new / (1.0 - beta_first**STEP)
    second_hat = second_new / (1.0 - beta_second**STEP)
    params_new = params_old - rate * (
        first_hat / (jnp.sqrt(second_hat) + adam_floor) + decay_rate * params_old
    )
    return (first_new, second_new, params_new)


def piece_rows(device_count):
    return [
        entries // (128 * device_count)
        for entries in (D * HQ * HD, D * HD, D * HD, HQ * HD * D, D * FF, D * FF, FF * D)
    ]


def piece_shapes():
    return [(D, HQ * HD), (D, HD), (D, HD), (HQ * HD, D), (D, FF), (D, FF), (FF, D)]


def split_rows(stacked, row_list):
    result = []
    row_start = 0
    for row_count in row_list:
        result.append(stacked[row_start : row_start + row_count])
        row_start = row_start + row_count
    return result


def matmul(left_side, right_side):
    return jnp.dot(left_side, right_side, preferred_element_type=jnp.float32)


LOW_COUNT = 8
LANES = 128
LOW_MASKS = (0, 4, 2, 6, 1, 5, 3, 7)
VMEM_BYTES = 56 * 1024 * 1024


def aligned(device_count):
    return device_count % LOW_COUNT == 0 and D % device_count == 0


def swap(value, mask):
    count = lax.axis_size(ALL_AXES)
    return lax.ppermute(value, ALL_AXES, [(source, source ^ mask) for source in range(count)])


def local_call(kernel, outs, operands, scratch=(), flops=0):
    specs = [pl.BlockSpec(memory_space=pltpu.SMEM)]
    specs = specs + [pl.BlockSpec(memory_space=pltpu.VMEM)] * len(operands)
    moved = sum(math.prod(value.shape) * value.dtype.itemsize for value in (*operands, *outs))
    return pl.pallas_call(
        kernel,
        out_shape=outs,
        in_specs=specs,
        out_specs=tuple(pl.BlockSpec(memory_space=pltpu.VMEM) for _ in outs),
        scratch_shapes=scratch,
        compiler_params=pltpu.CompilerParams(vmem_limit_bytes=VMEM_BYTES),
        cost_estimate=pl.CostEstimate(flops=flops, bytes_accessed=moved, transcendentals=0),
    )(lax.axis_index(ALL_AXES).astype(jnp.int32).reshape(1), *operands)


class Piece:
    def __init__(self, rows, columns, device_count):
        self.rows = rows
        self.columns = columns
        self.wide = rows == D
        self.blocks = columns // LANES
        self.own_rows = rows // device_count
        self.flat_rows = self.own_rows * self.blocks
        self.high_count = device_count // LOW_COUNT
        self.block_rows = self.own_rows * self.high_count
        self.size = self.block_rows * self.blocks


def pack_kernel(pieces, index_ref, *refs):
    high_count = pieces[0].high_count
    parts, out_ref, flat, packed = refs[:high_count], refs[-3], refs[-2], refs[-1]
    high = index_ref[0] // LOW_COUNT
    for step, part in enumerate(parts):
        flat[high ^ step] = part[...].astype(jnp.float32)
    start, target = 0, 0
    for piece in pieces:
        for block in range(piece.blocks):
            for place in range(high_count):
                packed[pl.ds(target, piece.own_rows), :] = flat[
                    place, pl.ds(start + block, piece.own_rows, stride=piece.blocks), :
                ]
                target = target + piece.own_rows
        start = start + piece.flat_rows
    out_ref[...] = packed[...].astype(jnp.bfloat16)


def unpack_kernel(pieces, index_ref, *refs):
    high_count = pieces[0].high_count
    terms, outs, flat, packed = refs[:3], refs[3:-2], refs[-2], refs[-1]
    high = index_ref[0] // LOW_COUNT
    packed[...] = sum(term[...].astype(jnp.float32) for term in terms)
    start, source = 0, 0
    for piece in pieces:
        for block in range(piece.blocks):
            for place in range(high_count):
                flat[place, pl.ds(start + block, piece.own_rows, stride=piece.blocks), :] = packed[
                    pl.ds(source, piece.own_rows), :
                ]
                source = source + piece.own_rows
        start = start + piece.flat_rows
    for step, out_ref in enumerate(outs):
        out_ref[...] = flat[high ^ step].astype(out_ref.dtype)


def assemble_kernel(pieces, index_ref, near_ref, far_ref, *out_refs):
    low = index_ref[0] % LOW_COUNT
    size = sum(piece.size for piece in pieces)
    for order, mask in enumerate(LOW_MASKS):
        source = near_ref if order < 4 else far_ref
        start = (order % 4) * size
        for piece, out_ref in zip(pieces, out_refs):
            for block in range(piece.blocks):
                columns = slice(block * LANES, (block + 1) * LANES)
                if piece.wide:
                    out_ref[order * piece.block_rows : (order + 1) * piece.block_rows, columns] = (
                        source[start : start + piece.block_rows, :]
                    )
                else:
                    for place in range(piece.high_count):
                        row = (place * LOW_COUNT + (low ^ mask)) * piece.own_rows
                        first = start + place * piece.own_rows
                        out_ref[
                            pl.ds(pl.multiple_of(row, piece.own_rows), piece.own_rows), columns
                        ] = source[first : first + piece.own_rows, :]
                start = start + piece.block_rows


def split_kernel(pieces, index_ref, *refs):
    in_refs, near_ref, far_ref = refs[:-2], refs[-2], refs[-1]
    low = index_ref[0] % LOW_COUNT
    size = sum(piece.size for piece in pieces)
    for order, mask in enumerate(LOW_MASKS):
        target = near_ref if order < 4 else far_ref
        start = (order % 4) * size
        for piece, in_ref in zip(pieces, in_refs):
            for block in range(piece.blocks):
                columns = slice(block * LANES, (block + 1) * LANES)
                if piece.wide:
                    target[start : start + piece.block_rows, :] = in_ref[
                        order * piece.block_rows : (order + 1) * piece.block_rows, columns
                    ].astype(jnp.bfloat16)
                else:
                    for place in range(piece.high_count):
                        row = (place * LOW_COUNT + (low ^ mask)) * piece.own_rows
                        first = start + place * piece.own_rows
                        target[first : first + piece.own_rows, :] = in_ref[
                            pl.ds(pl.multiple_of(row, piece.own_rows), piece.own_rows), columns
                        ].astype(jnp.bfloat16)
                start = start + piece.block_rows


def array(shape, kind):
    return jax.ShapeDtypeStruct(shape, kind)


def gather_blocks(pieces, rows):
    high_count = pieces[0].high_count
    size = sum(piece.size for piece in pieces)
    parts = [rows] + [swap(rows, step * LOW_COUNT) for step in range(1, high_count)]
    (own,) = local_call(
        functools.partial(pack_kernel, pieces),
        (array((size, LANES), jnp.bfloat16),),
        parts,
        (
            pltpu.VMEM((high_count, rows.shape[0], LANES), jnp.float32),
            pltpu.VMEM((size, LANES), jnp.float32),
        ),
    )
    beside, across = swap(own, 4), swap(own, 2)
    half = size // 2
    near = jnp.concatenate([own, beside, across, swap(across[:half], 4), swap(beside[half:], 2)])
    return near, swap(near, 1)


def assemble(pieces, near, far):
    return local_call(
        functools.partial(assemble_kernel, pieces),
        tuple(array((piece.rows, piece.columns), jnp.bfloat16) for piece in pieces),
        (near, far),
    )


def scatter_blocks(pieces, gradients):
    high_count = pieces[0].high_count
    size = sum(piece.size for piece in pieces)
    flat_rows = sum(piece.flat_rows for piece in pieces)
    near, far = local_call(
        functools.partial(split_kernel, pieces),
        (array((4 * size, LANES), jnp.bfloat16),) * 2,
        gradients,
    )
    total = near.astype(jnp.float32) + swap(far, 1).astype(jnp.float32)
    half = size // 2
    diagonal = total[3 * size :].astype(jnp.bfloat16)
    across = total[2 * size : 3 * size]
    beside = total[size : 2 * size]
    over_x = swap(diagonal[:half], 4).astype(jnp.float32)
    over_y = swap(diagonal[half:], 2).astype(jnp.float32)
    across = jnp.concatenate([across[:half] + over_x, across[half:]]).astype(jnp.bfloat16)
    beside = jnp.concatenate([beside[:half], beside[half:] + over_y]).astype(jnp.bfloat16)
    outs = local_call(
        functools.partial(unpack_kernel, pieces),
        (array((flat_rows, LANES), jnp.float32),)
        + (array((flat_rows, LANES), jnp.bfloat16),) * (high_count - 1),
        (total[:size], swap(beside, 4), swap(across, 2)),
        (
            pltpu.VMEM((high_count, flat_rows, LANES), jnp.float32),
            pltpu.VMEM((size, LANES), jnp.float32),
        ),
    )
    return outs[0] + sum(
        swap(send, step * LOW_COUNT).astype(jnp.float32) for step, send in enumerate(outs) if step
    )


def width_order(device_count):
    low = lax.axis_index(ALL_AXES) % LOW_COUNT
    rows = D // device_count
    high_count = device_count // LOW_COUNT
    column = jnp.arange(D, dtype=jnp.int32)
    place = column // (rows * high_count)
    mask = (place & 1) * 4 + ((place >> 1) & 1) * 2 + (place >> 2)
    high = (column // rows) % high_count
    picked = (high * LOW_COUNT + (low ^ mask)) * rows + column % rows
    return (jnp.arange(D, dtype=jnp.int32)[:, None] == picked[None, :]).astype(jnp.float32)


def gather_weights(master, device_count):
    shard_parts = [
        part_rows.astype(jnp.bfloat16) for part_rows in split_rows(master, piece_rows(device_count))
    ]
    if not aligned(device_count):
        full = [
            lax.all_gather(part, ALL_AXES, axis=0, tiled=True).reshape(shape_pair)
            for part, shape_pair in zip(shard_parts, piece_shapes())
        ]
        return full, None
    pieces = [Piece(*shape_pair, device_count) for shape_pair in piece_shapes()]
    full = []
    for first, last in CHUNKS:
        near, far = gather_blocks(pieces[first:last], jnp.concatenate(shard_parts[first:last]))
        full.extend(assemble(pieces[first:last], near, far))
    return full, width_order(device_count)


CHUNKS = ((0, 4), (4, 6), (6, 7))


def scatter_weights(gradients, device_count, chunk):
    if not aligned(device_count):
        return jnp.concatenate(
            [
                lax.psum_scatter(
                    piece.reshape(-1, 128), ALL_AXES, scatter_dimension=0, tiled=True
                )
                for piece in gradients
            ],
            axis=0,
        )
    pieces = [Piece(*shape_pair, device_count) for shape_pair in piece_shapes()[slice(*chunk)]]
    return scatter_blocks(pieces, [gradient.astype(jnp.bfloat16) for gradient in gradients])


def sum_gains(values, device_count):
    if not aligned(device_count):
        return lax.psum(values, ALL_AXES)
    values = values.reshape(-1, 128)
    mask = 1
    while mask < device_count:
        values = values + swap(values, mask)
        mask = mask * 2
    return values.reshape(-1)


def shards(
    tokens, doc_ids, cotangent, master, first_moment, second_moment, gains, gain_first, gain_second
):
    group_size = lax.axis_size("group")
    devices_all = lax.axis_size("dp") * group_size
    group_index = lax.axis_index("group")
    local_rows = tokens.shape[0]
    weights, order = gather_weights(master, devices_all)
    query_weight, key_weight, value_weight, out_weight, gate_weight, up_weight, down_weight = weights
    norm_input = gains[0:D]
    norm_attn = gains[D : 2 * D]
    norm_ffin = gains[2 * D : 3 * D]
    norm_ffout = gains[3 * D : 4 * D]
    norm_query = gains[4 * D : 4 * D + HD]
    norm_key = gains[4 * D + HD : 4 * D + 2 * HD]
    doc_row = doc_ids[0]
    first_row = group_index * local_rows
    angles = lax.dynamic_slice_in_dim(angles_of(positions(doc_row)), first_row, local_rows, 0)
    query_docs = lax.dynamic_slice_in_dim(doc_row, first_row, local_rows, 0)

    def ordered(rows_low):
        if order is None:
            return rows_low
        return matmul(rows_low, order.astype(jnp.bfloat16)).astype(jnp.bfloat16)

    def restored(rows_in):
        if order is None:
            return rows_in
        return jnp.einsum("te,de->td", rows_in, order, precision=lax.Precision.HIGHEST)

    inputs = tokens.astype(jnp.float32)
    normed, back_input = jax.vjp(rms_norm, inputs, norm_input)
    normed_low = normed.astype(jnp.bfloat16)
    normed_low = ordered(normed_low)
    query_proj = matmul(normed_low, query_weight)
    key_proj = matmul(normed_low, key_weight)
    value_proj = matmul(normed_low, value_weight)

    def query_prep(flat_rows, gain_vec):
        return rotate(rms_norm(flat_rows.reshape(local_rows, HQ, HD), gain_vec), angles[:, None, :])

    def key_prep(rows_in, gain_vec):
        return rotate(rms_norm(rows_in, gain_vec), angles)

    query_rot, back_query = jax.vjp(query_prep, query_proj, norm_query)
    key_rot, back_key = jax.vjp(key_prep, key_proj, norm_key)
    query_low = query_rot.astype(jnp.bfloat16)
    key_low = key_rot.astype(jnp.bfloat16)
    value_low = value_proj.astype(jnp.bfloat16)
    reach = min(-(-(WINDOW - 1) // local_rows), group_size - 1)
    key_value = jnp.concatenate([key_low, value_low], axis=1)
    key_value_list = [key_value]
    for offset in range(1, reach + 1):
        key_value_list.insert(0, shifted(key_value, "group", offset))
    key_value_all = jnp.concatenate(key_value_list, axis=0)
    key_all = key_value_all[:, :HD]
    value_all = key_value_all[:, HD:]
    key_count = (reach + 1) * local_rows
    doc_pad = jnp.concatenate([jnp.full((reach * local_rows,), -1, jnp.int32), doc_row])
    key_docs = lax.dynamic_slice_in_dim(doc_pad, first_row, key_count, 0)
    key_index = (group_index - reach) * local_rows + jnp.arange(key_count, dtype=jnp.int32)
    query_index = first_row + jnp.arange(local_rows, dtype=jnp.int32)
    distance = query_index[:, None] - key_index[None, :]
    allowed = (distance >= 0) & (distance < WINDOW) & (key_docs[None, :] == query_docs[:, None])

    def scores_of(key_rows_low):
        raw_scores = jnp.einsum(
            "qhd,kd->hqk", query_low, key_rows_low, preferred_element_type=jnp.float32
        ) * HD ** (-0.5)
        return jnp.where(allowed[None], raw_scores, -1e30)

    masked = scores_of(key_all)
    top_score = jnp.max(masked, axis=-1, keepdims=True)
    log_total = top_score + jnp.log(jnp.sum(jnp.exp(masked - top_score), axis=-1, keepdims=True))
    probs = jnp.exp(masked - log_total)
    attended = jnp.einsum(
        "hqk,kd->qhd", probs.astype(jnp.bfloat16), value_all, preferred_element_type=jnp.float32
    )
    attended_low = attended.reshape(local_rows, HQ * HD).astype(jnp.bfloat16)
    attn_out = matmul(attended_low, out_weight)
    branch_one, back_attn = jax.vjp(rms_norm, attn_out, norm_attn)
    middle = inputs + branch_one
    normed_two, back_ffin = jax.vjp(rms_norm, middle, norm_ffin)
    normed_two_low = normed_two.astype(jnp.bfloat16)
    normed_two_low = ordered(normed_two_low)
    gate_proj = matmul(normed_two_low, gate_weight)
    up_proj = matmul(normed_two_low, up_weight)
    hidden, back_hidden = jax.vjp(geglu, gate_proj, up_proj)
    hidden_low = hidden.astype(jnp.bfloat16)
    ffn_out = matmul(hidden_low, down_weight)
    branch_two, back_ffout = jax.vjp(rms_norm, ffn_out, norm_ffout)
    outputs = middle + branch_two
    grad_out = cotangent.astype(jnp.float32)
    grad_ffn, grad_gain_ffout = back_ffout(grad_out)
    grad_ffn_low = grad_ffn.astype(jnp.bfloat16)
    grad_down_w = jnp.einsum(
        "tf,td->fd", hidden_low, grad_ffn_low, preferred_element_type=jnp.float32
    )
    grad_hidden = jnp.einsum(
        "td,fd->tf", grad_ffn_low, down_weight, preferred_element_type=jnp.float32
    )
    grad_gate, grad_up = back_hidden(grad_hidden)
    grad_gate_low = grad_gate.astype(jnp.bfloat16)
    grad_up_low = grad_up.astype(jnp.bfloat16)
    grads_down = scatter_weights([grad_down_w], devices_all, CHUNKS[2])
    grad_gate_w = jnp.einsum(
        "td,tf->df", normed_two_low, grad_gate_low, preferred_element_type=jnp.float32
    )
    grad_up_w = jnp.einsum(
        "td,tf->df", normed_two_low, grad_up_low, preferred_element_type=jnp.float32
    )
    grads_gate_up = scatter_weights([grad_gate_w, grad_up_w], devices_all, CHUNKS[1])
    grad_normed_two = restored(
        jnp.einsum("tf,df->td", grad_gate_low, gate_weight, preferred_element_type=jnp.float32)
        + jnp.einsum("tf,df->td", grad_up_low, up_weight, preferred_element_type=jnp.float32)
    )
    grad_middle_norm, grad_gain_ffin = back_ffin(grad_normed_two)
    grad_middle = grad_out + grad_middle_norm
    grad_attn, grad_gain_attn = back_attn(grad_middle)
    grad_attn_low = grad_attn.astype(jnp.bfloat16)
    grad_out_w = jnp.einsum(
        "to,td->od", attended_low, grad_attn_low, preferred_element_type=jnp.float32
    )
    grad_attended = jnp.einsum(
        "td,od->to", grad_attn_low, out_weight, preferred_element_type=jnp.float32
    )
    grad_attended_low = grad_attended.astype(jnp.bfloat16).reshape(local_rows, HQ, HD)
    probs_again = jnp.exp(scores_of(key_all) - log_total)
    grad_probs = jnp.einsum(
        "qhd,kd->hqk", grad_attended_low, value_all, preferred_element_type=jnp.float32
    )
    grad_value_all = jnp.einsum(
        "hqk,qhd->kd",
        probs_again.astype(jnp.bfloat16),
        grad_attended_low,
        preferred_element_type=jnp.float32,
    )
    grad_scores = probs_again * (
        grad_probs - jnp.sum(probs_again * grad_probs, axis=-1, keepdims=True)
    )
    grad_scores_low = (grad_scores * HD ** (-0.5)).astype(jnp.bfloat16)
    grad_query = jnp.einsum(
        "hqk,kd->qhd", grad_scores_low, key_all, preferred_element_type=jnp.float32
    )
    grad_key_all = jnp.einsum(
        "hqk,qhd->kd", grad_scores_low, query_low, preferred_element_type=jnp.float32
    )
    grad_both_all = jnp.concatenate([grad_key_all, grad_value_all], axis=1)
    both_total = grad_both_all[reach * local_rows :]
    for offset in range(1, reach + 1):
        row_start = (reach - offset) * local_rows
        both_total = both_total + shifted(
            grad_both_all[row_start : row_start + local_rows].astype(jnp.bfloat16),
            "group",
            -offset,
        ).astype(jnp.float32)
    key_total = both_total[:, :HD]
    value_total = both_total[:, HD:]
    grad_query_proj, grad_gain_query = back_query(grad_query)
    grad_key_proj, grad_gain_key = back_key(key_total)
    grad_query_low = grad_query_proj.astype(jnp.bfloat16)
    grad_key_low = grad_key_proj.astype(jnp.bfloat16)
    grad_value_low = value_total.astype(jnp.bfloat16)
    grad_query_w = jnp.einsum(
        "td,te->de", normed_low, grad_query_low, preferred_element_type=jnp.float32
    )
    grad_key_w = jnp.einsum(
        "td,te->de", normed_low, grad_key_low, preferred_element_type=jnp.float32
    )
    grad_value_w = jnp.einsum(
        "td,te->de", normed_low, grad_value_low, preferred_element_type=jnp.float32
    )
    grads_attn = scatter_weights(
        [grad_query_w, grad_key_w, grad_value_w, grad_out_w], devices_all, CHUNKS[0]
    )
    grad_normed = restored(
        jnp.einsum("te,de->td", grad_query_low, query_weight, preferred_element_type=jnp.float32)
        + jnp.einsum("te,de->td", grad_key_low, key_weight, preferred_element_type=jnp.float32)
        + jnp.einsum("te,de->td", grad_value_low, value_weight, preferred_element_type=jnp.float32)
    )
    grad_input_norm, grad_gain_input = back_input(grad_normed)
    grad_inputs = grad_middle + grad_input_norm
    grads_local = jnp.concatenate([grads_attn, grads_gate_up, grads_down], axis=0)
    gain_grads = sum_gains(
        jnp.concatenate(
            [
                grad_gain_input,
                grad_gain_attn,
                grad_gain_ffin,
                grad_gain_ffout,
                grad_gain_query,
                grad_gain_key,
            ]
        ),
        devices_all,
    )
    moment_first, moment_second, master_new = adam_update(
        grads_local, first_moment, second_moment, master, learn_rate, weight_decay
    )
    gain_moment_first, gain_moment_second, gains_new = adam_update(
        gain_grads, gain_first, gain_second, gains, gain_rate, 0.0
    )
    return (
        outputs.astype(jnp.bfloat16),
        grad_inputs.astype(jnp.bfloat16),
        moment_first,
        moment_second,
        master_new,
        gain_moment_first,
        gain_moment_second,
        gains_new,
    )


def solution(mesh):
    placed = (
        P(("dp", "group"), None),
        P("dp", None),
        P(("dp", "group"), None),
        P(("dp", "group"), None),
        P(("dp", "group"), None),
        P(("dp", "group"), None),
        P(),
        P(),
        P(),
    )
    return jax.shard_map(
        shards,
        mesh=mesh,
        in_specs=placed,
        out_specs=(
            P(("dp", "group"), None),
            P(("dp", "group"), None),
            P(("dp", "group"), None),
            P(("dp", "group"), None),
            P(("dp", "group"), None),
            P(),
            P(),
            P(),
        ),
        check_vma=False,
    )
```

```python
import functools
import math

import jax
import jax.numpy as jnp
from jax import lax
from jax.experimental import pallas as pl
from jax.experimental.pallas import tpu as pltpu
from jax.sharding import PartitionSpec as P

D = 640
HQ = 4
HD = 256
FF = 2048
WINDOW = 512
STEP = 10
ALL_AXES = ("dp", "group")


norm_eps = 1e-06
rope_base = 10000.0
beta_first = 0.9
beta_second = 0.999
learn_rate = 0.05
gain_rate = 0.25
adam_floor = 1e-08
weight_decay = 0.1


def shifted(value, axis, steps):
    count = lax.axis_size(axis)
    initial, last = (max(0, -steps), min(count, count - steps))
    return lax.ppermute(value, axis, [(source, source + steps) for source in range(initial, last)])


def rms_norm(values, weight_vec):
    return (
        values
        * lax.rsqrt(jnp.mean(values * values, axis=-1, keepdims=True) + norm_eps)
        * (1.0 + weight_vec)
    )


def positions(doc_row):
    length = doc_row.shape[0]
    counter = jnp.arange(length, dtype=jnp.int32)
    starts_here = jnp.concatenate([jnp.ones((1,), jnp.bool_), doc_row[1:] != doc_row[:-1]])
    begins = lax.cummax(jnp.where(starts_here, counter, jnp.zeros_like(counter)), axis=0)
    return counter - begins


def angles_of(places):
    half_dim = HD // 2
    frequency = rope_base ** (-(jnp.arange(half_dim, dtype=jnp.float32) * 2.0 / HD))
    return places.astype(jnp.float32)[:, None] * frequency[None, :]


def rotate(values, angles):
    half_dim = values.shape[-1] // 2
    first_half = values[..., :half_dim]
    second_half = values[..., half_dim:]
    cosine = jnp.cos(angles)
    sine_part = jnp.sin(angles)
    return jnp.concatenate(
        [
            first_half * cosine - second_half * sine_part,
            second_half * cosine + first_half * sine_part,
        ],
        axis=-1,
    )


def geglu(gate_in, up_in):
    return jax.nn.gelu(gate_in, approximate=True) * up_in


def adam_update(gradient, first_old, second_old, params_old, rate, decay_rate):
    first_new = beta_first * first_old + (1.0 - beta_first) * gradient
    second_new = beta_second * second_old + (1.0 - beta_second) * gradient * gradient
    first_hat = first_new / (1.0 - beta_first**STEP)
    second_hat = second_new / (1.0 - beta_second**STEP)
    params_new = params_old - rate * (
        first_hat / (jnp.sqrt(second_hat) + adam_floor) + decay_rate * params_old
    )
    return (first_new, second_new, params_new)


def piece_rows(device_count):
    return [
        entries // (128 * device_count)
        for entries in (D * HQ * HD, D * HD, D * HD, HQ * HD * D, D * FF, D * FF, FF * D)
    ]


def piece_shapes():
    return [(D, HQ * HD), (D, HD), (D, HD), (HQ * HD, D), (D, FF), (D, FF), (FF, D)]


def split_rows(stacked, row_list):
    result = []
    row_start = 0
    for row_count in row_list:
        result.append(stacked[row_start : row_start + row_count])
        row_start = row_start + row_count
    return result


def matmul(left_side, right_side):
    return jnp.dot(left_side, right_side, preferred_element_type=jnp.float32)


LOW_COUNT = 8
LANES = 128
LOW_MASKS = (0, 4, 2, 6, 1, 5, 3, 7)
GELU_SCALE = (2.0 / math.pi) ** 0.5
GELU_CUBE = 0.044715
VMEM_BYTES = 56 * 1024 * 1024


def aligned(device_count):
    return device_count % LOW_COUNT == 0 and D % device_count == 0


def swap(value, mask):
    count = lax.axis_size(ALL_AXES)
    return lax.ppermute(value, ALL_AXES, [(source, source ^ mask) for source in range(count)])


def local_call(kernel, outs, operands, scratch=(), flops=0):
    specs = [pl.BlockSpec(memory_space=pltpu.SMEM)]
    specs = specs + [pl.BlockSpec(memory_space=pltpu.VMEM)] * len(operands)
    moved = sum(math.prod(value.shape) * value.dtype.itemsize for value in (*operands, *outs))
    return pl.pallas_call(
        kernel,
        out_shape=outs,
        in_specs=specs,
        out_specs=tuple(pl.BlockSpec(memory_space=pltpu.VMEM) for _ in outs),
        scratch_shapes=scratch,
        compiler_params=pltpu.CompilerParams(vmem_limit_bytes=VMEM_BYTES),
        cost_estimate=pl.CostEstimate(flops=flops, bytes_accessed=moved, transcendentals=0),
    )(lax.axis_index(ALL_AXES).astype(jnp.int32).reshape(1), *operands)


class Piece:
    def __init__(self, rows, columns, device_count):
        self.rows = rows
        self.columns = columns
        self.wide = rows == D
        self.blocks = columns // LANES
        self.own_rows = rows // device_count
        self.flat_rows = self.own_rows * self.blocks
        self.high_count = device_count // LOW_COUNT
        self.block_rows = self.own_rows * self.high_count
        self.size = self.block_rows * self.blocks


def pack_kernel(pieces, index_ref, *refs):
    high_count = pieces[0].high_count
    parts, out_ref, flat, packed = refs[:high_count], refs[-3], refs[-2], refs[-1]
    high = index_ref[0] // LOW_COUNT
    for step, part in enumerate(parts):
        flat[high ^ step] = part[...].astype(jnp.float32)
    start, target = 0, 0
    for piece in pieces:
        for block in range(piece.blocks):
            for place in range(high_count):
                packed[pl.ds(target, piece.own_rows), :] = flat[
                    place, pl.ds(start + block, piece.own_rows, stride=piece.blocks), :
                ]
                target = target + piece.own_rows
        start = start + piece.flat_rows
    out_ref[...] = packed[...].astype(jnp.bfloat16)


def unpack_kernel(pieces, index_ref, *refs):
    high_count = pieces[0].high_count
    terms, outs, flat, packed = refs[:3], refs[3:-2], refs[-2], refs[-1]
    high = index_ref[0] // LOW_COUNT
    packed[...] = sum(term[...].astype(jnp.float32) for term in terms)
    start, source = 0, 0
    for piece in pieces:
        for block in range(piece.blocks):
            for place in range(high_count):
                flat[place, pl.ds(start + block, piece.own_rows, stride=piece.blocks), :] = packed[
                    pl.ds(source, piece.own_rows), :
                ]
                source = source + piece.own_rows
        start = start + piece.flat_rows
    for step, out_ref in enumerate(outs):
        out_ref[...] = flat[high ^ step].astype(out_ref.dtype)


def assemble_kernel(pieces, index_ref, near_ref, far_ref, *out_refs):
    low = index_ref[0] % LOW_COUNT
    size = sum(piece.size for piece in pieces)
    for order, mask in enumerate(LOW_MASKS):
        source = near_ref if order < 4 else far_ref
        start = (order % 4) * size
        for piece, out_ref in zip(pieces, out_refs):
            for block in range(piece.blocks):
                columns = slice(block * LANES, (block + 1) * LANES)
                if piece.wide:
                    out_ref[order * piece.block_rows : (order + 1) * piece.block_rows, columns] = (
                        source[start : start + piece.block_rows, :]
                    )
                else:
                    for place in range(piece.high_count):
                        row = (place * LOW_COUNT + (low ^ mask)) * piece.own_rows
                        first = start + place * piece.own_rows
                        out_ref[
                            pl.ds(pl.multiple_of(row, piece.own_rows), piece.own_rows), columns
                        ] = source[first : first + piece.own_rows, :]
                start = start + piece.block_rows


def split_kernel(pieces, index_ref, *refs):
    in_refs, near_ref, far_ref = refs[:-2], refs[-2], refs[-1]
    low = index_ref[0] % LOW_COUNT
    size = sum(piece.size for piece in pieces)
    for order, mask in enumerate(LOW_MASKS):
        target = near_ref if order < 4 else far_ref
        start = (order % 4) * size
        for piece, in_ref in zip(pieces, in_refs):
            for block in range(piece.blocks):
                columns = slice(block * LANES, (block + 1) * LANES)
                if piece.wide:
                    target[start : start + piece.block_rows, :] = in_ref[
                        order * piece.block_rows : (order + 1) * piece.block_rows, columns
                    ].astype(jnp.bfloat16)
                else:
                    for place in range(piece.high_count):
                        row = (place * LOW_COUNT + (low ^ mask)) * piece.own_rows
                        first = start + place * piece.own_rows
                        target[first : first + piece.own_rows, :] = in_ref[
                            pl.ds(pl.multiple_of(row, piece.own_rows), piece.own_rows), columns
                        ].astype(jnp.bfloat16)
                start = start + piece.block_rows


def array(shape, kind):
    return jax.ShapeDtypeStruct(shape, kind)


def gather_blocks(pieces, rows):
    high_count = pieces[0].high_count
    size = sum(piece.size for piece in pieces)
    parts = [rows] + [swap(rows, step * LOW_COUNT) for step in range(1, high_count)]
    (own,) = local_call(
        functools.partial(pack_kernel, pieces),
        (array((size, LANES), jnp.bfloat16),),
        parts,
        (
            pltpu.VMEM((high_count, rows.shape[0], LANES), jnp.float32),
            pltpu.VMEM((size, LANES), jnp.float32),
        ),
    )
    beside, across = swap(own, 4), swap(own, 2)
    half = size // 2
    near = jnp.concatenate([own, beside, across, swap(across[:half], 4), swap(beside[half:], 2)])
    return near, swap(near, 1)


def assemble(pieces, near, far):
    return local_call(
        functools.partial(assemble_kernel, pieces),
        tuple(array((piece.rows, piece.columns), jnp.bfloat16) for piece in pieces),
        (near, far),
    )


def split(pieces, gradients):
    size = sum(piece.size for piece in pieces)
    return local_call(
        functools.partial(split_kernel, pieces),
        (array((4 * size, LANES), jnp.bfloat16),) * 2,
        [gradient.astype(jnp.bfloat16) for gradient in gradients],
    )


def scatter_blocks(pieces, near, far):
    high_count = pieces[0].high_count
    size = sum(piece.size for piece in pieces)
    flat_rows = sum(piece.flat_rows for piece in pieces)
    total = near.astype(jnp.float32) + swap(far, 1).astype(jnp.float32)
    half = size // 2
    diagonal = total[3 * size :].astype(jnp.bfloat16)
    across = total[2 * size : 3 * size]
    beside = total[size : 2 * size]
    over_x = swap(diagonal[:half], 4).astype(jnp.float32)
    over_y = swap(diagonal[half:], 2).astype(jnp.float32)
    across = jnp.concatenate([across[:half] + over_x, across[half:]]).astype(jnp.bfloat16)
    beside = jnp.concatenate([beside[:half], beside[half:] + over_y]).astype(jnp.bfloat16)
    outs = local_call(
        functools.partial(unpack_kernel, pieces),
        (array((flat_rows, LANES), jnp.float32),)
        + (array((flat_rows, LANES), jnp.bfloat16),) * (high_count - 1),
        (total[:size], swap(beside, 4), swap(across, 2)),
        (
            pltpu.VMEM((high_count, flat_rows, LANES), jnp.float32),
            pltpu.VMEM((size, LANES), jnp.float32),
        ),
    )
    return outs[0] + sum(
        swap(send, step * LOW_COUNT).astype(jnp.float32) for step, send in enumerate(outs) if step
    )


def norm_parts(values):
    scale = lax.rsqrt(jnp.mean(values * values, axis=-1, keepdims=True) + norm_eps)
    return scale, values * scale


def norm_back(scale, normal, upstream, weight_vec):
    weighted = upstream * (1.0 + weight_vec)
    inner = jnp.mean(weighted * normal, axis=-1, keepdims=True)
    return scale * (weighted - normal * inner), jnp.sum(normal * upstream, axis=0, keepdims=True)


def product(left_side, right_side, left_axis, right_axis):
    return lax.dot_general(
        left_side,
        right_side,
        (((left_axis,), (right_axis,)), ((), ())),
        preferred_element_type=jnp.float32,
    )


def unordered(rows_in, order_low):
    upper = rows_in.astype(jnp.bfloat16)
    lower = (rows_in - upper.astype(jnp.float32)).astype(jnp.bfloat16)
    return product(upper, order_low, 1, 1) + product(lower, order_low, 1, 1)


def wide_tile(near_ref, far_ref, size, start, rows):
    return jnp.concatenate(
        [
            ref[place * size + start : place * size + start + rows, :]
            for ref in (near_ref, far_ref)
            for place in range(4)
        ]
    )


def put_wide_tile(near_ref, far_ref, size, start, rows, tile):
    for order in range(LOW_COUNT):
        target = near_ref if order < 4 else far_ref
        first = (order % 4) * size + start
        target[first : first + rows, :] = tile[order * rows : (order + 1) * rows]


def tall_rows(piece, low):
    for order, mask in enumerate(LOW_MASKS):
        for block in range(piece.blocks):
            for place in range(piece.high_count):
                row = (place * LOW_COUNT + (low ^ mask)) * piece.own_rows
                yield (
                    order,
                    block * piece.block_rows + place * piece.own_rows,
                    pl.ds(pl.multiple_of(row, piece.own_rows), piece.own_rows),
                    slice(block * LANES, (block + 1) * LANES),
                )


def ffn_kernel(
    gate_piece,
    down_piece,
    index_ref,
    middle_ref,
    cotangent_ref,
    gain_in_ref,
    gain_out_ref,
    order_ref,
    near_ref,
    far_ref,
    near_down_ref,
    far_down_ref,
    block_out_ref,
    grad_middle_ref,
    grad_gain_in_ref,
    grad_gain_out_ref,
    grad_near_ref,
    grad_far_ref,
    grad_near_down_ref,
    grad_far_down_ref,
    down_ref,
    hidden_ref,
    gelu_ref,
    slope_ref,
):
    low = index_ref[0] % LOW_COUNT
    rows = gate_piece.block_rows
    size = 2 * gate_piece.size
    width = 2 * LANES
    for order, first, matrix_rows, columns in tall_rows(down_piece, low):
        source = near_down_ref if order < 4 else far_down_ref
        first = first + (order % 4) * down_piece.size
        down_ref[matrix_rows, columns] = source[first : first + down_piece.own_rows, :]

    def wide_tiles(step):
        return [
            jnp.concatenate(
                [
                    wide_tile(near_ref, far_ref, size, offset + block * rows, rows)
                    for block in (2 * step, 2 * step + 1)
                ],
                axis=1,
            )
            for offset in (0, gate_piece.size)
        ]

    middle = middle_ref[...]
    scale_in, normal_in = norm_parts(middle)
    order_low = order_ref[...]
    normed = (normal_in * (1.0 + gain_in_ref[...])).astype(jnp.bfloat16)
    normed = product(normed, order_low, 1, 0).astype(jnp.bfloat16)
    for step in range(FF // width):
        columns = slice(step * width, (step + 1) * width)
        gate_weight, up_weight = wide_tiles(step)
        gate = product(normed, gate_weight, 1, 0)
        up = product(normed, up_weight, 1, 0)
        square = gate * gate
        bend = jnp.tanh(GELU_SCALE * gate * (1.0 + GELU_CUBE * square))
        half = 0.5 * (1.0 + bend)
        gelu = gate * half
        slope = half + 0.5 * gate * (1.0 - bend * bend) * GELU_SCALE * (
            1.0 + 3.0 * GELU_CUBE * square
        )
        gelu_ref[:, columns] = gelu
        slope_ref[:, columns] = slope * up
        hidden_ref[:, columns] = (gelu * up).astype(jnp.bfloat16)
    hidden = hidden_ref[...]
    scale_out, normal_out = norm_parts(product(hidden, down_ref[...], 1, 0))
    block_out_ref[...] = (middle + normal_out * (1.0 + gain_out_ref[...])).astype(jnp.bfloat16)
    upstream = cotangent_ref[...].astype(jnp.float32)
    grad_ffn, grad_gain_out_ref[...] = norm_back(
        scale_out, normal_out, upstream, gain_out_ref[...]
    )
    grad_ffn = grad_ffn.astype(jnp.bfloat16)
    grad_normed = jnp.zeros(middle.shape, jnp.float32)
    for step in range(FF // width):
        columns = slice(step * width, (step + 1) * width)
        grad_hidden = product(grad_ffn, down_ref[columns, :], 1, 1)
        down_ref[columns, :] = product(hidden_ref[:, columns], grad_ffn, 0, 0).astype(jnp.bfloat16)
        grads = [
            (grad_hidden * slope_ref[:, columns]).astype(jnp.bfloat16),
            (grad_hidden * gelu_ref[:, columns]).astype(jnp.bfloat16),
        ]
        for place, (grad, weight) in enumerate(zip(grads, wide_tiles(step))):
            grad_weight = product(normed, grad, 0, 0).astype(jnp.bfloat16)
            for side in range(2):
                put_wide_tile(
                    grad_near_ref,
                    grad_far_ref,
                    size,
                    place * gate_piece.size + (2 * step + side) * rows,
                    rows,
                    grad_weight[:, side * LANES : (side + 1) * LANES],
                )
            grad_normed = grad_normed + product(grad, weight, 1, 1)
    for order, first, matrix_rows, columns in tall_rows(down_piece, low):
        target = grad_near_down_ref if order < 4 else grad_far_down_ref
        first = first + (order % 4) * down_piece.size
        target[first : first + down_piece.own_rows, :] = down_ref[matrix_rows, columns]
    grad_middle, grad_gain_in_ref[...] = norm_back(
        scale_in, normal_in, unordered(grad_normed, order_low), gain_in_ref[...]
    )
    grad_middle_ref[...] = upstream + grad_middle


def ffn_blocks(pieces, middle, cotangent, gain_in, gain_out, order, gate_up, down):
    rows = middle.shape[0]
    shapes = [array(value.shape, jnp.bfloat16) for value in (*gate_up, *down)]
    outs = local_call(
        functools.partial(ffn_kernel, pieces[4], pieces[6]),
        (
            array((rows, D), jnp.bfloat16),
            array((rows, D), jnp.float32),
            array((1, D), jnp.float32),
            array((1, D), jnp.float32),
            *shapes,
        ),
        (middle, cotangent, gain_in[None], gain_out[None], order, *gate_up, *down),
        (
            pltpu.VMEM((FF, D), jnp.bfloat16),
            pltpu.VMEM((rows, FF), jnp.bfloat16),
            pltpu.VMEM((rows, FF), jnp.float32),
            pltpu.VMEM((rows, FF), jnp.float32),
        ),
        flops=18 * rows * D * FF,
    )
    return outs[0], outs[1], outs[2][0], outs[3][0], outs[4:6], outs[6:8]


def ffn_plain(middle, cotangent, gain_in, gain_out, gate_weight, up_weight, down_weight):
    normed_two, back_ffin = jax.vjp(rms_norm, middle, gain_in)
    normed_two_low = normed_two.astype(jnp.bfloat16)
    gate_proj = matmul(normed_two_low, gate_weight)
    up_proj = matmul(normed_two_low, up_weight)
    hidden, back_hidden = jax.vjp(geglu, gate_proj, up_proj)
    hidden_low = hidden.astype(jnp.bfloat16)
    branch_two, back_ffout = jax.vjp(rms_norm, matmul(hidden_low, down_weight), gain_out)
    grad_out = cotangent.astype(jnp.float32)
    grad_ffn, grad_gain_ffout = back_ffout(grad_out)
    grad_ffn_low = grad_ffn.astype(jnp.bfloat16)
    grad_gate, grad_up = back_hidden(product(grad_ffn_low, down_weight, 1, 1))
    grad_gate_low = grad_gate.astype(jnp.bfloat16)
    grad_up_low = grad_up.astype(jnp.bfloat16)
    grad_weights = [
        product(normed_two_low, grad_gate_low, 0, 0),
        product(normed_two_low, grad_up_low, 0, 0),
        product(hidden_low, grad_ffn_low, 0, 0),
    ]
    grad_middle, grad_gain_ffin = back_ffin(
        product(grad_gate_low, gate_weight, 1, 1) + product(grad_up_low, up_weight, 1, 1)
    )
    return (
        (middle + branch_two).astype(jnp.bfloat16),
        grad_out + grad_middle,
        grad_gain_ffin,
        grad_gain_ffout,
        grad_weights,
    )


def width_order(device_count):
    low = lax.axis_index(ALL_AXES) % LOW_COUNT
    rows = D // device_count
    high_count = device_count // LOW_COUNT
    column = jnp.arange(D, dtype=jnp.int32)
    place = column // (rows * high_count)
    mask = (place & 1) * 4 + ((place >> 1) & 1) * 2 + (place >> 2)
    high = (column // rows) % high_count
    picked = (high * LOW_COUNT + (low ^ mask)) * rows + column % rows
    return (jnp.arange(D, dtype=jnp.int32)[:, None] == picked[None, :]).astype(jnp.float32)


def gather_weights(master, device_count, pieces):
    shard_parts = [
        part_rows.astype(jnp.bfloat16) for part_rows in split_rows(master, piece_rows(device_count))
    ]
    if pieces is None:
        full = [
            lax.all_gather(part, ALL_AXES, axis=0, tiled=True).reshape(shape_pair)
            for part, shape_pair in zip(shard_parts, piece_shapes())
        ]
        return full[:4], full[4:], None
    blocks = [
        gather_blocks(pieces[first:last], jnp.concatenate(shard_parts[first:last]))
        for first, last in CHUNKS
    ]
    return assemble(pieces[:4], *blocks[0]), blocks[1:], width_order(device_count)


CHUNKS = ((0, 4), (4, 6), (6, 7))


def scatter_plain(gradients):
    return jnp.concatenate(
        [
            lax.psum_scatter(piece.reshape(-1, 128), ALL_AXES, scatter_dimension=0, tiled=True)
            for piece in gradients
        ],
        axis=0,
    )


def sum_gains(values, device_count):
    if not aligned(device_count):
        return lax.psum(values, ALL_AXES)
    values = values.reshape(-1, 128)
    mask = 1
    while mask < device_count:
        values = values + swap(values, mask)
        mask = mask * 2
    return values.reshape(-1)


def shards(
    tokens, doc_ids, cotangent, master, first_moment, second_moment, gains, gain_first, gain_second
):
    group_size = lax.axis_size("group")
    devices_all = lax.axis_size("dp") * group_size
    group_index = lax.axis_index("group")
    local_rows = tokens.shape[0]
    pieces = None
    if aligned(devices_all):
        pieces = [Piece(*shape_pair, devices_all) for shape_pair in piece_shapes()]
    attention_weights, ffn_weights, order = gather_weights(master, devices_all, pieces)
    query_weight, key_weight, value_weight, out_weight = attention_weights
    norm_input = gains[0:D]
    norm_attn = gains[D : 2 * D]
    norm_ffin = gains[2 * D : 3 * D]
    norm_ffout = gains[3 * D : 4 * D]
    norm_query = gains[4 * D : 4 * D + HD]
    norm_key = gains[4 * D + HD : 4 * D + 2 * HD]
    doc_row = doc_ids[0]
    first_row = group_index * local_rows
    angles = lax.dynamic_slice_in_dim(angles_of(positions(doc_row)), first_row, local_rows, 0)
    query_docs = lax.dynamic_slice_in_dim(doc_row, first_row, local_rows, 0)

    def ordered(rows_low):
        if order is None:
            return rows_low
        return matmul(rows_low, order.astype(jnp.bfloat16)).astype(jnp.bfloat16)

    def restored(rows_in):
        if order is None:
            return rows_in
        return jnp.einsum("te,de->td", rows_in, order, precision=lax.Precision.HIGHEST)

    inputs = tokens.astype(jnp.float32)
    normed, back_input = jax.vjp(rms_norm, inputs, norm_input)
    normed_low = normed.astype(jnp.bfloat16)
    normed_low = ordered(normed_low)
    query_proj = matmul(normed_low, query_weight)
    key_proj = matmul(normed_low, key_weight)
    value_proj = matmul(normed_low, value_weight)

    def query_prep(flat_rows, gain_vec):
        return rotate(rms_norm(flat_rows.reshape(local_rows, HQ, HD), gain_vec), angles[:, None, :])

    def key_prep(rows_in, gain_vec):
        return rotate(rms_norm(rows_in, gain_vec), angles)

    query_rot, back_query = jax.vjp(query_prep, query_proj, norm_query)
    key_rot, back_key = jax.vjp(key_prep, key_proj, norm_key)
    query_low = query_rot.astype(jnp.bfloat16)
    key_low = key_rot.astype(jnp.bfloat16)
    value_low = value_proj.astype(jnp.bfloat16)
    reach = min(-(-(WINDOW - 1) // local_rows), group_size - 1)
    key_value = jnp.concatenate([key_low, value_low], axis=1)
    key_value_list = [key_value]
    for offset in range(1, reach + 1):
        key_value_list.insert(0, shifted(key_value, "group", offset))
    key_value_all = jnp.concatenate(key_value_list, axis=0)
    key_all = key_value_all[:, :HD]
    value_all = key_value_all[:, HD:]
    key_count = (reach + 1) * local_rows
    doc_pad = jnp.concatenate([jnp.full((reach * local_rows,), -1, jnp.int32), doc_row])
    key_docs = lax.dynamic_slice_in_dim(doc_pad, first_row, key_count, 0)
    key_index = (group_index - reach) * local_rows + jnp.arange(key_count, dtype=jnp.int32)
    query_index = first_row + jnp.arange(local_rows, dtype=jnp.int32)
    distance = query_index[:, None] - key_index[None, :]
    allowed = (distance >= 0) & (distance < WINDOW) & (key_docs[None, :] == query_docs[:, None])

    def scores_of(key_rows_low):
        raw_scores = jnp.einsum(
            "qhd,kd->hqk", query_low, key_rows_low, preferred_element_type=jnp.float32
        ) * HD ** (-0.5)
        return jnp.where(allowed[None], raw_scores, -1e30)

    masked = scores_of(key_all)
    top_score = jnp.max(masked, axis=-1, keepdims=True)
    log_total = top_score + jnp.log(jnp.sum(jnp.exp(masked - top_score), axis=-1, keepdims=True))
    probs = jnp.exp(masked - log_total)
    attended = jnp.einsum(
        "hqk,kd->qhd", probs.astype(jnp.bfloat16), value_all, preferred_element_type=jnp.float32
    )
    attended_low = attended.reshape(local_rows, HQ * HD).astype(jnp.bfloat16)
    attn_out = matmul(attended_low, out_weight)
    branch_one, back_attn = jax.vjp(rms_norm, attn_out, norm_attn)
    middle = inputs + branch_one
    if order is None:
        outputs, grad_middle, grad_gain_ffin, grad_gain_ffout, grads_ffn = ffn_plain(
            middle, cotangent, norm_ffin, norm_ffout, *ffn_weights
        )
        grads_ffn = scatter_plain(grads_ffn)
    else:
        outputs, grad_middle, grad_gain_ffin, grad_gain_ffout, grads_gate_up, grads_down = (
            ffn_blocks(
                pieces,
                middle,
                cotangent,
                norm_ffin,
                norm_ffout,
                order.astype(jnp.bfloat16),
                *ffn_weights,
            )
        )
        grads_ffn = jnp.concatenate(
            [
                scatter_blocks(pieces[4:6], *grads_gate_up),
                scatter_blocks(pieces[6:7], *grads_down),
            ]
        )
    grad_attn, grad_gain_attn = back_attn(grad_middle)
    grad_attn_low = grad_attn.astype(jnp.bfloat16)
    grad_out_w = jnp.einsum(
        "to,td->od", attended_low, grad_attn_low, preferred_element_type=jnp.float32
    )
    grad_attended = jnp.einsum(
        "td,od->to", grad_attn_low, out_weight, preferred_element_type=jnp.float32
    )
    grad_attended_low = grad_attended.astype(jnp.bfloat16).reshape(local_rows, HQ, HD)
    probs_again = jnp.exp(scores_of(key_all) - log_total)
    grad_probs = jnp.einsum(
        "qhd,kd->hqk", grad_attended_low, value_all, preferred_element_type=jnp.float32
    )
    grad_value_all = jnp.einsum(
        "hqk,qhd->kd",
        probs_again.astype(jnp.bfloat16),
        grad_attended_low,
        preferred_element_type=jnp.float32,
    )
    grad_scores = probs_again * (
        grad_probs - jnp.sum(probs_again * grad_probs, axis=-1, keepdims=True)
    )
    grad_scores_low = (grad_scores * HD ** (-0.5)).astype(jnp.bfloat16)
    grad_query = jnp.einsum(
        "hqk,kd->qhd", grad_scores_low, key_all, preferred_element_type=jnp.float32
    )
    grad_key_all = jnp.einsum(
        "hqk,qhd->kd", grad_scores_low, query_low, preferred_element_type=jnp.float32
    )
    grad_both_all = jnp.concatenate([grad_key_all, grad_value_all], axis=1)
    both_total = grad_both_all[reach * local_rows :]
    for offset in range(1, reach + 1):
        row_start = (reach - offset) * local_rows
        both_total = both_total + shifted(
            grad_both_all[row_start : row_start + local_rows].astype(jnp.bfloat16),
            "group",
            -offset,
        ).astype(jnp.float32)
    key_total = both_total[:, :HD]
    value_total = both_total[:, HD:]
    grad_query_proj, grad_gain_query = back_query(grad_query)
    grad_key_proj, grad_gain_key = back_key(key_total)
    grad_query_low = grad_query_proj.astype(jnp.bfloat16)
    grad_key_low = grad_key_proj.astype(jnp.bfloat16)
    grad_value_low = value_total.astype(jnp.bfloat16)
    grad_query_w = jnp.einsum(
        "td,te->de", normed_low, grad_query_low, preferred_element_type=jnp.float32
    )
    grad_key_w = jnp.einsum(
        "td,te->de", normed_low, grad_key_low, preferred_element_type=jnp.float32
    )
    grad_value_w = jnp.einsum(
        "td,te->de", normed_low, grad_value_low, preferred_element_type=jnp.float32
    )
    grads_attn = [grad_query_w, grad_key_w, grad_value_w, grad_out_w]
    if order is None:
        grads_attn = scatter_plain(grads_attn)
    else:
        grads_attn = scatter_blocks(pieces[:4], *split(pieces[:4], grads_attn))
    grad_normed = restored(
        jnp.einsum("te,de->td", grad_query_low, query_weight, preferred_element_type=jnp.float32)
        + jnp.einsum("te,de->td", grad_key_low, key_weight, preferred_element_type=jnp.float32)
        + jnp.einsum("te,de->td", grad_value_low, value_weight, preferred_element_type=jnp.float32)
    )
    grad_input_norm, grad_gain_input = back_input(grad_normed)
    grad_inputs = grad_middle + grad_input_norm
    grads_local = jnp.concatenate([grads_attn, grads_ffn], axis=0)
    gain_grads = sum_gains(
        jnp.concatenate(
            [
                grad_gain_input,
                grad_gain_attn,
                grad_gain_ffin,
                grad_gain_ffout,
                grad_gain_query,
                grad_gain_key,
            ]
        ),
        devices_all,
    )
    moment_first, moment_second, master_new = adam_update(
        grads_local, first_moment, second_moment, master, learn_rate, weight_decay
    )
    gain_moment_first, gain_moment_second, gains_new = adam_update(
        gain_grads, gain_first, gain_second, gains, gain_rate, 0.0
    )
    return (
        outputs,
        grad_inputs.astype(jnp.bfloat16),
        moment_first,
        moment_second,
        master_new,
        gain_moment_first,
        gain_moment_second,
        gains_new,
    )


def solution(mesh):
    placed = (
        P(("dp", "group"), None),
        P("dp", None),
        P(("dp", "group"), None),
        P(("dp", "group"), None),
        P(("dp", "group"), None),
        P(("dp", "group"), None),
        P(),
        P(),
        P(),
    )
    return jax.shard_map(
        shards,
        mesh=mesh,
        in_specs=placed,
        out_specs=(
            P(("dp", "group"), None),
            P(("dp", "group"), None),
            P(("dp", "group"), None),
            P(("dp", "group"), None),
            P(("dp", "group"), None),
            P(),
            P(),
            P(),
        ),
        check_vma=False,
    )
```

```python
import functools
import math

import jax
import jax.numpy as jnp
from jax import lax
from jax.experimental import pallas as pl
from jax.experimental.pallas import tpu as pltpu
from jax.sharding import PartitionSpec as P

D = 640
HQ = 4
HD = 256
FF = 2048
WINDOW = 512
STEP = 10
ALL_AXES = ("dp", "group")


norm_eps = 1e-06
rope_base = 10000.0
beta_first = 0.9
beta_second = 0.999
learn_rate = 0.05
gain_rate = 0.25
adam_floor = 1e-08
weight_decay = 0.1


def shifted(value, axis, steps):
    count = lax.axis_size(axis)
    initial, last = (max(0, -steps), min(count, count - steps))
    return lax.ppermute(value, axis, [(source, source + steps) for source in range(initial, last)])


def rms_norm(values, weight_vec):
    return (
        values
        * lax.rsqrt(jnp.mean(values * values, axis=-1, keepdims=True) + norm_eps)
        * (1.0 + weight_vec)
    )


def positions(doc_row):
    length = doc_row.shape[0]
    counter = jnp.arange(length, dtype=jnp.int32)
    starts_here = jnp.concatenate([jnp.ones((1,), jnp.bool_), doc_row[1:] != doc_row[:-1]])
    begins = lax.cummax(jnp.where(starts_here, counter, jnp.zeros_like(counter)), axis=0)
    return counter - begins


def angles_of(places):
    half_dim = HD // 2
    frequency = rope_base ** (-(jnp.arange(half_dim, dtype=jnp.float32) * 2.0 / HD))
    return places.astype(jnp.float32)[:, None] * frequency[None, :]


def rotate(values, angles):
    half_dim = values.shape[-1] // 2
    first_half = values[..., :half_dim]
    second_half = values[..., half_dim:]
    cosine = jnp.cos(angles)
    sine_part = jnp.sin(angles)
    return jnp.concatenate(
        [
            first_half * cosine - second_half * sine_part,
            second_half * cosine + first_half * sine_part,
        ],
        axis=-1,
    )


def geglu(gate_in, up_in):
    return jax.nn.gelu(gate_in, approximate=True) * up_in


def adam_update(gradient, first_old, second_old, params_old, rate, decay_rate):
    first_new = beta_first * first_old + (1.0 - beta_first) * gradient
    second_new = beta_second * second_old + (1.0 - beta_second) * gradient * gradient
    first_hat = first_new / (1.0 - beta_first**STEP)
    second_hat = second_new / (1.0 - beta_second**STEP)
    params_new = params_old - rate * (
        first_hat / (jnp.sqrt(second_hat) + adam_floor) + decay_rate * params_old
    )
    return (first_new, second_new, params_new)


def piece_rows(device_count):
    return [
        entries // (128 * device_count)
        for entries in (D * HQ * HD, D * HD, D * HD, HQ * HD * D, D * FF, D * FF, FF * D)
    ]


def piece_shapes():
    return [(D, HQ * HD), (D, HD), (D, HD), (HQ * HD, D), (D, FF), (D, FF), (FF, D)]


def split_rows(stacked, row_list):
    result = []
    row_start = 0
    for row_count in row_list:
        result.append(stacked[row_start : row_start + row_count])
        row_start = row_start + row_count
    return result


def matmul(left_side, right_side):
    return jnp.dot(left_side, right_side, preferred_element_type=jnp.float32)


LOW_COUNT = 8
LANES = 128
LOW_MASKS = (0, 4, 2, 6, 1, 5, 3, 7)
GELU_SCALE = (2.0 / math.pi) ** 0.5
GELU_CUBE = 0.044715
VMEM_BYTES = 56 * 1024 * 1024


def aligned(device_count):
    return device_count % LOW_COUNT == 0 and D % device_count == 0


def swap(value, mask):
    count = lax.axis_size(ALL_AXES)
    return lax.ppermute(value, ALL_AXES, [(source, source ^ mask) for source in range(count)])


def local_call(kernel, outs, operands, scratch=()):
    specs = [pl.BlockSpec(memory_space=pltpu.SMEM)]
    specs = specs + [pl.BlockSpec(memory_space=pltpu.VMEM)] * len(operands)
    return pl.pallas_call(
        kernel,
        out_shape=outs,
        in_specs=specs,
        out_specs=tuple(pl.BlockSpec(memory_space=pltpu.VMEM) for _ in outs),
        scratch_shapes=scratch,
        compiler_params=pltpu.CompilerParams(vmem_limit_bytes=VMEM_BYTES),
        cost_estimate=pl.CostEstimate(flops=0, bytes_accessed=0, transcendentals=0),
    )(lax.axis_index(ALL_AXES).astype(jnp.int32).reshape(1), *operands)


class Piece:
    def __init__(self, rows, columns, device_count):
        self.rows = rows
        self.columns = columns
        self.wide = rows == D
        self.blocks = columns // LANES
        self.own_rows = rows // device_count
        self.flat_rows = self.own_rows * self.blocks
        self.high_count = device_count // LOW_COUNT
        self.block_rows = self.own_rows * self.high_count
        self.size = self.block_rows * self.blocks


def pack_kernel(pieces, later_count, index_ref, *refs):
    high_count = pieces[0].high_count
    parts, later = refs[:high_count], refs[high_count : high_count + later_count]
    out_ref, later_outs = refs[high_count + later_count], refs[high_count + later_count + 1 : -2]
    flat, packed = refs[-2:]
    high = index_ref[0] // LOW_COUNT
    for step, part in enumerate(parts):
        flat[high ^ step] = part[...].astype(jnp.float32)
    start, target = 0, 0
    for piece in pieces:
        for block in range(piece.blocks):
            for place in range(high_count):
                packed[pl.ds(target, piece.own_rows), :] = flat[
                    place, pl.ds(start + block, piece.own_rows, stride=piece.blocks), :
                ]
                target = target + piece.own_rows
        start = start + piece.flat_rows
    out_ref[...] = packed[...].astype(jnp.bfloat16)
    for ref, later_out in zip(later, later_outs):
        later_out[...] = ref[...].astype(jnp.bfloat16)


def unpack_kernel(pieces, extra_count, index_ref, *refs):
    high_count = pieces[0].high_count
    size = sum(piece.size for piece in pieces)
    flat_rows = sum(piece.flat_rows for piece in pieces)
    terms, outs, flat, packed = refs[:3], refs[-2 - high_count : -2], refs[-2], refs[-1]
    high = index_ref[0] // LOW_COUNT
    packed[...] = sum(term[:size, :].astype(jnp.float32) for term in terms)
    start, source = 0, 0
    for piece in pieces:
        for block in range(piece.blocks):
            for place in range(high_count):
                flat[place, pl.ds(start + block, piece.own_rows, stride=piece.blocks), :] = packed[
                    pl.ds(source, piece.own_rows), :
                ]
                source = source + piece.own_rows
        start = start + piece.flat_rows
    for step, out_ref in enumerate(outs):
        out_ref[:flat_rows, :] = flat[high ^ step].astype(out_ref.dtype)
        if extra_count:
            extra = terms[2][size:, :].astype(jnp.float32) + refs[3][...].astype(jnp.float32)
            out_ref[flat_rows:, :] = extra.astype(out_ref.dtype)


def array(shape, kind):
    return jax.ShapeDtypeStruct(shape, kind)


def gather_blocks(pieces, rows, later=()):
    high_count = pieces[0].high_count
    size = sum(piece.size for piece in pieces)
    parts = [rows] + [swap(rows, step * LOW_COUNT) for step in range(1, high_count)]
    own, *later = local_call(
        functools.partial(pack_kernel, pieces, len(later)),
        (array((size, LANES), jnp.bfloat16),)
        + tuple(array(value.shape, jnp.bfloat16) for value in later),
        (*parts, *later),
        (
            pltpu.VMEM((high_count, rows.shape[0], LANES), jnp.float32),
            pltpu.VMEM((size, LANES), jnp.float32),
        ),
    )
    beside, across = swap(own, 4), swap(own, 2)
    half = size // 2
    near = jnp.concatenate([own, beside, across, swap(across[:half], 4), swap(beside[half:], 2)])
    return (near, swap(near, 1)), later


def scatter_blocks(pieces, near, far):
    high_count = pieces[0].high_count
    size = sum(piece.size for piece in pieces)
    flat_rows = sum(piece.flat_rows for piece in pieces)
    extra_count = near.shape[0] - 4 * size
    total = near.astype(jnp.float32) + swap(far, 1).astype(jnp.float32)
    half = size // 2
    over_x = swap(
        jnp.concatenate([total[3 * size : 3 * size + half], total[4 * size :]]).astype(
            jnp.bfloat16
        ),
        4,
    ).astype(jnp.float32)
    over_y = swap(total[3 * size + half : 4 * size].astype(jnp.bfloat16), 2).astype(jnp.float32)
    extra = total[4 * size :] + over_x[half:]
    across = jnp.concatenate(
        [total[2 * size : 2 * size + half] + over_x[:half], total[2 * size + half : 3 * size], extra]
    ).astype(jnp.bfloat16)
    beside = jnp.concatenate(
        [total[size : size + half], total[size + half : 2 * size] + over_y]
    ).astype(jnp.bfloat16)
    terms = [total[:size], swap(beside, 4), swap(across, 2)]
    if extra_count:
        terms.append(extra)
    outs = local_call(
        functools.partial(unpack_kernel, pieces, extra_count),
        (array((flat_rows + extra_count, LANES), jnp.float32),)
        + (array((flat_rows + extra_count, LANES), jnp.bfloat16),) * (high_count - 1),
        terms,
        (
            pltpu.VMEM((high_count, flat_rows, LANES), jnp.float32),
            pltpu.VMEM((size, LANES), jnp.float32),
        ),
    )
    return outs[0] + sum(
        swap(send, step * LOW_COUNT).astype(jnp.float32) for step, send in enumerate(outs) if step
    )


def norm_parts(values):
    scale = lax.rsqrt(jnp.mean(values * values, axis=-1, keepdims=True) + norm_eps)
    return scale, values * scale


def norm_back(scale, normal, upstream, weight_vec):
    weighted = upstream * (1.0 + weight_vec)
    inner = jnp.mean(weighted * normal, axis=-1, keepdims=True)
    return scale * (weighted - normal * inner), jnp.sum(normal * upstream, axis=0, keepdims=True)


def product(left_side, right_side, left_axis, right_axis):
    return lax.dot_general(
        left_side,
        right_side,
        (((left_axis,), (right_axis,)), ((), ())),
        preferred_element_type=jnp.float32,
    )


def unordered(rows_in, order_low):
    upper = rows_in.astype(jnp.bfloat16)
    lower = (rows_in - upper.astype(jnp.float32)).astype(jnp.bfloat16)
    return product(upper, order_low, 1, 1) + product(lower, order_low, 1, 1)


def wide_tile(near_ref, far_ref, size, start, rows):
    return jnp.concatenate(
        [
            ref[place * size + start : place * size + start + rows, :]
            for ref in (near_ref, far_ref)
            for place in range(4)
        ]
    )


def put_wide_tile(near_ref, far_ref, size, start, rows, tile):
    for order in range(LOW_COUNT):
        target = near_ref if order < 4 else far_ref
        first = (order % 4) * size + start
        target[first : first + rows, :] = tile[order * rows : (order + 1) * rows]


def tall_rows(piece, low):
    for order, mask in enumerate(LOW_MASKS):
        for block in range(piece.blocks):
            for place in range(piece.high_count):
                row = (place * LOW_COUNT + (low ^ mask)) * piece.own_rows
                yield (
                    order,
                    block * piece.block_rows + place * piece.own_rows,
                    pl.ds(pl.multiple_of(row, piece.own_rows), piece.own_rows),
                    slice(block * LANES, (block + 1) * LANES),
                )


def ffn_kernel(
    gate_piece,
    down_piece,
    index_ref,
    middle_ref,
    cotangent_ref,
    gain_in_ref,
    gain_out_ref,
    order_ref,
    near_ref,
    far_ref,
    near_down_ref,
    far_down_ref,
    block_out_ref,
    grad_middle_ref,
    grad_gain_in_ref,
    grad_gain_out_ref,
    grad_near_ref,
    grad_far_ref,
    grad_near_down_ref,
    grad_far_down_ref,
    down_ref,
    hidden_ref,
    gelu_ref,
    slope_ref,
):
    low = index_ref[0] % LOW_COUNT
    rows = gate_piece.block_rows
    size = 2 * gate_piece.size
    width = 2 * LANES
    for order, first, matrix_rows, columns in tall_rows(down_piece, low):
        source = near_down_ref if order < 4 else far_down_ref
        first = first + (order % 4) * down_piece.size
        down_ref[matrix_rows, columns] = source[first : first + down_piece.own_rows, :]

    def wide_tiles(step):
        return [
            jnp.concatenate(
                [
                    wide_tile(near_ref, far_ref, size, offset + block * rows, rows)
                    for block in (2 * step, 2 * step + 1)
                ],
                axis=1,
            )
            for offset in (0, gate_piece.size)
        ]

    middle = middle_ref[...]
    scale_in, normal_in = norm_parts(middle)
    order_low = order_ref[...]
    normed = (normal_in * (1.0 + gain_in_ref[...])).astype(jnp.bfloat16)
    normed = product(normed, order_low, 1, 0).astype(jnp.bfloat16)
    for step in range(FF // width):
        columns = slice(step * width, (step + 1) * width)
        gate_weight, up_weight = wide_tiles(step)
        gate = product(normed, gate_weight, 1, 0)
        up = product(normed, up_weight, 1, 0)
        square = gate * gate
        bend = jnp.tanh(GELU_SCALE * gate * (1.0 + GELU_CUBE * square))
        half = 0.5 * (1.0 + bend)
        gelu = gate * half
        slope = half + 0.5 * gate * (1.0 - bend * bend) * GELU_SCALE * (
            1.0 + 3.0 * GELU_CUBE * square
        )
        gelu_ref[:, columns] = gelu
        slope_ref[:, columns] = slope * up
        hidden_ref[:, columns] = (gelu * up).astype(jnp.bfloat16)
    hidden = hidden_ref[...]
    scale_out, normal_out = norm_parts(product(hidden, down_ref[...], 1, 0))
    block_out_ref[...] = (middle + normal_out * (1.0 + gain_out_ref[...])).astype(jnp.bfloat16)
    upstream = cotangent_ref[...].astype(jnp.float32)
    grad_ffn, grad_gain_out_ref[...] = norm_back(
        scale_out, normal_out, upstream, gain_out_ref[...]
    )
    grad_ffn = grad_ffn.astype(jnp.bfloat16)
    grad_normed = jnp.zeros(middle.shape, jnp.float32)
    for step in range(FF // width):
        columns = slice(step * width, (step + 1) * width)
        grad_hidden = product(grad_ffn, down_ref[columns, :], 1, 1)
        down_ref[columns, :] = product(hidden_ref[:, columns], grad_ffn, 0, 0).astype(jnp.bfloat16)
        grads = [
            (grad_hidden * slope_ref[:, columns]).astype(jnp.bfloat16),
            (grad_hidden * gelu_ref[:, columns]).astype(jnp.bfloat16),
        ]
        for place, (grad, weight) in enumerate(zip(grads, wide_tiles(step))):
            grad_weight = product(normed, grad, 0, 0).astype(jnp.bfloat16)
            for side in range(2):
                put_wide_tile(
                    grad_near_ref,
                    grad_far_ref,
                    size,
                    place * gate_piece.size + (2 * step + side) * rows,
                    rows,
                    grad_weight[:, side * LANES : (side + 1) * LANES],
                )
            grad_normed = grad_normed + product(grad, weight, 1, 1)
    for order, first, matrix_rows, columns in tall_rows(down_piece, low):
        target = grad_near_down_ref if order < 4 else grad_far_down_ref
        first = first + (order % 4) * down_piece.size
        target[first : first + down_piece.own_rows, :] = down_ref[matrix_rows, columns]
    grad_middle, grad_gain_in_ref[...] = norm_back(
        scale_in, normal_in, unordered(grad_normed, order_low), gain_in_ref[...]
    )
    grad_middle_ref[...] = upstream + grad_middle


def ffn_blocks(pieces, middle, cotangent, gain_in, gain_out, order, gate_up, down):
    rows = middle.shape[0]
    shapes = [array(value.shape, jnp.bfloat16) for value in (*gate_up, *down)]
    outs = local_call(
        functools.partial(ffn_kernel, pieces[4], pieces[6]),
        (
            array((rows, D), jnp.bfloat16),
            array((rows, D), jnp.float32),
            array((1, D), jnp.float32),
            array((1, D), jnp.float32),
            *shapes,
        ),
        (middle, cotangent, gain_in, gain_out, order, *gate_up, *down),
        (
            pltpu.VMEM((FF, D), jnp.bfloat16),
            pltpu.VMEM((rows, FF), jnp.bfloat16),
            pltpu.VMEM((rows, FF), jnp.float32),
            pltpu.VMEM((rows, FF), jnp.float32),
        ),
    )
    return outs[0], outs[1], outs[2], outs[3], outs[4:6], outs[6:8]


def turn(values, cosine, sine):
    first_half, second_half = values[:, : HD // 2], values[:, HD // 2 :]
    return jnp.concatenate(
        [first_half * cosine - second_half * sine, second_half * cosine + first_half * sine], axis=1
    )


def wide_head(near_ref, far_ref, size, start, rows):
    return jnp.concatenate(
        [wide_tile(near_ref, far_ref, size, start + side * rows, rows) for side in range(2)], axis=1
    )


def head_starts(pieces):
    rows = pieces[0].block_rows
    return [2 * rows * head for head in range(HQ + 2)]


def project_kernel(
    pieces,
    index_ref,
    tokens_ref,
    gain_ref,
    gain_query_ref,
    gain_key_ref,
    cosine_ref,
    sine_ref,
    order_ref,
    near_ref,
    far_ref,
    normed_ref,
    query_proj_ref,
    key_proj_ref,
    query_ref,
    key_value_ref,
):
    size = sum(piece.size for piece in pieces)
    rows = pieces[0].block_rows
    cosine, sine = cosine_ref[...], sine_ref[...]
    _, normal = norm_parts(tokens_ref[...].astype(jnp.float32))
    normed = (normal * (1.0 + gain_ref[...])).astype(jnp.bfloat16)
    normed = product(normed, order_ref[...], 1, 0).astype(jnp.bfloat16)
    normed_ref[...] = normed
    starts = head_starts(pieces)
    for head, start in enumerate(starts):
        proj = product(normed, wide_head(near_ref, far_ref, size, start, rows), 1, 0)
        columns = slice(head * HD, (head + 1) * HD)
        if head == HQ + 1:
            key_value_ref[:, HD:] = proj.astype(jnp.bfloat16)
            continue
        gain_vec = gain_query_ref[...] if head < HQ else gain_key_ref[...]
        _, normal = norm_parts(proj)
        turned = turn(normal * (1.0 + gain_vec), cosine, sine).astype(jnp.bfloat16)
        if head < HQ:
            query_proj_ref[:, columns] = proj
            query_ref[:, columns] = turned
        else:
            key_proj_ref[...] = proj
            key_value_ref[:, :HD] = turned


def attend_kernel(
    pieces,
    index_ref,
    tokens_ref,
    gain_ref,
    allowed_ref,
    query_ref,
    near_ref,
    far_ref,
    *refs,
):
    key_value_refs = refs[:-5]
    probs_ref, attended_ref, attn_out_ref, middle_ref, out_weight_ref = refs[-5:]
    out_piece = pieces[-1]
    low = index_ref[0] % LOW_COUNT
    size = sum(piece.size for piece in pieces)
    out_start = size - out_piece.size
    for order, first, matrix_rows, columns in tall_rows(out_piece, low):
        source = near_ref if order < 4 else far_ref
        first = first + (order % 4) * size + out_start
        out_weight_ref[matrix_rows, columns] = source[first : first + out_piece.own_rows, :]
    rows = tokens_ref.shape[0]
    allowed = allowed_ref[...] > 0.0
    keys = jnp.concatenate([ref[:, :HD] for ref in key_value_refs])
    values = jnp.concatenate([ref[:, HD:] for ref in key_value_refs])
    count = keys.shape[0]
    for head in range(HQ):
        columns = slice(head * HD, (head + 1) * HD)
        scores = product(query_ref[:, columns], keys, 1, 1) * HD ** (-0.5)
        scores = jnp.where(allowed, scores, -1e30)
        raised = jnp.exp(scores - jnp.max(scores, axis=-1, keepdims=True))
        probs = raised / jnp.sum(raised, axis=-1, keepdims=True)
        probs_ref[:, head * count : (head + 1) * count] = probs
        attended_ref[:, columns] = product(probs.astype(jnp.bfloat16), values, 1, 0).astype(
            jnp.bfloat16
        )
    attn_out = product(attended_ref[...], out_weight_ref[...], 1, 0)
    attn_out_ref[...] = attn_out
    _, normal = norm_parts(attn_out)
    middle_ref[...] = tokens_ref[...].astype(jnp.float32) + normal * (1.0 + gain_ref[...])


def attend_back_kernel(
    index_ref,
    grad_middle_ref,
    attn_out_ref,
    gain_ref,
    out_weight_ref,
    attended_ref,
    probs_ref,
    query_ref,
    *refs,
):
    part_count = (len(refs) - 3) // 2
    key_value_refs = refs[:part_count]
    grad_out_weight_ref, grad_query_ref, grad_gain_ref = refs[part_count : part_count + 3]
    grad_key_value_refs = refs[part_count + 3 :]
    rows = query_ref.shape[0]
    scale, normal = norm_parts(attn_out_ref[...])
    grad_attn, grad_gain_ref[...] = norm_back(scale, normal, grad_middle_ref[...], gain_ref[...])
    grad_attn = grad_attn.astype(jnp.bfloat16)
    grad_out_weight_ref[...] = product(attended_ref[...], grad_attn, 0, 0).astype(jnp.bfloat16)
    keys = jnp.concatenate([ref[:, :HD] for ref in key_value_refs])
    values = jnp.concatenate([ref[:, HD:] for ref in key_value_refs])
    count = keys.shape[0]
    grad_keys = jnp.zeros((count, HD), jnp.float32)
    grad_values = jnp.zeros((count, HD), jnp.float32)
    for head in range(HQ):
        columns = slice(head * HD, (head + 1) * HD)
        grad_attended = product(grad_attn, out_weight_ref[columns, :], 1, 1).astype(jnp.bfloat16)
        probs = probs_ref[:, head * count : (head + 1) * count]
        grad_probs = product(grad_attended, values, 1, 1)
        grad_values = grad_values + product(probs.astype(jnp.bfloat16), grad_attended, 0, 0)
        inner = jnp.sum(probs * grad_probs, axis=-1, keepdims=True)
        grad_scores = (probs * (grad_probs - inner) * HD ** (-0.5)).astype(jnp.bfloat16)
        grad_query_ref[:, columns] = product(grad_scores, keys, 1, 0)
        grad_keys = grad_keys + product(grad_scores, query_ref[:, columns], 0, 0)
    for part, ref in enumerate(grad_key_value_refs):
        ref[:, :HD] = grad_keys[part * rows : (part + 1) * rows].astype(ref.dtype)
        ref[:, HD:] = grad_values[part * rows : (part + 1) * rows].astype(ref.dtype)


def project_back_kernel(
    pieces,
    index_ref,
    tokens_ref,
    gain_ref,
    gain_query_ref,
    gain_key_ref,
    cosine_ref,
    sine_ref,
    order_ref,
    near_ref,
    far_ref,
    normed_ref,
    query_proj_ref,
    key_proj_ref,
    grad_query_ref,
    grad_middle_ref,
    grad_out_weight_ref,
    gain_attn_ref,
    gain_ffin_ref,
    gain_ffout_ref,
    *refs,
):
    key_value_refs = refs[:-4]
    input_grad_ref, grad_near_ref, grad_far_ref, grad_gain_ref = refs[-4:]
    low = index_ref[0] % LOW_COUNT
    size = sum(piece.size for piece in pieces)
    rows = pieces[0].block_rows
    cosine, sine = cosine_ref[...], sine_ref[...]
    normed = normed_ref[...]
    key_value = sum(ref[...].astype(jnp.float32) for ref in key_value_refs)
    grad_normed = jnp.zeros(tokens_ref.shape, jnp.float32)
    grad_gain_query = jnp.zeros((1, HD), jnp.float32)
    grad_gain_key = jnp.zeros((1, HD), jnp.float32)
    for head, start in enumerate(head_starts(pieces)):
        columns = slice(head * HD, (head + 1) * HD)
        if head < HQ:
            scale, normal = norm_parts(query_proj_ref[:, columns])
            upstream = turn(grad_query_ref[:, columns], cosine, -sine)
            grad, gain_row = norm_back(scale, normal, upstream, gain_query_ref[...])
            grad_gain_query = grad_gain_query + gain_row
        elif head == HQ:
            scale, normal = norm_parts(key_proj_ref[...])
            upstream = turn(key_value[:, :HD], cosine, -sine)
            grad, grad_gain_key = norm_back(scale, normal, upstream, gain_key_ref[...])
        else:
            grad = key_value[:, HD:]
        grad = grad.astype(jnp.bfloat16)
        weight = wide_head(near_ref, far_ref, size, start, rows)
        grad_normed = grad_normed + product(grad, weight, 1, 1)
        grad_weight = product(normed, grad, 0, 0).astype(jnp.bfloat16)
        for side in range(2):
            put_wide_tile(
                grad_near_ref,
                grad_far_ref,
                size,
                start + side * rows,
                rows,
                grad_weight[:, side * LANES : (side + 1) * LANES],
            )
    out_piece = pieces[-1]
    for order, first, matrix_rows, columns in tall_rows(out_piece, low):
        target = grad_near_ref if order < 4 else grad_far_ref
        first = first + (order % 4) * size + size - out_piece.size
        target[first : first + out_piece.own_rows, :] = grad_out_weight_ref[matrix_rows, columns]
    scale, normal = norm_parts(tokens_ref[...].astype(jnp.float32))
    grad_inputs, grad_gain_input = norm_back(
        scale, normal, unordered(grad_normed, order_ref[...]), gain_ref[...]
    )
    input_grad_ref[...] = (grad_middle_ref[...] + grad_inputs).astype(jnp.bfloat16)
    grad_gains = [
        grad_gain_input,
        gain_attn_ref[...],
        gain_ffin_ref[...],
        gain_ffout_ref[...],
        grad_gain_query,
        grad_gain_key,
    ]
    row = 0
    grad_gain_ref[...] = jnp.zeros(grad_gain_ref.shape, jnp.float32)
    for values in grad_gains:
        for start in range(0, values.shape[1], LANES):
            grad_gain_ref[row : row + 1, :] = values[:, start : start + LANES]
            row = row + 1
    for target in (grad_near_ref, grad_far_ref):
        target[4 * size :, :] = grad_gain_ref[...].astype(jnp.bfloat16)


def width_order(device_count):
    low = lax.axis_index(ALL_AXES) % LOW_COUNT
    rows = D // device_count
    high_count = device_count // LOW_COUNT
    column = jnp.arange(D, dtype=jnp.int32)
    place = column // (rows * high_count)
    mask = (place & 1) * 4 + ((place >> 1) & 1) * 2 + (place >> 2)
    high = (column // rows) % high_count
    picked = (high * LOW_COUNT + (low ^ mask)) * rows + column % rows
    return (jnp.arange(D, dtype=jnp.int32)[:, None] == picked[None, :]).astype(jnp.bfloat16)


GAIN_ROWS = 32


def shards_blocks(
    device_count,
    tokens,
    doc_ids,
    cotangent,
    master,
    first_moment,
    second_moment,
    gains,
    gain_first,
    gain_second,
):
    pieces = [Piece(*shape_pair, device_count) for shape_pair in piece_shapes()]
    attention_pieces = pieces[:4]
    local_rows = tokens.shape[0]
    group_size = lax.axis_size("group")
    first_row = lax.axis_index("group") * local_rows
    attention_rows = sum(piece.flat_rows for piece in attention_pieces)
    down_rows = pieces[6].flat_rows
    attention_blocks, later = gather_blocks(
        attention_pieces,
        master[:attention_rows].astype(jnp.bfloat16),
        (master[attention_rows:-down_rows], master[-down_rows:]),
    )
    gate_up_blocks, _ = gather_blocks(pieces[4:6], later[0])
    down_blocks, _ = gather_blocks(pieces[6:7], later[1])
    gain_parts = []
    for start, width in ((0, D), (D, D), (2 * D, D), (3 * D, D), (4 * D, HD), (4 * D + HD, HD)):
        gain_parts.append(gains[start : start + width][None])
    gain_input, gain_attn, gain_ffin, gain_ffout, gain_query, gain_key = gain_parts
    order = width_order(device_count)
    doc_row = doc_ids[0]
    angles = lax.dynamic_slice_in_dim(angles_of(positions(doc_row)), first_row, local_rows, 0)
    cosine, sine = jnp.cos(angles), jnp.sin(angles)
    query_docs = lax.dynamic_slice_in_dim(doc_row, first_row, local_rows, 0)
    reach = min(-(-(WINDOW - 1) // local_rows), group_size - 1)
    key_count = (reach + 1) * local_rows
    doc_pad = jnp.concatenate([jnp.full((reach * local_rows,), -1, jnp.int32), doc_row])
    key_docs = lax.dynamic_slice_in_dim(doc_pad, first_row, key_count, 0)
    key_index = first_row - reach * local_rows + jnp.arange(key_count, dtype=jnp.int32)
    query_index = first_row + jnp.arange(local_rows, dtype=jnp.int32)
    distance = query_index[:, None] - key_index[None, :]
    allowed = (distance >= 0) & (distance < WINDOW) & (key_docs[None, :] == query_docs[:, None])
    allowed = allowed.astype(jnp.float32)

    entry = (tokens, gain_input, gain_query, gain_key, cosine, sine, order)
    width = HQ * HD
    normed, query_proj, key_proj, query_rot, key_value = local_call(
        functools.partial(project_kernel, attention_pieces),
        (
            array((local_rows, D), jnp.bfloat16),
            array((local_rows, width), jnp.float32),
            array((local_rows, HD), jnp.float32),
            array((local_rows, width), jnp.bfloat16),
            array((local_rows, 2 * HD), jnp.bfloat16),
        ),
        (*entry, *attention_blocks),
    )
    key_values = [shifted(key_value, "group", offset) for offset in range(reach, 0, -1)]
    key_values.append(key_value)
    probs, attended, attn_out, middle, out_weight = local_call(
        functools.partial(attend_kernel, attention_pieces),
        (
            array((local_rows, HQ * key_count), jnp.float32),
            array((local_rows, width), jnp.bfloat16),
            array((local_rows, D), jnp.float32),
            array((local_rows, D), jnp.float32),
            array((width, D), jnp.bfloat16),
        ),
        (tokens, gain_attn, allowed, query_rot, *attention_blocks, *key_values),
    )
    outputs, grad_middle, grad_gain_ffin, grad_gain_ffout, grads_gate_up, grads_down = ffn_blocks(
        pieces, middle, cotangent, gain_ffin, gain_ffout, order, gate_up_blocks, down_blocks
    )
    grads_down = scatter_blocks(pieces[6:7], *grads_down)
    grads_gate_up = scatter_blocks(pieces[4:6], *grads_gate_up)
    grad_out_weight, grad_query, grad_gain_attn, *grad_key_values = local_call(
        attend_back_kernel,
        (
            array((width, D), jnp.bfloat16),
            array((local_rows, width), jnp.float32),
            array((1, D), jnp.float32),
            *(array((local_rows, 2 * HD), jnp.bfloat16),) * reach,
            array((local_rows, 2 * HD), jnp.float32),
        ),
        (
            grad_middle,
            attn_out,
            gain_attn,
            out_weight,
            attended,
            probs,
            query_rot,
            *key_values,
        ),
    )
    grad_key_values = [
        shifted(value, "group", place - reach) if place < reach else value
        for place, value in enumerate(grad_key_values)
    ]
    block_rows = attention_blocks[0].shape[0] + GAIN_ROWS
    grad_inputs, grad_near, grad_far, _ = local_call(
        functools.partial(project_back_kernel, attention_pieces),
        (
            array((local_rows, D), jnp.bfloat16),
            array((block_rows, LANES), jnp.bfloat16),
            array((block_rows, LANES), jnp.bfloat16),
            array((GAIN_ROWS, LANES), jnp.float32),
        ),
        (
            *entry,
            *attention_blocks,
            normed,
            query_proj,
            key_proj,
            grad_query,
            grad_middle,
            grad_out_weight,
            grad_gain_attn,
            grad_gain_ffin,
            grad_gain_ffout,
            *grad_key_values,
        ),
    )
    grads_attention = scatter_blocks(attention_pieces, grad_near, grad_far)
    gain_grads = grads_attention[attention_rows:].reshape(-1)[: gains.shape[0]]
    grads_local = jnp.concatenate([grads_attention[:attention_rows], grads_gate_up, grads_down])
    return (
        outputs,
        grad_inputs,
        *adam_update(grads_local, first_moment, second_moment, master, learn_rate, weight_decay),
        *adam_update(gain_grads, gain_first, gain_second, gains, gain_rate, 0.0),
    )


def shards(
    tokens, doc_ids, cotangent, master, first_moment, second_moment, gains, gain_first, gain_second
):
    group_size = lax.axis_size("group")
    devices_all = lax.axis_size("dp") * group_size
    if aligned(devices_all):
        return shards_blocks(
            devices_all,
            tokens,
            doc_ids,
            cotangent,
            master,
            first_moment,
            second_moment,
            gains,
            gain_first,
            gain_second,
        )
    group_index = lax.axis_index("group")
    local_rows = tokens.shape[0]
    shard_parts = [
        part_rows.astype(jnp.bfloat16) for part_rows in split_rows(master, piece_rows(devices_all))
    ]
    gathered = (
        lax.all_gather(shard_parts[0], ("dp", "group"), axis=0, tiled=True),
        lax.all_gather(shard_parts[1], ("dp", "group"), axis=0, tiled=True),
        lax.all_gather(shard_parts[2], ("dp", "group"), axis=0, tiled=True),
        lax.all_gather(shard_parts[3], ("dp", "group"), axis=0, tiled=True),
        lax.all_gather(shard_parts[4], ("dp", "group"), axis=0, tiled=True),
        lax.all_gather(shard_parts[5], ("dp", "group"), axis=0, tiled=True),
        lax.all_gather(shard_parts[6], ("dp", "group"), axis=0, tiled=True),
    )
    query_weight, key_weight, value_weight, out_weight, gate_weight, up_weight, down_weight = [
        full_rows.reshape(shape_pair) for full_rows, shape_pair in zip(gathered, piece_shapes())
    ]
    norm_input = gains[0:D]
    norm_attn = gains[D : 2 * D]
    norm_ffin = gains[2 * D : 3 * D]
    norm_ffout = gains[3 * D : 4 * D]
    norm_query = gains[4 * D : 4 * D + HD]
    norm_key = gains[4 * D + HD : 4 * D + 2 * HD]
    doc_row = doc_ids[0]
    first_row = group_index * local_rows
    angles = lax.dynamic_slice_in_dim(angles_of(positions(doc_row)), first_row, local_rows, 0)
    query_docs = lax.dynamic_slice_in_dim(doc_row, first_row, local_rows, 0)
    inputs = tokens.astype(jnp.float32)
    normed, back_input = jax.vjp(rms_norm, inputs, norm_input)
    normed_low = normed.astype(jnp.bfloat16)
    query_proj = matmul(normed_low, query_weight)
    key_proj = matmul(normed_low, key_weight)
    value_proj = matmul(normed_low, value_weight)

    def query_prep(flat_rows, gain_vec):
        return rotate(rms_norm(flat_rows.reshape(local_rows, HQ, HD), gain_vec), angles[:, None, :])

    def key_prep(rows_in, gain_vec):
        return rotate(rms_norm(rows_in, gain_vec), angles)

    query_rot, back_query = jax.vjp(query_prep, query_proj, norm_query)
    key_rot, back_key = jax.vjp(key_prep, key_proj, norm_key)
    query_low = query_rot.astype(jnp.bfloat16)
    key_low = key_rot.astype(jnp.bfloat16)
    value_low = value_proj.astype(jnp.bfloat16)
    reach = min(-(-(WINDOW - 1) // local_rows), group_size - 1)
    key_list = [key_low]
    value_list = [value_low]
    for offset in range(1, reach + 1):
        key_far, value_far = shifted((key_low, value_low), "group", offset)
        key_list.insert(0, key_far)
        value_list.insert(0, value_far)
    key_all = jnp.concatenate(key_list, axis=0)
    value_all = jnp.concatenate(value_list, axis=0)
    key_count = (reach + 1) * local_rows
    doc_pad = jnp.concatenate([jnp.full((reach * local_rows,), -1, jnp.int32), doc_row])
    key_docs = lax.dynamic_slice_in_dim(doc_pad, first_row, key_count, 0)
    key_index = (group_index - reach) * local_rows + jnp.arange(key_count, dtype=jnp.int32)
    query_index = first_row + jnp.arange(local_rows, dtype=jnp.int32)
    distance = query_index[:, None] - key_index[None, :]
    allowed = (distance >= 0) & (distance < WINDOW) & (key_docs[None, :] == query_docs[:, None])

    def scores_of(key_rows_low):
        raw_scores = jnp.einsum(
            "qhd,kd->hqk", query_low, key_rows_low, preferred_element_type=jnp.float32
        ) * HD ** (-0.5)
        return jnp.where(allowed[None], raw_scores, -1e30)

    masked = scores_of(key_all)
    top_score = jnp.max(masked, axis=-1, keepdims=True)
    log_total = top_score + jnp.log(jnp.sum(jnp.exp(masked - top_score), axis=-1, keepdims=True))
    probs = jnp.exp(masked - log_total)
    attended = jnp.einsum(
        "hqk,kd->qhd", probs.astype(jnp.bfloat16), value_all, preferred_element_type=jnp.float32
    )
    attended_low = attended.reshape(local_rows, HQ * HD).astype(jnp.bfloat16)
    attn_out = matmul(attended_low, out_weight)
    branch_one, back_attn = jax.vjp(rms_norm, attn_out, norm_attn)
    middle = inputs + branch_one
    normed_two, back_ffin = jax.vjp(rms_norm, middle, norm_ffin)
    normed_two_low = normed_two.astype(jnp.bfloat16)
    gate_proj = matmul(normed_two_low, gate_weight)
    up_proj = matmul(normed_two_low, up_weight)
    hidden, back_hidden = jax.vjp(geglu, gate_proj, up_proj)
    hidden_low = hidden.astype(jnp.bfloat16)
    ffn_out = matmul(hidden_low, down_weight)
    branch_two, back_ffout = jax.vjp(rms_norm, ffn_out, norm_ffout)
    outputs = middle + branch_two
    grad_out = cotangent.astype(jnp.float32)
    grad_ffn, grad_gain_ffout = back_ffout(grad_out)
    grad_ffn_low = grad_ffn.astype(jnp.bfloat16)
    grad_down_w = jnp.einsum(
        "tf,td->fd", hidden_low, grad_ffn_low, preferred_element_type=jnp.float32
    )
    grad_hidden = jnp.einsum(
        "td,fd->tf", grad_ffn_low, down_weight, preferred_element_type=jnp.float32
    )
    grad_gate, grad_up = back_hidden(grad_hidden)
    grad_gate_low = grad_gate.astype(jnp.bfloat16)
    grad_up_low = grad_up.astype(jnp.bfloat16)
    grad_gate_w = jnp.einsum(
        "td,tf->df", normed_two_low, grad_gate_low, preferred_element_type=jnp.float32
    )
    grad_up_w = jnp.einsum(
        "td,tf->df", normed_two_low, grad_up_low, preferred_element_type=jnp.float32
    )
    grad_normed_two = jnp.einsum(
        "tf,df->td", grad_gate_low, gate_weight, preferred_element_type=jnp.float32
    ) + jnp.einsum("tf,df->td", grad_up_low, up_weight, preferred_element_type=jnp.float32)
    grad_middle_norm, grad_gain_ffin = back_ffin(grad_normed_two)
    grad_middle = grad_out + grad_middle_norm
    grad_attn, grad_gain_attn = back_attn(grad_middle)
    grad_attn_low = grad_attn.astype(jnp.bfloat16)
    grad_out_w = jnp.einsum(
        "to,td->od", attended_low, grad_attn_low, preferred_element_type=jnp.float32
    )
    grad_attended = jnp.einsum(
        "td,od->to", grad_attn_low, out_weight, preferred_element_type=jnp.float32
    )
    grad_attended_low = grad_attended.astype(jnp.bfloat16).reshape(local_rows, HQ, HD)
    probs_again = jnp.exp(scores_of(key_all) - log_total)
    grad_probs = jnp.einsum(
        "qhd,kd->hqk", grad_attended_low, value_all, preferred_element_type=jnp.float32
    )
    grad_value_all = jnp.einsum(
        "hqk,qhd->kd",
        probs_again.astype(jnp.bfloat16),
        grad_attended_low,
        preferred_element_type=jnp.float32,
    )
    grad_scores = probs_again * (
        grad_probs - jnp.sum(probs_again * grad_probs, axis=-1, keepdims=True)
    )
    grad_scores_low = (grad_scores * HD ** (-0.5)).astype(jnp.bfloat16)
    grad_query = jnp.einsum(
        "hqk,kd->qhd", grad_scores_low, key_all, preferred_element_type=jnp.float32
    )
    grad_key_all = jnp.einsum(
        "hqk,qhd->kd", grad_scores_low, query_low, preferred_element_type=jnp.float32
    )
    key_total = grad_key_all[reach * local_rows :]
    value_total = grad_value_all[reach * local_rows :]
    for offset in range(1, reach + 1):
        row_start = (reach - offset) * local_rows
        key_back, value_back = (
            shifted(
                grad_key_all[row_start : row_start + local_rows].astype(jnp.bfloat16),
                "group",
                -offset,
            ).astype(jnp.float32),
            shifted(
                grad_value_all[row_start : row_start + local_rows].astype(jnp.bfloat16),
                "group",
                -offset,
            ).astype(jnp.float32),
        )
        key_total = key_total + key_back
        value_total = value_total + value_back
    grad_query_proj, grad_gain_query = back_query(grad_query)
    grad_key_proj, grad_gain_key = back_key(key_total)
    grad_query_low = grad_query_proj.astype(jnp.bfloat16)
    grad_key_low = grad_key_proj.astype(jnp.bfloat16)
    grad_value_low = value_total.astype(jnp.bfloat16)
    grad_query_w = jnp.einsum(
        "td,te->de", normed_low, grad_query_low, preferred_element_type=jnp.float32
    )
    grad_key_w = jnp.einsum(
        "td,te->de", normed_low, grad_key_low, preferred_element_type=jnp.float32
    )
    grad_value_w = jnp.einsum(
        "td,te->de", normed_low, grad_value_low, preferred_element_type=jnp.float32
    )
    grad_normed = jnp.einsum(
        "te,de->td", grad_query_low, query_weight, preferred_element_type=jnp.float32
    )
    grad_normed = grad_normed + jnp.einsum(
        "te,de->td", grad_key_low, key_weight, preferred_element_type=jnp.float32
    )
    grad_normed = grad_normed + jnp.einsum(
        "te,de->td", grad_value_low, value_weight, preferred_element_type=jnp.float32
    )
    grad_input_norm, grad_gain_input = back_input(grad_normed)
    grad_inputs = grad_middle + grad_input_norm
    flat_query = grad_query_w.reshape(-1, 128)
    flat_key = grad_key_w.reshape(-1, 128)
    flat_value = grad_value_w.reshape(-1, 128)
    flat_out = grad_out_w.reshape(-1, 128)
    flat_gate = grad_gate_w.reshape(-1, 128)
    flat_up = grad_up_w.reshape(-1, 128)
    flat_down = grad_down_w.reshape(-1, 128)
    reduced = (
        lax.psum_scatter(flat_query, ("dp", "group"), scatter_dimension=0, tiled=True),
        lax.psum_scatter(flat_key, ("dp", "group"), scatter_dimension=0, tiled=True),
        lax.psum_scatter(flat_value, ("dp", "group"), scatter_dimension=0, tiled=True),
        lax.psum_scatter(flat_out, ("dp", "group"), scatter_dimension=0, tiled=True),
        lax.psum_scatter(flat_gate, ("dp", "group"), scatter_dimension=0, tiled=True),
        lax.psum_scatter(flat_up, ("dp", "group"), scatter_dimension=0, tiled=True),
        lax.psum_scatter(flat_down, ("dp", "group"), scatter_dimension=0, tiled=True),
    )
    grads_local = jnp.concatenate(list(reduced), axis=0)
    gain_grads = lax.psum(
        jnp.concatenate(
            [
                grad_gain_input,
                grad_gain_attn,
                grad_gain_ffin,
                grad_gain_ffout,
                grad_gain_query,
                grad_gain_key,
            ]
        ),
        ("dp", "group"),
    )
    moment_first, moment_second, master_new = adam_update(
        grads_local, first_moment, second_moment, master, learn_rate, weight_decay
    )
    gain_moment_first, gain_moment_second, gains_new = adam_update(
        gain_grads, gain_first, gain_second, gains, gain_rate, 0.0
    )
    return (
        outputs.astype(jnp.bfloat16),
        grad_inputs.astype(jnp.bfloat16),
        moment_first,
        moment_second,
        master_new,
        gain_moment_first,
        gain_moment_second,
        gains_new,
    )


def solution(mesh):
    placed = (
        P(("dp", "group"), None),
        P("dp", None),
        P(("dp", "group"), None),
        P(("dp", "group"), None),
        P(("dp", "group"), None),
        P(("dp", "group"), None),
        P(),
        P(),
        P(),
    )
    return jax.shard_map(
        shards,
        mesh=mesh,
        in_specs=placed,
        out_specs=(
            P(("dp", "group"), None),
            P(("dp", "group"), None),
            P(("dp", "group"), None),
            P(("dp", "group"), None),
            P(("dp", "group"), None),
            P(),
            P(),
            P(),
        ),
        check_vma=False,
    )
```

```python
import functools
import math

import jax
import jax.numpy as jnp
from jax import lax
from jax.experimental import pallas as pl
from jax.experimental.pallas import tpu as pltpu
from jax.sharding import PartitionSpec as P

D = 640
HQ = 4
HD = 256
FF = 2048
WINDOW = 512
STEP = 10
ALL_AXES = ("dp", "group")


norm_eps = 1e-06
rope_base = 10000.0
beta_first = 0.9
beta_second = 0.999
learn_rate = 0.05
gain_rate = 0.25
adam_floor = 1e-08
weight_decay = 0.1


def shifted(value, axis, steps):
    count = lax.axis_size(axis)
    initial, last = (max(0, -steps), min(count, count - steps))
    return lax.ppermute(value, axis, [(source, source + steps) for source in range(initial, last)])


def rms_norm(values, weight_vec):
    return (
        values
        * lax.rsqrt(jnp.mean(values * values, axis=-1, keepdims=True) + norm_eps)
        * (1.0 + weight_vec)
    )


def positions(doc_row):
    length = doc_row.shape[0]
    counter = jnp.arange(length, dtype=jnp.int32)
    starts_here = jnp.concatenate([jnp.ones((1,), jnp.bool_), doc_row[1:] != doc_row[:-1]])
    begins = lax.cummax(jnp.where(starts_here, counter, jnp.zeros_like(counter)), axis=0)
    return counter - begins


def angles_of(places):
    half_dim = HD // 2
    frequency = rope_base ** (-(jnp.arange(half_dim, dtype=jnp.float32) * 2.0 / HD))
    return places.astype(jnp.float32)[:, None] * frequency[None, :]


def rotate(values, angles):
    half_dim = values.shape[-1] // 2
    first_half = values[..., :half_dim]
    second_half = values[..., half_dim:]
    cosine = jnp.cos(angles)
    sine_part = jnp.sin(angles)
    return jnp.concatenate(
        [
            first_half * cosine - second_half * sine_part,
            second_half * cosine + first_half * sine_part,
        ],
        axis=-1,
    )


def geglu(gate_in, up_in):
    return jax.nn.gelu(gate_in, approximate=True) * up_in


def adam_update(gradient, first_old, second_old, params_old, rate, decay_rate):
    first_new = beta_first * first_old + (1.0 - beta_first) * gradient
    second_new = beta_second * second_old + (1.0 - beta_second) * gradient * gradient
    first_hat = first_new / (1.0 - beta_first**STEP)
    second_hat = second_new / (1.0 - beta_second**STEP)
    params_new = params_old - rate * (
        first_hat / (jnp.sqrt(second_hat) + adam_floor) + decay_rate * params_old
    )
    return (first_new, second_new, params_new)


def piece_rows(device_count):
    return [
        entries // (128 * device_count)
        for entries in (D * HQ * HD, D * HD, D * HD, HQ * HD * D, D * FF, D * FF, FF * D)
    ]


def piece_shapes():
    return [(D, HQ * HD), (D, HD), (D, HD), (HQ * HD, D), (D, FF), (D, FF), (FF, D)]


def split_rows(stacked, row_list):
    result = []
    row_start = 0
    for row_count in row_list:
        result.append(stacked[row_start : row_start + row_count])
        row_start = row_start + row_count
    return result


def matmul(left_side, right_side):
    return jnp.dot(left_side, right_side, preferred_element_type=jnp.float32)


LOW_COUNT = 8
LANES = 128
LOW_MASKS = (0, 4, 2, 6, 1, 5, 3, 7)
GELU_SCALE = (2.0 / math.pi) ** 0.5
GELU_CUBE = 0.044715
VMEM_BYTES = 56 * 1024 * 1024


def aligned(device_count):
    return device_count % LOW_COUNT == 0 and D % device_count == 0


def swap(value, mask):
    count = lax.axis_size(ALL_AXES)
    return lax.ppermute(value, ALL_AXES, [(source, source ^ mask) for source in range(count)])


def local_call(kernel, outs, operands, scratch=(), behind=()):
    specs = [pl.BlockSpec(memory_space=pltpu.SMEM)]
    specs = specs + [pl.BlockSpec(memory_space=pltpu.VMEM)] * len(operands)
    specs = specs + [pl.BlockSpec(memory_space=pl.ANY)] * len(behind)
    first, last = 1 + len(operands), 1 + len(operands) + len(behind)

    def body(*refs):
        kernel(*refs[:first], *refs[last:])

    return pl.pallas_call(
        body,
        out_shape=outs,
        in_specs=specs,
        out_specs=tuple(pl.BlockSpec(memory_space=pltpu.VMEM) for _ in outs),
        scratch_shapes=scratch,
        compiler_params=pltpu.CompilerParams(vmem_limit_bytes=VMEM_BYTES),
        cost_estimate=pl.CostEstimate(flops=0, bytes_accessed=0, transcendentals=0),
    )(lax.axis_index(ALL_AXES).astype(jnp.int32).reshape(1), *operands, *behind)


class Piece:
    def __init__(self, rows, columns, device_count):
        self.rows = rows
        self.columns = columns
        self.wide = rows == D
        self.blocks = columns // LANES
        self.own_rows = rows // device_count
        self.flat_rows = self.own_rows * self.blocks
        self.high_count = device_count // LOW_COUNT
        self.block_rows = self.own_rows * self.high_count
        self.size = self.block_rows * self.blocks


def round_kernel(index_ref, in_ref, out_ref):
    out_ref[...] = in_ref[...].astype(jnp.bfloat16)


def halves_kernel(index_ref, first_ref, second_ref, first_out_ref, second_out_ref):
    half = first_out_ref.shape[0]
    first_out_ref[...] = first_ref[:half, :]
    second_out_ref[...] = second_ref[half:, :]


def pack_kernel(pieces, index_ref, *refs):
    high_count = pieces[0].high_count
    parts, out_ref, flat, packed = refs[:high_count], refs[-3], refs[-2], refs[-1]
    high = index_ref[0] // LOW_COUNT
    for step, part in enumerate(parts):
        flat[high ^ step] = part[...].astype(jnp.float32)
    start, target = 0, 0
    for piece in pieces:
        for block in range(piece.blocks):
            for place in range(high_count):
                packed[pl.ds(target, piece.own_rows), :] = flat[
                    place, pl.ds(start + block, piece.own_rows, stride=piece.blocks), :
                ]
                target = target + piece.own_rows
        start = start + piece.flat_rows
    out_ref[...] = packed[...].astype(jnp.bfloat16)


def unpack_kernel(pieces, extra_count, index_ref, *refs):
    high_count = pieces[0].high_count
    size = sum(piece.size for piece in pieces)
    flat_rows = sum(piece.flat_rows for piece in pieces)
    terms, outs, flat, packed = refs[:3], refs[-2 - high_count : -2], refs[-2], refs[-1]
    high = index_ref[0] // LOW_COUNT
    packed[...] = sum(term[:size, :].astype(jnp.float32) for term in terms)
    start, source = 0, 0
    for piece in pieces:
        for block in range(piece.blocks):
            for place in range(high_count):
                flat[place, pl.ds(start + block, piece.own_rows, stride=piece.blocks), :] = packed[
                    pl.ds(source, piece.own_rows), :
                ]
                source = source + piece.own_rows
        start = start + piece.flat_rows
    for step, out_ref in enumerate(outs):
        out_ref[:flat_rows, :] = flat[high ^ step].astype(out_ref.dtype)
        if extra_count:
            extra = terms[2][size:, :].astype(jnp.float32) + refs[3][...].astype(jnp.float32)
            out_ref[flat_rows:, :] = extra.astype(out_ref.dtype)


def array(shape, kind):
    return jax.ShapeDtypeStruct(shape, kind)


def gather_high(rows):
    high_count = lax.axis_size(ALL_AXES) // LOW_COUNT
    return [rows] + [swap(rows, step * LOW_COUNT) for step in range(1, high_count)]


def gather_near(pieces, parts, behind=()):
    high_count = pieces[0].high_count
    size = sum(piece.size for piece in pieces)
    (own,) = local_call(
        functools.partial(pack_kernel, pieces),
        (array((size, LANES), jnp.bfloat16),),
        parts,
        (
            pltpu.VMEM((high_count, parts[0].shape[0], LANES), jnp.float32),
            pltpu.VMEM((size, LANES), jnp.float32),
        ),
        behind,
    )
    return own, swap(own, 4), swap(own, 2)


def gather_diagonal(own, beside, across, behind=()):
    half = own.shape[0] // 2
    to_x, to_y = local_call(
        halves_kernel,
        (array((half, LANES), jnp.bfloat16),) * 2,
        (across, beside),
        (),
        behind,
    )
    three = jnp.concatenate([own, beside, across])
    diagonal = jnp.concatenate([swap(to_x, 4), swap(to_y, 2)])
    return three, diagonal, swap(three, 1), swap(diagonal, 1)


def sum_cores(near_three, near_one, far_three, far_one):
    one = near_one.astype(jnp.float32) + swap(far_one, 1).astype(jnp.float32)
    three = near_three.astype(jnp.float32) + swap(far_three, 1).astype(jnp.float32)
    return three, one


def scatter_blocks(pieces, three, one):
    high_count = pieces[0].high_count
    size = sum(piece.size for piece in pieces)
    flat_rows = sum(piece.flat_rows for piece in pieces)
    extra_count = one.shape[0] - size
    half = size // 2
    over_x = swap(jnp.concatenate([one[:half], one[size:]]).astype(jnp.bfloat16), 4)
    over_x = over_x.astype(jnp.float32)
    over_y = swap(one[half:size].astype(jnp.bfloat16), 2).astype(jnp.float32)
    extra = one[size:] + over_x[half:]
    across = jnp.concatenate(
        [three[2 * size : 2 * size + half] + over_x[:half], three[2 * size + half :], extra]
    ).astype(jnp.bfloat16)
    beside = jnp.concatenate(
        [three[size : size + half], three[size + half : 2 * size] + over_y]
    ).astype(jnp.bfloat16)
    terms = [three[:size], swap(beside, 4), swap(across, 2)]
    if extra_count:
        terms.append(extra)
    outs = local_call(
        functools.partial(unpack_kernel, pieces, extra_count),
        (array((flat_rows + extra_count, LANES), jnp.float32),)
        + (array((flat_rows + extra_count, LANES), jnp.bfloat16),) * (high_count - 1),
        terms,
        (
            pltpu.VMEM((high_count, flat_rows, LANES), jnp.float32),
            pltpu.VMEM((size, LANES), jnp.float32),
        ),
    )
    return outs[0] + sum(
        swap(send, step * LOW_COUNT).astype(jnp.float32) for step, send in enumerate(outs) if step
    )


def norm_parts(values):
    scale = lax.rsqrt(jnp.mean(values * values, axis=-1, keepdims=True) + norm_eps)
    return scale, values * scale


def norm_back(scale, normal, upstream, weight_vec):
    weighted = upstream * (1.0 + weight_vec)
    inner = jnp.mean(weighted * normal, axis=-1, keepdims=True)
    return scale * (weighted - normal * inner), jnp.sum(normal * upstream, axis=0, keepdims=True)


def product(left_side, right_side, left_axis, right_axis):
    return lax.dot_general(
        left_side,
        right_side,
        (((left_axis,), (right_axis,)), ((), ())),
        preferred_element_type=jnp.float32,
    )


def unordered(rows_in, order_low):
    upper = rows_in.astype(jnp.bfloat16)
    lower = (rows_in - upper.astype(jnp.float32)).astype(jnp.bfloat16)
    return product(upper, order_low, 1, 1) + product(lower, order_low, 1, 1)


def low_block(refs, size, order):
    three, one = refs[:2] if order < 4 else refs[2:]
    return (one, 0) if order % 4 == 3 else (three, order % 4 * size)


def wide_tile(refs, size, start, rows):
    tiles = []
    for order in range(LOW_COUNT):
        ref, first = low_block(refs, size, order)
        tiles.append(ref[first + start : first + start + rows, :])
    return jnp.concatenate(tiles)


def put_wide_tile(refs, size, start, rows, tile):
    for order in range(LOW_COUNT):
        ref, first = low_block(refs, size, order)
        ref[first + start : first + start + rows, :] = tile[order * rows : (order + 1) * rows]


def tall_rows(piece, low):
    for order, mask in enumerate(LOW_MASKS):
        for block in range(piece.blocks):
            for place in range(piece.high_count):
                row = (place * LOW_COUNT + (low ^ mask)) * piece.own_rows
                yield (
                    order,
                    block * piece.block_rows + place * piece.own_rows,
                    pl.ds(pl.multiple_of(row, piece.own_rows), piece.own_rows),
                    slice(block * LANES, (block + 1) * LANES),
                )


def ffn_kernel(
    gate_piece,
    down_piece,
    index_ref,
    middle_ref,
    cotangent_ref,
    gain_in_ref,
    gain_out_ref,
    order_ref,
    *refs,
):
    weight_refs, grad_refs = refs[:4], refs[8:12]
    block_out_ref, grad_middle_ref, grad_gain_in_ref, grad_gain_out_ref = refs[4:8]
    down_ref, hidden_ref, gelu_ref, slope_ref = refs[12:]
    low = index_ref[0] % LOW_COUNT
    rows = gate_piece.block_rows
    size = 2 * gate_piece.size + down_piece.size
    width = 2 * LANES
    for order, start, matrix_rows, columns in tall_rows(down_piece, low):
        source, first = low_block(weight_refs, size, order)
        first = first + start + 2 * gate_piece.size
        down_ref[matrix_rows, columns] = source[first : first + down_piece.own_rows, :]

    def wide_tiles(step):
        return [
            jnp.concatenate(
                [
                    wide_tile(weight_refs, size, offset + block * rows, rows)
                    for block in (2 * step, 2 * step + 1)
                ],
                axis=1,
            )
            for offset in (0, gate_piece.size)
        ]

    middle = middle_ref[...]
    scale_in, normal_in = norm_parts(middle)
    order_low = order_ref[...]
    normed = (normal_in * (1.0 + gain_in_ref[...])).astype(jnp.bfloat16)
    normed = product(normed, order_low, 1, 0).astype(jnp.bfloat16)
    for step in range(FF // width):
        columns = slice(step * width, (step + 1) * width)
        gate_weight, up_weight = wide_tiles(step)
        gate = product(normed, gate_weight, 1, 0)
        up = product(normed, up_weight, 1, 0)
        square = gate * gate
        bend = jnp.tanh(GELU_SCALE * gate * (1.0 + GELU_CUBE * square))
        half = 0.5 * (1.0 + bend)
        gelu = gate * half
        slope = half + 0.5 * gate * (1.0 - bend * bend) * GELU_SCALE * (
            1.0 + 3.0 * GELU_CUBE * square
        )
        gelu_ref[:, columns] = gelu
        slope_ref[:, columns] = slope * up
        hidden_ref[:, columns] = (gelu * up).astype(jnp.bfloat16)
    hidden = hidden_ref[...]
    scale_out, normal_out = norm_parts(product(hidden, down_ref[...], 1, 0))
    block_out_ref[...] = (middle + normal_out * (1.0 + gain_out_ref[...])).astype(jnp.bfloat16)
    upstream = cotangent_ref[...].astype(jnp.float32)
    grad_ffn, grad_gain_out_ref[...] = norm_back(
        scale_out, normal_out, upstream, gain_out_ref[...]
    )
    grad_ffn = grad_ffn.astype(jnp.bfloat16)
    grad_normed = jnp.zeros(middle.shape, jnp.float32)
    for step in range(FF // width):
        columns = slice(step * width, (step + 1) * width)
        grad_hidden = product(grad_ffn, down_ref[columns, :], 1, 1)
        down_ref[columns, :] = product(hidden_ref[:, columns], grad_ffn, 0, 0).astype(jnp.bfloat16)
        grads = [
            (grad_hidden * slope_ref[:, columns]).astype(jnp.bfloat16),
            (grad_hidden * gelu_ref[:, columns]).astype(jnp.bfloat16),
        ]
        for place, (grad, weight) in enumerate(zip(grads, wide_tiles(step))):
            grad_weight = product(normed, grad, 0, 0).astype(jnp.bfloat16)
            for side in range(2):
                put_wide_tile(
                    grad_refs,
                    size,
                    place * gate_piece.size + (2 * step + side) * rows,
                    rows,
                    grad_weight[:, side * LANES : (side + 1) * LANES],
                )
            grad_normed = grad_normed + product(grad, weight, 1, 1)
    for order, start, matrix_rows, columns in tall_rows(down_piece, low):
        target, first = low_block(grad_refs, size, order)
        first = first + start + 2 * gate_piece.size
        target[first : first + down_piece.own_rows, :] = down_ref[matrix_rows, columns]
    grad_middle, grad_gain_in_ref[...] = norm_back(
        scale_in, normal_in, unordered(grad_normed, order_low), gain_in_ref[...]
    )
    grad_middle_ref[...] = upstream + grad_middle


def ffn_blocks(pieces, middle, cotangent, gain_in, gain_out, order, blocks):
    rows = middle.shape[0]
    outs = local_call(
        functools.partial(ffn_kernel, pieces[4], pieces[6]),
        (
            array((rows, D), jnp.bfloat16),
            array((rows, D), jnp.float32),
            array((1, D), jnp.float32),
            array((1, D), jnp.float32),
            *(array(value.shape, jnp.bfloat16) for value in blocks),
        ),
        (middle, cotangent, gain_in, gain_out, order, *blocks),
        (
            pltpu.VMEM((FF, D), jnp.bfloat16),
            pltpu.VMEM((rows, FF), jnp.bfloat16),
            pltpu.VMEM((rows, FF), jnp.float32),
            pltpu.VMEM((rows, FF), jnp.float32),
        ),
    )
    return *outs[:4], outs[4:]


def turn(values, cosine, sine):
    first_half, second_half = values[:, : HD // 2], values[:, HD // 2 :]
    return jnp.concatenate(
        [first_half * cosine - second_half * sine, second_half * cosine + first_half * sine], axis=1
    )


def wide_head(refs, size, start, rows):
    return jnp.concatenate(
        [wide_tile(refs, size, start + side * rows, rows) for side in range(2)], axis=1
    )


def head_starts(pieces):
    rows = pieces[0].block_rows
    return [2 * rows * head for head in range(HQ + 2)]


def project_kernel(
    pieces,
    index_ref,
    tokens_ref,
    gain_ref,
    gain_query_ref,
    gain_key_ref,
    cosine_ref,
    sine_ref,
    order_ref,
    *refs,
):
    weight_refs = refs[:4]
    normed_ref, query_proj_ref, key_proj_ref, query_ref, key_value_ref = refs[4:]
    size = sum(piece.size for piece in pieces)
    rows = pieces[0].block_rows
    cosine, sine = cosine_ref[...], sine_ref[...]
    _, normal = norm_parts(tokens_ref[...].astype(jnp.float32))
    normed = (normal * (1.0 + gain_ref[...])).astype(jnp.bfloat16)
    normed = product(normed, order_ref[...], 1, 0).astype(jnp.bfloat16)
    normed_ref[...] = normed
    starts = head_starts(pieces)
    for head, start in enumerate(starts):
        proj = product(normed, wide_head(weight_refs, size, start, rows), 1, 0)
        columns = slice(head * HD, (head + 1) * HD)
        if head == HQ + 1:
            key_value_ref[:, HD:] = proj.astype(jnp.bfloat16)
            continue
        gain_vec = gain_query_ref[...] if head < HQ else gain_key_ref[...]
        _, normal = norm_parts(proj)
        turned = turn(normal * (1.0 + gain_vec), cosine, sine).astype(jnp.bfloat16)
        if head < HQ:
            query_proj_ref[:, columns] = proj
            query_ref[:, columns] = turned
        else:
            key_proj_ref[...] = proj
            key_value_ref[:, :HD] = turned


def attend_kernel(
    pieces,
    index_ref,
    tokens_ref,
    gain_ref,
    allowed_ref,
    query_ref,
    *refs,
):
    weight_refs, key_value_refs = refs[:4], refs[4:-5]
    probs_ref, attended_ref, attn_out_ref, middle_ref, out_weight_ref = refs[-5:]
    out_piece = pieces[-1]
    low = index_ref[0] % LOW_COUNT
    size = sum(piece.size for piece in pieces)
    out_start = size - out_piece.size
    for order, start, matrix_rows, columns in tall_rows(out_piece, low):
        source, first = low_block(weight_refs, size, order)
        first = first + start + out_start
        out_weight_ref[matrix_rows, columns] = source[first : first + out_piece.own_rows, :]
    rows = tokens_ref.shape[0]
    allowed = allowed_ref[...] > 0.0
    keys = jnp.concatenate([ref[:, :HD] for ref in key_value_refs])
    values = jnp.concatenate([ref[:, HD:] for ref in key_value_refs])
    count = keys.shape[0]
    for head in range(HQ):
        columns = slice(head * HD, (head + 1) * HD)
        scores = product(query_ref[:, columns], keys, 1, 1) * HD ** (-0.5)
        scores = jnp.where(allowed, scores, -1e30)
        raised = jnp.exp(scores - jnp.max(scores, axis=-1, keepdims=True))
        probs = raised / jnp.sum(raised, axis=-1, keepdims=True)
        probs_ref[:, head * count : (head + 1) * count] = probs
        attended_ref[:, columns] = product(probs.astype(jnp.bfloat16), values, 1, 0).astype(
            jnp.bfloat16
        )
    attn_out = product(attended_ref[...], out_weight_ref[...], 1, 0)
    attn_out_ref[...] = attn_out
    _, normal = norm_parts(attn_out)
    middle_ref[...] = tokens_ref[...].astype(jnp.float32) + normal * (1.0 + gain_ref[...])


def attend_back_kernel(
    index_ref,
    grad_middle_ref,
    attn_out_ref,
    gain_ref,
    out_weight_ref,
    attended_ref,
    probs_ref,
    query_ref,
    *refs,
):
    part_count = (len(refs) - 3) // 2
    key_value_refs = refs[:part_count]
    grad_out_weight_ref, grad_query_ref, grad_gain_ref = refs[part_count : part_count + 3]
    grad_key_value_refs = refs[part_count + 3 :]
    rows = query_ref.shape[0]
    scale, normal = norm_parts(attn_out_ref[...])
    grad_attn, grad_gain_ref[...] = norm_back(scale, normal, grad_middle_ref[...], gain_ref[...])
    grad_attn = grad_attn.astype(jnp.bfloat16)
    grad_out_weight_ref[...] = product(attended_ref[...], grad_attn, 0, 0).astype(jnp.bfloat16)
    keys = jnp.concatenate([ref[:, :HD] for ref in key_value_refs])
    values = jnp.concatenate([ref[:, HD:] for ref in key_value_refs])
    count = keys.shape[0]
    grad_keys = jnp.zeros((count, HD), jnp.float32)
    grad_values = jnp.zeros((count, HD), jnp.float32)
    for head in range(HQ):
        columns = slice(head * HD, (head + 1) * HD)
        grad_attended = product(grad_attn, out_weight_ref[columns, :], 1, 1).astype(jnp.bfloat16)
        probs = probs_ref[:, head * count : (head + 1) * count]
        grad_probs = product(grad_attended, values, 1, 1)
        grad_values = grad_values + product(probs.astype(jnp.bfloat16), grad_attended, 0, 0)
        inner = jnp.sum(probs * grad_probs, axis=-1, keepdims=True)
        grad_scores = (probs * (grad_probs - inner) * HD ** (-0.5)).astype(jnp.bfloat16)
        grad_query_ref[:, columns] = product(grad_scores, keys, 1, 0)
        grad_keys = grad_keys + product(grad_scores, query_ref[:, columns], 0, 0)
    for part, ref in enumerate(grad_key_value_refs):
        ref[:, :HD] = grad_keys[part * rows : (part + 1) * rows].astype(ref.dtype)
        ref[:, HD:] = grad_values[part * rows : (part + 1) * rows].astype(ref.dtype)


def project_back_kernel(
    pieces,
    index_ref,
    tokens_ref,
    gain_ref,
    gain_query_ref,
    gain_key_ref,
    cosine_ref,
    sine_ref,
    order_ref,
    normed_ref,
    query_proj_ref,
    key_proj_ref,
    grad_query_ref,
    grad_middle_ref,
    grad_out_weight_ref,
    gain_attn_ref,
    gain_ffin_ref,
    gain_ffout_ref,
    *refs,
):
    weight_refs, key_value_refs, grad_refs = refs[:4], refs[4:-6], refs[-6:-2]
    input_grad_ref, grad_gain_ref = refs[-2:]
    low = index_ref[0] % LOW_COUNT
    size = sum(piece.size for piece in pieces)
    rows = pieces[0].block_rows
    cosine, sine = cosine_ref[...], sine_ref[...]
    normed = normed_ref[...]
    key_value = sum(ref[...].astype(jnp.float32) for ref in key_value_refs)
    grad_normed = jnp.zeros(tokens_ref.shape, jnp.float32)
    grad_gain_query = jnp.zeros((1, HD), jnp.float32)
    grad_gain_key = jnp.zeros((1, HD), jnp.float32)
    for head, start in enumerate(head_starts(pieces)):
        columns = slice(head * HD, (head + 1) * HD)
        if head < HQ:
            scale, normal = norm_parts(query_proj_ref[:, columns])
            upstream = turn(grad_query_ref[:, columns], cosine, -sine)
            grad, gain_row = norm_back(scale, normal, upstream, gain_query_ref[...])
            grad_gain_query = grad_gain_query + gain_row
        elif head == HQ:
            scale, normal = norm_parts(key_proj_ref[...])
            upstream = turn(key_value[:, :HD], cosine, -sine)
            grad, grad_gain_key = norm_back(scale, normal, upstream, gain_key_ref[...])
        else:
            grad = key_value[:, HD:]
        grad = grad.astype(jnp.bfloat16)
        weight = wide_head(weight_refs, size, start, rows)
        grad_normed = grad_normed + product(grad, weight, 1, 1)
        grad_weight = product(normed, grad, 0, 0).astype(jnp.bfloat16)
        for side in range(2):
            put_wide_tile(
                grad_refs,
                size,
                start + side * rows,
                rows,
                grad_weight[:, side * LANES : (side + 1) * LANES],
            )
    out_piece = pieces[-1]
    for order, start, matrix_rows, columns in tall_rows(out_piece, low):
        target, first = low_block(grad_refs, size, order)
        first = first + start + size - out_piece.size
        target[first : first + out_piece.own_rows, :] = grad_out_weight_ref[matrix_rows, columns]
    scale, normal = norm_parts(tokens_ref[...].astype(jnp.float32))
    grad_inputs, grad_gain_input = norm_back(
        scale, normal, unordered(grad_normed, order_ref[...]), gain_ref[...]
    )
    input_grad_ref[...] = (grad_middle_ref[...] + grad_inputs).astype(jnp.bfloat16)
    grad_gains = [
        grad_gain_input,
        gain_attn_ref[...],
        gain_ffin_ref[...],
        gain_ffout_ref[...],
        grad_gain_query,
        grad_gain_key,
    ]
    row = 0
    grad_gain_ref[...] = jnp.zeros(grad_gain_ref.shape, jnp.float32)
    for values in grad_gains:
        for start in range(0, values.shape[1], LANES):
            grad_gain_ref[row : row + 1, :] = values[:, start : start + LANES]
            row = row + 1
    for target in (grad_refs[1], grad_refs[3]):
        target[size:, :] = grad_gain_ref[...].astype(jnp.bfloat16)


def width_order(device_count):
    low = lax.axis_index(ALL_AXES) % LOW_COUNT
    rows = D // device_count
    high_count = device_count // LOW_COUNT
    column = jnp.arange(D, dtype=jnp.int32)
    place = column // (rows * high_count)
    mask = (place & 1) * 4 + ((place >> 1) & 1) * 2 + (place >> 2)
    high = (column // rows) % high_count
    picked = (high * LOW_COUNT + (low ^ mask)) * rows + column % rows
    return (jnp.arange(D, dtype=jnp.int32)[:, None] == picked[None, :]).astype(jnp.bfloat16)


GAIN_ROWS = 32


def shards_blocks(
    device_count,
    tokens,
    doc_ids,
    cotangent,
    master,
    first_moment,
    second_moment,
    gains,
    gain_first,
    gain_second,
):
    pieces = [Piece(*shape_pair, device_count) for shape_pair in piece_shapes()]
    attention_pieces = pieces[:4]
    local_rows = tokens.shape[0]
    group_size = lax.axis_size("group")
    first_row = lax.axis_index("group") * local_rows
    attention_rows = sum(piece.flat_rows for piece in attention_pieces)
    attention_parts = gather_high(master[:attention_rows].astype(jnp.bfloat16))
    (ffn_rows,) = local_call(
        round_kernel,
        (array((master.shape[0] - attention_rows, LANES), jnp.bfloat16),),
        (master[attention_rows:],),
        (),
        attention_parts[1:],
    )
    ffn_parts = gather_high(ffn_rows)
    attention_blocks = gather_diagonal(*gather_near(attention_pieces, attention_parts))
    ffn_near = gather_near(pieces[4:7], ffn_parts, (attention_blocks[1],))
    gain_parts = []
    for start, width in ((0, D), (D, D), (2 * D, D), (3 * D, D), (4 * D, HD), (4 * D + HD, HD)):
        gain_parts.append(gains[start : start + width][None])
    gain_input, gain_attn, gain_ffin, gain_ffout, gain_query, gain_key = gain_parts
    order = width_order(device_count)
    doc_row = doc_ids[0]
    angles = lax.dynamic_slice_in_dim(angles_of(positions(doc_row)), first_row, local_rows, 0)
    cosine, sine = jnp.cos(angles), jnp.sin(angles)
    query_docs = lax.dynamic_slice_in_dim(doc_row, first_row, local_rows, 0)
    reach = min(-(-(WINDOW - 1) // local_rows), group_size - 1)
    key_count = (reach + 1) * local_rows
    doc_pad = jnp.concatenate([jnp.full((reach * local_rows,), -1, jnp.int32), doc_row])
    key_docs = lax.dynamic_slice_in_dim(doc_pad, first_row, key_count, 0)
    key_index = first_row - reach * local_rows + jnp.arange(key_count, dtype=jnp.int32)
    query_index = first_row + jnp.arange(local_rows, dtype=jnp.int32)
    distance = query_index[:, None] - key_index[None, :]
    allowed = (distance >= 0) & (distance < WINDOW) & (key_docs[None, :] == query_docs[:, None])
    allowed = allowed.astype(jnp.float32)

    entry = (tokens, gain_input, gain_query, gain_key, cosine, sine, order)
    width = HQ * HD
    normed, query_proj, key_proj, query_rot, key_value = local_call(
        functools.partial(project_kernel, attention_pieces),
        (
            array((local_rows, D), jnp.bfloat16),
            array((local_rows, width), jnp.float32),
            array((local_rows, HD), jnp.float32),
            array((local_rows, width), jnp.bfloat16),
            array((local_rows, 2 * HD), jnp.bfloat16),
        ),
        (*entry, *attention_blocks),
    )
    key_values = [shifted(key_value, "group", offset) for offset in range(reach, 0, -1)]
    key_values.append(key_value)
    probs, attended, attn_out, middle, out_weight = local_call(
        functools.partial(attend_kernel, attention_pieces),
        (
            array((local_rows, HQ * key_count), jnp.float32),
            array((local_rows, width), jnp.bfloat16),
            array((local_rows, D), jnp.float32),
            array((local_rows, D), jnp.float32),
            array((width, D), jnp.bfloat16),
        ),
        (tokens, gain_attn, allowed, query_rot, *attention_blocks, *key_values),
    )
    ffn_weights = gather_diagonal(*ffn_near, (key_value,))
    outputs, grad_middle, grad_gain_ffin, grad_gain_ffout, grads_ffn = ffn_blocks(
        pieces, middle, cotangent, gain_ffin, gain_ffout, order, ffn_weights
    )
    ffn_three, ffn_one = sum_cores(*grads_ffn)
    grads_ffn = scatter_blocks(pieces[4:7], ffn_three, ffn_one)
    grad_out_weight, grad_query, grad_gain_attn, *grad_key_values = local_call(
        attend_back_kernel,
        (
            array((width, D), jnp.bfloat16),
            array((local_rows, width), jnp.float32),
            array((1, D), jnp.float32),
            *(array((local_rows, 2 * HD), jnp.bfloat16),) * reach,
            array((local_rows, 2 * HD), jnp.float32),
        ),
        (
            grad_middle,
            attn_out,
            gain_attn,
            out_weight,
            attended,
            probs,
            query_rot,
            *key_values,
        ),
    )
    grad_key_values = [
        shifted(value, "group", place - reach) if place < reach else value
        for place, value in enumerate(grad_key_values)
    ]
    block_rows = attention_blocks[1].shape[0] + GAIN_ROWS
    *grads_attention, grad_inputs, _ = local_call(
        functools.partial(project_back_kernel, attention_pieces),
        (
            array(attention_blocks[0].shape, jnp.bfloat16),
            array((block_rows, LANES), jnp.bfloat16),
            array(attention_blocks[0].shape, jnp.bfloat16),
            array((block_rows, LANES), jnp.bfloat16),
            array((local_rows, D), jnp.bfloat16),
            array((GAIN_ROWS, LANES), jnp.float32),
        ),
        (
            *entry,
            normed,
            query_proj,
            key_proj,
            grad_query,
            grad_middle,
            grad_out_weight,
            grad_gain_attn,
            grad_gain_ffin,
            grad_gain_ffout,
            *attention_blocks,
            *grad_key_values,
        ),
        (),
        (ffn_three, ffn_one),
    )
    grads_attention = scatter_blocks(attention_pieces, *sum_cores(*grads_attention))
    gain_grads = grads_attention[attention_rows:].reshape(-1)[: gains.shape[0]]
    grads_local = jnp.concatenate([grads_attention[:attention_rows], grads_ffn])
    return (
        outputs,
        grad_inputs,
        *adam_update(grads_local, first_moment, second_moment, master, learn_rate, weight_decay),
        *adam_update(gain_grads, gain_first, gain_second, gains, gain_rate, 0.0),
    )


def shards(
    tokens, doc_ids, cotangent, master, first_moment, second_moment, gains, gain_first, gain_second
):
    group_size = lax.axis_size("group")
    devices_all = lax.axis_size("dp") * group_size
    if aligned(devices_all):
        return shards_blocks(
            devices_all,
            tokens,
            doc_ids,
            cotangent,
            master,
            first_moment,
            second_moment,
            gains,
            gain_first,
            gain_second,
        )
    group_index = lax.axis_index("group")
    local_rows = tokens.shape[0]
    shard_parts = [
        part_rows.astype(jnp.bfloat16) for part_rows in split_rows(master, piece_rows(devices_all))
    ]
    gathered = (
        lax.all_gather(shard_parts[0], ("dp", "group"), axis=0, tiled=True),
        lax.all_gather(shard_parts[1], ("dp", "group"), axis=0, tiled=True),
        lax.all_gather(shard_parts[2], ("dp", "group"), axis=0, tiled=True),
        lax.all_gather(shard_parts[3], ("dp", "group"), axis=0, tiled=True),
        lax.all_gather(shard_parts[4], ("dp", "group"), axis=0, tiled=True),
        lax.all_gather(shard_parts[5], ("dp", "group"), axis=0, tiled=True),
        lax.all_gather(shard_parts[6], ("dp", "group"), axis=0, tiled=True),
    )
    query_weight, key_weight, value_weight, out_weight, gate_weight, up_weight, down_weight = [
        full_rows.reshape(shape_pair) for full_rows, shape_pair in zip(gathered, piece_shapes())
    ]
    norm_input = gains[0:D]
    norm_attn = gains[D : 2 * D]
    norm_ffin = gains[2 * D : 3 * D]
    norm_ffout = gains[3 * D : 4 * D]
    norm_query = gains[4 * D : 4 * D + HD]
    norm_key = gains[4 * D + HD : 4 * D + 2 * HD]
    doc_row = doc_ids[0]
    first_row = group_index * local_rows
    angles = lax.dynamic_slice_in_dim(angles_of(positions(doc_row)), first_row, local_rows, 0)
    query_docs = lax.dynamic_slice_in_dim(doc_row, first_row, local_rows, 0)
    inputs = tokens.astype(jnp.float32)
    normed, back_input = jax.vjp(rms_norm, inputs, norm_input)
    normed_low = normed.astype(jnp.bfloat16)
    query_proj = matmul(normed_low, query_weight)
    key_proj = matmul(normed_low, key_weight)
    value_proj = matmul(normed_low, value_weight)

    def query_prep(flat_rows, gain_vec):
        return rotate(rms_norm(flat_rows.reshape(local_rows, HQ, HD), gain_vec), angles[:, None, :])

    def key_prep(rows_in, gain_vec):
        return rotate(rms_norm(rows_in, gain_vec), angles)

    query_rot, back_query = jax.vjp(query_prep, query_proj, norm_query)
    key_rot, back_key = jax.vjp(key_prep, key_proj, norm_key)
    query_low = query_rot.astype(jnp.bfloat16)
    key_low = key_rot.astype(jnp.bfloat16)
    value_low = value_proj.astype(jnp.bfloat16)
    reach = min(-(-(WINDOW - 1) // local_rows), group_size - 1)
    key_list = [key_low]
    value_list = [value_low]
    for offset in range(1, reach + 1):
        key_far, value_far = shifted((key_low, value_low), "group", offset)
        key_list.insert(0, key_far)
        value_list.insert(0, value_far)
    key_all = jnp.concatenate(key_list, axis=0)
    value_all = jnp.concatenate(value_list, axis=0)
    key_count = (reach + 1) * local_rows
    doc_pad = jnp.concatenate([jnp.full((reach * local_rows,), -1, jnp.int32), doc_row])
    key_docs = lax.dynamic_slice_in_dim(doc_pad, first_row, key_count, 0)
    key_index = (group_index - reach) * local_rows + jnp.arange(key_count, dtype=jnp.int32)
    query_index = first_row + jnp.arange(local_rows, dtype=jnp.int32)
    distance = query_index[:, None] - key_index[None, :]
    allowed = (distance >= 0) & (distance < WINDOW) & (key_docs[None, :] == query_docs[:, None])

    def scores_of(key_rows_low):
        raw_scores = jnp.einsum(
            "qhd,kd->hqk", query_low, key_rows_low, preferred_element_type=jnp.float32
        ) * HD ** (-0.5)
        return jnp.where(allowed[None], raw_scores, -1e30)

    masked = scores_of(key_all)
    top_score = jnp.max(masked, axis=-1, keepdims=True)
    log_total = top_score + jnp.log(jnp.sum(jnp.exp(masked - top_score), axis=-1, keepdims=True))
    probs = jnp.exp(masked - log_total)
    attended = jnp.einsum(
        "hqk,kd->qhd", probs.astype(jnp.bfloat16), value_all, preferred_element_type=jnp.float32
    )
    attended_low = attended.reshape(local_rows, HQ * HD).astype(jnp.bfloat16)
    attn_out = matmul(attended_low, out_weight)
    branch_one, back_attn = jax.vjp(rms_norm, attn_out, norm_attn)
    middle = inputs + branch_one
    normed_two, back_ffin = jax.vjp(rms_norm, middle, norm_ffin)
    normed_two_low = normed_two.astype(jnp.bfloat16)
    gate_proj = matmul(normed_two_low, gate_weight)
    up_proj = matmul(normed_two_low, up_weight)
    hidden, back_hidden = jax.vjp(geglu, gate_proj, up_proj)
    hidden_low = hidden.astype(jnp.bfloat16)
    ffn_out = matmul(hidden_low, down_weight)
    branch_two, back_ffout = jax.vjp(rms_norm, ffn_out, norm_ffout)
    outputs = middle + branch_two
    grad_out = cotangent.astype(jnp.float32)
    grad_ffn, grad_gain_ffout = back_ffout(grad_out)
    grad_ffn_low = grad_ffn.astype(jnp.bfloat16)
    grad_down_w = jnp.einsum(
        "tf,td->fd", hidden_low, grad_ffn_low, preferred_element_type=jnp.float32
    )
    grad_hidden = jnp.einsum(
        "td,fd->tf", grad_ffn_low, down_weight, preferred_element_type=jnp.float32
    )
    grad_gate, grad_up = back_hidden(grad_hidden)
    grad_gate_low = grad_gate.astype(jnp.bfloat16)
    grad_up_low = grad_up.astype(jnp.bfloat16)
    grad_gate_w = jnp.einsum(
        "td,tf->df", normed_two_low, grad_gate_low, preferred_element_type=jnp.float32
    )
    grad_up_w = jnp.einsum(
        "td,tf->df", normed_two_low, grad_up_low, preferred_element_type=jnp.float32
    )
    grad_normed_two = jnp.einsum(
        "tf,df->td", grad_gate_low, gate_weight, preferred_element_type=jnp.float32
    ) + jnp.einsum("tf,df->td", grad_up_low, up_weight, preferred_element_type=jnp.float32)
    grad_middle_norm, grad_gain_ffin = back_ffin(grad_normed_two)
    grad_middle = grad_out + grad_middle_norm
    grad_attn, grad_gain_attn = back_attn(grad_middle)
    grad_attn_low = grad_attn.astype(jnp.bfloat16)
    grad_out_w = jnp.einsum(
        "to,td->od", attended_low, grad_attn_low, preferred_element_type=jnp.float32
    )
    grad_attended = jnp.einsum(
        "td,od->to", grad_attn_low, out_weight, preferred_element_type=jnp.float32
    )
    grad_attended_low = grad_attended.astype(jnp.bfloat16).reshape(local_rows, HQ, HD)
    probs_again = jnp.exp(scores_of(key_all) - log_total)
    grad_probs = jnp.einsum(
        "qhd,kd->hqk", grad_attended_low, value_all, preferred_element_type=jnp.float32
    )
    grad_value_all = jnp.einsum(
        "hqk,qhd->kd",
        probs_again.astype(jnp.bfloat16),
        grad_attended_low,
        preferred_element_type=jnp.float32,
    )
    grad_scores = probs_again * (
        grad_probs - jnp.sum(probs_again * grad_probs, axis=-1, keepdims=True)
    )
    grad_scores_low = (grad_scores * HD ** (-0.5)).astype(jnp.bfloat16)
    grad_query = jnp.einsum(
        "hqk,kd->qhd", grad_scores_low, key_all, preferred_element_type=jnp.float32
    )
    grad_key_all = jnp.einsum(
        "hqk,qhd->kd", grad_scores_low, query_low, preferred_element_type=jnp.float32
    )
    key_total = grad_key_all[reach * local_rows :]
    value_total = grad_value_all[reach * local_rows :]
    for offset in range(1, reach + 1):
        row_start = (reach - offset) * local_rows
        key_back, value_back = (
            shifted(
                grad_key_all[row_start : row_start + local_rows].astype(jnp.bfloat16),
                "group",
                -offset,
            ).astype(jnp.float32),
            shifted(
                grad_value_all[row_start : row_start + local_rows].astype(jnp.bfloat16),
                "group",
                -offset,
            ).astype(jnp.float32),
        )
        key_total = key_total + key_back
        value_total = value_total + value_back
    grad_query_proj, grad_gain_query = back_query(grad_query)
    grad_key_proj, grad_gain_key = back_key(key_total)
    grad_query_low = grad_query_proj.astype(jnp.bfloat16)
    grad_key_low = grad_key_proj.astype(jnp.bfloat16)
    grad_value_low = value_total.astype(jnp.bfloat16)
    grad_query_w = jnp.einsum(
        "td,te->de", normed_low, grad_query_low, preferred_element_type=jnp.float32
    )
    grad_key_w = jnp.einsum(
        "td,te->de", normed_low, grad_key_low, preferred_element_type=jnp.float32
    )
    grad_value_w = jnp.einsum(
        "td,te->de", normed_low, grad_value_low, preferred_element_type=jnp.float32
    )
    grad_normed = jnp.einsum(
        "te,de->td", grad_query_low, query_weight, preferred_element_type=jnp.float32
    )
    grad_normed = grad_normed + jnp.einsum(
        "te,de->td", grad_key_low, key_weight, preferred_element_type=jnp.float32
    )
    grad_normed = grad_normed + jnp.einsum(
        "te,de->td", grad_value_low, value_weight, preferred_element_type=jnp.float32
    )
    grad_input_norm, grad_gain_input = back_input(grad_normed)
    grad_inputs = grad_middle + grad_input_norm
    flat_query = grad_query_w.reshape(-1, 128)
    flat_key = grad_key_w.reshape(-1, 128)
    flat_value = grad_value_w.reshape(-1, 128)
    flat_out = grad_out_w.reshape(-1, 128)
    flat_gate = grad_gate_w.reshape(-1, 128)
    flat_up = grad_up_w.reshape(-1, 128)
    flat_down = grad_down_w.reshape(-1, 128)
    reduced = (
        lax.psum_scatter(flat_query, ("dp", "group"), scatter_dimension=0, tiled=True),
        lax.psum_scatter(flat_key, ("dp", "group"), scatter_dimension=0, tiled=True),
        lax.psum_scatter(flat_value, ("dp", "group"), scatter_dimension=0, tiled=True),
        lax.psum_scatter(flat_out, ("dp", "group"), scatter_dimension=0, tiled=True),
        lax.psum_scatter(flat_gate, ("dp", "group"), scatter_dimension=0, tiled=True),
        lax.psum_scatter(flat_up, ("dp", "group"), scatter_dimension=0, tiled=True),
        lax.psum_scatter(flat_down, ("dp", "group"), scatter_dimension=0, tiled=True),
    )
    grads_local = jnp.concatenate(list(reduced), axis=0)
    gain_grads = lax.psum(
        jnp.concatenate(
            [
                grad_gain_input,
                grad_gain_attn,
                grad_gain_ffin,
                grad_gain_ffout,
                grad_gain_query,
                grad_gain_key,
            ]
        ),
        ("dp", "group"),
    )
    moment_first, moment_second, master_new = adam_update(
        grads_local, first_moment, second_moment, master, learn_rate, weight_decay
    )
    gain_moment_first, gain_moment_second, gains_new = adam_update(
        gain_grads, gain_first, gain_second, gains, gain_rate, 0.0
    )
    return (
        outputs.astype(jnp.bfloat16),
        grad_inputs.astype(jnp.bfloat16),
        moment_first,
        moment_second,
        master_new,
        gain_moment_first,
        gain_moment_second,
        gains_new,
    )


def solution(mesh):
    placed = (
        P(("dp", "group"), None),
        P("dp", None),
        P(("dp", "group"), None),
        P(("dp", "group"), None),
        P(("dp", "group"), None),
        P(("dp", "group"), None),
        P(),
        P(),
        P(),
    )
    return jax.shard_map(
        shards,
        mesh=mesh,
        in_specs=placed,
        out_specs=(
            P(("dp", "group"), None),
            P(("dp", "group"), None),
            P(("dp", "group"), None),
            P(("dp", "group"), None),
            P(("dp", "group"), None),
            P(),
            P(),
            P(),
        ),
        check_vma=False,
    )
```

```python
import functools
import math

import jax
import jax.numpy as jnp
from jax import lax
from jax.experimental import pallas as pl
from jax.experimental.pallas import tpu as pltpu
from jax.sharding import PartitionSpec as P

D = 640
HQ = 4
HD = 256
FF = 2048
WINDOW = 512
STEP = 10
ALL_AXES = ("dp", "group")


norm_eps = 1e-06
rope_base = 10000.0
beta_first = 0.9
beta_second = 0.999
learn_rate = 0.05
gain_rate = 0.25
adam_floor = 1e-08
weight_decay = 0.1


def shifted(value, axis, steps):
    count = lax.axis_size(axis)
    initial, last = (max(0, -steps), min(count, count - steps))
    return lax.ppermute(value, axis, [(source, source + steps) for source in range(initial, last)])


def rms_norm(values, weight_vec):
    return (
        values
        * lax.rsqrt(jnp.mean(values * values, axis=-1, keepdims=True) + norm_eps)
        * (1.0 + weight_vec)
    )


def positions(doc_row):
    length = doc_row.shape[0]
    counter = jnp.arange(length, dtype=jnp.int32)
    starts_here = jnp.concatenate([jnp.ones((1,), jnp.bool_), doc_row[1:] != doc_row[:-1]])
    begins = lax.cummax(jnp.where(starts_here, counter, jnp.zeros_like(counter)), axis=0)
    return counter - begins


def angles_of(places):
    half_dim = HD // 2
    frequency = rope_base ** (-(jnp.arange(half_dim, dtype=jnp.float32) * 2.0 / HD))
    return places.astype(jnp.float32)[:, None] * frequency[None, :]


def rotate(values, angles):
    half_dim = values.shape[-1] // 2
    first_half = values[..., :half_dim]
    second_half = values[..., half_dim:]
    cosine = jnp.cos(angles)
    sine_part = jnp.sin(angles)
    return jnp.concatenate(
        [
            first_half * cosine - second_half * sine_part,
            second_half * cosine + first_half * sine_part,
        ],
        axis=-1,
    )


def geglu(gate_in, up_in):
    return jax.nn.gelu(gate_in, approximate=True) * up_in


def adam_update(gradient, first_old, second_old, params_old, rate, decay_rate):
    first_new = beta_first * first_old + (1.0 - beta_first) * gradient
    second_new = beta_second * second_old + (1.0 - beta_second) * gradient * gradient
    first_hat = first_new / (1.0 - beta_first**STEP)
    second_hat = second_new / (1.0 - beta_second**STEP)
    params_new = params_old - rate * (
        first_hat / (jnp.sqrt(second_hat) + adam_floor) + decay_rate * params_old
    )
    return (first_new, second_new, params_new)


def piece_rows(device_count):
    return [
        entries // (128 * device_count)
        for entries in (D * HQ * HD, D * HD, D * HD, HQ * HD * D, D * FF, D * FF, FF * D)
    ]


def piece_shapes():
    return [(D, HQ * HD), (D, HD), (D, HD), (HQ * HD, D), (D, FF), (D, FF), (FF, D)]


def split_rows(stacked, row_list):
    result = []
    row_start = 0
    for row_count in row_list:
        result.append(stacked[row_start : row_start + row_count])
        row_start = row_start + row_count
    return result


def matmul(left_side, right_side):
    return jnp.dot(left_side, right_side, preferred_element_type=jnp.float32)


LOW_COUNT = 8
LANES = 128
LOW_MASKS = (0, 4, 2, 6, 1, 5, 3, 7)
GELU_SCALE = (2.0 / math.pi) ** 0.5
GELU_CUBE = 0.044715
VMEM_BYTES = 56 * 1024 * 1024


def aligned(device_count):
    return device_count % LOW_COUNT == 0 and D % device_count == 0


def swap(value, mask):
    count = lax.axis_size(ALL_AXES)
    return lax.ppermute(value, ALL_AXES, [(source, source ^ mask) for source in range(count)])


def local_call(kernel, outs, operands, scratch=(), behind=()):
    specs = [pl.BlockSpec(memory_space=pltpu.SMEM)]
    specs = specs + [pl.BlockSpec(memory_space=pltpu.VMEM)] * len(operands)
    specs = specs + [pl.BlockSpec(memory_space=pl.ANY)] * len(behind)
    first, last = 1 + len(operands), 1 + len(operands) + len(behind)

    def body(*refs):
        kernel(*refs[:first], *refs[last:])

    return pl.pallas_call(
        body,
        out_shape=outs,
        in_specs=specs,
        out_specs=tuple(pl.BlockSpec(memory_space=pltpu.VMEM) for _ in outs),
        scratch_shapes=scratch,
        compiler_params=pltpu.CompilerParams(vmem_limit_bytes=VMEM_BYTES),
        cost_estimate=pl.CostEstimate(flops=0, bytes_accessed=0, transcendentals=0),
    )(lax.axis_index(ALL_AXES).astype(jnp.int32).reshape(1), *operands, *behind)


class Piece:
    def __init__(self, rows, columns, device_count):
        self.rows = rows
        self.columns = columns
        self.wide = rows == D
        self.blocks = columns // LANES
        self.own_rows = rows // device_count
        self.flat_rows = self.own_rows * self.blocks
        self.high_count = device_count // LOW_COUNT
        self.block_rows = self.own_rows * self.high_count
        self.size = self.block_rows * self.blocks


def halves_kernel(index_ref, first_ref, second_ref, first_out_ref, second_out_ref):
    half = first_out_ref.shape[0]
    first_out_ref[...] = first_ref[:half, :]
    second_out_ref[...] = second_ref[half:, :]


def pack_kernel(pieces, later_count, index_ref, *refs):
    high_count = pieces[0].high_count
    parts, out_ref, flat, packed = refs[:high_count], refs[-3], refs[-2], refs[-1]
    if later_count:
        later_ref, out_ref = refs[high_count], refs[high_count + 1]
        refs[-3][...] = later_ref[later_ref.shape[0] - later_count :, :].astype(jnp.bfloat16)
    high = index_ref[0] // LOW_COUNT
    for step, part in enumerate(parts):
        flat[high ^ step] = part[...].astype(jnp.float32)
    start, target = 0, 0
    for piece in pieces:
        for block in range(piece.blocks):
            for place in range(high_count):
                packed[pl.ds(target, piece.own_rows), :] = flat[
                    place, pl.ds(start + block, piece.own_rows, stride=piece.blocks), :
                ]
                target = target + piece.own_rows
        start = start + piece.flat_rows
    out_ref[...] = packed[...].astype(jnp.bfloat16)


def sum_one_kernel(size, index_ref, near_ref, far_ref, to_x_ref, to_y_ref):
    total = near_ref[...].astype(jnp.float32) + far_ref[...].astype(jnp.float32)
    half = size // 2
    to_x_ref[:half, :] = total[:half].astype(jnp.bfloat16)
    if total.shape[0] > size:
        to_x_ref[half:, :] = total[size:].astype(jnp.bfloat16)
    to_y_ref[...] = total[half:size].astype(jnp.bfloat16)


def sum_three_kernel(
    size,
    index_ref,
    near_ref,
    far_ref,
    near_extra_ref,
    far_extra_ref,
    over_x_ref,
    over_y_ref,
    own_ref,
    beside_ref,
    across_ref,
    extra_ref,
):
    half = size // 2

    def both(first, last):
        return near_ref[first:last, :].astype(jnp.float32) + far_ref[first:last, :].astype(
            jnp.float32
        )

    own_ref[...] = both(0, size)
    beside_ref[:half, :] = both(size, size + half).astype(jnp.bfloat16)
    beside_ref[half:, :] = (
        both(size + half, 2 * size) + over_y_ref[...].astype(jnp.float32)
    ).astype(jnp.bfloat16)
    across_ref[:half, :] = (
        both(2 * size, 2 * size + half) + over_x_ref[:half, :].astype(jnp.float32)
    ).astype(jnp.bfloat16)
    across_ref[half:size, :] = both(2 * size + half, 3 * size).astype(jnp.bfloat16)
    if across_ref.shape[0] > size:
        extra = near_extra_ref[size:, :].astype(jnp.float32)
        extra = extra + far_extra_ref[size:, :].astype(jnp.float32)
        extra = extra + over_x_ref[half:, :].astype(jnp.float32)
        extra_ref[...] = extra
        across_ref[size:, :] = extra.astype(jnp.bfloat16)
    else:
        extra_ref[...] = jnp.zeros(extra_ref.shape, jnp.float32)


def unpack_kernel(pieces, index_ref, own_ref, beside_ref, across_ref, extra_ref, *refs):
    high_count = pieces[0].high_count
    size = sum(piece.size for piece in pieces)
    flat_rows = sum(piece.flat_rows for piece in pieces)
    outs, flat, packed = refs[:-2], refs[-2], refs[-1]
    high = index_ref[0] // LOW_COUNT
    packed[...] = (
        own_ref[...] + beside_ref[...].astype(jnp.float32) + across_ref[:size, :].astype(jnp.float32)
    )
    start, source = 0, 0
    for piece in pieces:
        for block in range(piece.blocks):
            for place in range(high_count):
                flat[place, pl.ds(start + block, piece.own_rows, stride=piece.blocks), :] = packed[
                    pl.ds(source, piece.own_rows), :
                ]
                source = source + piece.own_rows
        start = start + piece.flat_rows
    for step, out_ref in enumerate(outs):
        out_ref[:flat_rows, :] = flat[high ^ step].astype(out_ref.dtype)
        if out_ref.shape[0] > flat_rows:
            extra = extra_ref[...] + across_ref[size:, :].astype(jnp.float32)
            out_ref[flat_rows:, :] = extra.astype(out_ref.dtype)


def array(shape, kind):
    return jax.ShapeDtypeStruct(shape, kind)


def gather_high(rows):
    high_count = lax.axis_size(ALL_AXES) // LOW_COUNT
    return [rows] + [swap(rows, step * LOW_COUNT) for step in range(1, high_count)]


def gather_near(pieces, parts, later=None, later_count=0, behind=()):
    high_count = pieces[0].high_count
    size = sum(piece.size for piece in pieces)
    outs = (array((size, LANES), jnp.bfloat16),)
    if later_count:
        parts = (*parts, later)
        outs = outs + (array((later_count, LANES), jnp.bfloat16),)
    own, *rounded = local_call(
        functools.partial(pack_kernel, pieces, later_count),
        outs,
        parts,
        (
            pltpu.VMEM((high_count, parts[0].shape[0], LANES), jnp.float32),
            pltpu.VMEM((size, LANES), jnp.float32),
        ),
        behind,
    )
    return (own, swap(own, 4), swap(own, 2)), *rounded


def gather_diagonal(own, beside, across, behind=()):
    half = own.shape[0] // 2
    to_x, to_y = local_call(
        halves_kernel,
        (array((half, LANES), jnp.bfloat16),) * 2,
        (across, beside),
        (),
        behind,
    )
    near = (own, beside, across, swap(to_x, 4), swap(to_y, 2))
    return near + tuple(swap(value, 1) for value in near)


def scatter_start(pieces, near_three, near_one, far_three, far_one):
    size = sum(piece.size for piece in pieces)
    far_one = swap(far_one, 1)
    far_three = swap(far_three, 1)
    half = size // 2
    to_x, to_y = local_call(
        functools.partial(sum_one_kernel, size),
        (
            array((near_one.shape[0] - half, LANES), jnp.bfloat16),
            array((half, LANES), jnp.bfloat16),
        ),
        (near_one, far_one),
    )
    return (near_three, far_three, near_one, far_one, swap(to_x, 4), swap(to_y, 2)), to_y


def scatter_middle(pieces, started):
    size = sum(piece.size for piece in pieces)
    extra_count = started[2].shape[0] - size
    return local_call(
        functools.partial(sum_three_kernel, size),
        (
            array((size, LANES), jnp.float32),
            array((size, LANES), jnp.bfloat16),
            array((size + extra_count, LANES), jnp.bfloat16),
            array((max(extra_count, 8), LANES), jnp.float32),
        ),
        started,
    )


def scatter_end(pieces, own, beside, across, extra):
    high_count = pieces[0].high_count
    size = sum(piece.size for piece in pieces)
    flat_rows = sum(piece.flat_rows for piece in pieces)
    out_rows = flat_rows + across.shape[0] - size
    outs = local_call(
        functools.partial(unpack_kernel, pieces),
        (array((out_rows, LANES), jnp.float32),)
        + (array((out_rows, LANES), jnp.bfloat16),) * (high_count - 1),
        (own, swap(beside, 4), swap(across, 2), extra),
        (
            pltpu.VMEM((high_count, flat_rows, LANES), jnp.float32),
            pltpu.VMEM((size, LANES), jnp.float32),
        ),
    )
    return outs[0] + sum(
        swap(send, step * LOW_COUNT).astype(jnp.float32) for step, send in enumerate(outs) if step
    )


def norm_parts(values):
    scale = lax.rsqrt(jnp.mean(values * values, axis=-1, keepdims=True) + norm_eps)
    return scale, values * scale


def norm_back(scale, normal, upstream, weight_vec):
    weighted = upstream * (1.0 + weight_vec)
    inner = jnp.mean(weighted * normal, axis=-1, keepdims=True)
    return scale * (weighted - normal * inner), jnp.sum(normal * upstream, axis=0, keepdims=True)


def product(left_side, right_side, left_axis, right_axis):
    return lax.dot_general(
        left_side,
        right_side,
        (((left_axis,), (right_axis,)), ((), ())),
        preferred_element_type=jnp.float32,
    )


def unordered(rows_in, order_low):
    upper = rows_in.astype(jnp.bfloat16)
    lower = (rows_in - upper.astype(jnp.float32)).astype(jnp.bfloat16)
    return product(upper, order_low, 1, 1) + product(lower, order_low, 1, 1)


def weight_rows(refs, size, order, start, rows):
    refs = refs[:5] if order < 4 else refs[5:]
    ref = refs[order % 4]
    if order % 4 == 3 and 2 * start >= size:
        ref, start = refs[4], start - size // 2
    return ref[start : start + rows, :]


def put_rows(refs, size, order, start, rows):
    three, one = refs[:2] if order < 4 else refs[2:]
    if order % 4 == 3:
        one[start : start + rows.shape[0], :] = rows
    else:
        start = order % 4 * size + start
        three[start : start + rows.shape[0], :] = rows


def wide_tile(refs, size, start, rows):
    return jnp.concatenate(
        [weight_rows(refs, size, order, start, rows) for order in range(LOW_COUNT)]
    )


def put_wide_tile(refs, size, start, rows, tile):
    for order in range(LOW_COUNT):
        put_rows(refs, size, order, start, tile[order * rows : (order + 1) * rows])


def tall_rows(piece, low):
    for order, mask in enumerate(LOW_MASKS):
        for block in range(piece.blocks):
            for place in range(piece.high_count):
                row = (place * LOW_COUNT + (low ^ mask)) * piece.own_rows
                yield (
                    order,
                    block * piece.block_rows + place * piece.own_rows,
                    pl.ds(pl.multiple_of(row, piece.own_rows), piece.own_rows),
                    slice(block * LANES, (block + 1) * LANES),
                )


def ffn_kernel(
    gate_piece,
    down_piece,
    index_ref,
    middle_ref,
    cotangent_ref,
    gain_in_ref,
    gain_out_ref,
    order_ref,
    *refs,
):
    weight_refs, grad_refs = refs[:10], refs[14:18]
    block_out_ref, grad_middle_ref, grad_gain_in_ref, grad_gain_out_ref = refs[10:14]
    down_ref, hidden_ref, gelu_ref, slope_ref = refs[18:]
    low = index_ref[0] % LOW_COUNT
    rows = gate_piece.block_rows
    size = 2 * gate_piece.size + down_piece.size
    width = 2 * LANES
    for order, start, matrix_rows, columns in tall_rows(down_piece, low):
        start = start + 2 * gate_piece.size
        down_ref[matrix_rows, columns] = weight_rows(
            weight_refs, size, order, start, down_piece.own_rows
        )

    def wide_tiles(step):
        return [
            jnp.concatenate(
                [
                    wide_tile(weight_refs, size, offset + block * rows, rows)
                    for block in (2 * step, 2 * step + 1)
                ],
                axis=1,
            )
            for offset in (0, gate_piece.size)
        ]

    middle = middle_ref[...]
    scale_in, normal_in = norm_parts(middle)
    order_low = order_ref[...]
    normed = (normal_in * (1.0 + gain_in_ref[...])).astype(jnp.bfloat16)
    normed = product(normed, order_low, 1, 0).astype(jnp.bfloat16)
    for step in range(FF // width):
        columns = slice(step * width, (step + 1) * width)
        gate_weight, up_weight = wide_tiles(step)
        gate = product(normed, gate_weight, 1, 0)
        up = product(normed, up_weight, 1, 0)
        square = gate * gate
        bend = jnp.tanh(GELU_SCALE * gate * (1.0 + GELU_CUBE * square))
        half = 0.5 * (1.0 + bend)
        gelu = gate * half
        slope = half + 0.5 * gate * (1.0 - bend * bend) * GELU_SCALE * (
            1.0 + 3.0 * GELU_CUBE * square
        )
        gelu_ref[:, columns] = gelu
        slope_ref[:, columns] = slope * up
        hidden_ref[:, columns] = (gelu * up).astype(jnp.bfloat16)
    hidden = hidden_ref[...]
    scale_out, normal_out = norm_parts(product(hidden, down_ref[...], 1, 0))
    block_out_ref[...] = (middle + normal_out * (1.0 + gain_out_ref[...])).astype(jnp.bfloat16)
    upstream = cotangent_ref[...].astype(jnp.float32)
    grad_ffn, grad_gain_out_ref[...] = norm_back(
        scale_out, normal_out, upstream, gain_out_ref[...]
    )
    grad_ffn = grad_ffn.astype(jnp.bfloat16)
    grad_normed = jnp.zeros(middle.shape, jnp.float32)
    for step in range(FF // width):
        columns = slice(step * width, (step + 1) * width)
        grad_hidden = product(grad_ffn, down_ref[columns, :], 1, 1)
        down_ref[columns, :] = product(hidden_ref[:, columns], grad_ffn, 0, 0).astype(jnp.bfloat16)
        grads = [
            (grad_hidden * slope_ref[:, columns]).astype(jnp.bfloat16),
            (grad_hidden * gelu_ref[:, columns]).astype(jnp.bfloat16),
        ]
        for place, (grad, weight) in enumerate(zip(grads, wide_tiles(step))):
            grad_weight = product(normed, grad, 0, 0).astype(jnp.bfloat16)
            for side in range(2):
                put_wide_tile(
                    grad_refs,
                    size,
                    place * gate_piece.size + (2 * step + side) * rows,
                    rows,
                    grad_weight[:, side * LANES : (side + 1) * LANES],
                )
            grad_normed = grad_normed + product(grad, weight, 1, 1)
    for order, start, matrix_rows, columns in tall_rows(down_piece, low):
        start = start + 2 * gate_piece.size
        put_rows(grad_refs, size, order, start, down_ref[matrix_rows, columns])
    grad_middle, grad_gain_in_ref[...] = norm_back(
        scale_in, normal_in, unordered(grad_normed, order_low), gain_in_ref[...]
    )
    grad_middle_ref[...] = upstream + grad_middle


def grad_arrays(pieces, extra_count=0):
    size = sum(piece.size for piece in pieces)
    return (
        array((3 * size, LANES), jnp.bfloat16),
        array((size + extra_count, LANES), jnp.bfloat16),
    ) * 2


def ffn_blocks(pieces, middle, cotangent, gain_in, gain_out, order, blocks):
    rows = middle.shape[0]
    outs = local_call(
        functools.partial(ffn_kernel, pieces[4], pieces[6]),
        (
            array((rows, D), jnp.bfloat16),
            array((rows, D), jnp.float32),
            array((1, D), jnp.float32),
            array((1, D), jnp.float32),
            *grad_arrays(pieces[4:7]),
        ),
        (middle, cotangent, gain_in, gain_out, order, *blocks),
        (
            pltpu.VMEM((FF, D), jnp.bfloat16),
            pltpu.VMEM((rows, FF), jnp.bfloat16),
            pltpu.VMEM((rows, FF), jnp.float32),
            pltpu.VMEM((rows, FF), jnp.float32),
        ),
    )
    return *outs[:4], outs[4:]


def turn(values, cosine, sine):
    first_half, second_half = values[:, : HD // 2], values[:, HD // 2 :]
    return jnp.concatenate(
        [first_half * cosine - second_half * sine, second_half * cosine + first_half * sine], axis=1
    )


def wide_head(refs, size, start, rows):
    return jnp.concatenate(
        [wide_tile(refs, size, start + side * rows, rows) for side in range(2)], axis=1
    )


def head_starts(pieces):
    rows = pieces[0].block_rows
    return [2 * rows * head for head in range(HQ + 2)]


def project_kernel(
    pieces,
    index_ref,
    tokens_ref,
    gain_ref,
    gain_query_ref,
    gain_key_ref,
    cosine_ref,
    sine_ref,
    order_ref,
    *refs,
):
    weight_refs = refs[:10]
    normed_ref, query_proj_ref, key_proj_ref, query_ref, key_value_ref = refs[10:]
    size = sum(piece.size for piece in pieces)
    rows = pieces[0].block_rows
    cosine, sine = cosine_ref[...], sine_ref[...]
    _, normal = norm_parts(tokens_ref[...].astype(jnp.float32))
    normed = (normal * (1.0 + gain_ref[...])).astype(jnp.bfloat16)
    normed = product(normed, order_ref[...], 1, 0).astype(jnp.bfloat16)
    normed_ref[...] = normed
    starts = head_starts(pieces)
    for head, start in enumerate(starts):
        proj = product(normed, wide_head(weight_refs, size, start, rows), 1, 0)
        columns = slice(head * HD, (head + 1) * HD)
        if head == HQ + 1:
            key_value_ref[:, HD:] = proj.astype(jnp.bfloat16)
            continue
        gain_vec = gain_query_ref[...] if head < HQ else gain_key_ref[...]
        _, normal = norm_parts(proj)
        turned = turn(normal * (1.0 + gain_vec), cosine, sine).astype(jnp.bfloat16)
        if head < HQ:
            query_proj_ref[:, columns] = proj
            query_ref[:, columns] = turned
        else:
            key_proj_ref[...] = proj
            key_value_ref[:, :HD] = turned


def attend_kernel(
    pieces,
    index_ref,
    tokens_ref,
    gain_ref,
    allowed_ref,
    query_ref,
    *refs,
):
    weight_refs, key_value_refs = refs[:10], refs[10:-5]
    probs_ref, attended_ref, attn_out_ref, middle_ref, out_weight_ref = refs[-5:]
    out_piece = pieces[-1]
    low = index_ref[0] % LOW_COUNT
    size = sum(piece.size for piece in pieces)
    out_start = size - out_piece.size
    for order, start, matrix_rows, columns in tall_rows(out_piece, low):
        out_weight_ref[matrix_rows, columns] = weight_rows(
            weight_refs, size, order, start + out_start, out_piece.own_rows
        )
    rows = tokens_ref.shape[0]
    allowed = allowed_ref[...] > 0.0
    keys = jnp.concatenate([ref[:, :HD] for ref in key_value_refs])
    values = jnp.concatenate([ref[:, HD:] for ref in key_value_refs])
    count = keys.shape[0]
    for head in range(HQ):
        columns = slice(head * HD, (head + 1) * HD)
        scores = product(query_ref[:, columns], keys, 1, 1) * HD ** (-0.5)
        scores = jnp.where(allowed, scores, -1e30)
        raised = jnp.exp(scores - jnp.max(scores, axis=-1, keepdims=True))
        probs = raised / jnp.sum(raised, axis=-1, keepdims=True)
        probs_ref[:, head * count : (head + 1) * count] = probs
        attended_ref[:, columns] = product(probs.astype(jnp.bfloat16), values, 1, 0).astype(
            jnp.bfloat16
        )
    attn_out = product(attended_ref[...], out_weight_ref[...], 1, 0)
    attn_out_ref[...] = attn_out
    _, normal = norm_parts(attn_out)
    middle_ref[...] = tokens_ref[...].astype(jnp.float32) + normal * (1.0 + gain_ref[...])


def attend_back_kernel(
    index_ref,
    grad_middle_ref,
    attn_out_ref,
    gain_ref,
    out_weight_ref,
    attended_ref,
    probs_ref,
    query_ref,
    *refs,
):
    part_count = (len(refs) - 3) // 2
    key_value_refs = refs[:part_count]
    grad_out_weight_ref, grad_query_ref, grad_gain_ref = refs[part_count : part_count + 3]
    grad_key_value_refs = refs[part_count + 3 :]
    rows = query_ref.shape[0]
    scale, normal = norm_parts(attn_out_ref[...])
    grad_attn, grad_gain_ref[...] = norm_back(scale, normal, grad_middle_ref[...], gain_ref[...])
    grad_attn = grad_attn.astype(jnp.bfloat16)
    grad_out_weight_ref[...] = product(attended_ref[...], grad_attn, 0, 0).astype(jnp.bfloat16)
    keys = jnp.concatenate([ref[:, :HD] for ref in key_value_refs])
    values = jnp.concatenate([ref[:, HD:] for ref in key_value_refs])
    count = keys.shape[0]
    grad_keys = jnp.zeros((count, HD), jnp.float32)
    grad_values = jnp.zeros((count, HD), jnp.float32)
    for head in range(HQ):
        columns = slice(head * HD, (head + 1) * HD)
        grad_attended = product(grad_attn, out_weight_ref[columns, :], 1, 1).astype(jnp.bfloat16)
        probs = probs_ref[:, head * count : (head + 1) * count]
        grad_probs = product(grad_attended, values, 1, 1)
        grad_values = grad_values + product(probs.astype(jnp.bfloat16), grad_attended, 0, 0)
        inner = jnp.sum(probs * grad_probs, axis=-1, keepdims=True)
        grad_scores = (probs * (grad_probs - inner) * HD ** (-0.5)).astype(jnp.bfloat16)
        grad_query_ref[:, columns] = product(grad_scores, keys, 1, 0)
        grad_keys = grad_keys + product(grad_scores, query_ref[:, columns], 0, 0)
    for part, ref in enumerate(grad_key_value_refs):
        ref[:, :HD] = grad_keys[part * rows : (part + 1) * rows].astype(ref.dtype)
        ref[:, HD:] = grad_values[part * rows : (part + 1) * rows].astype(ref.dtype)


def project_back_kernel(
    pieces,
    index_ref,
    tokens_ref,
    gain_ref,
    gain_query_ref,
    gain_key_ref,
    cosine_ref,
    sine_ref,
    order_ref,
    normed_ref,
    query_proj_ref,
    key_proj_ref,
    grad_query_ref,
    grad_middle_ref,
    grad_out_weight_ref,
    gain_attn_ref,
    gain_ffin_ref,
    gain_ffout_ref,
    *refs,
):
    weight_refs, key_value_refs, grad_refs = refs[:10], refs[10:-6], refs[-6:-2]
    input_grad_ref, grad_gain_ref = refs[-2:]
    low = index_ref[0] % LOW_COUNT
    size = sum(piece.size for piece in pieces)
    rows = pieces[0].block_rows
    cosine, sine = cosine_ref[...], sine_ref[...]
    normed = normed_ref[...]
    key_value = sum(ref[...].astype(jnp.float32) for ref in key_value_refs)
    grad_normed = jnp.zeros(tokens_ref.shape, jnp.float32)
    grad_gain_query = jnp.zeros((1, HD), jnp.float32)
    grad_gain_key = jnp.zeros((1, HD), jnp.float32)
    for head, start in enumerate(head_starts(pieces)):
        columns = slice(head * HD, (head + 1) * HD)
        if head < HQ:
            scale, normal = norm_parts(query_proj_ref[:, columns])
            upstream = turn(grad_query_ref[:, columns], cosine, -sine)
            grad, gain_row = norm_back(scale, normal, upstream, gain_query_ref[...])
            grad_gain_query = grad_gain_query + gain_row
        elif head == HQ:
            scale, normal = norm_parts(key_proj_ref[...])
            upstream = turn(key_value[:, :HD], cosine, -sine)
            grad, grad_gain_key = norm_back(scale, normal, upstream, gain_key_ref[...])
        else:
            grad = key_value[:, HD:]
        grad = grad.astype(jnp.bfloat16)
        weight = wide_head(weight_refs, size, start, rows)
        grad_normed = grad_normed + product(grad, weight, 1, 1)
        grad_weight = product(normed, grad, 0, 0).astype(jnp.bfloat16)
        for side in range(2):
            put_wide_tile(
                grad_refs,
                size,
                start + side * rows,
                rows,
                grad_weight[:, side * LANES : (side + 1) * LANES],
            )
    out_piece = pieces[-1]
    for order, start, matrix_rows, columns in tall_rows(out_piece, low):
        start = start + size - out_piece.size
        put_rows(grad_refs, size, order, start, grad_out_weight_ref[matrix_rows, columns])
    scale, normal = norm_parts(tokens_ref[...].astype(jnp.float32))
    grad_inputs, grad_gain_input = norm_back(
        scale, normal, unordered(grad_normed, order_ref[...]), gain_ref[...]
    )
    input_grad_ref[...] = (grad_middle_ref[...] + grad_inputs).astype(jnp.bfloat16)
    grad_gains = [
        grad_gain_input,
        gain_attn_ref[...],
        gain_ffin_ref[...],
        gain_ffout_ref[...],
        grad_gain_query,
        grad_gain_key,
    ]
    row = 0
    grad_gain_ref[...] = jnp.zeros(grad_gain_ref.shape, jnp.float32)
    for values in grad_gains:
        for start in range(0, values.shape[1], LANES):
            grad_gain_ref[row : row + 1, :] = values[:, start : start + LANES]
            row = row + 1
    for target in (grad_refs[1], grad_refs[3]):
        target[size:, :] = grad_gain_ref[...].astype(jnp.bfloat16)


def width_order(device_count):
    low = lax.axis_index(ALL_AXES) % LOW_COUNT
    rows = D // device_count
    high_count = device_count // LOW_COUNT
    column = jnp.arange(D, dtype=jnp.int32)
    place = column // (rows * high_count)
    mask = (place & 1) * 4 + ((place >> 1) & 1) * 2 + (place >> 2)
    high = (column // rows) % high_count
    picked = (high * LOW_COUNT + (low ^ mask)) * rows + column % rows
    return (jnp.arange(D, dtype=jnp.int32)[:, None] == picked[None, :]).astype(jnp.bfloat16)


GAIN_ROWS = 32


def shards_blocks(
    device_count,
    tokens,
    doc_ids,
    cotangent,
    master,
    first_moment,
    second_moment,
    gains,
    gain_first,
    gain_second,
):
    pieces = [Piece(*shape_pair, device_count) for shape_pair in piece_shapes()]
    attention_pieces = pieces[:4]
    local_rows = tokens.shape[0]
    group_size = lax.axis_size("group")
    first_row = lax.axis_index("group") * local_rows
    attention_rows = sum(piece.flat_rows for piece in attention_pieces)
    ffn_pieces = pieces[4:7]
    attention_near, ffn_rows = gather_near(
        attention_pieces,
        gather_high(master[:attention_rows].astype(jnp.bfloat16)),
        master,
        master.shape[0] - attention_rows,
    )
    ffn_parts = gather_high(ffn_rows)
    attention_blocks = gather_diagonal(*attention_near, (ffn_parts[1],))
    (ffn_near,) = gather_near(ffn_pieces, ffn_parts, behind=(attention_blocks[3],))
    gain_parts = []
    for start, width in ((0, D), (D, D), (2 * D, D), (3 * D, D), (4 * D, HD), (4 * D + HD, HD)):
        gain_parts.append(gains[start : start + width][None])
    gain_input, gain_attn, gain_ffin, gain_ffout, gain_query, gain_key = gain_parts
    order = width_order(device_count)
    doc_row = doc_ids[0]
    angles = lax.dynamic_slice_in_dim(angles_of(positions(doc_row)), first_row, local_rows, 0)
    cosine, sine = jnp.cos(angles), jnp.sin(angles)
    query_docs = lax.dynamic_slice_in_dim(doc_row, first_row, local_rows, 0)
    reach = min(-(-(WINDOW - 1) // local_rows), group_size - 1)
    key_count = (reach + 1) * local_rows
    doc_pad = jnp.concatenate([jnp.full((reach * local_rows,), -1, jnp.int32), doc_row])
    key_docs = lax.dynamic_slice_in_dim(doc_pad, first_row, key_count, 0)
    key_index = first_row - reach * local_rows + jnp.arange(key_count, dtype=jnp.int32)
    query_index = first_row + jnp.arange(local_rows, dtype=jnp.int32)
    distance = query_index[:, None] - key_index[None, :]
    allowed = (distance >= 0) & (distance < WINDOW) & (key_docs[None, :] == query_docs[:, None])
    allowed = allowed.astype(jnp.float32)

    entry = (tokens, gain_input, gain_query, gain_key, cosine, sine, order)
    width = HQ * HD
    normed, query_proj, key_proj, query_rot, key_value = local_call(
        functools.partial(project_kernel, attention_pieces),
        (
            array((local_rows, D), jnp.bfloat16),
            array((local_rows, width), jnp.float32),
            array((local_rows, HD), jnp.float32),
            array((local_rows, width), jnp.bfloat16),
            array((local_rows, 2 * HD), jnp.bfloat16),
        ),
        (*entry, *attention_blocks),
        (),
        (ffn_near[0],),
    )
    key_values = [shifted(key_value, "group", offset) for offset in range(reach, 0, -1)]
    key_values.append(key_value)
    probs, attended, attn_out, middle, out_weight = local_call(
        functools.partial(attend_kernel, attention_pieces),
        (
            array((local_rows, HQ * key_count), jnp.float32),
            array((local_rows, width), jnp.bfloat16),
            array((local_rows, D), jnp.float32),
            array((local_rows, D), jnp.float32),
            array((width, D), jnp.bfloat16),
        ),
        (tokens, gain_attn, allowed, query_rot, *attention_blocks, *key_values),
    )
    ffn_weights = gather_diagonal(*ffn_near, (middle,))
    outputs, grad_middle, grad_gain_ffin, grad_gain_ffout, grads_ffn = ffn_blocks(
        pieces, middle, cotangent, gain_ffin, gain_ffout, order, ffn_weights
    )
    ffn_started, ffn_sent = scatter_start(ffn_pieces, *grads_ffn)
    grad_out_weight, grad_query, grad_gain_attn, *grad_key_values = local_call(
        attend_back_kernel,
        (
            array((width, D), jnp.bfloat16),
            array((local_rows, width), jnp.float32),
            array((1, D), jnp.float32),
            *(array((local_rows, 2 * HD), jnp.bfloat16),) * reach,
            array((local_rows, 2 * HD), jnp.float32),
        ),
        (
            grad_middle,
            attn_out,
            gain_attn,
            out_weight,
            attended,
            probs,
            query_rot,
            *key_values,
        ),
        (),
        (ffn_sent,),
    )
    ffn_sums = scatter_middle(ffn_pieces, ffn_started)
    grad_key_values = [
        shifted(value, "group", place - reach) if place < reach else value
        for place, value in enumerate(grad_key_values)
    ]
    *grads_attention, grad_inputs, _ = local_call(
        functools.partial(project_back_kernel, attention_pieces),
        (
            *grad_arrays(attention_pieces, GAIN_ROWS),
            array((local_rows, D), jnp.bfloat16),
            array((GAIN_ROWS, LANES), jnp.float32),
        ),
        (
            *entry,
            normed,
            query_proj,
            key_proj,
            grad_query,
            grad_middle,
            grad_out_weight,
            grad_gain_attn,
            grad_gain_ffin,
            grad_gain_ffout,
            *attention_blocks,
            *grad_key_values,
        ),
        (),
        (ffn_sums[1],),
    )
    grads_ffn = scatter_end(ffn_pieces, *ffn_sums)
    attention_started, _ = scatter_start(attention_pieces, *grads_attention)
    grads_attention = scatter_end(
        attention_pieces, *scatter_middle(attention_pieces, attention_started)
    )
    gain_grads = grads_attention[attention_rows:].reshape(-1)[: gains.shape[0]]
    grads_local = jnp.concatenate([grads_attention[:attention_rows], grads_ffn])
    return (
        outputs,
        grad_inputs,
        *adam_update(grads_local, first_moment, second_moment, master, learn_rate, weight_decay),
        *adam_update(gain_grads, gain_first, gain_second, gains, gain_rate, 0.0),
    )


def shards(
    tokens, doc_ids, cotangent, master, first_moment, second_moment, gains, gain_first, gain_second
):
    group_size = lax.axis_size("group")
    devices_all = lax.axis_size("dp") * group_size
    if aligned(devices_all):
        return shards_blocks(
            devices_all,
            tokens,
            doc_ids,
            cotangent,
            master,
            first_moment,
            second_moment,
            gains,
            gain_first,
            gain_second,
        )
    group_index = lax.axis_index("group")
    local_rows = tokens.shape[0]
    shard_parts = [
        part_rows.astype(jnp.bfloat16) for part_rows in split_rows(master, piece_rows(devices_all))
    ]
    gathered = (
        lax.all_gather(shard_parts[0], ("dp", "group"), axis=0, tiled=True),
        lax.all_gather(shard_parts[1], ("dp", "group"), axis=0, tiled=True),
        lax.all_gather(shard_parts[2], ("dp", "group"), axis=0, tiled=True),
        lax.all_gather(shard_parts[3], ("dp", "group"), axis=0, tiled=True),
        lax.all_gather(shard_parts[4], ("dp", "group"), axis=0, tiled=True),
        lax.all_gather(shard_parts[5], ("dp", "group"), axis=0, tiled=True),
        lax.all_gather(shard_parts[6], ("dp", "group"), axis=0, tiled=True),
    )
    query_weight, key_weight, value_weight, out_weight, gate_weight, up_weight, down_weight = [
        full_rows.reshape(shape_pair) for full_rows, shape_pair in zip(gathered, piece_shapes())
    ]
    norm_input = gains[0:D]
    norm_attn = gains[D : 2 * D]
    norm_ffin = gains[2 * D : 3 * D]
    norm_ffout = gains[3 * D : 4 * D]
    norm_query = gains[4 * D : 4 * D + HD]
    norm_key = gains[4 * D + HD : 4 * D + 2 * HD]
    doc_row = doc_ids[0]
    first_row = group_index * local_rows
    angles = lax.dynamic_slice_in_dim(angles_of(positions(doc_row)), first_row, local_rows, 0)
    query_docs = lax.dynamic_slice_in_dim(doc_row, first_row, local_rows, 0)
    inputs = tokens.astype(jnp.float32)
    normed, back_input = jax.vjp(rms_norm, inputs, norm_input)
    normed_low = normed.astype(jnp.bfloat16)
    query_proj = matmul(normed_low, query_weight)
    key_proj = matmul(normed_low, key_weight)
    value_proj = matmul(normed_low, value_weight)

    def query_prep(flat_rows, gain_vec):
        return rotate(rms_norm(flat_rows.reshape(local_rows, HQ, HD), gain_vec), angles[:, None, :])

    def key_prep(rows_in, gain_vec):
        return rotate(rms_norm(rows_in, gain_vec), angles)

    query_rot, back_query = jax.vjp(query_prep, query_proj, norm_query)
    key_rot, back_key = jax.vjp(key_prep, key_proj, norm_key)
    query_low = query_rot.astype(jnp.bfloat16)
    key_low = key_rot.astype(jnp.bfloat16)
    value_low = value_proj.astype(jnp.bfloat16)
    reach = min(-(-(WINDOW - 1) // local_rows), group_size - 1)
    key_list = [key_low]
    value_list = [value_low]
    for offset in range(1, reach + 1):
        key_far, value_far = shifted((key_low, value_low), "group", offset)
        key_list.insert(0, key_far)
        value_list.insert(0, value_far)
    key_all = jnp.concatenate(key_list, axis=0)
    value_all = jnp.concatenate(value_list, axis=0)
    key_count = (reach + 1) * local_rows
    doc_pad = jnp.concatenate([jnp.full((reach * local_rows,), -1, jnp.int32), doc_row])
    key_docs = lax.dynamic_slice_in_dim(doc_pad, first_row, key_count, 0)
    key_index = (group_index - reach) * local_rows + jnp.arange(key_count, dtype=jnp.int32)
    query_index = first_row + jnp.arange(local_rows, dtype=jnp.int32)
    distance = query_index[:, None] - key_index[None, :]
    allowed = (distance >= 0) & (distance < WINDOW) & (key_docs[None, :] == query_docs[:, None])

    def scores_of(key_rows_low):
        raw_scores = jnp.einsum(
            "qhd,kd->hqk", query_low, key_rows_low, preferred_element_type=jnp.float32
        ) * HD ** (-0.5)
        return jnp.where(allowed[None], raw_scores, -1e30)

    masked = scores_of(key_all)
    top_score = jnp.max(masked, axis=-1, keepdims=True)
    log_total = top_score + jnp.log(jnp.sum(jnp.exp(masked - top_score), axis=-1, keepdims=True))
    probs = jnp.exp(masked - log_total)
    attended = jnp.einsum(
        "hqk,kd->qhd", probs.astype(jnp.bfloat16), value_all, preferred_element_type=jnp.float32
    )
    attended_low = attended.reshape(local_rows, HQ * HD).astype(jnp.bfloat16)
    attn_out = matmul(attended_low, out_weight)
    branch_one, back_attn = jax.vjp(rms_norm, attn_out, norm_attn)
    middle = inputs + branch_one
    normed_two, back_ffin = jax.vjp(rms_norm, middle, norm_ffin)
    normed_two_low = normed_two.astype(jnp.bfloat16)
    gate_proj = matmul(normed_two_low, gate_weight)
    up_proj = matmul(normed_two_low, up_weight)
    hidden, back_hidden = jax.vjp(geglu, gate_proj, up_proj)
    hidden_low = hidden.astype(jnp.bfloat16)
    ffn_out = matmul(hidden_low, down_weight)
    branch_two, back_ffout = jax.vjp(rms_norm, ffn_out, norm_ffout)
    outputs = middle + branch_two
    grad_out = cotangent.astype(jnp.float32)
    grad_ffn, grad_gain_ffout = back_ffout(grad_out)
    grad_ffn_low = grad_ffn.astype(jnp.bfloat16)
    grad_down_w = jnp.einsum(
        "tf,td->fd", hidden_low, grad_ffn_low, preferred_element_type=jnp.float32
    )
    grad_hidden = jnp.einsum(
        "td,fd->tf", grad_ffn_low, down_weight, preferred_element_type=jnp.float32
    )
    grad_gate, grad_up = back_hidden(grad_hidden)
    grad_gate_low = grad_gate.astype(jnp.bfloat16)
    grad_up_low = grad_up.astype(jnp.bfloat16)
    grad_gate_w = jnp.einsum(
        "td,tf->df", normed_two_low, grad_gate_low, preferred_element_type=jnp.float32
    )
    grad_up_w = jnp.einsum(
        "td,tf->df", normed_two_low, grad_up_low, preferred_element_type=jnp.float32
    )
    grad_normed_two = jnp.einsum(
        "tf,df->td", grad_gate_low, gate_weight, preferred_element_type=jnp.float32
    ) + jnp.einsum("tf,df->td", grad_up_low, up_weight, preferred_element_type=jnp.float32)
    grad_middle_norm, grad_gain_ffin = back_ffin(grad_normed_two)
    grad_middle = grad_out + grad_middle_norm
    grad_attn, grad_gain_attn = back_attn(grad_middle)
    grad_attn_low = grad_attn.astype(jnp.bfloat16)
    grad_out_w = jnp.einsum(
        "to,td->od", attended_low, grad_attn_low, preferred_element_type=jnp.float32
    )
    grad_attended = jnp.einsum(
        "td,od->to", grad_attn_low, out_weight, preferred_element_type=jnp.float32
    )
    grad_attended_low = grad_attended.astype(jnp.bfloat16).reshape(local_rows, HQ, HD)
    probs_again = jnp.exp(scores_of(key_all) - log_total)
    grad_probs = jnp.einsum(
        "qhd,kd->hqk", grad_attended_low, value_all, preferred_element_type=jnp.float32
    )
    grad_value_all = jnp.einsum(
        "hqk,qhd->kd",
        probs_again.astype(jnp.bfloat16),
        grad_attended_low,
        preferred_element_type=jnp.float32,
    )
    grad_scores = probs_again * (
        grad_probs - jnp.sum(probs_again * grad_probs, axis=-1, keepdims=True)
    )
    grad_scores_low = (grad_scores * HD ** (-0.5)).astype(jnp.bfloat16)
    grad_query = jnp.einsum(
        "hqk,kd->qhd", grad_scores_low, key_all, preferred_element_type=jnp.float32
    )
    grad_key_all = jnp.einsum(
        "hqk,qhd->kd", grad_scores_low, query_low, preferred_element_type=jnp.float32
    )
    key_total = grad_key_all[reach * local_rows :]
    value_total = grad_value_all[reach * local_rows :]
    for offset in range(1, reach + 1):
        row_start = (reach - offset) * local_rows
        key_back, value_back = (
            shifted(
                grad_key_all[row_start : row_start + local_rows].astype(jnp.bfloat16),
                "group",
                -offset,
            ).astype(jnp.float32),
            shifted(
                grad_value_all[row_start : row_start + local_rows].astype(jnp.bfloat16),
                "group",
                -offset,
            ).astype(jnp.float32),
        )
        key_total = key_total + key_back
        value_total = value_total + value_back
    grad_query_proj, grad_gain_query = back_query(grad_query)
    grad_key_proj, grad_gain_key = back_key(key_total)
    grad_query_low = grad_query_proj.astype(jnp.bfloat16)
    grad_key_low = grad_key_proj.astype(jnp.bfloat16)
    grad_value_low = value_total.astype(jnp.bfloat16)
    grad_query_w = jnp.einsum(
        "td,te->de", normed_low, grad_query_low, preferred_element_type=jnp.float32
    )
    grad_key_w = jnp.einsum(
        "td,te->de", normed_low, grad_key_low, preferred_element_type=jnp.float32
    )
    grad_value_w = jnp.einsum(
        "td,te->de", normed_low, grad_value_low, preferred_element_type=jnp.float32
    )
    grad_normed = jnp.einsum(
        "te,de->td", grad_query_low, query_weight, preferred_element_type=jnp.float32
    )
    grad_normed = grad_normed + jnp.einsum(
        "te,de->td", grad_key_low, key_weight, preferred_element_type=jnp.float32
    )
    grad_normed = grad_normed + jnp.einsum(
        "te,de->td", grad_value_low, value_weight, preferred_element_type=jnp.float32
    )
    grad_input_norm, grad_gain_input = back_input(grad_normed)
    grad_inputs = grad_middle + grad_input_norm
    flat_query = grad_query_w.reshape(-1, 128)
    flat_key = grad_key_w.reshape(-1, 128)
    flat_value = grad_value_w.reshape(-1, 128)
    flat_out = grad_out_w.reshape(-1, 128)
    flat_gate = grad_gate_w.reshape(-1, 128)
    flat_up = grad_up_w.reshape(-1, 128)
    flat_down = grad_down_w.reshape(-1, 128)
    reduced = (
        lax.psum_scatter(flat_query, ("dp", "group"), scatter_dimension=0, tiled=True),
        lax.psum_scatter(flat_key, ("dp", "group"), scatter_dimension=0, tiled=True),
        lax.psum_scatter(flat_value, ("dp", "group"), scatter_dimension=0, tiled=True),
        lax.psum_scatter(flat_out, ("dp", "group"), scatter_dimension=0, tiled=True),
        lax.psum_scatter(flat_gate, ("dp", "group"), scatter_dimension=0, tiled=True),
        lax.psum_scatter(flat_up, ("dp", "group"), scatter_dimension=0, tiled=True),
        lax.psum_scatter(flat_down, ("dp", "group"), scatter_dimension=0, tiled=True),
    )
    grads_local = jnp.concatenate(list(reduced), axis=0)
    gain_grads = lax.psum(
        jnp.concatenate(
            [
                grad_gain_input,
                grad_gain_attn,
                grad_gain_ffin,
                grad_gain_ffout,
                grad_gain_query,
                grad_gain_key,
            ]
        ),
        ("dp", "group"),
    )
    moment_first, moment_second, master_new = adam_update(
        grads_local, first_moment, second_moment, master, learn_rate, weight_decay
    )
    gain_moment_first, gain_moment_second, gains_new = adam_update(
        gain_grads, gain_first, gain_second, gains, gain_rate, 0.0
    )
    return (
        outputs.astype(jnp.bfloat16),
        grad_inputs.astype(jnp.bfloat16),
        moment_first,
        moment_second,
        master_new,
        gain_moment_first,
        gain_moment_second,
        gains_new,
    )


def solution(mesh):
    placed = (
        P(("dp", "group"), None),
        P("dp", None),
        P(("dp", "group"), None),
        P(("dp", "group"), None),
        P(("dp", "group"), None),
        P(("dp", "group"), None),
        P(),
        P(),
        P(),
    )
    return jax.shard_map(
        shards,
        mesh=mesh,
        in_specs=placed,
        out_specs=(
            P(("dp", "group"), None),
            P(("dp", "group"), None),
            P(("dp", "group"), None),
            P(("dp", "group"), None),
            P(("dp", "group"), None),
            P(),
            P(),
            P(),
        ),
        check_vma=False,
    )
```

```python
import functools
import math

import jax
import jax.numpy as jnp
from jax import lax
from jax.experimental import pallas as pl
from jax.experimental.pallas import tpu as pltpu
from jax.sharding import PartitionSpec as P

D = 640
HQ = 4
HD = 256
FF = 2048
WINDOW = 512
STEP = 10
ALL_AXES = ("dp", "group")


norm_eps = 1e-06
rope_base = 10000.0
beta_first = 0.9
beta_second = 0.999
learn_rate = 0.05
gain_rate = 0.25
adam_floor = 1e-08
weight_decay = 0.1


def shifted(value, axis, steps):
    count = lax.axis_size(axis)
    initial, last = (max(0, -steps), min(count, count - steps))
    return lax.ppermute(value, axis, [(source, source + steps) for source in range(initial, last)])


def rms_norm(values, weight_vec):
    return (
        values
        * lax.rsqrt(jnp.mean(values * values, axis=-1, keepdims=True) + norm_eps)
        * (1.0 + weight_vec)
    )


def positions(doc_row):
    length = doc_row.shape[0]
    counter = jnp.arange(length, dtype=jnp.int32)
    starts_here = jnp.concatenate([jnp.ones((1,), jnp.bool_), doc_row[1:] != doc_row[:-1]])
    begins = lax.cummax(jnp.where(starts_here, counter, jnp.zeros_like(counter)), axis=0)
    return counter - begins


def angles_of(places):
    half_dim = HD // 2
    frequency = rope_base ** (-(jnp.arange(half_dim, dtype=jnp.float32) * 2.0 / HD))
    return places.astype(jnp.float32)[:, None] * frequency[None, :]


def rotate(values, angles):
    half_dim = values.shape[-1] // 2
    first_half = values[..., :half_dim]
    second_half = values[..., half_dim:]
    cosine = jnp.cos(angles)
    sine_part = jnp.sin(angles)
    return jnp.concatenate(
        [
            first_half * cosine - second_half * sine_part,
            second_half * cosine + first_half * sine_part,
        ],
        axis=-1,
    )


def geglu(gate_in, up_in):
    return jax.nn.gelu(gate_in, approximate=True) * up_in


def adam_update(gradient, first_old, second_old, params_old, rate, decay_rate):
    first_new = beta_first * first_old + (1.0 - beta_first) * gradient
    second_new = beta_second * second_old + (1.0 - beta_second) * gradient * gradient
    first_hat = first_new / (1.0 - beta_first**STEP)
    second_hat = second_new / (1.0 - beta_second**STEP)
    params_new = params_old - rate * (
        first_hat / (jnp.sqrt(second_hat) + adam_floor) + decay_rate * params_old
    )
    return (first_new, second_new, params_new)


def piece_rows(device_count):
    return [
        entries // (128 * device_count)
        for entries in (D * HQ * HD, D * HD, D * HD, HQ * HD * D, D * FF, D * FF, FF * D)
    ]


def piece_shapes():
    return [(D, HQ * HD), (D, HD), (D, HD), (HQ * HD, D), (D, FF), (D, FF), (FF, D)]


def split_rows(stacked, row_list):
    result = []
    row_start = 0
    for row_count in row_list:
        result.append(stacked[row_start : row_start + row_count])
        row_start = row_start + row_count
    return result


def matmul(left_side, right_side):
    return jnp.dot(left_side, right_side, preferred_element_type=jnp.float32)


LOW_COUNT = 8
LANES = 128
LOW_MASKS = (0, 4, 2, 6, 1, 5, 3, 7)
GELU_SCALE = (2.0 / math.pi) ** 0.5
GELU_CUBE = 0.044715
VMEM_BYTES = 56 * 1024 * 1024


def aligned(device_count):
    return device_count % LOW_COUNT == 0 and D % device_count == 0


def swap(value, mask):
    count = lax.axis_size(ALL_AXES)
    return lax.ppermute(value, ALL_AXES, [(source, source ^ mask) for source in range(count)])


def local_call(kernel, outs, operands, scratch=(), behind=()):
    specs = [pl.BlockSpec(memory_space=pltpu.SMEM)]
    specs = specs + [pl.BlockSpec(memory_space=pltpu.VMEM)] * len(operands)
    specs = specs + [pl.BlockSpec(memory_space=pl.ANY)] * len(behind)
    first, last = 1 + len(operands), 1 + len(operands) + len(behind)

    def body(*refs):
        kernel(*refs[:first], *refs[last:])

    return pl.pallas_call(
        body,
        out_shape=outs,
        in_specs=specs,
        out_specs=tuple(pl.BlockSpec(memory_space=pltpu.VMEM) for _ in outs),
        scratch_shapes=scratch,
        compiler_params=pltpu.CompilerParams(vmem_limit_bytes=VMEM_BYTES),
        cost_estimate=pl.CostEstimate(flops=0, bytes_accessed=0, transcendentals=0),
    )(lax.axis_index(ALL_AXES).astype(jnp.int32).reshape(1), *operands, *behind)


class Piece:
    def __init__(self, rows, columns, device_count):
        self.rows = rows
        self.columns = columns
        self.wide = rows == D
        self.blocks = columns // LANES
        self.own_rows = rows // device_count
        self.flat_rows = self.own_rows * self.blocks
        self.high_count = device_count // LOW_COUNT
        self.block_rows = self.own_rows * self.high_count
        self.size = self.block_rows * self.blocks


def round_kernel(index_ref, in_ref, out_ref):
    out_ref[...] = in_ref[in_ref.shape[0] - out_ref.shape[0] :, :].astype(jnp.bfloat16)


def join_kernel(index_ref, *refs):
    out_ref = refs[-1]
    rows = refs[0].shape[0]
    for place, ref in enumerate(refs[:-1]):
        out_ref[place * rows : (place + 1) * rows, :] = ref[...]


def pack_kernel(pieces, index_ref, *refs):
    high_count = pieces[0].high_count
    parts, out_refs, flat, packed = refs[:high_count], refs[-4:-2], refs[-2], refs[-1]
    high = index_ref[0] // LOW_COUNT
    for step, part in enumerate(parts):
        flat[high ^ step] = part[...].astype(jnp.float32)
    start, target = 0, 0
    for piece in pieces:
        for block in range(piece.blocks):
            for place in range(high_count):
                packed[pl.ds(target, piece.own_rows), :] = flat[
                    place, pl.ds(start + block, piece.own_rows, stride=piece.blocks), :
                ]
                target = target + piece.own_rows
        start = start + piece.flat_rows
    half = target // 2
    for place, out_ref in enumerate(out_refs):
        out_ref[...] = packed[place * half : (place + 1) * half, :].astype(jnp.bfloat16)


def sum_one_kernel(size, index_ref, near_ref, far_ref, to_x_ref, to_y_ref):
    total = near_ref[...].astype(jnp.float32) + far_ref[...].astype(jnp.float32)
    half = size // 2
    to_x_ref[:half, :] = total[:half].astype(jnp.bfloat16)
    if total.shape[0] > size:
        to_x_ref[half:, :] = total[size:].astype(jnp.bfloat16)
    to_y_ref[...] = total[half:size].astype(jnp.bfloat16)


def sum_three_kernel(
    size,
    index_ref,
    near_ref,
    far_ref,
    own_ref,
    beside_first_ref,
    beside_second_ref,
    across_first_ref,
    across_second_ref,
):
    half = size // 2
    outs = (beside_first_ref, beside_second_ref, across_first_ref, across_second_ref)
    own_ref[...] = near_ref[:size, :].astype(jnp.float32) + far_ref[:size, :].astype(jnp.float32)
    for place, out_ref in enumerate(outs):
        rows = slice(size + place * half, size + (place + 1) * half)
        total = near_ref[rows, :].astype(jnp.float32) + far_ref[rows, :].astype(jnp.float32)
        out_ref[...] = total.astype(out_ref.dtype)


def sum_passed_kernel(
    size,
    index_ref,
    beside_ref,
    across_ref,
    over_x_ref,
    over_y_ref,
    near_one_ref,
    far_one_ref,
    beside_out_ref,
    across_out_ref,
    extra_ref,
):
    half = size // 2
    beside_out_ref[...] = (beside_ref[...] + over_y_ref[...].astype(jnp.float32)).astype(
        jnp.bfloat16
    )
    across_out_ref[:half, :] = (
        across_ref[...] + over_x_ref[:half, :].astype(jnp.float32)
    ).astype(jnp.bfloat16)
    if across_out_ref.shape[0] > half:
        extra = near_one_ref[size:, :].astype(jnp.float32)
        extra = extra + far_one_ref[size:, :].astype(jnp.float32)
        extra = extra + over_x_ref[half:, :].astype(jnp.float32)
        extra_ref[...] = extra
        across_out_ref[half:, :] = extra.astype(jnp.bfloat16)
    else:
        extra_ref[...] = jnp.zeros(extra_ref.shape, jnp.float32)


def unpack_kernel(
    pieces,
    index_ref,
    own_ref,
    beside_first_ref,
    beside_second_ref,
    across_first_ref,
    across_second_ref,
    extra_ref,
    *refs,
):
    high_count = pieces[0].high_count
    half = sum(piece.size for piece in pieces) // 2
    flat_rows = sum(piece.flat_rows for piece in pieces)
    outs, flat, packed = refs[:-2], refs[-2], refs[-1]
    high = index_ref[0] // LOW_COUNT
    packed[:half, :] = (
        own_ref[:half, :]
        + beside_first_ref[...].astype(jnp.float32)
        + across_first_ref[:half, :].astype(jnp.float32)
    )
    packed[half:, :] = (
        own_ref[half:, :]
        + beside_second_ref[...].astype(jnp.float32)
        + across_second_ref[...].astype(jnp.float32)
    )
    start, source = 0, 0
    for piece in pieces:
        for block in range(piece.blocks):
            for place in range(high_count):
                flat[place, pl.ds(start + block, piece.own_rows, stride=piece.blocks), :] = packed[
                    pl.ds(source, piece.own_rows), :
                ]
                source = source + piece.own_rows
        start = start + piece.flat_rows
    for step, out_ref in enumerate(outs):
        out_ref[:flat_rows, :] = flat[high ^ step].astype(out_ref.dtype)
        if out_ref.shape[0] > flat_rows:
            extra = extra_ref[...] + across_first_ref[half:, :].astype(jnp.float32)
            out_ref[flat_rows:, :] = extra.astype(out_ref.dtype)


def array(shape, kind):
    return jax.ShapeDtypeStruct(shape, kind)


def gather_high(rows, doubling):
    high_count = lax.axis_size(ALL_AXES) // LOW_COUNT
    if not doubling:
        return [rows] + [swap(rows, step * LOW_COUNT) for step in range(1, high_count)]
    parts = {0: rows}
    mask = high_count // 2
    while mask:
        parts.update({step | mask: swap(value, mask * LOW_COUNT) for step, value in parts.items()})
        mask = mask // 2
    return [parts[step] for step in range(high_count)]


def gather_near(pieces, parts, behind=()):
    high_count = pieces[0].high_count
    size = sum(piece.size for piece in pieces)
    first, second = local_call(
        functools.partial(pack_kernel, pieces),
        (array((size // 2, LANES), jnp.bfloat16),) * 2,
        parts,
        (
            pltpu.VMEM((high_count, parts[0].shape[0], LANES), jnp.float32),
            pltpu.VMEM((size, LANES), jnp.float32),
        ),
        behind,
    )
    beside_second, across_first = swap(second, 4), swap(first, 2)
    beside_first, across_second = swap(first, 4), swap(second, 2)
    return (
        (first, second, beside_first, beside_second, across_first, across_second),
        (swap(across_first, 4), swap(beside_second, 2)),
    )


def gather_cores(three, diagonal, behind=()):
    (three,) = local_call(
        join_kernel,
        (array((6 * three[0].shape[0], LANES), jnp.bfloat16),),
        three,
        (),
        behind,
    )
    near = (three, *diagonal)
    return near + tuple(swap(value, 1) for value in near)


def scatter_cores(far_three, far_one):
    far_one = swap(far_one, 1)
    return swap(far_three, 1), far_one


def scatter_one(pieces, near_one, far_one, behind=()):
    half = sum(piece.size for piece in pieces) // 2
    to_x, to_y = local_call(
        functools.partial(sum_one_kernel, 2 * half),
        (
            array((near_one.shape[0] - half, LANES), jnp.bfloat16),
            array((half, LANES), jnp.bfloat16),
        ),
        (near_one, far_one),
        (),
        behind,
    )
    return swap(to_x, 4), swap(to_y, 2), to_y


def scatter_three(pieces, near_three, far_three, behind=()):
    size = sum(piece.size for piece in pieces)
    half = size // 2
    own, beside_first, beside_second, across_first, across_second = local_call(
        functools.partial(sum_three_kernel, size),
        (
            array((size, LANES), jnp.float32),
            array((half, LANES), jnp.bfloat16),
            array((half, LANES), jnp.float32),
            array((half, LANES), jnp.float32),
            array((half, LANES), jnp.bfloat16),
        ),
        (near_three, far_three),
        (),
        behind,
    )
    return own, swap(beside_first, 4), beside_second, across_first, swap(across_second, 2)


def scatter_passed(pieces, threes, over_x, over_y, near_one, far_one, behind=()):
    size = sum(piece.size for piece in pieces)
    extra_count = near_one.shape[0] - size
    own, beside_first, beside_second, across_first, across_second = threes
    beside_second, across_first, extra = local_call(
        functools.partial(sum_passed_kernel, size),
        (
            array((size // 2, LANES), jnp.bfloat16),
            array((size // 2 + extra_count, LANES), jnp.bfloat16),
            array((max(extra_count, 8), LANES), jnp.float32),
        ),
        (beside_second, across_first, over_x, over_y, near_one, far_one),
        (),
        behind,
    )
    terms = (
        own,
        beside_first,
        swap(beside_second, 4),
        swap(across_first, 2),
        across_second,
        extra,
    )
    return terms, beside_second


def scatter_high(pieces, terms):
    high_count = pieces[0].high_count
    size = sum(piece.size for piece in pieces)
    flat_rows = sum(piece.flat_rows for piece in pieces)
    out_rows = flat_rows + terms[3].shape[0] - size // 2
    outs = local_call(
        functools.partial(unpack_kernel, pieces),
        (array((out_rows, LANES), jnp.float32),)
        + (array((out_rows, LANES), jnp.bfloat16),) * (high_count - 1),
        terms,
        (
            pltpu.VMEM((high_count, flat_rows, LANES), jnp.float32),
            pltpu.VMEM((size, LANES), jnp.float32),
        ),
    )
    return outs[0] + sum(
        swap(send, step * LOW_COUNT).astype(jnp.float32) for step, send in enumerate(outs) if step
    )


def norm_parts(values):
    scale = lax.rsqrt(jnp.mean(values * values, axis=-1, keepdims=True) + norm_eps)
    return scale, values * scale


def norm_back(scale, normal, upstream, weight_vec):
    weighted = upstream * (1.0 + weight_vec)
    inner = jnp.mean(weighted * normal, axis=-1, keepdims=True)
    return scale * (weighted - normal * inner), jnp.sum(normal * upstream, axis=0, keepdims=True)


def product(left_side, right_side, left_axis, right_axis):
    return lax.dot_general(
        left_side,
        right_side,
        (((left_axis,), (right_axis,)), ((), ())),
        preferred_element_type=jnp.float32,
    )


def unordered(rows_in, order_low):
    upper = rows_in.astype(jnp.bfloat16)
    lower = (rows_in - upper.astype(jnp.float32)).astype(jnp.bfloat16)
    return product(upper, order_low, 1, 1) + product(lower, order_low, 1, 1)


def weight_rows(refs, size, order, start, rows):
    three, *diagonal = refs[:3] if order < 4 else refs[3:]
    if order % 4 == 3:
        second = int(2 * start >= size)
        ref, start = diagonal[second], start - second * (size // 2)
    else:
        ref, start = three, order % 4 * size + start
    return ref[start : start + rows, :]


def put_rows(refs, size, order, start, rows):
    three, one = refs[:2] if order < 4 else refs[2:]
    if order % 4 == 3:
        one[start : start + rows.shape[0], :] = rows
    else:
        start = order % 4 * size + start
        three[start : start + rows.shape[0], :] = rows


def wide_tile(refs, size, start, rows):
    return jnp.concatenate(
        [weight_rows(refs, size, order, start, rows) for order in range(LOW_COUNT)]
    )


def put_wide_tile(refs, size, start, rows, tile):
    for order in range(LOW_COUNT):
        put_rows(refs, size, order, start, tile[order * rows : (order + 1) * rows])


def tall_rows(piece, low):
    for order, mask in enumerate(LOW_MASKS):
        for block in range(piece.blocks):
            for place in range(piece.high_count):
                row = (place * LOW_COUNT + (low ^ mask)) * piece.own_rows
                yield (
                    order,
                    block * piece.block_rows + place * piece.own_rows,
                    pl.ds(pl.multiple_of(row, piece.own_rows), piece.own_rows),
                    slice(block * LANES, (block + 1) * LANES),
                )


def ffn_kernel(
    gate_piece,
    down_piece,
    index_ref,
    middle_ref,
    cotangent_ref,
    gain_in_ref,
    gain_out_ref,
    order_ref,
    *refs,
):
    weight_refs, grad_refs = refs[:6], refs[10:14]
    block_out_ref, grad_middle_ref, grad_gain_in_ref, grad_gain_out_ref = refs[6:10]
    down_ref, hidden_ref, gelu_ref, slope_ref = refs[14:]
    low = index_ref[0] % LOW_COUNT
    rows = gate_piece.block_rows
    size = 2 * gate_piece.size + down_piece.size
    width = 2 * LANES
    for order, start, matrix_rows, columns in tall_rows(down_piece, low):
        start = start + 2 * gate_piece.size
        down_ref[matrix_rows, columns] = weight_rows(
            weight_refs, size, order, start, down_piece.own_rows
        )

    def wide_tiles(step):
        return [
            jnp.concatenate(
                [
                    wide_tile(weight_refs, size, offset + block * rows, rows)
                    for block in (2 * step, 2 * step + 1)
                ],
                axis=1,
            )
            for offset in (0, gate_piece.size)
        ]

    middle = middle_ref[...]
    scale_in, normal_in = norm_parts(middle)
    order_low = order_ref[...]
    normed = (normal_in * (1.0 + gain_in_ref[...])).astype(jnp.bfloat16)
    normed = product(normed, order_low, 1, 0).astype(jnp.bfloat16)
    for step in range(FF // width):
        columns = slice(step * width, (step + 1) * width)
        gate_weight, up_weight = wide_tiles(step)
        gate = product(normed, gate_weight, 1, 0)
        up = product(normed, up_weight, 1, 0)
        square = gate * gate
        bend = jnp.tanh(GELU_SCALE * gate * (1.0 + GELU_CUBE * square))
        half = 0.5 * (1.0 + bend)
        gelu = gate * half
        slope = half + 0.5 * gate * (1.0 - bend * bend) * GELU_SCALE * (
            1.0 + 3.0 * GELU_CUBE * square
        )
        gelu_ref[:, columns] = gelu
        slope_ref[:, columns] = slope * up
        hidden_ref[:, columns] = (gelu * up).astype(jnp.bfloat16)
    hidden = hidden_ref[...]
    scale_out, normal_out = norm_parts(product(hidden, down_ref[...], 1, 0))
    block_out_ref[...] = (middle + normal_out * (1.0 + gain_out_ref[...])).astype(jnp.bfloat16)
    upstream = cotangent_ref[...].astype(jnp.float32)
    grad_ffn, grad_gain_out_ref[...] = norm_back(
        scale_out, normal_out, upstream, gain_out_ref[...]
    )
    grad_ffn = grad_ffn.astype(jnp.bfloat16)
    grad_normed = jnp.zeros(middle.shape, jnp.float32)
    for step in range(FF // width):
        columns = slice(step * width, (step + 1) * width)
        grad_hidden = product(grad_ffn, down_ref[columns, :], 1, 1)
        down_ref[columns, :] = product(hidden_ref[:, columns], grad_ffn, 0, 0).astype(jnp.bfloat16)
        grads = [
            (grad_hidden * slope_ref[:, columns]).astype(jnp.bfloat16),
            (grad_hidden * gelu_ref[:, columns]).astype(jnp.bfloat16),
        ]
        for place, (grad, weight) in enumerate(zip(grads, wide_tiles(step))):
            grad_weight = product(normed, grad, 0, 0).astype(jnp.bfloat16)
            for side in range(2):
                put_wide_tile(
                    grad_refs,
                    size,
                    place * gate_piece.size + (2 * step + side) * rows,
                    rows,
                    grad_weight[:, side * LANES : (side + 1) * LANES],
                )
            grad_normed = grad_normed + product(grad, weight, 1, 1)
    for order, start, matrix_rows, columns in tall_rows(down_piece, low):
        start = start + 2 * gate_piece.size
        put_rows(grad_refs, size, order, start, down_ref[matrix_rows, columns])
    grad_middle, grad_gain_in_ref[...] = norm_back(
        scale_in, normal_in, unordered(grad_normed, order_low), gain_in_ref[...]
    )
    grad_middle_ref[...] = upstream + grad_middle


def grad_arrays(pieces, extra_count=0):
    size = sum(piece.size for piece in pieces)
    return (
        array((3 * size, LANES), jnp.bfloat16),
        array((size + extra_count, LANES), jnp.bfloat16),
    ) * 2


def ffn_blocks(pieces, middle, cotangent, gain_in, gain_out, order, blocks):
    rows = middle.shape[0]
    outs = local_call(
        functools.partial(ffn_kernel, pieces[4], pieces[6]),
        (
            array((rows, D), jnp.bfloat16),
            array((rows, D), jnp.float32),
            array((1, D), jnp.float32),
            array((1, D), jnp.float32),
            *grad_arrays(pieces[4:7]),
        ),
        (middle, cotangent, gain_in, gain_out, order, *blocks),
        (
            pltpu.VMEM((FF, D), jnp.bfloat16),
            pltpu.VMEM((rows, FF), jnp.bfloat16),
            pltpu.VMEM((rows, FF), jnp.float32),
            pltpu.VMEM((rows, FF), jnp.float32),
        ),
    )
    return *outs[:4], outs[4:]


def turn(values, cosine, sine):
    first_half, second_half = values[:, : HD // 2], values[:, HD // 2 :]
    return jnp.concatenate(
        [first_half * cosine - second_half * sine, second_half * cosine + first_half * sine], axis=1
    )


def wide_head(refs, size, start, rows):
    return jnp.concatenate(
        [wide_tile(refs, size, start + side * rows, rows) for side in range(2)], axis=1
    )


def head_starts(pieces):
    rows = pieces[0].block_rows
    return [2 * rows * head for head in range(HQ + 2)]


def project_kernel(
    pieces,
    index_ref,
    tokens_ref,
    gain_ref,
    gain_query_ref,
    gain_key_ref,
    cosine_ref,
    sine_ref,
    order_ref,
    *refs,
):
    weight_refs = refs[:6]
    normed_ref, query_proj_ref, key_proj_ref, query_ref, key_value_ref = refs[6:]
    size = sum(piece.size for piece in pieces)
    rows = pieces[0].block_rows
    cosine, sine = cosine_ref[...], sine_ref[...]
    _, normal = norm_parts(tokens_ref[...].astype(jnp.float32))
    normed = (normal * (1.0 + gain_ref[...])).astype(jnp.bfloat16)
    normed = product(normed, order_ref[...], 1, 0).astype(jnp.bfloat16)
    normed_ref[...] = normed
    starts = head_starts(pieces)
    for head, start in enumerate(starts):
        proj = product(normed, wide_head(weight_refs, size, start, rows), 1, 0)
        columns = slice(head * HD, (head + 1) * HD)
        if head == HQ + 1:
            key_value_ref[:, HD:] = proj.astype(jnp.bfloat16)
            continue
        gain_vec = gain_query_ref[...] if head < HQ else gain_key_ref[...]
        _, normal = norm_parts(proj)
        turned = turn(normal * (1.0 + gain_vec), cosine, sine).astype(jnp.bfloat16)
        if head < HQ:
            query_proj_ref[:, columns] = proj
            query_ref[:, columns] = turned
        else:
            key_proj_ref[...] = proj
            key_value_ref[:, :HD] = turned


def attend_kernel(
    pieces,
    index_ref,
    tokens_ref,
    gain_ref,
    allowed_ref,
    query_ref,
    *refs,
):
    weight_refs, key_value_refs = refs[:6], refs[6:-5]
    probs_ref, attended_ref, attn_out_ref, middle_ref, out_weight_ref = refs[-5:]
    out_piece = pieces[-1]
    low = index_ref[0] % LOW_COUNT
    size = sum(piece.size for piece in pieces)
    out_start = size - out_piece.size
    for order, start, matrix_rows, columns in tall_rows(out_piece, low):
        out_weight_ref[matrix_rows, columns] = weight_rows(
            weight_refs, size, order, start + out_start, out_piece.own_rows
        )
    rows = tokens_ref.shape[0]
    allowed = allowed_ref[...] > 0.0
    keys = jnp.concatenate([ref[:, :HD] for ref in key_value_refs])
    values = jnp.concatenate([ref[:, HD:] for ref in key_value_refs])
    count = keys.shape[0]
    for head in range(HQ):
        columns = slice(head * HD, (head + 1) * HD)
        scores = product(query_ref[:, columns], keys, 1, 1) * HD ** (-0.5)
        scores = jnp.where(allowed, scores, -1e30)
        raised = jnp.exp(scores - jnp.max(scores, axis=-1, keepdims=True))
        probs = raised / jnp.sum(raised, axis=-1, keepdims=True)
        probs_ref[:, head * count : (head + 1) * count] = probs
        attended_ref[:, columns] = product(probs.astype(jnp.bfloat16), values, 1, 0).astype(
            jnp.bfloat16
        )
    attn_out = product(attended_ref[...], out_weight_ref[...], 1, 0)
    attn_out_ref[...] = attn_out
    _, normal = norm_parts(attn_out)
    middle_ref[...] = tokens_ref[...].astype(jnp.float32) + normal * (1.0 + gain_ref[...])


def attend_back_kernel(
    index_ref,
    grad_middle_ref,
    attn_out_ref,
    gain_ref,
    out_weight_ref,
    attended_ref,
    probs_ref,
    query_ref,
    *refs,
):
    part_count = (len(refs) - 3) // 2
    key_value_refs = refs[:part_count]
    grad_out_weight_ref, grad_query_ref, grad_gain_ref = refs[part_count : part_count + 3]
    grad_key_value_refs = refs[part_count + 3 :]
    rows = query_ref.shape[0]
    scale, normal = norm_parts(attn_out_ref[...])
    grad_attn, grad_gain_ref[...] = norm_back(scale, normal, grad_middle_ref[...], gain_ref[...])
    grad_attn = grad_attn.astype(jnp.bfloat16)
    grad_out_weight_ref[...] = product(attended_ref[...], grad_attn, 0, 0).astype(jnp.bfloat16)
    keys = jnp.concatenate([ref[:, :HD] for ref in key_value_refs])
    values = jnp.concatenate([ref[:, HD:] for ref in key_value_refs])
    count = keys.shape[0]
    grad_keys = jnp.zeros((count, HD), jnp.float32)
    grad_values = jnp.zeros((count, HD), jnp.float32)
    for head in range(HQ):
        columns = slice(head * HD, (head + 1) * HD)
        grad_attended = product(grad_attn, out_weight_ref[columns, :], 1, 1).astype(jnp.bfloat16)
        probs = probs_ref[:, head * count : (head + 1) * count]
        grad_probs = product(grad_attended, values, 1, 1)
        grad_values = grad_values + product(probs.astype(jnp.bfloat16), grad_attended, 0, 0)
        inner = jnp.sum(probs * grad_probs, axis=-1, keepdims=True)
        grad_scores = (probs * (grad_probs - inner) * HD ** (-0.5)).astype(jnp.bfloat16)
        grad_query_ref[:, columns] = product(grad_scores, keys, 1, 0)
        grad_keys = grad_keys + product(grad_scores, query_ref[:, columns], 0, 0)
    for part, ref in enumerate(grad_key_value_refs):
        ref[:, :HD] = grad_keys[part * rows : (part + 1) * rows].astype(ref.dtype)
        ref[:, HD:] = grad_values[part * rows : (part + 1) * rows].astype(ref.dtype)


def query_back_kernel(
    pieces,
    index_ref,
    gain_ref,
    cosine_ref,
    sine_ref,
    normed_ref,
    query_proj_ref,
    grad_query_ref,
    *refs,
):
    weight_refs = refs[:6]
    grad_weight_ref, grad_normed_ref, grad_gain_ref = refs[6:]
    size = sum(piece.size for piece in pieces)
    rows = pieces[0].block_rows
    cosine, sine = cosine_ref[...], sine_ref[...]
    normed = normed_ref[...]
    grad_normed = jnp.zeros(grad_normed_ref.shape, jnp.float32)
    grad_gain = jnp.zeros((1, HD), jnp.float32)
    for head, start in enumerate(head_starts(pieces)[:HQ]):
        columns = slice(head * HD, (head + 1) * HD)
        scale, normal = norm_parts(query_proj_ref[:, columns])
        upstream = turn(grad_query_ref[:, columns], cosine, -sine)
        grad, gain_row = norm_back(scale, normal, upstream, gain_ref[...])
        grad_gain = grad_gain + gain_row
        grad = grad.astype(jnp.bfloat16)
        weight = wide_head(weight_refs, size, start, rows)
        grad_normed = grad_normed + product(grad, weight, 1, 1)
        grad_weight_ref[:, columns] = product(normed, grad, 0, 0).astype(jnp.bfloat16)
    grad_normed_ref[...] = grad_normed
    grad_gain_ref[...] = grad_gain


def project_back_kernel(
    pieces,
    index_ref,
    tokens_ref,
    gain_ref,
    gain_key_ref,
    cosine_ref,
    sine_ref,
    order_ref,
    normed_ref,
    key_proj_ref,
    grad_query_weight_ref,
    grad_normed_ref,
    grad_middle_ref,
    grad_out_weight_ref,
    gain_attn_ref,
    gain_ffin_ref,
    gain_ffout_ref,
    gain_query_ref,
    *refs,
):
    weight_refs, key_value_refs, grad_refs = refs[:6], refs[6:-6], refs[-6:-2]
    input_grad_ref, grad_gain_ref = refs[-2:]
    low = index_ref[0] % LOW_COUNT
    size = sum(piece.size for piece in pieces)
    rows = pieces[0].block_rows
    normed = normed_ref[...]
    key_value = sum(ref[...].astype(jnp.float32) for ref in key_value_refs)
    scale, normal = norm_parts(key_proj_ref[...])
    upstream = turn(key_value[:, :HD], cosine_ref[...], -sine_ref[...])
    grad_key, grad_gain_key = norm_back(scale, normal, upstream, gain_key_ref[...])
    grad_normed = grad_normed_ref[...]
    for head, start in enumerate(head_starts(pieces)):
        if head < HQ:
            grad_weight = grad_query_weight_ref[:, head * HD : (head + 1) * HD]
        else:
            grad = (grad_key if head == HQ else key_value[:, HD:]).astype(jnp.bfloat16)
            weight = wide_head(weight_refs, size, start, rows)
            grad_normed = grad_normed + product(grad, weight, 1, 1)
            grad_weight = product(normed, grad, 0, 0).astype(jnp.bfloat16)
        for side in range(2):
            put_wide_tile(
                grad_refs,
                size,
                start + side * rows,
                rows,
                grad_weight[:, side * LANES : (side + 1) * LANES],
            )
    out_piece = pieces[-1]
    for order, start, matrix_rows, columns in tall_rows(out_piece, low):
        start = start + size - out_piece.size
        put_rows(grad_refs, size, order, start, grad_out_weight_ref[matrix_rows, columns])
    scale, normal = norm_parts(tokens_ref[...].astype(jnp.float32))
    grad_inputs, grad_gain_input = norm_back(
        scale, normal, unordered(grad_normed, order_ref[...]), gain_ref[...]
    )
    input_grad_ref[...] = (grad_middle_ref[...] + grad_inputs).astype(jnp.bfloat16)
    grad_gains = [
        grad_gain_input,
        gain_attn_ref[...],
        gain_ffin_ref[...],
        gain_ffout_ref[...],
        gain_query_ref[...],
        grad_gain_key,
    ]
    row = 0
    grad_gain_ref[...] = jnp.zeros(grad_gain_ref.shape, jnp.float32)
    for values in grad_gains:
        for start in range(0, values.shape[1], LANES):
            grad_gain_ref[row : row + 1, :] = values[:, start : start + LANES]
            row = row + 1
    for target in (grad_refs[1], grad_refs[3]):
        target[size:, :] = grad_gain_ref[...].astype(jnp.bfloat16)


def width_order(device_count):
    low = lax.axis_index(ALL_AXES) % LOW_COUNT
    rows = D // device_count
    high_count = device_count // LOW_COUNT
    column = jnp.arange(D, dtype=jnp.int32)
    place = column // (rows * high_count)
    mask = (place & 1) * 4 + ((place >> 1) & 1) * 2 + (place >> 2)
    high = (column // rows) % high_count
    picked = (high * LOW_COUNT + (low ^ mask)) * rows + column % rows
    return (jnp.arange(D, dtype=jnp.int32)[:, None] == picked[None, :]).astype(jnp.bfloat16)


GAIN_ROWS = 32


def shards_blocks(
    device_count,
    tokens,
    doc_ids,
    cotangent,
    master,
    first_moment,
    second_moment,
    gains,
    gain_first,
    gain_second,
):
    pieces = [Piece(*shape_pair, device_count) for shape_pair in piece_shapes()]
    attention_pieces = pieces[:4]
    local_rows = tokens.shape[0]
    group_size = lax.axis_size("group")
    first_row = lax.axis_index("group") * local_rows
    attention_rows = sum(piece.flat_rows for piece in attention_pieces)
    ffn_pieces = pieces[4:7]
    attention_parts = gather_high(master[:attention_rows].astype(jnp.bfloat16), False)
    (ffn_rows,) = local_call(
        round_kernel,
        (array((master.shape[0] - attention_rows, LANES), jnp.bfloat16),),
        (master,),
        (),
        (attention_parts[1],),
    )
    ffn_parts = gather_high(ffn_rows, True)
    attention_near = gather_near(attention_pieces, attention_parts)
    attention_blocks = gather_cores(*attention_near)
    ffn_near = gather_near(
        ffn_pieces, ffn_parts, (attention_blocks[0], *attention_near[1])
    )
    gain_parts = []
    for start, width in ((0, D), (D, D), (2 * D, D), (3 * D, D), (4 * D, HD), (4 * D + HD, HD)):
        gain_parts.append(gains[start : start + width][None])
    gain_input, gain_attn, gain_ffin, gain_ffout, gain_query, gain_key = gain_parts
    order = width_order(device_count)
    doc_row = doc_ids[0]
    angles = lax.dynamic_slice_in_dim(angles_of(positions(doc_row)), first_row, local_rows, 0)
    cosine, sine = jnp.cos(angles), jnp.sin(angles)
    query_docs = lax.dynamic_slice_in_dim(doc_row, first_row, local_rows, 0)
    reach = min(-(-(WINDOW - 1) // local_rows), group_size - 1)
    key_count = (reach + 1) * local_rows
    doc_pad = jnp.concatenate([jnp.full((reach * local_rows,), -1, jnp.int32), doc_row])
    key_docs = lax.dynamic_slice_in_dim(doc_pad, first_row, key_count, 0)
    key_index = first_row - reach * local_rows + jnp.arange(key_count, dtype=jnp.int32)
    query_index = first_row + jnp.arange(local_rows, dtype=jnp.int32)
    distance = query_index[:, None] - key_index[None, :]
    allowed = (distance >= 0) & (distance < WINDOW) & (key_docs[None, :] == query_docs[:, None])
    allowed = allowed.astype(jnp.float32)

    width = HQ * HD
    normed, query_proj, key_proj, query_rot, key_value = local_call(
        functools.partial(project_kernel, attention_pieces),
        (
            array((local_rows, D), jnp.bfloat16),
            array((local_rows, width), jnp.float32),
            array((local_rows, HD), jnp.float32),
            array((local_rows, width), jnp.bfloat16),
            array((local_rows, 2 * HD), jnp.bfloat16),
        ),
        (tokens, gain_input, gain_query, gain_key, cosine, sine, order, *attention_blocks),
    )
    ffn_weights = gather_cores(*ffn_near, (key_value,))
    key_values = [shifted(key_value, "group", offset) for offset in range(reach, 0, -1)]
    key_values.append(key_value)
    probs, attended, attn_out, middle, out_weight = local_call(
        functools.partial(attend_kernel, attention_pieces),
        (
            array((local_rows, HQ * key_count), jnp.float32),
            array((local_rows, width), jnp.bfloat16),
            array((local_rows, D), jnp.float32),
            array((local_rows, D), jnp.float32),
            array((width, D), jnp.bfloat16),
        ),
        (tokens, gain_attn, allowed, query_rot, *attention_blocks, *key_values),
        (),
        (ffn_weights[0],),
    )
    outputs, grad_middle, grad_gain_ffin, grad_gain_ffout, grads_ffn = ffn_blocks(
        pieces, middle, cotangent, gain_ffin, gain_ffout, order, ffn_weights
    )
    near_three, near_one, far_three, far_one = grads_ffn
    far_three, far_one = scatter_cores(far_three, far_one)
    grad_out_weight, grad_query, grad_gain_attn, *grad_key_values = local_call(
        attend_back_kernel,
        (
            array((width, D), jnp.bfloat16),
            array((local_rows, width), jnp.float32),
            array((1, D), jnp.float32),
            *(array((local_rows, 2 * HD), jnp.bfloat16),) * reach,
            array((local_rows, 2 * HD), jnp.float32),
        ),
        (
            grad_middle,
            attn_out,
            gain_attn,
            out_weight,
            attended,
            probs,
            query_rot,
            *key_values,
        ),
    )
    over_x, over_y, sent = scatter_one(ffn_pieces, near_one, far_one, (grad_query,))
    threes = scatter_three(ffn_pieces, near_three, far_three, (sent,))
    grad_query_weight, grad_normed, grad_gain_query = local_call(
        functools.partial(query_back_kernel, attention_pieces),
        (
            array((D, width), jnp.bfloat16),
            array((local_rows, D), jnp.float32),
            array((1, HD), jnp.float32),
        ),
        (gain_query, cosine, sine, normed, query_proj, grad_query, *attention_blocks),
        (),
        (threes[0],),
    )
    ffn_terms, sent = scatter_passed(
        ffn_pieces, threes, over_x, over_y, near_one, far_one, (grad_normed,)
    )
    grad_key_values = [
        shifted(value, "group", place - reach) if place < reach else value
        for place, value in enumerate(grad_key_values)
    ]
    *grads_attention, grad_inputs, _ = local_call(
        functools.partial(project_back_kernel, attention_pieces),
        (
            *grad_arrays(attention_pieces, GAIN_ROWS),
            array((local_rows, D), jnp.bfloat16),
            array((GAIN_ROWS, LANES), jnp.float32),
        ),
        (
            tokens,
            gain_input,
            gain_key,
            cosine,
            sine,
            order,
            normed,
            key_proj,
            grad_query_weight,
            grad_normed,
            grad_middle,
            grad_out_weight,
            grad_gain_attn,
            grad_gain_ffin,
            grad_gain_ffout,
            grad_gain_query,
            *attention_blocks,
            *grad_key_values,
        ),
        (),
        (threes[1], threes[4], sent),
    )
    grads_ffn = scatter_high(ffn_pieces, ffn_terms)
    near_three, near_one, far_three, far_one = grads_attention
    far_three, far_one = scatter_cores(far_three, far_one)
    over_x, over_y, sent = scatter_one(attention_pieces, near_one, far_one)
    threes = scatter_three(attention_pieces, near_three, far_three, (sent,))
    terms, _ = scatter_passed(attention_pieces, threes, over_x, over_y, near_one, far_one)
    grads_attention = scatter_high(attention_pieces, terms)
    gain_grads = grads_attention[attention_rows:].reshape(-1)[: gains.shape[0]]
    grads_local = jnp.concatenate([grads_attention[:attention_rows], grads_ffn])
    return (
        outputs,
        grad_inputs,
        *adam_update(grads_local, first_moment, second_moment, master, learn_rate, weight_decay),
        *adam_update(gain_grads, gain_first, gain_second, gains, gain_rate, 0.0),
    )


def shards(
    tokens, doc_ids, cotangent, master, first_moment, second_moment, gains, gain_first, gain_second
):
    group_size = lax.axis_size("group")
    devices_all = lax.axis_size("dp") * group_size
    if aligned(devices_all):
        return shards_blocks(
            devices_all,
            tokens,
            doc_ids,
            cotangent,
            master,
            first_moment,
            second_moment,
            gains,
            gain_first,
            gain_second,
        )
    group_index = lax.axis_index("group")
    local_rows = tokens.shape[0]
    shard_parts = [
        part_rows.astype(jnp.bfloat16) for part_rows in split_rows(master, piece_rows(devices_all))
    ]
    gathered = (
        lax.all_gather(shard_parts[0], ("dp", "group"), axis=0, tiled=True),
        lax.all_gather(shard_parts[1], ("dp", "group"), axis=0, tiled=True),
        lax.all_gather(shard_parts[2], ("dp", "group"), axis=0, tiled=True),
        lax.all_gather(shard_parts[3], ("dp", "group"), axis=0, tiled=True),
        lax.all_gather(shard_parts[4], ("dp", "group"), axis=0, tiled=True),
        lax.all_gather(shard_parts[5], ("dp", "group"), axis=0, tiled=True),
        lax.all_gather(shard_parts[6], ("dp", "group"), axis=0, tiled=True),
    )
    query_weight, key_weight, value_weight, out_weight, gate_weight, up_weight, down_weight = [
        full_rows.reshape(shape_pair) for full_rows, shape_pair in zip(gathered, piece_shapes())
    ]
    norm_input = gains[0:D]
    norm_attn = gains[D : 2 * D]
    norm_ffin = gains[2 * D : 3 * D]
    norm_ffout = gains[3 * D : 4 * D]
    norm_query = gains[4 * D : 4 * D + HD]
    norm_key = gains[4 * D + HD : 4 * D + 2 * HD]
    doc_row = doc_ids[0]
    first_row = group_index * local_rows
    angles = lax.dynamic_slice_in_dim(angles_of(positions(doc_row)), first_row, local_rows, 0)
    query_docs = lax.dynamic_slice_in_dim(doc_row, first_row, local_rows, 0)
    inputs = tokens.astype(jnp.float32)
    normed, back_input = jax.vjp(rms_norm, inputs, norm_input)
    normed_low = normed.astype(jnp.bfloat16)
    query_proj = matmul(normed_low, query_weight)
    key_proj = matmul(normed_low, key_weight)
    value_proj = matmul(normed_low, value_weight)

    def query_prep(flat_rows, gain_vec):
        return rotate(rms_norm(flat_rows.reshape(local_rows, HQ, HD), gain_vec), angles[:, None, :])

    def key_prep(rows_in, gain_vec):
        return rotate(rms_norm(rows_in, gain_vec), angles)

    query_rot, back_query = jax.vjp(query_prep, query_proj, norm_query)
    key_rot, back_key = jax.vjp(key_prep, key_proj, norm_key)
    query_low = query_rot.astype(jnp.bfloat16)
    key_low = key_rot.astype(jnp.bfloat16)
    value_low = value_proj.astype(jnp.bfloat16)
    reach = min(-(-(WINDOW - 1) // local_rows), group_size - 1)
    key_list = [key_low]
    value_list = [value_low]
    for offset in range(1, reach + 1):
        key_far, value_far = shifted((key_low, value_low), "group", offset)
        key_list.insert(0, key_far)
        value_list.insert(0, value_far)
    key_all = jnp.concatenate(key_list, axis=0)
    value_all = jnp.concatenate(value_list, axis=0)
    key_count = (reach + 1) * local_rows
    doc_pad = jnp.concatenate([jnp.full((reach * local_rows,), -1, jnp.int32), doc_row])
    key_docs = lax.dynamic_slice_in_dim(doc_pad, first_row, key_count, 0)
    key_index = (group_index - reach) * local_rows + jnp.arange(key_count, dtype=jnp.int32)
    query_index = first_row + jnp.arange(local_rows, dtype=jnp.int32)
    distance = query_index[:, None] - key_index[None, :]
    allowed = (distance >= 0) & (distance < WINDOW) & (key_docs[None, :] == query_docs[:, None])

    def scores_of(key_rows_low):
        raw_scores = jnp.einsum(
            "qhd,kd->hqk", query_low, key_rows_low, preferred_element_type=jnp.float32
        ) * HD ** (-0.5)
        return jnp.where(allowed[None], raw_scores, -1e30)

    masked = scores_of(key_all)
    top_score = jnp.max(masked, axis=-1, keepdims=True)
    log_total = top_score + jnp.log(jnp.sum(jnp.exp(masked - top_score), axis=-1, keepdims=True))
    probs = jnp.exp(masked - log_total)
    attended = jnp.einsum(
        "hqk,kd->qhd", probs.astype(jnp.bfloat16), value_all, preferred_element_type=jnp.float32
    )
    attended_low = attended.reshape(local_rows, HQ * HD).astype(jnp.bfloat16)
    attn_out = matmul(attended_low, out_weight)
    branch_one, back_attn = jax.vjp(rms_norm, attn_out, norm_attn)
    middle = inputs + branch_one
    normed_two, back_ffin = jax.vjp(rms_norm, middle, norm_ffin)
    normed_two_low = normed_two.astype(jnp.bfloat16)
    gate_proj = matmul(normed_two_low, gate_weight)
    up_proj = matmul(normed_two_low, up_weight)
    hidden, back_hidden = jax.vjp(geglu, gate_proj, up_proj)
    hidden_low = hidden.astype(jnp.bfloat16)
    ffn_out = matmul(hidden_low, down_weight)
    branch_two, back_ffout = jax.vjp(rms_norm, ffn_out, norm_ffout)
    outputs = middle + branch_two
    grad_out = cotangent.astype(jnp.float32)
    grad_ffn, grad_gain_ffout = back_ffout(grad_out)
    grad_ffn_low = grad_ffn.astype(jnp.bfloat16)
    grad_down_w = jnp.einsum(
        "tf,td->fd", hidden_low, grad_ffn_low, preferred_element_type=jnp.float32
    )
    grad_hidden = jnp.einsum(
        "td,fd->tf", grad_ffn_low, down_weight, preferred_element_type=jnp.float32
    )
    grad_gate, grad_up = back_hidden(grad_hidden)
    grad_gate_low = grad_gate.astype(jnp.bfloat16)
    grad_up_low = grad_up.astype(jnp.bfloat16)
    grad_gate_w = jnp.einsum(
        "td,tf->df", normed_two_low, grad_gate_low, preferred_element_type=jnp.float32
    )
    grad_up_w = jnp.einsum(
        "td,tf->df", normed_two_low, grad_up_low, preferred_element_type=jnp.float32
    )
    grad_normed_two = jnp.einsum(
        "tf,df->td", grad_gate_low, gate_weight, preferred_element_type=jnp.float32
    ) + jnp.einsum("tf,df->td", grad_up_low, up_weight, preferred_element_type=jnp.float32)
    grad_middle_norm, grad_gain_ffin = back_ffin(grad_normed_two)
    grad_middle = grad_out + grad_middle_norm
    grad_attn, grad_gain_attn = back_attn(grad_middle)
    grad_attn_low = grad_attn.astype(jnp.bfloat16)
    grad_out_w = jnp.einsum(
        "to,td->od", attended_low, grad_attn_low, preferred_element_type=jnp.float32
    )
    grad_attended = jnp.einsum(
        "td,od->to", grad_attn_low, out_weight, preferred_element_type=jnp.float32
    )
    grad_attended_low = grad_attended.astype(jnp.bfloat16).reshape(local_rows, HQ, HD)
    probs_again = jnp.exp(scores_of(key_all) - log_total)
    grad_probs = jnp.einsum(
        "qhd,kd->hqk", grad_attended_low, value_all, preferred_element_type=jnp.float32
    )
    grad_value_all = jnp.einsum(
        "hqk,qhd->kd",
        probs_again.astype(jnp.bfloat16),
        grad_attended_low,
        preferred_element_type=jnp.float32,
    )
    grad_scores = probs_again * (
        grad_probs - jnp.sum(probs_again * grad_probs, axis=-1, keepdims=True)
    )
    grad_scores_low = (grad_scores * HD ** (-0.5)).astype(jnp.bfloat16)
    grad_query = jnp.einsum(
        "hqk,kd->qhd", grad_scores_low, key_all, preferred_element_type=jnp.float32
    )
    grad_key_all = jnp.einsum(
        "hqk,qhd->kd", grad_scores_low, query_low, preferred_element_type=jnp.float32
    )
    key_total = grad_key_all[reach * local_rows :]
    value_total = grad_value_all[reach * local_rows :]
    for offset in range(1, reach + 1):
        row_start = (reach - offset) * local_rows
        key_back, value_back = (
            shifted(
                grad_key_all[row_start : row_start + local_rows].astype(jnp.bfloat16),
                "group",
                -offset,
            ).astype(jnp.float32),
            shifted(
                grad_value_all[row_start : row_start + local_rows].astype(jnp.bfloat16),
                "group",
                -offset,
            ).astype(jnp.float32),
        )
        key_total = key_total + key_back
        value_total = value_total + value_back
    grad_query_proj, grad_gain_query = back_query(grad_query)
    grad_key_proj, grad_gain_key = back_key(key_total)
    grad_query_low = grad_query_proj.astype(jnp.bfloat16)
    grad_key_low = grad_key_proj.astype(jnp.bfloat16)
    grad_value_low = value_total.astype(jnp.bfloat16)
    grad_query_w = jnp.einsum(
        "td,te->de", normed_low, grad_query_low, preferred_element_type=jnp.float32
    )
    grad_key_w = jnp.einsum(
        "td,te->de", normed_low, grad_key_low, preferred_element_type=jnp.float32
    )
    grad_value_w = jnp.einsum(
        "td,te->de", normed_low, grad_value_low, preferred_element_type=jnp.float32
    )
    grad_normed = jnp.einsum(
        "te,de->td", grad_query_low, query_weight, preferred_element_type=jnp.float32
    )
    grad_normed = grad_normed + jnp.einsum(
        "te,de->td", grad_key_low, key_weight, preferred_element_type=jnp.float32
    )
    grad_normed = grad_normed + jnp.einsum(
        "te,de->td", grad_value_low, value_weight, preferred_element_type=jnp.float32
    )
    grad_input_norm, grad_gain_input = back_input(grad_normed)
    grad_inputs = grad_middle + grad_input_norm
    flat_query = grad_query_w.reshape(-1, 128)
    flat_key = grad_key_w.reshape(-1, 128)
    flat_value = grad_value_w.reshape(-1, 128)
    flat_out = grad_out_w.reshape(-1, 128)
    flat_gate = grad_gate_w.reshape(-1, 128)
    flat_up = grad_up_w.reshape(-1, 128)
    flat_down = grad_down_w.reshape(-1, 128)
    reduced = (
        lax.psum_scatter(flat_query, ("dp", "group"), scatter_dimension=0, tiled=True),
        lax.psum_scatter(flat_key, ("dp", "group"), scatter_dimension=0, tiled=True),
        lax.psum_scatter(flat_value, ("dp", "group"), scatter_dimension=0, tiled=True),
        lax.psum_scatter(flat_out, ("dp", "group"), scatter_dimension=0, tiled=True),
        lax.psum_scatter(flat_gate, ("dp", "group"), scatter_dimension=0, tiled=True),
        lax.psum_scatter(flat_up, ("dp", "group"), scatter_dimension=0, tiled=True),
        lax.psum_scatter(flat_down, ("dp", "group"), scatter_dimension=0, tiled=True),
    )
    grads_local = jnp.concatenate(list(reduced), axis=0)
    gain_grads = lax.psum(
        jnp.concatenate(
            [
                grad_gain_input,
                grad_gain_attn,
                grad_gain_ffin,
                grad_gain_ffout,
                grad_gain_query,
                grad_gain_key,
            ]
        ),
        ("dp", "group"),
    )
    moment_first, moment_second, master_new = adam_update(
        grads_local, first_moment, second_moment, master, learn_rate, weight_decay
    )
    gain_moment_first, gain_moment_second, gains_new = adam_update(
        gain_grads, gain_first, gain_second, gains, gain_rate, 0.0
    )
    return (
        outputs.astype(jnp.bfloat16),
        grad_inputs.astype(jnp.bfloat16),
        moment_first,
        moment_second,
        master_new,
        gain_moment_first,
        gain_moment_second,
        gains_new,
    )


def solution(mesh):
    placed = (
        P(("dp", "group"), None),
        P("dp", None),
        P(("dp", "group"), None),
        P(("dp", "group"), None),
        P(("dp", "group"), None),
        P(("dp", "group"), None),
        P(),
        P(),
        P(),
    )
    return jax.shard_map(
        shards,
        mesh=mesh,
        in_specs=placed,
        out_specs=(
            P(("dp", "group"), None),
            P(("dp", "group"), None),
            P(("dp", "group"), None),
            P(("dp", "group"), None),
            P(("dp", "group"), None),
            P(),
            P(),
            P(),
        ),
        check_vma=False,
    )
```

```python
import functools
import math

import jax
import jax.numpy as jnp
from jax import lax
from jax.experimental import pallas as pl
from jax.experimental.pallas import tpu as pltpu
from jax.sharding import PartitionSpec as P

D = 640
HQ = 4
HD = 256
FF = 2048
WINDOW = 512
STEP = 10
ALL_AXES = ("dp", "group")


norm_eps = 1e-06
rope_base = 10000.0
beta_first = 0.9
beta_second = 0.999
learn_rate = 0.05
gain_rate = 0.25
adam_floor = 1e-08
weight_decay = 0.1


def shifted(value, axis, steps):
    count = lax.axis_size(axis)
    initial, last = (max(0, -steps), min(count, count - steps))
    return lax.ppermute(value, axis, [(source, source + steps) for source in range(initial, last)])


def rms_norm(values, weight_vec):
    return (
        values
        * lax.rsqrt(jnp.mean(values * values, axis=-1, keepdims=True) + norm_eps)
        * (1.0 + weight_vec)
    )


def positions(doc_row):
    length = doc_row.shape[0]
    counter = jnp.arange(length, dtype=jnp.int32)
    starts_here = jnp.concatenate([jnp.ones((1,), jnp.bool_), doc_row[1:] != doc_row[:-1]])
    begins = lax.cummax(jnp.where(starts_here, counter, jnp.zeros_like(counter)), axis=0)
    return counter - begins


def angles_of(places):
    half_dim = HD // 2
    frequency = rope_base ** (-(jnp.arange(half_dim, dtype=jnp.float32) * 2.0 / HD))
    return places.astype(jnp.float32)[:, None] * frequency[None, :]


def rotate(values, angles):
    half_dim = values.shape[-1] // 2
    first_half = values[..., :half_dim]
    second_half = values[..., half_dim:]
    cosine = jnp.cos(angles)
    sine_part = jnp.sin(angles)
    return jnp.concatenate(
        [
            first_half * cosine - second_half * sine_part,
            second_half * cosine + first_half * sine_part,
        ],
        axis=-1,
    )


def geglu(gate_in, up_in):
    return jax.nn.gelu(gate_in, approximate=True) * up_in


def adam_update(gradient, first_old, second_old, params_old, rate, decay_rate):
    first_new = beta_first * first_old + (1.0 - beta_first) * gradient
    second_new = beta_second * second_old + (1.0 - beta_second) * gradient * gradient
    first_hat = first_new / (1.0 - beta_first**STEP)
    second_hat = second_new / (1.0 - beta_second**STEP)
    params_new = params_old - rate * (
        first_hat / (jnp.sqrt(second_hat) + adam_floor) + decay_rate * params_old
    )
    return (first_new, second_new, params_new)


def piece_rows(device_count):
    return [
        entries // (128 * device_count)
        for entries in (D * HQ * HD, D * HD, D * HD, HQ * HD * D, D * FF, D * FF, FF * D)
    ]


def piece_shapes():
    return [(D, HQ * HD), (D, HD), (D, HD), (HQ * HD, D), (D, FF), (D, FF), (FF, D)]


def split_rows(stacked, row_list):
    result = []
    row_start = 0
    for row_count in row_list:
        result.append(stacked[row_start : row_start + row_count])
        row_start = row_start + row_count
    return result


def matmul(left_side, right_side):
    return jnp.dot(left_side, right_side, preferred_element_type=jnp.float32)


LOW_COUNT = 8
LANES = 128
LOW_MASKS = (0, 4, 2, 6, 1, 5, 3, 7)
GELU_SCALE = (2.0 / math.pi) ** 0.5
GELU_CUBE = 0.044715
VMEM_BYTES = 56 * 1024 * 1024


def aligned(device_count):
    return device_count % LOW_COUNT == 0 and D % device_count == 0


def swap(value, mask):
    count = lax.axis_size(ALL_AXES)
    return lax.ppermute(value, ALL_AXES, [(source, source ^ mask) for source in range(count)])


def local_call(kernel, outs, operands, scratch=(), behind=()):
    specs = [pl.BlockSpec(memory_space=pltpu.SMEM)]
    specs = specs + [pl.BlockSpec(memory_space=pltpu.VMEM)] * len(operands)
    specs = specs + [pl.BlockSpec(memory_space=pl.ANY)] * len(behind)
    first, last = 1 + len(operands), 1 + len(operands) + len(behind)

    def body(*refs):
        kernel(*refs[:first], *refs[last:])

    return pl.pallas_call(
        body,
        out_shape=outs,
        in_specs=specs,
        out_specs=tuple(pl.BlockSpec(memory_space=pltpu.VMEM) for _ in outs),
        scratch_shapes=scratch,
        compiler_params=pltpu.CompilerParams(vmem_limit_bytes=VMEM_BYTES),
        cost_estimate=pl.CostEstimate(flops=0, bytes_accessed=0, transcendentals=0),
    )(lax.axis_index(ALL_AXES).astype(jnp.int32).reshape(1), *operands, *behind)


class Piece:
    def __init__(self, rows, columns, device_count):
        self.rows = rows
        self.columns = columns
        self.wide = rows == D
        self.blocks = columns // LANES
        self.own_rows = rows // device_count
        self.flat_rows = self.own_rows * self.blocks
        self.high_count = device_count // LOW_COUNT
        self.block_rows = self.own_rows * self.high_count
        self.size = self.block_rows * self.blocks


def join_kernel(index_ref, *refs):
    out_ref = refs[-1]
    rows = refs[0].shape[0]
    for place, ref in enumerate(refs[:-1]):
        out_ref[place * rows : (place + 1) * rows, :] = ref[...]


def pack_kernel(pieces, index_ref, *refs):
    high_count = pieces[0].high_count
    parts, out_refs, flat, packed = refs[:high_count], refs[high_count:-2], refs[-2], refs[-1]
    high = index_ref[0] // LOW_COUNT
    for step, part in enumerate(parts):
        flat[high ^ step] = part[...].astype(jnp.float32)
    start, target = 0, 0
    for piece in pieces:
        for block in range(piece.blocks):
            for place in range(high_count):
                packed[pl.ds(target, piece.own_rows), :] = flat[
                    place, pl.ds(start + block, piece.own_rows, stride=piece.blocks), :
                ]
                target = target + piece.own_rows
        start = start + piece.flat_rows
    count = target // len(out_refs)
    for place, out_ref in enumerate(out_refs):
        out_ref[...] = packed[place * count : (place + 1) * count, :].astype(jnp.bfloat16)


def sum_one_kernel(size, index_ref, near_ref, far_ref, to_x_ref, to_y_ref):
    total = near_ref[...].astype(jnp.float32) + far_ref[...].astype(jnp.float32)
    half = size // 2
    to_x_ref[:half, :] = total[:half].astype(jnp.bfloat16)
    if total.shape[0] > size:
        to_x_ref[half:, :] = total[size:].astype(jnp.bfloat16)
    to_y_ref[...] = total[half:size].astype(jnp.bfloat16)


def sum_three_kernel(
    size,
    index_ref,
    near_ref,
    far_ref,
    own_ref,
    beside_first_ref,
    beside_second_ref,
    across_first_ref,
    across_second_ref,
):
    half = size // 2
    outs = (beside_first_ref, beside_second_ref, across_first_ref, across_second_ref)
    total = near_ref[:size, :].astype(jnp.float32) + far_ref[:size, :].astype(jnp.float32)
    own_ref[...] = total.astype(jnp.bfloat16)
    for place, out_ref in enumerate(outs):
        rows = slice(size + place * half, size + (place + 1) * half)
        total = near_ref[rows, :].astype(jnp.float32) + far_ref[rows, :].astype(jnp.float32)
        out_ref[...] = total.astype(jnp.bfloat16)


def sum_passed_kernel(
    size,
    index_ref,
    beside_ref,
    across_ref,
    over_x_ref,
    over_y_ref,
    near_one_ref,
    far_one_ref,
    beside_out_ref,
    across_out_ref,
    extra_ref,
):
    half = size // 2
    beside = beside_ref[...].astype(jnp.float32) + over_y_ref[...].astype(jnp.float32)
    beside_out_ref[...] = beside.astype(jnp.bfloat16)
    across = across_ref[...].astype(jnp.float32) + over_x_ref[:half, :].astype(jnp.float32)
    across_out_ref[:half, :] = across.astype(jnp.bfloat16)
    if across_out_ref.shape[0] > half:
        extra = near_one_ref[size:, :].astype(jnp.float32)
        extra = extra + far_one_ref[size:, :].astype(jnp.float32)
        extra = extra + over_x_ref[half:, :].astype(jnp.float32)
        extra_ref[...] = extra
        across_out_ref[half:, :] = extra.astype(jnp.bfloat16)
    else:
        extra_ref[...] = jnp.zeros(extra_ref.shape, jnp.float32)


def unpack_kernel(
    pieces,
    index_ref,
    own_ref,
    beside_first_ref,
    beside_second_ref,
    across_first_ref,
    across_second_ref,
    extra_ref,
    *refs,
):
    high_count = pieces[0].high_count
    half = sum(piece.size for piece in pieces) // 2
    flat_rows = sum(piece.flat_rows for piece in pieces)
    outs, flat, packed = refs[:-2], refs[-2], refs[-1]
    high = index_ref[0] // LOW_COUNT
    packed[:half, :] = (
        own_ref[:half, :].astype(jnp.float32)
        + beside_first_ref[...].astype(jnp.float32)
        + across_first_ref[:half, :].astype(jnp.float32)
    )
    packed[half:, :] = (
        own_ref[half:, :].astype(jnp.float32)
        + beside_second_ref[...].astype(jnp.float32)
        + across_second_ref[...].astype(jnp.float32)
    )
    start, source = 0, 0
    for piece in pieces:
        for block in range(piece.blocks):
            for place in range(high_count):
                flat[place, pl.ds(start + block, piece.own_rows, stride=piece.blocks), :] = packed[
                    pl.ds(source, piece.own_rows), :
                ]
                source = source + piece.own_rows
        start = start + piece.flat_rows
    for step, out_ref in enumerate(outs):
        out_ref[:flat_rows, :] = flat[high ^ step].astype(out_ref.dtype)
        if out_ref.shape[0] > flat_rows:
            extra = extra_ref[...] + across_first_ref[half:, :].astype(jnp.float32)
            out_ref[flat_rows:, :] = extra.astype(out_ref.dtype)


def array(shape, kind):
    return jax.ShapeDtypeStruct(shape, kind)


def gather_high(rows, doubling):
    high_count = lax.axis_size(ALL_AXES) // LOW_COUNT
    if not doubling:
        return [rows] + [swap(rows, step * LOW_COUNT) for step in range(1, high_count)]
    parts = {0: rows}
    mask = high_count // 2
    while mask:
        parts.update({step | mask: swap(value, mask * LOW_COUNT) for step, value in parts.items()})
        mask = mask // 2
    return [parts[step] for step in range(high_count)]


def gather_own(pieces, parts, count, behind=()):
    high_count = pieces[0].high_count
    size = sum(piece.size for piece in pieces)
    return local_call(
        functools.partial(pack_kernel, pieces),
        (array((size // count, LANES), jnp.bfloat16),) * count,
        parts,
        (
            pltpu.VMEM((high_count, parts[0].shape[0], LANES), jnp.float32),
            pltpu.VMEM((size, LANES), jnp.float32),
        ),
        behind,
    )


def gather_halves(first, second):
    beside_second, across_first = swap(second, 4), swap(first, 2)
    beside_first, across_second = swap(first, 4), swap(second, 2)
    return (
        (first, second, beside_first, beside_second, across_first, across_second),
        (swap(across_first, 4), swap(beside_second, 2)),
    )


def gather_wholes(own):
    beside, across = swap(own, 4), swap(own, 2)
    return (own, beside, across), (swap(across, 4),)


def gather_cores(three, diagonal, behind=()):
    (three,) = local_call(
        join_kernel,
        (array((len(three) * three[0].shape[0], LANES), jnp.bfloat16),),
        three,
        (),
        behind,
    )
    near = (three, *diagonal)
    return near + tuple(swap(value, 1) for value in near)


def scatter_cores(far_three, far_one):
    far_one = swap(far_one, 1)
    return swap(far_three, 1), far_one


def scatter_one(pieces, near_one, far_one, behind=()):
    half = sum(piece.size for piece in pieces) // 2
    to_x, to_y = local_call(
        functools.partial(sum_one_kernel, 2 * half),
        (
            array((near_one.shape[0] - half, LANES), jnp.bfloat16),
            array((half, LANES), jnp.bfloat16),
        ),
        (near_one, far_one),
        (),
        behind,
    )
    return swap(to_x, 4), swap(to_y, 2), to_y


def scatter_three(pieces, near_three, far_three, behind=()):
    size = sum(piece.size for piece in pieces)
    half = size // 2
    own, beside_first, beside_second, across_first, across_second = local_call(
        functools.partial(sum_three_kernel, size),
        (
            array((size, LANES), jnp.bfloat16),
            *(array((half, LANES), jnp.bfloat16),) * 4,
        ),
        (near_three, far_three),
        (),
        behind,
    )
    return own, swap(beside_first, 4), beside_second, across_first, swap(across_second, 2)


def scatter_passed(pieces, threes, over_x, over_y, near_one, far_one, behind=()):
    size = sum(piece.size for piece in pieces)
    extra_count = near_one.shape[0] - size
    own, beside_first, beside_second, across_first, across_second = threes
    beside_second, across_first, extra = local_call(
        functools.partial(sum_passed_kernel, size),
        (
            array((size // 2, LANES), jnp.bfloat16),
            array((size // 2 + extra_count, LANES), jnp.bfloat16),
            array((max(extra_count, 8), LANES), jnp.float32),
        ),
        (beside_second, across_first, over_x, over_y, near_one, far_one),
        (),
        behind,
    )
    terms = (
        own,
        beside_first,
        swap(beside_second, 4),
        swap(across_first, 2),
        across_second,
        extra,
    )
    return terms, beside_second


def scatter_high(pieces, terms):
    high_count = pieces[0].high_count
    size = sum(piece.size for piece in pieces)
    flat_rows = sum(piece.flat_rows for piece in pieces)
    out_rows = flat_rows + terms[3].shape[0] - size // 2
    outs = local_call(
        functools.partial(unpack_kernel, pieces),
        (array((out_rows, LANES), jnp.float32),)
        + (array((out_rows, LANES), jnp.bfloat16),) * (high_count - 1),
        terms,
        (
            pltpu.VMEM((high_count, flat_rows, LANES), jnp.float32),
            pltpu.VMEM((size, LANES), jnp.float32),
        ),
    )
    arrived = [swap(send, step * LOW_COUNT) for step, send in enumerate(outs) if step]
    return outs[0] + sum(value.astype(jnp.float32) for value in arrived), outs[0], arrived


def norm_parts(values):
    scale = lax.rsqrt(jnp.mean(values * values, axis=-1, keepdims=True) + norm_eps)
    return scale, values * scale


def norm_back(scale, normal, upstream, weight_vec):
    weighted = upstream * (1.0 + weight_vec)
    inner = jnp.mean(weighted * normal, axis=-1, keepdims=True)
    return scale * (weighted - normal * inner), jnp.sum(normal * upstream, axis=0, keepdims=True)


def product(left_side, right_side, left_axis, right_axis):
    return lax.dot_general(
        left_side,
        right_side,
        (((left_axis,), (right_axis,)), ((), ())),
        preferred_element_type=jnp.float32,
    )


def unordered(rows_in, order_low):
    upper = rows_in.astype(jnp.bfloat16)
    lower = (rows_in - upper.astype(jnp.float32)).astype(jnp.bfloat16)
    return product(upper, order_low, 1, 1) + product(lower, order_low, 1, 1)


def weight_rows(refs, size, order, start, rows):
    count = len(refs) // 2
    three, *diagonal = refs[:count] if order < 4 else refs[count:]
    if order % 4 == 3:
        part = size // len(diagonal)
        ref, start = diagonal[start // part], start % part
    else:
        ref, start = three, order % 4 * size + start
    return ref[start : start + rows, :]


def put_rows(refs, size, order, start, rows):
    three, one = refs[:2] if order < 4 else refs[2:]
    if order % 4 == 3:
        one[start : start + rows.shape[0], :] = rows
    else:
        start = order % 4 * size + start
        three[start : start + rows.shape[0], :] = rows


def wide_tile(refs, size, start, rows):
    return jnp.concatenate(
        [weight_rows(refs, size, order, start, rows) for order in range(LOW_COUNT)]
    )


def put_wide_tile(refs, size, start, rows, tile):
    for order in range(LOW_COUNT):
        put_rows(refs, size, order, start, tile[order * rows : (order + 1) * rows])


def tall_rows(piece, low):
    for order, mask in enumerate(LOW_MASKS):
        for block in range(piece.blocks):
            for place in range(piece.high_count):
                row = (place * LOW_COUNT + (low ^ mask)) * piece.own_rows
                yield (
                    order,
                    block * piece.block_rows + place * piece.own_rows,
                    pl.ds(pl.multiple_of(row, piece.own_rows), piece.own_rows),
                    slice(block * LANES, (block + 1) * LANES),
                )


def ffn_kernel(
    gate_piece,
    down_piece,
    index_ref,
    middle_ref,
    cotangent_ref,
    gain_in_ref,
    gain_out_ref,
    order_ref,
    *refs,
):
    weight_refs, grad_refs = refs[:6], refs[10:14]
    block_out_ref, grad_middle_ref, grad_gain_in_ref, grad_gain_out_ref = refs[6:10]
    down_ref, hidden_ref, gelu_ref, slope_ref = refs[14:]
    low = index_ref[0] % LOW_COUNT
    rows = gate_piece.block_rows
    size = 2 * gate_piece.size + down_piece.size
    width = 2 * LANES
    for order, start, matrix_rows, columns in tall_rows(down_piece, low):
        start = start + 2 * gate_piece.size
        down_ref[matrix_rows, columns] = weight_rows(
            weight_refs, size, order, start, down_piece.own_rows
        )

    def wide_tiles(step):
        return [
            jnp.concatenate(
                [
                    wide_tile(weight_refs, size, offset + block * rows, rows)
                    for block in (2 * step, 2 * step + 1)
                ],
                axis=1,
            )
            for offset in (0, gate_piece.size)
        ]

    middle = middle_ref[...]
    scale_in, normal_in = norm_parts(middle)
    order_low = order_ref[...]
    normed = (normal_in * (1.0 + gain_in_ref[...])).astype(jnp.bfloat16)
    normed = product(normed, order_low, 1, 0).astype(jnp.bfloat16)
    for step in range(FF // width):
        columns = slice(step * width, (step + 1) * width)
        gate_weight, up_weight = wide_tiles(step)
        gate = product(normed, gate_weight, 1, 0)
        up = product(normed, up_weight, 1, 0)
        square = gate * gate
        bend = jnp.tanh(GELU_SCALE * gate * (1.0 + GELU_CUBE * square))
        half = 0.5 * (1.0 + bend)
        gelu = gate * half
        slope = half + 0.5 * gate * (1.0 - bend * bend) * GELU_SCALE * (
            1.0 + 3.0 * GELU_CUBE * square
        )
        gelu_ref[:, columns] = gelu
        slope_ref[:, columns] = slope * up
        hidden_ref[:, columns] = (gelu * up).astype(jnp.bfloat16)
    hidden = hidden_ref[...]
    scale_out, normal_out = norm_parts(product(hidden, down_ref[...], 1, 0))
    block_out_ref[...] = (middle + normal_out * (1.0 + gain_out_ref[...])).astype(jnp.bfloat16)
    upstream = cotangent_ref[...].astype(jnp.float32)
    grad_ffn, grad_gain_out_ref[...] = norm_back(
        scale_out, normal_out, upstream, gain_out_ref[...]
    )
    grad_ffn = grad_ffn.astype(jnp.bfloat16)
    grad_normed = jnp.zeros(middle.shape, jnp.float32)
    for step in range(FF // width):
        columns = slice(step * width, (step + 1) * width)
        grad_hidden = product(grad_ffn, down_ref[columns, :], 1, 1)
        down_ref[columns, :] = product(hidden_ref[:, columns], grad_ffn, 0, 0).astype(jnp.bfloat16)
        grads = [
            (grad_hidden * slope_ref[:, columns]).astype(jnp.bfloat16),
            (grad_hidden * gelu_ref[:, columns]).astype(jnp.bfloat16),
        ]
        for place, (grad, weight) in enumerate(zip(grads, wide_tiles(step))):
            grad_weight = product(normed, grad, 0, 0).astype(jnp.bfloat16)
            for side in range(2):
                put_wide_tile(
                    grad_refs,
                    size,
                    place * gate_piece.size + (2 * step + side) * rows,
                    rows,
                    grad_weight[:, side * LANES : (side + 1) * LANES],
                )
            grad_normed = grad_normed + product(grad, weight, 1, 1)
    for order, start, matrix_rows, columns in tall_rows(down_piece, low):
        start = start + 2 * gate_piece.size
        put_rows(grad_refs, size, order, start, down_ref[matrix_rows, columns])
    grad_middle, grad_gain_in_ref[...] = norm_back(
        scale_in, normal_in, unordered(grad_normed, order_low), gain_in_ref[...]
    )
    grad_middle_ref[...] = upstream + grad_middle


def grad_arrays(pieces, extra_count=0):
    size = sum(piece.size for piece in pieces)
    return (
        array((3 * size, LANES), jnp.bfloat16),
        array((size + extra_count, LANES), jnp.bfloat16),
    ) * 2


def ffn_blocks(pieces, middle, cotangent, gain_in, gain_out, order, blocks):
    rows = middle.shape[0]
    outs = local_call(
        functools.partial(ffn_kernel, pieces[4], pieces[6]),
        (
            array((rows, D), jnp.bfloat16),
            array((rows, D), jnp.float32),
            array((1, D), jnp.float32),
            array((1, D), jnp.float32),
            *grad_arrays(pieces[4:7]),
        ),
        (middle, cotangent, gain_in, gain_out, order, *blocks),
        (
            pltpu.VMEM((FF, D), jnp.bfloat16),
            pltpu.VMEM((rows, FF), jnp.bfloat16),
            pltpu.VMEM((rows, FF), jnp.float32),
            pltpu.VMEM((rows, FF), jnp.float32),
        ),
    )
    return *outs[:4], outs[4:]


def turn(values, cosine, sine):
    first_half, second_half = values[:, : HD // 2], values[:, HD // 2 :]
    return jnp.concatenate(
        [first_half * cosine - second_half * sine, second_half * cosine + first_half * sine], axis=1
    )


def wide_head(refs, size, start, rows):
    return jnp.concatenate(
        [wide_tile(refs, size, start + side * rows, rows) for side in range(2)], axis=1
    )


def head_starts(pieces):
    rows = pieces[0].block_rows
    return [2 * rows * head for head in range(HQ + 2)]


def project_kernel(
    pieces,
    index_ref,
    tokens_ref,
    gain_ref,
    gain_query_ref,
    gain_key_ref,
    cosine_ref,
    sine_ref,
    order_ref,
    *refs,
):
    weight_refs = refs[:4]
    normed_ref, query_proj_ref, key_proj_ref, query_ref, key_value_ref = refs[4:]
    size = sum(piece.size for piece in pieces)
    rows = pieces[0].block_rows
    cosine, sine = cosine_ref[...], sine_ref[...]
    _, normal = norm_parts(tokens_ref[...].astype(jnp.float32))
    normed = (normal * (1.0 + gain_ref[...])).astype(jnp.bfloat16)
    normed = product(normed, order_ref[...], 1, 0).astype(jnp.bfloat16)
    normed_ref[...] = normed
    starts = head_starts(pieces)
    for head, start in enumerate(starts):
        proj = product(normed, wide_head(weight_refs, size, start, rows), 1, 0)
        columns = slice(head * HD, (head + 1) * HD)
        if head == HQ + 1:
            key_value_ref[:, HD:] = proj.astype(jnp.bfloat16)
            continue
        gain_vec = gain_query_ref[...] if head < HQ else gain_key_ref[...]
        _, normal = norm_parts(proj)
        turned = turn(normal * (1.0 + gain_vec), cosine, sine).astype(jnp.bfloat16)
        if head < HQ:
            query_proj_ref[:, columns] = proj
            query_ref[:, columns] = turned
        else:
            key_proj_ref[...] = proj
            key_value_ref[:, :HD] = turned


def attend_kernel(
    pieces,
    index_ref,
    tokens_ref,
    gain_ref,
    allowed_ref,
    query_ref,
    *refs,
):
    weight_refs, key_value_refs = refs[:4], refs[4:-5]
    probs_ref, attended_ref, attn_out_ref, middle_ref, out_weight_ref = refs[-5:]
    out_piece = pieces[-1]
    low = index_ref[0] % LOW_COUNT
    size = sum(piece.size for piece in pieces)
    out_start = size - out_piece.size
    for order, start, matrix_rows, columns in tall_rows(out_piece, low):
        out_weight_ref[matrix_rows, columns] = weight_rows(
            weight_refs, size, order, start + out_start, out_piece.own_rows
        )
    rows = tokens_ref.shape[0]
    allowed = allowed_ref[...] > 0.0
    keys = jnp.concatenate([ref[:, :HD] for ref in key_value_refs])
    values = jnp.concatenate([ref[:, HD:] for ref in key_value_refs])
    count = keys.shape[0]
    for head in range(HQ):
        columns = slice(head * HD, (head + 1) * HD)
        scores = product(query_ref[:, columns], keys, 1, 1) * HD ** (-0.5)
        scores = jnp.where(allowed, scores, -1e30)
        raised = jnp.exp(scores - jnp.max(scores, axis=-1, keepdims=True))
        probs = raised / jnp.sum(raised, axis=-1, keepdims=True)
        probs_ref[:, head * count : (head + 1) * count] = probs
        attended_ref[:, columns] = product(probs.astype(jnp.bfloat16), values, 1, 0).astype(
            jnp.bfloat16
        )
    attn_out = product(attended_ref[...], out_weight_ref[...], 1, 0)
    attn_out_ref[...] = attn_out
    _, normal = norm_parts(attn_out)
    middle_ref[...] = tokens_ref[...].astype(jnp.float32) + normal * (1.0 + gain_ref[...])


def attend_back_kernel(
    index_ref,
    grad_middle_ref,
    attn_out_ref,
    gain_ref,
    out_weight_ref,
    attended_ref,
    probs_ref,
    query_ref,
    *refs,
):
    part_count = (len(refs) - 3) // 2
    key_value_refs = refs[:part_count]
    grad_out_weight_ref, grad_query_ref, grad_gain_ref = refs[part_count : part_count + 3]
    grad_key_value_refs = refs[part_count + 3 :]
    rows = query_ref.shape[0]
    scale, normal = norm_parts(attn_out_ref[...])
    grad_attn, grad_gain_ref[...] = norm_back(scale, normal, grad_middle_ref[...], gain_ref[...])
    grad_attn = grad_attn.astype(jnp.bfloat16)
    grad_out_weight_ref[...] = product(attended_ref[...], grad_attn, 0, 0).astype(jnp.bfloat16)
    keys = jnp.concatenate([ref[:, :HD] for ref in key_value_refs])
    values = jnp.concatenate([ref[:, HD:] for ref in key_value_refs])
    count = keys.shape[0]
    grad_keys = jnp.zeros((count, HD), jnp.float32)
    grad_values = jnp.zeros((count, HD), jnp.float32)
    for head in range(HQ):
        columns = slice(head * HD, (head + 1) * HD)
        grad_attended = product(grad_attn, out_weight_ref[columns, :], 1, 1).astype(jnp.bfloat16)
        probs = probs_ref[:, head * count : (head + 1) * count]
        grad_probs = product(grad_attended, values, 1, 1)
        grad_values = grad_values + product(probs.astype(jnp.bfloat16), grad_attended, 0, 0)
        inner = jnp.sum(probs * grad_probs, axis=-1, keepdims=True)
        grad_scores = (probs * (grad_probs - inner) * HD ** (-0.5)).astype(jnp.bfloat16)
        grad_query_ref[:, columns] = product(grad_scores, keys, 1, 0)
        grad_keys = grad_keys + product(grad_scores, query_ref[:, columns], 0, 0)
    for part, ref in enumerate(grad_key_value_refs):
        ref[:, :HD] = grad_keys[part * rows : (part + 1) * rows].astype(ref.dtype)
        ref[:, HD:] = grad_values[part * rows : (part + 1) * rows].astype(ref.dtype)


def query_back_kernel(
    pieces,
    index_ref,
    gain_ref,
    cosine_ref,
    sine_ref,
    normed_ref,
    query_proj_ref,
    grad_query_ref,
    *refs,
):
    weight_refs = refs[:4]
    grad_weight_ref, grad_normed_ref, grad_gain_ref = refs[4:]
    size = sum(piece.size for piece in pieces)
    rows = pieces[0].block_rows
    cosine, sine = cosine_ref[...], sine_ref[...]
    normed = normed_ref[...]
    grad_normed = jnp.zeros(grad_normed_ref.shape, jnp.float32)
    grad_gain = jnp.zeros((1, HD), jnp.float32)
    for head, start in enumerate(head_starts(pieces)[:HQ]):
        columns = slice(head * HD, (head + 1) * HD)
        scale, normal = norm_parts(query_proj_ref[:, columns])
        upstream = turn(grad_query_ref[:, columns], cosine, -sine)
        grad, gain_row = norm_back(scale, normal, upstream, gain_ref[...])
        grad_gain = grad_gain + gain_row
        grad = grad.astype(jnp.bfloat16)
        weight = wide_head(weight_refs, size, start, rows)
        grad_normed = grad_normed + product(grad, weight, 1, 1)
        grad_weight_ref[:, columns] = product(normed, grad, 0, 0).astype(jnp.bfloat16)
    grad_normed_ref[...] = grad_normed
    grad_gain_ref[...] = grad_gain


def project_back_kernel(
    pieces,
    index_ref,
    tokens_ref,
    gain_ref,
    gain_key_ref,
    cosine_ref,
    sine_ref,
    order_ref,
    normed_ref,
    key_proj_ref,
    grad_query_weight_ref,
    grad_normed_ref,
    grad_middle_ref,
    grad_out_weight_ref,
    gain_attn_ref,
    gain_ffin_ref,
    gain_ffout_ref,
    gain_query_ref,
    *refs,
):
    weight_refs, key_value_refs, grad_refs = refs[:4], refs[4:-6], refs[-6:-2]
    input_grad_ref, grad_gain_ref = refs[-2:]
    low = index_ref[0] % LOW_COUNT
    size = sum(piece.size for piece in pieces)
    rows = pieces[0].block_rows
    normed = normed_ref[...]
    key_value = sum(ref[...].astype(jnp.float32) for ref in key_value_refs)
    scale, normal = norm_parts(key_proj_ref[...])
    upstream = turn(key_value[:, :HD], cosine_ref[...], -sine_ref[...])
    grad_key, grad_gain_key = norm_back(scale, normal, upstream, gain_key_ref[...])
    grad_normed = grad_normed_ref[...]
    for head, start in enumerate(head_starts(pieces)):
        if head < HQ:
            grad_weight = grad_query_weight_ref[:, head * HD : (head + 1) * HD]
        else:
            grad = (grad_key if head == HQ else key_value[:, HD:]).astype(jnp.bfloat16)
            weight = wide_head(weight_refs, size, start, rows)
            grad_normed = grad_normed + product(grad, weight, 1, 1)
            grad_weight = product(normed, grad, 0, 0).astype(jnp.bfloat16)
        for side in range(2):
            put_wide_tile(
                grad_refs,
                size,
                start + side * rows,
                rows,
                grad_weight[:, side * LANES : (side + 1) * LANES],
            )
    out_piece = pieces[-1]
    for order, start, matrix_rows, columns in tall_rows(out_piece, low):
        start = start + size - out_piece.size
        put_rows(grad_refs, size, order, start, grad_out_weight_ref[matrix_rows, columns])
    scale, normal = norm_parts(tokens_ref[...].astype(jnp.float32))
    grad_inputs, grad_gain_input = norm_back(
        scale, normal, unordered(grad_normed, order_ref[...]), gain_ref[...]
    )
    input_grad_ref[...] = (grad_middle_ref[...] + grad_inputs).astype(jnp.bfloat16)
    grad_gains = [
        grad_gain_input,
        gain_attn_ref[...],
        gain_ffin_ref[...],
        gain_ffout_ref[...],
        gain_query_ref[...],
        grad_gain_key,
    ]
    row = 0
    grad_gain_ref[...] = jnp.zeros(grad_gain_ref.shape, jnp.float32)
    for values in grad_gains:
        for start in range(0, values.shape[1], LANES):
            grad_gain_ref[row : row + 1, :] = values[:, start : start + LANES]
            row = row + 1
    for target in (grad_refs[1], grad_refs[3]):
        target[size:, :] = grad_gain_ref[...].astype(jnp.bfloat16)


def width_order(device_count):
    low = lax.axis_index(ALL_AXES) % LOW_COUNT
    rows = D // device_count
    high_count = device_count // LOW_COUNT
    column = jnp.arange(D, dtype=jnp.int32)
    place = column // (rows * high_count)
    mask = (place & 1) * 4 + ((place >> 1) & 1) * 2 + (place >> 2)
    high = (column // rows) % high_count
    picked = (high * LOW_COUNT + (low ^ mask)) * rows + column % rows
    return (jnp.arange(D, dtype=jnp.int32)[:, None] == picked[None, :]).astype(jnp.bfloat16)


GAIN_ROWS = 32


def shards_blocks(
    device_count,
    tokens,
    doc_ids,
    cotangent,
    master,
    first_moment,
    second_moment,
    gains,
    gain_first,
    gain_second,
):
    pieces = [Piece(*shape_pair, device_count) for shape_pair in piece_shapes()]
    attention_pieces = pieces[:4]
    local_rows = tokens.shape[0]
    group_size = lax.axis_size("group")
    first_row = lax.axis_index("group") * local_rows
    attention_rows = sum(piece.flat_rows for piece in attention_pieces)
    ffn_pieces = pieces[4:7]
    rounded = master.astype(jnp.bfloat16)
    attention_parts = gather_high(rounded[:attention_rows], False)
    ffn_rows = rounded[attention_rows:]
    ffn_parts = gather_high(ffn_rows, True)
    attention_near = gather_wholes(*gather_own(attention_pieces, attention_parts, 1))
    attention_blocks = gather_cores(*attention_near)
    ffn_near = gather_halves(
        *gather_own(ffn_pieces, ffn_parts, 2, (attention_blocks[0], *attention_near[1]))
    )
    gain_parts = []
    for start, width in ((0, D), (D, D), (2 * D, D), (3 * D, D), (4 * D, HD), (4 * D + HD, HD)):
        gain_parts.append(gains[start : start + width][None])
    gain_input, gain_attn, gain_ffin, gain_ffout, gain_query, gain_key = gain_parts
    order = width_order(device_count)
    doc_row = doc_ids[0]
    angles = lax.dynamic_slice_in_dim(angles_of(positions(doc_row)), first_row, local_rows, 0)
    cosine, sine = jnp.cos(angles), jnp.sin(angles)
    query_docs = lax.dynamic_slice_in_dim(doc_row, first_row, local_rows, 0)
    reach = min(-(-(WINDOW - 1) // local_rows), group_size - 1)
    key_count = (reach + 1) * local_rows
    doc_pad = jnp.concatenate([jnp.full((reach * local_rows,), -1, jnp.int32), doc_row])
    key_docs = lax.dynamic_slice_in_dim(doc_pad, first_row, key_count, 0)
    key_index = first_row - reach * local_rows + jnp.arange(key_count, dtype=jnp.int32)
    query_index = first_row + jnp.arange(local_rows, dtype=jnp.int32)
    distance = query_index[:, None] - key_index[None, :]
    allowed = (distance >= 0) & (distance < WINDOW) & (key_docs[None, :] == query_docs[:, None])
    allowed = allowed.astype(jnp.float32)

    width = HQ * HD
    normed, query_proj, key_proj, query_rot, key_value = local_call(
        functools.partial(project_kernel, attention_pieces),
        (
            array((local_rows, D), jnp.bfloat16),
            array((local_rows, width), jnp.float32),
            array((local_rows, HD), jnp.float32),
            array((local_rows, width), jnp.bfloat16),
            array((local_rows, 2 * HD), jnp.bfloat16),
        ),
        (tokens, gain_input, gain_query, gain_key, cosine, sine, order, *attention_blocks),
    )
    key_values = [shifted(key_value, "group", offset) for offset in range(reach, 0, -1)]
    ffn_weights = gather_cores(*ffn_near, key_values)
    key_values.append(key_value)
    probs, attended, attn_out, middle, out_weight = local_call(
        functools.partial(attend_kernel, attention_pieces),
        (
            array((local_rows, HQ * key_count), jnp.float32),
            array((local_rows, width), jnp.bfloat16),
            array((local_rows, D), jnp.float32),
            array((local_rows, D), jnp.float32),
            array((width, D), jnp.bfloat16),
        ),
        (tokens, gain_attn, allowed, query_rot, *attention_blocks, *key_values),
        (),
        (ffn_weights[0],),
    )
    outputs, grad_middle, grad_gain_ffin, grad_gain_ffout, grads_ffn = ffn_blocks(
        pieces, middle, cotangent, gain_ffin, gain_ffout, order, ffn_weights
    )
    near_three, near_one, far_three, far_one = grads_ffn
    far_three, far_one = scatter_cores(far_three, far_one)
    grad_out_weight, grad_query, grad_gain_attn, *grad_key_values = local_call(
        attend_back_kernel,
        (
            array((width, D), jnp.bfloat16),
            array((local_rows, width), jnp.float32),
            array((1, D), jnp.float32),
            *(array((local_rows, 2 * HD), jnp.bfloat16),) * reach,
            array((local_rows, 2 * HD), jnp.float32),
        ),
        (
            grad_middle,
            attn_out,
            gain_attn,
            out_weight,
            attended,
            probs,
            query_rot,
            *key_values,
        ),
    )
    grad_key_values = [
        shifted(value, "group", place - reach) if place < reach else value
        for place, value in enumerate(grad_key_values)
    ]
    over_x, over_y, sent = scatter_one(ffn_pieces, near_one, far_one, grad_key_values[:-1])
    threes = scatter_three(ffn_pieces, near_three, far_three, (sent,))
    grad_query_weight, grad_normed, grad_gain_query = local_call(
        functools.partial(query_back_kernel, attention_pieces),
        (
            array((D, width), jnp.bfloat16),
            array((local_rows, D), jnp.float32),
            array((1, HD), jnp.float32),
        ),
        (gain_query, cosine, sine, normed, query_proj, grad_query, *attention_blocks),
        (),
        (threes[0],),
    )
    *grads_attention, grad_inputs, _ = local_call(
        functools.partial(project_back_kernel, attention_pieces),
        (
            *grad_arrays(attention_pieces, GAIN_ROWS),
            array((local_rows, D), jnp.bfloat16),
            array((GAIN_ROWS, LANES), jnp.float32),
        ),
        (
            tokens,
            gain_input,
            gain_key,
            cosine,
            sine,
            order,
            normed,
            key_proj,
            grad_query_weight,
            grad_normed,
            grad_middle,
            grad_out_weight,
            grad_gain_attn,
            grad_gain_ffin,
            grad_gain_ffout,
            grad_gain_query,
            *attention_blocks,
            *grad_key_values,
        ),
        (),
        (over_x, over_y),
    )
    ffn_terms, _ = scatter_passed(
        ffn_pieces,
        threes,
        over_x,
        over_y,
        near_one,
        far_one,
        (grad_inputs, threes[1], threes[4]),
    )
    near_three, near_one, far_three, far_one = grads_attention
    far_three, far_one = scatter_cores(far_three, far_one)
    grads_ffn, sent, arrived = scatter_high(ffn_pieces, ffn_terms)
    over_x, over_y, sent = scatter_one(attention_pieces, near_one, far_one, (sent,))
    threes = scatter_three(attention_pieces, near_three, far_three, (sent, arrived[0]))
    terms, _ = scatter_passed(attention_pieces, threes, over_x, over_y, near_one, far_one)
    grads_attention, _, _ = scatter_high(attention_pieces, terms)
    gain_grads = grads_attention[attention_rows:].reshape(-1)[: gains.shape[0]]
    grads_local = jnp.concatenate([grads_attention[:attention_rows], grads_ffn])
    return (
        outputs,
        grad_inputs,
        *adam_update(grads_local, first_moment, second_moment, master, learn_rate, weight_decay),
        *adam_update(gain_grads, gain_first, gain_second, gains, gain_rate, 0.0),
    )


def shards(
    tokens, doc_ids, cotangent, master, first_moment, second_moment, gains, gain_first, gain_second
):
    group_size = lax.axis_size("group")
    devices_all = lax.axis_size("dp") * group_size
    if aligned(devices_all):
        return shards_blocks(
            devices_all,
            tokens,
            doc_ids,
            cotangent,
            master,
            first_moment,
            second_moment,
            gains,
            gain_first,
            gain_second,
        )
    group_index = lax.axis_index("group")
    local_rows = tokens.shape[0]
    shard_parts = [
        part_rows.astype(jnp.bfloat16) for part_rows in split_rows(master, piece_rows(devices_all))
    ]
    gathered = (
        lax.all_gather(shard_parts[0], ("dp", "group"), axis=0, tiled=True),
        lax.all_gather(shard_parts[1], ("dp", "group"), axis=0, tiled=True),
        lax.all_gather(shard_parts[2], ("dp", "group"), axis=0, tiled=True),
        lax.all_gather(shard_parts[3], ("dp", "group"), axis=0, tiled=True),
        lax.all_gather(shard_parts[4], ("dp", "group"), axis=0, tiled=True),
        lax.all_gather(shard_parts[5], ("dp", "group"), axis=0, tiled=True),
        lax.all_gather(shard_parts[6], ("dp", "group"), axis=0, tiled=True),
    )
    query_weight, key_weight, value_weight, out_weight, gate_weight, up_weight, down_weight = [
        full_rows.reshape(shape_pair) for full_rows, shape_pair in zip(gathered, piece_shapes())
    ]
    norm_input = gains[0:D]
    norm_attn = gains[D : 2 * D]
    norm_ffin = gains[2 * D : 3 * D]
    norm_ffout = gains[3 * D : 4 * D]
    norm_query = gains[4 * D : 4 * D + HD]
    norm_key = gains[4 * D + HD : 4 * D + 2 * HD]
    doc_row = doc_ids[0]
    first_row = group_index * local_rows
    angles = lax.dynamic_slice_in_dim(angles_of(positions(doc_row)), first_row, local_rows, 0)
    query_docs = lax.dynamic_slice_in_dim(doc_row, first_row, local_rows, 0)
    inputs = tokens.astype(jnp.float32)
    normed, back_input = jax.vjp(rms_norm, inputs, norm_input)
    normed_low = normed.astype(jnp.bfloat16)
    query_proj = matmul(normed_low, query_weight)
    key_proj = matmul(normed_low, key_weight)
    value_proj = matmul(normed_low, value_weight)

    def query_prep(flat_rows, gain_vec):
        return rotate(rms_norm(flat_rows.reshape(local_rows, HQ, HD), gain_vec), angles[:, None, :])

    def key_prep(rows_in, gain_vec):
        return rotate(rms_norm(rows_in, gain_vec), angles)

    query_rot, back_query = jax.vjp(query_prep, query_proj, norm_query)
    key_rot, back_key = jax.vjp(key_prep, key_proj, norm_key)
    query_low = query_rot.astype(jnp.bfloat16)
    key_low = key_rot.astype(jnp.bfloat16)
    value_low = value_proj.astype(jnp.bfloat16)
    reach = min(-(-(WINDOW - 1) // local_rows), group_size - 1)
    key_list = [key_low]
    value_list = [value_low]
    for offset in range(1, reach + 1):
        key_far, value_far = shifted((key_low, value_low), "group", offset)
        key_list.insert(0, key_far)
        value_list.insert(0, value_far)
    key_all = jnp.concatenate(key_list, axis=0)
    value_all = jnp.concatenate(value_list, axis=0)
    key_count = (reach + 1) * local_rows
    doc_pad = jnp.concatenate([jnp.full((reach * local_rows,), -1, jnp.int32), doc_row])
    key_docs = lax.dynamic_slice_in_dim(doc_pad, first_row, key_count, 0)
    key_index = (group_index - reach) * local_rows + jnp.arange(key_count, dtype=jnp.int32)
    query_index = first_row + jnp.arange(local_rows, dtype=jnp.int32)
    distance = query_index[:, None] - key_index[None, :]
    allowed = (distance >= 0) & (distance < WINDOW) & (key_docs[None, :] == query_docs[:, None])

    def scores_of(key_rows_low):
        raw_scores = jnp.einsum(
            "qhd,kd->hqk", query_low, key_rows_low, preferred_element_type=jnp.float32
        ) * HD ** (-0.5)
        return jnp.where(allowed[None], raw_scores, -1e30)

    masked = scores_of(key_all)
    top_score = jnp.max(masked, axis=-1, keepdims=True)
    log_total = top_score + jnp.log(jnp.sum(jnp.exp(masked - top_score), axis=-1, keepdims=True))
    probs = jnp.exp(masked - log_total)
    attended = jnp.einsum(
        "hqk,kd->qhd", probs.astype(jnp.bfloat16), value_all, preferred_element_type=jnp.float32
    )
    attended_low = attended.reshape(local_rows, HQ * HD).astype(jnp.bfloat16)
    attn_out = matmul(attended_low, out_weight)
    branch_one, back_attn = jax.vjp(rms_norm, attn_out, norm_attn)
    middle = inputs + branch_one
    normed_two, back_ffin = jax.vjp(rms_norm, middle, norm_ffin)
    normed_two_low = normed_two.astype(jnp.bfloat16)
    gate_proj = matmul(normed_two_low, gate_weight)
    up_proj = matmul(normed_two_low, up_weight)
    hidden, back_hidden = jax.vjp(geglu, gate_proj, up_proj)
    hidden_low = hidden.astype(jnp.bfloat16)
    ffn_out = matmul(hidden_low, down_weight)
    branch_two, back_ffout = jax.vjp(rms_norm, ffn_out, norm_ffout)
    outputs = middle + branch_two
    grad_out = cotangent.astype(jnp.float32)
    grad_ffn, grad_gain_ffout = back_ffout(grad_out)
    grad_ffn_low = grad_ffn.astype(jnp.bfloat16)
    grad_down_w = jnp.einsum(
        "tf,td->fd", hidden_low, grad_ffn_low, preferred_element_type=jnp.float32
    )
    grad_hidden = jnp.einsum(
        "td,fd->tf", grad_ffn_low, down_weight, preferred_element_type=jnp.float32
    )
    grad_gate, grad_up = back_hidden(grad_hidden)
    grad_gate_low = grad_gate.astype(jnp.bfloat16)
    grad_up_low = grad_up.astype(jnp.bfloat16)
    grad_gate_w = jnp.einsum(
        "td,tf->df", normed_two_low, grad_gate_low, preferred_element_type=jnp.float32
    )
    grad_up_w = jnp.einsum(
        "td,tf->df", normed_two_low, grad_up_low, preferred_element_type=jnp.float32
    )
    grad_normed_two = jnp.einsum(
        "tf,df->td", grad_gate_low, gate_weight, preferred_element_type=jnp.float32
    ) + jnp.einsum("tf,df->td", grad_up_low, up_weight, preferred_element_type=jnp.float32)
    grad_middle_norm, grad_gain_ffin = back_ffin(grad_normed_two)
    grad_middle = grad_out + grad_middle_norm
    grad_attn, grad_gain_attn = back_attn(grad_middle)
    grad_attn_low = grad_attn.astype(jnp.bfloat16)
    grad_out_w = jnp.einsum(
        "to,td->od", attended_low, grad_attn_low, preferred_element_type=jnp.float32
    )
    grad_attended = jnp.einsum(
        "td,od->to", grad_attn_low, out_weight, preferred_element_type=jnp.float32
    )
    grad_attended_low = grad_attended.astype(jnp.bfloat16).reshape(local_rows, HQ, HD)
    probs_again = jnp.exp(scores_of(key_all) - log_total)
    grad_probs = jnp.einsum(
        "qhd,kd->hqk", grad_attended_low, value_all, preferred_element_type=jnp.float32
    )
    grad_value_all = jnp.einsum(
        "hqk,qhd->kd",
        probs_again.astype(jnp.bfloat16),
        grad_attended_low,
        preferred_element_type=jnp.float32,
    )
    grad_scores = probs_again * (
        grad_probs - jnp.sum(probs_again * grad_probs, axis=-1, keepdims=True)
    )
    grad_scores_low = (grad_scores * HD ** (-0.5)).astype(jnp.bfloat16)
    grad_query = jnp.einsum(
        "hqk,kd->qhd", grad_scores_low, key_all, preferred_element_type=jnp.float32
    )
    grad_key_all = jnp.einsum(
        "hqk,qhd->kd", grad_scores_low, query_low, preferred_element_type=jnp.float32
    )
    key_total = grad_key_all[reach * local_rows :]
    value_total = grad_value_all[reach * local_rows :]
    for offset in range(1, reach + 1):
        row_start = (reach - offset) * local_rows
        key_back, value_back = (
            shifted(
                grad_key_all[row_start : row_start + local_rows].astype(jnp.bfloat16),
                "group",
                -offset,
            ).astype(jnp.float32),
            shifted(
                grad_value_all[row_start : row_start + local_rows].astype(jnp.bfloat16),
                "group",
                -offset,
            ).astype(jnp.float32),
        )
        key_total = key_total + key_back
        value_total = value_total + value_back
    grad_query_proj, grad_gain_query = back_query(grad_query)
    grad_key_proj, grad_gain_key = back_key(key_total)
    grad_query_low = grad_query_proj.astype(jnp.bfloat16)
    grad_key_low = grad_key_proj.astype(jnp.bfloat16)
    grad_value_low = value_total.astype(jnp.bfloat16)
    grad_query_w = jnp.einsum(
        "td,te->de", normed_low, grad_query_low, preferred_element_type=jnp.float32
    )
    grad_key_w = jnp.einsum(
        "td,te->de", normed_low, grad_key_low, preferred_element_type=jnp.float32
    )
    grad_value_w = jnp.einsum(
        "td,te->de", normed_low, grad_value_low, preferred_element_type=jnp.float32
    )
    grad_normed = jnp.einsum(
        "te,de->td", grad_query_low, query_weight, preferred_element_type=jnp.float32
    )
    grad_normed = grad_normed + jnp.einsum(
        "te,de->td", grad_key_low, key_weight, preferred_element_type=jnp.float32
    )
    grad_normed = grad_normed + jnp.einsum(
        "te,de->td", grad_value_low, value_weight, preferred_element_type=jnp.float32
    )
    grad_input_norm, grad_gain_input = back_input(grad_normed)
    grad_inputs = grad_middle + grad_input_norm
    flat_query = grad_query_w.reshape(-1, 128)
    flat_key = grad_key_w.reshape(-1, 128)
    flat_value = grad_value_w.reshape(-1, 128)
    flat_out = grad_out_w.reshape(-1, 128)
    flat_gate = grad_gate_w.reshape(-1, 128)
    flat_up = grad_up_w.reshape(-1, 128)
    flat_down = grad_down_w.reshape(-1, 128)
    reduced = (
        lax.psum_scatter(flat_query, ("dp", "group"), scatter_dimension=0, tiled=True),
        lax.psum_scatter(flat_key, ("dp", "group"), scatter_dimension=0, tiled=True),
        lax.psum_scatter(flat_value, ("dp", "group"), scatter_dimension=0, tiled=True),
        lax.psum_scatter(flat_out, ("dp", "group"), scatter_dimension=0, tiled=True),
        lax.psum_scatter(flat_gate, ("dp", "group"), scatter_dimension=0, tiled=True),
        lax.psum_scatter(flat_up, ("dp", "group"), scatter_dimension=0, tiled=True),
        lax.psum_scatter(flat_down, ("dp", "group"), scatter_dimension=0, tiled=True),
    )
    grads_local = jnp.concatenate(list(reduced), axis=0)
    gain_grads = lax.psum(
        jnp.concatenate(
            [
                grad_gain_input,
                grad_gain_attn,
                grad_gain_ffin,
                grad_gain_ffout,
                grad_gain_query,
                grad_gain_key,
            ]
        ),
        ("dp", "group"),
    )
    moment_first, moment_second, master_new = adam_update(
        grads_local, first_moment, second_moment, master, learn_rate, weight_decay
    )
    gain_moment_first, gain_moment_second, gains_new = adam_update(
        gain_grads, gain_first, gain_second, gains, gain_rate, 0.0
    )
    return (
        outputs.astype(jnp.bfloat16),
        grad_inputs.astype(jnp.bfloat16),
        moment_first,
        moment_second,
        master_new,
        gain_moment_first,
        gain_moment_second,
        gains_new,
    )


def solution(mesh):
    placed = (
        P(("dp", "group"), None),
        P("dp", None),
        P(("dp", "group"), None),
        P(("dp", "group"), None),
        P(("dp", "group"), None),
        P(("dp", "group"), None),
        P(),
        P(),
        P(),
    )
    return jax.shard_map(
        shards,
        mesh=mesh,
        in_specs=placed,
        out_specs=(
            P(("dp", "group"), None),
            P(("dp", "group"), None),
            P(("dp", "group"), None),
            P(("dp", "group"), None),
            P(("dp", "group"), None),
            P(),
            P(),
            P(),
        ),
        check_vma=False,
    )
```

```python
import functools
import math

import jax
import jax.numpy as jnp
from jax import lax
from jax.experimental import pallas as pl
from jax.experimental.pallas import tpu as pltpu
from jax.sharding import PartitionSpec as P

D = 640
HQ = 4
HD = 256
FF = 2048
WINDOW = 512
STEP = 10
ALL_AXES = ("dp", "group")


norm_eps = 1e-06
rope_base = 10000.0
beta_first = 0.9
beta_second = 0.999
learn_rate = 0.05
gain_rate = 0.25
adam_floor = 1e-08
weight_decay = 0.1


def shifted(value, axis, steps):
    count = lax.axis_size(axis)
    initial, last = (max(0, -steps), min(count, count - steps))
    return lax.ppermute(value, axis, [(source, source + steps) for source in range(initial, last)])


def rms_norm(values, weight_vec):
    return (
        values
        * lax.rsqrt(jnp.mean(values * values, axis=-1, keepdims=True) + norm_eps)
        * (1.0 + weight_vec)
    )


def positions(doc_row):
    length = doc_row.shape[0]
    counter = jnp.arange(length, dtype=jnp.int32)
    starts_here = jnp.concatenate([jnp.ones((1,), jnp.bool_), doc_row[1:] != doc_row[:-1]])
    begins = lax.cummax(jnp.where(starts_here, counter, jnp.zeros_like(counter)), axis=0)
    return counter - begins


def angles_of(places):
    half_dim = HD // 2
    frequency = rope_base ** (-(jnp.arange(half_dim, dtype=jnp.float32) * 2.0 / HD))
    return places.astype(jnp.float32)[:, None] * frequency[None, :]


def rotate(values, angles):
    half_dim = values.shape[-1] // 2
    first_half = values[..., :half_dim]
    second_half = values[..., half_dim:]
    cosine = jnp.cos(angles)
    sine_part = jnp.sin(angles)
    return jnp.concatenate(
        [
            first_half * cosine - second_half * sine_part,
            second_half * cosine + first_half * sine_part,
        ],
        axis=-1,
    )


def geglu(gate_in, up_in):
    return jax.nn.gelu(gate_in, approximate=True) * up_in


def adam_update(gradient, first_old, second_old, params_old, rate, decay_rate):
    first_new = beta_first * first_old + (1.0 - beta_first) * gradient
    second_new = beta_second * second_old + (1.0 - beta_second) * gradient * gradient
    first_hat = first_new / (1.0 - beta_first**STEP)
    second_hat = second_new / (1.0 - beta_second**STEP)
    params_new = params_old - rate * (
        first_hat / (jnp.sqrt(second_hat) + adam_floor) + decay_rate * params_old
    )
    return (first_new, second_new, params_new)


def piece_rows(device_count):
    return [
        entries // (128 * device_count)
        for entries in (D * HQ * HD, D * HD, D * HD, HQ * HD * D, D * FF, D * FF, FF * D)
    ]


def piece_shapes():
    return [(D, HQ * HD), (D, HD), (D, HD), (HQ * HD, D), (D, FF), (D, FF), (FF, D)]


def split_rows(stacked, row_list):
    result = []
    row_start = 0
    for row_count in row_list:
        result.append(stacked[row_start : row_start + row_count])
        row_start = row_start + row_count
    return result


def matmul(left_side, right_side):
    return jnp.dot(left_side, right_side, preferred_element_type=jnp.float32)


LOW_COUNT = 8
LANES = 128
LOW_MASKS = (0, 4, 2, 6, 1, 5, 3, 7)
GELU_SCALE = (2.0 / math.pi) ** 0.5
GELU_CUBE = 0.044715
VMEM_BYTES = 56 * 1024 * 1024


def aligned(device_count):
    groups = lax.axis_size("group") == 4
    return groups and device_count % LOW_COUNT == 0 and D % device_count == 0


def swap(value, mask):
    count = lax.axis_size(ALL_AXES)
    return lax.ppermute(value, ALL_AXES, [(source, source ^ mask) for source in range(count)])


def local_call(kernel, outs, operands, scratch=(), behind=()):
    specs = [pl.BlockSpec(memory_space=pltpu.SMEM)]
    specs = specs + [pl.BlockSpec(memory_space=pltpu.VMEM)] * len(operands)
    specs = specs + [pl.BlockSpec(memory_space=pl.ANY)] * len(behind)
    first, last = 1 + len(operands), 1 + len(operands) + len(behind)

    def body(*refs):
        kernel(*refs[:first], *refs[last:])

    return pl.pallas_call(
        body,
        out_shape=outs,
        in_specs=specs,
        out_specs=tuple(pl.BlockSpec(memory_space=pltpu.VMEM) for _ in outs),
        scratch_shapes=scratch,
        compiler_params=pltpu.CompilerParams(vmem_limit_bytes=VMEM_BYTES),
        cost_estimate=pl.CostEstimate(flops=0, bytes_accessed=0, transcendentals=0),
    )(lax.axis_index(ALL_AXES).astype(jnp.int32).reshape(1), *operands, *behind)


class Piece:
    def __init__(self, rows, columns, device_count):
        self.rows = rows
        self.columns = columns
        self.wide = rows == D
        self.blocks = columns // LANES
        self.own_rows = rows // device_count
        self.flat_rows = self.own_rows * self.blocks
        self.high_count = device_count // LOW_COUNT
        self.block_rows = self.own_rows * self.high_count
        self.size = self.block_rows * self.blocks


def pack_kernel(pieces, index_ref, *refs):
    high_count = pieces[0].high_count
    parts, out_refs, flat, packed = refs[:high_count], refs[high_count:-2], refs[-2], refs[-1]
    high = index_ref[0] // LOW_COUNT
    for step, part in enumerate(parts):
        flat[high ^ step] = part[...].astype(jnp.float32)
    start, target = 0, 0
    for piece in pieces:
        for block in range(piece.blocks):
            for place in range(high_count):
                packed[pl.ds(target, piece.own_rows), :] = flat[
                    place, pl.ds(start + block, piece.own_rows, stride=piece.blocks), :
                ]
                target = target + piece.own_rows
        start = start + piece.flat_rows
    count = target // len(out_refs)
    for place, out_ref in enumerate(out_refs):
        out_ref[...] = packed[place * count : (place + 1) * count, :].astype(jnp.bfloat16)


def sum_one_kernel(size, index_ref, near_ref, far_ref, to_x_ref, to_y_ref):
    total = near_ref[...].astype(jnp.float32) + far_ref[...].astype(jnp.float32)
    half = size // 2
    to_x_ref[:half, :] = total[:half].astype(jnp.bfloat16)
    if total.shape[0] > size:
        to_x_ref[half:, :] = total[size:].astype(jnp.bfloat16)
    to_y_ref[...] = total[half:size].astype(jnp.bfloat16)


def sum_three_kernel(
    size,
    index_ref,
    near_ref,
    far_ref,
    *refs,
):
    key_refs = refs[:-5]
    own_ref, beside_first_ref, beside_second_ref, across_first_ref, across_second_ref = refs[-5:]
    half = size // 2
    if key_refs:
        across_key_ref, cores_key_ref = key_refs
        rows = across_key_ref.shape[0]
        keys = across_key_ref[...] + cores_key_ref[rows:, :].astype(jnp.float32)
        for block in range(keys.shape[1] // LANES):
            first = half + block * rows
            columns = slice(block * LANES, (block + 1) * LANES)
            across_second_ref[first : first + rows, :] = keys[:, columns].astype(jnp.bfloat16)
    outs = (beside_first_ref, beside_second_ref, across_first_ref, across_second_ref)
    total = near_ref[:size, :].astype(jnp.float32) + far_ref[:size, :].astype(jnp.float32)
    own_ref[...] = total.astype(jnp.bfloat16)
    for place, out_ref in enumerate(outs):
        rows = slice(size + place * half, size + (place + 1) * half)
        total = near_ref[rows, :].astype(jnp.float32) + far_ref[rows, :].astype(jnp.float32)
        out_ref[:half, :] = total.astype(jnp.bfloat16)


def sum_passed_kernel(
    size,
    index_ref,
    beside_ref,
    across_ref,
    over_x_ref,
    over_y_ref,
    near_one_ref,
    far_one_ref,
    beside_out_ref,
    across_out_ref,
    extra_ref,
):
    half = size // 2
    beside = beside_ref[...].astype(jnp.float32) + over_y_ref[...].astype(jnp.float32)
    beside_out_ref[...] = beside.astype(jnp.bfloat16)
    across = across_ref[...].astype(jnp.float32) + over_x_ref[:half, :].astype(jnp.float32)
    across_out_ref[:half, :] = across.astype(jnp.bfloat16)
    if across_out_ref.shape[0] > half:
        extra = near_one_ref[size:, :].astype(jnp.float32)
        extra = extra + far_one_ref[size:, :].astype(jnp.float32)
        extra = extra + over_x_ref[half:, :].astype(jnp.float32)
        extra_ref[...] = extra
        across_out_ref[half:, :] = extra.astype(jnp.bfloat16)
    else:
        extra_ref[...] = jnp.zeros(extra_ref.shape, jnp.float32)


def unpack_kernel(
    pieces,
    index_ref,
    own_ref,
    beside_first_ref,
    beside_second_ref,
    across_first_ref,
    across_second_ref,
    extra_ref,
    *refs,
):
    high_count = pieces[0].high_count
    half = sum(piece.size for piece in pieces) // 2
    flat_rows = sum(piece.flat_rows for piece in pieces)
    outs, flat, packed = refs[:-2], refs[-2], refs[-1]
    high = index_ref[0] // LOW_COUNT
    packed[:half, :] = (
        own_ref[:half, :].astype(jnp.float32)
        + beside_first_ref[...].astype(jnp.float32)
        + across_first_ref[:half, :].astype(jnp.float32)
    )
    packed[half:, :] = (
        own_ref[half:, :].astype(jnp.float32)
        + beside_second_ref[...].astype(jnp.float32)
        + across_second_ref[:half, :].astype(jnp.float32)
    )
    start, source = 0, 0
    for piece in pieces:
        for block in range(piece.blocks):
            for place in range(high_count):
                flat[place, pl.ds(start + block, piece.own_rows, stride=piece.blocks), :] = packed[
                    pl.ds(source, piece.own_rows), :
                ]
                source = source + piece.own_rows
        start = start + piece.flat_rows
    for step, out_ref in enumerate(outs):
        out_ref[:flat_rows, :] = flat[high ^ step].astype(out_ref.dtype)
        if out_ref.shape[0] > flat_rows:
            extra = extra_ref[...] + across_first_ref[half:, :].astype(jnp.float32)
            out_ref[flat_rows:, :] = extra.astype(out_ref.dtype)


def array(shape, kind):
    return jax.ShapeDtypeStruct(shape, kind)


def gather_high(rows):
    high_count = lax.axis_size(ALL_AXES) // LOW_COUNT
    return [rows] + [swap(rows, step * LOW_COUNT) for step in range(1, high_count)]


def gather_own(pieces, parts, count, behind=()):
    high_count = pieces[0].high_count
    size = sum(piece.size for piece in pieces)
    return local_call(
        functools.partial(pack_kernel, pieces),
        (array((size // count, LANES), jnp.bfloat16),) * count,
        parts,
        (
            pltpu.VMEM((high_count, parts[0].shape[0], LANES), jnp.float32),
            pltpu.VMEM((size, LANES), jnp.float32),
        ),
        behind,
    )


def gather_halves(first, second):
    beside_second, across_first = swap(second, 4), swap(first, 2)
    beside_first, across_second = swap(first, 4), swap(second, 2)
    return (
        first,
        second,
        beside_first,
        beside_second,
        across_first,
        across_second,
        swap(across_first, 4),
        swap(beside_second, 2),
    )


def gather_wholes(own):
    beside, across = swap(own, 4), swap(own, 2)
    return own, beside, across, swap(across, 4)


def gather_cores(near):
    return near + tuple(swap(value, 1) for value in near)


def scatter_cores(far_three, far_one):
    far_one = swap(far_one, 1)
    return swap(far_three, 1), far_one


def scatter_one(pieces, near_one, far_one, behind=()):
    half = sum(piece.size for piece in pieces) // 2
    to_x, to_y = local_call(
        functools.partial(sum_one_kernel, 2 * half),
        (
            array((near_one.shape[0] - half, LANES), jnp.bfloat16),
            array((half, LANES), jnp.bfloat16),
        ),
        (near_one, far_one),
        (),
        behind,
    )
    return swap(to_x, 4), swap(to_y, 2), to_y


def scatter_three(pieces, near_three, far_three, behind=(), keys=()):
    size = sum(piece.size for piece in pieces)
    half = size // 2
    own, beside_first, beside_second, across_first, across_second = local_call(
        functools.partial(sum_three_kernel, size),
        (
            array((size, LANES), jnp.bfloat16),
            *(array((half, LANES), jnp.bfloat16),) * 3,
            array((half + (keys[0].size // LANES if keys else 0), LANES), jnp.bfloat16),
        ),
        (near_three, far_three, *keys),
        (),
        behind,
    )
    return own, swap(beside_first, 4), beside_second, across_first, swap(across_second, 2)


def scatter_passed(pieces, threes, over_x, over_y, near_one, far_one, behind=()):
    size = sum(piece.size for piece in pieces)
    extra_count = near_one.shape[0] - size
    own, beside_first, beside_second, across_first, across_second = threes
    beside_second, across_first, extra = local_call(
        functools.partial(sum_passed_kernel, size),
        (
            array((size // 2, LANES), jnp.bfloat16),
            array((size // 2 + extra_count, LANES), jnp.bfloat16),
            array((max(extra_count, 8), LANES), jnp.float32),
        ),
        (beside_second, across_first, over_x, over_y, near_one, far_one),
        (),
        behind,
    )
    terms = (
        own,
        beside_first,
        swap(beside_second, 4),
        swap(across_first, 2),
        across_second,
        extra,
    )
    return terms, beside_second


def scatter_high(pieces, terms, behind=()):
    high_count = pieces[0].high_count
    size = sum(piece.size for piece in pieces)
    flat_rows = sum(piece.flat_rows for piece in pieces)
    out_rows = flat_rows + terms[3].shape[0] - size // 2
    outs = local_call(
        functools.partial(unpack_kernel, pieces),
        (array((out_rows, LANES), jnp.float32),)
        + (array((out_rows, LANES), jnp.bfloat16),) * (high_count - 1),
        terms,
        (
            pltpu.VMEM((high_count, flat_rows, LANES), jnp.float32),
            pltpu.VMEM((size, LANES), jnp.float32),
        ),
        behind,
    )
    arrived = [swap(send, step * LOW_COUNT) for step, send in enumerate(outs) if step]
    return outs[0] + sum(value.astype(jnp.float32) for value in arrived), outs[0], arrived


def norm_parts(values):
    scale = lax.rsqrt(jnp.mean(values * values, axis=-1, keepdims=True) + norm_eps)
    return scale, values * scale


def norm_back(scale, normal, upstream, weight_vec):
    weighted = upstream * (1.0 + weight_vec)
    inner = jnp.mean(weighted * normal, axis=-1, keepdims=True)
    return scale * (weighted - normal * inner), jnp.sum(normal * upstream, axis=0, keepdims=True)


def product(left_side, right_side, left_axis, right_axis):
    return lax.dot_general(
        left_side,
        right_side,
        (((left_axis,), (right_axis,)), ((), ())),
        preferred_element_type=jnp.float32,
    )


def unordered(rows_in, order_low):
    upper = rows_in.astype(jnp.bfloat16)
    lower = (rows_in - upper.astype(jnp.float32)).astype(jnp.bfloat16)
    return product(upper, order_low, 1, 1) + product(lower, order_low, 1, 1)


def weight_rows(refs, size, order, start, rows):
    count = len(refs) // LOW_COUNT
    part = size // count
    return refs[order * count + start // part][start % part : start % part + rows, :]


def put_rows(refs, size, order, start, rows):
    three, one = refs[:2] if order < 4 else refs[2:]
    if order % 4 == 3:
        one[start : start + rows.shape[0], :] = rows
    else:
        start = order % 4 * size + start
        three[start : start + rows.shape[0], :] = rows


def wide_tile(refs, size, start, rows):
    return jnp.concatenate(
        [weight_rows(refs, size, order, start, rows) for order in range(LOW_COUNT)]
    )


def put_wide_tile(refs, size, start, rows, tile):
    for order in range(LOW_COUNT):
        put_rows(refs, size, order, start, tile[order * rows : (order + 1) * rows])


def tall_rows(piece, low):
    for order, mask in enumerate(LOW_MASKS):
        for block in range(piece.blocks):
            for place in range(piece.high_count):
                row = (place * LOW_COUNT + (low ^ mask)) * piece.own_rows
                yield (
                    order,
                    block * piece.block_rows + place * piece.own_rows,
                    pl.ds(pl.multiple_of(row, piece.own_rows), piece.own_rows),
                    slice(block * LANES, (block + 1) * LANES),
                )


def ffn_kernel(
    gate_piece,
    down_piece,
    index_ref,
    middle_ref,
    cotangent_ref,
    gain_in_ref,
    gain_out_ref,
    order_ref,
    *refs,
):
    weight_refs, grad_refs = refs[:16], refs[20:24]
    block_out_ref, grad_middle_ref, grad_gain_in_ref, grad_gain_out_ref = refs[16:20]
    down_ref, hidden_ref, gelu_ref, slope_ref = refs[24:]
    low = index_ref[0] % LOW_COUNT
    rows = gate_piece.block_rows
    size = 2 * gate_piece.size + down_piece.size
    width = 2 * LANES
    for order, start, matrix_rows, columns in tall_rows(down_piece, low):
        start = start + 2 * gate_piece.size
        down_ref[matrix_rows, columns] = weight_rows(
            weight_refs, size, order, start, down_piece.own_rows
        )

    def wide_tiles(step):
        return [
            jnp.concatenate(
                [
                    wide_tile(weight_refs, size, offset + block * rows, rows)
                    for block in (2 * step, 2 * step + 1)
                ],
                axis=1,
            )
            for offset in (0, gate_piece.size)
        ]

    middle = middle_ref[...]
    scale_in, normal_in = norm_parts(middle)
    order_low = order_ref[...]
    normed = (normal_in * (1.0 + gain_in_ref[...])).astype(jnp.bfloat16)
    normed = product(normed, order_low, 1, 0).astype(jnp.bfloat16)
    for step in range(FF // width):
        columns = slice(step * width, (step + 1) * width)
        gate_weight, up_weight = wide_tiles(step)
        gate = product(normed, gate_weight, 1, 0)
        up = product(normed, up_weight, 1, 0)
        square = gate * gate
        bend = jnp.tanh(GELU_SCALE * gate * (1.0 + GELU_CUBE * square))
        half = 0.5 * (1.0 + bend)
        gelu = gate * half
        slope = half + 0.5 * gate * (1.0 - bend * bend) * GELU_SCALE * (
            1.0 + 3.0 * GELU_CUBE * square
        )
        gelu_ref[:, columns] = gelu
        slope_ref[:, columns] = slope * up
        hidden_ref[:, columns] = (gelu * up).astype(jnp.bfloat16)
    hidden = hidden_ref[...]
    scale_out, normal_out = norm_parts(product(hidden, down_ref[...], 1, 0))
    block_out_ref[...] = (middle + normal_out * (1.0 + gain_out_ref[...])).astype(jnp.bfloat16)
    upstream = cotangent_ref[...].astype(jnp.float32)
    grad_ffn, grad_gain_out_ref[...] = norm_back(
        scale_out, normal_out, upstream, gain_out_ref[...]
    )
    grad_ffn = grad_ffn.astype(jnp.bfloat16)
    grad_normed = jnp.zeros(middle.shape, jnp.float32)
    for step in range(FF // width):
        columns = slice(step * width, (step + 1) * width)
        grad_hidden = product(grad_ffn, down_ref[columns, :], 1, 1)
        down_ref[columns, :] = product(hidden_ref[:, columns], grad_ffn, 0, 0).astype(jnp.bfloat16)
        grads = [
            (grad_hidden * slope_ref[:, columns]).astype(jnp.bfloat16),
            (grad_hidden * gelu_ref[:, columns]).astype(jnp.bfloat16),
        ]
        for place, (grad, weight) in enumerate(zip(grads, wide_tiles(step))):
            grad_weight = product(normed, grad, 0, 0).astype(jnp.bfloat16)
            for side in range(2):
                put_wide_tile(
                    grad_refs,
                    size,
                    place * gate_piece.size + (2 * step + side) * rows,
                    rows,
                    grad_weight[:, side * LANES : (side + 1) * LANES],
                )
            grad_normed = grad_normed + product(grad, weight, 1, 1)
    for order, start, matrix_rows, columns in tall_rows(down_piece, low):
        start = start + 2 * gate_piece.size
        put_rows(grad_refs, size, order, start, down_ref[matrix_rows, columns])
    grad_middle, grad_gain_in_ref[...] = norm_back(
        scale_in, normal_in, unordered(grad_normed, order_low), gain_in_ref[...]
    )
    grad_middle_ref[...] = upstream + grad_middle


def grad_arrays(pieces, extra_count=0):
    size = sum(piece.size for piece in pieces)
    return (
        array((3 * size, LANES), jnp.bfloat16),
        array((size + extra_count, LANES), jnp.bfloat16),
    ) * 2


def ffn_blocks(pieces, middle, cotangent, gain_in, gain_out, order, blocks):
    rows = middle.shape[0]
    outs = local_call(
        functools.partial(ffn_kernel, pieces[4], pieces[6]),
        (
            array((rows, D), jnp.bfloat16),
            array((rows, D), jnp.float32),
            array((1, D), jnp.float32),
            array((1, D), jnp.float32),
            *grad_arrays(pieces[4:7]),
        ),
        (middle, cotangent, gain_in, gain_out, order, *blocks),
        (
            pltpu.VMEM((FF, D), jnp.bfloat16),
            pltpu.VMEM((rows, FF), jnp.bfloat16),
            pltpu.VMEM((rows, FF), jnp.float32),
            pltpu.VMEM((rows, FF), jnp.float32),
        ),
    )
    return *outs[:4], outs[4:]


def turn(values, cosine, sine):
    first_half, second_half = values[:, : HD // 2], values[:, HD // 2 :]
    return jnp.concatenate(
        [first_half * cosine - second_half * sine, second_half * cosine + first_half * sine], axis=1
    )


def wide_head(refs, size, start, rows):
    return jnp.concatenate(
        [wide_tile(refs, size, start + side * rows, rows) for side in range(2)], axis=1
    )


def head_starts(pieces):
    rows = pieces[0].block_rows
    return [2 * rows * head for head in range(HQ + 2)]


def project_kernel(
    pieces,
    index_ref,
    tokens_ref,
    gain_ref,
    gain_query_ref,
    gain_key_ref,
    cosine_ref,
    sine_ref,
    order_ref,
    *refs,
):
    weight_refs = refs[:8]
    normed_ref, query_proj_ref, key_proj_ref, query_ref, key_value_ref = refs[8:]
    size = sum(piece.size for piece in pieces)
    rows = pieces[0].block_rows
    cosine, sine = cosine_ref[...], sine_ref[...]
    _, normal = norm_parts(tokens_ref[...].astype(jnp.float32))
    normed = (normal * (1.0 + gain_ref[...])).astype(jnp.bfloat16)
    normed = product(normed, order_ref[...], 1, 0).astype(jnp.bfloat16)
    normed_ref[...] = normed
    starts = head_starts(pieces)
    for head, start in enumerate(starts):
        proj = product(normed, wide_head(weight_refs, size, start, rows), 1, 0)
        columns = slice(head * HD, (head + 1) * HD)
        if head == HQ + 1:
            key_value_ref[:, HD:] = proj.astype(jnp.bfloat16)
            continue
        gain_vec = gain_query_ref[...] if head < HQ else gain_key_ref[...]
        _, normal = norm_parts(proj)
        turned = turn(normal * (1.0 + gain_vec), cosine, sine).astype(jnp.bfloat16)
        if head < HQ:
            query_proj_ref[:, columns] = proj
            query_ref[:, columns] = turned
        else:
            key_proj_ref[...] = proj
            key_value_ref[:, :HD] = turned


def attend_kernel(
    pieces,
    index_ref,
    tokens_ref,
    gain_ref,
    allowed_ref,
    query_ref,
    *refs,
):
    weight_refs, key_value_refs = refs[:8], refs[8:-5]
    probs_ref, attended_ref, attn_out_ref, middle_ref, out_weight_ref = refs[-5:]
    out_piece = pieces[-1]
    low = index_ref[0] % LOW_COUNT
    size = sum(piece.size for piece in pieces)
    out_start = size - out_piece.size
    for order, start, matrix_rows, columns in tall_rows(out_piece, low):
        out_weight_ref[matrix_rows, columns] = weight_rows(
            weight_refs, size, order, start + out_start, out_piece.own_rows
        )
    rows = tokens_ref.shape[0]
    allowed = allowed_ref[...] > 0.0
    keys = jnp.concatenate([ref[:, :HD] for ref in key_value_refs])
    values = jnp.concatenate([ref[:, HD:] for ref in key_value_refs])
    count = keys.shape[0]
    for head in range(HQ):
        columns = slice(head * HD, (head + 1) * HD)
        scores = product(query_ref[:, columns], keys, 1, 1) * HD ** (-0.5)
        scores = jnp.where(allowed, scores, -1e30)
        raised = jnp.exp(scores - jnp.max(scores, axis=-1, keepdims=True))
        probs = raised / jnp.sum(raised, axis=-1, keepdims=True)
        probs_ref[:, head * count : (head + 1) * count] = probs
        attended_ref[:, columns] = product(probs.astype(jnp.bfloat16), values, 1, 0).astype(
            jnp.bfloat16
        )
    attn_out = product(attended_ref[...], out_weight_ref[...], 1, 0)
    attn_out_ref[...] = attn_out
    _, normal = norm_parts(attn_out)
    middle_ref[...] = tokens_ref[...].astype(jnp.float32) + normal * (1.0 + gain_ref[...])


def attend_back_kernel(
    index_ref,
    grad_middle_ref,
    attn_out_ref,
    gain_ref,
    out_weight_ref,
    attended_ref,
    probs_ref,
    query_ref,
    *refs,
):
    key_value_refs = refs[:4]
    grad_out_weight_ref, grad_query_ref, grad_gain_ref = refs[4:7]
    grad_own_ref, grad_across_ref, grad_cores_ref = refs[7:]
    rows = query_ref.shape[0]
    scale, normal = norm_parts(attn_out_ref[...])
    grad_attn, grad_gain_ref[...] = norm_back(scale, normal, grad_middle_ref[...], gain_ref[...])
    grad_attn = grad_attn.astype(jnp.bfloat16)
    grad_out_weight_ref[...] = product(attended_ref[...], grad_attn, 0, 0).astype(jnp.bfloat16)
    keys = jnp.concatenate([ref[:, :HD] for ref in key_value_refs])
    values = jnp.concatenate([ref[:, HD:] for ref in key_value_refs])
    count = keys.shape[0]
    grad_keys = jnp.zeros((count, HD), jnp.float32)
    grad_values = jnp.zeros((count, HD), jnp.float32)
    for head in range(HQ):
        columns = slice(head * HD, (head + 1) * HD)
        grad_attended = product(grad_attn, out_weight_ref[columns, :], 1, 1).astype(jnp.bfloat16)
        probs = probs_ref[:, head * count : (head + 1) * count]
        grad_probs = product(grad_attended, values, 1, 1)
        grad_values = grad_values + product(probs.astype(jnp.bfloat16), grad_attended, 0, 0)
        inner = jnp.sum(probs * grad_probs, axis=-1, keepdims=True)
        grad_scores = (probs * (grad_probs - inner) * HD ** (-0.5)).astype(jnp.bfloat16)
        grad_query_ref[:, columns] = product(grad_scores, keys, 1, 0)
        grad_keys = grad_keys + product(grad_scores, query_ref[:, columns], 0, 0)
    targets = (
        grad_own_ref,
        grad_cores_ref.at[:rows],
        grad_across_ref,
        grad_cores_ref.at[rows:],
    )
    for part, ref in enumerate(targets):
        ref[:, :HD] = grad_keys[part * rows : (part + 1) * rows].astype(ref.dtype)
        ref[:, HD:] = grad_values[part * rows : (part + 1) * rows].astype(ref.dtype)


def query_back_kernel(
    pieces,
    index_ref,
    gain_ref,
    cosine_ref,
    sine_ref,
    normed_ref,
    query_proj_ref,
    grad_query_ref,
    *refs,
):
    weight_refs = refs[:8]
    grad_weight_ref, grad_normed_ref, grad_gain_ref = refs[8:]
    size = sum(piece.size for piece in pieces)
    rows = pieces[0].block_rows
    cosine, sine = cosine_ref[...], sine_ref[...]
    normed = normed_ref[...]
    grad_normed = jnp.zeros(grad_normed_ref.shape, jnp.float32)
    grad_gain = jnp.zeros((1, HD), jnp.float32)
    for head, start in enumerate(head_starts(pieces)[:HQ]):
        columns = slice(head * HD, (head + 1) * HD)
        scale, normal = norm_parts(query_proj_ref[:, columns])
        upstream = turn(grad_query_ref[:, columns], cosine, -sine)
        grad, gain_row = norm_back(scale, normal, upstream, gain_ref[...])
        grad_gain = grad_gain + gain_row
        grad = grad.astype(jnp.bfloat16)
        weight = wide_head(weight_refs, size, start, rows)
        grad_normed = grad_normed + product(grad, weight, 1, 1)
        grad_weight_ref[:, columns] = product(normed, grad, 0, 0).astype(jnp.bfloat16)
    grad_normed_ref[...] = grad_normed
    grad_gain_ref[...] = grad_gain


def project_back_kernel(
    pieces,
    index_ref,
    tokens_ref,
    gain_ref,
    gain_key_ref,
    cosine_ref,
    sine_ref,
    order_ref,
    normed_ref,
    key_proj_ref,
    grad_normed_ref,
    grad_middle_ref,
    gain_attn_ref,
    gain_ffin_ref,
    gain_ffout_ref,
    gain_query_ref,
    own_key_ref,
    cores_key_ref,
    across_key_ref,
    *refs,
):
    weight_refs = refs[:8]
    grad_weight_ref, input_grad_ref, grad_gain_ref = refs[8:]
    size = sum(piece.size for piece in pieces)
    rows = pieces[0].block_rows
    normed = normed_ref[...]
    key_rows = own_key_ref.shape[0]
    first = across_key_ref.shape[0] - 4 * key_rows
    key_value = own_key_ref[...] + cores_key_ref[:key_rows, :].astype(jnp.float32)
    key_value = key_value + jnp.concatenate(
        [
            across_key_ref[first + block * key_rows : first + (block + 1) * key_rows, :].astype(
                jnp.float32
            )
            for block in range(4)
        ],
        axis=1,
    )
    scale, normal = norm_parts(key_proj_ref[...])
    upstream = turn(key_value[:, :HD], cosine_ref[...], -sine_ref[...])
    grad_key, grad_gain_key = norm_back(scale, normal, upstream, gain_key_ref[...])
    grad_normed = grad_normed_ref[...]
    for place, start in enumerate(head_starts(pieces)[HQ:]):
        grad = (key_value[:, HD:] if place else grad_key).astype(jnp.bfloat16)
        weight = wide_head(weight_refs, size, start, rows)
        grad_normed = grad_normed + product(grad, weight, 1, 1)
        grad_weight_ref[:, place * HD : (place + 1) * HD] = product(normed, grad, 0, 0).astype(
            jnp.bfloat16
        )
    scale, normal = norm_parts(tokens_ref[...].astype(jnp.float32))
    grad_inputs, grad_gain_input = norm_back(
        scale, normal, unordered(grad_normed, order_ref[...]), gain_ref[...]
    )
    input_grad_ref[...] = (grad_middle_ref[...] + grad_inputs).astype(jnp.bfloat16)
    grad_gains = [
        grad_gain_input,
        gain_attn_ref[...],
        gain_ffin_ref[...],
        gain_ffout_ref[...],
        gain_query_ref[...],
        grad_gain_key,
    ]
    row = 0
    grad_gain_ref[...] = jnp.zeros(grad_gain_ref.shape, jnp.float32)
    for values in grad_gains:
        for start in range(0, values.shape[1], LANES):
            grad_gain_ref[row : row + 1, :] = values[:, start : start + LANES]
            row = row + 1


def split_kernel(
    pieces,
    index_ref,
    query_ref,
    key_value_ref,
    out_ref,
    gain_ref,
    *grad_refs,
):
    low = index_ref[0] % LOW_COUNT
    size = sum(piece.size for piece in pieces)
    rows = pieces[0].block_rows
    start = 0
    for matrix_ref in (query_ref, key_value_ref):
        for column in range(0, matrix_ref.shape[1], LANES):
            tile = matrix_ref[:, column : column + LANES]
            put_wide_tile(grad_refs, size, start, rows, tile)
            start = start + rows
    out_piece = pieces[-1]
    for order, first, matrix_rows, columns in tall_rows(out_piece, low):
        put_rows(grad_refs, size, order, start + first, out_ref[matrix_rows, columns])
    for target in (grad_refs[1], grad_refs[3]):
        target[size:, :] = gain_ref[...].astype(jnp.bfloat16)


def width_order(device_count):
    low = lax.axis_index(ALL_AXES) % LOW_COUNT
    rows = D // device_count
    high_count = device_count // LOW_COUNT
    column = jnp.arange(D, dtype=jnp.int32)
    place = column // (rows * high_count)
    mask = (place & 1) * 4 + ((place >> 1) & 1) * 2 + (place >> 2)
    high = (column // rows) % high_count
    picked = (high * LOW_COUNT + (low ^ mask)) * rows + column % rows
    return (jnp.arange(D, dtype=jnp.int32)[:, None] == picked[None, :]).astype(jnp.bfloat16)


GAIN_ROWS = 32


def shards_blocks(
    device_count,
    tokens,
    doc_ids,
    cotangent,
    master,
    first_moment,
    second_moment,
    gains,
    gain_first,
    gain_second,
):
    pieces = [Piece(*shape_pair, device_count) for shape_pair in piece_shapes()]
    attention_pieces = pieces[:4]
    local_rows = tokens.shape[0]
    group_size = lax.axis_size("group")
    first_row = lax.axis_index("group") * local_rows
    attention_rows = sum(piece.flat_rows for piece in attention_pieces)
    ffn_pieces = pieces[4:7]
    rounded = master.astype(jnp.bfloat16)
    attention_parts = gather_high(rounded[:attention_rows])
    ffn_rows = rounded[attention_rows:]
    ffn_parts = gather_high(ffn_rows)
    attention_near = gather_wholes(
        *gather_own(attention_pieces, attention_parts, 1, (ffn_parts[1],))
    )
    attention_blocks = gather_cores(attention_near)
    ffn_weights = gather_cores(
        gather_halves(*gather_own(ffn_pieces, ffn_parts, 2, attention_near[1:]))
    )
    gain_parts = []
    for start, width in ((0, D), (D, D), (2 * D, D), (3 * D, D), (4 * D, HD), (4 * D + HD, HD)):
        gain_parts.append(gains[start : start + width][None])
    gain_input, gain_attn, gain_ffin, gain_ffout, gain_query, gain_key = gain_parts
    order = width_order(device_count)
    doc_row = doc_ids[0]
    angles = lax.dynamic_slice_in_dim(angles_of(positions(doc_row)), first_row, local_rows, 0)
    cosine, sine = jnp.cos(angles), jnp.sin(angles)
    query_docs = lax.dynamic_slice_in_dim(doc_row, first_row, local_rows, 0)
    key_count = group_size * local_rows
    first_keys = [(lax.axis_index("group") ^ step) * local_rows for step in range(group_size)]
    key_docs = jnp.concatenate(
        [lax.dynamic_slice_in_dim(doc_row, start, local_rows, 0) for start in first_keys]
    )
    key_index = jnp.concatenate(
        [start + jnp.arange(local_rows, dtype=jnp.int32) for start in first_keys]
    )
    query_index = first_row + jnp.arange(local_rows, dtype=jnp.int32)
    distance = query_index[:, None] - key_index[None, :]
    allowed = (distance >= 0) & (distance < WINDOW) & (key_docs[None, :] == query_docs[:, None])
    allowed = allowed.astype(jnp.float32)

    width = HQ * HD
    normed, query_proj, key_proj, query_rot, key_value = local_call(
        functools.partial(project_kernel, attention_pieces),
        (
            array((local_rows, D), jnp.bfloat16),
            array((local_rows, width), jnp.float32),
            array((local_rows, HD), jnp.float32),
            array((local_rows, width), jnp.bfloat16),
            array((local_rows, 2 * HD), jnp.bfloat16),
        ),
        (tokens, gain_input, gain_query, gain_key, cosine, sine, order, *attention_blocks),
    )
    key_values = [key_value] + [swap(key_value, step) for step in range(1, group_size)]
    probs, attended, attn_out, middle, out_weight = local_call(
        functools.partial(attend_kernel, attention_pieces),
        (
            array((local_rows, HQ * key_count), jnp.float32),
            array((local_rows, width), jnp.bfloat16),
            array((local_rows, D), jnp.float32),
            array((local_rows, D), jnp.float32),
            array((width, D), jnp.bfloat16),
        ),
        (tokens, gain_attn, allowed, query_rot, *attention_blocks, *key_values),
    )
    outputs, grad_middle, grad_gain_ffin, grad_gain_ffout, grads_ffn = ffn_blocks(
        pieces, middle, cotangent, gain_ffin, gain_ffout, order, ffn_weights
    )
    near_three, near_one, far_three, far_one = grads_ffn
    far_three, far_one = scatter_cores(far_three, far_one)
    grad_out_weight, grad_query, grad_gain_attn, own_key, across_key, cores_key = local_call(
        attend_back_kernel,
        (
            array((width, D), jnp.bfloat16),
            array((local_rows, width), jnp.float32),
            array((1, D), jnp.float32),
            array((local_rows, 2 * HD), jnp.float32),
            array((local_rows, 2 * HD), jnp.float32),
            array((2 * local_rows, 2 * HD), jnp.bfloat16),
        ),
        (
            grad_middle,
            attn_out,
            gain_attn,
            out_weight,
            attended,
            probs,
            query_rot,
            *key_values,
        ),
    )
    cores_key = swap(cores_key, 1)
    over_x, over_y, sent = scatter_one(ffn_pieces, near_one, far_one, (grad_query,))
    threes = scatter_three(ffn_pieces, near_three, far_three, (sent,), (across_key, cores_key))
    grad_query_weight, grad_normed, grad_gain_query = local_call(
        functools.partial(query_back_kernel, attention_pieces),
        (
            array((D, width), jnp.bfloat16),
            array((local_rows, D), jnp.float32),
            array((1, HD), jnp.float32),
        ),
        (gain_query, cosine, sine, normed, query_proj, grad_query, *attention_blocks),
        (),
        (threes[0],),
    )
    ffn_terms, sent = scatter_passed(
        ffn_pieces, threes, over_x, over_y, near_one, far_one, (grad_normed,)
    )
    grad_key_weight, grad_inputs, grad_gains = local_call(
        functools.partial(project_back_kernel, attention_pieces),
        (
            array((D, 2 * HD), jnp.bfloat16),
            array((local_rows, D), jnp.bfloat16),
            array((GAIN_ROWS, LANES), jnp.float32),
        ),
        (
            tokens,
            gain_input,
            gain_key,
            cosine,
            sine,
            order,
            normed,
            key_proj,
            grad_normed,
            grad_middle,
            grad_gain_attn,
            grad_gain_ffin,
            grad_gain_ffout,
            grad_gain_query,
            own_key,
            cores_key,
            threes[4],
            *attention_blocks,
        ),
        (),
        (sent, threes[1]),
    )
    grads_ffn, sent, arrived = scatter_high(ffn_pieces, ffn_terms, (grad_inputs,))
    near_three, near_one, far_three, far_one = local_call(
        functools.partial(split_kernel, attention_pieces),
        grad_arrays(attention_pieces, GAIN_ROWS),
        (grad_query_weight, grad_key_weight, grad_out_weight, grad_gains),
        (),
        (sent,),
    )
    far_three, far_one = scatter_cores(far_three, far_one)
    over_x, over_y, sent = scatter_one(attention_pieces, near_one, far_one)
    threes = scatter_three(attention_pieces, near_three, far_three, (sent, arrived[0]))
    terms, _ = scatter_passed(attention_pieces, threes, over_x, over_y, near_one, far_one)
    grads_attention, _, _ = scatter_high(attention_pieces, terms, arrived)
    gain_grads = grads_attention[attention_rows:].reshape(-1)[: gains.shape[0]]
    grads_local = jnp.concatenate([grads_attention[:attention_rows], grads_ffn])
    return (
        outputs,
        grad_inputs,
        *adam_update(grads_local, first_moment, second_moment, master, learn_rate, weight_decay),
        *adam_update(gain_grads, gain_first, gain_second, gains, gain_rate, 0.0),
    )


def shards(
    tokens, doc_ids, cotangent, master, first_moment, second_moment, gains, gain_first, gain_second
):
    group_size = lax.axis_size("group")
    devices_all = lax.axis_size("dp") * group_size
    if aligned(devices_all):
        return shards_blocks(
            devices_all,
            tokens,
            doc_ids,
            cotangent,
            master,
            first_moment,
            second_moment,
            gains,
            gain_first,
            gain_second,
        )
    group_index = lax.axis_index("group")
    local_rows = tokens.shape[0]
    shard_parts = [
        part_rows.astype(jnp.bfloat16) for part_rows in split_rows(master, piece_rows(devices_all))
    ]
    gathered = (
        lax.all_gather(shard_parts[0], ("dp", "group"), axis=0, tiled=True),
        lax.all_gather(shard_parts[1], ("dp", "group"), axis=0, tiled=True),
        lax.all_gather(shard_parts[2], ("dp", "group"), axis=0, tiled=True),
        lax.all_gather(shard_parts[3], ("dp", "group"), axis=0, tiled=True),
        lax.all_gather(shard_parts[4], ("dp", "group"), axis=0, tiled=True),
        lax.all_gather(shard_parts[5], ("dp", "group"), axis=0, tiled=True),
        lax.all_gather(shard_parts[6], ("dp", "group"), axis=0, tiled=True),
    )
    query_weight, key_weight, value_weight, out_weight, gate_weight, up_weight, down_weight = [
        full_rows.reshape(shape_pair) for full_rows, shape_pair in zip(gathered, piece_shapes())
    ]
    norm_input = gains[0:D]
    norm_attn = gains[D : 2 * D]
    norm_ffin = gains[2 * D : 3 * D]
    norm_ffout = gains[3 * D : 4 * D]
    norm_query = gains[4 * D : 4 * D + HD]
    norm_key = gains[4 * D + HD : 4 * D + 2 * HD]
    doc_row = doc_ids[0]
    first_row = group_index * local_rows
    angles = lax.dynamic_slice_in_dim(angles_of(positions(doc_row)), first_row, local_rows, 0)
    query_docs = lax.dynamic_slice_in_dim(doc_row, first_row, local_rows, 0)
    inputs = tokens.astype(jnp.float32)
    normed, back_input = jax.vjp(rms_norm, inputs, norm_input)
    normed_low = normed.astype(jnp.bfloat16)
    query_proj = matmul(normed_low, query_weight)
    key_proj = matmul(normed_low, key_weight)
    value_proj = matmul(normed_low, value_weight)

    def query_prep(flat_rows, gain_vec):
        return rotate(rms_norm(flat_rows.reshape(local_rows, HQ, HD), gain_vec), angles[:, None, :])

    def key_prep(rows_in, gain_vec):
        return rotate(rms_norm(rows_in, gain_vec), angles)

    query_rot, back_query = jax.vjp(query_prep, query_proj, norm_query)
    key_rot, back_key = jax.vjp(key_prep, key_proj, norm_key)
    query_low = query_rot.astype(jnp.bfloat16)
    key_low = key_rot.astype(jnp.bfloat16)
    value_low = value_proj.astype(jnp.bfloat16)
    reach = min(-(-(WINDOW - 1) // local_rows), group_size - 1)
    key_list = [key_low]
    value_list = [value_low]
    for offset in range(1, reach + 1):
        key_far, value_far = shifted((key_low, value_low), "group", offset)
        key_list.insert(0, key_far)
        value_list.insert(0, value_far)
    key_all = jnp.concatenate(key_list, axis=0)
    value_all = jnp.concatenate(value_list, axis=0)
    key_count = (reach + 1) * local_rows
    doc_pad = jnp.concatenate([jnp.full((reach * local_rows,), -1, jnp.int32), doc_row])
    key_docs = lax.dynamic_slice_in_dim(doc_pad, first_row, key_count, 0)
    key_index = (group_index - reach) * local_rows + jnp.arange(key_count, dtype=jnp.int32)
    query_index = first_row + jnp.arange(local_rows, dtype=jnp.int32)
    distance = query_index[:, None] - key_index[None, :]
    allowed = (distance >= 0) & (distance < WINDOW) & (key_docs[None, :] == query_docs[:, None])

    def scores_of(key_rows_low):
        raw_scores = jnp.einsum(
            "qhd,kd->hqk", query_low, key_rows_low, preferred_element_type=jnp.float32
        ) * HD ** (-0.5)
        return jnp.where(allowed[None], raw_scores, -1e30)

    masked = scores_of(key_all)
    top_score = jnp.max(masked, axis=-1, keepdims=True)
    log_total = top_score + jnp.log(jnp.sum(jnp.exp(masked - top_score), axis=-1, keepdims=True))
    probs = jnp.exp(masked - log_total)
    attended = jnp.einsum(
        "hqk,kd->qhd", probs.astype(jnp.bfloat16), value_all, preferred_element_type=jnp.float32
    )
    attended_low = attended.reshape(local_rows, HQ * HD).astype(jnp.bfloat16)
    attn_out = matmul(attended_low, out_weight)
    branch_one, back_attn = jax.vjp(rms_norm, attn_out, norm_attn)
    middle = inputs + branch_one
    normed_two, back_ffin = jax.vjp(rms_norm, middle, norm_ffin)
    normed_two_low = normed_two.astype(jnp.bfloat16)
    gate_proj = matmul(normed_two_low, gate_weight)
    up_proj = matmul(normed_two_low, up_weight)
    hidden, back_hidden = jax.vjp(geglu, gate_proj, up_proj)
    hidden_low = hidden.astype(jnp.bfloat16)
    ffn_out = matmul(hidden_low, down_weight)
    branch_two, back_ffout = jax.vjp(rms_norm, ffn_out, norm_ffout)
    outputs = middle + branch_two
    grad_out = cotangent.astype(jnp.float32)
    grad_ffn, grad_gain_ffout = back_ffout(grad_out)
    grad_ffn_low = grad_ffn.astype(jnp.bfloat16)
    grad_down_w = jnp.einsum(
        "tf,td->fd", hidden_low, grad_ffn_low, preferred_element_type=jnp.float32
    )
    grad_hidden = jnp.einsum(
        "td,fd->tf", grad_ffn_low, down_weight, preferred_element_type=jnp.float32
    )
    grad_gate, grad_up = back_hidden(grad_hidden)
    grad_gate_low = grad_gate.astype(jnp.bfloat16)
    grad_up_low = grad_up.astype(jnp.bfloat16)
    grad_gate_w = jnp.einsum(
        "td,tf->df", normed_two_low, grad_gate_low, preferred_element_type=jnp.float32
    )
    grad_up_w = jnp.einsum(
        "td,tf->df", normed_two_low, grad_up_low, preferred_element_type=jnp.float32
    )
    grad_normed_two = jnp.einsum(
        "tf,df->td", grad_gate_low, gate_weight, preferred_element_type=jnp.float32
    ) + jnp.einsum("tf,df->td", grad_up_low, up_weight, preferred_element_type=jnp.float32)
    grad_middle_norm, grad_gain_ffin = back_ffin(grad_normed_two)
    grad_middle = grad_out + grad_middle_norm
    grad_attn, grad_gain_attn = back_attn(grad_middle)
    grad_attn_low = grad_attn.astype(jnp.bfloat16)
    grad_out_w = jnp.einsum(
        "to,td->od", attended_low, grad_attn_low, preferred_element_type=jnp.float32
    )
    grad_attended = jnp.einsum(
        "td,od->to", grad_attn_low, out_weight, preferred_element_type=jnp.float32
    )
    grad_attended_low = grad_attended.astype(jnp.bfloat16).reshape(local_rows, HQ, HD)
    probs_again = jnp.exp(scores_of(key_all) - log_total)
    grad_probs = jnp.einsum(
        "qhd,kd->hqk", grad_attended_low, value_all, preferred_element_type=jnp.float32
    )
    grad_value_all = jnp.einsum(
        "hqk,qhd->kd",
        probs_again.astype(jnp.bfloat16),
        grad_attended_low,
        preferred_element_type=jnp.float32,
    )
    grad_scores = probs_again * (
        grad_probs - jnp.sum(probs_again * grad_probs, axis=-1, keepdims=True)
    )
    grad_scores_low = (grad_scores * HD ** (-0.5)).astype(jnp.bfloat16)
    grad_query = jnp.einsum(
        "hqk,kd->qhd", grad_scores_low, key_all, preferred_element_type=jnp.float32
    )
    grad_key_all = jnp.einsum(
        "hqk,qhd->kd", grad_scores_low, query_low, preferred_element_type=jnp.float32
    )
    key_total = grad_key_all[reach * local_rows :]
    value_total = grad_value_all[reach * local_rows :]
    for offset in range(1, reach + 1):
        row_start = (reach - offset) * local_rows
        key_back, value_back = (
            shifted(
                grad_key_all[row_start : row_start + local_rows].astype(jnp.bfloat16),
                "group",
                -offset,
            ).astype(jnp.float32),
            shifted(
                grad_value_all[row_start : row_start + local_rows].astype(jnp.bfloat16),
                "group",
                -offset,
            ).astype(jnp.float32),
        )
        key_total = key_total + key_back
        value_total = value_total + value_back
    grad_query_proj, grad_gain_query = back_query(grad_query)
    grad_key_proj, grad_gain_key = back_key(key_total)
    grad_query_low = grad_query_proj.astype(jnp.bfloat16)
    grad_key_low = grad_key_proj.astype(jnp.bfloat16)
    grad_value_low = value_total.astype(jnp.bfloat16)
    grad_query_w = jnp.einsum(
        "td,te->de", normed_low, grad_query_low, preferred_element_type=jnp.float32
    )
    grad_key_w = jnp.einsum(
        "td,te->de", normed_low, grad_key_low, preferred_element_type=jnp.float32
    )
    grad_value_w = jnp.einsum(
        "td,te->de", normed_low, grad_value_low, preferred_element_type=jnp.float32
    )
    grad_normed = jnp.einsum(
        "te,de->td", grad_query_low, query_weight, preferred_element_type=jnp.float32
    )
    grad_normed = grad_normed + jnp.einsum(
        "te,de->td", grad_key_low, key_weight, preferred_element_type=jnp.float32
    )
    grad_normed = grad_normed + jnp.einsum(
        "te,de->td", grad_value_low, value_weight, preferred_element_type=jnp.float32
    )
    grad_input_norm, grad_gain_input = back_input(grad_normed)
    grad_inputs = grad_middle + grad_input_norm
    flat_query = grad_query_w.reshape(-1, 128)
    flat_key = grad_key_w.reshape(-1, 128)
    flat_value = grad_value_w.reshape(-1, 128)
    flat_out = grad_out_w.reshape(-1, 128)
    flat_gate = grad_gate_w.reshape(-1, 128)
    flat_up = grad_up_w.reshape(-1, 128)
    flat_down = grad_down_w.reshape(-1, 128)
    reduced = (
        lax.psum_scatter(flat_query, ("dp", "group"), scatter_dimension=0, tiled=True),
        lax.psum_scatter(flat_key, ("dp", "group"), scatter_dimension=0, tiled=True),
        lax.psum_scatter(flat_value, ("dp", "group"), scatter_dimension=0, tiled=True),
        lax.psum_scatter(flat_out, ("dp", "group"), scatter_dimension=0, tiled=True),
        lax.psum_scatter(flat_gate, ("dp", "group"), scatter_dimension=0, tiled=True),
        lax.psum_scatter(flat_up, ("dp", "group"), scatter_dimension=0, tiled=True),
        lax.psum_scatter(flat_down, ("dp", "group"), scatter_dimension=0, tiled=True),
    )
    grads_local = jnp.concatenate(list(reduced), axis=0)
    gain_grads = lax.psum(
        jnp.concatenate(
            [
                grad_gain_input,
                grad_gain_attn,
                grad_gain_ffin,
                grad_gain_ffout,
                grad_gain_query,
                grad_gain_key,
            ]
        ),
        ("dp", "group"),
    )
    moment_first, moment_second, master_new = adam_update(
        grads_local, first_moment, second_moment, master, learn_rate, weight_decay
    )
    gain_moment_first, gain_moment_second, gains_new = adam_update(
        gain_grads, gain_first, gain_second, gains, gain_rate, 0.0
    )
    return (
        outputs.astype(jnp.bfloat16),
        grad_inputs.astype(jnp.bfloat16),
        moment_first,
        moment_second,
        master_new,
        gain_moment_first,
        gain_moment_second,
        gains_new,
    )


def solution(mesh):
    placed = (
        P(("dp", "group"), None),
        P("dp", None),
        P(("dp", "group"), None),
        P(("dp", "group"), None),
        P(("dp", "group"), None),
        P(("dp", "group"), None),
        P(),
        P(),
        P(),
    )
    return jax.shard_map(
        shards,
        mesh=mesh,
        in_specs=placed,
        out_specs=(
            P(("dp", "group"), None),
            P(("dp", "group"), None),
            P(("dp", "group"), None),
            P(("dp", "group"), None),
            P(("dp", "group"), None),
            P(),
            P(),
            P(),
        ),
        check_vma=False,
    )
```

```python
import functools
import math

import jax
import jax.numpy as jnp
from jax import lax
from jax.experimental import pallas as pl
from jax.experimental.pallas import tpu as pltpu
from jax.sharding import PartitionSpec as P

D = 640
HQ = 4
HD = 256
FF = 2048
WINDOW = 512
STEP = 10
ALL_AXES = ("dp", "group")


norm_eps = 1e-06
rope_base = 10000.0
beta_first = 0.9
beta_second = 0.999
learn_rate = 0.05
gain_rate = 0.25
adam_floor = 1e-08
weight_decay = 0.1


def shifted(value, axis, steps):
    count = lax.axis_size(axis)
    initial, last = (max(0, -steps), min(count, count - steps))
    return lax.ppermute(value, axis, [(source, source + steps) for source in range(initial, last)])


def rms_norm(values, weight_vec):
    return (
        values
        * lax.rsqrt(jnp.mean(values * values, axis=-1, keepdims=True) + norm_eps)
        * (1.0 + weight_vec)
    )


def positions(doc_row):
    length = doc_row.shape[0]
    counter = jnp.arange(length, dtype=jnp.int32)
    starts_here = jnp.concatenate([jnp.ones((1,), jnp.bool_), doc_row[1:] != doc_row[:-1]])
    begins = lax.cummax(jnp.where(starts_here, counter, jnp.zeros_like(counter)), axis=0)
    return counter - begins


def angles_of(places):
    half_dim = HD // 2
    frequency = rope_base ** (-(jnp.arange(half_dim, dtype=jnp.float32) * 2.0 / HD))
    return places.astype(jnp.float32)[:, None] * frequency[None, :]


def rotate(values, angles):
    half_dim = values.shape[-1] // 2
    first_half = values[..., :half_dim]
    second_half = values[..., half_dim:]
    cosine = jnp.cos(angles)
    sine_part = jnp.sin(angles)
    return jnp.concatenate(
        [
            first_half * cosine - second_half * sine_part,
            second_half * cosine + first_half * sine_part,
        ],
        axis=-1,
    )


def geglu(gate_in, up_in):
    return jax.nn.gelu(gate_in, approximate=True) * up_in


def adam_update(gradient, first_old, second_old, params_old, rate, decay_rate):
    first_new = beta_first * first_old + (1.0 - beta_first) * gradient
    second_new = beta_second * second_old + (1.0 - beta_second) * gradient * gradient
    first_hat = first_new / (1.0 - beta_first**STEP)
    second_hat = second_new / (1.0 - beta_second**STEP)
    params_new = params_old - rate * (
        first_hat / (jnp.sqrt(second_hat) + adam_floor) + decay_rate * params_old
    )
    return (first_new, second_new, params_new)


def piece_rows(device_count):
    return [
        entries // (128 * device_count)
        for entries in (D * HQ * HD, D * HD, D * HD, HQ * HD * D, D * FF, D * FF, FF * D)
    ]


def piece_shapes():
    return [(D, HQ * HD), (D, HD), (D, HD), (HQ * HD, D), (D, FF), (D, FF), (FF, D)]


def split_rows(stacked, row_list):
    result = []
    row_start = 0
    for row_count in row_list:
        result.append(stacked[row_start : row_start + row_count])
        row_start = row_start + row_count
    return result


def matmul(left_side, right_side):
    return jnp.dot(left_side, right_side, preferred_element_type=jnp.float32)


LOW_COUNT = 8
LANES = 128
LOW_MASKS = (0, 4, 2, 6, 1, 5, 3, 7)
GELU_SCALE = (2.0 / math.pi) ** 0.5
GELU_CUBE = 0.044715
VMEM_BYTES = 56 * 1024 * 1024


def aligned(device_count):
    groups = lax.axis_size("group") == 4
    return groups and device_count % LOW_COUNT == 0 and D % device_count == 0


def swap(value, mask):
    count = lax.axis_size(ALL_AXES)
    return lax.ppermute(value, ALL_AXES, [(source, source ^ mask) for source in range(count)])


def local_call(kernel, outs, operands, scratch=(), behind=()):
    specs = [pl.BlockSpec(memory_space=pltpu.SMEM)]
    specs = specs + [pl.BlockSpec(memory_space=pltpu.VMEM)] * len(operands)
    specs = specs + [pl.BlockSpec(memory_space=pl.ANY)] * len(behind)
    first, last = 1 + len(operands), 1 + len(operands) + len(behind)

    def body(*refs):
        kernel(*refs[:first], *refs[last:])

    return pl.pallas_call(
        body,
        out_shape=outs,
        in_specs=specs,
        out_specs=tuple(pl.BlockSpec(memory_space=pltpu.VMEM) for _ in outs),
        scratch_shapes=scratch,
        compiler_params=pltpu.CompilerParams(vmem_limit_bytes=VMEM_BYTES),
        cost_estimate=pl.CostEstimate(flops=0, bytes_accessed=0, transcendentals=0),
    )(lax.axis_index(ALL_AXES).astype(jnp.int32).reshape(1), *operands, *behind)


class Piece:
    def __init__(self, rows, columns, device_count):
        self.rows = rows
        self.columns = columns
        self.wide = rows == D
        self.blocks = columns // LANES
        self.own_rows = rows // device_count
        self.flat_rows = self.own_rows * self.blocks
        self.high_count = device_count // LOW_COUNT
        self.block_rows = self.own_rows * self.high_count
        self.size = self.block_rows * self.blocks


def copy_kernel(index_ref, in_ref, out_ref):
    out_ref[...] = in_ref[...]


def pack_kernel(pieces, index_ref, *refs):
    high_count = pieces[0].high_count
    parts, out_refs, flat, packed = refs[:high_count], refs[high_count:-2], refs[-2], refs[-1]
    high = index_ref[0] // LOW_COUNT
    for step, part in enumerate(parts):
        flat[high ^ step] = part[...].astype(jnp.float32)
    start, target = 0, 0
    for piece in pieces:
        for block in range(piece.blocks):
            for place in range(high_count):
                packed[pl.ds(target, piece.own_rows), :] = flat[
                    place, pl.ds(start + block, piece.own_rows, stride=piece.blocks), :
                ]
                target = target + piece.own_rows
        start = start + piece.flat_rows
    count = target // len(out_refs)
    for place, out_ref in enumerate(out_refs):
        out_ref[...] = packed[place * count : (place + 1) * count, :].astype(jnp.bfloat16)


def sum_one_kernel(size, index_ref, near_ref, far_ref, to_x_ref, to_y_ref):
    total = near_ref[...].astype(jnp.float32) + far_ref[...].astype(jnp.float32)
    half = size // 2
    to_x_ref[:half, :] = total[:half].astype(jnp.bfloat16)
    if total.shape[0] > size:
        to_x_ref[half:, :] = total[size:].astype(jnp.bfloat16)
    to_y_ref[...] = total[half:size].astype(jnp.bfloat16)


def sum_three_kernel(
    size,
    index_ref,
    near_ref,
    far_ref,
    *refs,
):
    key_refs = refs[:-5]
    own_ref, beside_first_ref, beside_second_ref, across_first_ref, across_second_ref = refs[-5:]
    half = size // 2
    if key_refs:
        across_key_ref, cores_key_ref = key_refs
        rows = across_key_ref.shape[0]
        keys = across_key_ref[...] + cores_key_ref[rows:, :].astype(jnp.float32)
        for block in range(keys.shape[1] // LANES):
            first = half + block * rows
            columns = slice(block * LANES, (block + 1) * LANES)
            across_second_ref[first : first + rows, :] = keys[:, columns].astype(jnp.bfloat16)
    outs = (beside_first_ref, beside_second_ref, across_first_ref, across_second_ref)
    total = near_ref[:size, :].astype(jnp.float32) + far_ref[:size, :].astype(jnp.float32)
    own_ref[...] = total.astype(jnp.bfloat16)
    for place, out_ref in enumerate(outs):
        rows = slice(size + place * half, size + (place + 1) * half)
        total = near_ref[rows, :].astype(jnp.float32) + far_ref[rows, :].astype(jnp.float32)
        out_ref[:half, :] = total.astype(jnp.bfloat16)


def sum_passed_kernel(
    size,
    index_ref,
    beside_ref,
    across_ref,
    over_x_ref,
    over_y_ref,
    near_one_ref,
    far_one_ref,
    beside_out_ref,
    across_out_ref,
    extra_ref,
):
    half = size // 2
    beside = beside_ref[...].astype(jnp.float32) + over_y_ref[...].astype(jnp.float32)
    beside_out_ref[...] = beside.astype(jnp.bfloat16)
    across = across_ref[...].astype(jnp.float32) + over_x_ref[:half, :].astype(jnp.float32)
    across_out_ref[:half, :] = across.astype(jnp.bfloat16)
    if across_out_ref.shape[0] > half:
        extra = near_one_ref[size:, :].astype(jnp.float32)
        extra = extra + far_one_ref[size:, :].astype(jnp.float32)
        extra = extra + over_x_ref[half:, :].astype(jnp.float32)
        extra_ref[...] = extra
        across_out_ref[half:, :] = extra.astype(jnp.bfloat16)
    else:
        extra_ref[...] = jnp.zeros(extra_ref.shape, jnp.float32)


def unpack_kernel(
    pieces,
    index_ref,
    own_ref,
    beside_first_ref,
    beside_second_ref,
    across_first_ref,
    across_second_ref,
    extra_ref,
    *refs,
):
    high_count = pieces[0].high_count
    half = sum(piece.size for piece in pieces) // 2
    flat_rows = sum(piece.flat_rows for piece in pieces)
    outs, flat, packed = refs[:-2], refs[-2], refs[-1]
    high = index_ref[0] // LOW_COUNT
    packed[:half, :] = (
        own_ref[:half, :].astype(jnp.float32)
        + beside_first_ref[...].astype(jnp.float32)
        + across_first_ref[:half, :].astype(jnp.float32)
    )
    packed[half:, :] = (
        own_ref[half:, :].astype(jnp.float32)
        + beside_second_ref[...].astype(jnp.float32)
        + across_second_ref[:half, :].astype(jnp.float32)
    )
    start, source = 0, 0
    for piece in pieces:
        for block in range(piece.blocks):
            for place in range(high_count):
                flat[place, pl.ds(start + block, piece.own_rows, stride=piece.blocks), :] = packed[
                    pl.ds(source, piece.own_rows), :
                ]
                source = source + piece.own_rows
        start = start + piece.flat_rows
    for step, out_ref in enumerate(outs):
        out_ref[:flat_rows, :] = flat[high ^ step].astype(out_ref.dtype)
        if out_ref.shape[0] > flat_rows:
            extra = extra_ref[...] + across_first_ref[half:, :].astype(jnp.float32)
            out_ref[flat_rows:, :] = extra.astype(out_ref.dtype)


def array(shape, kind):
    return jax.ShapeDtypeStruct(shape, kind)


def gather_high(rows):
    high_count = lax.axis_size(ALL_AXES) // LOW_COUNT
    return [rows] + [swap(rows, step * LOW_COUNT) for step in range(1, high_count)]


def gather_own(pieces, parts, count, behind=()):
    high_count = pieces[0].high_count
    size = sum(piece.size for piece in pieces)
    return local_call(
        functools.partial(pack_kernel, pieces),
        (array((size // count, LANES), jnp.bfloat16),) * count,
        parts,
        (
            pltpu.VMEM((high_count, parts[0].shape[0], LANES), jnp.float32),
            pltpu.VMEM((size, LANES), jnp.float32),
        ),
        behind,
    )


def copied(value, behind):
    return local_call(copy_kernel, (array(value.shape, jnp.bfloat16),), (value,), (), behind)[0]


def gather_halves(first, second):
    return swap(second, 4), swap(first, 2)


def gather_rest(first, second, beside_second, across_first, behind, behind_last):
    return (
        first,
        second,
        swap(copied(first, behind), 4),
        beside_second,
        across_first,
        swap(second, 2),
        swap(across_first, 4),
        swap(copied(beside_second, behind_last), 2),
    )


def gather_wholes(own):
    beside, across = swap(own, 4), swap(own, 2)
    return own, beside, across, swap(across, 4)


def gather_cores(near):
    return near + tuple(swap(value, 1) for value in near)


def scatter_cores(far_three, far_one):
    far_one = swap(far_one, 1)
    return swap(far_three, 1), far_one


def scatter_one(pieces, near_one, far_one, behind=()):
    half = sum(piece.size for piece in pieces) // 2
    to_x, to_y = local_call(
        functools.partial(sum_one_kernel, 2 * half),
        (
            array((near_one.shape[0] - half, LANES), jnp.bfloat16),
            array((half, LANES), jnp.bfloat16),
        ),
        (near_one, far_one),
        (),
        behind,
    )
    return swap(to_x, 4), swap(to_y, 2), to_y


def scatter_three(pieces, near_three, far_three, behind=(), keys=()):
    size = sum(piece.size for piece in pieces)
    half = size // 2
    own, beside_first, beside_second, across_first, across_second = local_call(
        functools.partial(sum_three_kernel, size),
        (
            array((size, LANES), jnp.bfloat16),
            *(array((half, LANES), jnp.bfloat16),) * 3,
            array((half + (keys[0].size // LANES if keys else 0), LANES), jnp.bfloat16),
        ),
        (near_three, far_three, *keys),
        (),
        behind,
    )
    return own, swap(beside_first, 4), beside_second, across_first, swap(across_second, 2)


def scatter_passed(pieces, threes, over_x, over_y, near_one, far_one, behind=()):
    size = sum(piece.size for piece in pieces)
    extra_count = near_one.shape[0] - size
    own, beside_first, beside_second, across_first, across_second = threes
    beside_second, across_first, extra = local_call(
        functools.partial(sum_passed_kernel, size),
        (
            array((size // 2, LANES), jnp.bfloat16),
            array((size // 2 + extra_count, LANES), jnp.bfloat16),
            array((max(extra_count, 8), LANES), jnp.float32),
        ),
        (beside_second, across_first, over_x, over_y, near_one, far_one),
        (),
        behind,
    )
    terms = (
        own,
        beside_first,
        swap(beside_second, 4),
        swap(across_first, 2),
        across_second,
        extra,
    )
    return terms, beside_second


def scatter_high(pieces, terms, behind=()):
    high_count = pieces[0].high_count
    size = sum(piece.size for piece in pieces)
    flat_rows = sum(piece.flat_rows for piece in pieces)
    out_rows = flat_rows + terms[3].shape[0] - size // 2
    outs = local_call(
        functools.partial(unpack_kernel, pieces),
        (array((out_rows, LANES), jnp.float32),)
        + (array((out_rows, LANES), jnp.bfloat16),) * (high_count - 1),
        terms,
        (
            pltpu.VMEM((high_count, flat_rows, LANES), jnp.float32),
            pltpu.VMEM((size, LANES), jnp.float32),
        ),
        behind,
    )
    arrived = [swap(send, step * LOW_COUNT) for step, send in enumerate(outs) if step]
    return outs[0] + sum(value.astype(jnp.float32) for value in arrived), outs[0], arrived


def norm_parts(values):
    scale = lax.rsqrt(jnp.mean(values * values, axis=-1, keepdims=True) + norm_eps)
    return scale, values * scale


def norm_back(scale, normal, upstream, weight_vec):
    weighted = upstream * (1.0 + weight_vec)
    inner = jnp.mean(weighted * normal, axis=-1, keepdims=True)
    return scale * (weighted - normal * inner), jnp.sum(normal * upstream, axis=0, keepdims=True)


def product(left_side, right_side, left_axis, right_axis):
    return lax.dot_general(
        left_side,
        right_side,
        (((left_axis,), (right_axis,)), ((), ())),
        preferred_element_type=jnp.float32,
    )


def unordered(rows_in, order_low):
    upper = rows_in.astype(jnp.bfloat16)
    lower = (rows_in - upper.astype(jnp.float32)).astype(jnp.bfloat16)
    return product(upper, order_low, 1, 1) + product(lower, order_low, 1, 1)


def weight_rows(refs, size, order, start, rows):
    count = len(refs) // LOW_COUNT
    part = size // count
    return refs[order * count + start // part][start % part : start % part + rows, :]


def put_rows(refs, size, order, start, rows):
    three, one = refs[:2] if order < 4 else refs[2:]
    if order % 4 == 3:
        one[start : start + rows.shape[0], :] = rows
    else:
        start = order % 4 * size + start
        three[start : start + rows.shape[0], :] = rows


def wide_tile(refs, size, start, rows):
    return jnp.concatenate(
        [weight_rows(refs, size, order, start, rows) for order in range(LOW_COUNT)]
    )


def put_wide_tile(refs, size, start, rows, tile):
    for order in range(LOW_COUNT):
        put_rows(refs, size, order, start, tile[order * rows : (order + 1) * rows])


def tall_rows(piece, low):
    for order, mask in enumerate(LOW_MASKS):
        for block in range(piece.blocks):
            for place in range(piece.high_count):
                row = (place * LOW_COUNT + (low ^ mask)) * piece.own_rows
                yield (
                    order,
                    block * piece.block_rows + place * piece.own_rows,
                    pl.ds(pl.multiple_of(row, piece.own_rows), piece.own_rows),
                    slice(block * LANES, (block + 1) * LANES),
                )


def ffn_kernel(
    gate_piece,
    down_piece,
    index_ref,
    middle_ref,
    cotangent_ref,
    gain_in_ref,
    gain_out_ref,
    order_ref,
    *refs,
):
    weight_refs, grad_refs = refs[:16], refs[20:24]
    block_out_ref, grad_middle_ref, grad_gain_in_ref, grad_gain_out_ref = refs[16:20]
    down_ref, hidden_ref, gelu_ref, slope_ref = refs[24:]
    low = index_ref[0] % LOW_COUNT
    rows = gate_piece.block_rows
    size = 2 * gate_piece.size + down_piece.size
    width = 2 * LANES
    for order, start, matrix_rows, columns in tall_rows(down_piece, low):
        start = start + 2 * gate_piece.size
        down_ref[matrix_rows, columns] = weight_rows(
            weight_refs, size, order, start, down_piece.own_rows
        )

    def wide_tiles(step):
        return [
            jnp.concatenate(
                [
                    wide_tile(weight_refs, size, offset + block * rows, rows)
                    for block in (2 * step, 2 * step + 1)
                ],
                axis=1,
            )
            for offset in (0, gate_piece.size)
        ]

    middle = middle_ref[...]
    scale_in, normal_in = norm_parts(middle)
    order_low = order_ref[...]
    normed = (normal_in * (1.0 + gain_in_ref[...])).astype(jnp.bfloat16)
    normed = product(normed, order_low, 1, 0).astype(jnp.bfloat16)
    for step in range(FF // width):
        columns = slice(step * width, (step + 1) * width)
        gate_weight, up_weight = wide_tiles(step)
        gate = product(normed, gate_weight, 1, 0)
        up = product(normed, up_weight, 1, 0)
        square = gate * gate
        bend = jnp.tanh(GELU_SCALE * gate * (1.0 + GELU_CUBE * square))
        half = 0.5 * (1.0 + bend)
        gelu = gate * half
        slope = half + 0.5 * gate * (1.0 - bend * bend) * GELU_SCALE * (
            1.0 + 3.0 * GELU_CUBE * square
        )
        gelu_ref[:, columns] = gelu
        slope_ref[:, columns] = slope * up
        hidden_ref[:, columns] = (gelu * up).astype(jnp.bfloat16)
    hidden = hidden_ref[...]
    scale_out, normal_out = norm_parts(product(hidden, down_ref[...], 1, 0))
    block_out_ref[...] = (middle + normal_out * (1.0 + gain_out_ref[...])).astype(jnp.bfloat16)
    upstream = cotangent_ref[...].astype(jnp.float32)
    grad_ffn, grad_gain_out_ref[...] = norm_back(
        scale_out, normal_out, upstream, gain_out_ref[...]
    )
    grad_ffn = grad_ffn.astype(jnp.bfloat16)
    grad_normed = jnp.zeros(middle.shape, jnp.float32)
    for step in range(FF // width):
        columns = slice(step * width, (step + 1) * width)
        grad_hidden = product(grad_ffn, down_ref[columns, :], 1, 1)
        down_ref[columns, :] = product(hidden_ref[:, columns], grad_ffn, 0, 0).astype(jnp.bfloat16)
        grads = [
            (grad_hidden * slope_ref[:, columns]).astype(jnp.bfloat16),
            (grad_hidden * gelu_ref[:, columns]).astype(jnp.bfloat16),
        ]
        for place, (grad, weight) in enumerate(zip(grads, wide_tiles(step))):
            grad_weight = product(normed, grad, 0, 0).astype(jnp.bfloat16)
            for side in range(2):
                put_wide_tile(
                    grad_refs,
                    size,
                    place * gate_piece.size + (2 * step + side) * rows,
                    rows,
                    grad_weight[:, side * LANES : (side + 1) * LANES],
                )
            grad_normed = grad_normed + product(grad, weight, 1, 1)
    for order, start, matrix_rows, columns in tall_rows(down_piece, low):
        start = start + 2 * gate_piece.size
        put_rows(grad_refs, size, order, start, down_ref[matrix_rows, columns])
    grad_middle, grad_gain_in_ref[...] = norm_back(
        scale_in, normal_in, unordered(grad_normed, order_low), gain_in_ref[...]
    )
    grad_middle_ref[...] = upstream + grad_middle


def grad_arrays(pieces, extra_count=0):
    size = sum(piece.size for piece in pieces)
    return (
        array((3 * size, LANES), jnp.bfloat16),
        array((size + extra_count, LANES), jnp.bfloat16),
    ) * 2


def ffn_blocks(pieces, middle, cotangent, gain_in, gain_out, order, blocks):
    rows = middle.shape[0]
    outs = local_call(
        functools.partial(ffn_kernel, pieces[4], pieces[6]),
        (
            array((rows, D), jnp.bfloat16),
            array((rows, D), jnp.float32),
            array((1, D), jnp.float32),
            array((1, D), jnp.float32),
            *grad_arrays(pieces[4:7]),
        ),
        (middle, cotangent, gain_in, gain_out, order, *blocks),
        (
            pltpu.VMEM((FF, D), jnp.bfloat16),
            pltpu.VMEM((rows, FF), jnp.bfloat16),
            pltpu.VMEM((rows, FF), jnp.float32),
            pltpu.VMEM((rows, FF), jnp.float32),
        ),
    )
    return *outs[:4], outs[4:]


def turn(values, cosine, sine):
    first_half, second_half = values[:, : HD // 2], values[:, HD // 2 :]
    return jnp.concatenate(
        [first_half * cosine - second_half * sine, second_half * cosine + first_half * sine], axis=1
    )


def wide_head(refs, size, start, rows):
    return jnp.concatenate(
        [wide_tile(refs, size, start + side * rows, rows) for side in range(2)], axis=1
    )


def head_starts(pieces):
    rows = pieces[0].block_rows
    return [2 * rows * head for head in range(HQ + 2)]


def project_kernel(
    pieces,
    index_ref,
    tokens_ref,
    gain_ref,
    gain_query_ref,
    gain_key_ref,
    cosine_ref,
    sine_ref,
    order_ref,
    *refs,
):
    weight_refs = refs[:8]
    normed_ref, query_proj_ref, key_proj_ref, query_ref, key_value_ref = refs[8:]
    size = sum(piece.size for piece in pieces)
    rows = pieces[0].block_rows
    cosine, sine = cosine_ref[...], sine_ref[...]
    _, normal = norm_parts(tokens_ref[...].astype(jnp.float32))
    normed = (normal * (1.0 + gain_ref[...])).astype(jnp.bfloat16)
    normed = product(normed, order_ref[...], 1, 0).astype(jnp.bfloat16)
    normed_ref[...] = normed
    starts = head_starts(pieces)
    for head, start in enumerate(starts):
        proj = product(normed, wide_head(weight_refs, size, start, rows), 1, 0)
        columns = slice(head * HD, (head + 1) * HD)
        if head == HQ + 1:
            key_value_ref[:, HD:] = proj.astype(jnp.bfloat16)
            continue
        gain_vec = gain_query_ref[...] if head < HQ else gain_key_ref[...]
        _, normal = norm_parts(proj)
        turned = turn(normal * (1.0 + gain_vec), cosine, sine).astype(jnp.bfloat16)
        if head < HQ:
            query_proj_ref[:, columns] = proj
            query_ref[:, columns] = turned
        else:
            key_proj_ref[...] = proj
            key_value_ref[:, :HD] = turned


def attend_kernel(
    pieces,
    index_ref,
    tokens_ref,
    gain_ref,
    allowed_ref,
    query_ref,
    *refs,
):
    weight_refs, key_value_refs = refs[:8], refs[8:-5]
    probs_ref, attended_ref, attn_out_ref, middle_ref, out_weight_ref = refs[-5:]
    out_piece = pieces[-1]
    low = index_ref[0] % LOW_COUNT
    size = sum(piece.size for piece in pieces)
    out_start = size - out_piece.size
    for order, start, matrix_rows, columns in tall_rows(out_piece, low):
        out_weight_ref[matrix_rows, columns] = weight_rows(
            weight_refs, size, order, start + out_start, out_piece.own_rows
        )
    rows = tokens_ref.shape[0]
    allowed = allowed_ref[...] > 0.0
    keys = jnp.concatenate([ref[:, :HD] for ref in key_value_refs])
    values = jnp.concatenate([ref[:, HD:] for ref in key_value_refs])
    count = keys.shape[0]
    for head in range(HQ):
        columns = slice(head * HD, (head + 1) * HD)
        scores = product(query_ref[:, columns], keys, 1, 1) * HD ** (-0.5)
        scores = jnp.where(allowed, scores, -1e30)
        raised = jnp.exp(scores - jnp.max(scores, axis=-1, keepdims=True))
        probs = raised / jnp.sum(raised, axis=-1, keepdims=True)
        probs_ref[:, head * count : (head + 1) * count] = probs
        attended_ref[:, columns] = product(probs.astype(jnp.bfloat16), values, 1, 0).astype(
            jnp.bfloat16
        )
    attn_out = product(attended_ref[...], out_weight_ref[...], 1, 0)
    attn_out_ref[...] = attn_out
    _, normal = norm_parts(attn_out)
    middle_ref[...] = tokens_ref[...].astype(jnp.float32) + normal * (1.0 + gain_ref[...])


def attend_back_kernel(
    index_ref,
    grad_middle_ref,
    attn_out_ref,
    gain_ref,
    out_weight_ref,
    attended_ref,
    probs_ref,
    query_ref,
    *refs,
):
    key_value_refs = refs[:4]
    grad_out_weight_ref, grad_query_ref, grad_gain_ref = refs[4:7]
    grad_own_ref, grad_across_ref, grad_cores_ref = refs[7:]
    rows = query_ref.shape[0]
    scale, normal = norm_parts(attn_out_ref[...])
    grad_attn, grad_gain_ref[...] = norm_back(scale, normal, grad_middle_ref[...], gain_ref[...])
    grad_attn = grad_attn.astype(jnp.bfloat16)
    grad_out_weight_ref[...] = product(attended_ref[...], grad_attn, 0, 0).astype(jnp.bfloat16)
    keys = jnp.concatenate([ref[:, :HD] for ref in key_value_refs])
    values = jnp.concatenate([ref[:, HD:] for ref in key_value_refs])
    count = keys.shape[0]
    grad_keys = jnp.zeros((count, HD), jnp.float32)
    grad_values = jnp.zeros((count, HD), jnp.float32)
    for head in range(HQ):
        columns = slice(head * HD, (head + 1) * HD)
        grad_attended = product(grad_attn, out_weight_ref[columns, :], 1, 1).astype(jnp.bfloat16)
        probs = probs_ref[:, head * count : (head + 1) * count]
        grad_probs = product(grad_attended, values, 1, 1)
        grad_values = grad_values + product(probs.astype(jnp.bfloat16), grad_attended, 0, 0)
        inner = jnp.sum(probs * grad_probs, axis=-1, keepdims=True)
        grad_scores = (probs * (grad_probs - inner) * HD ** (-0.5)).astype(jnp.bfloat16)
        grad_query_ref[:, columns] = product(grad_scores, keys, 1, 0)
        grad_keys = grad_keys + product(grad_scores, query_ref[:, columns], 0, 0)
    targets = (
        grad_own_ref,
        grad_cores_ref.at[:rows],
        grad_across_ref,
        grad_cores_ref.at[rows:],
    )
    for part, ref in enumerate(targets):
        ref[:, :HD] = grad_keys[part * rows : (part + 1) * rows].astype(ref.dtype)
        ref[:, HD:] = grad_values[part * rows : (part + 1) * rows].astype(ref.dtype)


def query_back_kernel(
    pieces,
    index_ref,
    gain_ref,
    cosine_ref,
    sine_ref,
    normed_ref,
    query_proj_ref,
    grad_query_ref,
    *refs,
):
    weight_refs = refs[:8]
    grad_weight_ref, grad_normed_ref, grad_gain_ref = refs[8:]
    size = sum(piece.size for piece in pieces)
    rows = pieces[0].block_rows
    cosine, sine = cosine_ref[...], sine_ref[...]
    normed = normed_ref[...]
    grad_normed = jnp.zeros(grad_normed_ref.shape, jnp.float32)
    grad_gain = jnp.zeros((1, HD), jnp.float32)
    for head, start in enumerate(head_starts(pieces)[:HQ]):
        columns = slice(head * HD, (head + 1) * HD)
        scale, normal = norm_parts(query_proj_ref[:, columns])
        upstream = turn(grad_query_ref[:, columns], cosine, -sine)
        grad, gain_row = norm_back(scale, normal, upstream, gain_ref[...])
        grad_gain = grad_gain + gain_row
        grad = grad.astype(jnp.bfloat16)
        weight = wide_head(weight_refs, size, start, rows)
        grad_normed = grad_normed + product(grad, weight, 1, 1)
        grad_weight_ref[:, columns] = product(normed, grad, 0, 0).astype(jnp.bfloat16)
    grad_normed_ref[...] = grad_normed
    grad_gain_ref[...] = grad_gain


def project_back_kernel(
    pieces,
    index_ref,
    tokens_ref,
    gain_ref,
    gain_key_ref,
    cosine_ref,
    sine_ref,
    order_ref,
    normed_ref,
    key_proj_ref,
    grad_normed_ref,
    grad_middle_ref,
    gain_attn_ref,
    gain_ffin_ref,
    gain_ffout_ref,
    gain_query_ref,
    own_key_ref,
    cores_key_ref,
    across_key_ref,
    *refs,
):
    weight_refs = refs[:8]
    grad_weight_ref, input_grad_ref, grad_gain_ref = refs[8:]
    size = sum(piece.size for piece in pieces)
    rows = pieces[0].block_rows
    normed = normed_ref[...]
    key_rows = own_key_ref.shape[0]
    first = across_key_ref.shape[0] - 4 * key_rows
    key_value = own_key_ref[...] + cores_key_ref[:key_rows, :].astype(jnp.float32)
    key_value = key_value + jnp.concatenate(
        [
            across_key_ref[first + block * key_rows : first + (block + 1) * key_rows, :].astype(
                jnp.float32
            )
            for block in range(4)
        ],
        axis=1,
    )
    scale, normal = norm_parts(key_proj_ref[...])
    upstream = turn(key_value[:, :HD], cosine_ref[...], -sine_ref[...])
    grad_key, grad_gain_key = norm_back(scale, normal, upstream, gain_key_ref[...])
    grad_normed = grad_normed_ref[...]
    for place, start in enumerate(head_starts(pieces)[HQ:]):
        grad = (key_value[:, HD:] if place else grad_key).astype(jnp.bfloat16)
        weight = wide_head(weight_refs, size, start, rows)
        grad_normed = grad_normed + product(grad, weight, 1, 1)
        grad_weight_ref[:, place * HD : (place + 1) * HD] = product(normed, grad, 0, 0).astype(
            jnp.bfloat16
        )
    scale, normal = norm_parts(tokens_ref[...].astype(jnp.float32))
    grad_inputs, grad_gain_input = norm_back(
        scale, normal, unordered(grad_normed, order_ref[...]), gain_ref[...]
    )
    input_grad_ref[...] = (grad_middle_ref[...] + grad_inputs).astype(jnp.bfloat16)
    grad_gains = [
        grad_gain_input,
        gain_attn_ref[...],
        gain_ffin_ref[...],
        gain_ffout_ref[...],
        gain_query_ref[...],
        grad_gain_key,
    ]
    row = 0
    grad_gain_ref[...] = jnp.zeros(grad_gain_ref.shape, jnp.float32)
    for values in grad_gains:
        for start in range(0, values.shape[1], LANES):
            grad_gain_ref[row : row + 1, :] = values[:, start : start + LANES]
            row = row + 1


def split_kernel(
    pieces,
    index_ref,
    query_ref,
    key_value_ref,
    out_ref,
    gain_ref,
    *grad_refs,
):
    low = index_ref[0] % LOW_COUNT
    size = sum(piece.size for piece in pieces)
    rows = pieces[0].block_rows
    start = 0
    for matrix_ref in (query_ref, key_value_ref):
        for column in range(0, matrix_ref.shape[1], LANES):
            tile = matrix_ref[:, column : column + LANES]
            put_wide_tile(grad_refs, size, start, rows, tile)
            start = start + rows
    out_piece = pieces[-1]
    for order, first, matrix_rows, columns in tall_rows(out_piece, low):
        put_rows(grad_refs, size, order, start + first, out_ref[matrix_rows, columns])
    for target in (grad_refs[1], grad_refs[3]):
        target[size:, :] = gain_ref[...].astype(jnp.bfloat16)


def width_order(device_count):
    low = lax.axis_index(ALL_AXES) % LOW_COUNT
    rows = D // device_count
    high_count = device_count // LOW_COUNT
    column = jnp.arange(D, dtype=jnp.int32)
    place = column // (rows * high_count)
    mask = (place & 1) * 4 + ((place >> 1) & 1) * 2 + (place >> 2)
    high = (column // rows) % high_count
    picked = (high * LOW_COUNT + (low ^ mask)) * rows + column % rows
    return (jnp.arange(D, dtype=jnp.int32)[:, None] == picked[None, :]).astype(jnp.bfloat16)


GAIN_ROWS = 32


def shards_blocks(
    device_count,
    tokens,
    doc_ids,
    cotangent,
    master,
    first_moment,
    second_moment,
    gains,
    gain_first,
    gain_second,
):
    pieces = [Piece(*shape_pair, device_count) for shape_pair in piece_shapes()]
    attention_pieces = pieces[:4]
    local_rows = tokens.shape[0]
    group_size = lax.axis_size("group")
    first_row = lax.axis_index("group") * local_rows
    attention_rows = sum(piece.flat_rows for piece in attention_pieces)
    ffn_pieces = pieces[4:7]
    rounded = master.astype(jnp.bfloat16)
    attention_parts = gather_high(rounded[:attention_rows])
    ffn_rows = rounded[attention_rows:]
    ffn_parts = gather_high(ffn_rows)
    attention_near = gather_wholes(
        *gather_own(attention_pieces, attention_parts, 1, (ffn_parts[1],))
    )
    attention_blocks = gather_cores(attention_near)
    ffn_own = gather_own(ffn_pieces, ffn_parts, 2, attention_near[1:])
    ffn_passed = gather_halves(*ffn_own)
    gain_parts = []
    for start, width in ((0, D), (D, D), (2 * D, D), (3 * D, D), (4 * D, HD), (4 * D + HD, HD)):
        gain_parts.append(gains[start : start + width][None])
    gain_input, gain_attn, gain_ffin, gain_ffout, gain_query, gain_key = gain_parts
    order = width_order(device_count)
    doc_row = doc_ids[0]
    angles = lax.dynamic_slice_in_dim(angles_of(positions(doc_row)), first_row, local_rows, 0)
    cosine, sine = jnp.cos(angles), jnp.sin(angles)
    query_docs = lax.dynamic_slice_in_dim(doc_row, first_row, local_rows, 0)
    key_count = group_size * local_rows
    first_keys = [(lax.axis_index("group") ^ step) * local_rows for step in range(group_size)]
    key_docs = jnp.concatenate(
        [lax.dynamic_slice_in_dim(doc_row, start, local_rows, 0) for start in first_keys]
    )
    key_index = jnp.concatenate(
        [start + jnp.arange(local_rows, dtype=jnp.int32) for start in first_keys]
    )
    query_index = first_row + jnp.arange(local_rows, dtype=jnp.int32)
    distance = query_index[:, None] - key_index[None, :]
    allowed = (distance >= 0) & (distance < WINDOW) & (key_docs[None, :] == query_docs[:, None])
    allowed = allowed.astype(jnp.float32)

    width = HQ * HD
    normed, query_proj, key_proj, query_rot, key_value = local_call(
        functools.partial(project_kernel, attention_pieces),
        (
            array((local_rows, D), jnp.bfloat16),
            array((local_rows, width), jnp.float32),
            array((local_rows, HD), jnp.float32),
            array((local_rows, width), jnp.bfloat16),
            array((local_rows, 2 * HD), jnp.bfloat16),
        ),
        (tokens, gain_input, gain_query, gain_key, cosine, sine, order, *attention_blocks),
    )
    key_values = [key_value] + [swap(key_value, step) for step in range(1, group_size)]
    ffn_weights = gather_cores(
        gather_rest(*ffn_own, *ffn_passed, (key_value,), key_values[1:])
    )
    probs, attended, attn_out, middle, out_weight = local_call(
        functools.partial(attend_kernel, attention_pieces),
        (
            array((local_rows, HQ * key_count), jnp.float32),
            array((local_rows, width), jnp.bfloat16),
            array((local_rows, D), jnp.float32),
            array((local_rows, D), jnp.float32),
            array((width, D), jnp.bfloat16),
        ),
        (tokens, gain_attn, allowed, query_rot, *attention_blocks, *key_values),
    )
    outputs, grad_middle, grad_gain_ffin, grad_gain_ffout, grads_ffn = ffn_blocks(
        pieces, middle, cotangent, gain_ffin, gain_ffout, order, ffn_weights
    )
    near_three, near_one, far_three, far_one = grads_ffn
    far_three, far_one = scatter_cores(far_three, far_one)
    grad_out_weight, grad_query, grad_gain_attn, own_key, across_key, cores_key = local_call(
        attend_back_kernel,
        (
            array((width, D), jnp.bfloat16),
            array((local_rows, width), jnp.float32),
            array((1, D), jnp.float32),
            array((local_rows, 2 * HD), jnp.float32),
            array((local_rows, 2 * HD), jnp.float32),
            array((2 * local_rows, 2 * HD), jnp.bfloat16),
        ),
        (
            grad_middle,
            attn_out,
            gain_attn,
            out_weight,
            attended,
            probs,
            query_rot,
            *key_values,
        ),
    )
    cores_key = swap(cores_key, 1)
    over_x, over_y, sent = scatter_one(ffn_pieces, near_one, far_one, (grad_query,))
    threes = scatter_three(ffn_pieces, near_three, far_three, (sent,), (across_key, cores_key))
    grad_query_weight, grad_normed, grad_gain_query = local_call(
        functools.partial(query_back_kernel, attention_pieces),
        (
            array((D, width), jnp.bfloat16),
            array((local_rows, D), jnp.float32),
            array((1, HD), jnp.float32),
        ),
        (gain_query, cosine, sine, normed, query_proj, grad_query, *attention_blocks),
        (),
        (threes[0],),
    )
    ffn_terms, sent = scatter_passed(
        ffn_pieces, threes, over_x, over_y, near_one, far_one, (grad_normed,)
    )
    grad_key_weight, grad_inputs, grad_gains = local_call(
        functools.partial(project_back_kernel, attention_pieces),
        (
            array((D, 2 * HD), jnp.bfloat16),
            array((local_rows, D), jnp.bfloat16),
            array((GAIN_ROWS, LANES), jnp.float32),
        ),
        (
            tokens,
            gain_input,
            gain_key,
            cosine,
            sine,
            order,
            normed,
            key_proj,
            grad_normed,
            grad_middle,
            grad_gain_attn,
            grad_gain_ffin,
            grad_gain_ffout,
            grad_gain_query,
            own_key,
            cores_key,
            threes[4],
            *attention_blocks,
        ),
        (),
        (sent, threes[1]),
    )
    grads_ffn, sent, arrived = scatter_high(ffn_pieces, ffn_terms, (grad_inputs,))
    near_three, near_one, far_three, far_one = local_call(
        functools.partial(split_kernel, attention_pieces),
        grad_arrays(attention_pieces, GAIN_ROWS),
        (grad_query_weight, grad_key_weight, grad_out_weight, grad_gains),
        (),
        (sent,),
    )
    far_three, far_one = scatter_cores(far_three, far_one)
    over_x, over_y, sent = scatter_one(attention_pieces, near_one, far_one)
    threes = scatter_three(attention_pieces, near_three, far_three, (sent,))
    terms, _ = scatter_passed(
        attention_pieces, threes, over_x, over_y, near_one, far_one, (arrived[0],)
    )
    grads_attention, _, _ = scatter_high(attention_pieces, terms, arrived)
    gain_grads = grads_attention[attention_rows:].reshape(-1)[: gains.shape[0]]
    grads_local = jnp.concatenate([grads_attention[:attention_rows], grads_ffn])
    return (
        outputs,
        grad_inputs,
        *adam_update(grads_local, first_moment, second_moment, master, learn_rate, weight_decay),
        *adam_update(gain_grads, gain_first, gain_second, gains, gain_rate, 0.0),
    )


def shards(
    tokens, doc_ids, cotangent, master, first_moment, second_moment, gains, gain_first, gain_second
):
    group_size = lax.axis_size("group")
    devices_all = lax.axis_size("dp") * group_size
    if aligned(devices_all):
        return shards_blocks(
            devices_all,
            tokens,
            doc_ids,
            cotangent,
            master,
            first_moment,
            second_moment,
            gains,
            gain_first,
            gain_second,
        )
    group_index = lax.axis_index("group")
    local_rows = tokens.shape[0]
    shard_parts = [
        part_rows.astype(jnp.bfloat16) for part_rows in split_rows(master, piece_rows(devices_all))
    ]
    gathered = (
        lax.all_gather(shard_parts[0], ("dp", "group"), axis=0, tiled=True),
        lax.all_gather(shard_parts[1], ("dp", "group"), axis=0, tiled=True),
        lax.all_gather(shard_parts[2], ("dp", "group"), axis=0, tiled=True),
        lax.all_gather(shard_parts[3], ("dp", "group"), axis=0, tiled=True),
        lax.all_gather(shard_parts[4], ("dp", "group"), axis=0, tiled=True),
        lax.all_gather(shard_parts[5], ("dp", "group"), axis=0, tiled=True),
        lax.all_gather(shard_parts[6], ("dp", "group"), axis=0, tiled=True),
    )
    query_weight, key_weight, value_weight, out_weight, gate_weight, up_weight, down_weight = [
        full_rows.reshape(shape_pair) for full_rows, shape_pair in zip(gathered, piece_shapes())
    ]
    norm_input = gains[0:D]
    norm_attn = gains[D : 2 * D]
    norm_ffin = gains[2 * D : 3 * D]
    norm_ffout = gains[3 * D : 4 * D]
    norm_query = gains[4 * D : 4 * D + HD]
    norm_key = gains[4 * D + HD : 4 * D + 2 * HD]
    doc_row = doc_ids[0]
    first_row = group_index * local_rows
    angles = lax.dynamic_slice_in_dim(angles_of(positions(doc_row)), first_row, local_rows, 0)
    query_docs = lax.dynamic_slice_in_dim(doc_row, first_row, local_rows, 0)
    inputs = tokens.astype(jnp.float32)
    normed, back_input = jax.vjp(rms_norm, inputs, norm_input)
    normed_low = normed.astype(jnp.bfloat16)
    query_proj = matmul(normed_low, query_weight)
    key_proj = matmul(normed_low, key_weight)
    value_proj = matmul(normed_low, value_weight)

    def query_prep(flat_rows, gain_vec):
        return rotate(rms_norm(flat_rows.reshape(local_rows, HQ, HD), gain_vec), angles[:, None, :])

    def key_prep(rows_in, gain_vec):
        return rotate(rms_norm(rows_in, gain_vec), angles)

    query_rot, back_query = jax.vjp(query_prep, query_proj, norm_query)
    key_rot, back_key = jax.vjp(key_prep, key_proj, norm_key)
    query_low = query_rot.astype(jnp.bfloat16)
    key_low = key_rot.astype(jnp.bfloat16)
    value_low = value_proj.astype(jnp.bfloat16)
    reach = min(-(-(WINDOW - 1) // local_rows), group_size - 1)
    key_list = [key_low]
    value_list = [value_low]
    for offset in range(1, reach + 1):
        key_far, value_far = shifted((key_low, value_low), "group", offset)
        key_list.insert(0, key_far)
        value_list.insert(0, value_far)
    key_all = jnp.concatenate(key_list, axis=0)
    value_all = jnp.concatenate(value_list, axis=0)
    key_count = (reach + 1) * local_rows
    doc_pad = jnp.concatenate([jnp.full((reach * local_rows,), -1, jnp.int32), doc_row])
    key_docs = lax.dynamic_slice_in_dim(doc_pad, first_row, key_count, 0)
    key_index = (group_index - reach) * local_rows + jnp.arange(key_count, dtype=jnp.int32)
    query_index = first_row + jnp.arange(local_rows, dtype=jnp.int32)
    distance = query_index[:, None] - key_index[None, :]
    allowed = (distance >= 0) & (distance < WINDOW) & (key_docs[None, :] == query_docs[:, None])

    def scores_of(key_rows_low):
        raw_scores = jnp.einsum(
            "qhd,kd->hqk", query_low, key_rows_low, preferred_element_type=jnp.float32
        ) * HD ** (-0.5)
        return jnp.where(allowed[None], raw_scores, -1e30)

    masked = scores_of(key_all)
    top_score = jnp.max(masked, axis=-1, keepdims=True)
    log_total = top_score + jnp.log(jnp.sum(jnp.exp(masked - top_score), axis=-1, keepdims=True))
    probs = jnp.exp(masked - log_total)
    attended = jnp.einsum(
        "hqk,kd->qhd", probs.astype(jnp.bfloat16), value_all, preferred_element_type=jnp.float32
    )
    attended_low = attended.reshape(local_rows, HQ * HD).astype(jnp.bfloat16)
    attn_out = matmul(attended_low, out_weight)
    branch_one, back_attn = jax.vjp(rms_norm, attn_out, norm_attn)
    middle = inputs + branch_one
    normed_two, back_ffin = jax.vjp(rms_norm, middle, norm_ffin)
    normed_two_low = normed_two.astype(jnp.bfloat16)
    gate_proj = matmul(normed_two_low, gate_weight)
    up_proj = matmul(normed_two_low, up_weight)
    hidden, back_hidden = jax.vjp(geglu, gate_proj, up_proj)
    hidden_low = hidden.astype(jnp.bfloat16)
    ffn_out = matmul(hidden_low, down_weight)
    branch_two, back_ffout = jax.vjp(rms_norm, ffn_out, norm_ffout)
    outputs = middle + branch_two
    grad_out = cotangent.astype(jnp.float32)
    grad_ffn, grad_gain_ffout = back_ffout(grad_out)
    grad_ffn_low = grad_ffn.astype(jnp.bfloat16)
    grad_down_w = jnp.einsum(
        "tf,td->fd", hidden_low, grad_ffn_low, preferred_element_type=jnp.float32
    )
    grad_hidden = jnp.einsum(
        "td,fd->tf", grad_ffn_low, down_weight, preferred_element_type=jnp.float32
    )
    grad_gate, grad_up = back_hidden(grad_hidden)
    grad_gate_low = grad_gate.astype(jnp.bfloat16)
    grad_up_low = grad_up.astype(jnp.bfloat16)
    grad_gate_w = jnp.einsum(
        "td,tf->df", normed_two_low, grad_gate_low, preferred_element_type=jnp.float32
    )
    grad_up_w = jnp.einsum(
        "td,tf->df", normed_two_low, grad_up_low, preferred_element_type=jnp.float32
    )
    grad_normed_two = jnp.einsum(
        "tf,df->td", grad_gate_low, gate_weight, preferred_element_type=jnp.float32
    ) + jnp.einsum("tf,df->td", grad_up_low, up_weight, preferred_element_type=jnp.float32)
    grad_middle_norm, grad_gain_ffin = back_ffin(grad_normed_two)
    grad_middle = grad_out + grad_middle_norm
    grad_attn, grad_gain_attn = back_attn(grad_middle)
    grad_attn_low = grad_attn.astype(jnp.bfloat16)
    grad_out_w = jnp.einsum(
        "to,td->od", attended_low, grad_attn_low, preferred_element_type=jnp.float32
    )
    grad_attended = jnp.einsum(
        "td,od->to", grad_attn_low, out_weight, preferred_element_type=jnp.float32
    )
    grad_attended_low = grad_attended.astype(jnp.bfloat16).reshape(local_rows, HQ, HD)
    probs_again = jnp.exp(scores_of(key_all) - log_total)
    grad_probs = jnp.einsum(
        "qhd,kd->hqk", grad_attended_low, value_all, preferred_element_type=jnp.float32
    )
    grad_value_all = jnp.einsum(
        "hqk,qhd->kd",
        probs_again.astype(jnp.bfloat16),
        grad_attended_low,
        preferred_element_type=jnp.float32,
    )
    grad_scores = probs_again * (
        grad_probs - jnp.sum(probs_again * grad_probs, axis=-1, keepdims=True)
    )
    grad_scores_low = (grad_scores * HD ** (-0.5)).astype(jnp.bfloat16)
    grad_query = jnp.einsum(
        "hqk,kd->qhd", grad_scores_low, key_all, preferred_element_type=jnp.float32
    )
    grad_key_all = jnp.einsum(
        "hqk,qhd->kd", grad_scores_low, query_low, preferred_element_type=jnp.float32
    )
    key_total = grad_key_all[reach * local_rows :]
    value_total = grad_value_all[reach * local_rows :]
    for offset in range(1, reach + 1):
        row_start = (reach - offset) * local_rows
        key_back, value_back = (
            shifted(
                grad_key_all[row_start : row_start + local_rows].astype(jnp.bfloat16),
                "group",
                -offset,
            ).astype(jnp.float32),
            shifted(
                grad_value_all[row_start : row_start + local_rows].astype(jnp.bfloat16),
                "group",
                -offset,
            ).astype(jnp.float32),
        )
        key_total = key_total + key_back
        value_total = value_total + value_back
    grad_query_proj, grad_gain_query = back_query(grad_query)
    grad_key_proj, grad_gain_key = back_key(key_total)
    grad_query_low = grad_query_proj.astype(jnp.bfloat16)
    grad_key_low = grad_key_proj.astype(jnp.bfloat16)
    grad_value_low = value_total.astype(jnp.bfloat16)
    grad_query_w = jnp.einsum(
        "td,te->de", normed_low, grad_query_low, preferred_element_type=jnp.float32
    )
    grad_key_w = jnp.einsum(
        "td,te->de", normed_low, grad_key_low, preferred_element_type=jnp.float32
    )
    grad_value_w = jnp.einsum(
        "td,te->de", normed_low, grad_value_low, preferred_element_type=jnp.float32
    )
    grad_normed = jnp.einsum(
        "te,de->td", grad_query_low, query_weight, preferred_element_type=jnp.float32
    )
    grad_normed = grad_normed + jnp.einsum(
        "te,de->td", grad_key_low, key_weight, preferred_element_type=jnp.float32
    )
    grad_normed = grad_normed + jnp.einsum(
        "te,de->td", grad_value_low, value_weight, preferred_element_type=jnp.float32
    )
    grad_input_norm, grad_gain_input = back_input(grad_normed)
    grad_inputs = grad_middle + grad_input_norm
    flat_query = grad_query_w.reshape(-1, 128)
    flat_key = grad_key_w.reshape(-1, 128)
    flat_value = grad_value_w.reshape(-1, 128)
    flat_out = grad_out_w.reshape(-1, 128)
    flat_gate = grad_gate_w.reshape(-1, 128)
    flat_up = grad_up_w.reshape(-1, 128)
    flat_down = grad_down_w.reshape(-1, 128)
    reduced = (
        lax.psum_scatter(flat_query, ("dp", "group"), scatter_dimension=0, tiled=True),
        lax.psum_scatter(flat_key, ("dp", "group"), scatter_dimension=0, tiled=True),
        lax.psum_scatter(flat_value, ("dp", "group"), scatter_dimension=0, tiled=True),
        lax.psum_scatter(flat_out, ("dp", "group"), scatter_dimension=0, tiled=True),
        lax.psum_scatter(flat_gate, ("dp", "group"), scatter_dimension=0, tiled=True),
        lax.psum_scatter(flat_up, ("dp", "group"), scatter_dimension=0, tiled=True),
        lax.psum_scatter(flat_down, ("dp", "group"), scatter_dimension=0, tiled=True),
    )
    grads_local = jnp.concatenate(list(reduced), axis=0)
    gain_grads = lax.psum(
        jnp.concatenate(
            [
                grad_gain_input,
                grad_gain_attn,
                grad_gain_ffin,
                grad_gain_ffout,
                grad_gain_query,
                grad_gain_key,
            ]
        ),
        ("dp", "group"),
    )
    moment_first, moment_second, master_new = adam_update(
        grads_local, first_moment, second_moment, master, learn_rate, weight_decay
    )
    gain_moment_first, gain_moment_second, gains_new = adam_update(
        gain_grads, gain_first, gain_second, gains, gain_rate, 0.0
    )
    return (
        outputs.astype(jnp.bfloat16),
        grad_inputs.astype(jnp.bfloat16),
        moment_first,
        moment_second,
        master_new,
        gain_moment_first,
        gain_moment_second,
        gains_new,
    )


def solution(mesh):
    placed = (
        P(("dp", "group"), None),
        P("dp", None),
        P(("dp", "group"), None),
        P(("dp", "group"), None),
        P(("dp", "group"), None),
        P(("dp", "group"), None),
        P(),
        P(),
        P(),
    )
    return jax.shard_map(
        shards,
        mesh=mesh,
        in_specs=placed,
        out_specs=(
            P(("dp", "group"), None),
            P(("dp", "group"), None),
            P(("dp", "group"), None),
            P(("dp", "group"), None),
            P(("dp", "group"), None),
            P(),
            P(),
            P(),
        ),
        check_vma=False,
    )
```

```python
import functools
import math

import jax
import jax.numpy as jnp
from jax import lax
from jax.experimental import pallas as pl
from jax.experimental.pallas import tpu as pltpu
from jax.sharding import PartitionSpec as P

D = 640
HQ = 4
HD = 256
FF = 2048
WINDOW = 512
STEP = 10
ALL_AXES = ("dp", "group")


norm_eps = 1e-06
rope_base = 10000.0
beta_first = 0.9
beta_second = 0.999
learn_rate = 0.05
gain_rate = 0.25
adam_floor = 1e-08
weight_decay = 0.1


def shifted(value, axis, steps):
    count = lax.axis_size(axis)
    initial, last = (max(0, -steps), min(count, count - steps))
    return lax.ppermute(value, axis, [(source, source + steps) for source in range(initial, last)])


def rms_norm(values, weight_vec):
    return (
        values
        * lax.rsqrt(jnp.mean(values * values, axis=-1, keepdims=True) + norm_eps)
        * (1.0 + weight_vec)
    )


def positions(doc_row):
    length = doc_row.shape[0]
    counter = jnp.arange(length, dtype=jnp.int32)
    starts_here = jnp.concatenate([jnp.ones((1,), jnp.bool_), doc_row[1:] != doc_row[:-1]])
    begins = lax.cummax(jnp.where(starts_here, counter, jnp.zeros_like(counter)), axis=0)
    return counter - begins


def angles_of(places):
    half_dim = HD // 2
    frequency = rope_base ** (-(jnp.arange(half_dim, dtype=jnp.float32) * 2.0 / HD))
    return places.astype(jnp.float32)[:, None] * frequency[None, :]


def rotate(values, angles):
    half_dim = values.shape[-1] // 2
    first_half = values[..., :half_dim]
    second_half = values[..., half_dim:]
    cosine = jnp.cos(angles)
    sine_part = jnp.sin(angles)
    return jnp.concatenate(
        [
            first_half * cosine - second_half * sine_part,
            second_half * cosine + first_half * sine_part,
        ],
        axis=-1,
    )


def geglu(gate_in, up_in):
    return jax.nn.gelu(gate_in, approximate=True) * up_in


def adam_update(gradient, first_old, second_old, params_old, rate, decay_rate):
    first_new = beta_first * first_old + (1.0 - beta_first) * gradient
    second_new = beta_second * second_old + (1.0 - beta_second) * gradient * gradient
    first_hat = first_new / (1.0 - beta_first**STEP)
    second_hat = second_new / (1.0 - beta_second**STEP)
    params_new = params_old - rate * (
        first_hat / (jnp.sqrt(second_hat) + adam_floor) + decay_rate * params_old
    )
    return (first_new, second_new, params_new)


def piece_rows(device_count):
    return [
        entries // (128 * device_count)
        for entries in (D * HQ * HD, D * HD, D * HD, HQ * HD * D, D * FF, D * FF, FF * D)
    ]


def piece_shapes():
    return [(D, HQ * HD), (D, HD), (D, HD), (HQ * HD, D), (D, FF), (D, FF), (FF, D)]


def split_rows(stacked, row_list):
    result = []
    row_start = 0
    for row_count in row_list:
        result.append(stacked[row_start : row_start + row_count])
        row_start = row_start + row_count
    return result


def matmul(left_side, right_side):
    return jnp.dot(left_side, right_side, preferred_element_type=jnp.float32)


LOW_COUNT = 8
LANES = 128
LOW_MASKS = (0, 4, 2, 6, 1, 5, 3, 7)
GELU_SCALE = (2.0 / math.pi) ** 0.5
GELU_CUBE = 0.044715
VMEM_BYTES = 56 * 1024 * 1024


def aligned(device_count):
    groups = lax.axis_size("group") == 4
    return groups and device_count % LOW_COUNT == 0 and D % device_count == 0


def swap(value, mask):
    count = lax.axis_size(ALL_AXES)
    return lax.ppermute(value, ALL_AXES, [(source, source ^ mask) for source in range(count)])


def local_call(kernel, outs, operands, scratch=(), behind=()):
    specs = [pl.BlockSpec(memory_space=pltpu.SMEM)]
    specs = specs + [pl.BlockSpec(memory_space=pltpu.VMEM)] * len(operands)
    specs = specs + [pl.BlockSpec(memory_space=pl.ANY)] * len(behind)
    first, last = 1 + len(operands), 1 + len(operands) + len(behind)

    def body(*refs):
        kernel(*refs[:first], *refs[last:])

    return pl.pallas_call(
        body,
        out_shape=outs,
        in_specs=specs,
        out_specs=tuple(pl.BlockSpec(memory_space=pltpu.VMEM) for _ in outs),
        scratch_shapes=scratch,
        compiler_params=pltpu.CompilerParams(vmem_limit_bytes=VMEM_BYTES),
        cost_estimate=pl.CostEstimate(flops=0, bytes_accessed=0, transcendentals=0),
    )(lax.axis_index(ALL_AXES).astype(jnp.int32).reshape(1), *operands, *behind)


class Piece:
    def __init__(self, rows, columns, device_count):
        self.rows = rows
        self.columns = columns
        self.wide = rows == D
        self.blocks = columns // LANES
        self.own_rows = rows // device_count
        self.flat_rows = self.own_rows * self.blocks
        self.high_count = device_count // LOW_COUNT
        self.block_rows = self.own_rows * self.high_count
        self.size = self.block_rows * self.blocks


def copy_kernel(index_ref, in_ref, out_ref):
    out_ref[...] = in_ref[...]


def pack_kernel(pieces, index_ref, *refs):
    high_count = pieces[0].high_count
    parts, out_refs, flat, packed = refs[:high_count], refs[high_count:-2], refs[-2], refs[-1]
    high = index_ref[0] // LOW_COUNT
    for step, part in enumerate(parts):
        flat[high ^ step] = part[...].astype(jnp.float32)
    start, target = 0, 0
    for piece in pieces:
        for block in range(piece.blocks):
            for place in range(high_count):
                packed[pl.ds(target, piece.own_rows), :] = flat[
                    place, pl.ds(start + block, piece.own_rows, stride=piece.blocks), :
                ]
                target = target + piece.own_rows
        start = start + piece.flat_rows
    count = target // len(out_refs)
    for place, out_ref in enumerate(out_refs):
        out_ref[...] = packed[place * count : (place + 1) * count, :].astype(jnp.bfloat16)


def sum_one_kernel(size, index_ref, near_ref, far_ref, to_x_ref, to_y_ref):
    total = near_ref[...].astype(jnp.float32) + far_ref[...].astype(jnp.float32)
    half = size // 2
    to_x_ref[:half, :] = total[:half].astype(jnp.bfloat16)
    if total.shape[0] > size:
        to_x_ref[half:, :] = total[size:].astype(jnp.bfloat16)
    to_y_ref[...] = total[half:size].astype(jnp.bfloat16)


def sum_three_kernel(
    size,
    index_ref,
    near_ref,
    far_ref,
    *refs,
):
    key_refs = refs[:-5]
    own_ref, beside_first_ref, beside_second_ref, across_first_ref, across_second_ref = refs[-5:]
    half = size // 2
    if key_refs:
        across_key_ref, cores_key_ref = key_refs
        rows = across_key_ref.shape[0]
        keys = across_key_ref[...] + cores_key_ref[rows:, :].astype(jnp.float32)
        for block in range(keys.shape[1] // LANES):
            first = half + block * rows
            columns = slice(block * LANES, (block + 1) * LANES)
            across_second_ref[first : first + rows, :] = keys[:, columns].astype(jnp.bfloat16)
    outs = (beside_first_ref, beside_second_ref, across_first_ref, across_second_ref)
    total = near_ref[:size, :].astype(jnp.float32) + far_ref[:size, :].astype(jnp.float32)
    own_ref[...] = total.astype(jnp.bfloat16)
    for place, out_ref in enumerate(outs):
        rows = slice(size + place * half, size + (place + 1) * half)
        total = near_ref[rows, :].astype(jnp.float32) + far_ref[rows, :].astype(jnp.float32)
        out_ref[:half, :] = total.astype(jnp.bfloat16)


def sum_all_kernel(size, index_ref, near_three, near_one, far_three, far_one, *out_refs):
    sum_one_kernel(size, index_ref, near_one, far_one, *out_refs[:2])
    sum_three_kernel(size, index_ref, near_three, far_three, *out_refs[2:])


def sum_passed_kernel(
    size,
    index_ref,
    beside_ref,
    across_ref,
    over_x_ref,
    over_y_ref,
    near_one_ref,
    far_one_ref,
    beside_out_ref,
    across_out_ref,
    extra_ref,
):
    half = size // 2
    beside = beside_ref[...].astype(jnp.float32) + over_y_ref[...].astype(jnp.float32)
    beside_out_ref[...] = beside.astype(jnp.bfloat16)
    across = across_ref[...].astype(jnp.float32) + over_x_ref[:half, :].astype(jnp.float32)
    across_out_ref[:half, :] = across.astype(jnp.bfloat16)
    if across_out_ref.shape[0] > half:
        extra = near_one_ref[size:, :].astype(jnp.float32)
        extra = extra + far_one_ref[size:, :].astype(jnp.float32)
        extra = extra + over_x_ref[half:, :].astype(jnp.float32)
        extra_ref[...] = extra
        across_out_ref[half:, :] = extra.astype(jnp.bfloat16)
    else:
        extra_ref[...] = jnp.zeros(extra_ref.shape, jnp.float32)


def unpack_kernel(
    pieces,
    index_ref,
    own_ref,
    beside_first_ref,
    beside_second_ref,
    across_first_ref,
    across_second_ref,
    extra_ref,
    *refs,
):
    high_count = pieces[0].high_count
    half = sum(piece.size for piece in pieces) // 2
    flat_rows = sum(piece.flat_rows for piece in pieces)
    outs, flat, packed = refs[:-2], refs[-2], refs[-1]
    high = index_ref[0] // LOW_COUNT
    packed[:half, :] = (
        own_ref[:half, :].astype(jnp.float32)
        + beside_first_ref[...].astype(jnp.float32)
        + across_first_ref[:half, :].astype(jnp.float32)
    )
    packed[half:, :] = (
        own_ref[half:, :].astype(jnp.float32)
        + beside_second_ref[...].astype(jnp.float32)
        + across_second_ref[:half, :].astype(jnp.float32)
    )
    start, source = 0, 0
    for piece in pieces:
        for block in range(piece.blocks):
            for place in range(high_count):
                flat[place, pl.ds(start + block, piece.own_rows, stride=piece.blocks), :] = packed[
                    pl.ds(source, piece.own_rows), :
                ]
                source = source + piece.own_rows
        start = start + piece.flat_rows
    for step, out_ref in enumerate(outs):
        out_ref[:flat_rows, :] = flat[high ^ step].astype(out_ref.dtype)
        if out_ref.shape[0] > flat_rows:
            extra = extra_ref[...] + across_first_ref[half:, :].astype(jnp.float32)
            out_ref[flat_rows:, :] = extra.astype(out_ref.dtype)


def array(shape, kind):
    return jax.ShapeDtypeStruct(shape, kind)


def gather_high(rows):
    high_count = lax.axis_size(ALL_AXES) // LOW_COUNT
    return [rows] + [swap(rows, step * LOW_COUNT) for step in range(1, high_count)]


def gather_own(pieces, parts, count, behind=()):
    high_count = pieces[0].high_count
    size = sum(piece.size for piece in pieces)
    return local_call(
        functools.partial(pack_kernel, pieces),
        (array((size // count, LANES), jnp.bfloat16),) * count,
        parts,
        (
            pltpu.VMEM((high_count, parts[0].shape[0], LANES), jnp.float32),
            pltpu.VMEM((size, LANES), jnp.float32),
        ),
        behind,
    )


def copied(value, behind):
    return local_call(copy_kernel, (array(value.shape, jnp.bfloat16),), (value,), (), behind)[0]


def held(values, behind):
    count = len(values)
    return pl.pallas_call(
        lambda *refs: None,
        out_shape=tuple(array(value.shape, value.dtype) for value in values),
        in_specs=[pl.BlockSpec(memory_space=pl.ANY)] * (count + len(behind)),
        out_specs=tuple(pl.BlockSpec(memory_space=pl.ANY) for _ in values),
        input_output_aliases={place: place for place in range(count)},
        cost_estimate=pl.CostEstimate(flops=0, bytes_accessed=0, transcendentals=0),
    )(*values, *behind)


def gather_halves(first, second):
    return swap(second, 4), swap(first, 2)


def gather_rest(first, second, beside_second, across_first, behind, behind_last):
    return (
        first,
        second,
        swap(copied(first, behind), 4),
        beside_second,
        across_first,
        swap(second, 2),
        swap(across_first, 4),
        swap(copied(beside_second, behind_last), 2),
    )


def gather_wholes(own):
    beside, across = swap(own, 4), swap(own, 2)
    return own, beside, across, swap(across, 4)


def gather_cores(near):
    return near + tuple(swap(value, 1) for value in near)


def scatter_cores(far_three, far_one):
    far_one = swap(far_one, 1)
    return swap(far_three, 1), far_one


def scatter_one(pieces, near_one, far_one, behind=()):
    half = sum(piece.size for piece in pieces) // 2
    to_x, to_y = local_call(
        functools.partial(sum_one_kernel, 2 * half),
        (
            array((near_one.shape[0] - half, LANES), jnp.bfloat16),
            array((half, LANES), jnp.bfloat16),
        ),
        (near_one, far_one),
        (),
        behind,
    )
    return swap(to_x, 4), swap(to_y, 2), to_y


def scatter_three(pieces, near_three, far_three, behind=(), keys=()):
    size = sum(piece.size for piece in pieces)
    half = size // 2
    own, beside_first, beside_second, across_first, across_second = local_call(
        functools.partial(sum_three_kernel, size),
        (
            array((size, LANES), jnp.bfloat16),
            *(array((half, LANES), jnp.bfloat16),) * 3,
            array((half + (keys[0].size // LANES if keys else 0), LANES), jnp.bfloat16),
        ),
        (near_three, far_three, *keys),
        (),
        behind,
    )
    return own, swap(beside_first, 4), beside_second, across_first, swap(across_second, 2)


def scatter_all(pieces, near_three, near_one, far_three, far_one, behind=()):
    size = sum(piece.size for piece in pieces)
    half = size // 2
    to_x, to_y, own, beside_first, beside_second, across_first, across_second = local_call(
        functools.partial(sum_all_kernel, size),
        (
            array((near_one.shape[0] - half, LANES), jnp.bfloat16),
            array((half, LANES), jnp.bfloat16),
            array((size, LANES), jnp.bfloat16),
            *(array((half, LANES), jnp.bfloat16),) * 4,
        ),
        (near_three, near_one, far_three, far_one),
        (),
        behind,
    )
    over_x, over_y = swap(to_x, 4), swap(to_y, 2)
    return (
        over_x,
        over_y,
        (own, swap(beside_first, 4), beside_second, across_first, swap(across_second, 2)),
    )


def scatter_passed(pieces, threes, over_x, over_y, near_one, far_one, behind=()):
    size = sum(piece.size for piece in pieces)
    extra_count = near_one.shape[0] - size
    own, beside_first, beside_second, across_first, across_second = threes
    beside_second, across_first, extra = local_call(
        functools.partial(sum_passed_kernel, size),
        (
            array((size // 2, LANES), jnp.bfloat16),
            array((size // 2 + extra_count, LANES), jnp.bfloat16),
            array((max(extra_count, 8), LANES), jnp.float32),
        ),
        (beside_second, across_first, over_x, over_y, near_one, far_one),
        (),
        behind,
    )
    terms = (
        own,
        beside_first,
        swap(beside_second, 4),
        swap(across_first, 2),
        across_second,
        extra,
    )
    return terms, beside_second


def scatter_high(pieces, terms, behind=()):
    high_count = pieces[0].high_count
    size = sum(piece.size for piece in pieces)
    flat_rows = sum(piece.flat_rows for piece in pieces)
    out_rows = flat_rows + terms[3].shape[0] - size // 2
    outs = local_call(
        functools.partial(unpack_kernel, pieces),
        (array((out_rows, LANES), jnp.float32),)
        + (array((out_rows, LANES), jnp.bfloat16),) * (high_count - 1),
        terms,
        (
            pltpu.VMEM((high_count, flat_rows, LANES), jnp.float32),
            pltpu.VMEM((size, LANES), jnp.float32),
        ),
        behind,
    )
    arrived = [swap(send, step * LOW_COUNT) for step, send in enumerate(outs) if step]
    return outs[0] + sum(value.astype(jnp.float32) for value in arrived), outs[0], arrived


def norm_parts(values):
    scale = lax.rsqrt(jnp.mean(values * values, axis=-1, keepdims=True) + norm_eps)
    return scale, values * scale


def norm_back(scale, normal, upstream, weight_vec):
    weighted = upstream * (1.0 + weight_vec)
    inner = jnp.mean(weighted * normal, axis=-1, keepdims=True)
    return scale * (weighted - normal * inner), jnp.sum(normal * upstream, axis=0, keepdims=True)


def product(left_side, right_side, left_axis, right_axis):
    return lax.dot_general(
        left_side,
        right_side,
        (((left_axis,), (right_axis,)), ((), ())),
        preferred_element_type=jnp.float32,
    )


def unordered(rows_in, order_low):
    upper = rows_in.astype(jnp.bfloat16)
    lower = (rows_in - upper.astype(jnp.float32)).astype(jnp.bfloat16)
    return product(upper, order_low, 1, 1) + product(lower, order_low, 1, 1)


def weight_rows(refs, size, order, start, rows):
    count = len(refs) // LOW_COUNT
    part = size // count
    return refs[order * count + start // part][start % part : start % part + rows, :]


def put_rows(refs, size, order, start, rows):
    three, one = refs[:2] if order < 4 else refs[2:]
    if order % 4 == 3:
        one[start : start + rows.shape[0], :] = rows
    else:
        start = order % 4 * size + start
        three[start : start + rows.shape[0], :] = rows


def wide_tile(refs, size, start, rows):
    return jnp.concatenate(
        [weight_rows(refs, size, order, start, rows) for order in range(LOW_COUNT)]
    )


def put_wide_tile(refs, size, start, rows, tile):
    for order in range(LOW_COUNT):
        put_rows(refs, size, order, start, tile[order * rows : (order + 1) * rows])


def tall_rows(piece, low):
    for order, mask in enumerate(LOW_MASKS):
        for block in range(piece.blocks):
            for place in range(piece.high_count):
                row = (place * LOW_COUNT + (low ^ mask)) * piece.own_rows
                yield (
                    order,
                    block * piece.block_rows + place * piece.own_rows,
                    pl.ds(pl.multiple_of(row, piece.own_rows), piece.own_rows),
                    slice(block * LANES, (block + 1) * LANES),
                )


def ffn_kernel(
    gate_piece,
    down_piece,
    index_ref,
    middle_ref,
    cotangent_ref,
    gain_in_ref,
    gain_out_ref,
    order_ref,
    *refs,
):
    weight_refs, grad_refs = refs[:16], refs[20:24]
    block_out_ref, grad_middle_ref, grad_gain_in_ref, grad_gain_out_ref = refs[16:20]
    down_ref, hidden_ref, gelu_ref, slope_ref = refs[24:]
    low = index_ref[0] % LOW_COUNT
    rows = gate_piece.block_rows
    size = 2 * gate_piece.size + down_piece.size
    width = 2 * LANES
    for order, start, matrix_rows, columns in tall_rows(down_piece, low):
        start = start + 2 * gate_piece.size
        down_ref[matrix_rows, columns] = weight_rows(
            weight_refs, size, order, start, down_piece.own_rows
        )

    def wide_tiles(step):
        return [
            jnp.concatenate(
                [
                    wide_tile(weight_refs, size, offset + block * rows, rows)
                    for block in (2 * step, 2 * step + 1)
                ],
                axis=1,
            )
            for offset in (0, gate_piece.size)
        ]

    middle = middle_ref[...]
    scale_in, normal_in = norm_parts(middle)
    order_low = order_ref[...]
    normed = (normal_in * (1.0 + gain_in_ref[...])).astype(jnp.bfloat16)
    normed = product(normed, order_low, 1, 0).astype(jnp.bfloat16)
    for step in range(FF // width):
        columns = slice(step * width, (step + 1) * width)
        gate_weight, up_weight = wide_tiles(step)
        gate = product(normed, gate_weight, 1, 0)
        up = product(normed, up_weight, 1, 0)
        square = gate * gate
        bend = jnp.tanh(GELU_SCALE * gate * (1.0 + GELU_CUBE * square))
        half = 0.5 * (1.0 + bend)
        gelu = gate * half
        slope = half + 0.5 * gate * (1.0 - bend * bend) * GELU_SCALE * (
            1.0 + 3.0 * GELU_CUBE * square
        )
        gelu_ref[:, columns] = gelu
        slope_ref[:, columns] = slope * up
        hidden_ref[:, columns] = (gelu * up).astype(jnp.bfloat16)
    hidden = hidden_ref[...]
    scale_out, normal_out = norm_parts(product(hidden, down_ref[...], 1, 0))
    block_out_ref[...] = (middle + normal_out * (1.0 + gain_out_ref[...])).astype(jnp.bfloat16)
    upstream = cotangent_ref[...].astype(jnp.float32)
    grad_ffn, grad_gain_out_ref[...] = norm_back(
        scale_out, normal_out, upstream, gain_out_ref[...]
    )
    grad_ffn = grad_ffn.astype(jnp.bfloat16)
    grad_normed = jnp.zeros(middle.shape, jnp.float32)
    for step in range(FF // width):
        columns = slice(step * width, (step + 1) * width)
        grad_hidden = product(grad_ffn, down_ref[columns, :], 1, 1)
        down_ref[columns, :] = product(hidden_ref[:, columns], grad_ffn, 0, 0).astype(jnp.bfloat16)
        grads = [
            (grad_hidden * slope_ref[:, columns]).astype(jnp.bfloat16),
            (grad_hidden * gelu_ref[:, columns]).astype(jnp.bfloat16),
        ]
        for place, (grad, weight) in enumerate(zip(grads, wide_tiles(step))):
            grad_weight = product(normed, grad, 0, 0).astype(jnp.bfloat16)
            for side in range(2):
                put_wide_tile(
                    grad_refs,
                    size,
                    place * gate_piece.size + (2 * step + side) * rows,
                    rows,
                    grad_weight[:, side * LANES : (side + 1) * LANES],
                )
            grad_normed = grad_normed + product(grad, weight, 1, 1)
    for order, start, matrix_rows, columns in tall_rows(down_piece, low):
        start = start + 2 * gate_piece.size
        put_rows(grad_refs, size, order, start, down_ref[matrix_rows, columns])
    grad_middle, grad_gain_in_ref[...] = norm_back(
        scale_in, normal_in, unordered(grad_normed, order_low), gain_in_ref[...]
    )
    grad_middle_ref[...] = upstream + grad_middle


def grad_arrays(pieces, extra_count=0):
    size = sum(piece.size for piece in pieces)
    return (
        array((3 * size, LANES), jnp.bfloat16),
        array((size + extra_count, LANES), jnp.bfloat16),
    ) * 2


def ffn_blocks(pieces, middle, cotangent, gain_in, gain_out, order, blocks):
    rows = middle.shape[0]
    outs = local_call(
        functools.partial(ffn_kernel, pieces[4], pieces[6]),
        (
            array((rows, D), jnp.bfloat16),
            array((rows, D), jnp.float32),
            array((1, D), jnp.float32),
            array((1, D), jnp.float32),
            *grad_arrays(pieces[4:7]),
        ),
        (middle, cotangent, gain_in, gain_out, order, *blocks),
        (
            pltpu.VMEM((FF, D), jnp.bfloat16),
            pltpu.VMEM((rows, FF), jnp.bfloat16),
            pltpu.VMEM((rows, FF), jnp.float32),
            pltpu.VMEM((rows, FF), jnp.float32),
        ),
    )
    return *outs[:4], outs[4:]


def turn(values, cosine, sine):
    first_half, second_half = values[:, : HD // 2], values[:, HD // 2 :]
    return jnp.concatenate(
        [first_half * cosine - second_half * sine, second_half * cosine + first_half * sine], axis=1
    )


def wide_head(refs, size, start, rows):
    return jnp.concatenate(
        [wide_tile(refs, size, start + side * rows, rows) for side in range(2)], axis=1
    )


def head_starts(pieces):
    rows = pieces[0].block_rows
    return [2 * rows * head for head in range(HQ + 2)]


def project_kernel(
    pieces,
    index_ref,
    tokens_ref,
    gain_ref,
    gain_query_ref,
    gain_key_ref,
    cosine_ref,
    sine_ref,
    order_ref,
    *refs,
):
    weight_refs = refs[:8]
    normed_ref, query_proj_ref, key_proj_ref, query_ref, key_value_ref = refs[8:]
    size = sum(piece.size for piece in pieces)
    rows = pieces[0].block_rows
    cosine, sine = cosine_ref[...], sine_ref[...]
    _, normal = norm_parts(tokens_ref[...].astype(jnp.float32))
    normed = (normal * (1.0 + gain_ref[...])).astype(jnp.bfloat16)
    normed = product(normed, order_ref[...], 1, 0).astype(jnp.bfloat16)
    normed_ref[...] = normed
    starts = head_starts(pieces)
    for head, start in enumerate(starts):
        proj = product(normed, wide_head(weight_refs, size, start, rows), 1, 0)
        columns = slice(head * HD, (head + 1) * HD)
        if head == HQ + 1:
            key_value_ref[:, HD:] = proj.astype(jnp.bfloat16)
            continue
        gain_vec = gain_query_ref[...] if head < HQ else gain_key_ref[...]
        _, normal = norm_parts(proj)
        turned = turn(normal * (1.0 + gain_vec), cosine, sine).astype(jnp.bfloat16)
        if head < HQ:
            query_proj_ref[:, columns] = proj
            query_ref[:, columns] = turned
        else:
            key_proj_ref[...] = proj
            key_value_ref[:, :HD] = turned


def attend_kernel(
    pieces,
    index_ref,
    tokens_ref,
    gain_ref,
    allowed_ref,
    query_ref,
    *refs,
):
    weight_refs, key_value_refs = refs[:8], refs[8:-5]
    probs_ref, attended_ref, attn_out_ref, middle_ref, out_weight_ref = refs[-5:]
    out_piece = pieces[-1]
    low = index_ref[0] % LOW_COUNT
    size = sum(piece.size for piece in pieces)
    out_start = size - out_piece.size
    for order, start, matrix_rows, columns in tall_rows(out_piece, low):
        out_weight_ref[matrix_rows, columns] = weight_rows(
            weight_refs, size, order, start + out_start, out_piece.own_rows
        )
    rows = tokens_ref.shape[0]
    allowed = allowed_ref[...] > 0.0
    keys = jnp.concatenate([ref[:, :HD] for ref in key_value_refs])
    values = jnp.concatenate([ref[:, HD:] for ref in key_value_refs])
    count = keys.shape[0]
    for head in range(HQ):
        columns = slice(head * HD, (head + 1) * HD)
        scores = product(query_ref[:, columns], keys, 1, 1) * HD ** (-0.5)
        scores = jnp.where(allowed, scores, -1e30)
        raised = jnp.exp(scores - jnp.max(scores, axis=-1, keepdims=True))
        probs = raised / jnp.sum(raised, axis=-1, keepdims=True)
        probs_ref[:, head * count : (head + 1) * count] = probs
        attended_ref[:, columns] = product(probs.astype(jnp.bfloat16), values, 1, 0).astype(
            jnp.bfloat16
        )
    attn_out = product(attended_ref[...], out_weight_ref[...], 1, 0)
    attn_out_ref[...] = attn_out
    _, normal = norm_parts(attn_out)
    middle_ref[...] = tokens_ref[...].astype(jnp.float32) + normal * (1.0 + gain_ref[...])


def attend_back_kernel(
    index_ref,
    grad_middle_ref,
    attn_out_ref,
    gain_ref,
    out_weight_ref,
    attended_ref,
    probs_ref,
    query_ref,
    *refs,
):
    key_value_refs = refs[:4]
    grad_out_weight_ref, grad_query_ref, grad_gain_ref = refs[4:7]
    grad_own_ref, grad_across_ref, grad_cores_ref = refs[7:]
    rows = query_ref.shape[0]
    scale, normal = norm_parts(attn_out_ref[...])
    grad_attn, grad_gain_ref[...] = norm_back(scale, normal, grad_middle_ref[...], gain_ref[...])
    grad_attn = grad_attn.astype(jnp.bfloat16)
    grad_out_weight_ref[...] = product(attended_ref[...], grad_attn, 0, 0).astype(jnp.bfloat16)
    keys = jnp.concatenate([ref[:, :HD] for ref in key_value_refs])
    values = jnp.concatenate([ref[:, HD:] for ref in key_value_refs])
    count = keys.shape[0]
    grad_keys = jnp.zeros((count, HD), jnp.float32)
    grad_values = jnp.zeros((count, HD), jnp.float32)
    for head in range(HQ):
        columns = slice(head * HD, (head + 1) * HD)
        grad_attended = product(grad_attn, out_weight_ref[columns, :], 1, 1).astype(jnp.bfloat16)
        probs = probs_ref[:, head * count : (head + 1) * count]
        grad_probs = product(grad_attended, values, 1, 1)
        grad_values = grad_values + product(probs.astype(jnp.bfloat16), grad_attended, 0, 0)
        inner = jnp.sum(probs * grad_probs, axis=-1, keepdims=True)
        grad_scores = (probs * (grad_probs - inner) * HD ** (-0.5)).astype(jnp.bfloat16)
        grad_query_ref[:, columns] = product(grad_scores, keys, 1, 0)
        grad_keys = grad_keys + product(grad_scores, query_ref[:, columns], 0, 0)
    targets = (
        grad_own_ref,
        grad_cores_ref.at[:rows],
        grad_across_ref,
        grad_cores_ref.at[rows:],
    )
    for part, ref in enumerate(targets):
        ref[:, :HD] = grad_keys[part * rows : (part + 1) * rows].astype(ref.dtype)
        ref[:, HD:] = grad_values[part * rows : (part + 1) * rows].astype(ref.dtype)


def query_back_kernel(
    pieces,
    index_ref,
    gain_ref,
    cosine_ref,
    sine_ref,
    normed_ref,
    query_proj_ref,
    grad_query_ref,
    *refs,
):
    weight_refs = refs[:8]
    grad_weight_ref, grad_normed_ref, grad_gain_ref = refs[8:]
    size = sum(piece.size for piece in pieces)
    rows = pieces[0].block_rows
    cosine, sine = cosine_ref[...], sine_ref[...]
    normed = normed_ref[...]
    grad_normed = jnp.zeros(grad_normed_ref.shape, jnp.float32)
    grad_gain = jnp.zeros((1, HD), jnp.float32)
    for head, start in enumerate(head_starts(pieces)[:HQ]):
        columns = slice(head * HD, (head + 1) * HD)
        scale, normal = norm_parts(query_proj_ref[:, columns])
        upstream = turn(grad_query_ref[:, columns], cosine, -sine)
        grad, gain_row = norm_back(scale, normal, upstream, gain_ref[...])
        grad_gain = grad_gain + gain_row
        grad = grad.astype(jnp.bfloat16)
        weight = wide_head(weight_refs, size, start, rows)
        grad_normed = grad_normed + product(grad, weight, 1, 1)
        grad_weight_ref[:, columns] = product(normed, grad, 0, 0).astype(jnp.bfloat16)
    grad_normed_ref[...] = grad_normed
    grad_gain_ref[...] = grad_gain


def project_back_kernel(
    pieces,
    index_ref,
    tokens_ref,
    gain_ref,
    gain_key_ref,
    cosine_ref,
    sine_ref,
    order_ref,
    normed_ref,
    key_proj_ref,
    grad_normed_ref,
    grad_middle_ref,
    gain_attn_ref,
    gain_ffin_ref,
    gain_ffout_ref,
    gain_query_ref,
    own_key_ref,
    cores_key_ref,
    across_key_ref,
    *refs,
):
    weight_refs = refs[:8]
    grad_weight_ref, input_grad_ref, grad_gain_ref = refs[8:]
    size = sum(piece.size for piece in pieces)
    rows = pieces[0].block_rows
    normed = normed_ref[...]
    key_rows = own_key_ref.shape[0]
    first = across_key_ref.shape[0] - 4 * key_rows
    key_value = own_key_ref[...] + cores_key_ref[:key_rows, :].astype(jnp.float32)
    key_value = key_value + jnp.concatenate(
        [
            across_key_ref[first + block * key_rows : first + (block + 1) * key_rows, :].astype(
                jnp.float32
            )
            for block in range(4)
        ],
        axis=1,
    )
    scale, normal = norm_parts(key_proj_ref[...])
    upstream = turn(key_value[:, :HD], cosine_ref[...], -sine_ref[...])
    grad_key, grad_gain_key = norm_back(scale, normal, upstream, gain_key_ref[...])
    grad_normed = grad_normed_ref[...]
    for place, start in enumerate(head_starts(pieces)[HQ:]):
        grad = (key_value[:, HD:] if place else grad_key).astype(jnp.bfloat16)
        weight = wide_head(weight_refs, size, start, rows)
        grad_normed = grad_normed + product(grad, weight, 1, 1)
        grad_weight_ref[:, place * HD : (place + 1) * HD] = product(normed, grad, 0, 0).astype(
            jnp.bfloat16
        )
    scale, normal = norm_parts(tokens_ref[...].astype(jnp.float32))
    grad_inputs, grad_gain_input = norm_back(
        scale, normal, unordered(grad_normed, order_ref[...]), gain_ref[...]
    )
    input_grad_ref[...] = (grad_middle_ref[...] + grad_inputs).astype(jnp.bfloat16)
    grad_gains = [
        grad_gain_input,
        gain_attn_ref[...],
        gain_ffin_ref[...],
        gain_ffout_ref[...],
        gain_query_ref[...],
        grad_gain_key,
    ]
    row = 0
    grad_gain_ref[...] = jnp.zeros(grad_gain_ref.shape, jnp.float32)
    for values in grad_gains:
        for start in range(0, values.shape[1], LANES):
            grad_gain_ref[row : row + 1, :] = values[:, start : start + LANES]
            row = row + 1


def split_kernel(
    pieces,
    index_ref,
    query_ref,
    key_value_ref,
    out_ref,
    gain_ref,
    *grad_refs,
):
    low = index_ref[0] % LOW_COUNT
    size = sum(piece.size for piece in pieces)
    rows = pieces[0].block_rows
    start = 0
    for matrix_ref in (query_ref, key_value_ref):
        for column in range(0, matrix_ref.shape[1], LANES):
            tile = matrix_ref[:, column : column + LANES]
            put_wide_tile(grad_refs, size, start, rows, tile)
            start = start + rows
    out_piece = pieces[-1]
    for order, first, matrix_rows, columns in tall_rows(out_piece, low):
        put_rows(grad_refs, size, order, start + first, out_ref[matrix_rows, columns])
    for target in (grad_refs[1], grad_refs[3]):
        target[size:, :] = gain_ref[...].astype(jnp.bfloat16)


def width_order(device_count):
    low = lax.axis_index(ALL_AXES) % LOW_COUNT
    rows = D // device_count
    high_count = device_count // LOW_COUNT
    column = jnp.arange(D, dtype=jnp.int32)
    place = column // (rows * high_count)
    mask = (place & 1) * 4 + ((place >> 1) & 1) * 2 + (place >> 2)
    high = (column // rows) % high_count
    picked = (high * LOW_COUNT + (low ^ mask)) * rows + column % rows
    return (jnp.arange(D, dtype=jnp.int32)[:, None] == picked[None, :]).astype(jnp.bfloat16)


GAIN_ROWS = 32


def shards_blocks(
    device_count,
    tokens,
    doc_ids,
    cotangent,
    master,
    first_moment,
    second_moment,
    gains,
    gain_first,
    gain_second,
):
    pieces = [Piece(*shape_pair, device_count) for shape_pair in piece_shapes()]
    attention_pieces = pieces[:4]
    local_rows = tokens.shape[0]
    group_size = lax.axis_size("group")
    first_row = lax.axis_index("group") * local_rows
    attention_rows = sum(piece.flat_rows for piece in attention_pieces)
    ffn_pieces = pieces[4:7]
    rounded = master.astype(jnp.bfloat16)
    attention_parts = gather_high(rounded[:attention_rows])
    ffn_rows = rounded[attention_rows:]
    ffn_parts = gather_high(ffn_rows)
    attention_near = gather_wholes(
        *gather_own(attention_pieces, attention_parts, 1, (ffn_parts[1],))
    )
    own, beside, across, diagonal = attention_near
    own, beside = held((own, beside), (across, *ffn_parts[2:]))
    attention_blocks = gather_cores((own, beside, across, diagonal))
    ffn_own = gather_own(ffn_pieces, ffn_parts, 2, attention_near[1:])
    ffn_passed = gather_halves(*ffn_own)
    gain_parts = []
    for start, width in ((0, D), (D, D), (2 * D, D), (3 * D, D), (4 * D, HD), (4 * D + HD, HD)):
        gain_parts.append(gains[start : start + width][None])
    gain_input, gain_attn, gain_ffin, gain_ffout, gain_query, gain_key = gain_parts
    order = width_order(device_count)
    doc_row = doc_ids[0]
    angles = lax.dynamic_slice_in_dim(angles_of(positions(doc_row)), first_row, local_rows, 0)
    cosine, sine = jnp.cos(angles), jnp.sin(angles)
    query_docs = lax.dynamic_slice_in_dim(doc_row, first_row, local_rows, 0)
    key_count = group_size * local_rows
    first_keys = [(lax.axis_index("group") ^ step) * local_rows for step in range(group_size)]
    key_docs = jnp.concatenate(
        [lax.dynamic_slice_in_dim(doc_row, start, local_rows, 0) for start in first_keys]
    )
    key_index = jnp.concatenate(
        [start + jnp.arange(local_rows, dtype=jnp.int32) for start in first_keys]
    )
    query_index = first_row + jnp.arange(local_rows, dtype=jnp.int32)
    distance = query_index[:, None] - key_index[None, :]
    allowed = (distance >= 0) & (distance < WINDOW) & (key_docs[None, :] == query_docs[:, None])
    allowed = allowed.astype(jnp.float32)

    width = HQ * HD
    normed, query_proj, key_proj, query_rot, key_value = local_call(
        functools.partial(project_kernel, attention_pieces),
        (
            array((local_rows, D), jnp.bfloat16),
            array((local_rows, width), jnp.float32),
            array((local_rows, HD), jnp.float32),
            array((local_rows, width), jnp.bfloat16),
            array((local_rows, 2 * HD), jnp.bfloat16),
        ),
        (tokens, gain_input, gain_query, gain_key, cosine, sine, order, *attention_blocks),
    )
    key_values = [key_value] + [swap(key_value, step) for step in range(1, group_size)]
    probs, attended, attn_out, middle, out_weight = local_call(
        functools.partial(attend_kernel, attention_pieces),
        (
            array((local_rows, HQ * key_count), jnp.float32),
            array((local_rows, width), jnp.bfloat16),
            array((local_rows, D), jnp.float32),
            array((local_rows, D), jnp.float32),
            array((width, D), jnp.bfloat16),
        ),
        (tokens, gain_attn, allowed, query_rot, *attention_blocks, *key_values),
        (),
        ffn_passed,
    )
    ffn_weights = gather_cores(gather_rest(*ffn_own, *ffn_passed, (key_value,), (middle,)))
    outputs, grad_middle, grad_gain_ffin, grad_gain_ffout, grads_ffn = ffn_blocks(
        pieces, middle, cotangent, gain_ffin, gain_ffout, order, ffn_weights
    )
    near_three, near_one, far_three, far_one = grads_ffn
    far_three, far_one = scatter_cores(far_three, far_one)
    grad_out_weight, grad_query, grad_gain_attn, own_key, across_key, cores_key = local_call(
        attend_back_kernel,
        (
            array((width, D), jnp.bfloat16),
            array((local_rows, width), jnp.float32),
            array((1, D), jnp.float32),
            array((local_rows, 2 * HD), jnp.float32),
            array((local_rows, 2 * HD), jnp.float32),
            array((2 * local_rows, 2 * HD), jnp.bfloat16),
        ),
        (
            grad_middle,
            attn_out,
            gain_attn,
            out_weight,
            attended,
            probs,
            query_rot,
            *key_values,
        ),
    )
    cores_key = swap(cores_key, 1)
    over_x, over_y, sent = scatter_one(ffn_pieces, near_one, far_one, (grad_query,))
    threes = scatter_three(ffn_pieces, near_three, far_three, (sent,), (across_key, cores_key))
    grad_query_weight, grad_normed, grad_gain_query = local_call(
        functools.partial(query_back_kernel, attention_pieces),
        (
            array((D, width), jnp.bfloat16),
            array((local_rows, D), jnp.float32),
            array((1, HD), jnp.float32),
        ),
        (gain_query, cosine, sine, normed, query_proj, grad_query, *attention_blocks),
        (),
        (threes[0],),
    )
    ffn_terms, sent = scatter_passed(
        ffn_pieces, threes, over_x, over_y, near_one, far_one, (grad_normed,)
    )
    grad_key_weight, grad_inputs, grad_gains = local_call(
        functools.partial(project_back_kernel, attention_pieces),
        (
            array((D, 2 * HD), jnp.bfloat16),
            array((local_rows, D), jnp.bfloat16),
            array((GAIN_ROWS, LANES), jnp.float32),
        ),
        (
            tokens,
            gain_input,
            gain_key,
            cosine,
            sine,
            order,
            normed,
            key_proj,
            grad_normed,
            grad_middle,
            grad_gain_attn,
            grad_gain_ffin,
            grad_gain_ffout,
            grad_gain_query,
            own_key,
            cores_key,
            threes[4],
            *attention_blocks,
        ),
        (),
        (sent, threes[1]),
    )
    near_three, near_one, far_three, far_one = local_call(
        functools.partial(split_kernel, attention_pieces),
        grad_arrays(attention_pieces, GAIN_ROWS),
        (grad_query_weight, grad_key_weight, grad_out_weight, grad_gains),
    )
    far_three, far_one = held((far_three, far_one), ffn_terms[2:4])
    grads_ffn, sent, arrived = scatter_high(ffn_pieces, ffn_terms, (near_one,))
    far_three, far_one = scatter_cores(far_three, far_one)
    over_x, over_y, threes = scatter_all(
        attention_pieces, near_three, near_one, far_three, far_one, (sent,)
    )
    terms, _ = scatter_passed(
        attention_pieces, threes, over_x, over_y, near_one, far_one, (arrived[0],)
    )
    grads_attention, _, _ = scatter_high(attention_pieces, terms, arrived)
    gain_grads = grads_attention[attention_rows:].reshape(-1)[: gains.shape[0]]
    grads_local = jnp.concatenate([grads_attention[:attention_rows], grads_ffn])
    return (
        outputs,
        grad_inputs,
        *adam_update(grads_local, first_moment, second_moment, master, learn_rate, weight_decay),
        *adam_update(gain_grads, gain_first, gain_second, gains, gain_rate, 0.0),
    )


def shards(
    tokens, doc_ids, cotangent, master, first_moment, second_moment, gains, gain_first, gain_second
):
    group_size = lax.axis_size("group")
    devices_all = lax.axis_size("dp") * group_size
    if aligned(devices_all):
        return shards_blocks(
            devices_all,
            tokens,
            doc_ids,
            cotangent,
            master,
            first_moment,
            second_moment,
            gains,
            gain_first,
            gain_second,
        )
    group_index = lax.axis_index("group")
    local_rows = tokens.shape[0]
    shard_parts = [
        part_rows.astype(jnp.bfloat16) for part_rows in split_rows(master, piece_rows(devices_all))
    ]
    gathered = (
        lax.all_gather(shard_parts[0], ("dp", "group"), axis=0, tiled=True),
        lax.all_gather(shard_parts[1], ("dp", "group"), axis=0, tiled=True),
        lax.all_gather(shard_parts[2], ("dp", "group"), axis=0, tiled=True),
        lax.all_gather(shard_parts[3], ("dp", "group"), axis=0, tiled=True),
        lax.all_gather(shard_parts[4], ("dp", "group"), axis=0, tiled=True),
        lax.all_gather(shard_parts[5], ("dp", "group"), axis=0, tiled=True),
        lax.all_gather(shard_parts[6], ("dp", "group"), axis=0, tiled=True),
    )
    query_weight, key_weight, value_weight, out_weight, gate_weight, up_weight, down_weight = [
        full_rows.reshape(shape_pair) for full_rows, shape_pair in zip(gathered, piece_shapes())
    ]
    norm_input = gains[0:D]
    norm_attn = gains[D : 2 * D]
    norm_ffin = gains[2 * D : 3 * D]
    norm_ffout = gains[3 * D : 4 * D]
    norm_query = gains[4 * D : 4 * D + HD]
    norm_key = gains[4 * D + HD : 4 * D + 2 * HD]
    doc_row = doc_ids[0]
    first_row = group_index * local_rows
    angles = lax.dynamic_slice_in_dim(angles_of(positions(doc_row)), first_row, local_rows, 0)
    query_docs = lax.dynamic_slice_in_dim(doc_row, first_row, local_rows, 0)
    inputs = tokens.astype(jnp.float32)
    normed, back_input = jax.vjp(rms_norm, inputs, norm_input)
    normed_low = normed.astype(jnp.bfloat16)
    query_proj = matmul(normed_low, query_weight)
    key_proj = matmul(normed_low, key_weight)
    value_proj = matmul(normed_low, value_weight)

    def query_prep(flat_rows, gain_vec):
        return rotate(rms_norm(flat_rows.reshape(local_rows, HQ, HD), gain_vec), angles[:, None, :])

    def key_prep(rows_in, gain_vec):
        return rotate(rms_norm(rows_in, gain_vec), angles)

    query_rot, back_query = jax.vjp(query_prep, query_proj, norm_query)
    key_rot, back_key = jax.vjp(key_prep, key_proj, norm_key)
    query_low = query_rot.astype(jnp.bfloat16)
    key_low = key_rot.astype(jnp.bfloat16)
    value_low = value_proj.astype(jnp.bfloat16)
    reach = min(-(-(WINDOW - 1) // local_rows), group_size - 1)
    key_list = [key_low]
    value_list = [value_low]
    for offset in range(1, reach + 1):
        key_far, value_far = shifted((key_low, value_low), "group", offset)
        key_list.insert(0, key_far)
        value_list.insert(0, value_far)
    key_all = jnp.concatenate(key_list, axis=0)
    value_all = jnp.concatenate(value_list, axis=0)
    key_count = (reach + 1) * local_rows
    doc_pad = jnp.concatenate([jnp.full((reach * local_rows,), -1, jnp.int32), doc_row])
    key_docs = lax.dynamic_slice_in_dim(doc_pad, first_row, key_count, 0)
    key_index = (group_index - reach) * local_rows + jnp.arange(key_count, dtype=jnp.int32)
    query_index = first_row + jnp.arange(local_rows, dtype=jnp.int32)
    distance = query_index[:, None] - key_index[None, :]
    allowed = (distance >= 0) & (distance < WINDOW) & (key_docs[None, :] == query_docs[:, None])

    def scores_of(key_rows_low):
        raw_scores = jnp.einsum(
            "qhd,kd->hqk", query_low, key_rows_low, preferred_element_type=jnp.float32
        ) * HD ** (-0.5)
        return jnp.where(allowed[None], raw_scores, -1e30)

    masked = scores_of(key_all)
    top_score = jnp.max(masked, axis=-1, keepdims=True)
    log_total = top_score + jnp.log(jnp.sum(jnp.exp(masked - top_score), axis=-1, keepdims=True))
    probs = jnp.exp(masked - log_total)
    attended = jnp.einsum(
        "hqk,kd->qhd", probs.astype(jnp.bfloat16), value_all, preferred_element_type=jnp.float32
    )
    attended_low = attended.reshape(local_rows, HQ * HD).astype(jnp.bfloat16)
    attn_out = matmul(attended_low, out_weight)
    branch_one, back_attn = jax.vjp(rms_norm, attn_out, norm_attn)
    middle = inputs + branch_one
    normed_two, back_ffin = jax.vjp(rms_norm, middle, norm_ffin)
    normed_two_low = normed_two.astype(jnp.bfloat16)
    gate_proj = matmul(normed_two_low, gate_weight)
    up_proj = matmul(normed_two_low, up_weight)
    hidden, back_hidden = jax.vjp(geglu, gate_proj, up_proj)
    hidden_low = hidden.astype(jnp.bfloat16)
    ffn_out = matmul(hidden_low, down_weight)
    branch_two, back_ffout = jax.vjp(rms_norm, ffn_out, norm_ffout)
    outputs = middle + branch_two
    grad_out = cotangent.astype(jnp.float32)
    grad_ffn, grad_gain_ffout = back_ffout(grad_out)
    grad_ffn_low = grad_ffn.astype(jnp.bfloat16)
    grad_down_w = jnp.einsum(
        "tf,td->fd", hidden_low, grad_ffn_low, preferred_element_type=jnp.float32
    )
    grad_hidden = jnp.einsum(
        "td,fd->tf", grad_ffn_low, down_weight, preferred_element_type=jnp.float32
    )
    grad_gate, grad_up = back_hidden(grad_hidden)
    grad_gate_low = grad_gate.astype(jnp.bfloat16)
    grad_up_low = grad_up.astype(jnp.bfloat16)
    grad_gate_w = jnp.einsum(
        "td,tf->df", normed_two_low, grad_gate_low, preferred_element_type=jnp.float32
    )
    grad_up_w = jnp.einsum(
        "td,tf->df", normed_two_low, grad_up_low, preferred_element_type=jnp.float32
    )
    grad_normed_two = jnp.einsum(
        "tf,df->td", grad_gate_low, gate_weight, preferred_element_type=jnp.float32
    ) + jnp.einsum("tf,df->td", grad_up_low, up_weight, preferred_element_type=jnp.float32)
    grad_middle_norm, grad_gain_ffin = back_ffin(grad_normed_two)
    grad_middle = grad_out + grad_middle_norm
    grad_attn, grad_gain_attn = back_attn(grad_middle)
    grad_attn_low = grad_attn.astype(jnp.bfloat16)
    grad_out_w = jnp.einsum(
        "to,td->od", attended_low, grad_attn_low, preferred_element_type=jnp.float32
    )
    grad_attended = jnp.einsum(
        "td,od->to", grad_attn_low, out_weight, preferred_element_type=jnp.float32
    )
    grad_attended_low = grad_attended.astype(jnp.bfloat16).reshape(local_rows, HQ, HD)
    probs_again = jnp.exp(scores_of(key_all) - log_total)
    grad_probs = jnp.einsum(
        "qhd,kd->hqk", grad_attended_low, value_all, preferred_element_type=jnp.float32
    )
    grad_value_all = jnp.einsum(
        "hqk,qhd->kd",
        probs_again.astype(jnp.bfloat16),
        grad_attended_low,
        preferred_element_type=jnp.float32,
    )
    grad_scores = probs_again * (
        grad_probs - jnp.sum(probs_again * grad_probs, axis=-1, keepdims=True)
    )
    grad_scores_low = (grad_scores * HD ** (-0.5)).astype(jnp.bfloat16)
    grad_query = jnp.einsum(
        "hqk,kd->qhd", grad_scores_low, key_all, preferred_element_type=jnp.float32
    )
    grad_key_all = jnp.einsum(
        "hqk,qhd->kd", grad_scores_low, query_low, preferred_element_type=jnp.float32
    )
    key_total = grad_key_all[reach * local_rows :]
    value_total = grad_value_all[reach * local_rows :]
    for offset in range(1, reach + 1):
        row_start = (reach - offset) * local_rows
        key_back, value_back = (
            shifted(
                grad_key_all[row_start : row_start + local_rows].astype(jnp.bfloat16),
                "group",
                -offset,
            ).astype(jnp.float32),
            shifted(
                grad_value_all[row_start : row_start + local_rows].astype(jnp.bfloat16),
                "group",
                -offset,
            ).astype(jnp.float32),
        )
        key_total = key_total + key_back
        value_total = value_total + value_back
    grad_query_proj, grad_gain_query = back_query(grad_query)
    grad_key_proj, grad_gain_key = back_key(key_total)
    grad_query_low = grad_query_proj.astype(jnp.bfloat16)
    grad_key_low = grad_key_proj.astype(jnp.bfloat16)
    grad_value_low = value_total.astype(jnp.bfloat16)
    grad_query_w = jnp.einsum(
        "td,te->de", normed_low, grad_query_low, preferred_element_type=jnp.float32
    )
    grad_key_w = jnp.einsum(
        "td,te->de", normed_low, grad_key_low, preferred_element_type=jnp.float32
    )
    grad_value_w = jnp.einsum(
        "td,te->de", normed_low, grad_value_low, preferred_element_type=jnp.float32
    )
    grad_normed = jnp.einsum(
        "te,de->td", grad_query_low, query_weight, preferred_element_type=jnp.float32
    )
    grad_normed = grad_normed + jnp.einsum(
        "te,de->td", grad_key_low, key_weight, preferred_element_type=jnp.float32
    )
    grad_normed = grad_normed + jnp.einsum(
        "te,de->td", grad_value_low, value_weight, preferred_element_type=jnp.float32
    )
    grad_input_norm, grad_gain_input = back_input(grad_normed)
    grad_inputs = grad_middle + grad_input_norm
    flat_query = grad_query_w.reshape(-1, 128)
    flat_key = grad_key_w.reshape(-1, 128)
    flat_value = grad_value_w.reshape(-1, 128)
    flat_out = grad_out_w.reshape(-1, 128)
    flat_gate = grad_gate_w.reshape(-1, 128)
    flat_up = grad_up_w.reshape(-1, 128)
    flat_down = grad_down_w.reshape(-1, 128)
    reduced = (
        lax.psum_scatter(flat_query, ("dp", "group"), scatter_dimension=0, tiled=True),
        lax.psum_scatter(flat_key, ("dp", "group"), scatter_dimension=0, tiled=True),
        lax.psum_scatter(flat_value, ("dp", "group"), scatter_dimension=0, tiled=True),
        lax.psum_scatter(flat_out, ("dp", "group"), scatter_dimension=0, tiled=True),
        lax.psum_scatter(flat_gate, ("dp", "group"), scatter_dimension=0, tiled=True),
        lax.psum_scatter(flat_up, ("dp", "group"), scatter_dimension=0, tiled=True),
        lax.psum_scatter(flat_down, ("dp", "group"), scatter_dimension=0, tiled=True),
    )
    grads_local = jnp.concatenate(list(reduced), axis=0)
    gain_grads = lax.psum(
        jnp.concatenate(
            [
                grad_gain_input,
                grad_gain_attn,
                grad_gain_ffin,
                grad_gain_ffout,
                grad_gain_query,
                grad_gain_key,
            ]
        ),
        ("dp", "group"),
    )
    moment_first, moment_second, master_new = adam_update(
        grads_local, first_moment, second_moment, master, learn_rate, weight_decay
    )
    gain_moment_first, gain_moment_second, gains_new = adam_update(
        gain_grads, gain_first, gain_second, gains, gain_rate, 0.0
    )
    return (
        outputs.astype(jnp.bfloat16),
        grad_inputs.astype(jnp.bfloat16),
        moment_first,
        moment_second,
        master_new,
        gain_moment_first,
        gain_moment_second,
        gains_new,
    )


def solution(mesh):
    placed = (
        P(("dp", "group"), None),
        P("dp", None),
        P(("dp", "group"), None),
        P(("dp", "group"), None),
        P(("dp", "group"), None),
        P(("dp", "group"), None),
        P(),
        P(),
        P(),
    )
    return jax.shard_map(
        shards,
        mesh=mesh,
        in_specs=placed,
        out_specs=(
            P(("dp", "group"), None),
            P(("dp", "group"), None),
            P(("dp", "group"), None),
            P(("dp", "group"), None),
            P(("dp", "group"), None),
            P(),
            P(),
            P(),
        ),
        check_vma=False,
    )
```

```python
import functools
import math

import jax
import jax.numpy as jnp
from jax import lax
from jax.experimental import pallas as pl
from jax.experimental.pallas import tpu as pltpu
from jax.sharding import PartitionSpec as P

D = 640
HQ = 4
HD = 256
FF = 2048
WINDOW = 512
STEP = 10
ALL_AXES = ("dp", "group")


norm_eps = 1e-06
rope_base = 10000.0
beta_first = 0.9
beta_second = 0.999
learn_rate = 0.05
gain_rate = 0.25
adam_floor = 1e-08
weight_decay = 0.1


def shifted(value, axis, steps):
    count = lax.axis_size(axis)
    initial, last = (max(0, -steps), min(count, count - steps))
    return lax.ppermute(value, axis, [(source, source + steps) for source in range(initial, last)])


def rms_norm(values, weight_vec):
    return (
        values
        * lax.rsqrt(jnp.mean(values * values, axis=-1, keepdims=True) + norm_eps)
        * (1.0 + weight_vec)
    )


def positions(doc_row):
    length = doc_row.shape[0]
    counter = jnp.arange(length, dtype=jnp.int32)
    starts_here = jnp.concatenate([jnp.ones((1,), jnp.bool_), doc_row[1:] != doc_row[:-1]])
    begins = lax.cummax(jnp.where(starts_here, counter, jnp.zeros_like(counter)), axis=0)
    return counter - begins


def angles_of(places):
    half_dim = HD // 2
    frequency = rope_base ** (-(jnp.arange(half_dim, dtype=jnp.float32) * 2.0 / HD))
    return places.astype(jnp.float32)[:, None] * frequency[None, :]


def rotate(values, angles):
    half_dim = values.shape[-1] // 2
    first_half = values[..., :half_dim]
    second_half = values[..., half_dim:]
    cosine = jnp.cos(angles)
    sine_part = jnp.sin(angles)
    return jnp.concatenate(
        [
            first_half * cosine - second_half * sine_part,
            second_half * cosine + first_half * sine_part,
        ],
        axis=-1,
    )


def geglu(gate_in, up_in):
    return jax.nn.gelu(gate_in, approximate=True) * up_in


def adam_update(gradient, first_old, second_old, params_old, rate, decay_rate):
    first_new = beta_first * first_old + (1.0 - beta_first) * gradient
    second_new = beta_second * second_old + (1.0 - beta_second) * gradient * gradient
    first_hat = first_new / (1.0 - beta_first**STEP)
    second_hat = second_new / (1.0 - beta_second**STEP)
    params_new = params_old - rate * (
        first_hat / (jnp.sqrt(second_hat) + adam_floor) + decay_rate * params_old
    )
    return (first_new, second_new, params_new)


def piece_rows(device_count):
    return [
        entries // (128 * device_count)
        for entries in (D * HQ * HD, D * HD, D * HD, HQ * HD * D, D * FF, D * FF, FF * D)
    ]


def piece_shapes():
    return [(D, HQ * HD), (D, HD), (D, HD), (HQ * HD, D), (D, FF), (D, FF), (FF, D)]


def split_rows(stacked, row_list):
    result = []
    row_start = 0
    for row_count in row_list:
        result.append(stacked[row_start : row_start + row_count])
        row_start = row_start + row_count
    return result


def matmul(left_side, right_side):
    return jnp.dot(left_side, right_side, preferred_element_type=jnp.float32)


LOW_COUNT = 8
LANES = 128
LOW_MASKS = (0, 4, 2, 6, 1, 5, 3, 7)
GELU_SCALE = (2.0 / math.pi) ** 0.5
GELU_CUBE = 0.044715
VMEM_BYTES = 56 * 1024 * 1024


def aligned(device_count):
    groups = lax.axis_size("group") == 4
    return groups and device_count % LOW_COUNT == 0 and D % device_count == 0


def swap(value, mask):
    count = lax.axis_size(ALL_AXES)
    return lax.ppermute(value, ALL_AXES, [(source, source ^ mask) for source in range(count)])


def local_call(kernel, outs, operands, scratch=(), behind=()):
    specs = [pl.BlockSpec(memory_space=pltpu.SMEM)]
    specs = specs + [pl.BlockSpec(memory_space=pltpu.VMEM)] * len(operands)
    specs = specs + [pl.BlockSpec(memory_space=pl.ANY)] * len(behind)
    first, last = 1 + len(operands), 1 + len(operands) + len(behind)

    def body(*refs):
        kernel(*refs[:first], *refs[last:])

    return pl.pallas_call(
        body,
        out_shape=outs,
        in_specs=specs,
        out_specs=tuple(pl.BlockSpec(memory_space=pltpu.VMEM) for _ in outs),
        scratch_shapes=scratch,
        compiler_params=pltpu.CompilerParams(vmem_limit_bytes=VMEM_BYTES),
        cost_estimate=pl.CostEstimate(flops=0, bytes_accessed=0, transcendentals=0),
    )(lax.axis_index(ALL_AXES).astype(jnp.int32).reshape(1), *operands, *behind)


class Piece:
    def __init__(self, rows, columns, device_count):
        self.rows = rows
        self.columns = columns
        self.wide = rows == D
        self.blocks = columns // LANES
        self.own_rows = rows // device_count
        self.flat_rows = self.own_rows * self.blocks
        self.high_count = device_count // LOW_COUNT
        self.block_rows = self.own_rows * self.high_count
        self.size = self.block_rows * self.blocks


def copy_kernel(index_ref, in_ref, out_ref):
    out_ref[...] = in_ref[...]


def pack_kernel(pieces, index_ref, *refs):
    high_count = pieces[0].high_count
    parts, out_refs, flat, packed = refs[:high_count], refs[high_count:-2], refs[-2], refs[-1]
    high = index_ref[0] // LOW_COUNT
    for step, part in enumerate(parts):
        flat[high ^ step] = part[...].astype(jnp.float32)
    start, target = 0, 0
    for piece in pieces:
        for block in range(piece.blocks):
            for place in range(high_count):
                packed[pl.ds(target, piece.own_rows), :] = flat[
                    place, pl.ds(start + block, piece.own_rows, stride=piece.blocks), :
                ]
                target = target + piece.own_rows
        start = start + piece.flat_rows
    count = target // len(out_refs)
    for place, out_ref in enumerate(out_refs):
        out_ref[...] = packed[place * count : (place + 1) * count, :].astype(jnp.bfloat16)


def sum_one_kernel(size, index_ref, near_ref, far_ref, to_x_ref, to_y_ref):
    total = near_ref[...].astype(jnp.float32) + far_ref[...].astype(jnp.float32)
    half = size // 2
    to_x_ref[:half, :] = total[:half].astype(jnp.bfloat16)
    if total.shape[0] > size:
        to_x_ref[half:, :] = total[size:].astype(jnp.bfloat16)
    to_y_ref[...] = total[half:size].astype(jnp.bfloat16)


def sum_three_kernel(
    size,
    index_ref,
    near_ref,
    far_ref,
    *refs,
):
    key_refs = refs[:-5]
    own_ref, beside_first_ref, beside_second_ref, across_first_ref, across_second_ref = refs[-5:]
    half = size // 2
    if key_refs:
        across_key_ref, cores_key_ref = key_refs
        rows = across_key_ref.shape[0]
        keys = across_key_ref[...] + cores_key_ref[rows:, :].astype(jnp.float32)
        for block in range(keys.shape[1] // LANES):
            first = half + block * rows
            columns = slice(block * LANES, (block + 1) * LANES)
            across_second_ref[first : first + rows, :] = keys[:, columns].astype(jnp.bfloat16)
    outs = (beside_first_ref, beside_second_ref, across_first_ref, across_second_ref)
    total = near_ref[:size, :].astype(jnp.float32) + far_ref[:size, :].astype(jnp.float32)
    own_ref[...] = total.astype(jnp.bfloat16)
    for place, out_ref in enumerate(outs):
        rows = slice(size + place * half, size + (place + 1) * half)
        total = near_ref[rows, :].astype(jnp.float32) + far_ref[rows, :].astype(jnp.float32)
        out_ref[:half, :] = total.astype(jnp.bfloat16)


def sum_all_kernel(size, index_ref, near_three, near_one, far_three, far_one, *out_refs):
    sum_one_kernel(size, index_ref, near_one, far_one, *out_refs[:2])
    sum_three_kernel(size, index_ref, near_three, far_three, *out_refs[2:])


def sum_passed_kernel(
    size,
    index_ref,
    beside_ref,
    across_ref,
    over_x_ref,
    over_y_ref,
    near_one_ref,
    far_one_ref,
    beside_out_ref,
    across_out_ref,
    extra_ref,
):
    half = size // 2
    beside = beside_ref[...].astype(jnp.float32) + over_y_ref[...].astype(jnp.float32)
    beside_out_ref[...] = beside.astype(jnp.bfloat16)
    across = across_ref[...].astype(jnp.float32) + over_x_ref[:half, :].astype(jnp.float32)
    across_out_ref[:half, :] = across.astype(jnp.bfloat16)
    if across_out_ref.shape[0] > half:
        extra = near_one_ref[size:, :].astype(jnp.float32)
        extra = extra + far_one_ref[size:, :].astype(jnp.float32)
        extra = extra + over_x_ref[half:, :].astype(jnp.float32)
        extra_ref[...] = extra
        across_out_ref[half:, :] = extra.astype(jnp.bfloat16)
    else:
        extra_ref[...] = jnp.zeros(extra_ref.shape, jnp.float32)


def unpack_kernel(
    pieces,
    index_ref,
    own_ref,
    beside_first_ref,
    beside_second_ref,
    across_first_ref,
    across_second_ref,
    extra_ref,
    *refs,
):
    high_count = pieces[0].high_count
    half = sum(piece.size for piece in pieces) // 2
    flat_rows = sum(piece.flat_rows for piece in pieces)
    outs, flat, packed = refs[:-2], refs[-2], refs[-1]
    high = index_ref[0] // LOW_COUNT
    packed[:half, :] = (
        own_ref[:half, :].astype(jnp.float32)
        + beside_first_ref[...].astype(jnp.float32)
        + across_first_ref[:half, :].astype(jnp.float32)
    )
    packed[half:, :] = (
        own_ref[half:, :].astype(jnp.float32)
        + beside_second_ref[...].astype(jnp.float32)
        + across_second_ref[:half, :].astype(jnp.float32)
    )
    start, source = 0, 0
    for piece in pieces:
        for block in range(piece.blocks):
            for place in range(high_count):
                flat[place, pl.ds(start + block, piece.own_rows, stride=piece.blocks), :] = packed[
                    pl.ds(source, piece.own_rows), :
                ]
                source = source + piece.own_rows
        start = start + piece.flat_rows
    for step, out_ref in enumerate(outs):
        out_ref[:flat_rows, :] = flat[high ^ step].astype(out_ref.dtype)
        if out_ref.shape[0] > flat_rows:
            extra = extra_ref[...] + across_first_ref[half:, :].astype(jnp.float32)
            out_ref[flat_rows:, :] = extra.astype(out_ref.dtype)


def array(shape, kind):
    return jax.ShapeDtypeStruct(shape, kind)


def gather_high(rows):
    high_count = lax.axis_size(ALL_AXES) // LOW_COUNT
    return [rows] + [swap(rows, step * LOW_COUNT) for step in range(1, high_count)]


def gather_own(pieces, parts, count, behind=()):
    high_count = pieces[0].high_count
    size = sum(piece.size for piece in pieces)
    return local_call(
        functools.partial(pack_kernel, pieces),
        (array((size // count, LANES), jnp.bfloat16),) * count,
        parts,
        (
            pltpu.VMEM((high_count, parts[0].shape[0], LANES), jnp.float32),
            pltpu.VMEM((size, LANES), jnp.float32),
        ),
        behind,
    )


def copied(value, behind):
    return local_call(copy_kernel, (array(value.shape, jnp.bfloat16),), (value,), (), behind)[0]


def held(values, behind):
    count = len(values)
    return pl.pallas_call(
        lambda *refs: None,
        out_shape=tuple(array(value.shape, value.dtype) for value in values),
        in_specs=[pl.BlockSpec(memory_space=pl.ANY)] * (count + len(behind)),
        out_specs=tuple(pl.BlockSpec(memory_space=pl.ANY) for _ in values),
        input_output_aliases={place: place for place in range(count)},
        cost_estimate=pl.CostEstimate(flops=0, bytes_accessed=0, transcendentals=0),
    )(*values, *behind)


def gather_halves(first, second):
    return swap(second, 4), swap(first, 2)


def gather_rest(first, second, beside_second, across_first, keys, behind):
    beside_first, across_second = swap(copied(first, keys[:1]), 4), swap(second, 2)
    over_x, over_y = swap(across_first, 4), swap(copied(beside_second, keys[1:]), 2)
    diagonal = held((over_x, over_y), behind)
    return first, second, beside_first, beside_second, across_first, across_second, *diagonal


def gather_wholes(own):
    beside, across = swap(own, 4), swap(own, 2)
    return own, beside, across, swap(across, 4)


def gather_cores(near):
    return near + tuple(swap(value, 1) for value in near)


def scatter_cores(far_three, far_one):
    far_one = swap(far_one, 1)
    return swap(far_three, 1), far_one


def scatter_one(pieces, near_one, far_one, behind=()):
    half = sum(piece.size for piece in pieces) // 2
    to_x, to_y = local_call(
        functools.partial(sum_one_kernel, 2 * half),
        (
            array((near_one.shape[0] - half, LANES), jnp.bfloat16),
            array((half, LANES), jnp.bfloat16),
        ),
        (near_one, far_one),
        (),
        behind,
    )
    return swap(to_x, 4), swap(to_y, 2), to_y


def scatter_three(pieces, near_three, far_three, behind=(), keys=()):
    size = sum(piece.size for piece in pieces)
    half = size // 2
    own, beside_first, beside_second, across_first, across_second = local_call(
        functools.partial(sum_three_kernel, size),
        (
            array((size, LANES), jnp.bfloat16),
            *(array((half, LANES), jnp.bfloat16),) * 3,
            array((half + (keys[0].size // LANES if keys else 0), LANES), jnp.bfloat16),
        ),
        (near_three, far_three, *keys),
        (),
        behind,
    )
    return own, swap(beside_first, 4), beside_second, across_first, swap(across_second, 2)


def scatter_all(pieces, near_three, near_one, far_three, far_one, behind=()):
    size = sum(piece.size for piece in pieces)
    half = size // 2
    to_x, to_y, own, beside_first, beside_second, across_first, across_second = local_call(
        functools.partial(sum_all_kernel, size),
        (
            array((near_one.shape[0] - half, LANES), jnp.bfloat16),
            array((half, LANES), jnp.bfloat16),
            array((size, LANES), jnp.bfloat16),
            *(array((half, LANES), jnp.bfloat16),) * 4,
        ),
        (near_three, near_one, far_three, far_one),
        (),
        behind,
    )
    over_x, over_y = swap(to_x, 4), swap(to_y, 2)
    return (
        over_x,
        over_y,
        (own, swap(beside_first, 4), beside_second, across_first, swap(across_second, 2)),
    )


def scatter_passed(pieces, threes, over_x, over_y, near_one, far_one, behind=()):
    size = sum(piece.size for piece in pieces)
    extra_count = near_one.shape[0] - size
    own, beside_first, beside_second, across_first, across_second = threes
    beside_second, across_first, extra = local_call(
        functools.partial(sum_passed_kernel, size),
        (
            array((size // 2, LANES), jnp.bfloat16),
            array((size // 2 + extra_count, LANES), jnp.bfloat16),
            array((max(extra_count, 8), LANES), jnp.float32),
        ),
        (beside_second, across_first, over_x, over_y, near_one, far_one),
        (),
        behind,
    )
    terms = (
        own,
        beside_first,
        swap(beside_second, 4),
        swap(across_first, 2),
        across_second,
        extra,
    )
    return terms, beside_second


def scatter_high(pieces, terms, behind=()):
    high_count = pieces[0].high_count
    size = sum(piece.size for piece in pieces)
    flat_rows = sum(piece.flat_rows for piece in pieces)
    out_rows = flat_rows + terms[3].shape[0] - size // 2
    outs = local_call(
        functools.partial(unpack_kernel, pieces),
        (array((out_rows, LANES), jnp.float32),)
        + (array((out_rows, LANES), jnp.bfloat16),) * (high_count - 1),
        terms,
        (
            pltpu.VMEM((high_count, flat_rows, LANES), jnp.float32),
            pltpu.VMEM((size, LANES), jnp.float32),
        ),
        behind,
    )
    arrived = [swap(send, step * LOW_COUNT) for step, send in enumerate(outs) if step]
    return outs[0] + sum(value.astype(jnp.float32) for value in arrived), outs[0], arrived


def norm_parts(values):
    scale = lax.rsqrt(jnp.mean(values * values, axis=-1, keepdims=True) + norm_eps)
    return scale, values * scale


def norm_back(scale, normal, upstream, weight_vec):
    weighted = upstream * (1.0 + weight_vec)
    inner = jnp.mean(weighted * normal, axis=-1, keepdims=True)
    return scale * (weighted - normal * inner), jnp.sum(normal * upstream, axis=0, keepdims=True)


def product(left_side, right_side, left_axis, right_axis):
    return lax.dot_general(
        left_side,
        right_side,
        (((left_axis,), (right_axis,)), ((), ())),
        preferred_element_type=jnp.float32,
    )


def unordered(rows_in, order_low):
    upper = rows_in.astype(jnp.bfloat16)
    lower = (rows_in - upper.astype(jnp.float32)).astype(jnp.bfloat16)
    return product(upper, order_low, 1, 1) + product(lower, order_low, 1, 1)


def weight_rows(refs, size, order, start, rows):
    count = len(refs) // LOW_COUNT
    part = size // count
    return refs[order * count + start // part][start % part : start % part + rows, :]


def put_rows(refs, size, order, start, rows):
    three, one = refs[:2] if order < 4 else refs[2:]
    if order % 4 == 3:
        one[start : start + rows.shape[0], :] = rows
    else:
        start = order % 4 * size + start
        three[start : start + rows.shape[0], :] = rows


def wide_tile(refs, size, start, rows):
    return jnp.concatenate(
        [weight_rows(refs, size, order, start, rows) for order in range(LOW_COUNT)]
    )


def put_wide_tile(refs, size, start, rows, tile):
    for order in range(LOW_COUNT):
        put_rows(refs, size, order, start, tile[order * rows : (order + 1) * rows])


def tall_rows(piece, low):
    for order, mask in enumerate(LOW_MASKS):
        for block in range(piece.blocks):
            for place in range(piece.high_count):
                row = (place * LOW_COUNT + (low ^ mask)) * piece.own_rows
                yield (
                    order,
                    block * piece.block_rows + place * piece.own_rows,
                    pl.ds(pl.multiple_of(row, piece.own_rows), piece.own_rows),
                    slice(block * LANES, (block + 1) * LANES),
                )


def ffn_kernel(
    gate_piece,
    down_piece,
    index_ref,
    middle_ref,
    cotangent_ref,
    gain_in_ref,
    gain_out_ref,
    order_ref,
    *refs,
):
    weight_refs, grad_refs = refs[:16], refs[20:24]
    block_out_ref, grad_middle_ref, grad_gain_in_ref, grad_gain_out_ref = refs[16:20]
    down_ref, hidden_ref, gelu_ref, slope_ref = refs[24:]
    low = index_ref[0] % LOW_COUNT
    rows = gate_piece.block_rows
    size = 2 * gate_piece.size + down_piece.size
    width = 2 * LANES
    for order, start, matrix_rows, columns in tall_rows(down_piece, low):
        start = start + 2 * gate_piece.size
        down_ref[matrix_rows, columns] = weight_rows(
            weight_refs, size, order, start, down_piece.own_rows
        )

    def wide_tiles(step):
        return [
            jnp.concatenate(
                [
                    wide_tile(weight_refs, size, offset + block * rows, rows)
                    for block in (2 * step, 2 * step + 1)
                ],
                axis=1,
            )
            for offset in (0, gate_piece.size)
        ]

    middle = middle_ref[...]
    scale_in, normal_in = norm_parts(middle)
    order_low = order_ref[...]
    normed = (normal_in * (1.0 + gain_in_ref[...])).astype(jnp.bfloat16)
    normed = product(normed, order_low, 1, 0).astype(jnp.bfloat16)
    for step in range(FF // width):
        columns = slice(step * width, (step + 1) * width)
        gate_weight, up_weight = wide_tiles(step)
        gate = product(normed, gate_weight, 1, 0)
        up = product(normed, up_weight, 1, 0)
        square = gate * gate
        bend = jnp.tanh(GELU_SCALE * gate * (1.0 + GELU_CUBE * square))
        half = 0.5 * (1.0 + bend)
        gelu = gate * half
        slope = half + 0.5 * gate * (1.0 - bend * bend) * GELU_SCALE * (
            1.0 + 3.0 * GELU_CUBE * square
        )
        gelu_ref[:, columns] = gelu
        slope_ref[:, columns] = slope * up
        hidden_ref[:, columns] = (gelu * up).astype(jnp.bfloat16)
    hidden = hidden_ref[...]
    scale_out, normal_out = norm_parts(product(hidden, down_ref[...], 1, 0))
    block_out_ref[...] = (middle + normal_out * (1.0 + gain_out_ref[...])).astype(jnp.bfloat16)
    upstream = cotangent_ref[...].astype(jnp.float32)
    grad_ffn, grad_gain_out_ref[...] = norm_back(
        scale_out, normal_out, upstream, gain_out_ref[...]
    )
    grad_ffn = grad_ffn.astype(jnp.bfloat16)
    grad_normed = jnp.zeros(middle.shape, jnp.float32)
    for step in range(FF // width):
        columns = slice(step * width, (step + 1) * width)
        grad_hidden = product(grad_ffn, down_ref[columns, :], 1, 1)
        down_ref[columns, :] = product(hidden_ref[:, columns], grad_ffn, 0, 0).astype(jnp.bfloat16)
        grads = [
            (grad_hidden * slope_ref[:, columns]).astype(jnp.bfloat16),
            (grad_hidden * gelu_ref[:, columns]).astype(jnp.bfloat16),
        ]
        for place, (grad, weight) in enumerate(zip(grads, wide_tiles(step))):
            grad_weight = product(normed, grad, 0, 0).astype(jnp.bfloat16)
            for side in range(2):
                put_wide_tile(
                    grad_refs,
                    size,
                    place * gate_piece.size + (2 * step + side) * rows,
                    rows,
                    grad_weight[:, side * LANES : (side + 1) * LANES],
                )
            grad_normed = grad_normed + product(grad, weight, 1, 1)
    for order, start, matrix_rows, columns in tall_rows(down_piece, low):
        start = start + 2 * gate_piece.size
        put_rows(grad_refs, size, order, start, down_ref[matrix_rows, columns])
    grad_middle, grad_gain_in_ref[...] = norm_back(
        scale_in, normal_in, unordered(grad_normed, order_low), gain_in_ref[...]
    )
    grad_middle_ref[...] = upstream + grad_middle


def grad_arrays(pieces, extra_count=0):
    size = sum(piece.size for piece in pieces)
    return (
        array((3 * size, LANES), jnp.bfloat16),
        array((size + extra_count, LANES), jnp.bfloat16),
    ) * 2


def ffn_blocks(pieces, middle, cotangent, gain_in, gain_out, order, blocks):
    rows = middle.shape[0]
    outs = local_call(
        functools.partial(ffn_kernel, pieces[4], pieces[6]),
        (
            array((rows, D), jnp.bfloat16),
            array((rows, D), jnp.float32),
            array((1, D), jnp.float32),
            array((1, D), jnp.float32),
            *grad_arrays(pieces[4:7]),
        ),
        (middle, cotangent, gain_in, gain_out, order, *blocks),
        (
            pltpu.VMEM((FF, D), jnp.bfloat16),
            pltpu.VMEM((rows, FF), jnp.bfloat16),
            pltpu.VMEM((rows, FF), jnp.float32),
            pltpu.VMEM((rows, FF), jnp.float32),
        ),
    )
    return *outs[:4], outs[4:]


def turn(values, cosine, sine):
    first_half, second_half = values[:, : HD // 2], values[:, HD // 2 :]
    return jnp.concatenate(
        [first_half * cosine - second_half * sine, second_half * cosine + first_half * sine], axis=1
    )


def wide_head(refs, size, start, rows):
    return jnp.concatenate(
        [wide_tile(refs, size, start + side * rows, rows) for side in range(2)], axis=1
    )


def head_starts(pieces):
    rows = pieces[0].block_rows
    return [2 * rows * head for head in range(HQ + 2)]


def project_kernel(
    pieces,
    index_ref,
    tokens_ref,
    gain_ref,
    gain_query_ref,
    gain_key_ref,
    cosine_ref,
    sine_ref,
    order_ref,
    *refs,
):
    weight_refs = refs[:8]
    normed_ref, query_proj_ref, key_proj_ref, query_ref, key_value_ref = refs[8:]
    size = sum(piece.size for piece in pieces)
    rows = pieces[0].block_rows
    cosine, sine = cosine_ref[...], sine_ref[...]
    _, normal = norm_parts(tokens_ref[...].astype(jnp.float32))
    normed = (normal * (1.0 + gain_ref[...])).astype(jnp.bfloat16)
    normed = product(normed, order_ref[...], 1, 0).astype(jnp.bfloat16)
    normed_ref[...] = normed
    starts = head_starts(pieces)
    for head, start in enumerate(starts):
        proj = product(normed, wide_head(weight_refs, size, start, rows), 1, 0)
        columns = slice(head * HD, (head + 1) * HD)
        if head == HQ + 1:
            key_value_ref[:, HD:] = proj.astype(jnp.bfloat16)
            continue
        gain_vec = gain_query_ref[...] if head < HQ else gain_key_ref[...]
        _, normal = norm_parts(proj)
        turned = turn(normal * (1.0 + gain_vec), cosine, sine).astype(jnp.bfloat16)
        if head < HQ:
            query_proj_ref[:, columns] = proj
            query_ref[:, columns] = turned
        else:
            key_proj_ref[...] = proj
            key_value_ref[:, :HD] = turned


def attend_kernel(
    pieces,
    index_ref,
    tokens_ref,
    gain_ref,
    allowed_ref,
    query_ref,
    *refs,
):
    weight_refs, key_value_refs = refs[:8], refs[8:-5]
    probs_ref, attended_ref, attn_out_ref, middle_ref, out_weight_ref = refs[-5:]
    out_piece = pieces[-1]
    low = index_ref[0] % LOW_COUNT
    size = sum(piece.size for piece in pieces)
    out_start = size - out_piece.size
    for order, start, matrix_rows, columns in tall_rows(out_piece, low):
        out_weight_ref[matrix_rows, columns] = weight_rows(
            weight_refs, size, order, start + out_start, out_piece.own_rows
        )
    rows = tokens_ref.shape[0]
    allowed = allowed_ref[...] > 0.0
    keys = jnp.concatenate([ref[:, :HD] for ref in key_value_refs])
    values = jnp.concatenate([ref[:, HD:] for ref in key_value_refs])
    count = keys.shape[0]
    for head in range(HQ):
        columns = slice(head * HD, (head + 1) * HD)
        scores = product(query_ref[:, columns], keys, 1, 1) * HD ** (-0.5)
        scores = jnp.where(allowed, scores, -1e30)
        raised = jnp.exp(scores - jnp.max(scores, axis=-1, keepdims=True))
        probs = raised / jnp.sum(raised, axis=-1, keepdims=True)
        probs_ref[:, head * count : (head + 1) * count] = probs
        attended_ref[:, columns] = product(probs.astype(jnp.bfloat16), values, 1, 0).astype(
            jnp.bfloat16
        )
    attn_out = product(attended_ref[...], out_weight_ref[...], 1, 0)
    attn_out_ref[...] = attn_out
    _, normal = norm_parts(attn_out)
    middle_ref[...] = tokens_ref[...].astype(jnp.float32) + normal * (1.0 + gain_ref[...])


def attend_back_kernel(
    index_ref,
    grad_middle_ref,
    attn_out_ref,
    gain_ref,
    out_weight_ref,
    attended_ref,
    probs_ref,
    query_ref,
    *refs,
):
    key_value_refs = refs[:4]
    grad_out_weight_ref, grad_query_ref, grad_gain_ref = refs[4:7]
    grad_own_ref, grad_across_ref, grad_cores_ref = refs[7:]
    rows = query_ref.shape[0]
    scale, normal = norm_parts(attn_out_ref[...])
    grad_attn, grad_gain_ref[...] = norm_back(scale, normal, grad_middle_ref[...], gain_ref[...])
    grad_attn = grad_attn.astype(jnp.bfloat16)
    grad_out_weight_ref[...] = product(attended_ref[...], grad_attn, 0, 0).astype(jnp.bfloat16)
    keys = jnp.concatenate([ref[:, :HD] for ref in key_value_refs])
    values = jnp.concatenate([ref[:, HD:] for ref in key_value_refs])
    count = keys.shape[0]
    grad_keys = jnp.zeros((count, HD), jnp.float32)
    grad_values = jnp.zeros((count, HD), jnp.float32)
    for head in range(HQ):
        columns = slice(head * HD, (head + 1) * HD)
        grad_attended = product(grad_attn, out_weight_ref[columns, :], 1, 1).astype(jnp.bfloat16)
        probs = probs_ref[:, head * count : (head + 1) * count]
        grad_probs = product(grad_attended, values, 1, 1)
        grad_values = grad_values + product(probs.astype(jnp.bfloat16), grad_attended, 0, 0)
        inner = jnp.sum(probs * grad_probs, axis=-1, keepdims=True)
        grad_scores = (probs * (grad_probs - inner) * HD ** (-0.5)).astype(jnp.bfloat16)
        grad_query_ref[:, columns] = product(grad_scores, keys, 1, 0)
        grad_keys = grad_keys + product(grad_scores, query_ref[:, columns], 0, 0)
    targets = (
        grad_own_ref,
        grad_cores_ref.at[:rows],
        grad_across_ref,
        grad_cores_ref.at[rows:],
    )
    for part, ref in enumerate(targets):
        ref[:, :HD] = grad_keys[part * rows : (part + 1) * rows].astype(ref.dtype)
        ref[:, HD:] = grad_values[part * rows : (part + 1) * rows].astype(ref.dtype)


def query_back_kernel(
    pieces,
    index_ref,
    gain_ref,
    cosine_ref,
    sine_ref,
    normed_ref,
    query_proj_ref,
    grad_query_ref,
    *refs,
):
    weight_refs = refs[:8]
    grad_weight_ref, grad_normed_ref, grad_gain_ref = refs[8:]
    size = sum(piece.size for piece in pieces)
    rows = pieces[0].block_rows
    cosine, sine = cosine_ref[...], sine_ref[...]
    normed = normed_ref[...]
    grad_normed = jnp.zeros(grad_normed_ref.shape, jnp.float32)
    grad_gain = jnp.zeros((1, HD), jnp.float32)
    for head, start in enumerate(head_starts(pieces)[:HQ]):
        columns = slice(head * HD, (head + 1) * HD)
        scale, normal = norm_parts(query_proj_ref[:, columns])
        upstream = turn(grad_query_ref[:, columns], cosine, -sine)
        grad, gain_row = norm_back(scale, normal, upstream, gain_ref[...])
        grad_gain = grad_gain + gain_row
        grad = grad.astype(jnp.bfloat16)
        weight = wide_head(weight_refs, size, start, rows)
        grad_normed = grad_normed + product(grad, weight, 1, 1)
        grad_weight_ref[:, columns] = product(normed, grad, 0, 0).astype(jnp.bfloat16)
    grad_normed_ref[...] = grad_normed
    grad_gain_ref[...] = grad_gain


def project_back_kernel(
    pieces,
    index_ref,
    tokens_ref,
    gain_ref,
    gain_key_ref,
    cosine_ref,
    sine_ref,
    order_ref,
    normed_ref,
    key_proj_ref,
    grad_normed_ref,
    grad_middle_ref,
    gain_attn_ref,
    gain_ffin_ref,
    gain_ffout_ref,
    gain_query_ref,
    own_key_ref,
    cores_key_ref,
    across_key_ref,
    *refs,
):
    weight_refs = refs[:8]
    grad_weight_ref, input_grad_ref, grad_gain_ref = refs[8:]
    size = sum(piece.size for piece in pieces)
    rows = pieces[0].block_rows
    normed = normed_ref[...]
    key_rows = own_key_ref.shape[0]
    first = across_key_ref.shape[0] - 4 * key_rows
    key_value = own_key_ref[...] + cores_key_ref[:key_rows, :].astype(jnp.float32)
    key_value = key_value + jnp.concatenate(
        [
            across_key_ref[first + block * key_rows : first + (block + 1) * key_rows, :].astype(
                jnp.float32
            )
            for block in range(4)
        ],
        axis=1,
    )
    scale, normal = norm_parts(key_proj_ref[...])
    upstream = turn(key_value[:, :HD], cosine_ref[...], -sine_ref[...])
    grad_key, grad_gain_key = norm_back(scale, normal, upstream, gain_key_ref[...])
    grad_normed = grad_normed_ref[...]
    for place, start in enumerate(head_starts(pieces)[HQ:]):
        grad = (key_value[:, HD:] if place else grad_key).astype(jnp.bfloat16)
        weight = wide_head(weight_refs, size, start, rows)
        grad_normed = grad_normed + product(grad, weight, 1, 1)
        grad_weight_ref[:, place * HD : (place + 1) * HD] = product(normed, grad, 0, 0).astype(
            jnp.bfloat16
        )
    scale, normal = norm_parts(tokens_ref[...].astype(jnp.float32))
    grad_inputs, grad_gain_input = norm_back(
        scale, normal, unordered(grad_normed, order_ref[...]), gain_ref[...]
    )
    input_grad_ref[...] = (grad_middle_ref[...] + grad_inputs).astype(jnp.bfloat16)
    grad_gains = [
        grad_gain_input,
        gain_attn_ref[...],
        gain_ffin_ref[...],
        gain_ffout_ref[...],
        gain_query_ref[...],
        grad_gain_key,
    ]
    row = 0
    grad_gain_ref[...] = jnp.zeros(grad_gain_ref.shape, jnp.float32)
    for values in grad_gains:
        for start in range(0, values.shape[1], LANES):
            grad_gain_ref[row : row + 1, :] = values[:, start : start + LANES]
            row = row + 1


def split_kernel(
    pieces,
    index_ref,
    query_ref,
    key_value_ref,
    out_ref,
    gain_ref,
    *grad_refs,
):
    low = index_ref[0] % LOW_COUNT
    size = sum(piece.size for piece in pieces)
    rows = pieces[0].block_rows
    start = 0
    for matrix_ref in (query_ref, key_value_ref):
        for column in range(0, matrix_ref.shape[1], LANES):
            tile = matrix_ref[:, column : column + LANES]
            put_wide_tile(grad_refs, size, start, rows, tile)
            start = start + rows
    out_piece = pieces[-1]
    for order, first, matrix_rows, columns in tall_rows(out_piece, low):
        put_rows(grad_refs, size, order, start + first, out_ref[matrix_rows, columns])
    for target in (grad_refs[1], grad_refs[3]):
        target[size:, :] = gain_ref[...].astype(jnp.bfloat16)


def width_order(device_count):
    low = lax.axis_index(ALL_AXES) % LOW_COUNT
    rows = D // device_count
    high_count = device_count // LOW_COUNT
    column = jnp.arange(D, dtype=jnp.int32)
    place = column // (rows * high_count)
    mask = (place & 1) * 4 + ((place >> 1) & 1) * 2 + (place >> 2)
    high = (column // rows) % high_count
    picked = (high * LOW_COUNT + (low ^ mask)) * rows + column % rows
    return (jnp.arange(D, dtype=jnp.int32)[:, None] == picked[None, :]).astype(jnp.bfloat16)


GAIN_ROWS = 32


def shards_blocks(
    device_count,
    tokens,
    doc_ids,
    cotangent,
    master,
    first_moment,
    second_moment,
    gains,
    gain_first,
    gain_second,
):
    pieces = [Piece(*shape_pair, device_count) for shape_pair in piece_shapes()]
    attention_pieces = pieces[:4]
    local_rows = tokens.shape[0]
    group_size = lax.axis_size("group")
    first_row = lax.axis_index("group") * local_rows
    attention_rows = sum(piece.flat_rows for piece in attention_pieces)
    ffn_pieces = pieces[4:7]
    rounded = master.astype(jnp.bfloat16)
    attention_parts = gather_high(rounded[:attention_rows])
    ffn_rows = rounded[attention_rows:]
    ffn_parts = gather_high(ffn_rows)
    attention_near = gather_wholes(
        *gather_own(attention_pieces, attention_parts, 1, (ffn_parts[1],))
    )
    attention_blocks = gather_cores(attention_near)
    ffn_own = gather_own(ffn_pieces, ffn_parts, 2, attention_near[1:])
    ffn_passed = gather_halves(*ffn_own)
    gain_parts = []
    for start, width in ((0, D), (D, D), (2 * D, D), (3 * D, D), (4 * D, HD), (4 * D + HD, HD)):
        gain_parts.append(gains[start : start + width][None])
    gain_input, gain_attn, gain_ffin, gain_ffout, gain_query, gain_key = gain_parts
    order = width_order(device_count)
    doc_row = doc_ids[0]
    angles = lax.dynamic_slice_in_dim(angles_of(positions(doc_row)), first_row, local_rows, 0)
    cosine, sine = jnp.cos(angles), jnp.sin(angles)
    query_docs = lax.dynamic_slice_in_dim(doc_row, first_row, local_rows, 0)
    key_count = group_size * local_rows
    first_keys = [(lax.axis_index("group") ^ step) * local_rows for step in range(group_size)]
    key_docs = jnp.concatenate(
        [lax.dynamic_slice_in_dim(doc_row, start, local_rows, 0) for start in first_keys]
    )
    key_index = jnp.concatenate(
        [start + jnp.arange(local_rows, dtype=jnp.int32) for start in first_keys]
    )
    query_index = first_row + jnp.arange(local_rows, dtype=jnp.int32)
    distance = query_index[:, None] - key_index[None, :]
    allowed = (distance >= 0) & (distance < WINDOW) & (key_docs[None, :] == query_docs[:, None])
    allowed = allowed.astype(jnp.float32)

    width = HQ * HD
    normed, query_proj, key_proj, query_rot, key_value = local_call(
        functools.partial(project_kernel, attention_pieces),
        (
            array((local_rows, D), jnp.bfloat16),
            array((local_rows, width), jnp.float32),
            array((local_rows, HD), jnp.float32),
            array((local_rows, width), jnp.bfloat16),
            array((local_rows, 2 * HD), jnp.bfloat16),
        ),
        (tokens, gain_input, gain_query, gain_key, cosine, sine, order, *attention_blocks),
    )
    key_values = [key_value] + [swap(key_value, step) for step in range(1, group_size)]
    probs, attended, attn_out, middle, out_weight = local_call(
        functools.partial(attend_kernel, attention_pieces),
        (
            array((local_rows, HQ * key_count), jnp.float32),
            array((local_rows, width), jnp.bfloat16),
            array((local_rows, D), jnp.float32),
            array((local_rows, D), jnp.float32),
            array((width, D), jnp.bfloat16),
        ),
        (tokens, gain_attn, allowed, query_rot, *attention_blocks, *key_values),
    )
    ffn_weights = gather_cores(gather_rest(*ffn_own, *ffn_passed, key_values, (middle,)))
    outputs, grad_middle, grad_gain_ffin, grad_gain_ffout, grads_ffn = ffn_blocks(
        pieces, middle, cotangent, gain_ffin, gain_ffout, order, ffn_weights
    )
    near_three, near_one, far_three, far_one = grads_ffn
    far_three, far_one = scatter_cores(far_three, far_one)
    grad_out_weight, grad_query, grad_gain_attn, own_key, across_key, cores_key = local_call(
        attend_back_kernel,
        (
            array((width, D), jnp.bfloat16),
            array((local_rows, width), jnp.float32),
            array((1, D), jnp.float32),
            array((local_rows, 2 * HD), jnp.float32),
            array((local_rows, 2 * HD), jnp.float32),
            array((2 * local_rows, 2 * HD), jnp.bfloat16),
        ),
        (
            grad_middle,
            attn_out,
            gain_attn,
            out_weight,
            attended,
            probs,
            query_rot,
            *key_values,
        ),
    )
    cores_key = swap(cores_key, 1)
    over_x, over_y, sent = scatter_one(ffn_pieces, near_one, far_one, (grad_query,))
    threes = scatter_three(ffn_pieces, near_three, far_three, (sent,), (across_key, cores_key))
    grad_query_weight, grad_normed, grad_gain_query = local_call(
        functools.partial(query_back_kernel, attention_pieces),
        (
            array((D, width), jnp.bfloat16),
            array((local_rows, D), jnp.float32),
            array((1, HD), jnp.float32),
        ),
        (gain_query, cosine, sine, normed, query_proj, grad_query, *attention_blocks),
        (),
        (threes[0],),
    )
    ffn_terms, sent = scatter_passed(
        ffn_pieces, threes, over_x, over_y, near_one, far_one, (grad_normed,)
    )
    grad_key_weight, grad_inputs, grad_gains = local_call(
        functools.partial(project_back_kernel, attention_pieces),
        (
            array((D, 2 * HD), jnp.bfloat16),
            array((local_rows, D), jnp.bfloat16),
            array((GAIN_ROWS, LANES), jnp.float32),
        ),
        (
            tokens,
            gain_input,
            gain_key,
            cosine,
            sine,
            order,
            normed,
            key_proj,
            grad_normed,
            grad_middle,
            grad_gain_attn,
            grad_gain_ffin,
            grad_gain_ffout,
            grad_gain_query,
            own_key,
            cores_key,
            threes[4],
            *attention_blocks,
        ),
        (),
        (sent, threes[1]),
    )
    near_three, near_one, far_three, far_one = local_call(
        functools.partial(split_kernel, attention_pieces),
        grad_arrays(attention_pieces, GAIN_ROWS),
        (grad_query_weight, grad_key_weight, grad_out_weight, grad_gains),
    )
    far_three, far_one = held((far_three, far_one), ffn_terms[2:4])
    grads_ffn, sent, arrived = scatter_high(ffn_pieces, ffn_terms, (near_one,))
    far_three, far_one = scatter_cores(far_three, far_one)
    over_x, over_y, threes = scatter_all(
        attention_pieces, near_three, near_one, far_three, far_one, (sent,)
    )
    terms, _ = scatter_passed(
        attention_pieces, threes, over_x, over_y, near_one, far_one, (arrived[0],)
    )
    grads_attention, _, _ = scatter_high(attention_pieces, terms, arrived)
    gain_grads = grads_attention[attention_rows:].reshape(-1)[: gains.shape[0]]
    grads_local = jnp.concatenate([grads_attention[:attention_rows], grads_ffn])
    return (
        outputs,
        grad_inputs,
        *adam_update(grads_local, first_moment, second_moment, master, learn_rate, weight_decay),
        *adam_update(gain_grads, gain_first, gain_second, gains, gain_rate, 0.0),
    )


def shards(
    tokens, doc_ids, cotangent, master, first_moment, second_moment, gains, gain_first, gain_second
):
    group_size = lax.axis_size("group")
    devices_all = lax.axis_size("dp") * group_size
    if aligned(devices_all):
        return shards_blocks(
            devices_all,
            tokens,
            doc_ids,
            cotangent,
            master,
            first_moment,
            second_moment,
            gains,
            gain_first,
            gain_second,
        )
    group_index = lax.axis_index("group")
    local_rows = tokens.shape[0]
    shard_parts = [
        part_rows.astype(jnp.bfloat16) for part_rows in split_rows(master, piece_rows(devices_all))
    ]
    gathered = (
        lax.all_gather(shard_parts[0], ("dp", "group"), axis=0, tiled=True),
        lax.all_gather(shard_parts[1], ("dp", "group"), axis=0, tiled=True),
        lax.all_gather(shard_parts[2], ("dp", "group"), axis=0, tiled=True),
        lax.all_gather(shard_parts[3], ("dp", "group"), axis=0, tiled=True),
        lax.all_gather(shard_parts[4], ("dp", "group"), axis=0, tiled=True),
        lax.all_gather(shard_parts[5], ("dp", "group"), axis=0, tiled=True),
        lax.all_gather(shard_parts[6], ("dp", "group"), axis=0, tiled=True),
    )
    query_weight, key_weight, value_weight, out_weight, gate_weight, up_weight, down_weight = [
        full_rows.reshape(shape_pair) for full_rows, shape_pair in zip(gathered, piece_shapes())
    ]
    norm_input = gains[0:D]
    norm_attn = gains[D : 2 * D]
    norm_ffin = gains[2 * D : 3 * D]
    norm_ffout = gains[3 * D : 4 * D]
    norm_query = gains[4 * D : 4 * D + HD]
    norm_key = gains[4 * D + HD : 4 * D + 2 * HD]
    doc_row = doc_ids[0]
    first_row = group_index * local_rows
    angles = lax.dynamic_slice_in_dim(angles_of(positions(doc_row)), first_row, local_rows, 0)
    query_docs = lax.dynamic_slice_in_dim(doc_row, first_row, local_rows, 0)
    inputs = tokens.astype(jnp.float32)
    normed, back_input = jax.vjp(rms_norm, inputs, norm_input)
    normed_low = normed.astype(jnp.bfloat16)
    query_proj = matmul(normed_low, query_weight)
    key_proj = matmul(normed_low, key_weight)
    value_proj = matmul(normed_low, value_weight)

    def query_prep(flat_rows, gain_vec):
        return rotate(rms_norm(flat_rows.reshape(local_rows, HQ, HD), gain_vec), angles[:, None, :])

    def key_prep(rows_in, gain_vec):
        return rotate(rms_norm(rows_in, gain_vec), angles)

    query_rot, back_query = jax.vjp(query_prep, query_proj, norm_query)
    key_rot, back_key = jax.vjp(key_prep, key_proj, norm_key)
    query_low = query_rot.astype(jnp.bfloat16)
    key_low = key_rot.astype(jnp.bfloat16)
    value_low = value_proj.astype(jnp.bfloat16)
    reach = min(-(-(WINDOW - 1) // local_rows), group_size - 1)
    key_list = [key_low]
    value_list = [value_low]
    for offset in range(1, reach + 1):
        key_far, value_far = shifted((key_low, value_low), "group", offset)
        key_list.insert(0, key_far)
        value_list.insert(0, value_far)
    key_all = jnp.concatenate(key_list, axis=0)
    value_all = jnp.concatenate(value_list, axis=0)
    key_count = (reach + 1) * local_rows
    doc_pad = jnp.concatenate([jnp.full((reach * local_rows,), -1, jnp.int32), doc_row])
    key_docs = lax.dynamic_slice_in_dim(doc_pad, first_row, key_count, 0)
    key_index = (group_index - reach) * local_rows + jnp.arange(key_count, dtype=jnp.int32)
    query_index = first_row + jnp.arange(local_rows, dtype=jnp.int32)
    distance = query_index[:, None] - key_index[None, :]
    allowed = (distance >= 0) & (distance < WINDOW) & (key_docs[None, :] == query_docs[:, None])

    def scores_of(key_rows_low):
        raw_scores = jnp.einsum(
            "qhd,kd->hqk", query_low, key_rows_low, preferred_element_type=jnp.float32
        ) * HD ** (-0.5)
        return jnp.where(allowed[None], raw_scores, -1e30)

    masked = scores_of(key_all)
    top_score = jnp.max(masked, axis=-1, keepdims=True)
    log_total = top_score + jnp.log(jnp.sum(jnp.exp(masked - top_score), axis=-1, keepdims=True))
    probs = jnp.exp(masked - log_total)
    attended = jnp.einsum(
        "hqk,kd->qhd", probs.astype(jnp.bfloat16), value_all, preferred_element_type=jnp.float32
    )
    attended_low = attended.reshape(local_rows, HQ * HD).astype(jnp.bfloat16)
    attn_out = matmul(attended_low, out_weight)
    branch_one, back_attn = jax.vjp(rms_norm, attn_out, norm_attn)
    middle = inputs + branch_one
    normed_two, back_ffin = jax.vjp(rms_norm, middle, norm_ffin)
    normed_two_low = normed_two.astype(jnp.bfloat16)
    gate_proj = matmul(normed_two_low, gate_weight)
    up_proj = matmul(normed_two_low, up_weight)
    hidden, back_hidden = jax.vjp(geglu, gate_proj, up_proj)
    hidden_low = hidden.astype(jnp.bfloat16)
    ffn_out = matmul(hidden_low, down_weight)
    branch_two, back_ffout = jax.vjp(rms_norm, ffn_out, norm_ffout)
    outputs = middle + branch_two
    grad_out = cotangent.astype(jnp.float32)
    grad_ffn, grad_gain_ffout = back_ffout(grad_out)
    grad_ffn_low = grad_ffn.astype(jnp.bfloat16)
    grad_down_w = jnp.einsum(
        "tf,td->fd", hidden_low, grad_ffn_low, preferred_element_type=jnp.float32
    )
    grad_hidden = jnp.einsum(
        "td,fd->tf", grad_ffn_low, down_weight, preferred_element_type=jnp.float32
    )
    grad_gate, grad_up = back_hidden(grad_hidden)
    grad_gate_low = grad_gate.astype(jnp.bfloat16)
    grad_up_low = grad_up.astype(jnp.bfloat16)
    grad_gate_w = jnp.einsum(
        "td,tf->df", normed_two_low, grad_gate_low, preferred_element_type=jnp.float32
    )
    grad_up_w = jnp.einsum(
        "td,tf->df", normed_two_low, grad_up_low, preferred_element_type=jnp.float32
    )
    grad_normed_two = jnp.einsum(
        "tf,df->td", grad_gate_low, gate_weight, preferred_element_type=jnp.float32
    ) + jnp.einsum("tf,df->td", grad_up_low, up_weight, preferred_element_type=jnp.float32)
    grad_middle_norm, grad_gain_ffin = back_ffin(grad_normed_two)
    grad_middle = grad_out + grad_middle_norm
    grad_attn, grad_gain_attn = back_attn(grad_middle)
    grad_attn_low = grad_attn.astype(jnp.bfloat16)
    grad_out_w = jnp.einsum(
        "to,td->od", attended_low, grad_attn_low, preferred_element_type=jnp.float32
    )
    grad_attended = jnp.einsum(
        "td,od->to", grad_attn_low, out_weight, preferred_element_type=jnp.float32
    )
    grad_attended_low = grad_attended.astype(jnp.bfloat16).reshape(local_rows, HQ, HD)
    probs_again = jnp.exp(scores_of(key_all) - log_total)
    grad_probs = jnp.einsum(
        "qhd,kd->hqk", grad_attended_low, value_all, preferred_element_type=jnp.float32
    )
    grad_value_all = jnp.einsum(
        "hqk,qhd->kd",
        probs_again.astype(jnp.bfloat16),
        grad_attended_low,
        preferred_element_type=jnp.float32,
    )
    grad_scores = probs_again * (
        grad_probs - jnp.sum(probs_again * grad_probs, axis=-1, keepdims=True)
    )
    grad_scores_low = (grad_scores * HD ** (-0.5)).astype(jnp.bfloat16)
    grad_query = jnp.einsum(
        "hqk,kd->qhd", grad_scores_low, key_all, preferred_element_type=jnp.float32
    )
    grad_key_all = jnp.einsum(
        "hqk,qhd->kd", grad_scores_low, query_low, preferred_element_type=jnp.float32
    )
    key_total = grad_key_all[reach * local_rows :]
    value_total = grad_value_all[reach * local_rows :]
    for offset in range(1, reach + 1):
        row_start = (reach - offset) * local_rows
        key_back, value_back = (
            shifted(
                grad_key_all[row_start : row_start + local_rows].astype(jnp.bfloat16),
                "group",
                -offset,
            ).astype(jnp.float32),
            shifted(
                grad_value_all[row_start : row_start + local_rows].astype(jnp.bfloat16),
                "group",
                -offset,
            ).astype(jnp.float32),
        )
        key_total = key_total + key_back
        value_total = value_total + value_back
    grad_query_proj, grad_gain_query = back_query(grad_query)
    grad_key_proj, grad_gain_key = back_key(key_total)
    grad_query_low = grad_query_proj.astype(jnp.bfloat16)
    grad_key_low = grad_key_proj.astype(jnp.bfloat16)
    grad_value_low = value_total.astype(jnp.bfloat16)
    grad_query_w = jnp.einsum(
        "td,te->de", normed_low, grad_query_low, preferred_element_type=jnp.float32
    )
    grad_key_w = jnp.einsum(
        "td,te->de", normed_low, grad_key_low, preferred_element_type=jnp.float32
    )
    grad_value_w = jnp.einsum(
        "td,te->de", normed_low, grad_value_low, preferred_element_type=jnp.float32
    )
    grad_normed = jnp.einsum(
        "te,de->td", grad_query_low, query_weight, preferred_element_type=jnp.float32
    )
    grad_normed = grad_normed + jnp.einsum(
        "te,de->td", grad_key_low, key_weight, preferred_element_type=jnp.float32
    )
    grad_normed = grad_normed + jnp.einsum(
        "te,de->td", grad_value_low, value_weight, preferred_element_type=jnp.float32
    )
    grad_input_norm, grad_gain_input = back_input(grad_normed)
    grad_inputs = grad_middle + grad_input_norm
    flat_query = grad_query_w.reshape(-1, 128)
    flat_key = grad_key_w.reshape(-1, 128)
    flat_value = grad_value_w.reshape(-1, 128)
    flat_out = grad_out_w.reshape(-1, 128)
    flat_gate = grad_gate_w.reshape(-1, 128)
    flat_up = grad_up_w.reshape(-1, 128)
    flat_down = grad_down_w.reshape(-1, 128)
    reduced = (
        lax.psum_scatter(flat_query, ("dp", "group"), scatter_dimension=0, tiled=True),
        lax.psum_scatter(flat_key, ("dp", "group"), scatter_dimension=0, tiled=True),
        lax.psum_scatter(flat_value, ("dp", "group"), scatter_dimension=0, tiled=True),
        lax.psum_scatter(flat_out, ("dp", "group"), scatter_dimension=0, tiled=True),
        lax.psum_scatter(flat_gate, ("dp", "group"), scatter_dimension=0, tiled=True),
        lax.psum_scatter(flat_up, ("dp", "group"), scatter_dimension=0, tiled=True),
        lax.psum_scatter(flat_down, ("dp", "group"), scatter_dimension=0, tiled=True),
    )
    grads_local = jnp.concatenate(list(reduced), axis=0)
    gain_grads = lax.psum(
        jnp.concatenate(
            [
                grad_gain_input,
                grad_gain_attn,
                grad_gain_ffin,
                grad_gain_ffout,
                grad_gain_query,
                grad_gain_key,
            ]
        ),
        ("dp", "group"),
    )
    moment_first, moment_second, master_new = adam_update(
        grads_local, first_moment, second_moment, master, learn_rate, weight_decay
    )
    gain_moment_first, gain_moment_second, gains_new = adam_update(
        gain_grads, gain_first, gain_second, gains, gain_rate, 0.0
    )
    return (
        outputs.astype(jnp.bfloat16),
        grad_inputs.astype(jnp.bfloat16),
        moment_first,
        moment_second,
        master_new,
        gain_moment_first,
        gain_moment_second,
        gains_new,
    )


def solution(mesh):
    placed = (
        P(("dp", "group"), None),
        P("dp", None),
        P(("dp", "group"), None),
        P(("dp", "group"), None),
        P(("dp", "group"), None),
        P(("dp", "group"), None),
        P(),
        P(),
        P(),
    )
    return jax.shard_map(
        shards,
        mesh=mesh,
        in_specs=placed,
        out_specs=(
            P(("dp", "group"), None),
            P(("dp", "group"), None),
            P(("dp", "group"), None),
            P(("dp", "group"), None),
            P(("dp", "group"), None),
            P(),
            P(),
            P(),
        ),
        check_vma=False,
    )
```

```python
import functools
import math

import jax
import jax.numpy as jnp
from jax import lax
from jax.experimental import pallas as pl
from jax.experimental.pallas import tpu as pltpu
from jax.sharding import PartitionSpec as P

D = 640
HQ = 4
HD = 256
FF = 2048
WINDOW = 512
STEP = 10
ALL_AXES = ("dp", "group")


norm_eps = 1e-06
rope_base = 10000.0
beta_first = 0.9
beta_second = 0.999
learn_rate = 0.05
gain_rate = 0.25
adam_floor = 1e-08
weight_decay = 0.1


def shifted(value, axis, steps):
    count = lax.axis_size(axis)
    initial, last = (max(0, -steps), min(count, count - steps))
    return lax.ppermute(value, axis, [(source, source + steps) for source in range(initial, last)])


def rms_norm(values, weight_vec):
    return (
        values
        * lax.rsqrt(jnp.mean(values * values, axis=-1, keepdims=True) + norm_eps)
        * (1.0 + weight_vec)
    )


def positions(doc_row):
    length = doc_row.shape[0]
    counter = jnp.arange(length, dtype=jnp.int32)
    starts_here = jnp.concatenate([jnp.ones((1,), jnp.bool_), doc_row[1:] != doc_row[:-1]])
    begins = lax.cummax(jnp.where(starts_here, counter, jnp.zeros_like(counter)), axis=0)
    return counter - begins


def angles_of(places):
    half_dim = HD // 2
    frequency = rope_base ** (-(jnp.arange(half_dim, dtype=jnp.float32) * 2.0 / HD))
    return places.astype(jnp.float32)[:, None] * frequency[None, :]


def rotate(values, angles):
    half_dim = values.shape[-1] // 2
    first_half = values[..., :half_dim]
    second_half = values[..., half_dim:]
    cosine = jnp.cos(angles)
    sine_part = jnp.sin(angles)
    return jnp.concatenate(
        [
            first_half * cosine - second_half * sine_part,
            second_half * cosine + first_half * sine_part,
        ],
        axis=-1,
    )


def geglu(gate_in, up_in):
    return jax.nn.gelu(gate_in, approximate=True) * up_in


def adam_update(gradient, first_old, second_old, params_old, rate, decay_rate):
    first_new = beta_first * first_old + (1.0 - beta_first) * gradient
    second_new = beta_second * second_old + (1.0 - beta_second) * gradient * gradient
    first_hat = first_new / (1.0 - beta_first**STEP)
    second_hat = second_new / (1.0 - beta_second**STEP)
    params_new = params_old - rate * (
        first_hat / (jnp.sqrt(second_hat) + adam_floor) + decay_rate * params_old
    )
    return (first_new, second_new, params_new)


def piece_rows(device_count):
    return [
        entries // (128 * device_count)
        for entries in (D * HQ * HD, D * HD, D * HD, HQ * HD * D, D * FF, D * FF, FF * D)
    ]


def piece_shapes():
    return [(D, HQ * HD), (D, HD), (D, HD), (HQ * HD, D), (D, FF), (D, FF), (FF, D)]


def split_rows(stacked, row_list):
    result = []
    row_start = 0
    for row_count in row_list:
        result.append(stacked[row_start : row_start + row_count])
        row_start = row_start + row_count
    return result


def matmul(left_side, right_side):
    return jnp.dot(left_side, right_side, preferred_element_type=jnp.float32)


LOW_COUNT = 8
LANES = 128
LOW_MASKS = (0, 4, 2, 6, 1, 5, 3, 7)
GELU_SCALE = (2.0 / math.pi) ** 0.5
GELU_CUBE = 0.044715
VMEM_BYTES = 56 * 1024 * 1024


def aligned(device_count):
    groups = lax.axis_size("group") == 4
    return groups and device_count % LOW_COUNT == 0 and D % device_count == 0


def swap(value, mask):
    count = lax.axis_size(ALL_AXES)
    return lax.ppermute(value, ALL_AXES, [(source, source ^ mask) for source in range(count)])


def local_call(kernel, outs, operands, scratch=(), behind=()):
    specs = [pl.BlockSpec(memory_space=pltpu.SMEM)]
    specs = specs + [pl.BlockSpec(memory_space=pltpu.VMEM)] * len(operands)
    specs = specs + [pl.BlockSpec(memory_space=pl.ANY)] * len(behind)
    first, last = 1 + len(operands), 1 + len(operands) + len(behind)

    def body(*refs):
        kernel(*refs[:first], *refs[last:])

    return pl.pallas_call(
        body,
        out_shape=outs,
        in_specs=specs,
        out_specs=tuple(pl.BlockSpec(memory_space=pltpu.VMEM) for _ in outs),
        scratch_shapes=scratch,
        compiler_params=pltpu.CompilerParams(vmem_limit_bytes=VMEM_BYTES),
        cost_estimate=pl.CostEstimate(flops=0, bytes_accessed=0, transcendentals=0),
    )(lax.axis_index(ALL_AXES).astype(jnp.int32).reshape(1), *operands, *behind)


class Piece:
    def __init__(self, rows, columns, device_count):
        self.rows = rows
        self.columns = columns
        self.wide = rows == D
        self.blocks = columns // LANES
        self.own_rows = rows // device_count
        self.flat_rows = self.own_rows * self.blocks
        self.high_count = device_count // LOW_COUNT
        self.block_rows = self.own_rows * self.high_count
        self.size = self.block_rows * self.blocks


def copy_kernel(index_ref, in_ref, out_ref):
    out_ref[...] = in_ref[...]


def pack_kernel(pieces, index_ref, *refs):
    high_count = pieces[0].high_count
    parts, out_refs, flat, packed = refs[:high_count], refs[high_count:-2], refs[-2], refs[-1]
    high = index_ref[0] // LOW_COUNT
    for step, part in enumerate(parts):
        flat[high ^ step] = part[...].astype(jnp.float32)
    start, target = 0, 0
    for piece in pieces:
        for block in range(piece.blocks):
            for place in range(high_count):
                packed[pl.ds(target, piece.own_rows), :] = flat[
                    place, pl.ds(start + block, piece.own_rows, stride=piece.blocks), :
                ]
                target = target + piece.own_rows
        start = start + piece.flat_rows
    count = target // len(out_refs)
    for place, out_ref in enumerate(out_refs):
        out_ref[...] = packed[place * count : (place + 1) * count, :].astype(jnp.bfloat16)


def sum_one_kernel(
    size, index_ref, near_ref, far_ref, across_key_ref, cores_key_ref, to_x_ref, to_y_ref
):
    total = near_ref[...].astype(jnp.float32) + far_ref[...].astype(jnp.float32)
    half = size // 2
    to_x_ref[...] = total[:half].astype(jnp.bfloat16)
    to_y_ref[:half, :] = total[half:].astype(jnp.bfloat16)
    rows = across_key_ref.shape[0]
    keys = across_key_ref[...] + cores_key_ref[rows:, :].astype(jnp.float32)
    for block in range(keys.shape[1] // LANES):
        first = half + block * rows
        columns = slice(block * LANES, (block + 1) * LANES)
        to_y_ref[first : first + rows, :] = keys[:, columns].astype(jnp.bfloat16)


def sum_three_kernel(
    size,
    index_ref,
    near_ref,
    far_ref,
    own_ref,
    beside_first_ref,
    beside_second_ref,
    across_first_ref,
    across_second_ref,
):
    half = size // 2
    outs = (beside_first_ref, beside_second_ref, across_first_ref, across_second_ref)
    total = near_ref[:size, :].astype(jnp.float32) + far_ref[:size, :].astype(jnp.float32)
    own_ref[...] = total.astype(jnp.bfloat16)
    for place, out_ref in enumerate(outs):
        rows = slice(size + place * half, size + (place + 1) * half)
        total = near_ref[rows, :].astype(jnp.float32) + far_ref[rows, :].astype(jnp.float32)
        out_ref[...] = total.astype(jnp.bfloat16)


def sum_all_kernel(size, index_ref, near_three, near_one, far_three, far_one, *out_refs):
    extra = near_one[size:, :].astype(jnp.float32) + far_one[size:, :].astype(jnp.float32)
    for place, out_ref in enumerate(out_refs):
        near, far, first = near_three, far_three, place * size
        if place == 3:
            near, far, first = near_one, far_one, 0
        rows = slice(first, first + size)
        total = near[rows, :].astype(jnp.float32) + far[rows, :].astype(jnp.float32)
        out_ref[:size, :] = total.astype(jnp.bfloat16)
        out_ref[size:, :] = extra.astype(jnp.bfloat16)


def sum_passed_kernel(
    index_ref,
    beside_ref,
    across_ref,
    over_x_ref,
    over_y_ref,
    beside_out_ref,
    across_out_ref,
):
    half = beside_ref.shape[0]
    beside = beside_ref[...].astype(jnp.float32) + over_y_ref[:half, :].astype(jnp.float32)
    beside_out_ref[...] = beside.astype(jnp.bfloat16)
    across = across_ref[...].astype(jnp.float32) + over_x_ref[...].astype(jnp.float32)
    across_out_ref[...] = across.astype(jnp.bfloat16)


def unpack_kernel(pieces, term_rows, index_ref, *refs):
    high_count = pieces[0].high_count
    flat_rows = sum(piece.flat_rows for piece in pieces)
    terms, outs = refs[: -2 - high_count], refs[-2 - high_count : -2]
    flat, packed = refs[-2:]
    high = index_ref[0] // LOW_COUNT
    count = len(terms) * term_rows // packed.shape[0]
    for first in range(0, packed.shape[0], term_rows):
        place = first // term_rows * count
        packed[first : first + term_rows, :] = sum(
            term[:term_rows, :].astype(jnp.float32) for term in terms[place : place + count]
        )
    start, source = 0, 0
    for piece in pieces:
        for block in range(piece.blocks):
            for place in range(high_count):
                flat[place, pl.ds(start + block, piece.own_rows, stride=piece.blocks), :] = packed[
                    pl.ds(source, piece.own_rows), :
                ]
                source = source + piece.own_rows
        start = start + piece.flat_rows
    for step, out_ref in enumerate(outs):
        out_ref[:flat_rows, :] = flat[high ^ step].astype(out_ref.dtype)
        if out_ref.shape[0] > flat_rows:
            extra = sum(term[term_rows:, :].astype(jnp.float32) for term in terms)
            out_ref[flat_rows:, :] = extra.astype(out_ref.dtype)


def array(shape, kind):
    return jax.ShapeDtypeStruct(shape, kind)


def gather_high(rows):
    high_count = lax.axis_size(ALL_AXES) // LOW_COUNT
    return [rows] + [swap(rows, step * LOW_COUNT) for step in range(1, high_count)]


def gather_own(pieces, parts, count, behind=()):
    high_count = pieces[0].high_count
    size = sum(piece.size for piece in pieces)
    return local_call(
        functools.partial(pack_kernel, pieces),
        (array((size // count, LANES), jnp.bfloat16),) * count,
        parts,
        (
            pltpu.VMEM((high_count, parts[0].shape[0], LANES), jnp.float32),
            pltpu.VMEM((size, LANES), jnp.float32),
        ),
        behind,
    )


def copied(value, behind):
    return local_call(copy_kernel, (array(value.shape, jnp.bfloat16),), (value,), (), behind)[0]


def held(values, behind):
    count = len(values)
    return pl.pallas_call(
        lambda *refs: None,
        out_shape=tuple(array(value.shape, value.dtype) for value in values),
        in_specs=[pl.BlockSpec(memory_space=pl.ANY)] * (count + len(behind)),
        out_specs=tuple(pl.BlockSpec(memory_space=pl.ANY) for _ in values),
        input_output_aliases={place: place for place in range(count)},
        cost_estimate=pl.CostEstimate(flops=0, bytes_accessed=0, transcendentals=0),
    )(*values, *behind)


def gather_halves(first, second):
    return swap(second, 4), swap(first, 2)


def gather_rest(first, second, beside_second, across_first, keys, behind):
    beside_first, across_second = swap(copied(first, keys[:1]), 4), swap(second, 2)
    over_x, over_y = swap(across_first, 4), swap(copied(beside_second, keys[1:]), 2)
    diagonal = held((over_x, over_y), behind)
    return first, second, beside_first, beside_second, across_first, across_second, *diagonal


def gather_wholes(own):
    return own, swap(own, 4), swap(own, 2), swap(own, 6)


def gather_cores(near):
    return near + tuple(swap(value, 1) for value in near)


def scatter_cores(far_three, far_one):
    far_one = swap(far_one, 1)
    return swap(far_three, 1), far_one


def scatter_one(pieces, near_one, far_one, keys):
    half = sum(piece.size for piece in pieces) // 2
    to_x, to_y = local_call(
        functools.partial(sum_one_kernel, 2 * half),
        (
            array((half, LANES), jnp.bfloat16),
            array((half + keys[0].size // LANES, LANES), jnp.bfloat16),
        ),
        (near_one, far_one, *keys),
    )
    return swap(to_x, 4), swap(to_y, 2), to_x


def scatter_three(pieces, near_three, far_three, behind=()):
    size = sum(piece.size for piece in pieces)
    half = size // 2
    own, beside_first, beside_second, across_first, across_second = local_call(
        functools.partial(sum_three_kernel, size),
        (
            array((size, LANES), jnp.bfloat16),
            *(array((half, LANES), jnp.bfloat16),) * 4,
        ),
        (near_three, far_three),
        (),
        behind,
    )
    return own, swap(beside_first, 4), beside_second, across_first, swap(across_second, 2)


def scatter_passed(threes, over_x, over_y, behind=()):
    own, beside_first, beside_second, across_first, across_second = threes
    half = beside_second.shape[0]
    beside_second, across_first = local_call(
        sum_passed_kernel,
        (array((half, LANES), jnp.bfloat16),) * 2,
        (beside_second, across_first, over_x, over_y),
        (),
        behind,
    )
    terms = (
        own[:half],
        beside_first,
        swap(across_first, 2),
        own[half:],
        swap(beside_second, 4),
        across_second,
    )
    return terms, beside_second


def scatter_direct(pieces, near_three, near_one, far_three, far_one, behind=()):
    rows = near_one.shape[0]
    size = sum(piece.size for piece in pieces)
    own, beside, across, diagonal = local_call(
        functools.partial(sum_all_kernel, size),
        (array((rows, LANES), jnp.bfloat16),) * 4,
        (near_three, near_one, far_three, far_one),
        (),
        behind,
    )
    return (own, swap(beside, 4), swap(across, 2), swap(diagonal, 6)), own


def scatter_unpack(pieces, terms, extra_count=0, behind=()):
    high_count = pieces[0].high_count
    size = sum(piece.size for piece in pieces)
    flat_rows = sum(piece.flat_rows for piece in pieces)
    return local_call(
        functools.partial(unpack_kernel, pieces, terms[0].shape[0] - extra_count),
        (array((flat_rows + extra_count, LANES), jnp.float32),)
        + (array((flat_rows + extra_count, LANES), jnp.bfloat16),) * (high_count - 1),
        terms,
        (
            pltpu.VMEM((high_count, flat_rows, LANES), jnp.float32),
            pltpu.VMEM((size, LANES), jnp.float32),
        ),
        behind,
    )


def norm_parts(values):
    scale = lax.rsqrt(jnp.mean(values * values, axis=-1, keepdims=True) + norm_eps)
    return scale, values * scale


def norm_back(scale, normal, upstream, weight_vec):
    weighted = upstream * (1.0 + weight_vec)
    inner = jnp.mean(weighted * normal, axis=-1, keepdims=True)
    return scale * (weighted - normal * inner), jnp.sum(normal * upstream, axis=0, keepdims=True)


def product(left_side, right_side, left_axis, right_axis):
    return lax.dot_general(
        left_side,
        right_side,
        (((left_axis,), (right_axis,)), ((), ())),
        preferred_element_type=jnp.float32,
    )


def unordered(rows_in, order_low):
    upper = rows_in.astype(jnp.bfloat16)
    lower = (rows_in - upper.astype(jnp.float32)).astype(jnp.bfloat16)
    return product(upper, order_low, 1, 1) + product(lower, order_low, 1, 1)


def weight_rows(refs, size, order, start, rows):
    count = len(refs) // LOW_COUNT
    part = size // count
    return refs[order * count + start // part][start % part : start % part + rows, :]


def put_rows(refs, size, order, start, rows):
    three, one = refs[:2] if order < 4 else refs[2:]
    if order % 4 == 3:
        one[start : start + rows.shape[0], :] = rows
    else:
        start = order % 4 * size + start
        three[start : start + rows.shape[0], :] = rows


def wide_tile(refs, size, start, rows):
    return jnp.concatenate(
        [weight_rows(refs, size, order, start, rows) for order in range(LOW_COUNT)]
    )


def put_wide_tile(refs, size, start, rows, tile):
    for order in range(LOW_COUNT):
        put_rows(refs, size, order, start, tile[order * rows : (order + 1) * rows])


def tall_rows(piece, low):
    for order, mask in enumerate(LOW_MASKS):
        for block in range(piece.blocks):
            for place in range(piece.high_count):
                row = (place * LOW_COUNT + (low ^ mask)) * piece.own_rows
                yield (
                    order,
                    block * piece.block_rows + place * piece.own_rows,
                    pl.ds(pl.multiple_of(row, piece.own_rows), piece.own_rows),
                    slice(block * LANES, (block + 1) * LANES),
                )


def ffn_kernel(
    gate_piece,
    down_piece,
    index_ref,
    middle_ref,
    cotangent_ref,
    gain_in_ref,
    gain_out_ref,
    order_ref,
    *refs,
):
    weight_refs, grad_refs = refs[:16], refs[20:24]
    block_out_ref, grad_middle_ref, grad_gain_in_ref, grad_gain_out_ref = refs[16:20]
    down_ref, hidden_ref, gelu_ref, slope_ref = refs[24:]
    low = index_ref[0] % LOW_COUNT
    rows = gate_piece.block_rows
    size = 2 * gate_piece.size + down_piece.size
    width = 2 * LANES
    for order, start, matrix_rows, columns in tall_rows(down_piece, low):
        start = start + 2 * gate_piece.size
        down_ref[matrix_rows, columns] = weight_rows(
            weight_refs, size, order, start, down_piece.own_rows
        )

    def wide_tiles(step):
        return [
            jnp.concatenate(
                [
                    wide_tile(weight_refs, size, offset + block * rows, rows)
                    for block in (2 * step, 2 * step + 1)
                ],
                axis=1,
            )
            for offset in (0, gate_piece.size)
        ]

    middle = middle_ref[...]
    scale_in, normal_in = norm_parts(middle)
    order_low = order_ref[...]
    normed = (normal_in * (1.0 + gain_in_ref[...])).astype(jnp.bfloat16)
    normed = product(normed, order_low, 1, 0).astype(jnp.bfloat16)
    for step in range(FF // width):
        columns = slice(step * width, (step + 1) * width)
        gate_weight, up_weight = wide_tiles(step)
        gate = product(normed, gate_weight, 1, 0)
        up = product(normed, up_weight, 1, 0)
        square = gate * gate
        bend = jnp.tanh(GELU_SCALE * gate * (1.0 + GELU_CUBE * square))
        half = 0.5 * (1.0 + bend)
        gelu = gate * half
        slope = half + 0.5 * gate * (1.0 - bend * bend) * GELU_SCALE * (
            1.0 + 3.0 * GELU_CUBE * square
        )
        gelu_ref[:, columns] = gelu
        slope_ref[:, columns] = slope * up
        hidden_ref[:, columns] = (gelu * up).astype(jnp.bfloat16)
    hidden = hidden_ref[...]
    scale_out, normal_out = norm_parts(product(hidden, down_ref[...], 1, 0))
    block_out_ref[...] = (middle + normal_out * (1.0 + gain_out_ref[...])).astype(jnp.bfloat16)
    upstream = cotangent_ref[...].astype(jnp.float32)
    grad_ffn, grad_gain_out_ref[...] = norm_back(
        scale_out, normal_out, upstream, gain_out_ref[...]
    )
    grad_ffn = grad_ffn.astype(jnp.bfloat16)
    grad_normed = jnp.zeros(middle.shape, jnp.float32)
    for step in range(FF // width):
        columns = slice(step * width, (step + 1) * width)
        grad_hidden = product(grad_ffn, down_ref[columns, :], 1, 1)
        down_ref[columns, :] = product(hidden_ref[:, columns], grad_ffn, 0, 0).astype(jnp.bfloat16)
        grads = [
            (grad_hidden * slope_ref[:, columns]).astype(jnp.bfloat16),
            (grad_hidden * gelu_ref[:, columns]).astype(jnp.bfloat16),
        ]
        for place, (grad, weight) in enumerate(zip(grads, wide_tiles(step))):
            grad_weight = product(normed, grad, 0, 0).astype(jnp.bfloat16)
            for side in range(2):
                put_wide_tile(
                    grad_refs,
                    size,
                    place * gate_piece.size + (2 * step + side) * rows,
                    rows,
                    grad_weight[:, side * LANES : (side + 1) * LANES],
                )
            grad_normed = grad_normed + product(grad, weight, 1, 1)
    for order, start, matrix_rows, columns in tall_rows(down_piece, low):
        start = start + 2 * gate_piece.size
        put_rows(grad_refs, size, order, start, down_ref[matrix_rows, columns])
    grad_middle, grad_gain_in_ref[...] = norm_back(
        scale_in, normal_in, unordered(grad_normed, order_low), gain_in_ref[...]
    )
    grad_middle_ref[...] = upstream + grad_middle


def grad_arrays(pieces, extra_count=0):
    size = sum(piece.size for piece in pieces)
    return (
        array((3 * size, LANES), jnp.bfloat16),
        array((size + extra_count, LANES), jnp.bfloat16),
    ) * 2


def ffn_blocks(pieces, middle, cotangent, gain_in, gain_out, order, blocks):
    rows = middle.shape[0]
    outs = local_call(
        functools.partial(ffn_kernel, pieces[4], pieces[6]),
        (
            array((rows, D), jnp.bfloat16),
            array((rows, D), jnp.float32),
            array((1, D), jnp.float32),
            array((1, D), jnp.float32),
            *grad_arrays(pieces[4:7]),
        ),
        (middle, cotangent, gain_in, gain_out, order, *blocks),
        (
            pltpu.VMEM((FF, D), jnp.bfloat16),
            pltpu.VMEM((rows, FF), jnp.bfloat16),
            pltpu.VMEM((rows, FF), jnp.float32),
            pltpu.VMEM((rows, FF), jnp.float32),
        ),
    )
    return *outs[:4], outs[4:]


def turn(values, cosine, sine):
    first_half, second_half = values[:, : HD // 2], values[:, HD // 2 :]
    return jnp.concatenate(
        [first_half * cosine - second_half * sine, second_half * cosine + first_half * sine], axis=1
    )


def wide_head(refs, size, start, rows):
    return jnp.concatenate(
        [wide_tile(refs, size, start + side * rows, rows) for side in range(2)], axis=1
    )


def head_starts(pieces):
    rows = pieces[0].block_rows
    return [2 * rows * head for head in range(HQ + 2)]


def project_kernel(
    pieces,
    index_ref,
    tokens_ref,
    gain_ref,
    gain_query_ref,
    gain_key_ref,
    cosine_ref,
    sine_ref,
    order_ref,
    *refs,
):
    weight_refs = refs[:8]
    normed_ref, query_proj_ref, key_proj_ref, query_ref, key_value_ref = refs[8:]
    size = sum(piece.size for piece in pieces)
    rows = pieces[0].block_rows
    cosine, sine = cosine_ref[...], sine_ref[...]
    _, normal = norm_parts(tokens_ref[...].astype(jnp.float32))
    normed = (normal * (1.0 + gain_ref[...])).astype(jnp.bfloat16)
    normed = product(normed, order_ref[...], 1, 0).astype(jnp.bfloat16)
    normed_ref[...] = normed
    starts = head_starts(pieces)
    for head, start in enumerate(starts):
        proj = product(normed, wide_head(weight_refs, size, start, rows), 1, 0)
        columns = slice(head * HD, (head + 1) * HD)
        if head == HQ + 1:
            key_value_ref[:, HD:] = proj.astype(jnp.bfloat16)
            continue
        gain_vec = gain_query_ref[...] if head < HQ else gain_key_ref[...]
        _, normal = norm_parts(proj)
        turned = turn(normal * (1.0 + gain_vec), cosine, sine).astype(jnp.bfloat16)
        if head < HQ:
            query_proj_ref[:, columns] = proj
            query_ref[:, columns] = turned
        else:
            key_proj_ref[...] = proj
            key_value_ref[:, :HD] = turned


def attend_kernel(
    pieces,
    index_ref,
    tokens_ref,
    gain_ref,
    allowed_ref,
    query_ref,
    *refs,
):
    weight_refs, key_value_refs = refs[:8], refs[8:-5]
    probs_ref, attended_ref, attn_out_ref, middle_ref, out_weight_ref = refs[-5:]
    out_piece = pieces[-1]
    low = index_ref[0] % LOW_COUNT
    size = sum(piece.size for piece in pieces)
    out_start = size - out_piece.size
    for order, start, matrix_rows, columns in tall_rows(out_piece, low):
        out_weight_ref[matrix_rows, columns] = weight_rows(
            weight_refs, size, order, start + out_start, out_piece.own_rows
        )
    rows = tokens_ref.shape[0]
    allowed = allowed_ref[...] > 0.0
    keys = jnp.concatenate([ref[:, :HD] for ref in key_value_refs])
    values = jnp.concatenate([ref[:, HD:] for ref in key_value_refs])
    count = keys.shape[0]
    for head in range(HQ):
        columns = slice(head * HD, (head + 1) * HD)
        scores = product(query_ref[:, columns], keys, 1, 1) * HD ** (-0.5)
        scores = jnp.where(allowed, scores, -1e30)
        raised = jnp.exp(scores - jnp.max(scores, axis=-1, keepdims=True))
        probs = raised / jnp.sum(raised, axis=-1, keepdims=True)
        probs_ref[:, head * count : (head + 1) * count] = probs
        attended_ref[:, columns] = product(probs.astype(jnp.bfloat16), values, 1, 0).astype(
            jnp.bfloat16
        )
    attn_out = product(attended_ref[...], out_weight_ref[...], 1, 0)
    attn_out_ref[...] = attn_out
    _, normal = norm_parts(attn_out)
    middle_ref[...] = tokens_ref[...].astype(jnp.float32) + normal * (1.0 + gain_ref[...])


def attend_back_kernel(
    index_ref,
    grad_middle_ref,
    attn_out_ref,
    gain_ref,
    out_weight_ref,
    attended_ref,
    probs_ref,
    query_ref,
    *refs,
):
    key_value_refs = refs[:4]
    grad_out_weight_ref, grad_query_ref, grad_gain_ref = refs[4:7]
    grad_own_ref, grad_across_ref, grad_cores_ref = refs[7:]
    rows = query_ref.shape[0]
    scale, normal = norm_parts(attn_out_ref[...])
    grad_attn, grad_gain_ref[...] = norm_back(scale, normal, grad_middle_ref[...], gain_ref[...])
    grad_attn = grad_attn.astype(jnp.bfloat16)
    grad_out_weight_ref[...] = product(attended_ref[...], grad_attn, 0, 0).astype(jnp.bfloat16)
    keys = jnp.concatenate([ref[:, :HD] for ref in key_value_refs])
    values = jnp.concatenate([ref[:, HD:] for ref in key_value_refs])
    count = keys.shape[0]
    grad_keys = jnp.zeros((count, HD), jnp.float32)
    grad_values = jnp.zeros((count, HD), jnp.float32)
    for head in range(HQ):
        columns = slice(head * HD, (head + 1) * HD)
        grad_attended = product(grad_attn, out_weight_ref[columns, :], 1, 1).astype(jnp.bfloat16)
        probs = probs_ref[:, head * count : (head + 1) * count]
        grad_probs = product(grad_attended, values, 1, 1)
        grad_values = grad_values + product(probs.astype(jnp.bfloat16), grad_attended, 0, 0)
        inner = jnp.sum(probs * grad_probs, axis=-1, keepdims=True)
        grad_scores = (probs * (grad_probs - inner) * HD ** (-0.5)).astype(jnp.bfloat16)
        grad_query_ref[:, columns] = product(grad_scores, keys, 1, 0)
        grad_keys = grad_keys + product(grad_scores, query_ref[:, columns], 0, 0)
    targets = (
        grad_own_ref,
        grad_cores_ref.at[:rows],
        grad_across_ref,
        grad_cores_ref.at[rows:],
    )
    for part, ref in enumerate(targets):
        ref[:, :HD] = grad_keys[part * rows : (part + 1) * rows].astype(ref.dtype)
        ref[:, HD:] = grad_values[part * rows : (part + 1) * rows].astype(ref.dtype)


def query_back_kernel(
    pieces,
    index_ref,
    gain_ref,
    cosine_ref,
    sine_ref,
    normed_ref,
    query_proj_ref,
    grad_query_ref,
    *refs,
):
    weight_refs = refs[:8]
    grad_weight_ref, grad_normed_ref, grad_gain_ref = refs[8:]
    size = sum(piece.size for piece in pieces)
    rows = pieces[0].block_rows
    cosine, sine = cosine_ref[...], sine_ref[...]
    normed = normed_ref[...]
    grad_normed = jnp.zeros(grad_normed_ref.shape, jnp.float32)
    grad_gain = jnp.zeros((1, HD), jnp.float32)
    for head, start in enumerate(head_starts(pieces)[:HQ]):
        columns = slice(head * HD, (head + 1) * HD)
        scale, normal = norm_parts(query_proj_ref[:, columns])
        upstream = turn(grad_query_ref[:, columns], cosine, -sine)
        grad, gain_row = norm_back(scale, normal, upstream, gain_ref[...])
        grad_gain = grad_gain + gain_row
        grad = grad.astype(jnp.bfloat16)
        weight = wide_head(weight_refs, size, start, rows)
        grad_normed = grad_normed + product(grad, weight, 1, 1)
        grad_weight_ref[:, columns] = product(normed, grad, 0, 0).astype(jnp.bfloat16)
    grad_normed_ref[...] = grad_normed
    grad_gain_ref[...] = grad_gain


def project_back_kernel(
    pieces,
    index_ref,
    tokens_ref,
    gain_ref,
    gain_key_ref,
    cosine_ref,
    sine_ref,
    order_ref,
    normed_ref,
    key_proj_ref,
    grad_normed_ref,
    grad_middle_ref,
    gain_attn_ref,
    gain_ffin_ref,
    gain_ffout_ref,
    gain_query_ref,
    own_key_ref,
    cores_key_ref,
    across_key_ref,
    *refs,
):
    weight_refs = refs[:8]
    grad_weight_ref, input_grad_ref, grad_gain_ref = refs[8:]
    size = sum(piece.size for piece in pieces)
    rows = pieces[0].block_rows
    normed = normed_ref[...]
    key_rows = own_key_ref.shape[0]
    first = across_key_ref.shape[0] - 4 * key_rows
    key_value = own_key_ref[...] + cores_key_ref[:key_rows, :].astype(jnp.float32)
    key_value = key_value + jnp.concatenate(
        [
            across_key_ref[first + block * key_rows : first + (block + 1) * key_rows, :].astype(
                jnp.float32
            )
            for block in range(4)
        ],
        axis=1,
    )
    scale, normal = norm_parts(key_proj_ref[...])
    upstream = turn(key_value[:, :HD], cosine_ref[...], -sine_ref[...])
    grad_key, grad_gain_key = norm_back(scale, normal, upstream, gain_key_ref[...])
    grad_normed = grad_normed_ref[...]
    for place, start in enumerate(head_starts(pieces)[HQ:]):
        grad = (key_value[:, HD:] if place else grad_key).astype(jnp.bfloat16)
        weight = wide_head(weight_refs, size, start, rows)
        grad_normed = grad_normed + product(grad, weight, 1, 1)
        grad_weight_ref[:, place * HD : (place + 1) * HD] = product(normed, grad, 0, 0).astype(
            jnp.bfloat16
        )
    scale, normal = norm_parts(tokens_ref[...].astype(jnp.float32))
    grad_inputs, grad_gain_input = norm_back(
        scale, normal, unordered(grad_normed, order_ref[...]), gain_ref[...]
    )
    input_grad_ref[...] = (grad_middle_ref[...] + grad_inputs).astype(jnp.bfloat16)
    grad_gains = [
        grad_gain_input,
        gain_attn_ref[...],
        gain_ffin_ref[...],
        gain_ffout_ref[...],
        gain_query_ref[...],
        grad_gain_key,
    ]
    row = 0
    grad_gain_ref[...] = jnp.zeros(grad_gain_ref.shape, jnp.float32)
    for values in grad_gains:
        for start in range(0, values.shape[1], LANES):
            grad_gain_ref[row : row + 1, :] = values[:, start : start + LANES]
            row = row + 1


def split_kernel(
    pieces,
    index_ref,
    query_ref,
    key_value_ref,
    out_ref,
    gain_ref,
    *grad_refs,
):
    low = index_ref[0] % LOW_COUNT
    size = sum(piece.size for piece in pieces)
    rows = pieces[0].block_rows
    start = 0
    for matrix_ref in (query_ref, key_value_ref):
        for column in range(0, matrix_ref.shape[1], LANES):
            tile = matrix_ref[:, column : column + LANES]
            put_wide_tile(grad_refs, size, start, rows, tile)
            start = start + rows
    out_piece = pieces[-1]
    for order, first, matrix_rows, columns in tall_rows(out_piece, low):
        put_rows(grad_refs, size, order, start + first, out_ref[matrix_rows, columns])
    for target in (grad_refs[1], grad_refs[3]):
        target[size:, :] = gain_ref[...].astype(jnp.bfloat16)


def width_order(device_count):
    low = lax.axis_index(ALL_AXES) % LOW_COUNT
    rows = D // device_count
    high_count = device_count // LOW_COUNT
    column = jnp.arange(D, dtype=jnp.int32)
    place = column // (rows * high_count)
    mask = (place & 1) * 4 + ((place >> 1) & 1) * 2 + (place >> 2)
    high = (column // rows) % high_count
    picked = (high * LOW_COUNT + (low ^ mask)) * rows + column % rows
    return (jnp.arange(D, dtype=jnp.int32)[:, None] == picked[None, :]).astype(jnp.bfloat16)


GAIN_ROWS = 32


def shards_blocks(
    device_count,
    tokens,
    doc_ids,
    cotangent,
    master,
    first_moment,
    second_moment,
    gains,
    gain_first,
    gain_second,
):
    pieces = [Piece(*shape_pair, device_count) for shape_pair in piece_shapes()]
    attention_pieces = pieces[:4]
    local_rows = tokens.shape[0]
    group_size = lax.axis_size("group")
    first_row = lax.axis_index("group") * local_rows
    attention_rows = sum(piece.flat_rows for piece in attention_pieces)
    ffn_pieces = pieces[4:7]
    rounded = master.astype(jnp.bfloat16)
    attention_parts = gather_high(rounded[:attention_rows])
    ffn_rows = rounded[attention_rows:]
    ffn_parts = gather_high(ffn_rows)
    attention_near = gather_wholes(
        *gather_own(attention_pieces, attention_parts, 1, (ffn_parts[1],))
    )
    attention_near = tuple(held(attention_near, ffn_parts[2:]))
    attention_blocks = gather_cores(attention_near)
    ffn_own = gather_own(ffn_pieces, ffn_parts, 2, attention_near[1:])
    ffn_passed = gather_halves(*ffn_own)
    gain_parts = []
    for start, width in ((0, D), (D, D), (2 * D, D), (3 * D, D), (4 * D, HD), (4 * D + HD, HD)):
        gain_parts.append(gains[start : start + width][None])
    gain_input, gain_attn, gain_ffin, gain_ffout, gain_query, gain_key = gain_parts
    order = width_order(device_count)
    doc_row = doc_ids[0]
    angles = lax.dynamic_slice_in_dim(angles_of(positions(doc_row)), first_row, local_rows, 0)
    cosine, sine = jnp.cos(angles), jnp.sin(angles)
    query_docs = lax.dynamic_slice_in_dim(doc_row, first_row, local_rows, 0)
    key_count = group_size * local_rows
    first_keys = [(lax.axis_index("group") ^ step) * local_rows for step in range(group_size)]
    key_docs = jnp.concatenate(
        [lax.dynamic_slice_in_dim(doc_row, start, local_rows, 0) for start in first_keys]
    )
    key_index = jnp.concatenate(
        [start + jnp.arange(local_rows, dtype=jnp.int32) for start in first_keys]
    )
    query_index = first_row + jnp.arange(local_rows, dtype=jnp.int32)
    distance = query_index[:, None] - key_index[None, :]
    allowed = (distance >= 0) & (distance < WINDOW) & (key_docs[None, :] == query_docs[:, None])
    allowed = allowed.astype(jnp.float32)

    width = HQ * HD
    normed, query_proj, key_proj, query_rot, key_value = local_call(
        functools.partial(project_kernel, attention_pieces),
        (
            array((local_rows, D), jnp.bfloat16),
            array((local_rows, width), jnp.float32),
            array((local_rows, HD), jnp.float32),
            array((local_rows, width), jnp.bfloat16),
            array((local_rows, 2 * HD), jnp.bfloat16),
        ),
        (tokens, gain_input, gain_query, gain_key, cosine, sine, order, *attention_blocks),
    )
    key_values = [key_value] + [swap(key_value, step) for step in range(1, group_size)]
    probs, attended, attn_out, middle, out_weight = local_call(
        functools.partial(attend_kernel, attention_pieces),
        (
            array((local_rows, HQ * key_count), jnp.float32),
            array((local_rows, width), jnp.bfloat16),
            array((local_rows, D), jnp.float32),
            array((local_rows, D), jnp.float32),
            array((width, D), jnp.bfloat16),
        ),
        (tokens, gain_attn, allowed, query_rot, *attention_blocks, *key_values),
    )
    ffn_weights = gather_cores(gather_rest(*ffn_own, *ffn_passed, key_values, (middle,)))
    outputs, grad_middle, grad_gain_ffin, grad_gain_ffout, grads_ffn = ffn_blocks(
        pieces, middle, cotangent, gain_ffin, gain_ffout, order, ffn_weights
    )
    near_three, near_one, far_three, far_one = grads_ffn
    far_three, far_one = scatter_cores(far_three, far_one)
    grad_out_weight, grad_query, grad_gain_attn, own_key, across_key, cores_key = local_call(
        attend_back_kernel,
        (
            array((width, D), jnp.bfloat16),
            array((local_rows, width), jnp.float32),
            array((1, D), jnp.float32),
            array((local_rows, 2 * HD), jnp.float32),
            array((local_rows, 2 * HD), jnp.float32),
            array((2 * local_rows, 2 * HD), jnp.bfloat16),
        ),
        (
            grad_middle,
            attn_out,
            gain_attn,
            out_weight,
            attended,
            probs,
            query_rot,
            *key_values,
        ),
    )
    cores_key = swap(cores_key, 1)
    over_x, over_y, sent = scatter_one(ffn_pieces, near_one, far_one, (across_key, cores_key))
    threes = scatter_three(ffn_pieces, near_three, far_three, (swap(sent[:16], 1),))
    grad_query_weight, grad_normed, grad_gain_query = local_call(
        functools.partial(query_back_kernel, attention_pieces),
        (
            array((D, width), jnp.bfloat16),
            array((local_rows, D), jnp.float32),
            array((1, HD), jnp.float32),
        ),
        (gain_query, cosine, sine, normed, query_proj, grad_query, *attention_blocks),
        (),
        (threes[0],),
    )
    ffn_terms, sent = scatter_passed(threes, over_x, over_y, (grad_normed,))
    grad_key_weight, grad_inputs, grad_gains = local_call(
        functools.partial(project_back_kernel, attention_pieces),
        (
            array((D, 2 * HD), jnp.bfloat16),
            array((local_rows, D), jnp.bfloat16),
            array((GAIN_ROWS, LANES), jnp.float32),
        ),
        (
            tokens,
            gain_input,
            gain_key,
            cosine,
            sine,
            order,
            normed,
            key_proj,
            grad_normed,
            grad_middle,
            grad_gain_attn,
            grad_gain_ffin,
            grad_gain_ffout,
            grad_gain_query,
            own_key,
            cores_key,
            over_y,
            *attention_blocks,
        ),
        (),
        (sent, threes[1], threes[4]),
    )
    near_three, near_one, far_three, far_one = local_call(
        functools.partial(split_kernel, attention_pieces),
        grad_arrays(attention_pieces, GAIN_ROWS),
        (grad_query_weight, grad_key_weight, grad_out_weight, grad_gains),
    )
    far_three, far_one = held((far_three, far_one), (ffn_terms[2], ffn_terms[4]))
    own_ffn, first_plane, *planes = scatter_unpack(ffn_pieces, ffn_terms, 0, (near_one,))
    far_three, far_one = scatter_cores(far_three, far_one)
    terms, sent = scatter_direct(
        attention_pieces, near_three, near_one, far_three, far_one, (first_plane,)
    )
    planes = [first_plane, *held(planes, (sent,))]
    arrived = [swap(plane, step * LOW_COUNT) for step, plane in enumerate(planes, start=1)]
    grads_ffn = own_ffn + sum(value.astype(jnp.float32) for value in arrived)
    own_attention, *planes = scatter_unpack(attention_pieces, terms, GAIN_ROWS, arrived)
    grads_attention = own_attention + sum(
        swap(plane, step * LOW_COUNT).astype(jnp.float32)
        for step, plane in enumerate(planes, start=1)
    )
    gain_grads = grads_attention[attention_rows:].reshape(-1)[: gains.shape[0]]
    grads_local = jnp.concatenate([grads_attention[:attention_rows], grads_ffn])
    return (
        outputs,
        grad_inputs,
        *adam_update(grads_local, first_moment, second_moment, master, learn_rate, weight_decay),
        *adam_update(gain_grads, gain_first, gain_second, gains, gain_rate, 0.0),
    )


def shards(
    tokens, doc_ids, cotangent, master, first_moment, second_moment, gains, gain_first, gain_second
):
    group_size = lax.axis_size("group")
    devices_all = lax.axis_size("dp") * group_size
    if aligned(devices_all):
        return shards_blocks(
            devices_all,
            tokens,
            doc_ids,
            cotangent,
            master,
            first_moment,
            second_moment,
            gains,
            gain_first,
            gain_second,
        )
    group_index = lax.axis_index("group")
    local_rows = tokens.shape[0]
    shard_parts = [
        part_rows.astype(jnp.bfloat16) for part_rows in split_rows(master, piece_rows(devices_all))
    ]
    gathered = (
        lax.all_gather(shard_parts[0], ("dp", "group"), axis=0, tiled=True),
        lax.all_gather(shard_parts[1], ("dp", "group"), axis=0, tiled=True),
        lax.all_gather(shard_parts[2], ("dp", "group"), axis=0, tiled=True),
        lax.all_gather(shard_parts[3], ("dp", "group"), axis=0, tiled=True),
        lax.all_gather(shard_parts[4], ("dp", "group"), axis=0, tiled=True),
        lax.all_gather(shard_parts[5], ("dp", "group"), axis=0, tiled=True),
        lax.all_gather(shard_parts[6], ("dp", "group"), axis=0, tiled=True),
    )
    query_weight, key_weight, value_weight, out_weight, gate_weight, up_weight, down_weight = [
        full_rows.reshape(shape_pair) for full_rows, shape_pair in zip(gathered, piece_shapes())
    ]
    norm_input = gains[0:D]
    norm_attn = gains[D : 2 * D]
    norm_ffin = gains[2 * D : 3 * D]
    norm_ffout = gains[3 * D : 4 * D]
    norm_query = gains[4 * D : 4 * D + HD]
    norm_key = gains[4 * D + HD : 4 * D + 2 * HD]
    doc_row = doc_ids[0]
    first_row = group_index * local_rows
    angles = lax.dynamic_slice_in_dim(angles_of(positions(doc_row)), first_row, local_rows, 0)
    query_docs = lax.dynamic_slice_in_dim(doc_row, first_row, local_rows, 0)
    inputs = tokens.astype(jnp.float32)
    normed, back_input = jax.vjp(rms_norm, inputs, norm_input)
    normed_low = normed.astype(jnp.bfloat16)
    query_proj = matmul(normed_low, query_weight)
    key_proj = matmul(normed_low, key_weight)
    value_proj = matmul(normed_low, value_weight)

    def query_prep(flat_rows, gain_vec):
        return rotate(rms_norm(flat_rows.reshape(local_rows, HQ, HD), gain_vec), angles[:, None, :])

    def key_prep(rows_in, gain_vec):
        return rotate(rms_norm(rows_in, gain_vec), angles)

    query_rot, back_query = jax.vjp(query_prep, query_proj, norm_query)
    key_rot, back_key = jax.vjp(key_prep, key_proj, norm_key)
    query_low = query_rot.astype(jnp.bfloat16)
    key_low = key_rot.astype(jnp.bfloat16)
    value_low = value_proj.astype(jnp.bfloat16)
    reach = min(-(-(WINDOW - 1) // local_rows), group_size - 1)
    key_list = [key_low]
    value_list = [value_low]
    for offset in range(1, reach + 1):
        key_far, value_far = shifted((key_low, value_low), "group", offset)
        key_list.insert(0, key_far)
        value_list.insert(0, value_far)
    key_all = jnp.concatenate(key_list, axis=0)
    value_all = jnp.concatenate(value_list, axis=0)
    key_count = (reach + 1) * local_rows
    doc_pad = jnp.concatenate([jnp.full((reach * local_rows,), -1, jnp.int32), doc_row])
    key_docs = lax.dynamic_slice_in_dim(doc_pad, first_row, key_count, 0)
    key_index = (group_index - reach) * local_rows + jnp.arange(key_count, dtype=jnp.int32)
    query_index = first_row + jnp.arange(local_rows, dtype=jnp.int32)
    distance = query_index[:, None] - key_index[None, :]
    allowed = (distance >= 0) & (distance < WINDOW) & (key_docs[None, :] == query_docs[:, None])

    def scores_of(key_rows_low):
        raw_scores = jnp.einsum(
            "qhd,kd->hqk", query_low, key_rows_low, preferred_element_type=jnp.float32
        ) * HD ** (-0.5)
        return jnp.where(allowed[None], raw_scores, -1e30)

    masked = scores_of(key_all)
    top_score = jnp.max(masked, axis=-1, keepdims=True)
    log_total = top_score + jnp.log(jnp.sum(jnp.exp(masked - top_score), axis=-1, keepdims=True))
    probs = jnp.exp(masked - log_total)
    attended = jnp.einsum(
        "hqk,kd->qhd", probs.astype(jnp.bfloat16), value_all, preferred_element_type=jnp.float32
    )
    attended_low = attended.reshape(local_rows, HQ * HD).astype(jnp.bfloat16)
    attn_out = matmul(attended_low, out_weight)
    branch_one, back_attn = jax.vjp(rms_norm, attn_out, norm_attn)
    middle = inputs + branch_one
    normed_two, back_ffin = jax.vjp(rms_norm, middle, norm_ffin)
    normed_two_low = normed_two.astype(jnp.bfloat16)
    gate_proj = matmul(normed_two_low, gate_weight)
    up_proj = matmul(normed_two_low, up_weight)
    hidden, back_hidden = jax.vjp(geglu, gate_proj, up_proj)
    hidden_low = hidden.astype(jnp.bfloat16)
    ffn_out = matmul(hidden_low, down_weight)
    branch_two, back_ffout = jax.vjp(rms_norm, ffn_out, norm_ffout)
    outputs = middle + branch_two
    grad_out = cotangent.astype(jnp.float32)
    grad_ffn, grad_gain_ffout = back_ffout(grad_out)
    grad_ffn_low = grad_ffn.astype(jnp.bfloat16)
    grad_down_w = jnp.einsum(
        "tf,td->fd", hidden_low, grad_ffn_low, preferred_element_type=jnp.float32
    )
    grad_hidden = jnp.einsum(
        "td,fd->tf", grad_ffn_low, down_weight, preferred_element_type=jnp.float32
    )
    grad_gate, grad_up = back_hidden(grad_hidden)
    grad_gate_low = grad_gate.astype(jnp.bfloat16)
    grad_up_low = grad_up.astype(jnp.bfloat16)
    grad_gate_w = jnp.einsum(
        "td,tf->df", normed_two_low, grad_gate_low, preferred_element_type=jnp.float32
    )
    grad_up_w = jnp.einsum(
        "td,tf->df", normed_two_low, grad_up_low, preferred_element_type=jnp.float32
    )
    grad_normed_two = jnp.einsum(
        "tf,df->td", grad_gate_low, gate_weight, preferred_element_type=jnp.float32
    ) + jnp.einsum("tf,df->td", grad_up_low, up_weight, preferred_element_type=jnp.float32)
    grad_middle_norm, grad_gain_ffin = back_ffin(grad_normed_two)
    grad_middle = grad_out + grad_middle_norm
    grad_attn, grad_gain_attn = back_attn(grad_middle)
    grad_attn_low = grad_attn.astype(jnp.bfloat16)
    grad_out_w = jnp.einsum(
        "to,td->od", attended_low, grad_attn_low, preferred_element_type=jnp.float32
    )
    grad_attended = jnp.einsum(
        "td,od->to", grad_attn_low, out_weight, preferred_element_type=jnp.float32
    )
    grad_attended_low = grad_attended.astype(jnp.bfloat16).reshape(local_rows, HQ, HD)
    probs_again = jnp.exp(scores_of(key_all) - log_total)
    grad_probs = jnp.einsum(
        "qhd,kd->hqk", grad_attended_low, value_all, preferred_element_type=jnp.float32
    )
    grad_value_all = jnp.einsum(
        "hqk,qhd->kd",
        probs_again.astype(jnp.bfloat16),
        grad_attended_low,
        preferred_element_type=jnp.float32,
    )
    grad_scores = probs_again * (
        grad_probs - jnp.sum(probs_again * grad_probs, axis=-1, keepdims=True)
    )
    grad_scores_low = (grad_scores * HD ** (-0.5)).astype(jnp.bfloat16)
    grad_query = jnp.einsum(
        "hqk,kd->qhd", grad_scores_low, key_all, preferred_element_type=jnp.float32
    )
    grad_key_all = jnp.einsum(
        "hqk,qhd->kd", grad_scores_low, query_low, preferred_element_type=jnp.float32
    )
    key_total = grad_key_all[reach * local_rows :]
    value_total = grad_value_all[reach * local_rows :]
    for offset in range(1, reach + 1):
        row_start = (reach - offset) * local_rows
        key_back, value_back = (
            shifted(
                grad_key_all[row_start : row_start + local_rows].astype(jnp.bfloat16),
                "group",
                -offset,
            ).astype(jnp.float32),
            shifted(
                grad_value_all[row_start : row_start + local_rows].astype(jnp.bfloat16),
                "group",
                -offset,
            ).astype(jnp.float32),
        )
        key_total = key_total + key_back
        value_total = value_total + value_back
    grad_query_proj, grad_gain_query = back_query(grad_query)
    grad_key_proj, grad_gain_key = back_key(key_total)
    grad_query_low = grad_query_proj.astype(jnp.bfloat16)
    grad_key_low = grad_key_proj.astype(jnp.bfloat16)
    grad_value_low = value_total.astype(jnp.bfloat16)
    grad_query_w = jnp.einsum(
        "td,te->de", normed_low, grad_query_low, preferred_element_type=jnp.float32
    )
    grad_key_w = jnp.einsum(
        "td,te->de", normed_low, grad_key_low, preferred_element_type=jnp.float32
    )
    grad_value_w = jnp.einsum(
        "td,te->de", normed_low, grad_value_low, preferred_element_type=jnp.float32
    )
    grad_normed = jnp.einsum(
        "te,de->td", grad_query_low, query_weight, preferred_element_type=jnp.float32
    )
    grad_normed = grad_normed + jnp.einsum(
        "te,de->td", grad_key_low, key_weight, preferred_element_type=jnp.float32
    )
    grad_normed = grad_normed + jnp.einsum(
        "te,de->td", grad_value_low, value_weight, preferred_element_type=jnp.float32
    )
    grad_input_norm, grad_gain_input = back_input(grad_normed)
    grad_inputs = grad_middle + grad_input_norm
    flat_query = grad_query_w.reshape(-1, 128)
    flat_key = grad_key_w.reshape(-1, 128)
    flat_value = grad_value_w.reshape(-1, 128)
    flat_out = grad_out_w.reshape(-1, 128)
    flat_gate = grad_gate_w.reshape(-1, 128)
    flat_up = grad_up_w.reshape(-1, 128)
    flat_down = grad_down_w.reshape(-1, 128)
    reduced = (
        lax.psum_scatter(flat_query, ("dp", "group"), scatter_dimension=0, tiled=True),
        lax.psum_scatter(flat_key, ("dp", "group"), scatter_dimension=0, tiled=True),
        lax.psum_scatter(flat_value, ("dp", "group"), scatter_dimension=0, tiled=True),
        lax.psum_scatter(flat_out, ("dp", "group"), scatter_dimension=0, tiled=True),
        lax.psum_scatter(flat_gate, ("dp", "group"), scatter_dimension=0, tiled=True),
        lax.psum_scatter(flat_up, ("dp", "group"), scatter_dimension=0, tiled=True),
        lax.psum_scatter(flat_down, ("dp", "group"), scatter_dimension=0, tiled=True),
    )
    grads_local = jnp.concatenate(list(reduced), axis=0)
    gain_grads = lax.psum(
        jnp.concatenate(
            [
                grad_gain_input,
                grad_gain_attn,
                grad_gain_ffin,
                grad_gain_ffout,
                grad_gain_query,
                grad_gain_key,
            ]
        ),
        ("dp", "group"),
    )
    moment_first, moment_second, master_new = adam_update(
        grads_local, first_moment, second_moment, master, learn_rate, weight_decay
    )
    gain_moment_first, gain_moment_second, gains_new = adam_update(
        gain_grads, gain_first, gain_second, gains, gain_rate, 0.0
    )
    return (
        outputs.astype(jnp.bfloat16),
        grad_inputs.astype(jnp.bfloat16),
        moment_first,
        moment_second,
        master_new,
        gain_moment_first,
        gain_moment_second,
        gains_new,
    )


def solution(mesh):
    placed = (
        P(("dp", "group"), None),
        P("dp", None),
        P(("dp", "group"), None),
        P(("dp", "group"), None),
        P(("dp", "group"), None),
        P(("dp", "group"), None),
        P(),
        P(),
        P(),
    )
    return jax.shard_map(
        shards,
        mesh=mesh,
        in_specs=placed,
        out_specs=(
            P(("dp", "group"), None),
            P(("dp", "group"), None),
            P(("dp", "group"), None),
            P(("dp", "group"), None),
            P(("dp", "group"), None),
            P(),
            P(),
            P(),
        ),
        check_vma=False,
    )
```

```python
import functools
import math

import jax
import jax.numpy as jnp
from jax import lax
from jax.experimental import pallas as pl
from jax.experimental.pallas import tpu as pltpu
from jax.sharding import PartitionSpec as P

D = 640
HQ = 4
HD = 256
FF = 2048
WINDOW = 512
STEP = 10
ALL_AXES = ("dp", "group")


norm_eps = 1e-06
rope_base = 10000.0
beta_first = 0.9
beta_second = 0.999
learn_rate = 0.05
gain_rate = 0.25
adam_floor = 1e-08
weight_decay = 0.1


def shifted(value, axis, steps):
    count = lax.axis_size(axis)
    initial, last = (max(0, -steps), min(count, count - steps))
    return lax.ppermute(value, axis, [(source, source + steps) for source in range(initial, last)])


def rms_norm(values, weight_vec):
    return (
        values
        * lax.rsqrt(jnp.mean(values * values, axis=-1, keepdims=True) + norm_eps)
        * (1.0 + weight_vec)
    )


def positions(doc_row):
    length = doc_row.shape[0]
    counter = jnp.arange(length, dtype=jnp.int32)
    starts_here = jnp.concatenate([jnp.ones((1,), jnp.bool_), doc_row[1:] != doc_row[:-1]])
    begins = lax.cummax(jnp.where(starts_here, counter, jnp.zeros_like(counter)), axis=0)
    return counter - begins


def angles_of(places):
    half_dim = HD // 2
    frequency = rope_base ** (-(jnp.arange(half_dim, dtype=jnp.float32) * 2.0 / HD))
    return places.astype(jnp.float32)[:, None] * frequency[None, :]


def rotate(values, angles):
    half_dim = values.shape[-1] // 2
    first_half = values[..., :half_dim]
    second_half = values[..., half_dim:]
    cosine = jnp.cos(angles)
    sine_part = jnp.sin(angles)
    return jnp.concatenate(
        [
            first_half * cosine - second_half * sine_part,
            second_half * cosine + first_half * sine_part,
        ],
        axis=-1,
    )


def geglu(gate_in, up_in):
    return jax.nn.gelu(gate_in, approximate=True) * up_in


def adam_update(gradient, first_old, second_old, params_old, rate, decay_rate):
    first_new = beta_first * first_old + (1.0 - beta_first) * gradient
    second_new = beta_second * second_old + (1.0 - beta_second) * gradient * gradient
    first_hat = first_new / (1.0 - beta_first**STEP)
    second_hat = second_new / (1.0 - beta_second**STEP)
    params_new = params_old - rate * (
        first_hat / (jnp.sqrt(second_hat) + adam_floor) + decay_rate * params_old
    )
    return (first_new, second_new, params_new)


def piece_rows(device_count):
    return [
        entries // (128 * device_count)
        for entries in (D * HQ * HD, D * HD, D * HD, HQ * HD * D, D * FF, D * FF, FF * D)
    ]


def piece_shapes():
    return [(D, HQ * HD), (D, HD), (D, HD), (HQ * HD, D), (D, FF), (D, FF), (FF, D)]


def split_rows(stacked, row_list):
    result = []
    row_start = 0
    for row_count in row_list:
        result.append(stacked[row_start : row_start + row_count])
        row_start = row_start + row_count
    return result


def matmul(left_side, right_side):
    return jnp.dot(left_side, right_side, preferred_element_type=jnp.float32)


LOW_COUNT = 8
LANES = 128
LOW_MASKS = (0, 4, 2, 6, 1, 5, 3, 7)
GELU_SCALE = (2.0 / math.pi) ** 0.5
GELU_CUBE = 0.044715
VMEM_BYTES = 56 * 1024 * 1024


def aligned(device_count):
    groups = lax.axis_size("group") == 4
    return groups and device_count % LOW_COUNT == 0 and D % device_count == 0


def swap(value, mask):
    count = lax.axis_size(ALL_AXES)
    return lax.ppermute(value, ALL_AXES, [(source, source ^ mask) for source in range(count)])


def local_call(kernel, outs, operands, scratch=(), behind=()):
    specs = [pl.BlockSpec(memory_space=pltpu.SMEM)]
    specs = specs + [pl.BlockSpec(memory_space=pltpu.VMEM)] * len(operands)
    specs = specs + [pl.BlockSpec(memory_space=pl.ANY)] * len(behind)
    first, last = 1 + len(operands), 1 + len(operands) + len(behind)

    def body(*refs):
        kernel(*refs[:first], *refs[last:])

    return pl.pallas_call(
        body,
        out_shape=outs,
        in_specs=specs,
        out_specs=tuple(pl.BlockSpec(memory_space=pltpu.VMEM) for _ in outs),
        scratch_shapes=scratch,
        compiler_params=pltpu.CompilerParams(vmem_limit_bytes=VMEM_BYTES),
        cost_estimate=pl.CostEstimate(flops=0, bytes_accessed=0, transcendentals=0),
    )(lax.axis_index(ALL_AXES).astype(jnp.int32).reshape(1), *operands, *behind)


class Piece:
    def __init__(self, rows, columns, device_count):
        self.rows = rows
        self.columns = columns
        self.wide = rows == D
        self.blocks = columns // LANES
        self.own_rows = rows // device_count
        self.flat_rows = self.own_rows * self.blocks
        self.high_count = device_count // LOW_COUNT
        self.block_rows = self.own_rows * self.high_count
        self.size = self.block_rows * self.blocks


def copy_kernel(index_ref, in_ref, out_ref):
    out_ref[...] = in_ref[...]


def pack_kernel(pieces, index_ref, *refs):
    high_count = pieces[0].high_count
    parts, out_refs, flat, packed = refs[:high_count], refs[high_count:-2], refs[-2], refs[-1]
    high = index_ref[0] // LOW_COUNT
    for step, part in enumerate(parts):
        flat[high ^ step] = part[...].astype(jnp.float32)
    start, target = 0, 0
    for piece in pieces:
        for block in range(piece.blocks):
            for place in range(high_count):
                packed[pl.ds(target, piece.own_rows), :] = flat[
                    place, pl.ds(start + block, piece.own_rows, stride=piece.blocks), :
                ]
                target = target + piece.own_rows
        start = start + piece.flat_rows
    count = target // len(out_refs)
    for place, out_ref in enumerate(out_refs):
        out_ref[...] = packed[place * count : (place + 1) * count, :].astype(jnp.bfloat16)


def sum_one_kernel(index_ref, near_ref, far_ref, to_x_ref, to_y_ref):
    total = near_ref[...].astype(jnp.float32) + far_ref[...].astype(jnp.float32)
    half = to_x_ref.shape[0]
    to_x_ref[...] = total[:half].astype(jnp.bfloat16)
    to_y_ref[...] = total[half:].astype(jnp.bfloat16)


def sum_halves_kernel(starts, index_ref, near_ref, far_ref, *refs):
    key_refs, out_refs = refs[: -len(starts)], refs[-len(starts) :]
    half = near_ref.shape[0] // 6
    for first, out_ref in zip(starts, out_refs):
        rows = slice(first, first + half)
        total = near_ref[rows, :].astype(jnp.float32) + far_ref[rows, :].astype(jnp.float32)
        out_ref[:half, :] = total.astype(jnp.bfloat16)
    if key_refs:
        across_key_ref, cores_key_ref = key_refs
        rows = across_key_ref.shape[0]
        keys = across_key_ref[...] + cores_key_ref[rows:, :].astype(jnp.float32)
        for block in range(keys.shape[1] // LANES):
            first = half + block * rows
            columns = slice(block * LANES, (block + 1) * LANES)
            out_refs[-1][first : first + rows, :] = keys[:, columns].astype(jnp.bfloat16)


def sum_all_kernel(size, index_ref, near_three, near_one, far_three, far_one, *out_refs):
    extra = near_one[size:, :].astype(jnp.float32) + far_one[size:, :].astype(jnp.float32)
    for place, out_ref in enumerate(out_refs):
        near, far, first = near_three, far_three, place * size
        if place == 3:
            near, far, first = near_one, far_one, 0
        rows = slice(first, first + size)
        total = near[rows, :].astype(jnp.float32) + far[rows, :].astype(jnp.float32)
        out_ref[:size, :] = total.astype(jnp.bfloat16)
        out_ref[size:, :] = extra.astype(jnp.bfloat16)


def sum_passed_kernel(
    index_ref,
    beside_ref,
    across_ref,
    over_x_ref,
    over_y_ref,
    beside_out_ref,
    across_out_ref,
):
    beside = beside_ref[...].astype(jnp.float32) + over_y_ref[...].astype(jnp.float32)
    beside_out_ref[...] = beside.astype(jnp.bfloat16)
    across = across_ref[...].astype(jnp.float32) + over_x_ref[...].astype(jnp.float32)
    across_out_ref[...] = across.astype(jnp.bfloat16)


def unpack_kernel(pieces, term_rows, index_ref, *refs):
    high_count = pieces[0].high_count
    flat_rows = sum(piece.flat_rows for piece in pieces)
    terms, outs = refs[: -2 - high_count], refs[-2 - high_count : -2]
    flat, packed = refs[-2:]
    high = index_ref[0] // LOW_COUNT
    count = len(terms) * term_rows // packed.shape[0]
    for first in range(0, packed.shape[0], term_rows):
        place = first // term_rows * count
        packed[first : first + term_rows, :] = sum(
            term[:term_rows, :].astype(jnp.float32) for term in terms[place : place + count]
        )
    start, source = 0, 0
    for piece in pieces:
        for block in range(piece.blocks):
            for place in range(high_count):
                flat[place, pl.ds(start + block, piece.own_rows, stride=piece.blocks), :] = packed[
                    pl.ds(source, piece.own_rows), :
                ]
                source = source + piece.own_rows
        start = start + piece.flat_rows
    for step, out_ref in enumerate(outs):
        out_ref[:flat_rows, :] = flat[high ^ step].astype(out_ref.dtype)
        if out_ref.shape[0] > flat_rows:
            extra = sum(term[term_rows:, :].astype(jnp.float32) for term in terms)
            out_ref[flat_rows:, :] = extra.astype(out_ref.dtype)


def array(shape, kind):
    return jax.ShapeDtypeStruct(shape, kind)


def gather_high(rows):
    high_count = lax.axis_size(ALL_AXES) // LOW_COUNT
    return [rows] + [swap(rows, step * LOW_COUNT) for step in range(1, high_count)]


def gather_own(pieces, parts, count, behind=()):
    high_count = pieces[0].high_count
    size = sum(piece.size for piece in pieces)
    return local_call(
        functools.partial(pack_kernel, pieces),
        (array((size // count, LANES), jnp.bfloat16),) * count,
        parts,
        (
            pltpu.VMEM((high_count, parts[0].shape[0], LANES), jnp.float32),
            pltpu.VMEM((size, LANES), jnp.float32),
        ),
        behind,
    )


def copied(value, behind):
    return local_call(copy_kernel, (array(value.shape, jnp.bfloat16),), (value,), (), behind)[0]


def held(values, behind):
    count = len(values)
    return pl.pallas_call(
        lambda *refs: None,
        out_shape=tuple(array(value.shape, value.dtype) for value in values),
        in_specs=[pl.BlockSpec(memory_space=pl.ANY)] * (count + len(behind)),
        out_specs=tuple(pl.BlockSpec(memory_space=pl.ANY) for _ in values),
        input_output_aliases={place: place for place in range(count)},
        cost_estimate=pl.CostEstimate(flops=0, bytes_accessed=0, transcendentals=0),
    )(*values, *behind)


def gather_halves(first, second):
    return swap(second, 4), swap(first, 2)


def gather_rest(first, second, beside_second, across_first, keys, behind):
    beside_first, across_second = swap(copied(first, keys[:1]), 4), swap(second, 2)
    over_x, over_y = swap(across_first, 4), swap(copied(beside_second, keys[1:]), 2)
    diagonal = held((over_x, over_y), behind)
    return first, second, beside_first, beside_second, across_first, across_second, *diagonal


def gather_wholes(own):
    return own, swap(own, 4), swap(own, 2), swap(own, 6)


def gather_cores(near):
    return near + tuple(swap(value, 1) for value in near)


def scatter_cores(far_three, far_one):
    far_one = swap(far_one, 1)
    return swap(far_three, 1), far_one


def scatter_one(near_one, far_one):
    half = near_one.shape[0] // 2
    to_x, to_y = local_call(
        sum_one_kernel, (array((half, LANES), jnp.bfloat16),) * 2, (near_one, far_one)
    )
    return swap(to_x, 4), swap(to_y, 2), to_x


def scatter_free(near_three, far_three, keys):
    half = near_three.shape[0] // 6
    beside_first, across_second = local_call(
        functools.partial(sum_halves_kernel, (2 * half, 5 * half)),
        (
            array((half, LANES), jnp.bfloat16),
            array((half + keys[0].size // LANES, LANES), jnp.bfloat16),
        ),
        (near_three, far_three, *keys),
    )
    return swap(beside_first, 4), swap(across_second, 2), beside_first


def scatter_rest(near_three, far_three, behind):
    half = near_three.shape[0] // 6
    return local_call(
        functools.partial(sum_halves_kernel, (0, half, 3 * half, 4 * half)),
        (array((half, LANES), jnp.bfloat16),) * 4,
        (near_three, far_three),
        (),
        behind,
    )


def scatter_passed(free, rest, over_x, over_y, behind=()):
    beside_first, across_second = free
    own_first, own_second, beside_second, across_first = rest
    half = own_first.shape[0]
    beside_second, across_first = local_call(
        sum_passed_kernel,
        (array((half, LANES), jnp.bfloat16),) * 2,
        (beside_second, across_first, over_x, over_y),
        (),
        behind,
    )
    terms = (
        own_first,
        beside_first,
        swap(across_first, 2),
        own_second,
        swap(beside_second, 4),
        across_second,
    )
    return terms, beside_second


def scatter_direct(pieces, near_three, near_one, far_three, far_one, behind=()):
    rows = near_one.shape[0]
    size = sum(piece.size for piece in pieces)
    own, beside, across, diagonal = local_call(
        functools.partial(sum_all_kernel, size),
        (array((rows, LANES), jnp.bfloat16),) * 4,
        (near_three, near_one, far_three, far_one),
        (),
        behind,
    )
    return own, swap(beside, 4), swap(across, 2), swap(diagonal, 6)


def scatter_unpack(pieces, terms, extra_count=0, behind=()):
    high_count = pieces[0].high_count
    size = sum(piece.size for piece in pieces)
    flat_rows = sum(piece.flat_rows for piece in pieces)
    return local_call(
        functools.partial(unpack_kernel, pieces, terms[0].shape[0] - extra_count),
        (array((flat_rows + extra_count, LANES), jnp.float32),)
        + (array((flat_rows + extra_count, LANES), jnp.bfloat16),) * (high_count - 1),
        terms,
        (
            pltpu.VMEM((high_count, flat_rows, LANES), jnp.float32),
            pltpu.VMEM((size, LANES), jnp.float32),
        ),
        behind,
    )


def norm_parts(values):
    scale = lax.rsqrt(jnp.mean(values * values, axis=-1, keepdims=True) + norm_eps)
    return scale, values * scale


def norm_back(scale, normal, upstream, weight_vec):
    weighted = upstream * (1.0 + weight_vec)
    inner = jnp.mean(weighted * normal, axis=-1, keepdims=True)
    return scale * (weighted - normal * inner), jnp.sum(normal * upstream, axis=0, keepdims=True)


def product(left_side, right_side, left_axis, right_axis):
    return lax.dot_general(
        left_side,
        right_side,
        (((left_axis,), (right_axis,)), ((), ())),
        preferred_element_type=jnp.float32,
    )


def unordered(rows_in, order_low):
    upper = rows_in.astype(jnp.bfloat16)
    lower = (rows_in - upper.astype(jnp.float32)).astype(jnp.bfloat16)
    return product(upper, order_low, 1, 1) + product(lower, order_low, 1, 1)


def weight_rows(refs, size, order, start, rows):
    count = len(refs) // LOW_COUNT
    part = size // count
    return refs[order * count + start // part][start % part : start % part + rows, :]


def put_rows(refs, size, order, start, rows):
    three, one = refs[:2] if order < 4 else refs[2:]
    if order % 4 == 3:
        one[start : start + rows.shape[0], :] = rows
    else:
        start = order % 4 * size + start
        three[start : start + rows.shape[0], :] = rows


def wide_tile(refs, size, start, rows):
    return jnp.concatenate(
        [weight_rows(refs, size, order, start, rows) for order in range(LOW_COUNT)]
    )


def put_wide_tile(refs, size, start, rows, tile):
    for order in range(LOW_COUNT):
        put_rows(refs, size, order, start, tile[order * rows : (order + 1) * rows])


def tall_rows(piece, low):
    for order, mask in enumerate(LOW_MASKS):
        for block in range(piece.blocks):
            for place in range(piece.high_count):
                row = (place * LOW_COUNT + (low ^ mask)) * piece.own_rows
                yield (
                    order,
                    block * piece.block_rows + place * piece.own_rows,
                    pl.ds(pl.multiple_of(row, piece.own_rows), piece.own_rows),
                    slice(block * LANES, (block + 1) * LANES),
                )


def ffn_kernel(
    gate_piece,
    down_piece,
    index_ref,
    middle_ref,
    cotangent_ref,
    gain_in_ref,
    gain_out_ref,
    order_ref,
    *refs,
):
    weight_refs, grad_refs = refs[:16], refs[20:24]
    block_out_ref, grad_middle_ref, grad_gain_in_ref, grad_gain_out_ref = refs[16:20]
    down_ref, hidden_ref, gelu_ref, slope_ref = refs[24:]
    low = index_ref[0] % LOW_COUNT
    rows = gate_piece.block_rows
    size = 2 * gate_piece.size + down_piece.size
    width = 2 * LANES
    for order, start, matrix_rows, columns in tall_rows(down_piece, low):
        start = start + 2 * gate_piece.size
        down_ref[matrix_rows, columns] = weight_rows(
            weight_refs, size, order, start, down_piece.own_rows
        )

    def wide_tiles(step):
        return [
            jnp.concatenate(
                [
                    wide_tile(weight_refs, size, offset + block * rows, rows)
                    for block in (2 * step, 2 * step + 1)
                ],
                axis=1,
            )
            for offset in (0, gate_piece.size)
        ]

    middle = middle_ref[...]
    scale_in, normal_in = norm_parts(middle)
    order_low = order_ref[...]
    normed = (normal_in * (1.0 + gain_in_ref[...])).astype(jnp.bfloat16)
    normed = product(normed, order_low, 1, 0).astype(jnp.bfloat16)
    for step in range(FF // width):
        columns = slice(step * width, (step + 1) * width)
        gate_weight, up_weight = wide_tiles(step)
        gate = product(normed, gate_weight, 1, 0)
        up = product(normed, up_weight, 1, 0)
        square = gate * gate
        bend = jnp.tanh(GELU_SCALE * gate * (1.0 + GELU_CUBE * square))
        half = 0.5 * (1.0 + bend)
        gelu = gate * half
        slope = half + 0.5 * gate * (1.0 - bend * bend) * GELU_SCALE * (
            1.0 + 3.0 * GELU_CUBE * square
        )
        gelu_ref[:, columns] = gelu
        slope_ref[:, columns] = slope * up
        hidden_ref[:, columns] = (gelu * up).astype(jnp.bfloat16)
    hidden = hidden_ref[...]
    scale_out, normal_out = norm_parts(product(hidden, down_ref[...], 1, 0))
    block_out_ref[...] = (middle + normal_out * (1.0 + gain_out_ref[...])).astype(jnp.bfloat16)
    upstream = cotangent_ref[...].astype(jnp.float32)
    grad_ffn, grad_gain_out_ref[...] = norm_back(
        scale_out, normal_out, upstream, gain_out_ref[...]
    )
    grad_ffn = grad_ffn.astype(jnp.bfloat16)
    grad_normed = jnp.zeros(middle.shape, jnp.float32)
    for step in range(FF // width):
        columns = slice(step * width, (step + 1) * width)
        grad_hidden = product(grad_ffn, down_ref[columns, :], 1, 1)
        down_ref[columns, :] = product(hidden_ref[:, columns], grad_ffn, 0, 0).astype(jnp.bfloat16)
        grads = [
            (grad_hidden * slope_ref[:, columns]).astype(jnp.bfloat16),
            (grad_hidden * gelu_ref[:, columns]).astype(jnp.bfloat16),
        ]
        for place, (grad, weight) in enumerate(zip(grads, wide_tiles(step))):
            grad_weight = product(normed, grad, 0, 0).astype(jnp.bfloat16)
            for side in range(2):
                put_wide_tile(
                    grad_refs,
                    size,
                    place * gate_piece.size + (2 * step + side) * rows,
                    rows,
                    grad_weight[:, side * LANES : (side + 1) * LANES],
                )
            grad_normed = grad_normed + product(grad, weight, 1, 1)
    for order, start, matrix_rows, columns in tall_rows(down_piece, low):
        start = start + 2 * gate_piece.size
        put_rows(grad_refs, size, order, start, down_ref[matrix_rows, columns])
    grad_middle, grad_gain_in_ref[...] = norm_back(
        scale_in, normal_in, unordered(grad_normed, order_low), gain_in_ref[...]
    )
    grad_middle_ref[...] = upstream + grad_middle


def grad_arrays(pieces, extra_count=0):
    size = sum(piece.size for piece in pieces)
    return (
        array((3 * size, LANES), jnp.bfloat16),
        array((size + extra_count, LANES), jnp.bfloat16),
    ) * 2


def ffn_blocks(pieces, middle, cotangent, gain_in, gain_out, order, blocks):
    rows = middle.shape[0]
    outs = local_call(
        functools.partial(ffn_kernel, pieces[4], pieces[6]),
        (
            array((rows, D), jnp.bfloat16),
            array((rows, D), jnp.float32),
            array((1, D), jnp.float32),
            array((1, D), jnp.float32),
            *grad_arrays(pieces[4:7]),
        ),
        (middle, cotangent, gain_in, gain_out, order, *blocks),
        (
            pltpu.VMEM((FF, D), jnp.bfloat16),
            pltpu.VMEM((rows, FF), jnp.bfloat16),
            pltpu.VMEM((rows, FF), jnp.float32),
            pltpu.VMEM((rows, FF), jnp.float32),
        ),
    )
    return *outs[:4], outs[4:]


def turn(values, cosine, sine):
    first_half, second_half = values[:, : HD // 2], values[:, HD // 2 :]
    return jnp.concatenate(
        [first_half * cosine - second_half * sine, second_half * cosine + first_half * sine], axis=1
    )


def wide_head(refs, size, start, rows):
    return jnp.concatenate(
        [wide_tile(refs, size, start + side * rows, rows) for side in range(2)], axis=1
    )


def head_starts(pieces):
    rows = pieces[0].block_rows
    return [2 * rows * head for head in range(HQ + 2)]


def project_kernel(
    pieces,
    index_ref,
    tokens_ref,
    gain_ref,
    gain_query_ref,
    gain_key_ref,
    cosine_ref,
    sine_ref,
    order_ref,
    *refs,
):
    weight_refs = refs[:8]
    normed_ref, query_proj_ref, key_proj_ref, query_ref, key_value_ref = refs[8:]
    size = sum(piece.size for piece in pieces)
    rows = pieces[0].block_rows
    cosine, sine = cosine_ref[...], sine_ref[...]
    _, normal = norm_parts(tokens_ref[...].astype(jnp.float32))
    normed = (normal * (1.0 + gain_ref[...])).astype(jnp.bfloat16)
    normed = product(normed, order_ref[...], 1, 0).astype(jnp.bfloat16)
    normed_ref[...] = normed
    starts = head_starts(pieces)
    for head, start in enumerate(starts):
        proj = product(normed, wide_head(weight_refs, size, start, rows), 1, 0)
        columns = slice(head * HD, (head + 1) * HD)
        if head == HQ + 1:
            key_value_ref[:, HD:] = proj.astype(jnp.bfloat16)
            continue
        gain_vec = gain_query_ref[...] if head < HQ else gain_key_ref[...]
        _, normal = norm_parts(proj)
        turned = turn(normal * (1.0 + gain_vec), cosine, sine).astype(jnp.bfloat16)
        if head < HQ:
            query_proj_ref[:, columns] = proj
            query_ref[:, columns] = turned
        else:
            key_proj_ref[...] = proj
            key_value_ref[:, :HD] = turned


def attend_kernel(
    pieces,
    index_ref,
    tokens_ref,
    gain_ref,
    allowed_ref,
    query_ref,
    *refs,
):
    weight_refs, key_value_refs = refs[:8], refs[8:-5]
    probs_ref, attended_ref, attn_out_ref, middle_ref, out_weight_ref = refs[-5:]
    out_piece = pieces[-1]
    low = index_ref[0] % LOW_COUNT
    size = sum(piece.size for piece in pieces)
    out_start = size - out_piece.size
    for order, start, matrix_rows, columns in tall_rows(out_piece, low):
        out_weight_ref[matrix_rows, columns] = weight_rows(
            weight_refs, size, order, start + out_start, out_piece.own_rows
        )
    rows = tokens_ref.shape[0]
    allowed = allowed_ref[...] > 0.0
    keys = jnp.concatenate([ref[:, :HD] for ref in key_value_refs])
    values = jnp.concatenate([ref[:, HD:] for ref in key_value_refs])
    count = keys.shape[0]
    for head in range(HQ):
        columns = slice(head * HD, (head + 1) * HD)
        scores = product(query_ref[:, columns], keys, 1, 1) * HD ** (-0.5)
        scores = jnp.where(allowed, scores, -1e30)
        raised = jnp.exp(scores - jnp.max(scores, axis=-1, keepdims=True))
        probs = raised / jnp.sum(raised, axis=-1, keepdims=True)
        probs_ref[:, head * count : (head + 1) * count] = probs
        attended_ref[:, columns] = product(probs.astype(jnp.bfloat16), values, 1, 0).astype(
            jnp.bfloat16
        )
    attn_out = product(attended_ref[...], out_weight_ref[...], 1, 0)
    attn_out_ref[...] = attn_out
    _, normal = norm_parts(attn_out)
    middle_ref[...] = tokens_ref[...].astype(jnp.float32) + normal * (1.0 + gain_ref[...])


def attend_back_kernel(
    index_ref,
    grad_middle_ref,
    attn_out_ref,
    gain_ref,
    out_weight_ref,
    attended_ref,
    probs_ref,
    query_ref,
    *refs,
):
    key_value_refs = refs[:4]
    grad_out_weight_ref, grad_query_ref, grad_gain_ref = refs[4:7]
    grad_own_ref, grad_across_ref, grad_cores_ref = refs[7:]
    rows = query_ref.shape[0]
    scale, normal = norm_parts(attn_out_ref[...])
    grad_attn, grad_gain_ref[...] = norm_back(scale, normal, grad_middle_ref[...], gain_ref[...])
    grad_attn = grad_attn.astype(jnp.bfloat16)
    grad_out_weight_ref[...] = product(attended_ref[...], grad_attn, 0, 0).astype(jnp.bfloat16)
    keys = jnp.concatenate([ref[:, :HD] for ref in key_value_refs])
    values = jnp.concatenate([ref[:, HD:] for ref in key_value_refs])
    count = keys.shape[0]
    grad_keys = jnp.zeros((count, HD), jnp.float32)
    grad_values = jnp.zeros((count, HD), jnp.float32)
    for head in range(HQ):
        columns = slice(head * HD, (head + 1) * HD)
        grad_attended = product(grad_attn, out_weight_ref[columns, :], 1, 1).astype(jnp.bfloat16)
        probs = probs_ref[:, head * count : (head + 1) * count]
        grad_probs = product(grad_attended, values, 1, 1)
        grad_values = grad_values + product(probs.astype(jnp.bfloat16), grad_attended, 0, 0)
        inner = jnp.sum(probs * grad_probs, axis=-1, keepdims=True)
        grad_scores = (probs * (grad_probs - inner) * HD ** (-0.5)).astype(jnp.bfloat16)
        grad_query_ref[:, columns] = product(grad_scores, keys, 1, 0)
        grad_keys = grad_keys + product(grad_scores, query_ref[:, columns], 0, 0)
    targets = (
        grad_own_ref,
        grad_cores_ref.at[:rows],
        grad_across_ref,
        grad_cores_ref.at[rows:],
    )
    for part, ref in enumerate(targets):
        ref[:, :HD] = grad_keys[part * rows : (part + 1) * rows].astype(ref.dtype)
        ref[:, HD:] = grad_values[part * rows : (part + 1) * rows].astype(ref.dtype)


def query_back_kernel(
    pieces,
    index_ref,
    gain_ref,
    cosine_ref,
    sine_ref,
    normed_ref,
    query_proj_ref,
    grad_query_ref,
    *refs,
):
    weight_refs = refs[:8]
    grad_weight_ref, grad_normed_ref, grad_gain_ref = refs[8:]
    size = sum(piece.size for piece in pieces)
    rows = pieces[0].block_rows
    cosine, sine = cosine_ref[...], sine_ref[...]
    normed = normed_ref[...]
    grad_normed = jnp.zeros(grad_normed_ref.shape, jnp.float32)
    grad_gain = jnp.zeros((1, HD), jnp.float32)
    for head, start in enumerate(head_starts(pieces)[:HQ]):
        columns = slice(head * HD, (head + 1) * HD)
        scale, normal = norm_parts(query_proj_ref[:, columns])
        upstream = turn(grad_query_ref[:, columns], cosine, -sine)
        grad, gain_row = norm_back(scale, normal, upstream, gain_ref[...])
        grad_gain = grad_gain + gain_row
        grad = grad.astype(jnp.bfloat16)
        weight = wide_head(weight_refs, size, start, rows)
        grad_normed = grad_normed + product(grad, weight, 1, 1)
        grad_weight_ref[:, columns] = product(normed, grad, 0, 0).astype(jnp.bfloat16)
    grad_normed_ref[...] = grad_normed
    grad_gain_ref[...] = grad_gain


def project_back_kernel(
    pieces,
    index_ref,
    tokens_ref,
    gain_ref,
    gain_key_ref,
    cosine_ref,
    sine_ref,
    order_ref,
    normed_ref,
    key_proj_ref,
    grad_normed_ref,
    grad_middle_ref,
    gain_attn_ref,
    gain_ffin_ref,
    gain_ffout_ref,
    gain_query_ref,
    own_key_ref,
    cores_key_ref,
    across_key_ref,
    *refs,
):
    weight_refs = refs[:8]
    grad_weight_ref, input_grad_ref, grad_gain_ref = refs[8:]
    size = sum(piece.size for piece in pieces)
    rows = pieces[0].block_rows
    normed = normed_ref[...]
    key_rows = own_key_ref.shape[0]
    key_value = own_key_ref[...] + cores_key_ref[:key_rows, :].astype(jnp.float32)
    first = across_key_ref.shape[0] - 4 * key_rows
    key_value = key_value + jnp.concatenate(
        [
            across_key_ref[first + block * key_rows : first + (block + 1) * key_rows, :].astype(
                jnp.float32
            )
            for block in range(4)
        ],
        axis=1,
    )
    scale, normal = norm_parts(key_proj_ref[...])
    upstream = turn(key_value[:, :HD], cosine_ref[...], -sine_ref[...])
    grad_key, grad_gain_key = norm_back(scale, normal, upstream, gain_key_ref[...])
    grad_normed = grad_normed_ref[...]
    for place, start in enumerate(head_starts(pieces)[HQ:]):
        grad = (key_value[:, HD:] if place else grad_key).astype(jnp.bfloat16)
        weight = wide_head(weight_refs, size, start, rows)
        grad_normed = grad_normed + product(grad, weight, 1, 1)
        grad_weight_ref[:, place * HD : (place + 1) * HD] = product(normed, grad, 0, 0).astype(
            jnp.bfloat16
        )
    scale, normal = norm_parts(tokens_ref[...].astype(jnp.float32))
    grad_inputs, grad_gain_input = norm_back(
        scale, normal, unordered(grad_normed, order_ref[...]), gain_ref[...]
    )
    input_grad_ref[...] = (grad_middle_ref[...] + grad_inputs).astype(jnp.bfloat16)
    grad_gains = [
        grad_gain_input,
        gain_attn_ref[...],
        gain_ffin_ref[...],
        gain_ffout_ref[...],
        gain_query_ref[...],
        grad_gain_key,
    ]
    row = 0
    grad_gain_ref[...] = jnp.zeros(grad_gain_ref.shape, jnp.float32)
    for values in grad_gains:
        for start in range(0, values.shape[1], LANES):
            grad_gain_ref[row : row + 1, :] = values[:, start : start + LANES]
            row = row + 1


def split_kernel(
    pieces,
    index_ref,
    query_ref,
    key_value_ref,
    out_ref,
    gain_ref,
    *grad_refs,
):
    low = index_ref[0] % LOW_COUNT
    size = sum(piece.size for piece in pieces)
    rows = pieces[0].block_rows
    start = 0
    for matrix_ref in (query_ref, key_value_ref):
        for column in range(0, matrix_ref.shape[1], LANES):
            tile = matrix_ref[:, column : column + LANES]
            put_wide_tile(grad_refs, size, start, rows, tile)
            start = start + rows
    out_piece = pieces[-1]
    for order, first, matrix_rows, columns in tall_rows(out_piece, low):
        put_rows(grad_refs, size, order, start + first, out_ref[matrix_rows, columns])
    for target in (grad_refs[1], grad_refs[3]):
        target[size:, :] = gain_ref[...].astype(jnp.bfloat16)


def width_order(device_count):
    low = lax.axis_index(ALL_AXES) % LOW_COUNT
    rows = D // device_count
    high_count = device_count // LOW_COUNT
    column = jnp.arange(D, dtype=jnp.int32)
    place = column // (rows * high_count)
    mask = (place & 1) * 4 + ((place >> 1) & 1) * 2 + (place >> 2)
    high = (column // rows) % high_count
    picked = (high * LOW_COUNT + (low ^ mask)) * rows + column % rows
    return (jnp.arange(D, dtype=jnp.int32)[:, None] == picked[None, :]).astype(jnp.bfloat16)


GAIN_ROWS = 32


def shards_blocks(
    device_count,
    tokens,
    doc_ids,
    cotangent,
    master,
    first_moment,
    second_moment,
    gains,
    gain_first,
    gain_second,
):
    pieces = [Piece(*shape_pair, device_count) for shape_pair in piece_shapes()]
    attention_pieces = pieces[:4]
    local_rows = tokens.shape[0]
    group_size = lax.axis_size("group")
    first_row = lax.axis_index("group") * local_rows
    attention_rows = sum(piece.flat_rows for piece in attention_pieces)
    ffn_pieces = pieces[4:7]
    rounded = master.astype(jnp.bfloat16)
    attention_parts = gather_high(rounded[:attention_rows])
    ffn_rows = rounded[attention_rows:]
    ffn_parts = gather_high(ffn_rows)
    attention_near = gather_wholes(
        *gather_own(attention_pieces, attention_parts, 1, (ffn_parts[1],))
    )
    attention_near = tuple(held(attention_near, ffn_parts[2:]))
    attention_blocks = gather_cores(attention_near)
    ffn_own = gather_own(ffn_pieces, ffn_parts, 2, attention_near[1:])
    ffn_passed = gather_halves(*ffn_own)
    gain_parts = []
    for start, width in ((0, D), (D, D), (2 * D, D), (3 * D, D), (4 * D, HD), (4 * D + HD, HD)):
        gain_parts.append(gains[start : start + width][None])
    gain_input, gain_attn, gain_ffin, gain_ffout, gain_query, gain_key = gain_parts
    order = width_order(device_count)
    doc_row = doc_ids[0]
    angles = lax.dynamic_slice_in_dim(angles_of(positions(doc_row)), first_row, local_rows, 0)
    cosine, sine = jnp.cos(angles), jnp.sin(angles)
    query_docs = lax.dynamic_slice_in_dim(doc_row, first_row, local_rows, 0)
    key_count = group_size * local_rows
    first_keys = [(lax.axis_index("group") ^ step) * local_rows for step in range(group_size)]
    key_docs = jnp.concatenate(
        [lax.dynamic_slice_in_dim(doc_row, start, local_rows, 0) for start in first_keys]
    )
    key_index = jnp.concatenate(
        [start + jnp.arange(local_rows, dtype=jnp.int32) for start in first_keys]
    )
    query_index = first_row + jnp.arange(local_rows, dtype=jnp.int32)
    distance = query_index[:, None] - key_index[None, :]
    allowed = (distance >= 0) & (distance < WINDOW) & (key_docs[None, :] == query_docs[:, None])
    allowed = allowed.astype(jnp.float32)

    width = HQ * HD
    normed, query_proj, key_proj, query_rot, key_value = local_call(
        functools.partial(project_kernel, attention_pieces),
        (
            array((local_rows, D), jnp.bfloat16),
            array((local_rows, width), jnp.float32),
            array((local_rows, HD), jnp.float32),
            array((local_rows, width), jnp.bfloat16),
            array((local_rows, 2 * HD), jnp.bfloat16),
        ),
        (tokens, gain_input, gain_query, gain_key, cosine, sine, order, *attention_blocks),
    )
    key_values = [key_value] + [swap(key_value, step) for step in range(1, group_size)]
    probs, attended, attn_out, middle, out_weight = local_call(
        functools.partial(attend_kernel, attention_pieces),
        (
            array((local_rows, HQ * key_count), jnp.float32),
            array((local_rows, width), jnp.bfloat16),
            array((local_rows, D), jnp.float32),
            array((local_rows, D), jnp.float32),
            array((width, D), jnp.bfloat16),
        ),
        (tokens, gain_attn, allowed, query_rot, *attention_blocks, *key_values),
    )
    ffn_weights = gather_cores(gather_rest(*ffn_own, *ffn_passed, key_values, (middle,)))
    outputs, grad_middle, grad_gain_ffin, grad_gain_ffout, grads_ffn = ffn_blocks(
        pieces, middle, cotangent, gain_ffin, gain_ffout, order, ffn_weights
    )
    near_three, near_one, far_three, far_one = grads_ffn
    far_three, far_one = scatter_cores(far_three, far_one)
    over_x, over_y, sent = scatter_one(near_one, far_one)
    sent = swap(sent[:16], 1)
    grad_out_weight, grad_query, grad_gain_attn, own_key, across_key, cores_key = local_call(
        attend_back_kernel,
        (
            array((width, D), jnp.bfloat16),
            array((local_rows, width), jnp.float32),
            array((1, D), jnp.float32),
            array((local_rows, 2 * HD), jnp.float32),
            array((local_rows, 2 * HD), jnp.float32),
            array((2 * local_rows, 2 * HD), jnp.bfloat16),
        ),
        (
            grad_middle,
            attn_out,
            gain_attn,
            out_weight,
            attended,
            probs,
            query_rot,
            *key_values,
        ),
        (),
        (sent,),
    )
    cores_key = swap(cores_key, 1)
    *free, sent = scatter_free(near_three, far_three, (across_key, cores_key))
    rest = scatter_rest(near_three, far_three, (sent,))
    grad_query_weight, grad_normed, grad_gain_query = local_call(
        functools.partial(query_back_kernel, attention_pieces),
        (
            array((D, width), jnp.bfloat16),
            array((local_rows, D), jnp.float32),
            array((1, HD), jnp.float32),
        ),
        (gain_query, cosine, sine, normed, query_proj, grad_query, *attention_blocks),
        (),
        (rest[0],),
    )
    ffn_terms, sent = scatter_passed(free, rest, over_x, over_y)
    grad_key_weight, grad_inputs, grad_gains = local_call(
        functools.partial(project_back_kernel, attention_pieces),
        (
            array((D, 2 * HD), jnp.bfloat16),
            array((local_rows, D), jnp.bfloat16),
            array((GAIN_ROWS, LANES), jnp.float32),
        ),
        (
            tokens,
            gain_input,
            gain_key,
            cosine,
            sine,
            order,
            normed,
            key_proj,
            grad_normed,
            grad_middle,
            grad_gain_attn,
            grad_gain_ffin,
            grad_gain_ffout,
            grad_gain_query,
            own_key,
            cores_key,
            free[1],
            *attention_blocks,
        ),
        (),
        (sent, free[0]),
    )
    near_three, near_one, far_three, far_one = local_call(
        functools.partial(split_kernel, attention_pieces),
        grad_arrays(attention_pieces, GAIN_ROWS),
        (grad_query_weight, grad_key_weight, grad_out_weight, grad_gains),
    )
    far_three, far_one = held((far_three, far_one), (ffn_terms[2], ffn_terms[4]))
    own_ffn, *planes = scatter_unpack(ffn_pieces, ffn_terms, 0, (near_one,))
    far_three, far_one = scatter_cores(far_three, far_one)
    terms = scatter_direct(
        attention_pieces, near_three, near_one, far_three, far_one, (own_ffn,)
    )
    arrived = [swap(plane, step * LOW_COUNT) for step, plane in enumerate(planes, start=1)]
    grads_ffn = own_ffn + sum(value.astype(jnp.float32) for value in arrived)
    own_attention, *planes = scatter_unpack(attention_pieces, terms, GAIN_ROWS, arrived)
    grads_attention = own_attention + sum(
        swap(plane, step * LOW_COUNT).astype(jnp.float32)
        for step, plane in enumerate(planes, start=1)
    )
    gain_grads = grads_attention[attention_rows:].reshape(-1)[: gains.shape[0]]
    grads_local = jnp.concatenate([grads_attention[:attention_rows], grads_ffn])
    return (
        outputs,
        grad_inputs,
        *adam_update(grads_local, first_moment, second_moment, master, learn_rate, weight_decay),
        *adam_update(gain_grads, gain_first, gain_second, gains, gain_rate, 0.0),
    )


def shards(
    tokens, doc_ids, cotangent, master, first_moment, second_moment, gains, gain_first, gain_second
):
    group_size = lax.axis_size("group")
    devices_all = lax.axis_size("dp") * group_size
    if aligned(devices_all):
        return shards_blocks(
            devices_all,
            tokens,
            doc_ids,
            cotangent,
            master,
            first_moment,
            second_moment,
            gains,
            gain_first,
            gain_second,
        )
    group_index = lax.axis_index("group")
    local_rows = tokens.shape[0]
    shard_parts = [
        part_rows.astype(jnp.bfloat16) for part_rows in split_rows(master, piece_rows(devices_all))
    ]
    gathered = (
        lax.all_gather(shard_parts[0], ("dp", "group"), axis=0, tiled=True),
        lax.all_gather(shard_parts[1], ("dp", "group"), axis=0, tiled=True),
        lax.all_gather(shard_parts[2], ("dp", "group"), axis=0, tiled=True),
        lax.all_gather(shard_parts[3], ("dp", "group"), axis=0, tiled=True),
        lax.all_gather(shard_parts[4], ("dp", "group"), axis=0, tiled=True),
        lax.all_gather(shard_parts[5], ("dp", "group"), axis=0, tiled=True),
        lax.all_gather(shard_parts[6], ("dp", "group"), axis=0, tiled=True),
    )
    query_weight, key_weight, value_weight, out_weight, gate_weight, up_weight, down_weight = [
        full_rows.reshape(shape_pair) for full_rows, shape_pair in zip(gathered, piece_shapes())
    ]
    norm_input = gains[0:D]
    norm_attn = gains[D : 2 * D]
    norm_ffin = gains[2 * D : 3 * D]
    norm_ffout = gains[3 * D : 4 * D]
    norm_query = gains[4 * D : 4 * D + HD]
    norm_key = gains[4 * D + HD : 4 * D + 2 * HD]
    doc_row = doc_ids[0]
    first_row = group_index * local_rows
    angles = lax.dynamic_slice_in_dim(angles_of(positions(doc_row)), first_row, local_rows, 0)
    query_docs = lax.dynamic_slice_in_dim(doc_row, first_row, local_rows, 0)
    inputs = tokens.astype(jnp.float32)
    normed, back_input = jax.vjp(rms_norm, inputs, norm_input)
    normed_low = normed.astype(jnp.bfloat16)
    query_proj = matmul(normed_low, query_weight)
    key_proj = matmul(normed_low, key_weight)
    value_proj = matmul(normed_low, value_weight)

    def query_prep(flat_rows, gain_vec):
        return rotate(rms_norm(flat_rows.reshape(local_rows, HQ, HD), gain_vec), angles[:, None, :])

    def key_prep(rows_in, gain_vec):
        return rotate(rms_norm(rows_in, gain_vec), angles)

    query_rot, back_query = jax.vjp(query_prep, query_proj, norm_query)
    key_rot, back_key = jax.vjp(key_prep, key_proj, norm_key)
    query_low = query_rot.astype(jnp.bfloat16)
    key_low = key_rot.astype(jnp.bfloat16)
    value_low = value_proj.astype(jnp.bfloat16)
    reach = min(-(-(WINDOW - 1) // local_rows), group_size - 1)
    key_list = [key_low]
    value_list = [value_low]
    for offset in range(1, reach + 1):
        key_far, value_far = shifted((key_low, value_low), "group", offset)
        key_list.insert(0, key_far)
        value_list.insert(0, value_far)
    key_all = jnp.concatenate(key_list, axis=0)
    value_all = jnp.concatenate(value_list, axis=0)
    key_count = (reach + 1) * local_rows
    doc_pad = jnp.concatenate([jnp.full((reach * local_rows,), -1, jnp.int32), doc_row])
    key_docs = lax.dynamic_slice_in_dim(doc_pad, first_row, key_count, 0)
    key_index = (group_index - reach) * local_rows + jnp.arange(key_count, dtype=jnp.int32)
    query_index = first_row + jnp.arange(local_rows, dtype=jnp.int32)
    distance = query_index[:, None] - key_index[None, :]
    allowed = (distance >= 0) & (distance < WINDOW) & (key_docs[None, :] == query_docs[:, None])

    def scores_of(key_rows_low):
        raw_scores = jnp.einsum(
            "qhd,kd->hqk", query_low, key_rows_low, preferred_element_type=jnp.float32
        ) * HD ** (-0.5)
        return jnp.where(allowed[None], raw_scores, -1e30)

    masked = scores_of(key_all)
    top_score = jnp.max(masked, axis=-1, keepdims=True)
    log_total = top_score + jnp.log(jnp.sum(jnp.exp(masked - top_score), axis=-1, keepdims=True))
    probs = jnp.exp(masked - log_total)
    attended = jnp.einsum(
        "hqk,kd->qhd", probs.astype(jnp.bfloat16), value_all, preferred_element_type=jnp.float32
    )
    attended_low = attended.reshape(local_rows, HQ * HD).astype(jnp.bfloat16)
    attn_out = matmul(attended_low, out_weight)
    branch_one, back_attn = jax.vjp(rms_norm, attn_out, norm_attn)
    middle = inputs + branch_one
    normed_two, back_ffin = jax.vjp(rms_norm, middle, norm_ffin)
    normed_two_low = normed_two.astype(jnp.bfloat16)
    gate_proj = matmul(normed_two_low, gate_weight)
    up_proj = matmul(normed_two_low, up_weight)
    hidden, back_hidden = jax.vjp(geglu, gate_proj, up_proj)
    hidden_low = hidden.astype(jnp.bfloat16)
    ffn_out = matmul(hidden_low, down_weight)
    branch_two, back_ffout = jax.vjp(rms_norm, ffn_out, norm_ffout)
    outputs = middle + branch_two
    grad_out = cotangent.astype(jnp.float32)
    grad_ffn, grad_gain_ffout = back_ffout(grad_out)
    grad_ffn_low = grad_ffn.astype(jnp.bfloat16)
    grad_down_w = jnp.einsum(
        "tf,td->fd", hidden_low, grad_ffn_low, preferred_element_type=jnp.float32
    )
    grad_hidden = jnp.einsum(
        "td,fd->tf", grad_ffn_low, down_weight, preferred_element_type=jnp.float32
    )
    grad_gate, grad_up = back_hidden(grad_hidden)
    grad_gate_low = grad_gate.astype(jnp.bfloat16)
    grad_up_low = grad_up.astype(jnp.bfloat16)
    grad_gate_w = jnp.einsum(
        "td,tf->df", normed_two_low, grad_gate_low, preferred_element_type=jnp.float32
    )
    grad_up_w = jnp.einsum(
        "td,tf->df", normed_two_low, grad_up_low, preferred_element_type=jnp.float32
    )
    grad_normed_two = jnp.einsum(
        "tf,df->td", grad_gate_low, gate_weight, preferred_element_type=jnp.float32
    ) + jnp.einsum("tf,df->td", grad_up_low, up_weight, preferred_element_type=jnp.float32)
    grad_middle_norm, grad_gain_ffin = back_ffin(grad_normed_two)
    grad_middle = grad_out + grad_middle_norm
    grad_attn, grad_gain_attn = back_attn(grad_middle)
    grad_attn_low = grad_attn.astype(jnp.bfloat16)
    grad_out_w = jnp.einsum(
        "to,td->od", attended_low, grad_attn_low, preferred_element_type=jnp.float32
    )
    grad_attended = jnp.einsum(
        "td,od->to", grad_attn_low, out_weight, preferred_element_type=jnp.float32
    )
    grad_attended_low = grad_attended.astype(jnp.bfloat16).reshape(local_rows, HQ, HD)
    probs_again = jnp.exp(scores_of(key_all) - log_total)
    grad_probs = jnp.einsum(
        "qhd,kd->hqk", grad_attended_low, value_all, preferred_element_type=jnp.float32
    )
    grad_value_all = jnp.einsum(
        "hqk,qhd->kd",
        probs_again.astype(jnp.bfloat16),
        grad_attended_low,
        preferred_element_type=jnp.float32,
    )
    grad_scores = probs_again * (
        grad_probs - jnp.sum(probs_again * grad_probs, axis=-1, keepdims=True)
    )
    grad_scores_low = (grad_scores * HD ** (-0.5)).astype(jnp.bfloat16)
    grad_query = jnp.einsum(
        "hqk,kd->qhd", grad_scores_low, key_all, preferred_element_type=jnp.float32
    )
    grad_key_all = jnp.einsum(
        "hqk,qhd->kd", grad_scores_low, query_low, preferred_element_type=jnp.float32
    )
    key_total = grad_key_all[reach * local_rows :]
    value_total = grad_value_all[reach * local_rows :]
    for offset in range(1, reach + 1):
        row_start = (reach - offset) * local_rows
        key_back, value_back = (
            shifted(
                grad_key_all[row_start : row_start + local_rows].astype(jnp.bfloat16),
                "group",
                -offset,
            ).astype(jnp.float32),
            shifted(
                grad_value_all[row_start : row_start + local_rows].astype(jnp.bfloat16),
                "group",
                -offset,
            ).astype(jnp.float32),
        )
        key_total = key_total + key_back
        value_total = value_total + value_back
    grad_query_proj, grad_gain_query = back_query(grad_query)
    grad_key_proj, grad_gain_key = back_key(key_total)
    grad_query_low = grad_query_proj.astype(jnp.bfloat16)
    grad_key_low = grad_key_proj.astype(jnp.bfloat16)
    grad_value_low = value_total.astype(jnp.bfloat16)
    grad_query_w = jnp.einsum(
        "td,te->de", normed_low, grad_query_low, preferred_element_type=jnp.float32
    )
    grad_key_w = jnp.einsum(
        "td,te->de", normed_low, grad_key_low, preferred_element_type=jnp.float32
    )
    grad_value_w = jnp.einsum(
        "td,te->de", normed_low, grad_value_low, preferred_element_type=jnp.float32
    )
    grad_normed = jnp.einsum(
        "te,de->td", grad_query_low, query_weight, preferred_element_type=jnp.float32
    )
    grad_normed = grad_normed + jnp.einsum(
        "te,de->td", grad_key_low, key_weight, preferred_element_type=jnp.float32
    )
    grad_normed = grad_normed + jnp.einsum(
        "te,de->td", grad_value_low, value_weight, preferred_element_type=jnp.float32
    )
    grad_input_norm, grad_gain_input = back_input(grad_normed)
    grad_inputs = grad_middle + grad_input_norm
    flat_query = grad_query_w.reshape(-1, 128)
    flat_key = grad_key_w.reshape(-1, 128)
    flat_value = grad_value_w.reshape(-1, 128)
    flat_out = grad_out_w.reshape(-1, 128)
    flat_gate = grad_gate_w.reshape(-1, 128)
    flat_up = grad_up_w.reshape(-1, 128)
    flat_down = grad_down_w.reshape(-1, 128)
    reduced = (
        lax.psum_scatter(flat_query, ("dp", "group"), scatter_dimension=0, tiled=True),
        lax.psum_scatter(flat_key, ("dp", "group"), scatter_dimension=0, tiled=True),
        lax.psum_scatter(flat_value, ("dp", "group"), scatter_dimension=0, tiled=True),
        lax.psum_scatter(flat_out, ("dp", "group"), scatter_dimension=0, tiled=True),
        lax.psum_scatter(flat_gate, ("dp", "group"), scatter_dimension=0, tiled=True),
        lax.psum_scatter(flat_up, ("dp", "group"), scatter_dimension=0, tiled=True),
        lax.psum_scatter(flat_down, ("dp", "group"), scatter_dimension=0, tiled=True),
    )
    grads_local = jnp.concatenate(list(reduced), axis=0)
    gain_grads = lax.psum(
        jnp.concatenate(
            [
                grad_gain_input,
                grad_gain_attn,
                grad_gain_ffin,
                grad_gain_ffout,
                grad_gain_query,
                grad_gain_key,
            ]
        ),
        ("dp", "group"),
    )
    moment_first, moment_second, master_new = adam_update(
        grads_local, first_moment, second_moment, master, learn_rate, weight_decay
    )
    gain_moment_first, gain_moment_second, gains_new = adam_update(
        gain_grads, gain_first, gain_second, gains, gain_rate, 0.0
    )
    return (
        outputs.astype(jnp.bfloat16),
        grad_inputs.astype(jnp.bfloat16),
        moment_first,
        moment_second,
        master_new,
        gain_moment_first,
        gain_moment_second,
        gains_new,
    )


def solution(mesh):
    placed = (
        P(("dp", "group"), None),
        P("dp", None),
        P(("dp", "group"), None),
        P(("dp", "group"), None),
        P(("dp", "group"), None),
        P(("dp", "group"), None),
        P(),
        P(),
        P(),
    )
    return jax.shard_map(
        shards,
        mesh=mesh,
        in_specs=placed,
        out_specs=(
            P(("dp", "group"), None),
            P(("dp", "group"), None),
            P(("dp", "group"), None),
            P(("dp", "group"), None),
            P(("dp", "group"), None),
            P(),
            P(),
            P(),
        ),
        check_vma=False,
    )
```

```python
import functools
import math

import jax
import jax.numpy as jnp
from jax import lax
from jax.experimental import pallas as pl
from jax.experimental.pallas import tpu as pltpu
from jax.sharding import PartitionSpec as P

D = 640
HQ = 4
HD = 256
FF = 2048
WINDOW = 512
STEP = 10
ALL_AXES = ("dp", "group")


norm_eps = 1e-06
rope_base = 10000.0
beta_first = 0.9
beta_second = 0.999
learn_rate = 0.05
gain_rate = 0.25
adam_floor = 1e-08
weight_decay = 0.1


def shifted(value, axis, steps):
    count = lax.axis_size(axis)
    initial, last = (max(0, -steps), min(count, count - steps))
    return lax.ppermute(value, axis, [(source, source + steps) for source in range(initial, last)])


def rms_norm(values, weight_vec):
    return (
        values
        * lax.rsqrt(jnp.mean(values * values, axis=-1, keepdims=True) + norm_eps)
        * (1.0 + weight_vec)
    )


def positions(doc_row):
    length = doc_row.shape[0]
    counter = jnp.arange(length, dtype=jnp.int32)
    starts_here = jnp.concatenate([jnp.ones((1,), jnp.bool_), doc_row[1:] != doc_row[:-1]])
    begins = lax.cummax(jnp.where(starts_here, counter, jnp.zeros_like(counter)), axis=0)
    return counter - begins


def angles_of(places):
    half_dim = HD // 2
    frequency = rope_base ** (-(jnp.arange(half_dim, dtype=jnp.float32) * 2.0 / HD))
    return places.astype(jnp.float32)[:, None] * frequency[None, :]


def rotate(values, angles):
    half_dim = values.shape[-1] // 2
    first_half = values[..., :half_dim]
    second_half = values[..., half_dim:]
    cosine = jnp.cos(angles)
    sine_part = jnp.sin(angles)
    return jnp.concatenate(
        [
            first_half * cosine - second_half * sine_part,
            second_half * cosine + first_half * sine_part,
        ],
        axis=-1,
    )


def geglu(gate_in, up_in):
    return jax.nn.gelu(gate_in, approximate=True) * up_in


def adam_update(gradient, first_old, second_old, params_old, rate, decay_rate):
    first_new = beta_first * first_old + (1.0 - beta_first) * gradient
    second_new = beta_second * second_old + (1.0 - beta_second) * gradient * gradient
    first_hat = first_new / (1.0 - beta_first**STEP)
    second_hat = second_new / (1.0 - beta_second**STEP)
    params_new = params_old - rate * (
        first_hat / (jnp.sqrt(second_hat) + adam_floor) + decay_rate * params_old
    )
    return (first_new, second_new, params_new)


def piece_rows(device_count):
    return [
        entries // (128 * device_count)
        for entries in (D * HQ * HD, D * HD, D * HD, HQ * HD * D, D * FF, D * FF, FF * D)
    ]


def piece_shapes():
    return [(D, HQ * HD), (D, HD), (D, HD), (HQ * HD, D), (D, FF), (D, FF), (FF, D)]


def split_rows(stacked, row_list):
    result = []
    row_start = 0
    for row_count in row_list:
        result.append(stacked[row_start : row_start + row_count])
        row_start = row_start + row_count
    return result


def matmul(left_side, right_side):
    return jnp.dot(left_side, right_side, preferred_element_type=jnp.float32)


LOW_COUNT = 8
LANES = 128
LOW_MASKS = (0, 4, 2, 6, 1, 5, 3, 7)
GELU_SCALE = (2.0 / math.pi) ** 0.5
GELU_CUBE = 0.044715
VMEM_BYTES = 56 * 1024 * 1024


def aligned(device_count):
    groups = lax.axis_size("group") == 4
    return groups and device_count % LOW_COUNT == 0 and D % device_count == 0


def swap(value, mask):
    count = lax.axis_size(ALL_AXES)
    return lax.ppermute(value, ALL_AXES, [(source, source ^ mask) for source in range(count)])


def local_call(kernel, outs, operands, scratch=(), behind=()):
    specs = [pl.BlockSpec(memory_space=pltpu.SMEM)]
    specs = specs + [pl.BlockSpec(memory_space=pltpu.VMEM)] * len(operands)
    specs = specs + [pl.BlockSpec(memory_space=pl.ANY)] * len(behind)
    first, last = 1 + len(operands), 1 + len(operands) + len(behind)

    def body(*refs):
        kernel(*refs[:first], *refs[last:])

    return pl.pallas_call(
        body,
        out_shape=outs,
        in_specs=specs,
        out_specs=tuple(pl.BlockSpec(memory_space=pltpu.VMEM) for _ in outs),
        scratch_shapes=scratch,
        compiler_params=pltpu.CompilerParams(vmem_limit_bytes=VMEM_BYTES),
        cost_estimate=pl.CostEstimate(flops=0, bytes_accessed=0, transcendentals=0),
    )(lax.axis_index(ALL_AXES).astype(jnp.int32).reshape(1), *operands, *behind)


class Piece:
    def __init__(self, rows, columns, device_count):
        self.rows = rows
        self.columns = columns
        self.wide = rows == D
        self.blocks = columns // LANES
        self.own_rows = rows // device_count
        self.flat_rows = self.own_rows * self.blocks
        self.high_count = device_count // LOW_COUNT
        self.block_rows = self.own_rows * self.high_count
        self.size = self.block_rows * self.blocks


def copy_kernel(index_ref, in_ref, out_ref):
    out_ref[...] = in_ref[...]


def pack_kernel(pieces, index_ref, *refs):
    high_count = pieces[0].high_count
    parts, out_refs, flat, packed = refs[:high_count], refs[high_count:-2], refs[-2], refs[-1]
    high = index_ref[0] // LOW_COUNT
    for step, part in enumerate(parts):
        flat[high ^ step] = part[...].astype(jnp.float32)
    start, target = 0, 0
    for piece in pieces:
        for block in range(piece.blocks):
            for place in range(high_count):
                packed[pl.ds(target, piece.own_rows), :] = flat[
                    place, pl.ds(start + block, piece.own_rows, stride=piece.blocks), :
                ]
                target = target + piece.own_rows
        start = start + piece.flat_rows
    count = target // len(out_refs)
    for place, out_ref in enumerate(out_refs):
        out_ref[...] = packed[place * count : (place + 1) * count, :].astype(jnp.bfloat16)


def sum_one_kernel(size, index_ref, near_ref, far_ref, to_x_ref, to_y_ref):
    total = near_ref[...].astype(jnp.float32) + far_ref[...].astype(jnp.float32)
    half = size // 2
    to_x_ref[:half, :] = total[:half].astype(jnp.bfloat16)
    if total.shape[0] > size:
        to_x_ref[half:, :] = total[size:].astype(jnp.bfloat16)
    to_y_ref[...] = total[half:size].astype(jnp.bfloat16)


def sum_three_kernel(
    size,
    index_ref,
    near_ref,
    far_ref,
    *refs,
):
    key_refs = refs[:-5]
    own_ref, beside_first_ref, beside_second_ref, across_first_ref, across_second_ref = refs[-5:]
    half = size // 2
    if key_refs:
        across_key_ref, cores_key_ref = key_refs
        rows = across_key_ref.shape[0]
        keys = across_key_ref[...] + cores_key_ref[rows:, :].astype(jnp.float32)
        for block in range(keys.shape[1] // LANES):
            first = half + block * rows
            columns = slice(block * LANES, (block + 1) * LANES)
            across_second_ref[first : first + rows, :] = keys[:, columns].astype(jnp.bfloat16)
    outs = (beside_first_ref, beside_second_ref, across_first_ref, across_second_ref)
    total = near_ref[:size, :].astype(jnp.float32) + far_ref[:size, :].astype(jnp.float32)
    own_ref[...] = total.astype(jnp.bfloat16)
    for place, out_ref in enumerate(outs):
        rows = slice(size + place * half, size + (place + 1) * half)
        total = near_ref[rows, :].astype(jnp.float32) + far_ref[rows, :].astype(jnp.float32)
        out_ref[:half, :] = total.astype(jnp.bfloat16)


def sum_all_kernel(size, index_ref, near_three, near_one, far_three, far_one, *out_refs):
    sum_one_kernel(size, index_ref, near_one, far_one, *out_refs[:2])
    sum_three_kernel(size, index_ref, near_three, far_three, *out_refs[2:])


def sum_passed_kernel(
    size,
    index_ref,
    beside_ref,
    across_ref,
    over_x_ref,
    over_y_ref,
    near_one_ref,
    far_one_ref,
    beside_out_ref,
    across_out_ref,
    extra_ref,
):
    half = size // 2
    beside = beside_ref[...].astype(jnp.float32) + over_y_ref[...].astype(jnp.float32)
    beside_out_ref[...] = beside.astype(jnp.bfloat16)
    across = across_ref[...].astype(jnp.float32) + over_x_ref[:half, :].astype(jnp.float32)
    across_out_ref[:half, :] = across.astype(jnp.bfloat16)
    if across_out_ref.shape[0] > half:
        extra = near_one_ref[size:, :].astype(jnp.float32)
        extra = extra + far_one_ref[size:, :].astype(jnp.float32)
        extra = extra + over_x_ref[half:, :].astype(jnp.float32)
        extra_ref[...] = extra
        across_out_ref[half:, :] = extra.astype(jnp.bfloat16)
    else:
        extra_ref[...] = jnp.zeros(extra_ref.shape, jnp.float32)


def unpack_kernel(
    pieces,
    index_ref,
    own_ref,
    beside_first_ref,
    beside_second_ref,
    across_first_ref,
    across_second_ref,
    extra_ref,
    *refs,
):
    high_count = pieces[0].high_count
    half = sum(piece.size for piece in pieces) // 2
    flat_rows = sum(piece.flat_rows for piece in pieces)
    outs, flat, packed = refs[:-2], refs[-2], refs[-1]
    high = index_ref[0] // LOW_COUNT
    packed[:half, :] = (
        own_ref[:half, :].astype(jnp.float32)
        + beside_first_ref[...].astype(jnp.float32)
        + across_first_ref[:half, :].astype(jnp.float32)
    )
    packed[half:, :] = (
        own_ref[half:, :].astype(jnp.float32)
        + beside_second_ref[...].astype(jnp.float32)
        + across_second_ref[:half, :].astype(jnp.float32)
    )
    start, source = 0, 0
    for piece in pieces:
        for block in range(piece.blocks):
            for place in range(high_count):
                flat[place, pl.ds(start + block, piece.own_rows, stride=piece.blocks), :] = packed[
                    pl.ds(source, piece.own_rows), :
                ]
                source = source + piece.own_rows
        start = start + piece.flat_rows
    for step, out_ref in enumerate(outs):
        out_ref[:flat_rows, :] = flat[high ^ step].astype(out_ref.dtype)
        if out_ref.shape[0] > flat_rows:
            extra = extra_ref[...] + across_first_ref[half:, :].astype(jnp.float32)
            out_ref[flat_rows:, :] = extra.astype(out_ref.dtype)


def array(shape, kind):
    return jax.ShapeDtypeStruct(shape, kind)


def gather_high(rows):
    high_count = lax.axis_size(ALL_AXES) // LOW_COUNT
    return [rows] + [swap(rows, step * LOW_COUNT) for step in range(1, high_count)]


def gather_own(pieces, parts, count, behind=()):
    high_count = pieces[0].high_count
    size = sum(piece.size for piece in pieces)
    return local_call(
        functools.partial(pack_kernel, pieces),
        (array((size // count, LANES), jnp.bfloat16),) * count,
        parts,
        (
            pltpu.VMEM((high_count, parts[0].shape[0], LANES), jnp.float32),
            pltpu.VMEM((size, LANES), jnp.float32),
        ),
        behind,
    )


def copied(value, behind):
    return local_call(copy_kernel, (array(value.shape, jnp.bfloat16),), (value,), (), behind)[0]


def held(values, behind):
    count = len(values)
    return pl.pallas_call(
        lambda *refs: None,
        out_shape=tuple(array(value.shape, value.dtype) for value in values),
        in_specs=[pl.BlockSpec(memory_space=pl.ANY)] * (count + len(behind)),
        out_specs=tuple(pl.BlockSpec(memory_space=pl.ANY) for _ in values),
        input_output_aliases={place: place for place in range(count)},
        cost_estimate=pl.CostEstimate(flops=0, bytes_accessed=0, transcendentals=0),
    )(*values, *behind)


def gather_halves(first, second):
    return swap(second, 4), swap(first, 2)


def gather_rest(first, second, beside_second, across_first, keys, behind):
    beside_first, across_second = swap(copied(first, keys[:1]), 4), swap(second, 2)
    over_x, over_y = swap(across_first, 4), swap(copied(beside_second, keys[1:]), 2)
    diagonal = held((over_x, over_y), behind)
    return first, second, beside_first, beside_second, across_first, across_second, *diagonal


def gather_wholes(own):
    return own, swap(own, 4), swap(own, 2), swap(own, 6)


def gather_cores(near):
    return near + tuple(swap(value, 1) for value in near)


def scatter_cores(far_three, far_one):
    far_one = swap(far_one, 1)
    return swap(far_three, 1), far_one


def scatter_one(pieces, near_one, far_one, behind=()):
    half = sum(piece.size for piece in pieces) // 2
    to_x, to_y = local_call(
        functools.partial(sum_one_kernel, 2 * half),
        (
            array((near_one.shape[0] - half, LANES), jnp.bfloat16),
            array((half, LANES), jnp.bfloat16),
        ),
        (near_one, far_one),
        (),
        behind,
    )
    return swap(to_x, 4), swap(to_y, 2), to_y


def scatter_three(pieces, near_three, far_three, behind=(), keys=()):
    size = sum(piece.size for piece in pieces)
    half = size // 2
    own, beside_first, beside_second, across_first, across_second = local_call(
        functools.partial(sum_three_kernel, size),
        (
            array((size, LANES), jnp.bfloat16),
            *(array((half, LANES), jnp.bfloat16),) * 3,
            array((half + (keys[0].size // LANES if keys else 0), LANES), jnp.bfloat16),
        ),
        (near_three, far_three, *keys),
        (),
        behind,
    )
    return own, swap(beside_first, 4), beside_second, across_first, swap(across_second, 2)


def scatter_all(pieces, near_three, near_one, far_three, far_one, behind=()):
    size = sum(piece.size for piece in pieces)
    half = size // 2
    to_x, to_y, own, beside_first, beside_second, across_first, across_second = local_call(
        functools.partial(sum_all_kernel, size),
        (
            array((near_one.shape[0] - half, LANES), jnp.bfloat16),
            array((half, LANES), jnp.bfloat16),
            array((size, LANES), jnp.bfloat16),
            *(array((half, LANES), jnp.bfloat16),) * 4,
        ),
        (near_three, near_one, far_three, far_one),
        (),
        behind,
    )
    over_x, over_y = swap(to_x, 4), swap(to_y, 2)
    return (
        over_x,
        over_y,
        (own, swap(beside_first, 4), beside_second, across_first, swap(across_second, 2)),
    )


def scatter_passed(pieces, threes, over_x, over_y, near_one, far_one, behind=()):
    size = sum(piece.size for piece in pieces)
    extra_count = near_one.shape[0] - size
    own, beside_first, beside_second, across_first, across_second = threes
    beside_second, across_first, extra = local_call(
        functools.partial(sum_passed_kernel, size),
        (
            array((size // 2, LANES), jnp.bfloat16),
            array((size // 2 + extra_count, LANES), jnp.bfloat16),
            array((max(extra_count, 8), LANES), jnp.float32),
        ),
        (beside_second, across_first, over_x, over_y, near_one, far_one),
        (),
        behind,
    )
    terms = (
        own,
        beside_first,
        swap(beside_second, 4),
        swap(across_first, 2),
        across_second,
        extra,
    )
    return terms, beside_second


def scatter_high(pieces, terms, behind=()):
    high_count = pieces[0].high_count
    size = sum(piece.size for piece in pieces)
    flat_rows = sum(piece.flat_rows for piece in pieces)
    out_rows = flat_rows + terms[3].shape[0] - size // 2
    outs = local_call(
        functools.partial(unpack_kernel, pieces),
        (array((out_rows, LANES), jnp.float32),)
        + (array((out_rows, LANES), jnp.bfloat16),) * (high_count - 1),
        terms,
        (
            pltpu.VMEM((high_count, flat_rows, LANES), jnp.float32),
            pltpu.VMEM((size, LANES), jnp.float32),
        ),
        behind,
    )
    arrived = [swap(send, step * LOW_COUNT) for step, send in enumerate(outs) if step]
    return outs[0] + sum(value.astype(jnp.float32) for value in arrived), outs[0], arrived


def norm_parts(values):
    scale = lax.rsqrt(jnp.mean(values * values, axis=-1, keepdims=True) + norm_eps)
    return scale, values * scale


def norm_back(scale, normal, upstream, weight_vec):
    weighted = upstream * (1.0 + weight_vec)
    inner = jnp.mean(weighted * normal, axis=-1, keepdims=True)
    return scale * (weighted - normal * inner), jnp.sum(normal * upstream, axis=0, keepdims=True)


def product(left_side, right_side, left_axis, right_axis):
    return lax.dot_general(
        left_side,
        right_side,
        (((left_axis,), (right_axis,)), ((), ())),
        preferred_element_type=jnp.float32,
    )


def turned_over(rows_low):
    return rows_low.astype(jnp.float32).T.astype(jnp.bfloat16)


def unordered(rows_in, order_low):
    upper = rows_in.astype(jnp.bfloat16)
    lower = (rows_in - upper.astype(jnp.float32)).astype(jnp.bfloat16)
    return product(upper, order_low, 1, 1) + product(lower, order_low, 1, 1)


def weight_rows(refs, size, order, start, rows):
    count = len(refs) // LOW_COUNT
    part = size // count
    return refs[order * count + start // part][start % part : start % part + rows, :]


def put_rows(refs, size, order, start, rows):
    three, one = refs[:2] if order < 4 else refs[2:]
    if order % 4 == 3:
        one[start : start + rows.shape[0], :] = rows
    else:
        start = order % 4 * size + start
        three[start : start + rows.shape[0], :] = rows


def wide_tile(refs, size, start, rows):
    return jnp.concatenate(
        [weight_rows(refs, size, order, start, rows) for order in range(LOW_COUNT)]
    )


def put_wide_tile(refs, size, start, rows, tile):
    for order in range(LOW_COUNT):
        put_rows(refs, size, order, start, tile[order * rows : (order + 1) * rows])


def tall_rows(piece, low):
    for order, mask in enumerate(LOW_MASKS):
        for block in range(piece.blocks):
            for place in range(piece.high_count):
                row = (place * LOW_COUNT + (low ^ mask)) * piece.own_rows
                yield (
                    order,
                    block * piece.block_rows + place * piece.own_rows,
                    pl.ds(pl.multiple_of(row, piece.own_rows), piece.own_rows),
                    slice(block * LANES, (block + 1) * LANES),
                )


def ffn_kernel(
    gate_piece,
    down_piece,
    index_ref,
    middle_ref,
    cotangent_ref,
    gain_in_ref,
    gain_out_ref,
    order_ref,
    *refs,
):
    weight_refs, grad_refs = refs[:16], refs[20:24]
    block_out_ref, grad_middle_ref, grad_gain_in_ref, grad_gain_out_ref = refs[16:20]
    down_ref, hidden_ref, gelu_ref, slope_ref = refs[24:]
    low = index_ref[0] % LOW_COUNT
    rows = gate_piece.block_rows
    size = 2 * gate_piece.size + down_piece.size
    width = 2 * LANES
    for order, start, matrix_rows, columns in tall_rows(down_piece, low):
        start = start + 2 * gate_piece.size
        down_ref[matrix_rows, columns] = weight_rows(
            weight_refs, size, order, start, down_piece.own_rows
        )

    def wide_tiles(step):
        return [
            jnp.concatenate(
                [
                    wide_tile(weight_refs, size, offset + block * rows, rows)
                    for block in (2 * step, 2 * step + 1)
                ],
                axis=1,
            )
            for offset in (0, gate_piece.size)
        ]

    middle = middle_ref[...]
    scale_in, normal_in = norm_parts(middle)
    order_low = order_ref[...]
    normed = (normal_in * (1.0 + gain_in_ref[...])).astype(jnp.bfloat16)
    normed = product(normed, order_low, 1, 0).astype(jnp.bfloat16)
    normed_turned = turned_over(normed)
    for step in range(FF // width):
        columns = slice(step * width, (step + 1) * width)
        gate_weight, up_weight = wide_tiles(step)
        gate = product(normed, gate_weight, 1, 0)
        up = product(normed, up_weight, 1, 0)
        square = gate * gate
        bend = jnp.tanh(GELU_SCALE * gate * (1.0 + GELU_CUBE * square))
        half = 0.5 * (1.0 + bend)
        gelu = gate * half
        slope = half + 0.5 * gate * (1.0 - bend * bend) * GELU_SCALE * (
            1.0 + 3.0 * GELU_CUBE * square
        )
        gelu_ref[:, columns] = gelu
        slope_ref[:, columns] = slope * up
        hidden_ref[:, columns] = (gelu * up).astype(jnp.bfloat16)
    hidden = hidden_ref[...]
    scale_out, normal_out = norm_parts(product(hidden, down_ref[...], 1, 0))
    block_out_ref[...] = (middle + normal_out * (1.0 + gain_out_ref[...])).astype(jnp.bfloat16)
    upstream = cotangent_ref[...].astype(jnp.float32)
    grad_ffn, grad_gain_out_ref[...] = norm_back(
        scale_out, normal_out, upstream, gain_out_ref[...]
    )
    grad_ffn = grad_ffn.astype(jnp.bfloat16)
    grad_normed = jnp.zeros(middle.shape, jnp.float32)
    for step in range(FF // width):
        columns = slice(step * width, (step + 1) * width)
        grad_hidden = product(grad_ffn, down_ref[columns, :], 1, 1)
        down_ref[columns, :] = product(hidden_ref[:, columns], grad_ffn, 0, 0).astype(jnp.bfloat16)
        grads = [
            (grad_hidden * slope_ref[:, columns]).astype(jnp.bfloat16),
            (grad_hidden * gelu_ref[:, columns]).astype(jnp.bfloat16),
        ]
        for place, (grad, weight) in enumerate(zip(grads, wide_tiles(step))):
            grad_weight = product(normed_turned, grad, 1, 0).astype(jnp.bfloat16)
            for side in range(2):
                put_wide_tile(
                    grad_refs,
                    size,
                    place * gate_piece.size + (2 * step + side) * rows,
                    rows,
                    grad_weight[:, side * LANES : (side + 1) * LANES],
                )
            grad_normed = grad_normed + product(grad, weight, 1, 1)
    for order, start, matrix_rows, columns in tall_rows(down_piece, low):
        start = start + 2 * gate_piece.size
        put_rows(grad_refs, size, order, start, down_ref[matrix_rows, columns])
    grad_middle, grad_gain_in_ref[...] = norm_back(
        scale_in, normal_in, unordered(grad_normed, order_low), gain_in_ref[...]
    )
    grad_middle_ref[...] = upstream + grad_middle


def grad_arrays(pieces, extra_count=0):
    size = sum(piece.size for piece in pieces)
    return (
        array((3 * size, LANES), jnp.bfloat16),
        array((size + extra_count, LANES), jnp.bfloat16),
    ) * 2


def ffn_blocks(pieces, middle, cotangent, gain_in, gain_out, order, blocks):
    rows = middle.shape[0]
    outs = local_call(
        functools.partial(ffn_kernel, pieces[4], pieces[6]),
        (
            array((rows, D), jnp.bfloat16),
            array((rows, D), jnp.float32),
            array((1, D), jnp.float32),
            array((1, D), jnp.float32),
            *grad_arrays(pieces[4:7]),
        ),
        (middle, cotangent, gain_in, gain_out, order, *blocks),
        (
            pltpu.VMEM((FF, D), jnp.bfloat16),
            pltpu.VMEM((rows, FF), jnp.bfloat16),
            pltpu.VMEM((rows, FF), jnp.float32),
            pltpu.VMEM((rows, FF), jnp.float32),
        ),
    )
    return *outs[:4], outs[4:]


def turn(values, cosine, sine):
    first_half, second_half = values[:, : HD // 2], values[:, HD // 2 :]
    return jnp.concatenate(
        [first_half * cosine - second_half * sine, second_half * cosine + first_half * sine], axis=1
    )


def wide_head(refs, size, start, rows):
    return jnp.concatenate(
        [wide_tile(refs, size, start + side * rows, rows) for side in range(2)], axis=1
    )


def head_starts(pieces):
    rows = pieces[0].block_rows
    return [2 * rows * head for head in range(HQ + 2)]


def project_kernel(
    pieces,
    index_ref,
    tokens_ref,
    gain_ref,
    gain_query_ref,
    gain_key_ref,
    cosine_ref,
    sine_ref,
    order_ref,
    *refs,
):
    weight_refs = refs[:8]
    normed_ref, query_proj_ref, key_proj_ref, query_ref, key_value_ref = refs[8:]
    size = sum(piece.size for piece in pieces)
    rows = pieces[0].block_rows
    cosine, sine = cosine_ref[...], sine_ref[...]
    _, normal = norm_parts(tokens_ref[...].astype(jnp.float32))
    normed = (normal * (1.0 + gain_ref[...])).astype(jnp.bfloat16)
    normed = product(normed, order_ref[...], 1, 0).astype(jnp.bfloat16)
    normed_ref[...] = normed
    starts = head_starts(pieces)
    for head, start in enumerate(starts):
        proj = product(normed, wide_head(weight_refs, size, start, rows), 1, 0)
        columns = slice(head * HD, (head + 1) * HD)
        if head == HQ + 1:
            key_value_ref[:, HD:] = proj.astype(jnp.bfloat16)
            continue
        gain_vec = gain_query_ref[...] if head < HQ else gain_key_ref[...]
        _, normal = norm_parts(proj)
        turned = turn(normal * (1.0 + gain_vec), cosine, sine).astype(jnp.bfloat16)
        if head < HQ:
            query_proj_ref[:, columns] = proj
            query_ref[:, columns] = turned
        else:
            key_proj_ref[...] = proj
            key_value_ref[:, :HD] = turned


def attend_kernel(
    pieces,
    index_ref,
    tokens_ref,
    gain_ref,
    allowed_ref,
    query_ref,
    *refs,
):
    weight_refs, key_value_refs = refs[:8], refs[8:-5]
    probs_ref, attended_ref, attn_out_ref, middle_ref, out_weight_ref = refs[-5:]
    out_piece = pieces[-1]
    low = index_ref[0] % LOW_COUNT
    size = sum(piece.size for piece in pieces)
    out_start = size - out_piece.size
    for order, start, matrix_rows, columns in tall_rows(out_piece, low):
        out_weight_ref[matrix_rows, columns] = weight_rows(
            weight_refs, size, order, start + out_start, out_piece.own_rows
        )
    rows = tokens_ref.shape[0]
    allowed = allowed_ref[...] > 0.0
    keys = jnp.concatenate([ref[:, :HD] for ref in key_value_refs])
    values = jnp.concatenate([ref[:, HD:] for ref in key_value_refs])
    count = keys.shape[0]
    for head in range(HQ):
        columns = slice(head * HD, (head + 1) * HD)
        scores = product(query_ref[:, columns], keys, 1, 1) * HD ** (-0.5)
        scores = jnp.where(allowed, scores, -1e30)
        raised = jnp.exp(scores - jnp.max(scores, axis=-1, keepdims=True))
        probs = raised / jnp.sum(raised, axis=-1, keepdims=True)
        probs_ref[:, head * count : (head + 1) * count] = probs
        attended_ref[:, columns] = product(probs.astype(jnp.bfloat16), values, 1, 0).astype(
            jnp.bfloat16
        )
    attn_out = product(attended_ref[...], out_weight_ref[...], 1, 0)
    attn_out_ref[...] = attn_out
    _, normal = norm_parts(attn_out)
    middle_ref[...] = tokens_ref[...].astype(jnp.float32) + normal * (1.0 + gain_ref[...])


def attend_back_kernel(
    index_ref,
    grad_middle_ref,
    attn_out_ref,
    gain_ref,
    out_weight_ref,
    attended_ref,
    probs_ref,
    query_ref,
    *refs,
):
    key_value_refs = refs[:4]
    grad_out_weight_ref, grad_query_ref, grad_gain_ref = refs[4:7]
    grad_own_ref, grad_across_ref, grad_cores_ref = refs[7:]
    rows = query_ref.shape[0]
    scale, normal = norm_parts(attn_out_ref[...])
    grad_attn, grad_gain_ref[...] = norm_back(scale, normal, grad_middle_ref[...], gain_ref[...])
    grad_attn = grad_attn.astype(jnp.bfloat16)
    grad_out_weight_ref[...] = product(attended_ref[...], grad_attn, 0, 0).astype(jnp.bfloat16)
    keys = jnp.concatenate([ref[:, :HD] for ref in key_value_refs])
    values = jnp.concatenate([ref[:, HD:] for ref in key_value_refs])
    count = keys.shape[0]
    grad_keys = jnp.zeros((count, HD), jnp.float32)
    grad_values = jnp.zeros((count, HD), jnp.float32)
    for head in range(HQ):
        columns = slice(head * HD, (head + 1) * HD)
        grad_attended = product(grad_attn, out_weight_ref[columns, :], 1, 1).astype(jnp.bfloat16)
        probs = probs_ref[:, head * count : (head + 1) * count]
        grad_probs = product(grad_attended, values, 1, 1)
        grad_values = grad_values + product(probs.astype(jnp.bfloat16), grad_attended, 0, 0)
        inner = jnp.sum(probs * grad_probs, axis=-1, keepdims=True)
        grad_scores = (probs * (grad_probs - inner) * HD ** (-0.5)).astype(jnp.bfloat16)
        grad_query_ref[:, columns] = product(grad_scores, keys, 1, 0)
        grad_keys = grad_keys + product(grad_scores, query_ref[:, columns], 0, 0)
    targets = (
        grad_own_ref,
        grad_cores_ref.at[:rows],
        grad_across_ref,
        grad_cores_ref.at[rows:],
    )
    for part, ref in enumerate(targets):
        ref[:, :HD] = grad_keys[part * rows : (part + 1) * rows].astype(ref.dtype)
        ref[:, HD:] = grad_values[part * rows : (part + 1) * rows].astype(ref.dtype)


def query_back_kernel(
    pieces,
    index_ref,
    gain_ref,
    cosine_ref,
    sine_ref,
    normed_ref,
    query_proj_ref,
    grad_query_ref,
    *refs,
):
    weight_refs = refs[:8]
    grad_weight_ref, grad_normed_ref, grad_gain_ref = refs[8:]
    size = sum(piece.size for piece in pieces)
    rows = pieces[0].block_rows
    cosine, sine = cosine_ref[...], sine_ref[...]
    normed_turned = turned_over(normed_ref[...])
    grad_normed = jnp.zeros(grad_normed_ref.shape, jnp.float32)
    grad_gain = jnp.zeros((1, HD), jnp.float32)
    for head, start in enumerate(head_starts(pieces)[:HQ]):
        columns = slice(head * HD, (head + 1) * HD)
        scale, normal = norm_parts(query_proj_ref[:, columns])
        upstream = turn(grad_query_ref[:, columns], cosine, -sine)
        grad, gain_row = norm_back(scale, normal, upstream, gain_ref[...])
        grad_gain = grad_gain + gain_row
        grad = grad.astype(jnp.bfloat16)
        weight = wide_head(weight_refs, size, start, rows)
        grad_normed = grad_normed + product(grad, weight, 1, 1)
        grad_weight_ref[:, columns] = product(normed_turned, grad, 1, 0).astype(jnp.bfloat16)
    grad_normed_ref[...] = grad_normed
    grad_gain_ref[...] = grad_gain


def project_back_kernel(
    pieces,
    index_ref,
    tokens_ref,
    gain_ref,
    gain_key_ref,
    cosine_ref,
    sine_ref,
    order_ref,
    normed_ref,
    key_proj_ref,
    grad_normed_ref,
    grad_middle_ref,
    gain_attn_ref,
    gain_ffin_ref,
    gain_ffout_ref,
    gain_query_ref,
    own_key_ref,
    cores_key_ref,
    across_key_ref,
    *refs,
):
    weight_refs = refs[:8]
    grad_weight_ref, input_grad_ref, grad_gain_ref = refs[8:]
    size = sum(piece.size for piece in pieces)
    rows = pieces[0].block_rows
    normed = normed_ref[...]
    key_rows = own_key_ref.shape[0]
    first = across_key_ref.shape[0] - 4 * key_rows
    key_value = own_key_ref[...] + cores_key_ref[:key_rows, :].astype(jnp.float32)
    key_value = key_value + jnp.concatenate(
        [
            across_key_ref[first + block * key_rows : first + (block + 1) * key_rows, :].astype(
                jnp.float32
            )
            for block in range(4)
        ],
        axis=1,
    )
    scale, normal = norm_parts(key_proj_ref[...])
    upstream = turn(key_value[:, :HD], cosine_ref[...], -sine_ref[...])
    grad_key, grad_gain_key = norm_back(scale, normal, upstream, gain_key_ref[...])
    grad_normed = grad_normed_ref[...]
    for place, start in enumerate(head_starts(pieces)[HQ:]):
        grad = (key_value[:, HD:] if place else grad_key).astype(jnp.bfloat16)
        weight = wide_head(weight_refs, size, start, rows)
        grad_normed = grad_normed + product(grad, weight, 1, 1)
        grad_weight_ref[:, place * HD : (place + 1) * HD] = product(normed, grad, 0, 0).astype(
            jnp.bfloat16
        )
    scale, normal = norm_parts(tokens_ref[...].astype(jnp.float32))
    grad_inputs, grad_gain_input = norm_back(
        scale, normal, unordered(grad_normed, order_ref[...]), gain_ref[...]
    )
    input_grad_ref[...] = (grad_middle_ref[...] + grad_inputs).astype(jnp.bfloat16)
    grad_gains = [
        grad_gain_input,
        gain_attn_ref[...],
        gain_ffin_ref[...],
        gain_ffout_ref[...],
        gain_query_ref[...],
        grad_gain_key,
    ]
    row = 0
    grad_gain_ref[...] = jnp.zeros(grad_gain_ref.shape, jnp.float32)
    for values in grad_gains:
        for start in range(0, values.shape[1], LANES):
            grad_gain_ref[row : row + 1, :] = values[:, start : start + LANES]
            row = row + 1


def split_kernel(
    pieces,
    index_ref,
    query_ref,
    key_value_ref,
    out_ref,
    gain_ref,
    *grad_refs,
):
    low = index_ref[0] % LOW_COUNT
    size = sum(piece.size for piece in pieces)
    rows = pieces[0].block_rows
    start = 0
    for matrix_ref in (query_ref, key_value_ref):
        for column in range(0, matrix_ref.shape[1], LANES):
            tile = matrix_ref[:, column : column + LANES]
            put_wide_tile(grad_refs, size, start, rows, tile)
            start = start + rows
    out_piece = pieces[-1]
    for order, first, matrix_rows, columns in tall_rows(out_piece, low):
        put_rows(grad_refs, size, order, start + first, out_ref[matrix_rows, columns])
    for target in (grad_refs[1], grad_refs[3]):
        target[size:, :] = gain_ref[...].astype(jnp.bfloat16)


def width_order(device_count):
    low = lax.axis_index(ALL_AXES) % LOW_COUNT
    rows = D // device_count
    high_count = device_count // LOW_COUNT
    column = jnp.arange(D, dtype=jnp.int32)
    place = column // (rows * high_count)
    mask = (place & 1) * 4 + ((place >> 1) & 1) * 2 + (place >> 2)
    high = (column // rows) % high_count
    picked = (high * LOW_COUNT + (low ^ mask)) * rows + column % rows
    return (jnp.arange(D, dtype=jnp.int32)[:, None] == picked[None, :]).astype(jnp.bfloat16)


GAIN_ROWS = 32


def shards_blocks(
    device_count,
    tokens,
    doc_ids,
    cotangent,
    master,
    first_moment,
    second_moment,
    gains,
    gain_first,
    gain_second,
):
    pieces = [Piece(*shape_pair, device_count) for shape_pair in piece_shapes()]
    attention_pieces = pieces[:4]
    local_rows = tokens.shape[0]
    group_size = lax.axis_size("group")
    first_row = lax.axis_index("group") * local_rows
    attention_rows = sum(piece.flat_rows for piece in attention_pieces)
    ffn_pieces = pieces[4:7]
    rounded = master.astype(jnp.bfloat16)
    attention_parts = gather_high(rounded[:attention_rows])
    ffn_rows = rounded[attention_rows:]
    ffn_parts = gather_high(ffn_rows)
    attention_near = gather_wholes(
        *gather_own(attention_pieces, attention_parts, 1, (ffn_parts[1],))
    )
    attention_near = tuple(held(attention_near, ffn_parts[2:]))
    attention_blocks = gather_cores(attention_near)
    ffn_own = gather_own(ffn_pieces, ffn_parts, 2, attention_near[1:])
    ffn_passed = gather_halves(*ffn_own)
    gain_parts = []
    for start, width in ((0, D), (D, D), (2 * D, D), (3 * D, D), (4 * D, HD), (4 * D + HD, HD)):
        gain_parts.append(gains[start : start + width][None])
    gain_input, gain_attn, gain_ffin, gain_ffout, gain_query, gain_key = gain_parts
    order = width_order(device_count)
    doc_row = doc_ids[0]
    angles = lax.dynamic_slice_in_dim(angles_of(positions(doc_row)), first_row, local_rows, 0)
    cosine, sine = jnp.cos(angles), jnp.sin(angles)
    query_docs = lax.dynamic_slice_in_dim(doc_row, first_row, local_rows, 0)
    key_count = group_size * local_rows
    first_keys = [(lax.axis_index("group") ^ step) * local_rows for step in range(group_size)]
    key_docs = jnp.concatenate(
        [lax.dynamic_slice_in_dim(doc_row, start, local_rows, 0) for start in first_keys]
    )
    key_index = jnp.concatenate(
        [start + jnp.arange(local_rows, dtype=jnp.int32) for start in first_keys]
    )
    query_index = first_row + jnp.arange(local_rows, dtype=jnp.int32)
    distance = query_index[:, None] - key_index[None, :]
    allowed = (distance >= 0) & (distance < WINDOW) & (key_docs[None, :] == query_docs[:, None])
    allowed = allowed.astype(jnp.float32)

    width = HQ * HD
    normed, query_proj, key_proj, query_rot, key_value = local_call(
        functools.partial(project_kernel, attention_pieces),
        (
            array((local_rows, D), jnp.bfloat16),
            array((local_rows, width), jnp.float32),
            array((local_rows, HD), jnp.float32),
            array((local_rows, width), jnp.bfloat16),
            array((local_rows, 2 * HD), jnp.bfloat16),
        ),
        (tokens, gain_input, gain_query, gain_key, cosine, sine, order, *attention_blocks),
    )
    key_values = [key_value] + [swap(key_value, step) for step in range(1, group_size)]
    probs, attended, attn_out, middle, out_weight = local_call(
        functools.partial(attend_kernel, attention_pieces),
        (
            array((local_rows, HQ * key_count), jnp.float32),
            array((local_rows, width), jnp.bfloat16),
            array((local_rows, D), jnp.float32),
            array((local_rows, D), jnp.float32),
            array((width, D), jnp.bfloat16),
        ),
        (tokens, gain_attn, allowed, query_rot, *attention_blocks, *key_values),
    )
    ffn_weights = gather_cores(gather_rest(*ffn_own, *ffn_passed, key_values, (middle,)))
    outputs, grad_middle, grad_gain_ffin, grad_gain_ffout, grads_ffn = ffn_blocks(
        pieces, middle, cotangent, gain_ffin, gain_ffout, order, ffn_weights
    )
    near_three, near_one, far_three, far_one = grads_ffn
    far_three, far_one = scatter_cores(far_three, far_one)
    grad_out_weight, grad_query, grad_gain_attn, own_key, across_key, cores_key = local_call(
        attend_back_kernel,
        (
            array((width, D), jnp.bfloat16),
            array((local_rows, width), jnp.float32),
            array((1, D), jnp.float32),
            array((local_rows, 2 * HD), jnp.float32),
            array((local_rows, 2 * HD), jnp.float32),
            array((2 * local_rows, 2 * HD), jnp.bfloat16),
        ),
        (
            grad_middle,
            attn_out,
            gain_attn,
            out_weight,
            attended,
            probs,
            query_rot,
            *key_values,
        ),
    )
    cores_key = swap(cores_key, 1)
    over_x, over_y, sent = scatter_one(ffn_pieces, near_one, far_one, (grad_query,))
    threes = scatter_three(ffn_pieces, near_three, far_three, (sent,), (across_key, cores_key))
    grad_query_weight, grad_normed, grad_gain_query = local_call(
        functools.partial(query_back_kernel, attention_pieces),
        (
            array((D, width), jnp.bfloat16),
            array((local_rows, D), jnp.float32),
            array((1, HD), jnp.float32),
        ),
        (gain_query, cosine, sine, normed, query_proj, grad_query, *attention_blocks),
        (),
        (threes[0],),
    )
    ffn_terms, sent = scatter_passed(
        ffn_pieces, threes, over_x, over_y, near_one, far_one, (grad_normed,)
    )
    grad_key_weight, grad_inputs, grad_gains = local_call(
        functools.partial(project_back_kernel, attention_pieces),
        (
            array((D, 2 * HD), jnp.bfloat16),
            array((local_rows, D), jnp.bfloat16),
            array((GAIN_ROWS, LANES), jnp.float32),
        ),
        (
            tokens,
            gain_input,
            gain_key,
            cosine,
            sine,
            order,
            normed,
            key_proj,
            grad_normed,
            grad_middle,
            grad_gain_attn,
            grad_gain_ffin,
            grad_gain_ffout,
            grad_gain_query,
            own_key,
            cores_key,
            threes[4],
            *attention_blocks,
        ),
        (),
        (sent, threes[1]),
    )
    near_three, near_one, far_three, far_one = local_call(
        functools.partial(split_kernel, attention_pieces),
        grad_arrays(attention_pieces, GAIN_ROWS),
        (grad_query_weight, grad_key_weight, grad_out_weight, grad_gains),
    )
    far_three, far_one = held((far_three, far_one), ffn_terms[2:4])
    grads_ffn, sent, arrived = scatter_high(ffn_pieces, ffn_terms, (near_one,))
    far_three, far_one = scatter_cores(far_three, far_one)
    over_x, over_y, threes = scatter_all(
        attention_pieces, near_three, near_one, far_three, far_one, (sent,)
    )
    terms, _ = scatter_passed(
        attention_pieces, threes, over_x, over_y, near_one, far_one, (arrived[0],)
    )
    grads_attention, _, _ = scatter_high(attention_pieces, terms, arrived)
    gain_grads = grads_attention[attention_rows:].reshape(-1)[: gains.shape[0]]
    grads_local = jnp.concatenate([grads_attention[:attention_rows], grads_ffn])
    return (
        outputs,
        grad_inputs,
        *adam_update(grads_local, first_moment, second_moment, master, learn_rate, weight_decay),
        *adam_update(gain_grads, gain_first, gain_second, gains, gain_rate, 0.0),
    )


def shards(
    tokens, doc_ids, cotangent, master, first_moment, second_moment, gains, gain_first, gain_second
):
    group_size = lax.axis_size("group")
    devices_all = lax.axis_size("dp") * group_size
    if aligned(devices_all):
        return shards_blocks(
            devices_all,
            tokens,
            doc_ids,
            cotangent,
            master,
            first_moment,
            second_moment,
            gains,
            gain_first,
            gain_second,
        )
    group_index = lax.axis_index("group")
    local_rows = tokens.shape[0]
    shard_parts = [
        part_rows.astype(jnp.bfloat16) for part_rows in split_rows(master, piece_rows(devices_all))
    ]
    gathered = (
        lax.all_gather(shard_parts[0], ("dp", "group"), axis=0, tiled=True),
        lax.all_gather(shard_parts[1], ("dp", "group"), axis=0, tiled=True),
        lax.all_gather(shard_parts[2], ("dp", "group"), axis=0, tiled=True),
        lax.all_gather(shard_parts[3], ("dp", "group"), axis=0, tiled=True),
        lax.all_gather(shard_parts[4], ("dp", "group"), axis=0, tiled=True),
        lax.all_gather(shard_parts[5], ("dp", "group"), axis=0, tiled=True),
        lax.all_gather(shard_parts[6], ("dp", "group"), axis=0, tiled=True),
    )
    query_weight, key_weight, value_weight, out_weight, gate_weight, up_weight, down_weight = [
        full_rows.reshape(shape_pair) for full_rows, shape_pair in zip(gathered, piece_shapes())
    ]
    norm_input = gains[0:D]
    norm_attn = gains[D : 2 * D]
    norm_ffin = gains[2 * D : 3 * D]
    norm_ffout = gains[3 * D : 4 * D]
    norm_query = gains[4 * D : 4 * D + HD]
    norm_key = gains[4 * D + HD : 4 * D + 2 * HD]
    doc_row = doc_ids[0]
    first_row = group_index * local_rows
    angles = lax.dynamic_slice_in_dim(angles_of(positions(doc_row)), first_row, local_rows, 0)
    query_docs = lax.dynamic_slice_in_dim(doc_row, first_row, local_rows, 0)
    inputs = tokens.astype(jnp.float32)
    normed, back_input = jax.vjp(rms_norm, inputs, norm_input)
    normed_low = normed.astype(jnp.bfloat16)
    query_proj = matmul(normed_low, query_weight)
    key_proj = matmul(normed_low, key_weight)
    value_proj = matmul(normed_low, value_weight)

    def query_prep(flat_rows, gain_vec):
        return rotate(rms_norm(flat_rows.reshape(local_rows, HQ, HD), gain_vec), angles[:, None, :])

    def key_prep(rows_in, gain_vec):
        return rotate(rms_norm(rows_in, gain_vec), angles)

    query_rot, back_query = jax.vjp(query_prep, query_proj, norm_query)
    key_rot, back_key = jax.vjp(key_prep, key_proj, norm_key)
    query_low = query_rot.astype(jnp.bfloat16)
    key_low = key_rot.astype(jnp.bfloat16)
    value_low = value_proj.astype(jnp.bfloat16)
    reach = min(-(-(WINDOW - 1) // local_rows), group_size - 1)
    key_list = [key_low]
    value_list = [value_low]
    for offset in range(1, reach + 1):
        key_far, value_far = shifted((key_low, value_low), "group", offset)
        key_list.insert(0, key_far)
        value_list.insert(0, value_far)
    key_all = jnp.concatenate(key_list, axis=0)
    value_all = jnp.concatenate(value_list, axis=0)
    key_count = (reach + 1) * local_rows
    doc_pad = jnp.concatenate([jnp.full((reach * local_rows,), -1, jnp.int32), doc_row])
    key_docs = lax.dynamic_slice_in_dim(doc_pad, first_row, key_count, 0)
    key_index = (group_index - reach) * local_rows + jnp.arange(key_count, dtype=jnp.int32)
    query_index = first_row + jnp.arange(local_rows, dtype=jnp.int32)
    distance = query_index[:, None] - key_index[None, :]
    allowed = (distance >= 0) & (distance < WINDOW) & (key_docs[None, :] == query_docs[:, None])

    def scores_of(key_rows_low):
        raw_scores = jnp.einsum(
            "qhd,kd->hqk", query_low, key_rows_low, preferred_element_type=jnp.float32
        ) * HD ** (-0.5)
        return jnp.where(allowed[None], raw_scores, -1e30)

    masked = scores_of(key_all)
    top_score = jnp.max(masked, axis=-1, keepdims=True)
    log_total = top_score + jnp.log(jnp.sum(jnp.exp(masked - top_score), axis=-1, keepdims=True))
    probs = jnp.exp(masked - log_total)
    attended = jnp.einsum(
        "hqk,kd->qhd", probs.astype(jnp.bfloat16), value_all, preferred_element_type=jnp.float32
    )
    attended_low = attended.reshape(local_rows, HQ * HD).astype(jnp.bfloat16)
    attn_out = matmul(attended_low, out_weight)
    branch_one, back_attn = jax.vjp(rms_norm, attn_out, norm_attn)
    middle = inputs + branch_one
    normed_two, back_ffin = jax.vjp(rms_norm, middle, norm_ffin)
    normed_two_low = normed_two.astype(jnp.bfloat16)
    gate_proj = matmul(normed_two_low, gate_weight)
    up_proj = matmul(normed_two_low, up_weight)
    hidden, back_hidden = jax.vjp(geglu, gate_proj, up_proj)
    hidden_low = hidden.astype(jnp.bfloat16)
    ffn_out = matmul(hidden_low, down_weight)
    branch_two, back_ffout = jax.vjp(rms_norm, ffn_out, norm_ffout)
    outputs = middle + branch_two
    grad_out = cotangent.astype(jnp.float32)
    grad_ffn, grad_gain_ffout = back_ffout(grad_out)
    grad_ffn_low = grad_ffn.astype(jnp.bfloat16)
    grad_down_w = jnp.einsum(
        "tf,td->fd", hidden_low, grad_ffn_low, preferred_element_type=jnp.float32
    )
    grad_hidden = jnp.einsum(
        "td,fd->tf", grad_ffn_low, down_weight, preferred_element_type=jnp.float32
    )
    grad_gate, grad_up = back_hidden(grad_hidden)
    grad_gate_low = grad_gate.astype(jnp.bfloat16)
    grad_up_low = grad_up.astype(jnp.bfloat16)
    grad_gate_w = jnp.einsum(
        "td,tf->df", normed_two_low, grad_gate_low, preferred_element_type=jnp.float32
    )
    grad_up_w = jnp.einsum(
        "td,tf->df", normed_two_low, grad_up_low, preferred_element_type=jnp.float32
    )
    grad_normed_two = jnp.einsum(
        "tf,df->td", grad_gate_low, gate_weight, preferred_element_type=jnp.float32
    ) + jnp.einsum("tf,df->td", grad_up_low, up_weight, preferred_element_type=jnp.float32)
    grad_middle_norm, grad_gain_ffin = back_ffin(grad_normed_two)
    grad_middle = grad_out + grad_middle_norm
    grad_attn, grad_gain_attn = back_attn(grad_middle)
    grad_attn_low = grad_attn.astype(jnp.bfloat16)
    grad_out_w = jnp.einsum(
        "to,td->od", attended_low, grad_attn_low, preferred_element_type=jnp.float32
    )
    grad_attended = jnp.einsum(
        "td,od->to", grad_attn_low, out_weight, preferred_element_type=jnp.float32
    )
    grad_attended_low = grad_attended.astype(jnp.bfloat16).reshape(local_rows, HQ, HD)
    probs_again = jnp.exp(scores_of(key_all) - log_total)
    grad_probs = jnp.einsum(
        "qhd,kd->hqk", grad_attended_low, value_all, preferred_element_type=jnp.float32
    )
    grad_value_all = jnp.einsum(
        "hqk,qhd->kd",
        probs_again.astype(jnp.bfloat16),
        grad_attended_low,
        preferred_element_type=jnp.float32,
    )
    grad_scores = probs_again * (
        grad_probs - jnp.sum(probs_again * grad_probs, axis=-1, keepdims=True)
    )
    grad_scores_low = (grad_scores * HD ** (-0.5)).astype(jnp.bfloat16)
    grad_query = jnp.einsum(
        "hqk,kd->qhd", grad_scores_low, key_all, preferred_element_type=jnp.float32
    )
    grad_key_all = jnp.einsum(
        "hqk,qhd->kd", grad_scores_low, query_low, preferred_element_type=jnp.float32
    )
    key_total = grad_key_all[reach * local_rows :]
    value_total = grad_value_all[reach * local_rows :]
    for offset in range(1, reach + 1):
        row_start = (reach - offset) * local_rows
        key_back, value_back = (
            shifted(
                grad_key_all[row_start : row_start + local_rows].astype(jnp.bfloat16),
                "group",
                -offset,
            ).astype(jnp.float32),
            shifted(
                grad_value_all[row_start : row_start + local_rows].astype(jnp.bfloat16),
                "group",
                -offset,
            ).astype(jnp.float32),
        )
        key_total = key_total + key_back
        value_total = value_total + value_back
    grad_query_proj, grad_gain_query = back_query(grad_query)
    grad_key_proj, grad_gain_key = back_key(key_total)
    grad_query_low = grad_query_proj.astype(jnp.bfloat16)
    grad_key_low = grad_key_proj.astype(jnp.bfloat16)
    grad_value_low = value_total.astype(jnp.bfloat16)
    grad_query_w = jnp.einsum(
        "td,te->de", normed_low, grad_query_low, preferred_element_type=jnp.float32
    )
    grad_key_w = jnp.einsum(
        "td,te->de", normed_low, grad_key_low, preferred_element_type=jnp.float32
    )
    grad_value_w = jnp.einsum(
        "td,te->de", normed_low, grad_value_low, preferred_element_type=jnp.float32
    )
    grad_normed = jnp.einsum(
        "te,de->td", grad_query_low, query_weight, preferred_element_type=jnp.float32
    )
    grad_normed = grad_normed + jnp.einsum(
        "te,de->td", grad_key_low, key_weight, preferred_element_type=jnp.float32
    )
    grad_normed = grad_normed + jnp.einsum(
        "te,de->td", grad_value_low, value_weight, preferred_element_type=jnp.float32
    )
    grad_input_norm, grad_gain_input = back_input(grad_normed)
    grad_inputs = grad_middle + grad_input_norm
    flat_query = grad_query_w.reshape(-1, 128)
    flat_key = grad_key_w.reshape(-1, 128)
    flat_value = grad_value_w.reshape(-1, 128)
    flat_out = grad_out_w.reshape(-1, 128)
    flat_gate = grad_gate_w.reshape(-1, 128)
    flat_up = grad_up_w.reshape(-1, 128)
    flat_down = grad_down_w.reshape(-1, 128)
    reduced = (
        lax.psum_scatter(flat_query, ("dp", "group"), scatter_dimension=0, tiled=True),
        lax.psum_scatter(flat_key, ("dp", "group"), scatter_dimension=0, tiled=True),
        lax.psum_scatter(flat_value, ("dp", "group"), scatter_dimension=0, tiled=True),
        lax.psum_scatter(flat_out, ("dp", "group"), scatter_dimension=0, tiled=True),
        lax.psum_scatter(flat_gate, ("dp", "group"), scatter_dimension=0, tiled=True),
        lax.psum_scatter(flat_up, ("dp", "group"), scatter_dimension=0, tiled=True),
        lax.psum_scatter(flat_down, ("dp", "group"), scatter_dimension=0, tiled=True),
    )
    grads_local = jnp.concatenate(list(reduced), axis=0)
    gain_grads = lax.psum(
        jnp.concatenate(
            [
                grad_gain_input,
                grad_gain_attn,
                grad_gain_ffin,
                grad_gain_ffout,
                grad_gain_query,
                grad_gain_key,
            ]
        ),
        ("dp", "group"),
    )
    moment_first, moment_second, master_new = adam_update(
        grads_local, first_moment, second_moment, master, learn_rate, weight_decay
    )
    gain_moment_first, gain_moment_second, gains_new = adam_update(
        gain_grads, gain_first, gain_second, gains, gain_rate, 0.0
    )
    return (
        outputs.astype(jnp.bfloat16),
        grad_inputs.astype(jnp.bfloat16),
        moment_first,
        moment_second,
        master_new,
        gain_moment_first,
        gain_moment_second,
        gains_new,
    )


def solution(mesh):
    placed = (
        P(("dp", "group"), None),
        P("dp", None),
        P(("dp", "group"), None),
        P(("dp", "group"), None),
        P(("dp", "group"), None),
        P(("dp", "group"), None),
        P(),
        P(),
        P(),
    )
    return jax.shard_map(
        shards,
        mesh=mesh,
        in_specs=placed,
        out_specs=(
            P(("dp", "group"), None),
            P(("dp", "group"), None),
            P(("dp", "group"), None),
            P(("dp", "group"), None),
            P(("dp", "group"), None),
            P(),
            P(),
            P(),
        ),
        check_vma=False,
    )
```

```python
import functools
import math

import jax
import jax.numpy as jnp
from jax import lax
from jax.experimental import pallas as pl
from jax.experimental.pallas import tpu as pltpu
from jax.sharding import PartitionSpec as P

D = 640
HQ = 4
HD = 256
FF = 2048
WINDOW = 512
STEP = 10
ALL_AXES = ("dp", "group")


norm_eps = 1e-06
rope_base = 10000.0
beta_first = 0.9
beta_second = 0.999
learn_rate = 0.05
gain_rate = 0.25
adam_floor = 1e-08
weight_decay = 0.1


def shifted(value, axis, steps):
    count = lax.axis_size(axis)
    initial, last = (max(0, -steps), min(count, count - steps))
    return lax.ppermute(value, axis, [(source, source + steps) for source in range(initial, last)])


def rms_norm(values, weight_vec):
    return (
        values
        * lax.rsqrt(jnp.mean(values * values, axis=-1, keepdims=True) + norm_eps)
        * (1.0 + weight_vec)
    )


def positions(doc_row):
    length = doc_row.shape[0]
    counter = jnp.arange(length, dtype=jnp.int32)
    starts_here = jnp.concatenate([jnp.ones((1,), jnp.bool_), doc_row[1:] != doc_row[:-1]])
    begins = lax.cummax(jnp.where(starts_here, counter, jnp.zeros_like(counter)), axis=0)
    return counter - begins


def angles_of(places):
    half_dim = HD // 2
    frequency = rope_base ** (-(jnp.arange(half_dim, dtype=jnp.float32) * 2.0 / HD))
    return places.astype(jnp.float32)[:, None] * frequency[None, :]


def rotate(values, angles):
    half_dim = values.shape[-1] // 2
    first_half = values[..., :half_dim]
    second_half = values[..., half_dim:]
    cosine = jnp.cos(angles)
    sine_part = jnp.sin(angles)
    return jnp.concatenate(
        [
            first_half * cosine - second_half * sine_part,
            second_half * cosine + first_half * sine_part,
        ],
        axis=-1,
    )


def geglu(gate_in, up_in):
    return jax.nn.gelu(gate_in, approximate=True) * up_in


def adam_update(gradient, first_old, second_old, params_old, rate, decay_rate):
    first_new = beta_first * first_old + (1.0 - beta_first) * gradient
    second_new = beta_second * second_old + (1.0 - beta_second) * gradient * gradient
    first_hat = first_new / (1.0 - beta_first**STEP)
    second_hat = second_new / (1.0 - beta_second**STEP)
    params_new = params_old - rate * (
        first_hat / (jnp.sqrt(second_hat) + adam_floor) + decay_rate * params_old
    )
    return (first_new, second_new, params_new)


def piece_rows(device_count):
    return [
        entries // (128 * device_count)
        for entries in (D * HQ * HD, D * HD, D * HD, HQ * HD * D, D * FF, D * FF, FF * D)
    ]


def piece_shapes():
    return [(D, HQ * HD), (D, HD), (D, HD), (HQ * HD, D), (D, FF), (D, FF), (FF, D)]


def split_rows(stacked, row_list):
    result = []
    row_start = 0
    for row_count in row_list:
        result.append(stacked[row_start : row_start + row_count])
        row_start = row_start + row_count
    return result


def matmul(left_side, right_side):
    return jnp.dot(left_side, right_side, preferred_element_type=jnp.float32)


LOW_COUNT = 8
LANES = 128
LOW_MASKS = (0, 4, 2, 6, 1, 5, 3, 7)
GELU_SCALE = (2.0 / math.pi) ** 0.5
GELU_CUBE = 0.044715
VMEM_BYTES = 56 * 1024 * 1024


def aligned(device_count):
    groups = lax.axis_size("group") == 4
    return groups and device_count % LOW_COUNT == 0 and D % device_count == 0


def swap(value, mask):
    count = lax.axis_size(ALL_AXES)
    return lax.ppermute(value, ALL_AXES, [(source, source ^ mask) for source in range(count)])


def local_call(kernel, outs, operands, scratch=(), behind=()):
    specs = [pl.BlockSpec(memory_space=pltpu.SMEM)]
    specs = specs + [pl.BlockSpec(memory_space=pltpu.VMEM)] * len(operands)
    specs = specs + [pl.BlockSpec(memory_space=pl.ANY)] * len(behind)
    first, last = 1 + len(operands), 1 + len(operands) + len(behind)

    def body(*refs):
        kernel(*refs[:first], *refs[last:])

    return pl.pallas_call(
        body,
        out_shape=outs,
        in_specs=specs,
        out_specs=tuple(pl.BlockSpec(memory_space=pltpu.VMEM) for _ in outs),
        scratch_shapes=scratch,
        compiler_params=pltpu.CompilerParams(vmem_limit_bytes=VMEM_BYTES),
        cost_estimate=pl.CostEstimate(flops=0, bytes_accessed=0, transcendentals=0),
    )(lax.axis_index(ALL_AXES).astype(jnp.int32).reshape(1), *operands, *behind)


class Piece:
    def __init__(self, rows, columns, device_count):
        self.rows = rows
        self.columns = columns
        self.wide = rows == D
        self.blocks = columns // LANES
        self.own_rows = rows // device_count
        self.flat_rows = self.own_rows * self.blocks
        self.high_count = device_count // LOW_COUNT
        self.block_rows = self.own_rows * self.high_count
        self.size = self.block_rows * self.blocks


def copy_kernel(index_ref, in_ref, out_ref):
    out_ref[...] = in_ref[...]


def pack_kernel(pieces, index_ref, *refs):
    high_count = pieces[0].high_count
    parts, out_refs, flat, packed = refs[:high_count], refs[high_count:-2], refs[-2], refs[-1]
    high = index_ref[0] // LOW_COUNT
    for step, part in enumerate(parts):
        flat[high ^ step] = part[...].astype(jnp.float32)
    start, target = 0, 0
    for piece in pieces:
        for block in range(piece.blocks):
            for place in range(high_count):
                packed[pl.ds(target, piece.own_rows), :] = flat[
                    place, pl.ds(start + block, piece.own_rows, stride=piece.blocks), :
                ]
                target = target + piece.own_rows
        start = start + piece.flat_rows
    count = target // len(out_refs)
    for place, out_ref in enumerate(out_refs):
        out_ref[...] = packed[place * count : (place + 1) * count, :].astype(jnp.bfloat16)


def sum_one_kernel(size, index_ref, near_ref, far_ref, to_x_ref, to_y_ref):
    total = near_ref[...].astype(jnp.float32) + far_ref[...].astype(jnp.float32)
    half = size // 2
    to_x_ref[:half, :] = total[:half].astype(jnp.bfloat16)
    if total.shape[0] > size:
        to_x_ref[half:, :] = total[size:].astype(jnp.bfloat16)
    to_y_ref[...] = total[half:size].astype(jnp.bfloat16)


def sum_three_kernel(
    size,
    index_ref,
    near_ref,
    far_ref,
    *refs,
):
    key_refs = refs[:-5]
    own_ref, beside_first_ref, beside_second_ref, across_first_ref, across_second_ref = refs[-5:]
    half = size // 2
    if key_refs:
        across_key_ref, cores_key_ref = key_refs
        rows = across_key_ref.shape[0]
        keys = across_key_ref[...] + cores_key_ref[rows:, :].astype(jnp.float32)
        for block in range(keys.shape[1] // LANES):
            first = half + block * rows
            columns = slice(block * LANES, (block + 1) * LANES)
            across_second_ref[first : first + rows, :] = keys[:, columns].astype(jnp.bfloat16)
    outs = (beside_first_ref, beside_second_ref, across_first_ref, across_second_ref)
    total = near_ref[:size, :].astype(jnp.float32) + far_ref[:size, :].astype(jnp.float32)
    own_ref[...] = total.astype(jnp.bfloat16)
    for place, out_ref in enumerate(outs):
        rows = slice(size + place * half, size + (place + 1) * half)
        total = near_ref[rows, :].astype(jnp.float32) + far_ref[rows, :].astype(jnp.float32)
        out_ref[:half, :] = total.astype(jnp.bfloat16)


def sum_all_kernel(size, index_ref, near_three, near_one, far_three, far_one, *out_refs):
    sum_one_kernel(size, index_ref, near_one, far_one, *out_refs[:2])
    sum_three_kernel(size, index_ref, near_three, far_three, *out_refs[2:])


def sum_passed_kernel(
    size,
    index_ref,
    beside_ref,
    across_ref,
    over_x_ref,
    over_y_ref,
    near_one_ref,
    far_one_ref,
    beside_out_ref,
    across_out_ref,
    extra_ref,
):
    half = size // 2
    beside = beside_ref[...].astype(jnp.float32) + over_y_ref[...].astype(jnp.float32)
    beside_out_ref[...] = beside.astype(jnp.bfloat16)
    across = across_ref[...].astype(jnp.float32) + over_x_ref[:half, :].astype(jnp.float32)
    across_out_ref[:half, :] = across.astype(jnp.bfloat16)
    if across_out_ref.shape[0] > half:
        extra = near_one_ref[size:, :].astype(jnp.float32)
        extra = extra + far_one_ref[size:, :].astype(jnp.float32)
        extra = extra + over_x_ref[half:, :].astype(jnp.float32)
        extra_ref[...] = extra
        across_out_ref[half:, :] = extra.astype(jnp.bfloat16)
    else:
        extra_ref[...] = jnp.zeros(extra_ref.shape, jnp.float32)


def unpack_kernel(
    pieces,
    index_ref,
    own_ref,
    beside_first_ref,
    beside_second_ref,
    across_first_ref,
    across_second_ref,
    extra_ref,
    *refs,
):
    high_count = pieces[0].high_count
    half = sum(piece.size for piece in pieces) // 2
    flat_rows = sum(piece.flat_rows for piece in pieces)
    outs, flat, packed = refs[:-2], refs[-2], refs[-1]
    high = index_ref[0] // LOW_COUNT
    packed[:half, :] = (
        own_ref[:half, :].astype(jnp.float32)
        + beside_first_ref[...].astype(jnp.float32)
        + across_first_ref[:half, :].astype(jnp.float32)
    )
    packed[half:, :] = (
        own_ref[half:, :].astype(jnp.float32)
        + beside_second_ref[...].astype(jnp.float32)
        + across_second_ref[:half, :].astype(jnp.float32)
    )
    start, source = 0, 0
    for piece in pieces:
        for block in range(piece.blocks):
            for place in range(high_count):
                flat[place, pl.ds(start + block, piece.own_rows, stride=piece.blocks), :] = packed[
                    pl.ds(source, piece.own_rows), :
                ]
                source = source + piece.own_rows
        start = start + piece.flat_rows
    for step, out_ref in enumerate(outs):
        out_ref[:flat_rows, :] = flat[high ^ step].astype(out_ref.dtype)
        if out_ref.shape[0] > flat_rows:
            extra = extra_ref[...] + across_first_ref[half:, :].astype(jnp.float32)
            out_ref[flat_rows:, :] = extra.astype(out_ref.dtype)


def array(shape, kind):
    return jax.ShapeDtypeStruct(shape, kind)


def gather_high(rows):
    high_count = lax.axis_size(ALL_AXES) // LOW_COUNT
    return [rows] + [swap(rows, step * LOW_COUNT) for step in range(1, high_count)]


def gather_own(pieces, parts, count, behind=()):
    high_count = pieces[0].high_count
    size = sum(piece.size for piece in pieces)
    return local_call(
        functools.partial(pack_kernel, pieces),
        (array((size // count, LANES), jnp.bfloat16),) * count,
        parts,
        (
            pltpu.VMEM((high_count, parts[0].shape[0], LANES), jnp.float32),
            pltpu.VMEM((size, LANES), jnp.float32),
        ),
        behind,
    )


def copied(value, behind):
    return local_call(copy_kernel, (array(value.shape, jnp.bfloat16),), (value,), (), behind)[0]


def held(values, behind):
    count = len(values)
    return pl.pallas_call(
        lambda *refs: None,
        out_shape=tuple(array(value.shape, value.dtype) for value in values),
        in_specs=[pl.BlockSpec(memory_space=pl.ANY)] * (count + len(behind)),
        out_specs=tuple(pl.BlockSpec(memory_space=pl.ANY) for _ in values),
        input_output_aliases={place: place for place in range(count)},
        cost_estimate=pl.CostEstimate(flops=0, bytes_accessed=0, transcendentals=0),
    )(*values, *behind)


def gather_halves(first, second):
    return swap(second, 4), swap(first, 2)


def gather_rest(first, second, beside_second, across_first, keys, behind):
    beside_first, across_second = swap(copied(first, keys[:1]), 4), swap(second, 2)
    over_x = swap(across_first, 4)
    over_y = swap(copied(beside_second, (*keys[1:], across_second)), 2)
    diagonal = held((over_x, over_y), behind)
    return first, second, beside_first, beside_second, across_first, across_second, *diagonal


def gather_wholes(own):
    return own, swap(own, 4), swap(own, 2), swap(own, 6)


def gather_cores(near):
    return near + tuple(swap(value, 1) for value in near)


def scatter_cores(far_three, far_one):
    far_one = swap(far_one, 1)
    return swap(far_three, 1), far_one


def scatter_one(pieces, near_one, far_one, behind=()):
    half = sum(piece.size for piece in pieces) // 2
    to_x, to_y = local_call(
        functools.partial(sum_one_kernel, 2 * half),
        (
            array((near_one.shape[0] - half, LANES), jnp.bfloat16),
            array((half, LANES), jnp.bfloat16),
        ),
        (near_one, far_one),
        (),
        behind,
    )
    return swap(to_x, 4), swap(to_y, 2), to_y


def scatter_three(pieces, near_three, far_three, behind=(), keys=()):
    size = sum(piece.size for piece in pieces)
    half = size // 2
    own, beside_first, beside_second, across_first, across_second = local_call(
        functools.partial(sum_three_kernel, size),
        (
            array((size, LANES), jnp.bfloat16),
            *(array((half, LANES), jnp.bfloat16),) * 3,
            array((half + (keys[0].size // LANES if keys else 0), LANES), jnp.bfloat16),
        ),
        (near_three, far_three, *keys),
        (),
        behind,
    )
    return own, swap(beside_first, 4), beside_second, across_first, swap(across_second, 2)


def scatter_all(pieces, near_three, near_one, far_three, far_one, behind=()):
    size = sum(piece.size for piece in pieces)
    half = size // 2
    to_x, to_y, own, beside_first, beside_second, across_first, across_second = local_call(
        functools.partial(sum_all_kernel, size),
        (
            array((near_one.shape[0] - half, LANES), jnp.bfloat16),
            array((half, LANES), jnp.bfloat16),
            array((size, LANES), jnp.bfloat16),
            *(array((half, LANES), jnp.bfloat16),) * 4,
        ),
        (near_three, near_one, far_three, far_one),
        (),
        behind,
    )
    over_x, over_y = swap(to_x, 4), swap(to_y, 2)
    return (
        over_x,
        over_y,
        (own, swap(beside_first, 4), beside_second, across_first, swap(across_second, 2)),
    )


def scatter_passed(pieces, threes, over_x, over_y, near_one, far_one, behind=()):
    size = sum(piece.size for piece in pieces)
    extra_count = near_one.shape[0] - size
    own, beside_first, beside_second, across_first, across_second = threes
    beside_second, across_first, extra = local_call(
        functools.partial(sum_passed_kernel, size),
        (
            array((size // 2, LANES), jnp.bfloat16),
            array((size // 2 + extra_count, LANES), jnp.bfloat16),
            array((max(extra_count, 8), LANES), jnp.float32),
        ),
        (beside_second, across_first, over_x, over_y, near_one, far_one),
        (),
        behind,
    )
    terms = (
        own,
        beside_first,
        swap(beside_second, 4),
        swap(across_first, 2),
        across_second,
        extra,
    )
    return terms, beside_second


def scatter_high(pieces, terms, behind=()):
    high_count = pieces[0].high_count
    size = sum(piece.size for piece in pieces)
    flat_rows = sum(piece.flat_rows for piece in pieces)
    out_rows = flat_rows + terms[3].shape[0] - size // 2
    outs = local_call(
        functools.partial(unpack_kernel, pieces),
        (array((out_rows, LANES), jnp.float32),)
        + (array((out_rows, LANES), jnp.bfloat16),) * (high_count - 1),
        terms,
        (
            pltpu.VMEM((high_count, flat_rows, LANES), jnp.float32),
            pltpu.VMEM((size, LANES), jnp.float32),
        ),
        behind,
    )
    arrived = [swap(send, step * LOW_COUNT) for step, send in enumerate(outs) if step]
    return outs[0] + sum(value.astype(jnp.float32) for value in arrived), outs[0], arrived


def norm_parts(values):
    scale = lax.rsqrt(jnp.mean(values * values, axis=-1, keepdims=True) + norm_eps)
    return scale, values * scale


def norm_back(scale, normal, upstream, weight_vec):
    weighted = upstream * (1.0 + weight_vec)
    inner = jnp.mean(weighted * normal, axis=-1, keepdims=True)
    return scale * (weighted - normal * inner), jnp.sum(normal * upstream, axis=0, keepdims=True)


def product(left_side, right_side, left_axis, right_axis):
    return lax.dot_general(
        left_side,
        right_side,
        (((left_axis,), (right_axis,)), ((), ())),
        preferred_element_type=jnp.float32,
    )


def turned_over(rows_low):
    return rows_low.astype(jnp.float32).T.astype(jnp.bfloat16)


def unordered(rows_in, order_low):
    upper = rows_in.astype(jnp.bfloat16)
    lower = (rows_in - upper.astype(jnp.float32)).astype(jnp.bfloat16)
    return product(upper, order_low, 1, 1) + product(lower, order_low, 1, 1)


def weight_rows(refs, size, order, start, rows):
    count = len(refs) // LOW_COUNT
    part = size // count
    return refs[order * count + start // part][start % part : start % part + rows, :]


def put_rows(refs, size, order, start, rows):
    three, one = refs[:2] if order < 4 else refs[2:]
    if order % 4 == 3:
        one[start : start + rows.shape[0], :] = rows
    else:
        start = order % 4 * size + start
        three[start : start + rows.shape[0], :] = rows


def wide_tile(refs, size, start, rows):
    return jnp.concatenate(
        [weight_rows(refs, size, order, start, rows) for order in range(LOW_COUNT)]
    )


def put_wide_tile(refs, size, start, rows, tile):
    for order in range(LOW_COUNT):
        put_rows(refs, size, order, start, tile[order * rows : (order + 1) * rows])


def tall_rows(piece, low):
    for order, mask in enumerate(LOW_MASKS):
        for block in range(piece.blocks):
            for place in range(piece.high_count):
                row = (place * LOW_COUNT + (low ^ mask)) * piece.own_rows
                yield (
                    order,
                    block * piece.block_rows + place * piece.own_rows,
                    pl.ds(pl.multiple_of(row, piece.own_rows), piece.own_rows),
                    slice(block * LANES, (block + 1) * LANES),
                )


def ffn_kernel(
    gate_piece,
    down_piece,
    index_ref,
    middle_ref,
    cotangent_ref,
    gain_in_ref,
    gain_out_ref,
    order_ref,
    *refs,
):
    weight_refs, grad_refs = refs[:16], refs[20:24]
    block_out_ref, grad_middle_ref, grad_gain_in_ref, grad_gain_out_ref = refs[16:20]
    down_ref, hidden_ref, gelu_ref, slope_ref = refs[24:]
    low = index_ref[0] % LOW_COUNT
    rows = gate_piece.block_rows
    size = 2 * gate_piece.size + down_piece.size
    width = 2 * LANES
    for order, start, matrix_rows, columns in tall_rows(down_piece, low):
        start = start + 2 * gate_piece.size
        down_ref[matrix_rows, columns] = weight_rows(
            weight_refs, size, order, start, down_piece.own_rows
        )

    def wide_tiles(step):
        return [
            jnp.concatenate(
                [
                    wide_tile(weight_refs, size, offset + block * rows, rows)
                    for block in (2 * step, 2 * step + 1)
                ],
                axis=1,
            )
            for offset in (0, gate_piece.size)
        ]

    middle = middle_ref[...]
    scale_in, normal_in = norm_parts(middle)
    order_low = order_ref[...]
    normed = (normal_in * (1.0 + gain_in_ref[...])).astype(jnp.bfloat16)
    normed = product(normed, order_low, 1, 0).astype(jnp.bfloat16)
    normed_turned = turned_over(normed)
    for step in range(FF // width):
        columns = slice(step * width, (step + 1) * width)
        gate_weight, up_weight = wide_tiles(step)
        gate = product(normed, gate_weight, 1, 0)
        up = product(normed, up_weight, 1, 0)
        square = gate * gate
        bend = jnp.tanh(GELU_SCALE * gate * (1.0 + GELU_CUBE * square))
        half = 0.5 * (1.0 + bend)
        gelu = gate * half
        slope = half + 0.5 * gate * (1.0 - bend * bend) * GELU_SCALE * (
            1.0 + 3.0 * GELU_CUBE * square
        )
        gelu_ref[:, columns] = gelu
        slope_ref[:, columns] = slope * up
        hidden_ref[:, columns] = (gelu * up).astype(jnp.bfloat16)
    hidden = hidden_ref[...]
    scale_out, normal_out = norm_parts(product(hidden, down_ref[...], 1, 0))
    block_out_ref[...] = (middle + normal_out * (1.0 + gain_out_ref[...])).astype(jnp.bfloat16)
    upstream = cotangent_ref[...].astype(jnp.float32)
    grad_ffn, grad_gain_out_ref[...] = norm_back(
        scale_out, normal_out, upstream, gain_out_ref[...]
    )
    grad_ffn = grad_ffn.astype(jnp.bfloat16)
    grad_normed = jnp.zeros(middle.shape, jnp.float32)
    for step in range(FF // width):
        columns = slice(step * width, (step + 1) * width)
        grad_hidden = product(grad_ffn, down_ref[columns, :], 1, 1)
        down_ref[columns, :] = product(hidden_ref[:, columns], grad_ffn, 0, 0).astype(jnp.bfloat16)
        grads = [
            (grad_hidden * slope_ref[:, columns]).astype(jnp.bfloat16),
            (grad_hidden * gelu_ref[:, columns]).astype(jnp.bfloat16),
        ]
        for place, (grad, weight) in enumerate(zip(grads, wide_tiles(step))):
            grad_weight = product(normed_turned, grad, 1, 0).astype(jnp.bfloat16)
            for side in range(2):
                put_wide_tile(
                    grad_refs,
                    size,
                    place * gate_piece.size + (2 * step + side) * rows,
                    rows,
                    grad_weight[:, side * LANES : (side + 1) * LANES],
                )
            grad_normed = grad_normed + product(grad, weight, 1, 1)
    for order, start, matrix_rows, columns in tall_rows(down_piece, low):
        start = start + 2 * gate_piece.size
        put_rows(grad_refs, size, order, start, down_ref[matrix_rows, columns])
    grad_middle, grad_gain_in_ref[...] = norm_back(
        scale_in, normal_in, unordered(grad_normed, order_low), gain_in_ref[...]
    )
    grad_middle_ref[...] = upstream + grad_middle


def grad_arrays(pieces, extra_count=0):
    size = sum(piece.size for piece in pieces)
    return (
        array((3 * size, LANES), jnp.bfloat16),
        array((size + extra_count, LANES), jnp.bfloat16),
    ) * 2


def ffn_blocks(pieces, middle, cotangent, gain_in, gain_out, order, blocks):
    rows = middle.shape[0]
    outs = local_call(
        functools.partial(ffn_kernel, pieces[4], pieces[6]),
        (
            array((rows, D), jnp.bfloat16),
            array((rows, D), jnp.float32),
            array((1, D), jnp.float32),
            array((1, D), jnp.float32),
            *grad_arrays(pieces[4:7]),
        ),
        (middle, cotangent, gain_in, gain_out, order, *blocks),
        (
            pltpu.VMEM((FF, D), jnp.bfloat16),
            pltpu.VMEM((rows, FF), jnp.bfloat16),
            pltpu.VMEM((rows, FF), jnp.float32),
            pltpu.VMEM((rows, FF), jnp.float32),
        ),
    )
    return *outs[:4], outs[4:]


def turn(values, cosine, sine):
    first_half, second_half = values[:, : HD // 2], values[:, HD // 2 :]
    return jnp.concatenate(
        [first_half * cosine - second_half * sine, second_half * cosine + first_half * sine], axis=1
    )


def wide_head(refs, size, start, rows):
    return jnp.concatenate(
        [wide_tile(refs, size, start + side * rows, rows) for side in range(2)], axis=1
    )


def head_starts(pieces):
    rows = pieces[0].block_rows
    return [2 * rows * head for head in range(HQ + 2)]


def project_kernel(
    pieces,
    index_ref,
    tokens_ref,
    gain_ref,
    gain_query_ref,
    gain_key_ref,
    cosine_ref,
    sine_ref,
    order_ref,
    *refs,
):
    weight_refs = refs[:8]
    normed_ref, query_proj_ref, key_proj_ref, query_ref, key_value_ref = refs[8:]
    size = sum(piece.size for piece in pieces)
    rows = pieces[0].block_rows
    cosine, sine = cosine_ref[...], sine_ref[...]
    _, normal = norm_parts(tokens_ref[...].astype(jnp.float32))
    normed = (normal * (1.0 + gain_ref[...])).astype(jnp.bfloat16)
    normed = product(normed, order_ref[...], 1, 0).astype(jnp.bfloat16)
    normed_ref[...] = normed
    starts = head_starts(pieces)
    for head, start in enumerate(starts):
        proj = product(normed, wide_head(weight_refs, size, start, rows), 1, 0)
        columns = slice(head * HD, (head + 1) * HD)
        if head == HQ + 1:
            key_value_ref[:, HD:] = proj.astype(jnp.bfloat16)
            continue
        gain_vec = gain_query_ref[...] if head < HQ else gain_key_ref[...]
        _, normal = norm_parts(proj)
        turned = turn(normal * (1.0 + gain_vec), cosine, sine).astype(jnp.bfloat16)
        if head < HQ:
            query_proj_ref[:, columns] = proj
            query_ref[:, columns] = turned
        else:
            key_proj_ref[...] = proj
            key_value_ref[:, :HD] = turned


def attend_kernel(
    pieces,
    index_ref,
    tokens_ref,
    gain_ref,
    allowed_ref,
    query_ref,
    *refs,
):
    weight_refs, key_value_refs = refs[:8], refs[8:-5]
    probs_ref, attended_ref, attn_out_ref, middle_ref, out_weight_ref = refs[-5:]
    out_piece = pieces[-1]
    low = index_ref[0] % LOW_COUNT
    size = sum(piece.size for piece in pieces)
    out_start = size - out_piece.size
    for order, start, matrix_rows, columns in tall_rows(out_piece, low):
        out_weight_ref[matrix_rows, columns] = weight_rows(
            weight_refs, size, order, start + out_start, out_piece.own_rows
        )
    rows = tokens_ref.shape[0]
    allowed = allowed_ref[...] > 0.0
    keys = jnp.concatenate([ref[:, :HD] for ref in key_value_refs])
    values = jnp.concatenate([ref[:, HD:] for ref in key_value_refs])
    count = keys.shape[0]
    for head in range(HQ):
        columns = slice(head * HD, (head + 1) * HD)
        scores = product(query_ref[:, columns], keys, 1, 1) * HD ** (-0.5)
        scores = jnp.where(allowed, scores, -1e30)
        raised = jnp.exp(scores - jnp.max(scores, axis=-1, keepdims=True))
        probs = raised / jnp.sum(raised, axis=-1, keepdims=True)
        probs_ref[:, head * count : (head + 1) * count] = probs
        attended_ref[:, columns] = product(probs.astype(jnp.bfloat16), values, 1, 0).astype(
            jnp.bfloat16
        )
    attn_out = product(attended_ref[...], out_weight_ref[...], 1, 0)
    attn_out_ref[...] = attn_out
    _, normal = norm_parts(attn_out)
    middle_ref[...] = tokens_ref[...].astype(jnp.float32) + normal * (1.0 + gain_ref[...])


def attend_back_kernel(
    index_ref,
    grad_middle_ref,
    attn_out_ref,
    gain_ref,
    out_weight_ref,
    attended_ref,
    probs_ref,
    query_ref,
    *refs,
):
    key_value_refs = refs[:4]
    grad_out_weight_ref, grad_query_ref, grad_gain_ref = refs[4:7]
    grad_own_ref, grad_across_ref, grad_cores_ref = refs[7:]
    rows = query_ref.shape[0]
    scale, normal = norm_parts(attn_out_ref[...])
    grad_attn, grad_gain_ref[...] = norm_back(scale, normal, grad_middle_ref[...], gain_ref[...])
    grad_attn = grad_attn.astype(jnp.bfloat16)
    grad_out_weight_ref[...] = product(attended_ref[...], grad_attn, 0, 0).astype(jnp.bfloat16)
    keys = jnp.concatenate([ref[:, :HD] for ref in key_value_refs])
    values = jnp.concatenate([ref[:, HD:] for ref in key_value_refs])
    count = keys.shape[0]
    grad_keys = jnp.zeros((count, HD), jnp.float32)
    grad_values = jnp.zeros((count, HD), jnp.float32)
    for head in range(HQ):
        columns = slice(head * HD, (head + 1) * HD)
        grad_attended = product(grad_attn, out_weight_ref[columns, :], 1, 1).astype(jnp.bfloat16)
        probs = probs_ref[:, head * count : (head + 1) * count]
        grad_probs = product(grad_attended, values, 1, 1)
        grad_values = grad_values + product(probs.astype(jnp.bfloat16), grad_attended, 0, 0)
        inner = jnp.sum(probs * grad_probs, axis=-1, keepdims=True)
        grad_scores = (probs * (grad_probs - inner) * HD ** (-0.5)).astype(jnp.bfloat16)
        grad_query_ref[:, columns] = product(grad_scores, keys, 1, 0)
        grad_keys = grad_keys + product(grad_scores, query_ref[:, columns], 0, 0)
    targets = (
        grad_own_ref,
        grad_cores_ref.at[:rows],
        grad_across_ref,
        grad_cores_ref.at[rows:],
    )
    for part, ref in enumerate(targets):
        ref[:, :HD] = grad_keys[part * rows : (part + 1) * rows].astype(ref.dtype)
        ref[:, HD:] = grad_values[part * rows : (part + 1) * rows].astype(ref.dtype)


def query_back_kernel(
    pieces,
    index_ref,
    gain_ref,
    cosine_ref,
    sine_ref,
    normed_ref,
    query_proj_ref,
    grad_query_ref,
    *refs,
):
    weight_refs = refs[:8]
    grad_weight_ref, grad_normed_ref, grad_gain_ref = refs[8:]
    size = sum(piece.size for piece in pieces)
    rows = pieces[0].block_rows
    cosine, sine = cosine_ref[...], sine_ref[...]
    normed_turned = turned_over(normed_ref[...])
    grad_normed = jnp.zeros(grad_normed_ref.shape, jnp.float32)
    grad_gain = jnp.zeros((1, HD), jnp.float32)
    for head, start in enumerate(head_starts(pieces)[:HQ]):
        columns = slice(head * HD, (head + 1) * HD)
        scale, normal = norm_parts(query_proj_ref[:, columns])
        upstream = turn(grad_query_ref[:, columns], cosine, -sine)
        grad, gain_row = norm_back(scale, normal, upstream, gain_ref[...])
        grad_gain = grad_gain + gain_row
        grad = grad.astype(jnp.bfloat16)
        weight = wide_head(weight_refs, size, start, rows)
        grad_normed = grad_normed + product(grad, weight, 1, 1)
        grad_weight_ref[:, columns] = product(normed_turned, grad, 1, 0).astype(jnp.bfloat16)
    grad_normed_ref[...] = grad_normed
    grad_gain_ref[...] = grad_gain


def project_back_kernel(
    pieces,
    index_ref,
    tokens_ref,
    gain_ref,
    gain_key_ref,
    cosine_ref,
    sine_ref,
    order_ref,
    normed_ref,
    key_proj_ref,
    grad_normed_ref,
    grad_middle_ref,
    gain_attn_ref,
    gain_ffin_ref,
    gain_ffout_ref,
    gain_query_ref,
    own_key_ref,
    cores_key_ref,
    across_key_ref,
    *refs,
):
    weight_refs = refs[:8]
    grad_weight_ref, input_grad_ref, grad_gain_ref = refs[8:]
    size = sum(piece.size for piece in pieces)
    rows = pieces[0].block_rows
    normed = normed_ref[...]
    key_rows = own_key_ref.shape[0]
    first = across_key_ref.shape[0] - 4 * key_rows
    key_value = own_key_ref[...] + cores_key_ref[:key_rows, :].astype(jnp.float32)
    key_value = key_value + jnp.concatenate(
        [
            across_key_ref[first + block * key_rows : first + (block + 1) * key_rows, :].astype(
                jnp.float32
            )
            for block in range(4)
        ],
        axis=1,
    )
    scale, normal = norm_parts(key_proj_ref[...])
    upstream = turn(key_value[:, :HD], cosine_ref[...], -sine_ref[...])
    grad_key, grad_gain_key = norm_back(scale, normal, upstream, gain_key_ref[...])
    grad_normed = grad_normed_ref[...]
    for place, start in enumerate(head_starts(pieces)[HQ:]):
        grad = (key_value[:, HD:] if place else grad_key).astype(jnp.bfloat16)
        weight = wide_head(weight_refs, size, start, rows)
        grad_normed = grad_normed + product(grad, weight, 1, 1)
        grad_weight_ref[:, place * HD : (place + 1) * HD] = product(normed, grad, 0, 0).astype(
            jnp.bfloat16
        )
    scale, normal = norm_parts(tokens_ref[...].astype(jnp.float32))
    grad_inputs, grad_gain_input = norm_back(
        scale, normal, unordered(grad_normed, order_ref[...]), gain_ref[...]
    )
    input_grad_ref[...] = (grad_middle_ref[...] + grad_inputs).astype(jnp.bfloat16)
    grad_gains = [
        grad_gain_input,
        gain_attn_ref[...],
        gain_ffin_ref[...],
        gain_ffout_ref[...],
        gain_query_ref[...],
        grad_gain_key,
    ]
    row = 0
    grad_gain_ref[...] = jnp.zeros(grad_gain_ref.shape, jnp.float32)
    for values in grad_gains:
        for start in range(0, values.shape[1], LANES):
            grad_gain_ref[row : row + 1, :] = values[:, start : start + LANES]
            row = row + 1


def split_kernel(
    pieces,
    index_ref,
    query_ref,
    key_value_ref,
    out_ref,
    gain_ref,
    *grad_refs,
):
    low = index_ref[0] % LOW_COUNT
    size = sum(piece.size for piece in pieces)
    rows = pieces[0].block_rows
    start = 0
    for matrix_ref in (query_ref, key_value_ref):
        for column in range(0, matrix_ref.shape[1], LANES):
            tile = matrix_ref[:, column : column + LANES]
            put_wide_tile(grad_refs, size, start, rows, tile)
            start = start + rows
    out_piece = pieces[-1]
    for order, first, matrix_rows, columns in tall_rows(out_piece, low):
        put_rows(grad_refs, size, order, start + first, out_ref[matrix_rows, columns])
    for target in (grad_refs[1], grad_refs[3]):
        target[size:, :] = gain_ref[...].astype(jnp.bfloat16)


def width_order(device_count):
    low = lax.axis_index(ALL_AXES) % LOW_COUNT
    rows = D // device_count
    high_count = device_count // LOW_COUNT
    column = jnp.arange(D, dtype=jnp.int32)
    place = column // (rows * high_count)
    mask = (place & 1) * 4 + ((place >> 1) & 1) * 2 + (place >> 2)
    high = (column // rows) % high_count
    picked = (high * LOW_COUNT + (low ^ mask)) * rows + column % rows
    return (jnp.arange(D, dtype=jnp.int32)[:, None] == picked[None, :]).astype(jnp.bfloat16)


GAIN_ROWS = 32


def shards_blocks(
    device_count,
    tokens,
    doc_ids,
    cotangent,
    master,
    first_moment,
    second_moment,
    gains,
    gain_first,
    gain_second,
):
    pieces = [Piece(*shape_pair, device_count) for shape_pair in piece_shapes()]
    attention_pieces = pieces[:4]
    local_rows = tokens.shape[0]
    group_size = lax.axis_size("group")
    first_row = lax.axis_index("group") * local_rows
    attention_rows = sum(piece.flat_rows for piece in attention_pieces)
    ffn_pieces = pieces[4:7]
    rounded = master.astype(jnp.bfloat16)
    attention_parts = gather_high(rounded[:attention_rows])
    ffn_rows = rounded[attention_rows:]
    ffn_parts = gather_high(ffn_rows)
    attention_near = gather_wholes(
        *gather_own(attention_pieces, attention_parts, 1, (ffn_parts[1],))
    )
    attention_near = tuple(held(attention_near, ffn_parts[2:]))
    attention_blocks = gather_cores(attention_near)
    ffn_own = gather_own(ffn_pieces, ffn_parts, 2, attention_near[1:])
    ffn_passed = gather_halves(*ffn_own)
    gain_parts = []
    for start, width in ((0, D), (D, D), (2 * D, D), (3 * D, D), (4 * D, HD), (4 * D + HD, HD)):
        gain_parts.append(gains[start : start + width][None])
    gain_input, gain_attn, gain_ffin, gain_ffout, gain_query, gain_key = gain_parts
    order = width_order(device_count)
    doc_row = doc_ids[0]
    angles = lax.dynamic_slice_in_dim(angles_of(positions(doc_row)), first_row, local_rows, 0)
    cosine, sine = jnp.cos(angles), jnp.sin(angles)
    query_docs = lax.dynamic_slice_in_dim(doc_row, first_row, local_rows, 0)
    key_count = group_size * local_rows
    first_keys = [(lax.axis_index("group") ^ step) * local_rows for step in range(group_size)]
    key_docs = jnp.concatenate(
        [lax.dynamic_slice_in_dim(doc_row, start, local_rows, 0) for start in first_keys]
    )
    key_index = jnp.concatenate(
        [start + jnp.arange(local_rows, dtype=jnp.int32) for start in first_keys]
    )
    query_index = first_row + jnp.arange(local_rows, dtype=jnp.int32)
    distance = query_index[:, None] - key_index[None, :]
    allowed = (distance >= 0) & (distance < WINDOW) & (key_docs[None, :] == query_docs[:, None])
    allowed = allowed.astype(jnp.float32)

    width = HQ * HD
    normed, query_proj, key_proj, query_rot, key_value = local_call(
        functools.partial(project_kernel, attention_pieces),
        (
            array((local_rows, D), jnp.bfloat16),
            array((local_rows, width), jnp.float32),
            array((local_rows, HD), jnp.float32),
            array((local_rows, width), jnp.bfloat16),
            array((local_rows, 2 * HD), jnp.bfloat16),
        ),
        (tokens, gain_input, gain_query, gain_key, cosine, sine, order, *attention_blocks),
    )
    key_values = [key_value] + [swap(key_value, step) for step in range(1, group_size)]
    probs, attended, attn_out, middle, out_weight = local_call(
        functools.partial(attend_kernel, attention_pieces),
        (
            array((local_rows, HQ * key_count), jnp.float32),
            array((local_rows, width), jnp.bfloat16),
            array((local_rows, D), jnp.float32),
            array((local_rows, D), jnp.float32),
            array((width, D), jnp.bfloat16),
        ),
        (tokens, gain_attn, allowed, query_rot, *attention_blocks, *key_values),
    )
    ffn_weights = gather_cores(gather_rest(*ffn_own, *ffn_passed, key_values, (middle,)))
    outputs, grad_middle, grad_gain_ffin, grad_gain_ffout, grads_ffn = ffn_blocks(
        pieces, middle, cotangent, gain_ffin, gain_ffout, order, ffn_weights
    )
    near_three, near_one, far_three, far_one = grads_ffn
    far_three, far_one = scatter_cores(far_three, far_one)
    grad_out_weight, grad_query, grad_gain_attn, own_key, across_key, cores_key = local_call(
        attend_back_kernel,
        (
            array((width, D), jnp.bfloat16),
            array((local_rows, width), jnp.float32),
            array((1, D), jnp.float32),
            array((local_rows, 2 * HD), jnp.float32),
            array((local_rows, 2 * HD), jnp.float32),
            array((2 * local_rows, 2 * HD), jnp.bfloat16),
        ),
        (
            grad_middle,
            attn_out,
            gain_attn,
            out_weight,
            attended,
            probs,
            query_rot,
            *key_values,
        ),
    )
    cores_key = swap(cores_key, 1)
    over_x, over_y, sent = scatter_one(ffn_pieces, near_one, far_one, (grad_query,))
    threes = scatter_three(ffn_pieces, near_three, far_three, (sent,), (across_key, cores_key))
    grad_query_weight, grad_normed, grad_gain_query = local_call(
        functools.partial(query_back_kernel, attention_pieces),
        (
            array((D, width), jnp.bfloat16),
            array((local_rows, D), jnp.float32),
            array((1, HD), jnp.float32),
        ),
        (gain_query, cosine, sine, normed, query_proj, grad_query, *attention_blocks),
        (),
        (threes[0],),
    )
    ffn_terms, sent = scatter_passed(
        ffn_pieces, threes, over_x, over_y, near_one, far_one, (grad_normed,)
    )
    grad_key_weight, grad_inputs, grad_gains = local_call(
        functools.partial(project_back_kernel, attention_pieces),
        (
            array((D, 2 * HD), jnp.bfloat16),
            array((local_rows, D), jnp.bfloat16),
            array((GAIN_ROWS, LANES), jnp.float32),
        ),
        (
            tokens,
            gain_input,
            gain_key,
            cosine,
            sine,
            order,
            normed,
            key_proj,
            grad_normed,
            grad_middle,
            grad_gain_attn,
            grad_gain_ffin,
            grad_gain_ffout,
            grad_gain_query,
            own_key,
            cores_key,
            threes[4],
            *attention_blocks,
        ),
        (),
        (sent, threes[1]),
    )
    near_three, near_one, far_three, far_one = local_call(
        functools.partial(split_kernel, attention_pieces),
        grad_arrays(attention_pieces, GAIN_ROWS),
        (grad_query_weight, grad_key_weight, grad_out_weight, grad_gains),
    )
    far_three, far_one = held((far_three, far_one), ffn_terms[2:4])
    grads_ffn, sent, arrived = scatter_high(ffn_pieces, ffn_terms, (near_one,))
    far_three, far_one = scatter_cores(far_three, far_one)
    over_x, over_y, threes = scatter_all(
        attention_pieces, near_three, near_one, far_three, far_one, (sent,)
    )
    terms, _ = scatter_passed(
        attention_pieces, threes, over_x, over_y, near_one, far_one, (arrived[0],)
    )
    grads_attention, _, _ = scatter_high(attention_pieces, terms, arrived)
    gain_grads = grads_attention[attention_rows:].reshape(-1)[: gains.shape[0]]
    grads_local = jnp.concatenate([grads_attention[:attention_rows], grads_ffn])
    return (
        outputs,
        grad_inputs,
        *adam_update(grads_local, first_moment, second_moment, master, learn_rate, weight_decay),
        *adam_update(gain_grads, gain_first, gain_second, gains, gain_rate, 0.0),
    )


def shards(
    tokens, doc_ids, cotangent, master, first_moment, second_moment, gains, gain_first, gain_second
):
    group_size = lax.axis_size("group")
    devices_all = lax.axis_size("dp") * group_size
    if aligned(devices_all):
        return shards_blocks(
            devices_all,
            tokens,
            doc_ids,
            cotangent,
            master,
            first_moment,
            second_moment,
            gains,
            gain_first,
            gain_second,
        )
    group_index = lax.axis_index("group")
    local_rows = tokens.shape[0]
    shard_parts = [
        part_rows.astype(jnp.bfloat16) for part_rows in split_rows(master, piece_rows(devices_all))
    ]
    gathered = (
        lax.all_gather(shard_parts[0], ("dp", "group"), axis=0, tiled=True),
        lax.all_gather(shard_parts[1], ("dp", "group"), axis=0, tiled=True),
        lax.all_gather(shard_parts[2], ("dp", "group"), axis=0, tiled=True),
        lax.all_gather(shard_parts[3], ("dp", "group"), axis=0, tiled=True),
        lax.all_gather(shard_parts[4], ("dp", "group"), axis=0, tiled=True),
        lax.all_gather(shard_parts[5], ("dp", "group"), axis=0, tiled=True),
        lax.all_gather(shard_parts[6], ("dp", "group"), axis=0, tiled=True),
    )
    query_weight, key_weight, value_weight, out_weight, gate_weight, up_weight, down_weight = [
        full_rows.reshape(shape_pair) for full_rows, shape_pair in zip(gathered, piece_shapes())
    ]
    norm_input = gains[0:D]
    norm_attn = gains[D : 2 * D]
    norm_ffin = gains[2 * D : 3 * D]
    norm_ffout = gains[3 * D : 4 * D]
    norm_query = gains[4 * D : 4 * D + HD]
    norm_key = gains[4 * D + HD : 4 * D + 2 * HD]
    doc_row = doc_ids[0]
    first_row = group_index * local_rows
    angles = lax.dynamic_slice_in_dim(angles_of(positions(doc_row)), first_row, local_rows, 0)
    query_docs = lax.dynamic_slice_in_dim(doc_row, first_row, local_rows, 0)
    inputs = tokens.astype(jnp.float32)
    normed, back_input = jax.vjp(rms_norm, inputs, norm_input)
    normed_low = normed.astype(jnp.bfloat16)
    query_proj = matmul(normed_low, query_weight)
    key_proj = matmul(normed_low, key_weight)
    value_proj = matmul(normed_low, value_weight)

    def query_prep(flat_rows, gain_vec):
        return rotate(rms_norm(flat_rows.reshape(local_rows, HQ, HD), gain_vec), angles[:, None, :])

    def key_prep(rows_in, gain_vec):
        return rotate(rms_norm(rows_in, gain_vec), angles)

    query_rot, back_query = jax.vjp(query_prep, query_proj, norm_query)
    key_rot, back_key = jax.vjp(key_prep, key_proj, norm_key)
    query_low = query_rot.astype(jnp.bfloat16)
    key_low = key_rot.astype(jnp.bfloat16)
    value_low = value_proj.astype(jnp.bfloat16)
    reach = min(-(-(WINDOW - 1) // local_rows), group_size - 1)
    key_list = [key_low]
    value_list = [value_low]
    for offset in range(1, reach + 1):
        key_far, value_far = shifted((key_low, value_low), "group", offset)
        key_list.insert(0, key_far)
        value_list.insert(0, value_far)
    key_all = jnp.concatenate(key_list, axis=0)
    value_all = jnp.concatenate(value_list, axis=0)
    key_count = (reach + 1) * local_rows
    doc_pad = jnp.concatenate([jnp.full((reach * local_rows,), -1, jnp.int32), doc_row])
    key_docs = lax.dynamic_slice_in_dim(doc_pad, first_row, key_count, 0)
    key_index = (group_index - reach) * local_rows + jnp.arange(key_count, dtype=jnp.int32)
    query_index = first_row + jnp.arange(local_rows, dtype=jnp.int32)
    distance = query_index[:, None] - key_index[None, :]
    allowed = (distance >= 0) & (distance < WINDOW) & (key_docs[None, :] == query_docs[:, None])

    def scores_of(key_rows_low):
        raw_scores = jnp.einsum(
            "qhd,kd->hqk", query_low, key_rows_low, preferred_element_type=jnp.float32
        ) * HD ** (-0.5)
        return jnp.where(allowed[None], raw_scores, -1e30)

    masked = scores_of(key_all)
    top_score = jnp.max(masked, axis=-1, keepdims=True)
    log_total = top_score + jnp.log(jnp.sum(jnp.exp(masked - top_score), axis=-1, keepdims=True))
    probs = jnp.exp(masked - log_total)
    attended = jnp.einsum(
        "hqk,kd->qhd", probs.astype(jnp.bfloat16), value_all, preferred_element_type=jnp.float32
    )
    attended_low = attended.reshape(local_rows, HQ * HD).astype(jnp.bfloat16)
    attn_out = matmul(attended_low, out_weight)
    branch_one, back_attn = jax.vjp(rms_norm, attn_out, norm_attn)
    middle = inputs + branch_one
    normed_two, back_ffin = jax.vjp(rms_norm, middle, norm_ffin)
    normed_two_low = normed_two.astype(jnp.bfloat16)
    gate_proj = matmul(normed_two_low, gate_weight)
    up_proj = matmul(normed_two_low, up_weight)
    hidden, back_hidden = jax.vjp(geglu, gate_proj, up_proj)
    hidden_low = hidden.astype(jnp.bfloat16)
    ffn_out = matmul(hidden_low, down_weight)
    branch_two, back_ffout = jax.vjp(rms_norm, ffn_out, norm_ffout)
    outputs = middle + branch_two
    grad_out = cotangent.astype(jnp.float32)
    grad_ffn, grad_gain_ffout = back_ffout(grad_out)
    grad_ffn_low = grad_ffn.astype(jnp.bfloat16)
    grad_down_w = jnp.einsum(
        "tf,td->fd", hidden_low, grad_ffn_low, preferred_element_type=jnp.float32
    )
    grad_hidden = jnp.einsum(
        "td,fd->tf", grad_ffn_low, down_weight, preferred_element_type=jnp.float32
    )
    grad_gate, grad_up = back_hidden(grad_hidden)
    grad_gate_low = grad_gate.astype(jnp.bfloat16)
    grad_up_low = grad_up.astype(jnp.bfloat16)
    grad_gate_w = jnp.einsum(
        "td,tf->df", normed_two_low, grad_gate_low, preferred_element_type=jnp.float32
    )
    grad_up_w = jnp.einsum(
        "td,tf->df", normed_two_low, grad_up_low, preferred_element_type=jnp.float32
    )
    grad_normed_two = jnp.einsum(
        "tf,df->td", grad_gate_low, gate_weight, preferred_element_type=jnp.float32
    ) + jnp.einsum("tf,df->td", grad_up_low, up_weight, preferred_element_type=jnp.float32)
    grad_middle_norm, grad_gain_ffin = back_ffin(grad_normed_two)
    grad_middle = grad_out + grad_middle_norm
    grad_attn, grad_gain_attn = back_attn(grad_middle)
    grad_attn_low = grad_attn.astype(jnp.bfloat16)
    grad_out_w = jnp.einsum(
        "to,td->od", attended_low, grad_attn_low, preferred_element_type=jnp.float32
    )
    grad_attended = jnp.einsum(
        "td,od->to", grad_attn_low, out_weight, preferred_element_type=jnp.float32
    )
    grad_attended_low = grad_attended.astype(jnp.bfloat16).reshape(local_rows, HQ, HD)
    probs_again = jnp.exp(scores_of(key_all) - log_total)
    grad_probs = jnp.einsum(
        "qhd,kd->hqk", grad_attended_low, value_all, preferred_element_type=jnp.float32
    )
    grad_value_all = jnp.einsum(
        "hqk,qhd->kd",
        probs_again.astype(jnp.bfloat16),
        grad_attended_low,
        preferred_element_type=jnp.float32,
    )
    grad_scores = probs_again * (
        grad_probs - jnp.sum(probs_again * grad_probs, axis=-1, keepdims=True)
    )
    grad_scores_low = (grad_scores * HD ** (-0.5)).astype(jnp.bfloat16)
    grad_query = jnp.einsum(
        "hqk,kd->qhd", grad_scores_low, key_all, preferred_element_type=jnp.float32
    )
    grad_key_all = jnp.einsum(
        "hqk,qhd->kd", grad_scores_low, query_low, preferred_element_type=jnp.float32
    )
    key_total = grad_key_all[reach * local_rows :]
    value_total = grad_value_all[reach * local_rows :]
    for offset in range(1, reach + 1):
        row_start = (reach - offset) * local_rows
        key_back, value_back = (
            shifted(
                grad_key_all[row_start : row_start + local_rows].astype(jnp.bfloat16),
                "group",
                -offset,
            ).astype(jnp.float32),
            shifted(
                grad_value_all[row_start : row_start + local_rows].astype(jnp.bfloat16),
                "group",
                -offset,
            ).astype(jnp.float32),
        )
        key_total = key_total + key_back
        value_total = value_total + value_back
    grad_query_proj, grad_gain_query = back_query(grad_query)
    grad_key_proj, grad_gain_key = back_key(key_total)
    grad_query_low = grad_query_proj.astype(jnp.bfloat16)
    grad_key_low = grad_key_proj.astype(jnp.bfloat16)
    grad_value_low = value_total.astype(jnp.bfloat16)
    grad_query_w = jnp.einsum(
        "td,te->de", normed_low, grad_query_low, preferred_element_type=jnp.float32
    )
    grad_key_w = jnp.einsum(
        "td,te->de", normed_low, grad_key_low, preferred_element_type=jnp.float32
    )
    grad_value_w = jnp.einsum(
        "td,te->de", normed_low, grad_value_low, preferred_element_type=jnp.float32
    )
    grad_normed = jnp.einsum(
        "te,de->td", grad_query_low, query_weight, preferred_element_type=jnp.float32
    )
    grad_normed = grad_normed + jnp.einsum(
        "te,de->td", grad_key_low, key_weight, preferred_element_type=jnp.float32
    )
    grad_normed = grad_normed + jnp.einsum(
        "te,de->td", grad_value_low, value_weight, preferred_element_type=jnp.float32
    )
    grad_input_norm, grad_gain_input = back_input(grad_normed)
    grad_inputs = grad_middle + grad_input_norm
    flat_query = grad_query_w.reshape(-1, 128)
    flat_key = grad_key_w.reshape(-1, 128)
    flat_value = grad_value_w.reshape(-1, 128)
    flat_out = grad_out_w.reshape(-1, 128)
    flat_gate = grad_gate_w.reshape(-1, 128)
    flat_up = grad_up_w.reshape(-1, 128)
    flat_down = grad_down_w.reshape(-1, 128)
    reduced = (
        lax.psum_scatter(flat_query, ("dp", "group"), scatter_dimension=0, tiled=True),
        lax.psum_scatter(flat_key, ("dp", "group"), scatter_dimension=0, tiled=True),
        lax.psum_scatter(flat_value, ("dp", "group"), scatter_dimension=0, tiled=True),
        lax.psum_scatter(flat_out, ("dp", "group"), scatter_dimension=0, tiled=True),
        lax.psum_scatter(flat_gate, ("dp", "group"), scatter_dimension=0, tiled=True),
        lax.psum_scatter(flat_up, ("dp", "group"), scatter_dimension=0, tiled=True),
        lax.psum_scatter(flat_down, ("dp", "group"), scatter_dimension=0, tiled=True),
    )
    grads_local = jnp.concatenate(list(reduced), axis=0)
    gain_grads = lax.psum(
        jnp.concatenate(
            [
                grad_gain_input,
                grad_gain_attn,
                grad_gain_ffin,
                grad_gain_ffout,
                grad_gain_query,
                grad_gain_key,
            ]
        ),
        ("dp", "group"),
    )
    moment_first, moment_second, master_new = adam_update(
        grads_local, first_moment, second_moment, master, learn_rate, weight_decay
    )
    gain_moment_first, gain_moment_second, gains_new = adam_update(
        gain_grads, gain_first, gain_second, gains, gain_rate, 0.0
    )
    return (
        outputs.astype(jnp.bfloat16),
        grad_inputs.astype(jnp.bfloat16),
        moment_first,
        moment_second,
        master_new,
        gain_moment_first,
        gain_moment_second,
        gains_new,
    )


def solution(mesh):
    placed = (
        P(("dp", "group"), None),
        P("dp", None),
        P(("dp", "group"), None),
        P(("dp", "group"), None),
        P(("dp", "group"), None),
        P(("dp", "group"), None),
        P(),
        P(),
        P(),
    )
    return jax.shard_map(
        shards,
        mesh=mesh,
        in_specs=placed,
        out_specs=(
            P(("dp", "group"), None),
            P(("dp", "group"), None),
            P(("dp", "group"), None),
            P(("dp", "group"), None),
            P(("dp", "group"), None),
            P(),
            P(),
            P(),
        ),
        check_vma=False,
    )
```

```python
import functools
import math

import jax
import jax.numpy as jnp
from jax import lax
from jax.experimental import pallas as pl
from jax.experimental.pallas import tpu as pltpu
from jax.sharding import PartitionSpec as P

D = 640
HQ = 4
HD = 256
FF = 2048
WINDOW = 512
STEP = 10
ALL_AXES = ("dp", "group")


norm_eps = 1e-06
rope_base = 10000.0
beta_first = 0.9
beta_second = 0.999
learn_rate = 0.05
gain_rate = 0.25
adam_floor = 1e-08
weight_decay = 0.1


def shifted(value, axis, steps):
    count = lax.axis_size(axis)
    initial, last = (max(0, -steps), min(count, count - steps))
    return lax.ppermute(value, axis, [(source, source + steps) for source in range(initial, last)])


def rms_norm(values, weight_vec):
    return (
        values
        * lax.rsqrt(jnp.mean(values * values, axis=-1, keepdims=True) + norm_eps)
        * (1.0 + weight_vec)
    )


def positions(doc_row):
    length = doc_row.shape[0]
    counter = jnp.arange(length, dtype=jnp.int32)
    starts_here = jnp.concatenate([jnp.ones((1,), jnp.bool_), doc_row[1:] != doc_row[:-1]])
    begins = lax.cummax(jnp.where(starts_here, counter, jnp.zeros_like(counter)), axis=0)
    return counter - begins


def angles_of(places):
    half_dim = HD // 2
    frequency = rope_base ** (-(jnp.arange(half_dim, dtype=jnp.float32) * 2.0 / HD))
    return places.astype(jnp.float32)[:, None] * frequency[None, :]


def rotate(values, angles):
    half_dim = values.shape[-1] // 2
    first_half = values[..., :half_dim]
    second_half = values[..., half_dim:]
    cosine = jnp.cos(angles)
    sine_part = jnp.sin(angles)
    return jnp.concatenate(
        [
            first_half * cosine - second_half * sine_part,
            second_half * cosine + first_half * sine_part,
        ],
        axis=-1,
    )


def geglu(gate_in, up_in):
    return jax.nn.gelu(gate_in, approximate=True) * up_in


def adam_update(gradient, first_old, second_old, params_old, rate, decay_rate):
    first_new = beta_first * first_old + (1.0 - beta_first) * gradient
    second_new = beta_second * second_old + (1.0 - beta_second) * gradient * gradient
    first_hat = first_new / (1.0 - beta_first**STEP)
    second_hat = second_new / (1.0 - beta_second**STEP)
    params_new = params_old - rate * (
        first_hat / (jnp.sqrt(second_hat) + adam_floor) + decay_rate * params_old
    )
    return (first_new, second_new, params_new)


def piece_rows(device_count):
    return [
        entries // (128 * device_count)
        for entries in (D * HQ * HD, D * HD, D * HD, HQ * HD * D, D * FF, D * FF, FF * D)
    ]


def piece_shapes():
    return [(D, HQ * HD), (D, HD), (D, HD), (HQ * HD, D), (D, FF), (D, FF), (FF, D)]


def split_rows(stacked, row_list):
    result = []
    row_start = 0
    for row_count in row_list:
        result.append(stacked[row_start : row_start + row_count])
        row_start = row_start + row_count
    return result


def matmul(left_side, right_side):
    return jnp.dot(left_side, right_side, preferred_element_type=jnp.float32)


LOW_COUNT = 8
LANES = 128
LOW_MASKS = (0, 4, 2, 6, 1, 5, 3, 7)
GELU_SCALE = (2.0 / math.pi) ** 0.5
GELU_CUBE = 0.044715
SPARE_ROWS = 128
VMEM_BYTES = 56 * 1024 * 1024


def aligned(device_count):
    groups = lax.axis_size("group") == 4
    return groups and device_count % LOW_COUNT == 0 and D % device_count == 0


def swap(value, mask):
    count = lax.axis_size(ALL_AXES)
    return lax.ppermute(value, ALL_AXES, [(source, source ^ mask) for source in range(count)])


def local_call(kernel, outs, operands, scratch=(), behind=()):
    specs = [pl.BlockSpec(memory_space=pltpu.SMEM)]
    specs = specs + [pl.BlockSpec(memory_space=pltpu.VMEM)] * len(operands)
    specs = specs + [pl.BlockSpec(memory_space=pl.ANY)] * len(behind)
    first, last = 1 + len(operands), 1 + len(operands) + len(behind)

    def body(*refs):
        kernel(*refs[:first], *refs[last:])

    return pl.pallas_call(
        body,
        out_shape=outs,
        in_specs=specs,
        out_specs=tuple(pl.BlockSpec(memory_space=pltpu.VMEM) for _ in outs),
        scratch_shapes=scratch,
        compiler_params=pltpu.CompilerParams(vmem_limit_bytes=VMEM_BYTES),
        cost_estimate=pl.CostEstimate(flops=0, bytes_accessed=0, transcendentals=0),
    )(lax.axis_index(ALL_AXES).astype(jnp.int32).reshape(1), *operands, *behind)


class Piece:
    def __init__(self, rows, columns, device_count):
        self.rows = rows
        self.columns = columns
        self.wide = rows == D
        self.blocks = columns // LANES
        self.own_rows = rows // device_count
        self.flat_rows = self.own_rows * self.blocks
        self.high_count = device_count // LOW_COUNT
        self.block_rows = self.own_rows * self.high_count
        self.size = self.block_rows * self.blocks


def copy_kernel(index_ref, in_ref, out_ref):
    out_ref[...] = in_ref[...]


def pack_kernel(pieces, index_ref, *refs):
    high_count = pieces[0].high_count
    parts, out_refs, flat, packed = refs[:high_count], refs[high_count:-2], refs[-2], refs[-1]
    high = index_ref[0] // LOW_COUNT
    for step, part in enumerate(parts):
        flat[high ^ step, : part.shape[0], :] = part[...].astype(jnp.float32)
    start, target = 0, 0
    for piece in pieces:
        for block in range(piece.blocks):
            for place in range(high_count):
                packed[pl.ds(target, piece.own_rows), :] = flat[
                    place, pl.ds(start + block, piece.own_rows, stride=piece.blocks), :
                ]
                target = target + piece.own_rows
        start = start + piece.flat_rows
    count = target // len(out_refs)
    for place, out_ref in enumerate(out_refs):
        out_ref[...] = packed[place * count : (place + 1) * count, :].astype(jnp.bfloat16)


def sum_one_kernel(size, index_ref, near_ref, far_ref, to_x_ref, to_y_ref):
    total = near_ref[...].astype(jnp.float32) + far_ref[...].astype(jnp.float32)
    half = size // 2
    to_x_ref[:half, :] = total[:half].astype(jnp.bfloat16)
    if total.shape[0] > size:
        to_x_ref[half:, :] = total[size:].astype(jnp.bfloat16)
    to_y_ref[...] = total[half:size].astype(jnp.bfloat16)


def sum_three_kernel(
    size,
    index_ref,
    near_ref,
    far_ref,
    *refs,
):
    key_refs = refs[:-5]
    own_ref, beside_first_ref, beside_second_ref, across_first_ref, across_second_ref = refs[-5:]
    half = size // 2
    if key_refs:
        across_key_ref, cores_key_ref = key_refs
        rows = across_key_ref.shape[0]
        keys = across_key_ref[...] + cores_key_ref[rows:, :].astype(jnp.float32)
        for block in range(keys.shape[1] // LANES):
            first = half + block * rows
            columns = slice(block * LANES, (block + 1) * LANES)
            across_second_ref[first : first + rows, :] = keys[:, columns].astype(jnp.bfloat16)
    outs = (beside_first_ref, beside_second_ref, across_first_ref, across_second_ref)
    total = near_ref[:size, :].astype(jnp.float32) + far_ref[:size, :].astype(jnp.float32)
    own_ref[...] = total.astype(jnp.bfloat16)
    for place, out_ref in enumerate(outs):
        rows = slice(size + place * half, size + (place + 1) * half)
        total = near_ref[rows, :].astype(jnp.float32) + far_ref[rows, :].astype(jnp.float32)
        out_ref[:half, :] = total.astype(jnp.bfloat16)


def sum_all_kernel(size, index_ref, near_three, near_one, far_three, far_one, *out_refs):
    sum_one_kernel(size, index_ref, near_one, far_one, *out_refs[:2])
    sum_three_kernel(size, index_ref, near_three, far_three, *out_refs[2:])


def sum_passed_kernel(
    size,
    index_ref,
    beside_ref,
    across_ref,
    over_x_ref,
    over_y_ref,
    near_one_ref,
    far_one_ref,
    beside_out_ref,
    across_out_ref,
    extra_ref,
):
    half = size // 2
    beside = beside_ref[...].astype(jnp.float32) + over_y_ref[...].astype(jnp.float32)
    beside_out_ref[...] = beside.astype(jnp.bfloat16)
    across = across_ref[...].astype(jnp.float32) + over_x_ref[:half, :].astype(jnp.float32)
    across_out_ref[:half, :] = across.astype(jnp.bfloat16)
    if across_out_ref.shape[0] > half:
        extra = near_one_ref[size:, :].astype(jnp.float32)
        extra = extra + far_one_ref[size:, :].astype(jnp.float32)
        extra = extra + over_x_ref[half:, :].astype(jnp.float32)
        extra_ref[...] = extra
        across_out_ref[half:, :] = extra.astype(jnp.bfloat16)
    else:
        extra_ref[...] = jnp.zeros(extra_ref.shape, jnp.float32)


def unpack_kernel(
    pieces,
    index_ref,
    own_ref,
    beside_first_ref,
    beside_second_ref,
    across_first_ref,
    across_second_ref,
    extra_ref,
    *refs,
):
    high_count = pieces[0].high_count
    half = sum(piece.size for piece in pieces) // 2
    flat_rows = sum(piece.flat_rows for piece in pieces)
    outs, flat, packed = refs[:-2], refs[-2], refs[-1]
    high = index_ref[0] // LOW_COUNT
    packed[:half, :] = (
        own_ref[:half, :].astype(jnp.float32)
        + beside_first_ref[...].astype(jnp.float32)
        + across_first_ref[:half, :].astype(jnp.float32)
    )
    packed[half:, :] = (
        own_ref[half:, :].astype(jnp.float32)
        + beside_second_ref[...].astype(jnp.float32)
        + across_second_ref[:half, :].astype(jnp.float32)
    )
    start, source = 0, 0
    for piece in pieces:
        for block in range(piece.blocks):
            for place in range(high_count):
                flat[place, pl.ds(start + block, piece.own_rows, stride=piece.blocks), :] = packed[
                    pl.ds(source, piece.own_rows), :
                ]
                source = source + piece.own_rows
        start = start + piece.flat_rows
    for step, out_ref in enumerate(outs):
        out_ref[:flat_rows, :] = flat[high ^ step, :flat_rows, :].astype(out_ref.dtype)
        if out_ref.shape[0] > flat_rows:
            extra = extra_ref[...] + across_first_ref[half:, :].astype(jnp.float32)
            out_ref[flat_rows:, :] = extra.astype(out_ref.dtype)


def array(shape, kind):
    return jax.ShapeDtypeStruct(shape, kind)


def gather_high(rows):
    high_count = lax.axis_size(ALL_AXES) // LOW_COUNT
    return [rows] + [swap(rows, step * LOW_COUNT) for step in range(1, high_count)]


def gather_own(pieces, parts, count, behind=()):
    high_count = pieces[0].high_count
    size = sum(piece.size for piece in pieces)
    return local_call(
        functools.partial(pack_kernel, pieces),
        (array((size // count, LANES), jnp.bfloat16),) * count,
        parts,
        (
            pltpu.VMEM((high_count, parts[0].shape[0] + SPARE_ROWS, LANES), jnp.float32),
            pltpu.VMEM((size, LANES), jnp.float32),
        ),
        behind,
    )


def copied(value, behind):
    return local_call(copy_kernel, (array(value.shape, jnp.bfloat16),), (value,), (), behind)[0]


def held(values, behind):
    count = len(values)
    return pl.pallas_call(
        lambda *refs: None,
        out_shape=tuple(array(value.shape, value.dtype) for value in values),
        in_specs=[pl.BlockSpec(memory_space=pl.ANY)] * (count + len(behind)),
        out_specs=tuple(pl.BlockSpec(memory_space=pl.ANY) for _ in values),
        input_output_aliases={place: place for place in range(count)},
        cost_estimate=pl.CostEstimate(flops=0, bytes_accessed=0, transcendentals=0),
    )(*values, *behind)


def gather_halves(first, second):
    return swap(second, 4), swap(first, 2)


def gather_rest(first, second, beside_second, across_first, keys, behind):
    beside_first, across_second = swap(copied(first, keys[:1]), 4), swap(second, 2)
    over_x, over_y = swap(across_first, 4), swap(copied(beside_second, keys[1:]), 2)
    diagonal = held((over_x, over_y), behind)
    return first, second, beside_first, beside_second, across_first, across_second, *diagonal


def gather_wholes(own):
    return own, swap(own, 4), swap(own, 2), swap(own, 6)


def gather_cores(near):
    return near + tuple(swap(value, 1) for value in near)


def scatter_cores(far_three, far_one):
    far_one = swap(far_one, 1)
    return swap(far_three, 1), far_one


def scatter_one(pieces, near_one, far_one, behind=()):
    half = sum(piece.size for piece in pieces) // 2
    to_x, to_y = local_call(
        functools.partial(sum_one_kernel, 2 * half),
        (
            array((near_one.shape[0] - half, LANES), jnp.bfloat16),
            array((half, LANES), jnp.bfloat16),
        ),
        (near_one, far_one),
        (),
        behind,
    )
    return swap(to_x, 4), swap(to_y, 2), to_y


def scatter_three(pieces, near_three, far_three, behind=(), keys=()):
    size = sum(piece.size for piece in pieces)
    half = size // 2
    own, beside_first, beside_second, across_first, across_second = local_call(
        functools.partial(sum_three_kernel, size),
        (
            array((size, LANES), jnp.bfloat16),
            *(array((half, LANES), jnp.bfloat16),) * 3,
            array((half + (keys[0].size // LANES if keys else 0), LANES), jnp.bfloat16),
        ),
        (near_three, far_three, *keys),
        (),
        behind,
    )
    return own, swap(beside_first, 4), beside_second, across_first, swap(across_second, 2)


def scatter_all(pieces, near_three, near_one, far_three, far_one, behind=()):
    size = sum(piece.size for piece in pieces)
    half = size // 2
    to_x, to_y, own, beside_first, beside_second, across_first, across_second = local_call(
        functools.partial(sum_all_kernel, size),
        (
            array((near_one.shape[0] - half, LANES), jnp.bfloat16),
            array((half, LANES), jnp.bfloat16),
            array((size, LANES), jnp.bfloat16),
            *(array((half, LANES), jnp.bfloat16),) * 4,
        ),
        (near_three, near_one, far_three, far_one),
        (),
        behind,
    )
    over_x, over_y = swap(to_x, 4), swap(to_y, 2)
    return (
        over_x,
        over_y,
        (own, swap(beside_first, 4), beside_second, across_first, swap(across_second, 2)),
    )


def scatter_passed(pieces, threes, over_x, over_y, near_one, far_one, behind=()):
    size = sum(piece.size for piece in pieces)
    extra_count = near_one.shape[0] - size
    own, beside_first, beside_second, across_first, across_second = threes
    beside_second, across_first, extra = local_call(
        functools.partial(sum_passed_kernel, size),
        (
            array((size // 2, LANES), jnp.bfloat16),
            array((size // 2 + extra_count, LANES), jnp.bfloat16),
            array((max(extra_count, 8), LANES), jnp.float32),
        ),
        (beside_second, across_first, over_x, over_y, near_one, far_one),
        (),
        behind,
    )
    terms = (
        own,
        beside_first,
        swap(beside_second, 4),
        swap(across_first, 2),
        across_second,
        extra,
    )
    return terms, beside_second


def scatter_high(pieces, terms, behind=()):
    high_count = pieces[0].high_count
    size = sum(piece.size for piece in pieces)
    flat_rows = sum(piece.flat_rows for piece in pieces)
    out_rows = flat_rows + terms[3].shape[0] - size // 2
    outs = local_call(
        functools.partial(unpack_kernel, pieces),
        (array((out_rows, LANES), jnp.float32),)
        + (array((out_rows, LANES), jnp.bfloat16),) * (high_count - 1),
        terms,
        (
            pltpu.VMEM((high_count, flat_rows + SPARE_ROWS, LANES), jnp.float32),
            pltpu.VMEM((size, LANES), jnp.float32),
        ),
        behind,
    )
    arrived = [swap(send, step * LOW_COUNT) for step, send in enumerate(outs) if step]
    return outs[0] + sum(value.astype(jnp.float32) for value in arrived), outs[0], arrived


def norm_parts(values):
    scale = lax.rsqrt(jnp.mean(values * values, axis=-1, keepdims=True) + norm_eps)
    return scale, values * scale


def norm_back(scale, normal, upstream, weight_vec):
    weighted = upstream * (1.0 + weight_vec)
    inner = jnp.mean(weighted * normal, axis=-1, keepdims=True)
    return scale * (weighted - normal * inner), jnp.sum(normal * upstream, axis=0, keepdims=True)


def product(left_side, right_side, left_axis, right_axis):
    return lax.dot_general(
        left_side,
        right_side,
        (((left_axis,), (right_axis,)), ((), ())),
        preferred_element_type=jnp.float32,
    )


def turned_over(rows_low):
    return rows_low.astype(jnp.float32).T.astype(jnp.bfloat16)


def unordered(rows_in, order_low):
    upper = rows_in.astype(jnp.bfloat16)
    lower = (rows_in - upper.astype(jnp.float32)).astype(jnp.bfloat16)
    return product(upper, order_low, 1, 1) + product(lower, order_low, 1, 1)


def weight_rows(refs, size, order, start, rows):
    count = len(refs) // LOW_COUNT
    part = size // count
    return refs[order * count + start // part][start % part : start % part + rows, :]


def put_rows(refs, size, order, start, rows):
    three, one = refs[:2] if order < 4 else refs[2:]
    if order % 4 == 3:
        one[start : start + rows.shape[0], :] = rows
    else:
        start = order % 4 * size + start
        three[start : start + rows.shape[0], :] = rows


def wide_tile(refs, size, start, rows):
    return jnp.concatenate(
        [weight_rows(refs, size, order, start, rows) for order in range(LOW_COUNT)]
    )


def put_wide_tile(refs, size, start, rows, tile):
    for order in range(LOW_COUNT):
        put_rows(refs, size, order, start, tile[order * rows : (order + 1) * rows])


def tall_rows(piece, low):
    for order, mask in enumerate(LOW_MASKS):
        for block in range(piece.blocks):
            for place in range(piece.high_count):
                row = (place * LOW_COUNT + (low ^ mask)) * piece.own_rows
                yield (
                    order,
                    block * piece.block_rows + place * piece.own_rows,
                    pl.ds(pl.multiple_of(row, piece.own_rows), piece.own_rows),
                    slice(block * LANES, (block + 1) * LANES),
                )


def ffn_kernel(
    gate_piece,
    down_piece,
    index_ref,
    middle_ref,
    cotangent_ref,
    gain_in_ref,
    gain_out_ref,
    order_ref,
    *refs,
):
    weight_refs, grad_refs = refs[:16], refs[20:24]
    block_out_ref, grad_middle_ref, grad_gain_in_ref, grad_gain_out_ref = refs[16:20]
    down_ref, hidden_ref, gelu_ref, slope_ref = refs[24:]
    low = index_ref[0] % LOW_COUNT
    rows = gate_piece.block_rows
    size = 2 * gate_piece.size + down_piece.size
    width = 2 * LANES
    for order, start, matrix_rows, columns in tall_rows(down_piece, low):
        start = start + 2 * gate_piece.size
        down_ref[matrix_rows, columns] = weight_rows(
            weight_refs, size, order, start, down_piece.own_rows
        )

    def wide_tiles(step):
        return [
            jnp.concatenate(
                [
                    wide_tile(weight_refs, size, offset + block * rows, rows)
                    for block in (2 * step, 2 * step + 1)
                ],
                axis=1,
            )
            for offset in (0, gate_piece.size)
        ]

    middle = middle_ref[...]
    scale_in, normal_in = norm_parts(middle)
    order_low = order_ref[...]
    normed = (normal_in * (1.0 + gain_in_ref[...])).astype(jnp.bfloat16)
    normed = product(normed, order_low, 1, 0).astype(jnp.bfloat16)
    normed_turned = turned_over(normed)
    for step in range(FF // width):
        columns = slice(step * width, (step + 1) * width)
        gate_weight, up_weight = wide_tiles(step)
        gate = product(normed, gate_weight, 1, 0)
        up = product(normed, up_weight, 1, 0)
        square = gate * gate
        bend = jnp.tanh(GELU_SCALE * gate * (1.0 + GELU_CUBE * square))
        half = 0.5 * (1.0 + bend)
        gelu = gate * half
        slope = half + 0.5 * gate * (1.0 - bend * bend) * GELU_SCALE * (
            1.0 + 3.0 * GELU_CUBE * square
        )
        gelu_ref[:, columns] = gelu
        slope_ref[:, columns] = slope * up
        hidden_ref[:, columns] = (gelu * up).astype(jnp.bfloat16)
    hidden = hidden_ref[...]
    scale_out, normal_out = norm_parts(product(hidden, down_ref[...], 1, 0))
    block_out_ref[...] = (middle + normal_out * (1.0 + gain_out_ref[...])).astype(jnp.bfloat16)
    upstream = cotangent_ref[...].astype(jnp.float32)
    grad_ffn, grad_gain_out_ref[...] = norm_back(
        scale_out, normal_out, upstream, gain_out_ref[...]
    )
    grad_ffn = grad_ffn.astype(jnp.bfloat16)
    grad_normed = jnp.zeros(middle.shape, jnp.float32)
    for step in range(FF // width):
        columns = slice(step * width, (step + 1) * width)
        grad_hidden = product(grad_ffn, down_ref[columns, :], 1, 1)
        down_ref[columns, :] = product(hidden_ref[:, columns], grad_ffn, 0, 0).astype(jnp.bfloat16)
        grads = [
            (grad_hidden * slope_ref[:, columns]).astype(jnp.bfloat16),
            (grad_hidden * gelu_ref[:, columns]).astype(jnp.bfloat16),
        ]
        for place, (grad, weight) in enumerate(zip(grads, wide_tiles(step))):
            grad_weight = product(normed_turned, grad, 1, 0).astype(jnp.bfloat16)
            for side in range(2):
                put_wide_tile(
                    grad_refs,
                    size,
                    place * gate_piece.size + (2 * step + side) * rows,
                    rows,
                    grad_weight[:, side * LANES : (side + 1) * LANES],
                )
            grad_normed = grad_normed + product(grad, weight, 1, 1)
    for order, start, matrix_rows, columns in tall_rows(down_piece, low):
        start = start + 2 * gate_piece.size
        put_rows(grad_refs, size, order, start, down_ref[matrix_rows, columns])
    grad_middle, grad_gain_in_ref[...] = norm_back(
        scale_in, normal_in, unordered(grad_normed, order_low), gain_in_ref[...]
    )
    grad_middle_ref[...] = upstream + grad_middle


def grad_arrays(pieces, extra_count=0):
    size = sum(piece.size for piece in pieces)
    return (
        array((3 * size, LANES), jnp.bfloat16),
        array((size + extra_count, LANES), jnp.bfloat16),
    ) * 2


def ffn_blocks(pieces, middle, cotangent, gain_in, gain_out, order, blocks):
    rows = middle.shape[0]
    outs = local_call(
        functools.partial(ffn_kernel, pieces[4], pieces[6]),
        (
            array((rows, D), jnp.bfloat16),
            array((rows, D), jnp.float32),
            array((1, D), jnp.float32),
            array((1, D), jnp.float32),
            *grad_arrays(pieces[4:7]),
        ),
        (middle, cotangent, gain_in, gain_out, order, *blocks),
        (
            pltpu.VMEM((FF, D), jnp.bfloat16),
            pltpu.VMEM((rows, FF), jnp.bfloat16),
            pltpu.VMEM((rows, FF), jnp.float32),
            pltpu.VMEM((rows, FF), jnp.float32),
        ),
    )
    return *outs[:4], outs[4:]


def turn(values, cosine, sine):
    first_half, second_half = values[:, : HD // 2], values[:, HD // 2 :]
    return jnp.concatenate(
        [first_half * cosine - second_half * sine, second_half * cosine + first_half * sine], axis=1
    )


def wide_head(refs, size, start, rows):
    return jnp.concatenate(
        [wide_tile(refs, size, start + side * rows, rows) for side in range(2)], axis=1
    )


def head_starts(pieces):
    rows = pieces[0].block_rows
    return [2 * rows * head for head in range(HQ + 2)]


def project_kernel(
    pieces,
    index_ref,
    tokens_ref,
    gain_ref,
    gain_query_ref,
    gain_key_ref,
    cosine_ref,
    sine_ref,
    order_ref,
    *refs,
):
    weight_refs = refs[:8]
    normed_ref, query_proj_ref, key_proj_ref, query_ref, key_value_ref = refs[8:]
    size = sum(piece.size for piece in pieces)
    rows = pieces[0].block_rows
    cosine, sine = cosine_ref[...], sine_ref[...]
    _, normal = norm_parts(tokens_ref[...].astype(jnp.float32))
    normed = (normal * (1.0 + gain_ref[...])).astype(jnp.bfloat16)
    normed = product(normed, order_ref[...], 1, 0).astype(jnp.bfloat16)
    normed_ref[...] = normed
    starts = head_starts(pieces)
    for head, start in enumerate(starts):
        proj = product(normed, wide_head(weight_refs, size, start, rows), 1, 0)
        columns = slice(head * HD, (head + 1) * HD)
        if head == HQ + 1:
            key_value_ref[:, HD:] = proj.astype(jnp.bfloat16)
            continue
        gain_vec = gain_query_ref[...] if head < HQ else gain_key_ref[...]
        _, normal = norm_parts(proj)
        turned = turn(normal * (1.0 + gain_vec), cosine, sine).astype(jnp.bfloat16)
        if head < HQ:
            query_proj_ref[:, columns] = proj
            query_ref[:, columns] = turned
        else:
            key_proj_ref[...] = proj
            key_value_ref[:, :HD] = turned


def attend_kernel(
    pieces,
    index_ref,
    tokens_ref,
    gain_ref,
    allowed_ref,
    query_ref,
    *refs,
):
    weight_refs, key_value_refs = refs[:8], refs[8:-5]
    probs_ref, attended_ref, attn_out_ref, middle_ref, out_weight_ref = refs[-5:]
    out_piece = pieces[-1]
    low = index_ref[0] % LOW_COUNT
    size = sum(piece.size for piece in pieces)
    out_start = size - out_piece.size
    for order, start, matrix_rows, columns in tall_rows(out_piece, low):
        out_weight_ref[matrix_rows, columns] = weight_rows(
            weight_refs, size, order, start + out_start, out_piece.own_rows
        )
    rows = tokens_ref.shape[0]
    allowed = allowed_ref[...] > 0.0
    keys = jnp.concatenate([ref[:, :HD] for ref in key_value_refs])
    values = jnp.concatenate([ref[:, HD:] for ref in key_value_refs])
    count = keys.shape[0]
    for head in range(HQ):
        columns = slice(head * HD, (head + 1) * HD)
        scores = product(query_ref[:, columns], keys, 1, 1) * HD ** (-0.5)
        scores = jnp.where(allowed, scores, -1e30)
        raised = jnp.exp(scores - jnp.max(scores, axis=-1, keepdims=True))
        probs = raised / jnp.sum(raised, axis=-1, keepdims=True)
        probs_ref[:, head * count : (head + 1) * count] = probs
        attended_ref[:, columns] = product(probs.astype(jnp.bfloat16), values, 1, 0).astype(
            jnp.bfloat16
        )
    attn_out = product(attended_ref[...], out_weight_ref[...], 1, 0)
    attn_out_ref[...] = attn_out
    _, normal = norm_parts(attn_out)
    middle_ref[...] = tokens_ref[...].astype(jnp.float32) + normal * (1.0 + gain_ref[...])


def attend_back_kernel(
    index_ref,
    grad_middle_ref,
    attn_out_ref,
    gain_ref,
    out_weight_ref,
    attended_ref,
    probs_ref,
    query_ref,
    *refs,
):
    key_value_refs = refs[:4]
    grad_out_weight_ref, grad_query_ref, grad_gain_ref = refs[4:7]
    grad_own_ref, grad_across_ref, grad_cores_ref = refs[7:]
    rows = query_ref.shape[0]
    scale, normal = norm_parts(attn_out_ref[...])
    grad_attn, grad_gain_ref[...] = norm_back(scale, normal, grad_middle_ref[...], gain_ref[...])
    grad_attn = grad_attn.astype(jnp.bfloat16)
    grad_out_weight_ref[...] = product(attended_ref[...], grad_attn, 0, 0).astype(jnp.bfloat16)
    keys = jnp.concatenate([ref[:, :HD] for ref in key_value_refs])
    values = jnp.concatenate([ref[:, HD:] for ref in key_value_refs])
    count = keys.shape[0]
    grad_keys = jnp.zeros((count, HD), jnp.float32)
    grad_values = jnp.zeros((count, HD), jnp.float32)
    for head in range(HQ):
        columns = slice(head * HD, (head + 1) * HD)
        grad_attended = product(grad_attn, out_weight_ref[columns, :], 1, 1).astype(jnp.bfloat16)
        probs = probs_ref[:, head * count : (head + 1) * count]
        grad_probs = product(grad_attended, values, 1, 1)
        grad_values = grad_values + product(probs.astype(jnp.bfloat16), grad_attended, 0, 0)
        inner = jnp.sum(probs * grad_probs, axis=-1, keepdims=True)
        grad_scores = (probs * (grad_probs - inner) * HD ** (-0.5)).astype(jnp.bfloat16)
        grad_query_ref[:, columns] = product(grad_scores, keys, 1, 0)
        grad_keys = grad_keys + product(grad_scores, query_ref[:, columns], 0, 0)
    targets = (
        grad_own_ref,
        grad_cores_ref.at[:rows],
        grad_across_ref,
        grad_cores_ref.at[rows:],
    )
    for part, ref in enumerate(targets):
        ref[:, :HD] = grad_keys[part * rows : (part + 1) * rows].astype(ref.dtype)
        ref[:, HD:] = grad_values[part * rows : (part + 1) * rows].astype(ref.dtype)


def query_back_kernel(
    pieces,
    index_ref,
    gain_ref,
    cosine_ref,
    sine_ref,
    normed_ref,
    query_proj_ref,
    grad_query_ref,
    *refs,
):
    weight_refs = refs[:8]
    grad_weight_ref, grad_normed_ref, grad_gain_ref = refs[8:]
    size = sum(piece.size for piece in pieces)
    rows = pieces[0].block_rows
    cosine, sine = cosine_ref[...], sine_ref[...]
    normed_turned = turned_over(normed_ref[...])
    grad_normed = jnp.zeros(grad_normed_ref.shape, jnp.float32)
    grad_gain = jnp.zeros((1, HD), jnp.float32)
    for head, start in enumerate(head_starts(pieces)[:HQ]):
        columns = slice(head * HD, (head + 1) * HD)
        scale, normal = norm_parts(query_proj_ref[:, columns])
        upstream = turn(grad_query_ref[:, columns], cosine, -sine)
        grad, gain_row = norm_back(scale, normal, upstream, gain_ref[...])
        grad_gain = grad_gain + gain_row
        grad = grad.astype(jnp.bfloat16)
        weight = wide_head(weight_refs, size, start, rows)
        grad_normed = grad_normed + product(grad, weight, 1, 1)
        grad_weight_ref[:, columns] = product(normed_turned, grad, 1, 0).astype(jnp.bfloat16)
    grad_normed_ref[...] = grad_normed
    grad_gain_ref[...] = grad_gain


def project_back_kernel(
    pieces,
    index_ref,
    tokens_ref,
    gain_ref,
    gain_key_ref,
    cosine_ref,
    sine_ref,
    order_ref,
    normed_ref,
    key_proj_ref,
    grad_normed_ref,
    grad_middle_ref,
    gain_attn_ref,
    gain_ffin_ref,
    gain_ffout_ref,
    gain_query_ref,
    own_key_ref,
    cores_key_ref,
    across_key_ref,
    *refs,
):
    weight_refs = refs[:8]
    grad_weight_ref, input_grad_ref, grad_gain_ref = refs[8:]
    size = sum(piece.size for piece in pieces)
    rows = pieces[0].block_rows
    normed = normed_ref[...]
    key_rows = own_key_ref.shape[0]
    first = across_key_ref.shape[0] - 4 * key_rows
    key_value = own_key_ref[...] + cores_key_ref[:key_rows, :].astype(jnp.float32)
    key_value = key_value + jnp.concatenate(
        [
            across_key_ref[first + block * key_rows : first + (block + 1) * key_rows, :].astype(
                jnp.float32
            )
            for block in range(4)
        ],
        axis=1,
    )
    scale, normal = norm_parts(key_proj_ref[...])
    upstream = turn(key_value[:, :HD], cosine_ref[...], -sine_ref[...])
    grad_key, grad_gain_key = norm_back(scale, normal, upstream, gain_key_ref[...])
    grad_normed = grad_normed_ref[...]
    for place, start in enumerate(head_starts(pieces)[HQ:]):
        grad = (key_value[:, HD:] if place else grad_key).astype(jnp.bfloat16)
        weight = wide_head(weight_refs, size, start, rows)
        grad_normed = grad_normed + product(grad, weight, 1, 1)
        grad_weight_ref[:, place * HD : (place + 1) * HD] = product(normed, grad, 0, 0).astype(
            jnp.bfloat16
        )
    scale, normal = norm_parts(tokens_ref[...].astype(jnp.float32))
    grad_inputs, grad_gain_input = norm_back(
        scale, normal, unordered(grad_normed, order_ref[...]), gain_ref[...]
    )
    input_grad_ref[...] = (grad_middle_ref[...] + grad_inputs).astype(jnp.bfloat16)
    grad_gains = [
        grad_gain_input,
        gain_attn_ref[...],
        gain_ffin_ref[...],
        gain_ffout_ref[...],
        gain_query_ref[...],
        grad_gain_key,
    ]
    row = 0
    grad_gain_ref[...] = jnp.zeros(grad_gain_ref.shape, jnp.float32)
    for values in grad_gains:
        for start in range(0, values.shape[1], LANES):
            grad_gain_ref[row : row + 1, :] = values[:, start : start + LANES]
            row = row + 1


def split_kernel(
    pieces,
    index_ref,
    query_ref,
    key_value_ref,
    out_ref,
    gain_ref,
    *grad_refs,
):
    low = index_ref[0] % LOW_COUNT
    size = sum(piece.size for piece in pieces)
    rows = pieces[0].block_rows
    start = 0
    for matrix_ref in (query_ref, key_value_ref):
        for column in range(0, matrix_ref.shape[1], LANES):
            tile = matrix_ref[:, column : column + LANES]
            put_wide_tile(grad_refs, size, start, rows, tile)
            start = start + rows
    out_piece = pieces[-1]
    for order, first, matrix_rows, columns in tall_rows(out_piece, low):
        put_rows(grad_refs, size, order, start + first, out_ref[matrix_rows, columns])
    for target in (grad_refs[1], grad_refs[3]):
        target[size:, :] = gain_ref[...].astype(jnp.bfloat16)


def width_order(device_count):
    low = lax.axis_index(ALL_AXES) % LOW_COUNT
    rows = D // device_count
    high_count = device_count // LOW_COUNT
    column = jnp.arange(D, dtype=jnp.int32)
    place = column // (rows * high_count)
    mask = (place & 1) * 4 + ((place >> 1) & 1) * 2 + (place >> 2)
    high = (column // rows) % high_count
    picked = (high * LOW_COUNT + (low ^ mask)) * rows + column % rows
    return (jnp.arange(D, dtype=jnp.int32)[:, None] == picked[None, :]).astype(jnp.bfloat16)


GAIN_ROWS = 32


def shards_blocks(
    device_count,
    tokens,
    doc_ids,
    cotangent,
    master,
    first_moment,
    second_moment,
    gains,
    gain_first,
    gain_second,
):
    pieces = [Piece(*shape_pair, device_count) for shape_pair in piece_shapes()]
    attention_pieces = pieces[:4]
    local_rows = tokens.shape[0]
    group_size = lax.axis_size("group")
    first_row = lax.axis_index("group") * local_rows
    attention_rows = sum(piece.flat_rows for piece in attention_pieces)
    ffn_pieces = pieces[4:7]
    rounded = master.astype(jnp.bfloat16)
    attention_parts = gather_high(rounded[:attention_rows])
    ffn_rows = rounded[attention_rows:]
    ffn_parts = gather_high(ffn_rows)
    attention_near = gather_wholes(
        *gather_own(attention_pieces, attention_parts, 1, (ffn_parts[1],))
    )
    attention_near = tuple(held(attention_near, ffn_parts[2:]))
    attention_blocks = gather_cores(attention_near)
    ffn_own = gather_own(ffn_pieces, ffn_parts, 2, attention_near[1:])
    ffn_passed = gather_halves(*ffn_own)
    gain_parts = []
    for start, width in ((0, D), (D, D), (2 * D, D), (3 * D, D), (4 * D, HD), (4 * D + HD, HD)):
        gain_parts.append(gains[start : start + width][None])
    gain_input, gain_attn, gain_ffin, gain_ffout, gain_query, gain_key = gain_parts
    order = width_order(device_count)
    doc_row = doc_ids[0]
    angles = lax.dynamic_slice_in_dim(angles_of(positions(doc_row)), first_row, local_rows, 0)
    cosine, sine = jnp.cos(angles), jnp.sin(angles)
    query_docs = lax.dynamic_slice_in_dim(doc_row, first_row, local_rows, 0)
    key_count = group_size * local_rows
    first_keys = [(lax.axis_index("group") ^ step) * local_rows for step in range(group_size)]
    key_docs = jnp.concatenate(
        [lax.dynamic_slice_in_dim(doc_row, start, local_rows, 0) for start in first_keys]
    )
    key_index = jnp.concatenate(
        [start + jnp.arange(local_rows, dtype=jnp.int32) for start in first_keys]
    )
    query_index = first_row + jnp.arange(local_rows, dtype=jnp.int32)
    distance = query_index[:, None] - key_index[None, :]
    allowed = (distance >= 0) & (distance < WINDOW) & (key_docs[None, :] == query_docs[:, None])
    allowed = allowed.astype(jnp.float32)

    width = HQ * HD
    normed, query_proj, key_proj, query_rot, key_value = local_call(
        functools.partial(project_kernel, attention_pieces),
        (
            array((local_rows, D), jnp.bfloat16),
            array((local_rows, width), jnp.float32),
            array((local_rows, HD), jnp.float32),
            array((local_rows, width), jnp.bfloat16),
            array((local_rows, 2 * HD), jnp.bfloat16),
        ),
        (tokens, gain_input, gain_query, gain_key, cosine, sine, order, *attention_blocks),
    )
    key_values = [key_value] + [swap(key_value, step) for step in range(1, group_size)]
    probs, attended, attn_out, middle, out_weight = local_call(
        functools.partial(attend_kernel, attention_pieces),
        (
            array((local_rows, HQ * key_count), jnp.float32),
            array((local_rows, width), jnp.bfloat16),
            array((local_rows, D), jnp.float32),
            array((local_rows, D), jnp.float32),
            array((width, D), jnp.bfloat16),
        ),
        (tokens, gain_attn, allowed, query_rot, *attention_blocks, *key_values),
    )
    ffn_weights = gather_cores(gather_rest(*ffn_own, *ffn_passed, key_values, (middle,)))
    outputs, grad_middle, grad_gain_ffin, grad_gain_ffout, grads_ffn = ffn_blocks(
        pieces, middle, cotangent, gain_ffin, gain_ffout, order, ffn_weights
    )
    near_three, near_one, far_three, far_one = grads_ffn
    far_three, far_one = scatter_cores(far_three, far_one)
    grad_out_weight, grad_query, grad_gain_attn, own_key, across_key, cores_key = local_call(
        attend_back_kernel,
        (
            array((width, D), jnp.bfloat16),
            array((local_rows, width), jnp.float32),
            array((1, D), jnp.float32),
            array((local_rows, 2 * HD), jnp.float32),
            array((local_rows, 2 * HD), jnp.float32),
            array((2 * local_rows, 2 * HD), jnp.bfloat16),
        ),
        (
            grad_middle,
            attn_out,
            gain_attn,
            out_weight,
            attended,
            probs,
            query_rot,
            *key_values,
        ),
    )
    cores_key = swap(cores_key, 1)
    over_x, over_y, sent = scatter_one(ffn_pieces, near_one, far_one, (grad_query,))
    threes = scatter_three(ffn_pieces, near_three, far_three, (sent,), (across_key, cores_key))
    grad_query_weight, grad_normed, grad_gain_query = local_call(
        functools.partial(query_back_kernel, attention_pieces),
        (
            array((D, width), jnp.bfloat16),
            array((local_rows, D), jnp.float32),
            array((1, HD), jnp.float32),
        ),
        (gain_query, cosine, sine, normed, query_proj, grad_query, *attention_blocks),
        (),
        (threes[0],),
    )
    ffn_terms, sent = scatter_passed(
        ffn_pieces, threes, over_x, over_y, near_one, far_one, (grad_normed,)
    )
    grad_key_weight, grad_inputs, grad_gains = local_call(
        functools.partial(project_back_kernel, attention_pieces),
        (
            array((D, 2 * HD), jnp.bfloat16),
            array((local_rows, D), jnp.bfloat16),
            array((GAIN_ROWS, LANES), jnp.float32),
        ),
        (
            tokens,
            gain_input,
            gain_key,
            cosine,
            sine,
            order,
            normed,
            key_proj,
            grad_normed,
            grad_middle,
            grad_gain_attn,
            grad_gain_ffin,
            grad_gain_ffout,
            grad_gain_query,
            own_key,
            cores_key,
            threes[4],
            *attention_blocks,
        ),
        (),
        (sent, threes[1]),
    )
    near_three, near_one, far_three, far_one = local_call(
        functools.partial(split_kernel, attention_pieces),
        grad_arrays(attention_pieces, GAIN_ROWS),
        (grad_query_weight, grad_key_weight, grad_out_weight, grad_gains),
    )
    far_three, far_one = held((far_three, far_one), ffn_terms[2:4])
    grads_ffn, sent, arrived = scatter_high(ffn_pieces, ffn_terms, (near_one,))
    far_three, far_one = scatter_cores(far_three, far_one)
    over_x, over_y, threes = scatter_all(
        attention_pieces, near_three, near_one, far_three, far_one, (sent,)
    )
    terms, _ = scatter_passed(
        attention_pieces, threes, over_x, over_y, near_one, far_one, (arrived[0],)
    )
    grads_attention, _, _ = scatter_high(attention_pieces, terms, arrived)
    gain_grads = grads_attention[attention_rows:].reshape(-1)[: gains.shape[0]]
    grads_local = jnp.concatenate([grads_attention[:attention_rows], grads_ffn])
    return (
        outputs,
        grad_inputs,
        *adam_update(grads_local, first_moment, second_moment, master, learn_rate, weight_decay),
        *adam_update(gain_grads, gain_first, gain_second, gains, gain_rate, 0.0),
    )


def shards(
    tokens, doc_ids, cotangent, master, first_moment, second_moment, gains, gain_first, gain_second
):
    group_size = lax.axis_size("group")
    devices_all = lax.axis_size("dp") * group_size
    if aligned(devices_all):
        return shards_blocks(
            devices_all,
            tokens,
            doc_ids,
            cotangent,
            master,
            first_moment,
            second_moment,
            gains,
            gain_first,
            gain_second,
        )
    group_index = lax.axis_index("group")
    local_rows = tokens.shape[0]
    shard_parts = [
        part_rows.astype(jnp.bfloat16) for part_rows in split_rows(master, piece_rows(devices_all))
    ]
    gathered = (
        lax.all_gather(shard_parts[0], ("dp", "group"), axis=0, tiled=True),
        lax.all_gather(shard_parts[1], ("dp", "group"), axis=0, tiled=True),
        lax.all_gather(shard_parts[2], ("dp", "group"), axis=0, tiled=True),
        lax.all_gather(shard_parts[3], ("dp", "group"), axis=0, tiled=True),
        lax.all_gather(shard_parts[4], ("dp", "group"), axis=0, tiled=True),
        lax.all_gather(shard_parts[5], ("dp", "group"), axis=0, tiled=True),
        lax.all_gather(shard_parts[6], ("dp", "group"), axis=0, tiled=True),
    )
    query_weight, key_weight, value_weight, out_weight, gate_weight, up_weight, down_weight = [
        full_rows.reshape(shape_pair) for full_rows, shape_pair in zip(gathered, piece_shapes())
    ]
    norm_input = gains[0:D]
    norm_attn = gains[D : 2 * D]
    norm_ffin = gains[2 * D : 3 * D]
    norm_ffout = gains[3 * D : 4 * D]
    norm_query = gains[4 * D : 4 * D + HD]
    norm_key = gains[4 * D + HD : 4 * D + 2 * HD]
    doc_row = doc_ids[0]
    first_row = group_index * local_rows
    angles = lax.dynamic_slice_in_dim(angles_of(positions(doc_row)), first_row, local_rows, 0)
    query_docs = lax.dynamic_slice_in_dim(doc_row, first_row, local_rows, 0)
    inputs = tokens.astype(jnp.float32)
    normed, back_input = jax.vjp(rms_norm, inputs, norm_input)
    normed_low = normed.astype(jnp.bfloat16)
    query_proj = matmul(normed_low, query_weight)
    key_proj = matmul(normed_low, key_weight)
    value_proj = matmul(normed_low, value_weight)

    def query_prep(flat_rows, gain_vec):
        return rotate(rms_norm(flat_rows.reshape(local_rows, HQ, HD), gain_vec), angles[:, None, :])

    def key_prep(rows_in, gain_vec):
        return rotate(rms_norm(rows_in, gain_vec), angles)

    query_rot, back_query = jax.vjp(query_prep, query_proj, norm_query)
    key_rot, back_key = jax.vjp(key_prep, key_proj, norm_key)
    query_low = query_rot.astype(jnp.bfloat16)
    key_low = key_rot.astype(jnp.bfloat16)
    value_low = value_proj.astype(jnp.bfloat16)
    reach = min(-(-(WINDOW - 1) // local_rows), group_size - 1)
    key_list = [key_low]
    value_list = [value_low]
    for offset in range(1, reach + 1):
        key_far, value_far = shifted((key_low, value_low), "group", offset)
        key_list.insert(0, key_far)
        value_list.insert(0, value_far)
    key_all = jnp.concatenate(key_list, axis=0)
    value_all = jnp.concatenate(value_list, axis=0)
    key_count = (reach + 1) * local_rows
    doc_pad = jnp.concatenate([jnp.full((reach * local_rows,), -1, jnp.int32), doc_row])
    key_docs = lax.dynamic_slice_in_dim(doc_pad, first_row, key_count, 0)
    key_index = (group_index - reach) * local_rows + jnp.arange(key_count, dtype=jnp.int32)
    query_index = first_row + jnp.arange(local_rows, dtype=jnp.int32)
    distance = query_index[:, None] - key_index[None, :]
    allowed = (distance >= 0) & (distance < WINDOW) & (key_docs[None, :] == query_docs[:, None])

    def scores_of(key_rows_low):
        raw_scores = jnp.einsum(
            "qhd,kd->hqk", query_low, key_rows_low, preferred_element_type=jnp.float32
        ) * HD ** (-0.5)
        return jnp.where(allowed[None], raw_scores, -1e30)

    masked = scores_of(key_all)
    top_score = jnp.max(masked, axis=-1, keepdims=True)
    log_total = top_score + jnp.log(jnp.sum(jnp.exp(masked - top_score), axis=-1, keepdims=True))
    probs = jnp.exp(masked - log_total)
    attended = jnp.einsum(
        "hqk,kd->qhd", probs.astype(jnp.bfloat16), value_all, preferred_element_type=jnp.float32
    )
    attended_low = attended.reshape(local_rows, HQ * HD).astype(jnp.bfloat16)
    attn_out = matmul(attended_low, out_weight)
    branch_one, back_attn = jax.vjp(rms_norm, attn_out, norm_attn)
    middle = inputs + branch_one
    normed_two, back_ffin = jax.vjp(rms_norm, middle, norm_ffin)
    normed_two_low = normed_two.astype(jnp.bfloat16)
    gate_proj = matmul(normed_two_low, gate_weight)
    up_proj = matmul(normed_two_low, up_weight)
    hidden, back_hidden = jax.vjp(geglu, gate_proj, up_proj)
    hidden_low = hidden.astype(jnp.bfloat16)
    ffn_out = matmul(hidden_low, down_weight)
    branch_two, back_ffout = jax.vjp(rms_norm, ffn_out, norm_ffout)
    outputs = middle + branch_two
    grad_out = cotangent.astype(jnp.float32)
    grad_ffn, grad_gain_ffout = back_ffout(grad_out)
    grad_ffn_low = grad_ffn.astype(jnp.bfloat16)
    grad_down_w = jnp.einsum(
        "tf,td->fd", hidden_low, grad_ffn_low, preferred_element_type=jnp.float32
    )
    grad_hidden = jnp.einsum(
        "td,fd->tf", grad_ffn_low, down_weight, preferred_element_type=jnp.float32
    )
    grad_gate, grad_up = back_hidden(grad_hidden)
    grad_gate_low = grad_gate.astype(jnp.bfloat16)
    grad_up_low = grad_up.astype(jnp.bfloat16)
    grad_gate_w = jnp.einsum(
        "td,tf->df", normed_two_low, grad_gate_low, preferred_element_type=jnp.float32
    )
    grad_up_w = jnp.einsum(
        "td,tf->df", normed_two_low, grad_up_low, preferred_element_type=jnp.float32
    )
    grad_normed_two = jnp.einsum(
        "tf,df->td", grad_gate_low, gate_weight, preferred_element_type=jnp.float32
    ) + jnp.einsum("tf,df->td", grad_up_low, up_weight, preferred_element_type=jnp.float32)
    grad_middle_norm, grad_gain_ffin = back_ffin(grad_normed_two)
    grad_middle = grad_out + grad_middle_norm
    grad_attn, grad_gain_attn = back_attn(grad_middle)
    grad_attn_low = grad_attn.astype(jnp.bfloat16)
    grad_out_w = jnp.einsum(
        "to,td->od", attended_low, grad_attn_low, preferred_element_type=jnp.float32
    )
    grad_attended = jnp.einsum(
        "td,od->to", grad_attn_low, out_weight, preferred_element_type=jnp.float32
    )
    grad_attended_low = grad_attended.astype(jnp.bfloat16).reshape(local_rows, HQ, HD)
    probs_again = jnp.exp(scores_of(key_all) - log_total)
    grad_probs = jnp.einsum(
        "qhd,kd->hqk", grad_attended_low, value_all, preferred_element_type=jnp.float32
    )
    grad_value_all = jnp.einsum(
        "hqk,qhd->kd",
        probs_again.astype(jnp.bfloat16),
        grad_attended_low,
        preferred_element_type=jnp.float32,
    )
    grad_scores = probs_again * (
        grad_probs - jnp.sum(probs_again * grad_probs, axis=-1, keepdims=True)
    )
    grad_scores_low = (grad_scores * HD ** (-0.5)).astype(jnp.bfloat16)
    grad_query = jnp.einsum(
        "hqk,kd->qhd", grad_scores_low, key_all, preferred_element_type=jnp.float32
    )
    grad_key_all = jnp.einsum(
        "hqk,qhd->kd", grad_scores_low, query_low, preferred_element_type=jnp.float32
    )
    key_total = grad_key_all[reach * local_rows :]
    value_total = grad_value_all[reach * local_rows :]
    for offset in range(1, reach + 1):
        row_start = (reach - offset) * local_rows
        key_back, value_back = (
            shifted(
                grad_key_all[row_start : row_start + local_rows].astype(jnp.bfloat16),
                "group",
                -offset,
            ).astype(jnp.float32),
            shifted(
                grad_value_all[row_start : row_start + local_rows].astype(jnp.bfloat16),
                "group",
                -offset,
            ).astype(jnp.float32),
        )
        key_total = key_total + key_back
        value_total = value_total + value_back
    grad_query_proj, grad_gain_query = back_query(grad_query)
    grad_key_proj, grad_gain_key = back_key(key_total)
    grad_query_low = grad_query_proj.astype(jnp.bfloat16)
    grad_key_low = grad_key_proj.astype(jnp.bfloat16)
    grad_value_low = value_total.astype(jnp.bfloat16)
    grad_query_w = jnp.einsum(
        "td,te->de", normed_low, grad_query_low, preferred_element_type=jnp.float32
    )
    grad_key_w = jnp.einsum(
        "td,te->de", normed_low, grad_key_low, preferred_element_type=jnp.float32
    )
    grad_value_w = jnp.einsum(
        "td,te->de", normed_low, grad_value_low, preferred_element_type=jnp.float32
    )
    grad_normed = jnp.einsum(
        "te,de->td", grad_query_low, query_weight, preferred_element_type=jnp.float32
    )
    grad_normed = grad_normed + jnp.einsum(
        "te,de->td", grad_key_low, key_weight, preferred_element_type=jnp.float32
    )
    grad_normed = grad_normed + jnp.einsum(
        "te,de->td", grad_value_low, value_weight, preferred_element_type=jnp.float32
    )
    grad_input_norm, grad_gain_input = back_input(grad_normed)
    grad_inputs = grad_middle + grad_input_norm
    flat_query = grad_query_w.reshape(-1, 128)
    flat_key = grad_key_w.reshape(-1, 128)
    flat_value = grad_value_w.reshape(-1, 128)
    flat_out = grad_out_w.reshape(-1, 128)
    flat_gate = grad_gate_w.reshape(-1, 128)
    flat_up = grad_up_w.reshape(-1, 128)
    flat_down = grad_down_w.reshape(-1, 128)
    reduced = (
        lax.psum_scatter(flat_query, ("dp", "group"), scatter_dimension=0, tiled=True),
        lax.psum_scatter(flat_key, ("dp", "group"), scatter_dimension=0, tiled=True),
        lax.psum_scatter(flat_value, ("dp", "group"), scatter_dimension=0, tiled=True),
        lax.psum_scatter(flat_out, ("dp", "group"), scatter_dimension=0, tiled=True),
        lax.psum_scatter(flat_gate, ("dp", "group"), scatter_dimension=0, tiled=True),
        lax.psum_scatter(flat_up, ("dp", "group"), scatter_dimension=0, tiled=True),
        lax.psum_scatter(flat_down, ("dp", "group"), scatter_dimension=0, tiled=True),
    )
    grads_local = jnp.concatenate(list(reduced), axis=0)
    gain_grads = lax.psum(
        jnp.concatenate(
            [
                grad_gain_input,
                grad_gain_attn,
                grad_gain_ffin,
                grad_gain_ffout,
                grad_gain_query,
                grad_gain_key,
            ]
        ),
        ("dp", "group"),
    )
    moment_first, moment_second, master_new = adam_update(
        grads_local, first_moment, second_moment, master, learn_rate, weight_decay
    )
    gain_moment_first, gain_moment_second, gains_new = adam_update(
        gain_grads, gain_first, gain_second, gains, gain_rate, 0.0
    )
    return (
        outputs.astype(jnp.bfloat16),
        grad_inputs.astype(jnp.bfloat16),
        moment_first,
        moment_second,
        master_new,
        gain_moment_first,
        gain_moment_second,
        gains_new,
    )


def solution(mesh):
    placed = (
        P(("dp", "group"), None),
        P("dp", None),
        P(("dp", "group"), None),
        P(("dp", "group"), None),
        P(("dp", "group"), None),
        P(("dp", "group"), None),
        P(),
        P(),
        P(),
    )
    return jax.shard_map(
        shards,
        mesh=mesh,
        in_specs=placed,
        out_specs=(
            P(("dp", "group"), None),
            P(("dp", "group"), None),
            P(("dp", "group"), None),
            P(("dp", "group"), None),
            P(("dp", "group"), None),
            P(),
            P(),
            P(),
        ),
        check_vma=False,
    )
```
